128 devices in a mesh: section: 4 (over y_lo, core), dp: 32 (over z, x, y_hi).
Axes of the slice: x: 4, y: 4 (y_hi: 2, y_lo: 2; y = y_hi * 2 + y_lo), z: 4, core: 2. Of those that a mesh axis runs over, the one named last changes fastest.
Arguments:
- inputs: bfloat16 [2, 64, 160, 768], P(None, 'dp'), may hold values from -6 to 6
- cotangent: bfloat16 [2, 64, 160, 768], P(None, 'dp'), may hold values from -6 to 6
- lengths: int32 [2, 64], P(None, 'dp'), may hold values from 80 to 160, as said below
- cdr_spans: int32 [2, 64, 2], P(None, 'dp'), may hold values from 0 to 160, as said below
- mask_vector: bfloat16 [768], replicated, may hold values from -6 to 6
- w_qkv: bfloat16 [1536, 2304], P('section'), may hold values from -0.21875 to 0.21875
- qv_bias: bfloat16 [3072], P('section'), may hold values from -2 to 2
- w_out: bfloat16 [1536, 768], P('section'), may hold values from -1.75 to 1.75
- b_out: bfloat16 [1536], P('section'), may hold values from -2 to 2
- norm1_gain: bfloat16 [1536], P('section'), may hold values from 0.5 to 1.5
- norm1_bias: bfloat16 [1536], P('section'), may hold values from -2 to 2
- w_up: bfloat16 [1536, 3072], P('section'), may hold values from -0.21875 to 0.21875
- b_up: bfloat16 [6144], P('section'), may hold values from -2 to 2
- w_down: bfloat16 [6144, 768], P('section'), may hold values from -0.15625 to 0.15625
- b_down: bfloat16 [1536], P('section'), may hold values from -2 to 2
- norm2_gain: bfloat16 [1536], P('section'), may hold values from 0.5 to 1.5
- norm2_bias: bfloat16 [1536], P('section'), may hold values from -2 to 2
Outputs:
- layer_outputs: bfloat16 [4, 64, 160, 768], P('section', 'dp')
- input_grads: bfloat16 [4, 64, 160, 768], P('section', 'dp')
- mask_grad: float32 [768], replicated
- grad_w_qkv: float32 [1536, 2304], P('section')
- grad_qv_bias: float32 [3072], P('section')
- grad_w_out: float32 [1536, 768], P('section')
- grad_b_out: float32 [1536], P('section')
- grad_norm1_gain: float32 [1536], P('section')
- grad_norm1_bias: float32 [1536], P('section')
- grad_w_up: float32 [1536, 3072], P('section')
- grad_b_up: float32 [6144], P('section')
- grad_w_down: float32 [6144, 768], P('section')
- grad_b_down: float32 [1536], P('section')
- grad_norm2_gain: float32 [1536], P('section')
- grad_norm2_bias: float32 [1536], P('section')
The draws below stay inside these ranges and needn't reach their ends.
Inputs may be any that keep to these rules, and one draw needn't show every extreme that they name: `lengths`: positions from a chain's length to 159 are padding. `cdr_spans`: start < end <= the chain's length and end - start <= 12.
All inputs are finite; a program needn't handle non-finite values.
Results may differ from the reference program's by a relative error of at most 0.03.
Values may be sent and summed in bfloat16 or wider, within the bound.
No kernel may reach another device: no remote copies, remote signals or barrier semaphores. Data moves between devices by JAX's collectives and lax.ppermute only.
A program may use at most 256 MiB of HBM per device.

```python
import math
import jax
import jax.numpy as jnp
from jax import lax

D = 768
HEADS = 12
FF = 3072
HEAD_DIM = 64
LEN = 160
SPAN = 12
CHAINS = 64


def chain_table(key):
    chain_total = 2 * CHAINS
    short_len = LEN // 2
    long_pick = jax.random.randint(jax.random.fold_in(key, 101), (), 0, chain_total)
    offset_pick = jax.random.randint(jax.random.fold_in(key, 102), (), 0, chain_total - 1)
    short_pick = (long_pick + 1 + offset_pick) % chain_total
    chain_lens = jax.random.randint(jax.random.fold_in(key, 103), (chain_total,), short_len, LEN + 1)
    chain_slot = jnp.arange(chain_total, dtype=jnp.int32)
    chain_lens = jnp.where(chain_slot == long_pick, LEN, chain_lens)
    chain_lens = jnp.where(chain_slot == short_pick, short_len, chain_lens)
    return (chain_lens.astype(jnp.int32), chain_slot, long_pick, short_pick)


def draw_lengths(key, part):
    chain_lens, chain_slot, long_pick, short_pick = chain_table(key)
    return chain_lens.reshape(2, CHAINS).astype(jnp.int32)


def draw_cdr_spans(key, part):
    chain_lens, chain_slot, long_pick, short_pick = chain_table(key)
    key = jax.random.fold_in(key, 7)
    chain_total = 2 * CHAINS
    span_lens = jax.random.randint(jax.random.fold_in(key, 1), (chain_total,), 1, SPAN + 1)
    span_lens = jnp.where(chain_slot == long_pick, SPAN, span_lens)
    starts = jax.random.randint(jax.random.fold_in(key, 2), (chain_total,), 0, chain_lens - span_lens + 1)
    starts = jnp.where(chain_slot == long_pick, LEN - SPAN, starts)
    starts = jnp.where(chain_slot == short_pick, 0, starts)
    spans = jnp.stack([starts, starts + span_lens], axis=-1)
    return spans.reshape(2, CHAINS, 2).astype(jnp.int32)


def block_scale(stream_key, dims, shards, low, top_value):
    factor_of, own = 1.0, jax.random.fold_in(stream_key, 6)
    for dim, blocks in shards:
        heights = jnp.exp(jax.random.uniform(jax.random.fold_in(own, dim), (blocks,), jnp.float32, low / len(shards), top_value / len(shards)))
        factor_of = factor_of * jnp.repeat(heights, dims[dim] // blocks).reshape([-1 if axis == dim else 1 for axis in range(len(dims))])
    return factor_of


def noise(key, dims, width, reach, shards=(), kind=jnp.bfloat16):
    drawn = width * jax.random.normal(key, dims, jnp.float32)
    if shards:
        drawn = drawn * block_scale(key, dims, shards, -0.22, 0.18)
    return jnp.clip(drawn, -reach, reach).astype(kind)


def setup_inputs(seed: int = 0) -> dict:
    arg_keys = jax.random.split(jax.random.key(seed), 18)
    inputs = noise(arg_keys[0], (2, CHAINS, LEN, D), 1.0, 6.0, ((1, 32),))
    cotangent = noise(arg_keys[1], (2, CHAINS, LEN, D), 1.0, 6.0, ((1, 32),))
    lengths = draw_lengths(jax.random.fold_in(arg_keys[17], 71), 0)
    cdr_spans = draw_cdr_spans(jax.random.fold_in(arg_keys[17], 71), 0)
    mask_vector = noise(arg_keys[4], (D,), 1.0, 6.0)
    w_qkv = noise(arg_keys[5], (2 * D, 3 * D), D ** -0.5, 0.21875, ((0, 4),))
    qv_bias = noise(arg_keys[6], (4 * D,), 0.3, 2.0, ((0, 4),))
    w_out = noise(arg_keys[7], (2 * D, D), (max(D // 64, 1)) ** -0.5, 1.75, ((0, 4),))
    b_out = noise(arg_keys[8], (2 * D,), 0.3, 2.0, ((0, 4),))
    norm1_gain = jnp.clip(1.0 + 0.1 * jax.random.normal(arg_keys[9], (2 * D,), jnp.float32), 0.5, 1.5).astype(jnp.bfloat16)
    norm1_bias = noise(arg_keys[10], (2 * D,), 0.3, 2.0, ((0, 4),))
    w_up = noise(arg_keys[11], (2 * D, FF), D ** -0.5, 0.21875, ((0, 4),))
    b_up = noise(arg_keys[12], (2 * FF,), 0.3, 2.0, ((0, 4),))
    w_down = noise(arg_keys[13], (2 * FF, D), (FF // 2) ** -0.5, 0.15625, ((0, 4),))
    b_down = noise(arg_keys[14], (2 * D,), 0.3, 2.0, ((0, 4),))
    norm2_gain = jnp.clip(1.0 + 0.1 * jax.random.normal(arg_keys[15], (2 * D,), jnp.float32), 0.5, 1.5).astype(jnp.bfloat16)
    norm2_bias = noise(arg_keys[16], (2 * D,), 0.3, 2.0, ((0, 4),))
    return dict(inputs=inputs, cotangent=cotangent, lengths=lengths, cdr_spans=cdr_spans, mask_vector=mask_vector, w_qkv=w_qkv, qv_bias=qv_bias, w_out=w_out, b_out=b_out, norm1_gain=norm1_gain, norm1_bias=norm1_bias, w_up=w_up, b_up=b_up, w_down=w_down, b_down=b_down, norm2_gain=norm2_gain, norm2_bias=norm2_bias)


@jax.custom_vjp
def low(v):
    return lax.optimization_barrier(v.astype(jnp.bfloat16)).astype(jnp.float32)

@jax.custom_vjp
def low_back(v):
    return v

def low_keep(v):
    return (low(v), None)

def low_pass(kept, grad):
    return (grad,)

def back_keep(v):
    return (v, None)

def back_low(kept, grad):
    return (low(grad),)
low.defvjp(low_keep, low_pass)
low_back.defvjp(back_keep, back_low)

def matmul(left_side, right_side):
    return jnp.dot(left_side, right_side, precision=lax.Precision.HIGHEST, preferred_element_type=jnp.float32)

def norm_rows(values, norm_gain, norm_shift):
    center = values - lax.optimization_barrier(jnp.mean(values, axis=-1, keepdims=True))
    spread = lax.optimization_barrier(jnp.mean(center * center, axis=-1, keepdims=True))
    return center * lax.rsqrt(spread + 1e-05) * norm_gain + norm_shift

def attend_block(block_in):
    queries, key_heads, value_heads, key_valid = block_in
    scale = 1.0 / math.sqrt(HEAD_DIM)
    scores = jnp.einsum('clhe,cmhe->chlm', queries, key_heads, precision=lax.Precision.HIGHEST) * scale
    scores = low_back(jnp.where(key_valid[:, None, None, :], scores, -1000000000.0))
    softmax_w = low(jax.nn.softmax(scores, axis=-1))
    return jnp.einsum('chlm,cmhe->clhe', softmax_w, value_heads, precision=lax.Precision.HIGHEST)

def take_rows(tensor, layer_index):
    half_rows = tensor.shape[0] // 2
    return tensor[layer_index * half_rows:(layer_index + 1) * half_rows]

def layer(hidden, params, key_valid):
    w_qkv, qv_bias, w_out, b_out, norm1_gain, norm1_bias, w_up, b_up, w_down, b_down, norm2_gain, norm2_bias = params
    chains, length, model_width = hidden.shape
    rows_flat = hidden.reshape(-1, model_width)
    full_bias = jnp.concatenate([qv_bias[:model_width], jnp.zeros((model_width,), jnp.float32), qv_bias[model_width:]])
    projected = low(low_back(matmul(rows_flat, w_qkv) + full_bias))
    projected = projected.reshape(chains, length, 3, HEADS, HEAD_DIM)
    per_block = math.gcd(chains, 16)
    blocks = (projected[:, :, 0], projected[:, :, 1], projected[:, :, 2], key_valid)
    blocks = tuple((tensor.reshape((chains // per_block, per_block) + tensor.shape[1:]) for tensor in blocks))
    attended = lax.map(jax.checkpoint(attend_block), blocks)
    attended = low(low_back(attended.reshape(-1, model_width)))
    branch = low_back(matmul(attended, w_out) + b_out)
    normed = low(norm_rows(rows_flat + branch, norm1_gain, norm1_bias))
    hidden_pre = low_back(matmul(normed, w_up) + b_up)
    active = low(jax.nn.gelu(hidden_pre, approximate=False))
    second = low_back(matmul(active, w_down) + b_down)
    return norm_rows(normed + second, norm2_gain, norm2_bias).reshape(chains, length, model_width)

def reference(inputs, cotangent, lengths, cdr_spans, mask_vector, w_qkv, qv_bias, w_out, b_out, norm1_gain, norm1_bias, w_up, b_up, w_down, b_down, norm2_gain, norm2_bias):
    chain_total = 2 * CHAINS
    positions = jnp.arange(LEN, dtype=jnp.int32)
    chain_lens = lengths.reshape(chain_total).astype(jnp.int32)
    key_valid = positions[None, :] < chain_lens[:, None]
    span_flat = cdr_spans.reshape(chain_total, 2).astype(jnp.int32)
    masked = (positions[None, :] >= span_flat[:, 0:1]) & (positions[None, :] < span_flat[:, 1:2])
    inputs_f = inputs.reshape(chain_total, LEN, D).astype(jnp.float32)
    mask_f = mask_vector.astype(jnp.float32)
    params = tuple((tensor.astype(jnp.float32) for tensor in (w_qkv, qv_bias, w_out, b_out, norm1_gain, norm1_bias, w_up, b_up, w_down, b_down, norm2_gain, norm2_bias)))
    carried = jnp.zeros_like(inputs_f)

    def forward(entry, mask_entry, layer_params, carried_in):
        layer_zero = tuple((take_rows(tensor, 0) for tensor in layer_params))
        layer_one = tuple((take_rows(tensor, 1) for tensor in layer_params))
        hidden = jnp.where(masked[:, :, None], mask_entry[None, None, :], entry)
        first_out = low(low_back(layer(hidden, layer_zero, key_valid)))
        second_out = layer(first_out + carried_in, layer_one, key_valid)
        return (first_out, second_out)
    (first_out, second_out), pullback = jax.vjp(forward, inputs_f, mask_f, params, carried)
    upstream = cotangent.reshape(chain_total, LEN, D).astype(jnp.float32)
    grad_inputs, grad_mask, grad_params, grad_carried = pullback((jnp.zeros_like(first_out), upstream))
    shape_four = (2, CHAINS, LEN, D)
    layer_outputs = jnp.concatenate([first_out.reshape(shape_four), second_out.reshape(shape_four)], 0).astype(jnp.bfloat16)
    input_grads = jnp.concatenate([grad_inputs.reshape(shape_four), grad_carried.reshape(shape_four)], 0).astype(jnp.bfloat16)
    return (layer_outputs, input_grads, grad_mask, grad_params[0], grad_params[1], grad_params[2], grad_params[3], grad_params[4], grad_params[5], grad_params[6], grad_params[7], grad_params[8], grad_params[9], grad_params[10], grad_params[11])
```

```python
import math

import jax
import jax.numpy as jnp
from jax import lax
from jax.sharding import PartitionSpec as P

HEADS = 12


EPSILON = 1e-05


def partner(x, axis, bit):
    return lax.ppermute(x, axis, [(i, i ^ 1 << bit) for i in range(lax.axis_size(axis))])


def norm_rows(values, norm_gain, norm_shift):
    center = values - jnp.mean(values, axis=-1, keepdims=True)
    spread = jnp.mean(center * center, axis=-1, keepdims=True)
    return center * lax.rsqrt(spread + EPSILON) * norm_gain + norm_shift


def gelu_exact(values):
    return jax.nn.gelu(values, approximate=False)


def contract_rows(left_side, right_side):
    return lax.dot_general(
        left_side, right_side, (((0,), (0,)), ((), ())), preferred_element_type=jnp.float32
    )


def contract_cols(left_side, right_side):
    return lax.dot_general(
        left_side, right_side, (((1,), (1,)), ((), ())), preferred_element_type=jnp.float32
    )


def assemble(own_part, partner_part, pair_half):
    lower = jnp.where(pair_half == 0, own_part, partner_part)
    upper = jnp.where(pair_half == 0, partner_part, own_part)
    return jnp.concatenate([lower, upper], axis=0)


def take_half(tensor, which_half):
    half_rows = tensor.shape[0] // 2
    return lax.dynamic_slice_in_dim(tensor, which_half * half_rows, half_rows, 0)


def forward_parts(layer_in, params, key_valid):
    (
        w_qkv,
        qv_bias,
        w_out,
        b_out,
        norm1_gain,
        norm1_bias,
        w_up,
        b_up,
        w_down,
        b_down,
        norm2_gain,
        norm2_bias,
    ) = params
    chains, length, model_width = layer_in.shape
    head_dim = model_width // HEADS
    scale = 1.0 / math.sqrt(head_dim)
    rows_in = layer_in.reshape(-1, model_width)
    full_bias = jnp.concatenate(
        [
            qv_bias[:model_width].astype(jnp.float32),
            jnp.zeros((model_width,), jnp.float32),
            qv_bias[model_width:].astype(jnp.float32),
        ]
    )
    projected = (jnp.dot(rows_in, w_qkv, preferred_element_type=jnp.float32) + full_bias).astype(
        jnp.bfloat16
    )
    projected = projected.reshape(chains, length, 3, HEADS, head_dim)
    queries = projected[:, :, 0]
    key_heads = projected[:, :, 1]
    value_heads = projected[:, :, 2]
    scores = (
        jnp.einsum("clhe,cmhe->chlm", queries, key_heads, preferred_element_type=jnp.float32)
        * scale
    )
    scores = jnp.where(key_valid[:, None, None, :], scores, -1000000000.0)
    top_score = jnp.max(scores, axis=-1, keepdims=True)
    log_total = top_score + jnp.log(jnp.sum(jnp.exp(scores - top_score), axis=-1, keepdims=True))
    softmax_w = jnp.exp(scores - log_total)
    weights_low = softmax_w.astype(jnp.bfloat16)
    attended = jnp.einsum(
        "chlm,cmhe->clhe", weights_low, value_heads, preferred_element_type=jnp.float32
    )
    attended = attended.reshape(-1, model_width).astype(jnp.bfloat16)
    branch = jnp.dot(attended, w_out, preferred_element_type=jnp.float32) + b_out.astype(
        jnp.float32
    )
    residual_one = rows_in.astype(jnp.float32) + branch
    normed_low = norm_rows(
        residual_one, norm1_gain.astype(jnp.float32), norm1_bias.astype(jnp.float32)
    ).astype(jnp.bfloat16)
    hidden_pre = jnp.dot(normed_low, w_up, preferred_element_type=jnp.float32) + b_up.astype(
        jnp.float32
    )
    active_low = gelu_exact(hidden_pre).astype(jnp.bfloat16)
    second = jnp.dot(active_low, w_down, preferred_element_type=jnp.float32) + b_down.astype(
        jnp.float32
    )
    residual_two = normed_low.astype(jnp.float32) + second
    output = norm_rows(residual_two, norm2_gain.astype(jnp.float32), norm2_bias.astype(jnp.float32))
    kept_parts = (
        rows_in,
        queries,
        key_heads,
        value_heads,
        softmax_w,
        weights_low,
        attended,
        residual_one,
        normed_low,
        hidden_pre,
        active_low,
        residual_two,
    )
    return (output.reshape(chains, length, model_width), kept_parts)


def layer_backward(layer_in, params, kept_parts, upstream):
    (
        w_qkv,
        qv_bias,
        w_out,
        b_out,
        norm1_gain,
        norm1_bias,
        w_up,
        b_up,
        w_down,
        b_down,
        norm2_gain,
        norm2_bias,
    ) = params
    chains, length, model_width = layer_in.shape
    head_dim = model_width // HEADS
    scale = 1.0 / math.sqrt(head_dim)
    (
        rows_in,
        queries,
        key_heads,
        value_heads,
        softmax_w,
        weights_low,
        attended,
        residual_one,
        normed_low,
        hidden_pre,
        active_low,
        residual_two,
    ) = kept_parts
    primal_two, norm_two_pull = jax.vjp(
        norm_rows, residual_two, norm2_gain.astype(jnp.float32), norm2_bias.astype(jnp.float32)
    )
    d_res_two, d_norm2_gain, d_norm2_bias = norm_two_pull(upstream.reshape(-1, model_width))
    d_second = d_res_two.astype(jnp.bfloat16)
    d_w_down = contract_rows(active_low, d_second)
    d_b_down = jnp.sum(d_second.astype(jnp.float32), axis=0)
    d_active = contract_cols(d_second, w_down)
    primal_gelu, gelu_pull = jax.vjp(gelu_exact, hidden_pre)
    d_hidden = gelu_pull(d_active)[0].astype(jnp.bfloat16)
    d_w_up = contract_rows(normed_low, d_hidden)
    d_b_up = jnp.sum(d_hidden.astype(jnp.float32), axis=0)
    d_normed = d_res_two + contract_cols(d_hidden, w_up)
    primal_one, norm_one_pull = jax.vjp(
        norm_rows, residual_one, norm1_gain.astype(jnp.float32), norm1_bias.astype(jnp.float32)
    )
    d_res_one, d_norm1_gain, d_norm1_bias = norm_one_pull(d_normed)
    d_branch = d_res_one.astype(jnp.bfloat16)
    d_w_out = contract_rows(attended, d_branch)
    d_b_out = jnp.sum(d_branch.astype(jnp.float32), axis=0)
    d_attended = (
        contract_cols(d_branch, w_out).astype(jnp.bfloat16).reshape(chains, length, HEADS, head_dim)
    )
    d_weights = jnp.einsum(
        "clhe,cmhe->chlm", d_attended, value_heads, preferred_element_type=jnp.float32
    )
    row_term = jnp.sum(softmax_w * d_weights, axis=-1, keepdims=True)
    d_scores = (softmax_w * (d_weights - row_term)).astype(jnp.bfloat16)
    d_queries = (
        jnp.einsum("chlm,cmhe->clhe", d_scores, key_heads, preferred_element_type=jnp.float32)
        * scale
    )
    d_keys = (
        jnp.einsum("chlm,clhe->cmhe", d_scores, queries, preferred_element_type=jnp.float32) * scale
    )
    d_values = jnp.einsum(
        "chlm,clhe->cmhe", weights_low, d_attended, preferred_element_type=jnp.float32
    )
    d_projected = (
        jnp.stack([d_queries, d_keys, d_values], axis=2)
        .reshape(-1, 3 * model_width)
        .astype(jnp.bfloat16)
    )
    d_w_qkv = contract_rows(rows_in, d_projected)
    column_sums = jnp.sum(d_projected.astype(jnp.float32), axis=0)
    d_qv_bias = jnp.concatenate([column_sums[:model_width], column_sums[2 * model_width :]])
    d_input = d_res_one + contract_cols(d_projected, w_qkv)
    layer_grads = (
        d_w_qkv,
        d_qv_bias,
        d_w_out,
        d_b_out,
        d_norm1_gain,
        d_norm1_bias,
        d_w_up,
        d_b_up,
        d_w_down,
        d_b_down,
        d_norm2_gain,
        d_norm2_bias,
    )
    return (d_input.reshape(chains, length, model_width), layer_grads)


BITS = ("zw", "zu", "xw", "xu", "y")
ORDERS = (
    (("zw", "zu", "xw", "xu"), ("zu", "zw", "xu", "xw")),
    (("xw", "xu", "zw", "zu"), ("xu", "xw", "zu", "zw")),
)


def flip_dp(index, bit):
    z, x, y = index // 8, index // 2 % 4, index % 2
    if bit == "zw":
        z ^= 1
    elif bit == "zu":
        z ^= 3
    elif bit == "xw":
        x ^= 1
    elif bit == "xu":
        x ^= 3
    else:
        y ^= 1
    return z * 8 + x * 2 + y


def flip_pairs(bit_of_core):
    pairs = []
    for section in range(4):
        for index in range(32):
            pairs.append(
                (section * 32 + index, section * 32 + flip_dp(index, bit_of_core[section % 2]))
            )
    return pairs


def exchange(value, bit_of_core):
    return lax.ppermute(value, ("section", "dp"), flip_pairs(bit_of_core))


def own_bits():
    index = lax.axis_index("dp")
    z, x, y = index // 8, index // 2 % 4, index % 2
    return {
        "zu": z // 2,
        "zw": (z // 2) ^ (z % 2),
        "xu": x // 2,
        "xw": (x // 2) ^ (x % 2),
        "y": y,
    }


def own_bit(bits, core, part, step):
    return jnp.where(core == 0, bits[ORDERS[0][part][step]], bits[ORDERS[1][part][step]])


def add_low(left_side, right_side):
    return (left_side.astype(jnp.float32) + right_side.astype(jnp.float32)).astype(jnp.bfloat16)


def reduce_rows(pack, extra, bits, core):
    half = pack.shape[0] // 2
    parts = [pack[:half], pack[half:]]
    for step in range(4):
        for part in range(2):
            bit = own_bit(bits, core, part, step)
            rows = parts[part].shape[0] // 2
            keep = lax.dynamic_slice_in_dim(parts[part], bit * rows, rows, 0)
            send = lax.dynamic_slice_in_dim(parts[part], (1 - bit) * rows, rows, 0)
            flips = (ORDERS[0][part][step], ORDERS[1][part][step])
            if part == 0 and extra is not None:
                got = exchange(jnp.concatenate([send, extra], axis=0), flips)
                extra = add_low(extra, got[rows:])
                got = got[:rows]
            else:
                got = exchange(send, flips)
            parts[part] = add_low(keep, got)
    rows = parts[0].shape[0]
    both = jnp.concatenate(parts + ([extra] if extra is not None else []), axis=0)
    both = add_low(both, exchange(both, ("y", "y")))
    parts = [both[:rows], both[rows : 2 * rows]]
    if extra is not None:
        extra = both[2 * rows :]
    for step in reversed(range(4)):
        for part in range(2):
            bit = own_bit(bits, core, part, step)
            flips = (ORDERS[0][part][step], ORDERS[1][part][step])
            got = exchange(parts[part], flips)
            parts[part] = assemble(parts[part], got, bit)
    return jnp.concatenate(parts, axis=0), extra


def fold(tensor):
    return jnp.concatenate(
        [tensor[:, at : at + 768] for at in range(0, tensor.shape[1], 768)], axis=0
    )


def unfold(rows, count):
    return jnp.concatenate(jnp.split(rows, count, axis=0), axis=1)


def per_device(
    inputs,
    cotangent,
    lengths,
    cdr_spans,
    mask_vector,
    w_qkv,
    qv_bias,
    w_out,
    b_out,
    norm1_gain,
    norm1_bias,
    w_up,
    b_up,
    w_down,
    b_down,
    norm2_gain,
    norm2_bias,
):
    section_index = lax.axis_index("section")
    is_first = section_index < 2
    pair_half = section_index % 2
    big = (w_qkv, w_out, w_up, w_down)
    small = jnp.concatenate(
        [qv_bias, b_out, norm1_gain, norm1_bias, b_up, b_down, norm2_gain, norm2_bias]
    )
    partner_big = partner(big, "section", 0)
    partner_small = partner(small, "section", 0)
    w_qkv, w_out, w_up, w_down = (
        assemble(own_part, partner_part, pair_half)
        for own_part, partner_part in zip(big, partner_big)
    )
    low_small = jnp.where(pair_half == 0, small, partner_small)
    high_small = jnp.where(pair_half == 0, partner_small, small)
    sizes = (768, 384, 384, 384, 1536, 384, 384, 384)
    smalls = []
    at = 0
    for size in sizes:
        smalls.append(jnp.concatenate([low_small[at : at + size], high_small[at : at + size]]))
        at += size
    qv_bias, b_out, norm1_gain, norm1_bias, b_up, b_down, norm2_gain, norm2_bias = smalls
    params = (
        w_qkv,
        qv_bias,
        w_out,
        b_out,
        norm1_gain,
        norm1_bias,
        w_up,
        b_up,
        w_down,
        b_down,
        norm2_gain,
        norm2_bias,
    )
    my_inputs = lax.dynamic_index_in_dim(inputs, pair_half, 0, keepdims=False)
    my_cotangent = lax.dynamic_index_in_dim(cotangent, pair_half, 0, keepdims=False)
    my_lengths = lax.dynamic_index_in_dim(lengths, pair_half, 0, keepdims=False)
    my_spans = lax.dynamic_index_in_dim(cdr_spans, pair_half, 0, keepdims=False)
    chain_rows, seq_len, model_width = my_inputs.shape
    positions = jnp.arange(seq_len, dtype=jnp.int32)
    key_valid = positions[None, :] < my_lengths[:, None]
    masked = (positions[None, :] >= my_spans[:, 0:1]) & (positions[None, :] < my_spans[:, 1:2])
    entered = jnp.where(masked[:, :, None], mask_vector[None, None, :], my_inputs)

    first_out, _ = forward_parts(entered, params, key_valid)
    received = lax.ppermute(first_out.astype(jnp.bfloat16), "section", [(0, 2), (1, 3)])
    layer_in = jnp.where(is_first, entered, received)
    output, kept_parts = forward_parts(layer_in, params, key_valid)
    layer_outputs = output.astype(jnp.bfloat16)[None]
    upper_grad, _ = layer_backward(layer_in, params, kept_parts, my_cotangent.astype(jnp.float32))
    returned = lax.ppermute(upper_grad.astype(jnp.bfloat16), "section", [(2, 0), (3, 1)])
    upstream = jnp.where(is_first, returned, my_cotangent).astype(jnp.float32)
    all_grads, layer_grads = layer_backward(layer_in, params, kept_parts, upstream)
    dropped = masked[:, :, None] & is_first
    input_grads = jnp.where(dropped, 0.0, all_grads).astype(jnp.bfloat16)[None]
    mask_term = jnp.sum(jnp.where(dropped, all_grads, 0.0), axis=(0, 1))

    (
        d_w_qkv,
        d_qv_bias,
        d_w_out,
        d_b_out,
        d_norm1_gain,
        d_norm1_bias,
        d_w_up,
        d_b_up,
        d_w_down,
        d_b_down,
        d_norm2_gain,
        d_norm2_bias,
    ) = layer_grads

    def pair_sum(tensor):
        low = tensor.astype(jnp.bfloat16)
        got = partner(take_half(low, 1 - pair_half), "section", 0)
        return add_low(take_half(low, pair_half), got)

    bits = own_bits()
    early = jnp.concatenate([pair_sum(d_w_down), fold(pair_sum(d_w_up))], axis=0)
    grads_small = (
        d_qv_bias,
        d_b_out,
        d_norm1_gain,
        d_norm1_bias,
        d_b_up,
        d_b_down,
        d_norm2_gain,
        d_norm2_bias,
    )
    own_small = jnp.concatenate([take_half(t, pair_half) for t in grads_small])
    other_small = jnp.concatenate([take_half(t, 1 - pair_half) for t in grads_small])
    summed_small = own_small + partner(other_small.astype(jnp.bfloat16), "section", 0).astype(
        jnp.float32
    )
    extra = jnp.concatenate(
        [
            summed_small.astype(jnp.bfloat16).reshape(6, 768),
            mask_term.astype(jnp.bfloat16)[None],
            jnp.zeros((9, 768), jnp.bfloat16),
        ],
        axis=0,
    )
    late = jnp.concatenate([pair_sum(d_w_out), fold(pair_sum(d_w_qkv))], axis=0)
    early, _ = reduce_rows(early, None, bits, pair_half)
    late, extra = reduce_rows(late, extra, bits, pair_half)
    mask_row = extra[6:7]
    mask_row = mask_row.astype(jnp.float32) + partner(mask_row, "section", 0).astype(jnp.float32)
    mask_low = mask_row.astype(jnp.bfloat16)
    mask_row = mask_row + partner(mask_low, "section", 1).astype(jnp.float32)
    mask_grad = mask_row.astype(jnp.bfloat16).astype(jnp.float32)[0]

    flat_small = extra[:6].reshape(-1).astype(jnp.float32)
    out_small = []
    at = 0
    for size in sizes:
        out_small.append(flat_small[at : at + size])
        at += size
    g_qv, g_bo, g_n1g, g_n1b, g_bu, g_bd, g_n2g, g_n2b = out_small
    g_down = early[:1536].astype(jnp.float32)
    g_up = unfold(early[1536:], 4).astype(jnp.float32)
    g_out = late[:384].astype(jnp.float32)
    g_qkv = unfold(late[384:], 3).astype(jnp.float32)
    return (
        layer_outputs,
        input_grads,
        mask_grad,
        g_qkv,
        g_qv,
        g_out,
        g_bo,
        g_n1g,
        g_n1b,
        g_up,
        g_bu,
        g_down,
        g_bd,
        g_n2g,
        g_n2b,
    )


def solution(mesh):
    in_specs = (
        P(None, "dp", None, None),
        P(None, "dp", None, None),
        P(None, "dp"),
        P(None, "dp", None),
        P(),
        P("section", None),
        P("section"),
        P("section", None),
        P("section"),
        P("section"),
        P("section"),
        P("section", None),
        P("section"),
        P("section", None),
        P("section"),
        P("section"),
        P("section"),
    )
    out_specs = (
        P("section", "dp", None, None),
        P("section", "dp", None, None),
        P(),
        P("section", None),
        P("section"),
        P("section", None),
        P("section"),
        P("section"),
        P("section"),
        P("section", None),
        P("section"),
        P("section", None),
        P("section"),
        P("section"),
        P("section"),
    )
    return jax.shard_map(
        per_device, mesh=mesh, in_specs=in_specs, out_specs=out_specs, check_vma=False
    )
```

```python
import functools
import math

import jax
import jax.numpy as jnp
from jax import lax
from jax.experimental import pallas as pl
from jax.experimental.pallas import tpu as pltpu
from jax.sharding import PartitionSpec as P

EPSILON = 1e-05
F32 = jnp.float32
LOW = jnp.bfloat16
WIDTH = 768
LENGTH = 160
ROWS = 320
HIDDEN = 3072
PAIRS = 6
TILE = 256
SCALE = 0.125
SIZES = (768, 384, 384, 384, 1536, 384, 384, 384)
QV, B_OUT, N1G, N1B, B_UP, B_DOWN, N2G, N2B = (sum(SIZES[:at]) for at in range(8))
SMALL = sum(SIZES)
VMEM_LIMIT = 56 * 1024 * 1024


def dot_nn(left_side, right_side):
    return jnp.dot(left_side, right_side, preferred_element_type=F32)


def dot_nt(left_side, right_side):
    return lax.dot_general(
        left_side, right_side, (((1,), (1,)), ((), ())), preferred_element_type=F32
    )


def dot_tn(left_side, right_side):
    return lax.dot_general(
        left_side, right_side, (((0,), (0,)), ((), ())), preferred_element_type=F32
    )


def columns(tile, width=TILE):
    return pl.ds(pl.multiple_of(tile * width, width), width)


def fetch(half, own, other, dest, sems):
    rows = own.shape[0]
    copies = (
        pltpu.make_async_copy(own, dest.at[pl.ds(half * rows, rows)], sems.at[0]),
        pltpu.make_async_copy(other, dest.at[pl.ds((1 - half) * rows, rows)], sems.at[1]),
    )
    for copy in copies:
        copy.start()
    return copies


def wait_all(copies):
    for copy in copies:
        copy.wait()


def whole(smalls, at, size):
    return jnp.concatenate([smalls[0:1, at : at + size], smalls[1:2, at : at + size]], axis=1)


def split_heads(tensor):
    lane = lax.broadcasted_iota(jnp.int32, tensor.shape, 1)
    zero = jnp.zeros_like(tensor)
    return jnp.concatenate(
        [jnp.where(lane < 64, tensor, zero), jnp.where(lane < 64, zero, tensor)], axis=0
    )


def join_heads(tensor):
    lane = lax.broadcasted_iota(jnp.int32, (LENGTH, 128), 1)
    return jnp.where(lane < 64, tensor[:LENGTH], tensor[LENGTH:])


def normalize(values):
    center = values - jnp.mean(values, axis=-1, keepdims=True)
    spread = jnp.mean(center * center, axis=-1, keepdims=True)
    inverse = lax.rsqrt(spread + EPSILON)
    return center * inverse, inverse


def normalize_back(upstream, gain, normal, inverse):
    scaled = upstream * gain
    first = jnp.mean(scaled, axis=-1, keepdims=True)
    second = jnp.mean(scaled * normal, axis=-1, keepdims=True)
    return inverse * (scaled - first - normal * second)


def gelu_parts(values):
    size = jnp.abs(values)
    below = 1.0 + (0.3275911 * math.sqrt(0.5)) * size
    t = pl.reciprocal(below, approx=True)
    t = t * (2.0 - below * t)
    series = t * (
        0.5 * 0.254829592
        + t
        * (
            0.5 * -0.284496736
            + t * (0.5 * 1.421413741 + t * (0.5 * -1.453152027 + t * (0.5 * 1.061405429)))
        )
    )
    bell = jnp.exp(-0.5 * values * values)
    tail = series * bell
    share = jnp.where(values >= 0.0, 1.0 - tail, tail)
    return values * share, share + values * bell * (1.0 / math.sqrt(2.0 * math.pi))


def attend_body(h, wqkv, wout, smalls, lens, qkv, probs, mixed, normal1, inverse1, u):
    x = h[...]
    for block, bias in ((0, smalls[0:1, QV : QV + 768]), (1, None), (2, smalls[1:2, QV : QV + 768])):
        for tile in range(3):
            at = block * WIDTH + tile * TILE
            part = dot_nn(x, wqkv[:, at : at + TILE])
            if bias is not None:
                part = part + bias[:, tile * TILE : (tile + 1) * TILE]
            qkv[:, at : at + TILE] = part.astype(LOW)

    def heads(index, carry):
        chain = index // PAIRS
        pair = index % PAIRS
        rows = pl.ds(pl.multiple_of(chain * LENGTH, LENGTH), LENGTH)
        q = qkv[rows, columns(pair, 128)]
        k = qkv[rows, columns(pair + PAIRS, 128)]
        v = qkv[rows, columns(pair + 2 * PAIRS, 128)]
        scores = dot_nt(split_heads(q), k) * SCALE
        key = lax.broadcasted_iota(jnp.int32, scores.shape, 1)
        scores = jnp.where(key < lens[chain], scores, -1000000000.0)
        grown = jnp.exp(scores - jnp.max(scores, axis=-1, keepdims=True))
        weights = (grown / jnp.sum(grown, axis=-1, keepdims=True)).astype(LOW)
        if probs is not None:
            probs[index] = weights
        mixed[rows, columns(pair, 128)] = join_heads(dot_nn(weights, v)).astype(LOW)
        return carry

    lax.fori_loop(0, 2 * PAIRS, heads, 0)
    branch = dot_nn(mixed[...], wout[...]) + whole(smalls, B_OUT, 384)
    normal, inverse = normalize(x.astype(F32) + branch)
    if normal1 is not None:
        normal1[...] = normal
        inverse1[...] = inverse
    u[...] = (normal * whole(smalls, N1G, 384) + whole(smalls, N1B, 384)).astype(LOW)


def feed_body(u, wup, wdown, smalls, slope, active, normal2, inverse2, y, total):
    x = u[...]
    total[...] = x.astype(F32) + whole(smalls, B_DOWN, 384)

    def step(tile, carry):
        place = columns(tile)
        bias = smalls[
            pl.ds(tile // 6, 1), pl.ds(pl.multiple_of(B_UP + (tile % 6) * TILE, 128), TILE)
        ]
        grown, tangent = gelu_parts(dot_nn(x, wup[:, place]) + bias)
        f = grown.astype(LOW)
        if slope is not None:
            slope[:, place] = tangent.astype(LOW)
            active[:, place] = f
        total[...] += dot_nn(f, wdown[place, :])
        return carry

    lax.fori_loop(0, HIDDEN // TILE, step, 0)
    normal, inverse = normalize(total[...])
    if normal2 is not None:
        normal2[...] = normal
        inverse2[...] = inverse
    y[...] = (normal * whole(smalls, N2G, 384) + whole(smalls, N2B, 384)).astype(LOW)


def put_halves(target, at, row):
    size = row.shape[1] // 2
    target[0:1, at : at + size] = row[:, :size]
    target[1:2, at : at + size] = row[:, size:]


def column_sum(values):
    return jnp.sum(values, axis=0, keepdims=True)


def feed_back_body(
    gy, wup, wdown, smalls, slope, normal1, inverse1, normal2, inverse2, gz, ga, gr1, gb, gsmall, total
):
    up = gy[...].astype(F32)
    normal = normal2[...]
    put_halves(gsmall, N2G, column_sum(up * normal))
    put_halves(gsmall, N2B, column_sum(up))
    grad = normalize_back(up, whole(smalls, N2G, 384), normal, inverse2[...])
    z = grad.astype(LOW)
    gz[...] = z
    put_halves(gsmall, B_DOWN, column_sum(z.astype(F32)))
    total[...] = grad

    def step(tile, carry):
        place = columns(tile)
        inner = dot_nt(z, wdown[place, :]) * slope[:, place].astype(F32)
        a = inner.astype(LOW)
        ga[:, place] = a
        gsmall[pl.ds(tile // 6, 1), pl.ds(pl.multiple_of(B_UP + (tile % 6) * TILE, 128), TILE)] = (
            column_sum(a.astype(F32))
        )
        total[...] += dot_nt(a, wup[:, place])
        return carry

    lax.fori_loop(0, HIDDEN // TILE, step, 0)
    up = total[...]
    normal = normal1[...]
    put_halves(gsmall, N1G, column_sum(up * normal))
    put_halves(gsmall, N1B, column_sum(up))
    grad = normalize_back(up, whole(smalls, N1G, 384), normal, inverse1[...])
    gr1[...] = grad
    b = grad.astype(LOW)
    gb[...] = b
    put_halves(gsmall, B_OUT, column_sum(b.astype(F32)))


def attend_back_body(gb, gr1, wqkv, wout, spans, first, qkv, probs, gqkv, gh, gqv, gmask, go):
    go[...] = dot_nt(gb[...], wout[...]).astype(LOW)

    def heads(index, carry):
        chain = index // PAIRS
        pair = index % PAIRS
        rows = pl.ds(pl.multiple_of(chain * LENGTH, LENGTH), LENGTH)
        q = split_heads(qkv[rows, columns(pair, 128)])
        k = qkv[rows, columns(pair + PAIRS, 128)]
        v = qkv[rows, columns(pair + 2 * PAIRS, 128)]
        g = split_heads(go[rows, columns(pair, 128)])
        weights = probs[index]
        wide = weights.astype(F32)
        inner = dot_nt(g, v)
        inner = wide * (inner - jnp.sum(wide * inner, axis=-1, keepdims=True))
        s = inner.astype(LOW)
        gqkv[rows, columns(pair, 128)] = (join_heads(dot_nn(s, k)) * SCALE).astype(LOW)
        gqkv[rows, columns(pair + PAIRS, 128)] = (dot_tn(s, q) * SCALE).astype(LOW)
        gqkv[rows, columns(pair + 2 * PAIRS, 128)] = dot_tn(weights, g).astype(LOW)
        return carry

    lax.fori_loop(0, 2 * PAIRS, heads, 0)
    gqv[0:1, :] = column_sum(gqkv[:, :WIDTH].astype(F32))
    gqv[1:2, :] = column_sum(gqkv[:, 2 * WIDTH :].astype(F32))
    full = gr1[...] + dot_nt(gqkv[...], wqkv[...])
    row = lax.broadcasted_iota(jnp.int32, (ROWS, 1), 0)
    dropped = row < 0
    for chain in range(2):
        start = spans[chain, 0] + chain * LENGTH
        end = spans[chain, 1] + chain * LENGTH
        dropped = dropped | ((row >= start) & (row < end))
    dropped = dropped & (first[0] > 0)
    zero = jnp.zeros_like(full)
    gh[...] = jnp.where(dropped, zero, full).astype(LOW)
    gmask[...] = column_sum(jnp.where(dropped, full, zero))


VMEM = pl.BlockSpec(memory_space=pltpu.VMEM)
SMEM = pl.BlockSpec(memory_space=pltpu.SMEM)
ANY = pl.BlockSpec(memory_space=pl.ANY)


def shape(dims, kind=LOW):
    return jax.ShapeDtypeStruct(dims, kind)


def kernel_call(body, ins, outs, scratch, flops, moved, name):
    return pl.pallas_call(
        body,
        in_specs=ins,
        out_specs=[VMEM] * len(outs),
        out_shape=outs,
        scratch_shapes=scratch,
        compiler_params=pltpu.CompilerParams(vmem_limit_bytes=VMEM_LIMIT),
        cost_estimate=pl.CostEstimate(flops=flops, bytes_accessed=moved, transcendentals=0),
        name=name,
    )


QKV_SHAPE = (ROWS, 3 * WIDTH)
PROBS_SHAPE = (2 * PAIRS, 2 * LENGTH, LENGTH)
ROW_SHAPE = (ROWS, WIDTH)
MACS = ROWS * WIDTH * WIDTH * 2


def attend(h, half, lens, weights, smalls, save):
    def body(h, half, lens, smalls, qo, qp, oo, op, *rest):
        if save:
            qkv, probs, mixed, normal1, inverse1, u, wqkv, wout, sems = rest
        else:
            u, qkv, mixed, wqkv, wout, sems = rest
            probs = normal1 = inverse1 = None
        first = fetch(half[0], qo, qp, wqkv, sems.at[0])
        second = fetch(half[0], oo, op, wout, sems.at[1])
        wait_all(first)
        wait_all(second)
        attend_body(h, wqkv, wout, smalls, lens, qkv, probs, mixed, normal1, inverse1, u)

    outs = [shape(ROW_SHAPE)]
    scratch = [
        pltpu.VMEM((WIDTH, 3 * WIDTH), LOW),
        pltpu.VMEM((WIDTH, WIDTH), LOW),
        pltpu.SemaphoreType.DMA((2, 2)),
    ]
    if save:
        outs = [
            shape(QKV_SHAPE),
            shape(PROBS_SHAPE),
            shape(ROW_SHAPE),
            shape(ROW_SHAPE, F32),
            shape((ROWS, 1), F32),
        ] + outs
    else:
        scratch = [pltpu.VMEM(QKV_SHAPE, LOW), pltpu.VMEM(ROW_SHAPE, LOW)] + scratch
    return kernel_call(
        body, [VMEM, SMEM, SMEM, VMEM] + [ANY] * 4, outs, scratch, 4 * MACS, 8000000, "attend"
    )(h, half, lens, smalls, *weights[0], *weights[1])


def feed(u, half, weights, smalls, save):
    def body(u, half, smalls, uo, up, do, dp, *rest):
        if save:
            slope, active, normal2, inverse2, y, total, wup, wdown, sems = rest
        else:
            y, total, wup, wdown, sems = rest
            slope = active = normal2 = inverse2 = None
        first = fetch(half[0], uo, up, wup, sems.at[0])
        second = fetch(half[0], do, dp, wdown, sems.at[1])
        wait_all(first)
        wait_all(second)
        feed_body(u, wup, wdown, smalls, slope, active, normal2, inverse2, y, total)

    outs = [shape(ROW_SHAPE)]
    scratch = [
        pltpu.VMEM(ROW_SHAPE, F32),
        pltpu.VMEM((WIDTH, HIDDEN), LOW),
        pltpu.VMEM((HIDDEN, WIDTH), LOW),
        pltpu.SemaphoreType.DMA((2, 2)),
    ]
    if save:
        outs = [
            shape((ROWS, HIDDEN)),
            shape((ROWS, HIDDEN)),
            shape(ROW_SHAPE, F32),
            shape((ROWS, 1), F32),
        ] + outs
    return kernel_call(
        body, [VMEM, SMEM, VMEM] + [ANY] * 4, outs, scratch, 8 * MACS, 14000000, "feed"
    )(u, half, smalls, *weights[2], *weights[3])


def feed_back(gy, half, weights, smalls, slope, normal1, inverse1, normal2, inverse2):
    def body(gy, half, smalls, uo, up, do, dp, slope, n1, i1, n2, i2, *rest):
        gz, ga, gr1, gb, gsmall, total, wup, wdown, sems = rest
        second = fetch(half[0], do, dp, wdown, sems.at[1])
        first = fetch(half[0], uo, up, wup, sems.at[0])
        wait_all(second)
        wait_all(first)
        feed_back_body(
            gy, wup, wdown, smalls, slope, n1, i1, n2, i2, gz, ga, gr1, gb, gsmall, total
        )

    outs = [
        shape(ROW_SHAPE),
        shape((ROWS, HIDDEN)),
        shape(ROW_SHAPE, F32),
        shape(ROW_SHAPE),
        shape((2, SMALL), F32),
    ]
    scratch = [
        pltpu.VMEM(ROW_SHAPE, F32),
        pltpu.VMEM((WIDTH, HIDDEN), LOW),
        pltpu.VMEM((HIDDEN, WIDTH), LOW),
        pltpu.SemaphoreType.DMA((2, 2)),
    ]
    return kernel_call(
        body,
        [VMEM, SMEM, VMEM] + [ANY] * 4 + [VMEM] * 5,
        outs,
        scratch,
        8 * MACS,
        18000000,
        "feed_back",
    )(
        gy,
        half,
        smalls,
        *weights[2],
        *weights[3],
        slope,
        normal1,
        inverse1,
        normal2,
        inverse2,
    )


def attend_back(gb, gr1, half, spans, first, weights, qkv, probs):
    def body(gb, gr1, half, spans, first, qo, qp, oo, op, qkv, probs, *rest):
        gqkv, gh, gqv, gmask, go, wqkv, wout, sems = rest
        second = fetch(half[0], oo, op, wout, sems.at[1])
        start = fetch(half[0], qo, qp, wqkv, sems.at[0])
        wait_all(second)
        wait_all(start)
        attend_back_body(gb, gr1, wqkv, wout, spans, first, qkv, probs, gqkv, gh, gqv, gmask, go)

    outs = [
        shape(QKV_SHAPE),
        shape(ROW_SHAPE),
        shape((2, WIDTH), F32),
        shape((1, WIDTH), F32),
    ]
    scratch = [
        pltpu.VMEM(ROW_SHAPE, LOW),
        pltpu.VMEM((WIDTH, 3 * WIDTH), LOW),
        pltpu.VMEM((WIDTH, WIDTH), LOW),
        pltpu.SemaphoreType.DMA((2, 2)),
    ]
    return kernel_call(
        body,
        [VMEM, VMEM, SMEM, SMEM, SMEM] + [ANY] * 4 + [VMEM] * 2,
        outs,
        scratch,
        4 * MACS,
        12000000,
        "attend_back",
    )(gb, gr1, half, spans, first, *weights[0], *weights[1], qkv, probs)


def partner(x, axis, bit):
    return lax.ppermute(x, axis, [(i, i ^ 1 << bit) for i in range(lax.axis_size(axis))])


def assemble(own_part, partner_part, pair_half):
    lower = jnp.where(pair_half == 0, own_part, partner_part)
    upper = jnp.where(pair_half == 0, partner_part, own_part)
    return jnp.concatenate([lower, upper], axis=0)


def take_half(tensor, which_half):
    half_rows = tensor.shape[0] // 2
    return lax.dynamic_slice_in_dim(tensor, which_half * half_rows, half_rows, 0)


ORDERS = (
    (("zw", "zu", "xw", "xu"), ("zu", "zw", "xu", "xw")),
    (("xw", "xu", "zw", "zu"), ("xu", "xw", "zu", "zw")),
)


def flip_dp(index, bit):
    z, x, y = index // 8, index // 2 % 4, index % 2
    if bit == "zw":
        z ^= 1
    elif bit == "zu":
        z ^= 3
    elif bit == "xw":
        x ^= 1
    elif bit == "xu":
        x ^= 3
    else:
        y ^= 1
    return z * 8 + x * 2 + y


def flip_pairs(bit_of_core):
    pairs = []
    for section in range(4):
        for index in range(32):
            pairs.append(
                (section * 32 + index, section * 32 + flip_dp(index, bit_of_core[section % 2]))
            )
    return pairs


def exchange(value, bit_of_core):
    return lax.ppermute(value, ("section", "dp"), flip_pairs(bit_of_core))


def own_bits():
    index = lax.axis_index("dp")
    z, x, y = index // 8, index // 2 % 4, index % 2
    return {
        "zu": z // 2,
        "zw": (z // 2) ^ (z % 2),
        "xu": x // 2,
        "xw": (x // 2) ^ (x % 2),
        "y": y,
    }


def own_bit(bits, core, part, step):
    return jnp.where(core == 0, bits[ORDERS[0][part][step]], bits[ORDERS[1][part][step]])


def add_low(left_side, right_side):
    return (left_side.astype(jnp.float32) + right_side.astype(jnp.float32)).astype(jnp.bfloat16)


def reduce_rows(pack, extra, bits, core):
    half = pack.shape[0] // 2
    parts = [pack[:half], pack[half:]]
    for step in range(4):
        for part in range(2):
            bit = own_bit(bits, core, part, step)
            rows = parts[part].shape[0] // 2
            keep = lax.dynamic_slice_in_dim(parts[part], bit * rows, rows, 0)
            send = lax.dynamic_slice_in_dim(parts[part], (1 - bit) * rows, rows, 0)
            flips = (ORDERS[0][part][step], ORDERS[1][part][step])
            if part == 0 and extra is not None:
                got = exchange(jnp.concatenate([send, extra], axis=0), flips)
                extra = add_low(extra, got[rows:])
                got = got[:rows]
            else:
                got = exchange(send, flips)
            parts[part] = add_low(keep, got)
    rows = parts[0].shape[0]
    both = jnp.concatenate(parts + ([extra] if extra is not None else []), axis=0)
    both = add_low(both, exchange(both, ("y", "y")))
    parts = [both[:rows], both[rows : 2 * rows]]
    if extra is not None:
        extra = both[2 * rows :]
    for step in reversed(range(4)):
        for part in range(2):
            bit = own_bit(bits, core, part, step)
            flips = (ORDERS[0][part][step], ORDERS[1][part][step])
            got = exchange(parts[part], flips)
            parts[part] = assemble(parts[part], got, bit)
    return jnp.concatenate(parts, axis=0), extra


def fold(tensor):
    return jnp.concatenate(
        [tensor[:, at : at + 768] for at in range(0, tensor.shape[1], 768)], axis=0
    )


def unfold(rows, count):
    return jnp.concatenate(jnp.split(rows, count, axis=0), axis=1)


def per_device(
    inputs,
    cotangent,
    lengths,
    cdr_spans,
    mask_vector,
    w_qkv,
    qv_bias,
    w_out,
    b_out,
    norm1_gain,
    norm1_bias,
    w_up,
    b_up,
    w_down,
    b_down,
    norm2_gain,
    norm2_bias,
):
    section_index = lax.axis_index("section")
    is_first = section_index < 2
    pair_half = section_index % 2
    half = pair_half.astype(jnp.int32).reshape(1)
    first = is_first.astype(jnp.int32).reshape(1)
    big = (w_qkv, w_out, w_up, w_down)
    small = jnp.concatenate(
        [qv_bias, b_out, norm1_gain, norm1_bias, b_up, b_down, norm2_gain, norm2_bias]
    )
    partner_small = partner(small, "section", 0)
    weights = [(tensor, partner(tensor, "section", 0)) for tensor in big]
    smalls = jnp.where(
        pair_half == 0,
        jnp.stack([small, partner_small]),
        jnp.stack([partner_small, small]),
    ).astype(F32)
    my_inputs = lax.dynamic_index_in_dim(inputs, pair_half, 0, keepdims=False)
    my_cotangent = lax.dynamic_index_in_dim(cotangent, pair_half, 0, keepdims=False)
    lens = lax.dynamic_index_in_dim(lengths, pair_half, 0, keepdims=False)
    spans = lax.dynamic_index_in_dim(cdr_spans, pair_half, 0, keepdims=False)
    positions = jnp.arange(LENGTH, dtype=jnp.int32)
    masked = (positions[None, :] >= spans[:, 0:1]) & (positions[None, :] < spans[:, 1:2])
    entered = jnp.where(masked[:, :, None], mask_vector[None, None, :], my_inputs)
    entered = entered.reshape(ROWS, WIDTH)
    my_cotangent = my_cotangent.reshape(ROWS, WIDTH)

    (u,) = attend(entered, half, lens, weights, smalls, False)
    (first_out,) = feed(u, half, weights, smalls, False)
    received = lax.ppermute(first_out, "section", [(0, 2), (1, 3)])
    layer_in = jnp.where(is_first, entered, received)
    qkv, probs, mixed, normal1, inverse1, u = attend(layer_in, half, lens, weights, smalls, True)
    slope, active, normal2, inverse2, output = feed(u, half, weights, smalls, True)

    def back(upstream):
        gz, ga, gr1, gb, gsmall = feed_back(
            upstream, half, weights, smalls, slope, normal1, inverse1, normal2, inverse2
        )
        gqkv, gh, gqv, gmask = attend_back(gb, gr1, half, spans, first, weights, qkv, probs)
        return gz, ga, gb, gsmall, gqkv, gh, gqv, gmask

    upper_grad = back(my_cotangent)[5]
    returned = lax.ppermute(upper_grad, "section", [(2, 0), (3, 1)])
    upstream = jnp.where(is_first, returned, my_cotangent)
    gz, ga, gb, gsmall, gqkv, gh, gqv, gmask = back(upstream)

    def pair_sum(left_side, right_side):
        low = dot_tn(left_side, right_side).astype(LOW)
        got = partner(take_half(low, 1 - pair_half), "section", 0)
        return add_low(take_half(low, pair_half), got)

    bits = own_bits()
    early = jnp.concatenate([pair_sum(active, gz), fold(pair_sum(u, ga))], axis=0)
    gsmall = jnp.concatenate([gqv, gsmall[:, WIDTH:]], axis=1)
    own_small = lax.dynamic_index_in_dim(gsmall, pair_half, 0, keepdims=False)
    other_small = lax.dynamic_index_in_dim(gsmall, 1 - pair_half, 0, keepdims=False)
    summed_small = own_small + partner(other_small.astype(LOW), "section", 0).astype(F32)
    extra = jnp.concatenate(
        [
            summed_small.astype(LOW).reshape(6, WIDTH),
            gmask.astype(LOW),
            jnp.zeros((9, WIDTH), LOW),
        ],
        axis=0,
    )
    late = jnp.concatenate([pair_sum(mixed, gb), fold(pair_sum(layer_in, gqkv))], axis=0)
    early, _ = reduce_rows(early, None, bits, pair_half)
    late, extra = reduce_rows(late, extra, bits, pair_half)
    mask_row = extra[6:7]
    mask_row = mask_row.astype(F32) + partner(mask_row, "section", 0).astype(F32)
    mask_low = mask_row.astype(LOW)
    mask_row = mask_low.astype(F32) + partner(mask_low, "section", 1).astype(F32)
    mask_grad = mask_row[0]

    flat_small = extra[:6].reshape(-1).astype(F32)
    out_small = []
    at = 0
    for size in SIZES:
        out_small.append(flat_small[at : at + size])
        at += size
    g_qv, g_bo, g_n1g, g_n1b, g_bu, g_bd, g_n2g, g_n2b = out_small
    return (
        output.reshape(1, 2, LENGTH, WIDTH),
        gh.reshape(1, 2, LENGTH, WIDTH),
        mask_grad,
        unfold(late[384:], 3).astype(F32),
        g_qv,
        late[:384].astype(F32),
        g_bo,
        g_n1g,
        g_n1b,
        unfold(early[1536:], 4).astype(F32),
        g_bu,
        early[:1536].astype(F32),
        g_bd,
        g_n2g,
        g_n2b,
    )


def solution(mesh):
    in_specs = (
        P(None, "dp", None, None),
        P(None, "dp", None, None),
        P(None, "dp"),
        P(None, "dp", None),
        P(),
        P("section", None),
        P("section"),
        P("section", None),
        P("section"),
        P("section"),
        P("section"),
        P("section", None),
        P("section"),
        P("section", None),
        P("section"),
        P("section"),
        P("section"),
    )
    out_specs = (
        P("section", "dp", None, None),
        P("section", "dp", None, None),
        P(),
        P("section", None),
        P("section"),
        P("section", None),
        P("section"),
        P("section"),
        P("section"),
        P("section", None),
        P("section"),
        P("section", None),
        P("section"),
        P("section"),
        P("section"),
    )
    return jax.shard_map(
        per_device, mesh=mesh, in_specs=in_specs, out_specs=out_specs, check_vma=False
    )
```

```python
import functools
import math

import jax
import jax.numpy as jnp
from jax import lax
from jax.experimental import pallas as pl
from jax.experimental.pallas import tpu as pltpu
from jax.sharding import PartitionSpec as P

EPSILON = 1e-05
F32 = jnp.float32
LOW = jnp.bfloat16
WIDTH = 768
LENGTH = 160
ROWS = 320
HIDDEN = 3072
PAIRS = 6
TILE = 256
SCALE = 0.125
SIZES = (768, 384, 384, 384, 1536, 384, 384, 384)
QV, B_OUT, N1G, N1B, B_UP, B_DOWN, N2G, N2B = (sum(SIZES[:at]) for at in range(8))
SMALL = sum(SIZES)
VMEM_LIMIT = 56 * 1024 * 1024


def dot_nn(left_side, right_side):
    return jnp.dot(left_side, right_side, preferred_element_type=F32)


def dot_nt(left_side, right_side):
    return lax.dot_general(
        left_side, right_side, (((1,), (1,)), ((), ())), preferred_element_type=F32
    )


def dot_tn(left_side, right_side):
    return lax.dot_general(
        left_side, right_side, (((0,), (0,)), ((), ())), preferred_element_type=F32
    )


def columns(tile, width=TILE):
    return pl.ds(pl.multiple_of(tile * width, width), width)


def fetch(half, own, other, dest, sems):
    rows = own.shape[0]
    copies = (
        pltpu.make_async_copy(own, dest.at[pl.ds(half * rows, rows)], sems.at[0]),
        pltpu.make_async_copy(other, dest.at[pl.ds((1 - half) * rows, rows)], sems.at[1]),
    )
    for copy in copies:
        copy.start()
    return copies


def wait_all(copies):
    for copy in copies:
        copy.wait()


def whole(smalls, at, size):
    return jnp.concatenate([smalls[0:1, at : at + size], smalls[1:2, at : at + size]], axis=1)


def split_heads(tensor):
    lane = lax.broadcasted_iota(jnp.int32, tensor.shape, 1)
    zero = jnp.zeros_like(tensor)
    return jnp.concatenate(
        [jnp.where(lane < 64, tensor, zero), jnp.where(lane < 64, zero, tensor)], axis=0
    )


def join_heads(tensor):
    lane = lax.broadcasted_iota(jnp.int32, (LENGTH, 128), 1)
    return jnp.where(lane < 64, tensor[:LENGTH], tensor[LENGTH:])


def normalize(values):
    center = values - jnp.mean(values, axis=-1, keepdims=True)
    spread = jnp.mean(center * center, axis=-1, keepdims=True)
    inverse = lax.rsqrt(spread + EPSILON)
    return center * inverse, inverse


def normalize_back(upstream, gain, normal, inverse):
    scaled = upstream * gain
    first = jnp.mean(scaled, axis=-1, keepdims=True)
    second = jnp.mean(scaled * normal, axis=-1, keepdims=True)
    return inverse * (scaled - first - normal * second)


def gelu_parts(values):
    size = jnp.abs(values)
    below = 1.0 + (0.3275911 * math.sqrt(0.5)) * size
    t = pl.reciprocal(below, approx=True)
    t = t * (2.0 - below * t)
    series = t * (
        0.5 * 0.254829592
        + t
        * (
            0.5 * -0.284496736
            + t * (0.5 * 1.421413741 + t * (0.5 * -1.453152027 + t * (0.5 * 1.061405429)))
        )
    )
    bell = jnp.exp(-0.5 * values * values)
    tail = series * bell
    share = jnp.where(values >= 0.0, 1.0 - tail, tail)
    return values * share, share + values * bell * (1.0 / math.sqrt(2.0 * math.pi))


def attend_body(h, wqkv, wout, smalls, lens, qkv, probs, mixed, normal1, inverse1, u):
    x = h[...]
    for block, bias in ((0, smalls[0:1, QV : QV + 768]), (1, None), (2, smalls[1:2, QV : QV + 768])):
        for tile in range(3):
            at = block * WIDTH + tile * TILE
            part = dot_nn(x, wqkv[:, at : at + TILE])
            if bias is not None:
                part = part + bias[:, tile * TILE : (tile + 1) * TILE]
            qkv[:, at : at + TILE] = part.astype(LOW)

    def heads(index, carry):
        chain = index // PAIRS
        pair = index % PAIRS
        rows = pl.ds(pl.multiple_of(chain * LENGTH, LENGTH), LENGTH)
        q = qkv[rows, columns(pair, 128)]
        k = qkv[rows, columns(pair + PAIRS, 128)]
        v = qkv[rows, columns(pair + 2 * PAIRS, 128)]
        scores = dot_nt(split_heads(q), k) * SCALE
        key = lax.broadcasted_iota(jnp.int32, scores.shape, 1)
        scores = jnp.where(key < lens[chain], scores, -1000000000.0)
        grown = jnp.exp(scores - jnp.max(scores, axis=-1, keepdims=True))
        weights = (grown / jnp.sum(grown, axis=-1, keepdims=True)).astype(LOW)
        if probs is not None:
            probs[index] = weights
        mixed[rows, columns(pair, 128)] = join_heads(dot_nn(weights, v)).astype(LOW)
        return carry

    lax.fori_loop(0, 2 * PAIRS, heads, 0)
    branch = dot_nn(mixed[...], wout[...]) + whole(smalls, B_OUT, 384)
    normal, inverse = normalize(x.astype(F32) + branch)
    if normal1 is not None:
        normal1[...] = normal
        inverse1[...] = inverse
    u[...] = (normal * whole(smalls, N1G, 384) + whole(smalls, N1B, 384)).astype(LOW)


def feed_body(u, wup, wdown, smalls, slope, active, normal2, inverse2, y, total):
    x = u[...]
    total[...] = x.astype(F32) + whole(smalls, B_DOWN, 384)

    def step(tile, carry):
        place = columns(tile)
        bias = smalls[
            pl.ds(tile // 6, 1), pl.ds(pl.multiple_of(B_UP + (tile % 6) * TILE, 128), TILE)
        ]
        grown, tangent = gelu_parts(dot_nn(x, wup[:, place]) + bias)
        f = grown.astype(LOW)
        if slope is not None:
            slope[:, place] = tangent.astype(LOW)
            active[:, place] = f
        total[...] += dot_nn(f, wdown[place, :])
        return carry

    lax.fori_loop(0, HIDDEN // TILE, step, 0)
    normal, inverse = normalize(total[...])
    if normal2 is not None:
        normal2[...] = normal
        inverse2[...] = inverse
    y[...] = (normal * whole(smalls, N2G, 384) + whole(smalls, N2B, 384)).astype(LOW)


def put_halves(target, at, row):
    size = row.shape[1] // 2
    target[0:1, at : at + size] = row[:, :size]
    target[1:2, at : at + size] = row[:, size:]


def column_sum(values):
    return jnp.sum(values, axis=0, keepdims=True)


def top_back_body(up, smalls, normal2, inverse2, gr2, gz, gsmall):
    normal = normal2[...]
    put_halves(gsmall, N2G, column_sum(up * normal))
    put_halves(gsmall, N2B, column_sum(up))
    grad = normalize_back(up, whole(smalls, N2G, 384), normal, inverse2[...])
    z = grad.astype(LOW)
    gz[...] = z
    put_halves(gsmall, B_DOWN, column_sum(z.astype(F32)))
    gr2[...] = grad


def feed_back_body(
    gr2, gz, wup, wdown, smalls, slope, normal1, inverse1, ga, gr1, gb, gsmall, total
):
    z = gz[...]
    total[...] = gr2[...]

    def step(tile, carry):
        place = columns(tile)
        inner = dot_nt(z, wdown[place, :]) * slope[:, place].astype(F32)
        a = inner.astype(LOW)
        ga[:, place] = a
        gsmall[pl.ds(tile // 6, 1), pl.ds(pl.multiple_of(B_UP + (tile % 6) * TILE, 128), TILE)] = (
            column_sum(a.astype(F32))
        )
        total[...] += dot_nt(a, wup[:, place])
        return carry

    lax.fori_loop(0, HIDDEN // TILE, step, 0)
    up = total[...]
    normal = normal1[...]
    put_halves(gsmall, N1G, column_sum(up * normal))
    put_halves(gsmall, N1B, column_sum(up))
    grad = normalize_back(up, whole(smalls, N1G, 384), normal, inverse1[...])
    gr1[...] = grad
    b = grad.astype(LOW)
    gb[...] = b
    put_halves(gsmall, B_OUT, column_sum(b.astype(F32)))


def span_rows(spans):
    row = lax.broadcasted_iota(jnp.int32, (ROWS, 1), 0)
    inside = row < 0
    for chain in range(2):
        start = spans[chain, 0] + chain * LENGTH
        end = spans[chain, 1] + chain * LENGTH
        inside = inside | ((row >= start) & (row < end))
    return inside


def pick_halves(half, own, other, smalls):
    low = half[0] == 0
    smalls[0:1, :] = jnp.where(low, own[...], other[...])
    smalls[1:2, :] = jnp.where(low, other[...], own[...])


def attend_back_body(gb, gr1, wqkv, wout, spans, first, qkv, probs, gqkv, gh, gqv, gmask, go):
    go[...] = dot_nt(gb[...], wout[...]).astype(LOW)

    def heads(index, carry):
        chain = index // PAIRS
        pair = index % PAIRS
        rows = pl.ds(pl.multiple_of(chain * LENGTH, LENGTH), LENGTH)
        q = split_heads(qkv[rows, columns(pair, 128)])
        k = qkv[rows, columns(pair + PAIRS, 128)]
        v = qkv[rows, columns(pair + 2 * PAIRS, 128)]
        g = split_heads(go[rows, columns(pair, 128)])
        weights = probs[index]
        wide = weights.astype(F32)
        inner = dot_nt(g, v)
        inner = wide * (inner - jnp.sum(wide * inner, axis=-1, keepdims=True))
        s = inner.astype(LOW)
        gqkv[rows, columns(pair, 128)] = (join_heads(dot_nn(s, k)) * SCALE).astype(LOW)
        gqkv[rows, columns(pair + PAIRS, 128)] = (dot_tn(s, q) * SCALE).astype(LOW)
        gqkv[rows, columns(pair + 2 * PAIRS, 128)] = dot_tn(weights, g).astype(LOW)
        return carry

    lax.fori_loop(0, 2 * PAIRS, heads, 0)
    gqv[0:1, :] = column_sum(gqkv[:, :WIDTH].astype(F32))
    gqv[1:2, :] = column_sum(gqkv[:, 2 * WIDTH :].astype(F32))
    full = gr1[...] + dot_nt(gqkv[...], wqkv[...])
    dropped = span_rows(spans) & (first[0] > 0)
    zero = jnp.zeros_like(full)
    gh[...] = jnp.where(dropped, zero, full).astype(LOW)
    gmask[...] = column_sum(jnp.where(dropped, full, zero))


VMEM = pl.BlockSpec(memory_space=pltpu.VMEM)
SMEM = pl.BlockSpec(memory_space=pltpu.SMEM)
ANY = pl.BlockSpec(memory_space=pl.ANY)


def shape(dims, kind=LOW):
    return jax.ShapeDtypeStruct(dims, kind)


def kernel_call(body, ins, outs, scratch, flops, moved, name):
    return pl.pallas_call(
        body,
        in_specs=ins,
        out_specs=[VMEM] * len(outs),
        out_shape=outs,
        scratch_shapes=scratch,
        compiler_params=pltpu.CompilerParams(vmem_limit_bytes=VMEM_LIMIT),
        cost_estimate=pl.CostEstimate(flops=flops, bytes_accessed=moved, transcendentals=0),
        name=name,
    )


QKV_SHAPE = (ROWS, 3 * WIDTH)
PROBS_SHAPE = (2 * PAIRS, 2 * LENGTH, LENGTH)
ROW_SHAPE = (ROWS, WIDTH)
MACS = ROWS * WIDTH * WIDTH * 2


SMALL_SCRATCH = pltpu.VMEM((2, SMALL), F32)


def pack_small(vectors):
    def body(*refs):
        at = 0
        for size, ref in zip(SIZES, refs):
            refs[-1][0:1, at : at + size] = ref[...].astype(F32)
            at += size

    return kernel_call(body, [VMEM] * 8, [shape((1, SMALL), F32)], [], 1000, 30000, "pack_small")(
        *[vector.reshape(1, -1) for vector in vectors]
    )[0]


def attend_first(inputs, half, lens, spans, mask_vector, weights, smalls):
    def body(x, half, lens, spans, mask, so, sp, qo, qp, oo, op, u, h, raw, small, qkv, mixed, wqkv, wout, sems):
        enter = pltpu.make_async_copy(x.at[half[0]], raw, sems.at[2, 0])
        enter.start()
        first = fetch(half[0], qo, qp, wqkv, sems.at[0])
        second = fetch(half[0], oo, op, wout, sems.at[1])
        pick_halves(half, so, sp, small)
        enter.wait()
        h[...] = jnp.where(span_rows(spans), mask[...], raw[...].reshape(ROWS, WIDTH))
        wait_all(first)
        wait_all(second)
        attend_body(h, wqkv, wout, small, lens, qkv, None, mixed, None, None, u)

    return kernel_call(
        body,
        [ANY, SMEM, SMEM, SMEM, VMEM, VMEM, VMEM] + [ANY] * 4,
        [shape(ROW_SHAPE), shape(ROW_SHAPE)],
        [
            pltpu.VMEM((2, LENGTH, WIDTH), LOW),
            SMALL_SCRATCH,
            pltpu.VMEM(QKV_SHAPE, LOW),
            pltpu.VMEM(ROW_SHAPE, LOW),
            pltpu.VMEM((WIDTH, 3 * WIDTH), LOW),
            pltpu.VMEM((WIDTH, WIDTH), LOW),
            pltpu.SemaphoreType.DMA((3, 2)),
        ],
        4 * MACS,
        8000000,
        "attend_first",
    )(inputs, half, lens, spans, mask_vector.reshape(1, WIDTH), *smalls, *weights[0], *weights[1])


def attend(h0, received, half, first, lens, weights, smalls):
    def body(h0, received, half, first, lens, so, sp, qo, qp, oo, op, *rest):
        h, qkv, probs, mixed, normal1, inverse1, u, small, wqkv, wout, sems = rest
        one = fetch(half[0], qo, qp, wqkv, sems.at[0])
        two = fetch(half[0], oo, op, wout, sems.at[1])
        pick_halves(half, so, sp, small)
        h[...] = jnp.where(first[0] > 0, h0[...], received[...])
        wait_all(one)
        wait_all(two)
        attend_body(h, wqkv, wout, small, lens, qkv, probs, mixed, normal1, inverse1, u)

    return kernel_call(
        body,
        [VMEM, VMEM, SMEM, SMEM, SMEM, VMEM, VMEM] + [ANY] * 4,
        [
            shape(ROW_SHAPE),
            shape(QKV_SHAPE),
            shape(PROBS_SHAPE),
            shape(ROW_SHAPE),
            shape(ROW_SHAPE, F32),
            shape((ROWS, 1), F32),
            shape(ROW_SHAPE),
        ],
        [
            SMALL_SCRATCH,
            pltpu.VMEM((WIDTH, 3 * WIDTH), LOW),
            pltpu.VMEM((WIDTH, WIDTH), LOW),
            pltpu.SemaphoreType.DMA((2, 2)),
        ],
        4 * MACS,
        8000000,
        "attend",
    )(h0, received, half, first, lens, *smalls, *weights[0], *weights[1])


FEED_SCRATCH = [
    SMALL_SCRATCH,
    pltpu.VMEM(ROW_SHAPE, F32),
    pltpu.VMEM((WIDTH, HIDDEN), LOW),
    pltpu.VMEM((HIDDEN, WIDTH), LOW),
    pltpu.SemaphoreType.DMA((2, 2)),
]


def feed(u, half, weights, smalls, save):
    def body(u, half, so, sp, uo, up, do, dp, *rest):
        if save:
            slope, active, normal2, inverse2, y, small, total, wup, wdown, sems = rest
        else:
            y, small, total, wup, wdown, sems = rest
            slope = active = normal2 = inverse2 = None
        first = fetch(half[0], uo, up, wup, sems.at[0])
        second = fetch(half[0], do, dp, wdown, sems.at[1])
        pick_halves(half, so, sp, small)
        wait_all(first)
        wait_all(second)
        feed_body(u, wup, wdown, small, slope, active, normal2, inverse2, y, total)

    outs = [shape(ROW_SHAPE)]
    if save:
        outs = [
            shape((ROWS, HIDDEN)),
            shape((ROWS, HIDDEN)),
            shape(ROW_SHAPE, F32),
            shape((ROWS, 1), F32),
        ] + outs
    return kernel_call(
        body, [VMEM, SMEM, VMEM, VMEM] + [ANY] * 4, outs, FEED_SCRATCH, 8 * MACS, 14000000, "feed"
    )(u, half, *smalls, *weights[2], *weights[3])


TOP_OUTS = [shape(ROW_SHAPE, F32), shape(ROW_SHAPE), shape((2, SMALL), F32)]


def top_back(cotangent, returned, half, first, smalls, normal2, inverse2):
    def body(cot, returned, half, first, so, sp, n2, i2, gr2, gz, gsmall, raw, small, sem):
        enter = pltpu.make_async_copy(cot.at[half[0]], raw, sem)
        enter.start()
        pick_halves(half, so, sp, small)
        enter.wait()
        up = raw[...].reshape(ROWS, WIDTH)
        if returned is not None:
            up = jnp.where(first[0] > 0, returned[...], up)
        top_back_body(up.astype(F32), small, n2, i2, gr2, gz, gsmall)

    scratch = [pltpu.VMEM((2, LENGTH, WIDTH), LOW), SMALL_SCRATCH, pltpu.SemaphoreType.DMA]
    if returned is None:
        return kernel_call(
            lambda cot, *rest: body(cot, None, *rest),
            [ANY, SMEM, SMEM, VMEM, VMEM, VMEM, VMEM],
            TOP_OUTS,
            scratch,
            1000000,
            4000000,
            "top_back",
        )(cotangent, half, first, *smalls, normal2, inverse2)
    return kernel_call(
        body,
        [ANY, VMEM, SMEM, SMEM, VMEM, VMEM, VMEM, VMEM],
        TOP_OUTS,
        scratch,
        1000000,
        4000000,
        "top_back",
    )(cotangent, returned, half, first, *smalls, normal2, inverse2)


def feed_back(gr2, gz, half, weights, smalls, slope, normal1, inverse1, after=()):
    def body(gr2, gz, half, so, sp, uo, up, do, dp, slope, n1, i1, *rest):
        ga, gr1, gb, gsmall, small, total, wup, wdown, sems = rest[len(after) :]
        second = fetch(half[0], do, dp, wdown, sems.at[1])
        first = fetch(half[0], uo, up, wup, sems.at[0])
        pick_halves(half, so, sp, small)
        wait_all(second)
        wait_all(first)
        feed_back_body(gr2, gz, wup, wdown, small, slope, n1, i1, ga, gr1, gb, gsmall, total)

    return kernel_call(
        body,
        [VMEM, VMEM, SMEM, VMEM, VMEM] + [ANY] * 4 + [VMEM] * 3 + [ANY] * len(after),
        [
            shape((ROWS, HIDDEN)),
            shape(ROW_SHAPE, F32),
            shape(ROW_SHAPE),
            shape((2, SMALL), F32),
        ],
        FEED_SCRATCH,
        8 * MACS,
        18000000,
        "feed_back",
    )(gr2, gz, half, *smalls, *weights[2], *weights[3], slope, normal1, inverse1, *after)


def attend_back(gb, gr1, half, spans, first, weights, qkv, probs, after=()):
    def body(gb, gr1, half, spans, first, qo, qp, oo, op, qkv, probs, *rest):
        gqkv, gh, gqv, gmask, go, wqkv, wout, sems = rest[len(after) :]
        second = fetch(half[0], oo, op, wout, sems.at[1])
        start = fetch(half[0], qo, qp, wqkv, sems.at[0])
        wait_all(second)
        wait_all(start)
        attend_back_body(gb, gr1, wqkv, wout, spans, first, qkv, probs, gqkv, gh, gqv, gmask, go)

    return kernel_call(
        body,
        [VMEM, VMEM, SMEM, SMEM, SMEM] + [ANY] * 4 + [VMEM] * 2 + [ANY] * len(after),
        [
            shape(QKV_SHAPE),
            shape(ROW_SHAPE),
            shape((2, WIDTH), F32),
            shape((1, WIDTH), F32),
        ],
        [
            pltpu.VMEM(ROW_SHAPE, LOW),
            pltpu.VMEM((WIDTH, 3 * WIDTH), LOW),
            pltpu.VMEM((WIDTH, WIDTH), LOW),
            pltpu.SemaphoreType.DMA((2, 2)),
        ],
        4 * MACS,
        12000000,
        "attend_back",
    )(gb, gr1, half, spans, first, *weights[0], *weights[1], qkv, probs, *after)


def partner(x, axis, bit):
    return lax.ppermute(x, axis, [(i, i ^ 1 << bit) for i in range(lax.axis_size(axis))])


Z_FIRST = ("zw", "zu", "xw", "xu")
Z_OTHER = ("zu", "zw", "xu", "xw")
X_FIRST = ("xw", "xu", "zw", "zu")
X_OTHER = ("xu", "xw", "zu", "zw")
ONE = (Z_FIRST, X_FIRST)
TWO = (Z_OTHER, X_OTHER)


def flip_dp(index, bit):
    z, x, y = index // 8, index // 2 % 4, index % 2
    if bit == "zw":
        z ^= 1
    elif bit == "zu":
        z ^= 3
    elif bit == "xw":
        x ^= 1
    elif bit == "xu":
        x ^= 3
    else:
        y ^= 1
    return z * 8 + x * 2 + y


def exchange(value, bit_of_core):
    pairs = []
    for section in range(4):
        for index in range(32):
            pairs.append(
                (section * 32 + index, section * 32 + flip_dp(index, bit_of_core[section % 2]))
            )
    return lax.ppermute(value, ("section", "dp"), pairs)


def own_bits():
    index = lax.axis_index("dp")
    z, x = index // 8, index // 2 % 4
    return {
        "zu": z // 2,
        "zw": (z // 2) ^ (z % 2),
        "xu": x // 2,
        "xw": (x // 2) ^ (x % 2),
    }


def add_low(left_side, right_side):
    return (left_side.astype(F32) + right_side.astype(F32)).astype(LOW)


class Chain:
    def __init__(self, value, orders, bits, core):
        self.value = value
        self.flips = [(orders[0][step], orders[1][step]) for step in range(4)]
        self.bits = [jnp.where(core == 0, bits[a], bits[b]) for a, b in self.flips]

    def halve(self, step):
        bit = self.bits[step]
        rows = self.value.shape[0] // 2
        keep = lax.dynamic_slice_in_dim(self.value, bit * rows, rows, 0)
        send = lax.dynamic_slice_in_dim(self.value, (1 - bit) * rows, rows, 0)
        self.value = add_low(keep, exchange(send, self.flips[step]))

    def across(self):
        self.value = add_low(self.value, exchange(self.value, ("y", "y")))

    def double(self, step):
        got = exchange(self.value, self.flips[step])
        bit = self.bits[step]
        lower = jnp.where(bit == 0, self.value, got)
        upper = jnp.where(bit == 0, got, self.value)
        self.value = jnp.concatenate([lower, upper], axis=0)

    def run(self):
        for step in range(4):
            self.halve(step)
        self.across()
        for step in (3, 2, 1, 0):
            self.double(step)
        return self.value


def per_device(
    inputs,
    cotangent,
    lengths,
    cdr_spans,
    mask_vector,
    w_qkv,
    qv_bias,
    w_out,
    b_out,
    norm1_gain,
    norm1_bias,
    w_up,
    b_up,
    w_down,
    b_down,
    norm2_gain,
    norm2_bias,
):
    section_index = lax.axis_index("section")
    core = section_index % 2
    half = core.astype(jnp.int32).reshape(1)
    first = (section_index < 2).astype(jnp.int32).reshape(1)
    weights = [(tensor, partner(tensor, "section", 0)) for tensor in (w_qkv, w_out, w_up, w_down)]
    small = pack_small(
        (qv_bias, b_out, norm1_gain, norm1_bias, b_up, b_down, norm2_gain, norm2_bias)
    )
    smalls = (small, partner(small, "section", 0))
    lens = lax.dynamic_index_in_dim(lengths, core, 0, keepdims=False)
    spans = lax.dynamic_index_in_dim(cdr_spans, core, 0, keepdims=False)

    u, h0 = attend_first(inputs, half, lens, spans, mask_vector, weights, smalls)
    (first_out,) = feed(u, half, weights, smalls, False)
    received = lax.ppermute(first_out, "section", [(0, 2), (1, 3)])
    h, qkv, probs, mixed, normal1, inverse1, u = attend(
        h0, received, half, first, lens, weights, smalls
    )
    slope, active, normal2, inverse2, output = feed(u, half, weights, smalls, True)
    gr2, gz, _ = top_back(cotangent, None, half, first, smalls, normal2, inverse2)
    _, gr1, gb, _ = feed_back(gr2, gz, half, weights, smalls, slope, normal1, inverse1)
    _, upper_grad, _, _ = attend_back(gb, gr1, half, spans, first, weights, qkv, probs)
    returned = lax.ppermute(upper_grad, "section", [(2, 0), (3, 1)])

    bits = own_bits()

    def columns_of(tensor, which):
        size = tensor.shape[1] // 2
        return lax.dynamic_slice_in_dim(tensor, which * size, size, 1)

    def weight_grad(left_side, right_side):
        other = dot_tn(columns_of(left_side, 1 - core), right_side).astype(LOW)
        got = partner(other, "section", 0)
        return (dot_tn(columns_of(left_side, core), right_side) + got.astype(F32)).astype(LOW)

    gr2, gz, top_small = top_back(cotangent, returned, half, first, smalls, normal2, inverse2)
    down = Chain(weight_grad(active, gz), ONE, bits, core)
    ga, gr1, gb, low_small = feed_back(
        gr2, gz, half, weights, smalls, slope, normal1, inverse1, (down.value,)
    )
    up = Chain(weight_grad(u, ga), TWO, bits, core)
    gqkv, gh, gqv, gmask = attend_back(
        gb, gr1, half, spans, first, weights, qkv, probs, (up.value,)
    )
    late_qkv = weight_grad(h, gqkv)
    late_out = weight_grad(mixed, gb)
    late_one = Chain(late_qkv[:, :1536], ONE, bits, core)
    gsmall = jnp.concatenate(
        [gqv, low_small[:, B_OUT:B_DOWN], top_small[:, B_DOWN:]], axis=1
    )
    own_small = lax.dynamic_index_in_dim(gsmall, core, 0, keepdims=False)
    other_small = lax.dynamic_index_in_dim(gsmall, 1 - core, 0, keepdims=False)
    summed_small = own_small + partner(other_small.astype(LOW), "section", 0).astype(F32)
    extra = jnp.concatenate(
        [
            summed_small.astype(LOW).reshape(6, WIDTH),
            gmask.astype(LOW),
            jnp.zeros((9, WIDTH), LOW),
        ],
        axis=0,
    )
    extra = jnp.concatenate([extra[:8], extra[8:]], axis=1)
    late_two = Chain(jnp.concatenate([late_qkv[:, 1536:], late_out], axis=1), TWO, bits, core)

    for step in range(4):
        late_one.halve(step)
        bit = late_two.bits[step]
        rows = late_two.value.shape[0] // 2
        keep = lax.dynamic_slice_in_dim(late_two.value, bit * rows, rows, 0)
        send = lax.dynamic_slice_in_dim(late_two.value, (1 - bit) * rows, rows, 0)
        got = exchange(jnp.concatenate([send, extra], axis=0), late_two.flips[step])
        extra = add_low(extra, got[rows:])
        late_two.value = add_low(keep, got[:rows])
    rows = late_one.value.shape[0]
    both = jnp.concatenate([late_one.value, late_two.value, extra], axis=0)
    both = add_low(both, exchange(both, ("y", "y")))
    late_one.value = both[:rows]
    late_two.value = both[rows : 2 * rows]
    extra = both[2 * rows :]
    for step in (3, 2, 1, 0):
        late_one.double(step)
        late_two.double(step)
    extra = jnp.concatenate([extra[:, :WIDTH], extra[:, WIDTH:]], axis=0)
    mask_row = extra[6:7]
    mask_row = mask_row.astype(F32) + partner(mask_row, "section", 0).astype(F32)
    mask_low = mask_row.astype(LOW)
    mask_row = mask_low.astype(F32) + partner(mask_low, "section", 1).astype(F32)
    mask_grad = mask_row[0]

    flat_small = extra[:6].reshape(-1).astype(F32)
    out_small = []
    at = 0
    for size in SIZES:
        out_small.append(flat_small[at : at + size])
        at += size
    g_qv, g_bo, g_n1g, g_n1b, g_bu, g_bd, g_n2g, g_n2b = out_small
    g_qkv = jnp.concatenate([late_one.value, late_two.value[:, :WIDTH]], axis=1)
    return (
        output.reshape(1, 2, LENGTH, WIDTH),
        gh.reshape(1, 2, LENGTH, WIDTH),
        mask_grad,
        g_qkv.astype(F32),
        g_qv,
        late_two.value[:, WIDTH:].astype(F32),
        g_bo,
        g_n1g,
        g_n1b,
        up.run().astype(F32),
        g_bu,
        down.run().astype(F32),
        g_bd,
        g_n2g,
        g_n2b,
    )


def solution(mesh):
    in_specs = (
        P(None, "dp", None, None),
        P(None, "dp", None, None),
        P(None, "dp"),
        P(None, "dp", None),
        P(),
        P("section", None),
        P("section"),
        P("section", None),
        P("section"),
        P("section"),
        P("section"),
        P("section", None),
        P("section"),
        P("section", None),
        P("section"),
        P("section"),
        P("section"),
    )
    out_specs = (
        P("section", "dp", None, None),
        P("section", "dp", None, None),
        P(),
        P("section", None),
        P("section"),
        P("section", None),
        P("section"),
        P("section"),
        P("section"),
        P("section", None),
        P("section"),
        P("section", None),
        P("section"),
        P("section"),
        P("section"),
    )
    return jax.shard_map(
        per_device, mesh=mesh, in_specs=in_specs, out_specs=out_specs, check_vma=False
    )
```

```python
import functools
import math

import jax
import jax.numpy as jnp
from jax import lax
from jax.experimental import pallas as pl
from jax.experimental.pallas import tpu as pltpu
from jax.sharding import PartitionSpec as P

EPSILON = 1e-05
F32 = jnp.float32
LOW = jnp.bfloat16
WIDTH = 768
LENGTH = 160
ROWS = 320
HIDDEN = 3072
PAIRS = 6
SCALE = 0.125
SIZES = (768, 384, 384, 384, 1536, 384, 384, 384)
QV, B_OUT, N1G, N1B, B_UP, B_DOWN, N2G, N2B = (sum(SIZES[:at]) for at in range(8))
SMALL = sum(SIZES)
VMEM_LIMIT = 58 * 1024 * 1024


def dot_nn(left_side, right_side):
    return jnp.dot(left_side, right_side, preferred_element_type=F32)


def dot_nt(left_side, right_side):
    return lax.dot_general(
        left_side, right_side, (((1,), (1,)), ((), ())), preferred_element_type=F32
    )


def dot_tn(left_side, right_side):
    return lax.dot_general(
        left_side, right_side, (((0,), (0,)), ((), ())), preferred_element_type=F32
    )


class Weight:
    def __init__(self, half, own, other, dest, sems):
        rows = own.shape[0]
        self.dest = dest
        self.copies = [
            pltpu.make_async_copy(own, dest.at[pl.ds(half * rows, rows)], sems.at[0]),
            pltpu.make_async_copy(other, dest.at[pl.ds((1 - half) * rows, rows)], sems.at[1]),
        ]
        for copy in self.copies:
            copy.start()

    def get(self):
        for copy in self.copies:
            copy.wait()
        self.copies = []
        return self.dest[...]


def whole(smalls, at, size):
    return jnp.concatenate([smalls[0:1, at : at + size], smalls[1:2, at : at + size]], axis=1)


def split_heads(tensor):
    lane = lax.broadcasted_iota(jnp.int32, tensor.shape, 1)
    zero = jnp.zeros_like(tensor)
    return jnp.concatenate(
        [jnp.where(lane < 64, tensor, zero), jnp.where(lane < 64, zero, tensor)], axis=0
    )


def join_heads(tensor):
    lane = lax.broadcasted_iota(jnp.int32, (LENGTH, 128), 1)
    return jnp.where(lane < 64, tensor[:LENGTH], tensor[LENGTH:])


def normalize(values):
    center = values - jnp.mean(values, axis=-1, keepdims=True)
    spread = jnp.mean(center * center, axis=-1, keepdims=True)
    inverse = lax.rsqrt(spread + EPSILON)
    return center * inverse, inverse


def normalize_back(upstream, gain, normal, inverse):
    scaled = upstream * gain
    first = jnp.mean(scaled, axis=-1, keepdims=True)
    second = jnp.mean(scaled * normal, axis=-1, keepdims=True)
    return inverse * (scaled - first - normal * second)


def gelu_parts(values):
    size = jnp.abs(values)
    below = 1.0 + (0.3275911 * math.sqrt(0.5)) * size
    t = pl.reciprocal(below, approx=True)
    t = t * (2.0 - below * t)
    series = t * (
        0.5 * 0.254829592
        + t
        * (
            0.5 * -0.284496736
            + t * (0.5 * 1.421413741 + t * (0.5 * -1.453152027 + t * (0.5 * 1.061405429)))
        )
    )
    bell = jnp.exp(-0.5 * values * values)
    tail = series * bell
    share = jnp.where(values >= 0.0, 1.0 - tail, tail)
    return values * share, share + values * bell * (1.0 / math.sqrt(2.0 * math.pi))


def column_sum(values):
    return jnp.sum(values, axis=0, keepdims=True)


def put_halves(target, at, row):
    size = row.shape[1] // 2
    target[0:1, at : at + size] = row[:, :size]
    target[1:2, at : at + size] = row[:, size:]


def places():
    for index in range(2 * PAIRS):
        chain, pair = divmod(index, PAIRS)
        rows = pl.ds(chain * LENGTH, LENGTH)
        yield index, chain, rows, [pl.ds((pair + block * PAIRS) * 128, 128) for block in range(3)]


def attend_body(h, wqkv, wout, smalls, lens, half, qkv, probs, mixed, normal1, inverse1, u):
    x = h[...]
    bias = jnp.concatenate(
        [smalls[0:1, :WIDTH], jnp.zeros((1, WIDTH), F32), smalls[1:2, :WIDTH]], axis=1
    )
    qkv[...] = (dot_nn(x, wqkv.get()) + bias).astype(LOW)
    for index, chain, rows, (at_q, at_k, at_v) in places():
        scores = dot_nt(split_heads(qkv[rows, at_q]), qkv[rows, at_k]) * SCALE
        key = lax.broadcasted_iota(jnp.int32, scores.shape, 1)
        scores = jnp.where(key < lens[half[0], chain], scores, -1000000000.0)
        grown = jnp.exp(scores - jnp.max(scores, axis=-1, keepdims=True))
        weights = (grown * (1.0 / jnp.sum(grown, axis=-1, keepdims=True))).astype(LOW)
        if probs is not None:
            probs[index] = weights
        mixed[rows, at_q] = join_heads(dot_nn(weights, qkv[rows, at_v])).astype(LOW)
    branch = dot_nn(mixed[...], wout.get()) + whole(smalls, B_OUT, 384)
    normal, inverse = normalize(x.astype(F32) + branch)
    if normal1 is not None:
        normal1[...] = normal
        inverse1[...] = inverse
    u[...] = (normal * whole(smalls, N1G, 384) + whole(smalls, N1B, 384)).astype(LOW)


CHUNK = 1024


def feed_body(u, wup, wdown, smalls, slope, active, normal2, inverse2, y):
    x = u[...]
    bias = whole(smalls, B_UP, 1536)
    up = wup.get()
    for at in range(0, HIDDEN, CHUNK):
        grown, tangent = gelu_parts(dot_nn(x, up[:, at : at + CHUNK]) + bias[:, at : at + CHUNK])
        active[:, at : at + CHUNK] = grown.astype(LOW)
        if slope is not None:
            slope[:, at : at + CHUNK] = tangent.astype(LOW)
    total = x.astype(F32) + whole(smalls, B_DOWN, 384) + dot_nn(active[...], wdown.get())
    normal, inverse = normalize(total)
    if normal2 is not None:
        normal2[...] = normal
        inverse2[...] = inverse
    y[...] = (normal * whole(smalls, N2G, 384) + whole(smalls, N2B, 384)).astype(LOW)


def feed_back_body(
    up, wup, wdown, smalls, slope, normal1, inverse1, normal2, inverse2, gz, ga, gr1, gb, gsmall
):
    normal = normal2[...]
    put_halves(gsmall, N2G, column_sum(up * normal))
    put_halves(gsmall, N2B, column_sum(up))
    grad = normalize_back(up, whole(smalls, N2G, 384), normal, inverse2[...])
    z = grad.astype(LOW)
    gz[...] = z
    put_halves(gsmall, B_DOWN, column_sum(z.astype(F32)))
    down = wdown.get()
    sums = []
    for at in range(0, HIDDEN, CHUNK):
        inner = dot_nt(z, down[at : at + CHUNK, :]) * slope[:, at : at + CHUNK].astype(F32)
        a = inner.astype(LOW)
        ga[:, at : at + CHUNK] = a
        sums.append(column_sum(a.astype(F32)))
    put_halves(gsmall, B_UP, jnp.concatenate(sums, axis=1))
    up = grad + dot_nt(ga[...], wup.get())
    normal = normal1[...]
    put_halves(gsmall, N1G, column_sum(up * normal))
    put_halves(gsmall, N1B, column_sum(up))
    grad = normalize_back(up, whole(smalls, N1G, 384), normal, inverse1[...])
    gr1[...] = grad
    b = grad.astype(LOW)
    gb[...] = b
    put_halves(gsmall, B_OUT, column_sum(b.astype(F32)))


def heads_back_body(gb, wout, qkv, probs, gqkv, gqv, go):
    go[...] = dot_nt(gb[...], wout.get()).astype(LOW)
    for index, chain, rows, (at_q, at_k, at_v) in places():
        k = qkv[rows, at_k]
        g = split_heads(go[rows, at_q])
        weights = probs[index]
        wide = weights.astype(F32)
        inner = dot_nt(g, qkv[rows, at_v])
        inner = wide * (inner - jnp.sum(wide * inner, axis=-1, keepdims=True))
        s = inner.astype(LOW)
        gqkv[rows, at_q] = (join_heads(dot_nn(s, k)) * SCALE).astype(LOW)
        gqkv[rows, at_k] = (dot_tn(s, split_heads(qkv[rows, at_q])) * SCALE).astype(LOW)
        gqkv[rows, at_v] = dot_tn(weights, g).astype(LOW)
    if gqv is not None:
        gqv[0:1, :] = column_sum(gqkv[:, :WIDTH].astype(F32))
        gqv[1:2, :] = column_sum(gqkv[:, 2 * WIDTH :].astype(F32))


def span_rows(spans, half):
    row = lax.broadcasted_iota(jnp.int32, (ROWS, 1), 0)
    inside = row < 0
    for chain in range(2):
        start = spans[half[0], chain, 0] + chain * LENGTH
        end = spans[half[0], chain, 1] + chain * LENGTH
        inside = inside | ((row >= start) & (row < end))
    return inside


def pick_halves(half, own, other, smalls):
    low = half[0] == 0
    smalls[0:1, :] = jnp.where(low, own[:, :SMALL], other[:, :SMALL])
    smalls[1:2, :] = jnp.where(low, other[:, :SMALL], own[:, :SMALL])


VMEM = pl.BlockSpec(memory_space=pltpu.VMEM)
SMEM = pl.BlockSpec(memory_space=pltpu.SMEM)
ANY = pl.BlockSpec(memory_space=pl.ANY)
SMALL_SCRATCH = pltpu.VMEM((2, SMALL), F32)
QKV_SHAPE = (ROWS, 3 * WIDTH)
PROBS_SHAPE = (2 * PAIRS, 2 * LENGTH, LENGTH)
ROW_SHAPE = (ROWS, WIDTH)
FEED_SHAPE = (ROWS, HIDDEN)
MACS = ROWS * WIDTH * WIDTH * 2
ATTEND_WEIGHTS = [pltpu.VMEM((WIDTH, 3 * WIDTH), LOW), pltpu.VMEM((WIDTH, WIDTH), LOW)]
FEED_WEIGHTS = [pltpu.VMEM((WIDTH, HIDDEN), LOW), pltpu.VMEM((HIDDEN, WIDTH), LOW)]


def shape(dims, kind=LOW):
    return jax.ShapeDtypeStruct(dims, kind)


def kernel_call(body, ins, outs, scratch, flops, moved, name, out_specs=None):
    return pl.pallas_call(
        body,
        in_specs=ins,
        out_specs=out_specs or [VMEM] * len(outs),
        out_shape=outs,
        scratch_shapes=scratch,
        compiler_params=pltpu.CompilerParams(vmem_limit_bytes=VMEM_LIMIT),
        cost_estimate=pl.CostEstimate(flops=flops, bytes_accessed=moved, transcendentals=0),
        name=name,
    )


def attend_first(inputs, half, lens, spans, weights, smalls):
    def body(x, half, lens, spans, so, sp, qo, qp, oo, op, u, h, raw, small, qkv, mixed, wq, wo, sems):
        enter = pltpu.make_async_copy(x.at[half[0]], raw, sems.at[2, 0])
        enter.start()
        wqkv = Weight(half[0], qo, qp, wq, sems.at[0])
        wout = Weight(half[0], oo, op, wo, sems.at[1])
        pick_halves(half, so, sp, small)
        enter.wait()
        mask = so[:, SMALL:].astype(LOW)
        h[...] = jnp.where(span_rows(spans, half), mask, raw[...].reshape(ROWS, WIDTH))
        attend_body(h, wqkv, wout, small, lens, half, qkv, None, mixed, None, None, u)

    return kernel_call(
        body,
        [ANY, SMEM, SMEM, SMEM, VMEM, VMEM] + [ANY] * 4,
        [shape(ROW_SHAPE), shape(ROW_SHAPE)],
        [
            pltpu.VMEM((2, LENGTH, WIDTH), LOW),
            SMALL_SCRATCH,
            pltpu.VMEM(QKV_SHAPE, LOW),
            pltpu.VMEM(ROW_SHAPE, LOW),
            *ATTEND_WEIGHTS,
            pltpu.SemaphoreType.DMA((3, 2)),
        ],
        4 * MACS,
        8000000,
        "attend_first",
    )(inputs, half, lens, spans, *smalls, *weights[0], *weights[1])


def feed_first(u, half, weights, smalls):
    def body(u, half, so, sp, uo, up, do, dp, y, small, active, wu, wd, sems):
        wup = Weight(half[0], uo, up, wu, sems.at[0])
        wdown = Weight(half[0], do, dp, wd, sems.at[1])
        pick_halves(half, so, sp, small)
        feed_body(u, wup, wdown, small, None, active, None, None, y)

    return kernel_call(
        body,
        [VMEM, SMEM, VMEM, VMEM] + [ANY] * 4,
        [shape(ROW_SHAPE)],
        [
            SMALL_SCRATCH,
            pltpu.VMEM(FEED_SHAPE, LOW),
            *FEED_WEIGHTS,
            pltpu.SemaphoreType.DMA((2, 2)),
        ],
        8 * MACS,
        14000000,
        "feed_first",
    )(u, half, *smalls, *weights[2], *weights[3])[0]


KEPT = [
    shape(ROW_SHAPE),
    shape(QKV_SHAPE),
    shape(PROBS_SHAPE),
    shape(ROW_SHAPE),
    shape(ROW_SHAPE, F32),
    shape((ROWS, 1), F32),
    shape(ROW_SHAPE),
    shape(FEED_SHAPE),
    shape(FEED_SHAPE),
    shape(ROW_SHAPE, F32),
    shape((ROWS, 1), F32),
    shape(ROW_SHAPE),
]


def middle(h0, received, cotangent, half, first, lens, weights, smalls):
    def body(h0, received, cot, half, first, lens, so, sp, qo, qp, oo, op, uo, up, do, dp, *rest):
        outs, rest = rest[: len(KEPT)], rest[len(KEPT) :]
        gh, small, gz, ga, gr1, gb, gsmall, gqkv, go, raw, wq, wo, wu, wd = rest[:14]
        keeps, sems, out_sems, raw_sem = rest[14:-3], *rest[-3:]
        h, qkv, probs, mixed, normal1, inverse1, u, slope, active, normal2, inverse2, y = keeps
        wqkv = Weight(half[0], qo, qp, wq, sems.at[0])
        wout = Weight(half[0], oo, op, wo, sems.at[1])
        wup = Weight(half[0], uo, up, wu, sems.at[2])
        wdown = Weight(half[0], do, dp, wd, sems.at[3])
        enter = pltpu.make_async_copy(cot.at[half[0]], raw, raw_sem)
        enter.start()
        pick_halves(half, so, sp, small)
        leaving = []

        def leave(places):
            for place in places:
                copy = pltpu.make_async_copy(keeps[place], outs[place], out_sems.at[place])
                copy.start()
                leaving.append(copy)

        h[...] = jnp.where(first[0] > 0, h0[...], received[...])
        attend_body(h, wqkv, wout, small, lens, half, qkv, probs, mixed, normal1, inverse1, u)
        leave(range(7))
        feed_body(u, wup, wdown, small, slope, active, normal2, inverse2, y)
        leave(range(7, 12))
        enter.wait()
        upstream = raw[...].reshape(ROWS, WIDTH).astype(F32)
        feed_back_body(
            upstream, wup, wdown, small, slope, normal1, inverse1, normal2, inverse2, gz, ga, gr1, gb, gsmall
        )
        heads_back_body(gb, wout, qkv, probs, gqkv, None, go)
        gh[...] = (gr1[...] + dot_nt(gqkv[...], wqkv.get())).astype(LOW)
        for copy in leaving:
            copy.wait()

    return kernel_call(
        body,
        [VMEM, VMEM, ANY, SMEM, SMEM, SMEM, VMEM, VMEM] + [ANY] * 8,
        KEPT + [shape(ROW_SHAPE)],
        [
            SMALL_SCRATCH,
            pltpu.VMEM(ROW_SHAPE, LOW),
            pltpu.VMEM(FEED_SHAPE, LOW),
            pltpu.VMEM(ROW_SHAPE, F32),
            pltpu.VMEM(ROW_SHAPE, LOW),
            SMALL_SCRATCH,
            pltpu.VMEM(QKV_SHAPE, LOW),
            pltpu.VMEM(ROW_SHAPE, LOW),
            pltpu.VMEM((2, LENGTH, WIDTH), LOW),
            *ATTEND_WEIGHTS,
            *FEED_WEIGHTS,
            *[pltpu.VMEM(kept.shape, kept.dtype) for kept in KEPT],
            pltpu.SemaphoreType.DMA((4, 2)),
            pltpu.SemaphoreType.DMA((len(KEPT),)),
            pltpu.SemaphoreType.DMA,
        ],
        24 * MACS,
        45000000,
        "middle",
        [ANY] * len(KEPT) + [VMEM],
    )(
        h0, received, cotangent, half, first, lens, *smalls,
        *weights[0], *weights[1], *weights[2], *weights[3],
    )


def back_feed(cotangent, returned, half, first, weights, smalls, slope, n1, i1, n2, i2):
    def body(cot, returned, half, first, so, sp, uo, up, do, dp, slope, n1, i1, n2, i2, *rest):
        gz, ga, gr1, gb, gsmall, small, raw, wu, wd, sems = rest
        enter = pltpu.make_async_copy(cot.at[half[0]], raw, sems.at[2, 0])
        enter.start()
        wdown = Weight(half[0], do, dp, wd, sems.at[1])
        wup = Weight(half[0], uo, up, wu, sems.at[0])
        pick_halves(half, so, sp, small)
        enter.wait()
        upstream = jnp.where(first[0] > 0, returned[...], raw[...].reshape(ROWS, WIDTH))
        feed_back_body(
            upstream.astype(F32), wup, wdown, small, slope, n1, i1, n2, i2, gz, ga, gr1, gb, gsmall
        )

    return kernel_call(
        body,
        [ANY, VMEM, SMEM, SMEM, VMEM, VMEM] + [ANY] * 4 + [VMEM] * 5,
        [
            shape(ROW_SHAPE),
            shape(FEED_SHAPE),
            shape(ROW_SHAPE, F32),
            shape(ROW_SHAPE),
            shape((2, SMALL), F32),
        ],
        [
            SMALL_SCRATCH,
            pltpu.VMEM((2, LENGTH, WIDTH), LOW),
            *FEED_WEIGHTS,
            pltpu.SemaphoreType.DMA((3, 2)),
        ],
        8 * MACS,
        18000000,
        "back_feed",
    )(cotangent, returned, half, first, *smalls, *weights[2], *weights[3], slope, n1, i1, n2, i2)


def back_heads(gb, half, weights, qkv, probs, after=()):
    def body(gb, half, oo, op, qkv, probs, *rest):
        gqkv, gqv, go, wo, sems = rest[len(after) :]
        wout = Weight(half[0], oo, op, wo, sems)
        heads_back_body(gb, wout, qkv, probs, gqkv, gqv, go)

    return kernel_call(
        body,
        [VMEM, SMEM] + [ANY] * 2 + [VMEM] * 2 + [ANY] * len(after),
        [shape(QKV_SHAPE), shape((2, WIDTH), F32)],
        [pltpu.VMEM(ROW_SHAPE, LOW), ATTEND_WEIGHTS[1], pltpu.SemaphoreType.DMA((2,))],
        2 * MACS,
        8000000,
        "back_heads",
    )(gb, half, *weights[1], qkv, probs, *after)


def back_input(gqkv, gr1, half, first, spans, weights, after=()):
    def body(gqkv, gr1, half, first, spans, qo, qp, *rest):
        gh, gmask, wq, sems = rest[len(after) :]
        wqkv = Weight(half[0], qo, qp, wq, sems)
        full = gr1[...] + dot_nt(gqkv[...], wqkv.get())
        dropped = span_rows(spans, half) & (first[0] > 0)
        zero = jnp.zeros_like(full)
        gh[...] = jnp.where(dropped, zero, full).astype(LOW)
        gmask[...] = column_sum(jnp.where(dropped, full, zero))

    return kernel_call(
        body,
        [VMEM, VMEM, SMEM, SMEM, SMEM] + [ANY] * (2 + len(after)),
        [shape(ROW_SHAPE), shape((1, WIDTH), F32)],
        [ATTEND_WEIGHTS[0], pltpu.SemaphoreType.DMA((2,))],
        3 * MACS,
        6000000,
        "back_input",
    )(gqkv, gr1, half, first, spans, *weights[0], *after)


def partner(x, axis, bit):
    return lax.ppermute(x, axis, [(i, i ^ 1 << bit) for i in range(lax.axis_size(axis))])


Z_FIRST = ("zw", "zu", "xw", "xu")
Z_OTHER = ("zu", "zw", "xu", "xw")
X_FIRST = ("xw", "xu", "zw", "zu")
X_OTHER = ("xu", "xw", "zu", "zw")
ONE = (Z_FIRST, X_FIRST)
TWO = (Z_OTHER, X_OTHER)


def flip_dp(index, bit):
    z, x, y = index // 8, index // 2 % 4, index % 2
    if bit == "zw":
        z ^= 1
    elif bit == "zu":
        z ^= 3
    elif bit == "xw":
        x ^= 1
    elif bit == "xu":
        x ^= 3
    else:
        y ^= 1
    return z * 8 + x * 2 + y


def exchange(value, bit_of_core):
    pairs = []
    for section in range(4):
        for index in range(32):
            pairs.append(
                (section * 32 + index, section * 32 + flip_dp(index, bit_of_core[section % 2]))
            )
    return lax.ppermute(value, ("section", "dp"), pairs)


def own_bits():
    index = lax.axis_index("dp")
    z, x = index // 8, index // 2 % 4
    return {
        "zu": z // 2,
        "zw": (z // 2) ^ (z % 2),
        "xu": x // 2,
        "xw": (x // 2) ^ (x % 2),
    }


def add_low(left_side, right_side):
    return (left_side.astype(F32) + right_side.astype(F32)).astype(LOW)


class Chain:
    def __init__(self, value, orders, bits, core):
        self.value = value
        self.flips = [(orders[0][step], orders[1][step]) for step in range(4)]
        self.bits = [jnp.where(core == 0, bits[a], bits[b]) for a, b in self.flips]

    def halve(self, step):
        bit = self.bits[step]
        rows = self.value.shape[0] // 2
        keep = lax.dynamic_slice_in_dim(self.value, bit * rows, rows, 0)
        send = lax.dynamic_slice_in_dim(self.value, (1 - bit) * rows, rows, 0)
        self.value = add_low(keep, exchange(send, self.flips[step]))

    def across(self):
        self.value = add_low(self.value, exchange(self.value, ("y", "y")))

    def double(self, step):
        got = exchange(self.value, self.flips[step])
        bit = self.bits[step]
        lower = jnp.where(bit == 0, self.value, got)
        upper = jnp.where(bit == 0, got, self.value)
        self.value = jnp.concatenate([lower, upper], axis=0)

    def run(self):
        for step in range(4):
            self.halve(step)
        self.across()
        for step in (3, 2, 1, 0):
            self.double(step)
        return self.value


def pack_vectors(vectors):
    size = sum(vector.shape[0] for vector in vectors)
    total = jnp.zeros((size,), F32)
    at = 0
    for vector in vectors:
        total = total + jnp.pad(vector.astype(F32), (at, size - at - vector.shape[0]))
        at += vector.shape[0]
    return total.reshape(1, size)


def per_device(
    inputs,
    cotangent,
    lengths,
    cdr_spans,
    mask_vector,
    w_qkv,
    qv_bias,
    w_out,
    b_out,
    norm1_gain,
    norm1_bias,
    w_up,
    b_up,
    w_down,
    b_down,
    norm2_gain,
    norm2_bias,
):
    section_index = lax.axis_index("section")
    core = section_index % 2
    half = core.astype(jnp.int32).reshape(1)
    first = (section_index < 2).astype(jnp.int32).reshape(1)
    small = pack_vectors(
        (
            qv_bias,
            b_out,
            norm1_gain,
            norm1_bias,
            b_up,
            b_down,
            norm2_gain,
            norm2_bias,
            mask_vector,
        )
    )
    smalls = (small, partner(small, "section", 0))
    weights = [(tensor, partner(tensor, "section", 0)) for tensor in (w_qkv, w_out, w_up, w_down)]

    u, h0 = attend_first(inputs, half, lengths, cdr_spans, weights, smalls)
    first_out = feed_first(u, half, weights, smalls)
    received = lax.ppermute(first_out, "section", [(0, 2), (1, 3)])
    kept = middle(h0, received, cotangent, half, first, lengths, weights, smalls)
    h, qkv, probs, mixed, normal1, inverse1, u, slope, active, normal2, inverse2, output = kept[:12]
    returned = lax.ppermute(kept[12], "section", [(2, 0), (3, 1)])

    bits = own_bits()

    def columns_of(tensor, which):
        size = tensor.shape[1] // 2
        return lax.dynamic_slice_in_dim(tensor, which * size, size, 1)

    def weight_grad(left_side, right_side):
        other = dot_tn(columns_of(left_side, 1 - core), right_side).astype(LOW)
        got = partner(other, "section", 0)
        return (dot_tn(columns_of(left_side, core), right_side) + got.astype(F32)).astype(LOW)

    gz, ga, gr1, gb, gsmall = back_feed(
        cotangent, returned, half, first, weights, smalls, slope, normal1, inverse1, normal2, inverse2
    )
    down = Chain(weight_grad(active, gz), ONE, bits, core)
    up = Chain(weight_grad(u, ga), TWO, bits, core)
    gqkv, gqv = back_heads(gb, half, weights, qkv, probs, (down.value, up.value))
    late_qkv = weight_grad(h, gqkv)
    late_out = weight_grad(mixed, gb)
    gh, gmask = back_input(gqkv, gr1, half, first, cdr_spans, weights, (late_qkv, late_out))
    late_one = Chain(late_qkv[:, :1536], ONE, bits, core)
    gsmall = jnp.concatenate([gqv, gsmall[:, WIDTH:]], axis=1)
    own_small = lax.dynamic_index_in_dim(gsmall, core, 0, keepdims=False)
    other_small = lax.dynamic_index_in_dim(gsmall, 1 - core, 0, keepdims=False)
    summed_small = own_small + partner(other_small.astype(LOW), "section", 0).astype(F32)
    extra = jnp.concatenate(
        [
            summed_small.astype(LOW).reshape(6, WIDTH),
            gmask.astype(LOW),
            jnp.zeros((9, WIDTH), LOW),
        ],
        axis=0,
    )
    extra = jnp.concatenate([extra[:8], extra[8:]], axis=1)
    late_two = Chain(jnp.concatenate([late_qkv[:, 1536:], late_out], axis=1), TWO, bits, core)

    for step in range(4):
        late_one.halve(step)
        bit = late_two.bits[step]
        rows = late_two.value.shape[0] // 2
        keep = lax.dynamic_slice_in_dim(late_two.value, bit * rows, rows, 0)
        send = lax.dynamic_slice_in_dim(late_two.value, (1 - bit) * rows, rows, 0)
        got = exchange(jnp.concatenate([send, extra], axis=0), late_two.flips[step])
        extra = add_low(extra, got[rows:])
        late_two.value = add_low(keep, got[:rows])
    rows = late_one.value.shape[0]
    both = jnp.concatenate([late_one.value, late_two.value, extra], axis=0)
    both = add_low(both, exchange(both, ("y", "y")))
    late_one.value = both[:rows]
    late_two.value = both[rows : 2 * rows]
    extra = both[2 * rows :]
    for step in (3, 2, 1, 0):
        late_one.double(step)
        late_two.double(step)
    extra = jnp.concatenate([extra[:, :WIDTH], extra[:, WIDTH:]], axis=0)
    mask_row = extra[6:7]
    mask_row = mask_row.astype(F32) + partner(mask_row, "section", 0).astype(F32)
    mask_low = mask_row.astype(LOW)
    mask_row = mask_low.astype(F32) + partner(mask_low, "section", 1).astype(F32)
    mask_grad = mask_row[0]

    flat_small = extra[:6].reshape(-1).astype(F32)
    out_small = []
    at = 0
    for size in SIZES:
        out_small.append(flat_small[at : at + size])
        at += size
    g_qv, g_bo, g_n1g, g_n1b, g_bu, g_bd, g_n2g, g_n2b = out_small
    g_qkv = jnp.concatenate([late_one.value, late_two.value[:, :WIDTH]], axis=1)
    return (
        output.reshape(1, 2, LENGTH, WIDTH),
        gh.reshape(1, 2, LENGTH, WIDTH),
        mask_grad,
        g_qkv.astype(F32),
        g_qv,
        late_two.value[:, WIDTH:].astype(F32),
        g_bo,
        g_n1g,
        g_n1b,
        up.run().astype(F32),
        g_bu,
        down.run().astype(F32),
        g_bd,
        g_n2g,
        g_n2b,
    )


def solution(mesh):
    in_specs = (
        P(None, "dp", None, None),
        P(None, "dp", None, None),
        P(None, "dp"),
        P(None, "dp", None),
        P(),
        P("section", None),
        P("section"),
        P("section", None),
        P("section"),
        P("section"),
        P("section"),
        P("section", None),
        P("section"),
        P("section", None),
        P("section"),
        P("section"),
        P("section"),
    )
    out_specs = (
        P("section", "dp", None, None),
        P("section", "dp", None, None),
        P(),
        P("section", None),
        P("section"),
        P("section", None),
        P("section"),
        P("section"),
        P("section"),
        P("section", None),
        P("section"),
        P("section", None),
        P("section"),
        P("section"),
        P("section"),
    )
    return jax.shard_map(
        per_device, mesh=mesh, in_specs=in_specs, out_specs=out_specs, check_vma=False
    )
```

```python
import functools
import math

import jax
import jax.numpy as jnp
from jax import lax
from jax.experimental import pallas as pl
from jax.experimental.pallas import tpu as pltpu
from jax.sharding import PartitionSpec as P

EPSILON = 1e-05
F32 = jnp.float32
LOW = jnp.bfloat16
WIDTH = 768
LENGTH = 160
ROWS = 320
HIDDEN = 3072
PAIRS = 6
SCALE = 0.125
SIZES = (768, 384, 384, 384, 1536, 384, 384, 384)
QV, B_OUT, N1G, N1B, B_UP, B_DOWN, N2G, N2B = (sum(SIZES[:at]) for at in range(8))
SMALL = sum(SIZES)
VMEM_LIMIT = 58 * 1024 * 1024


def dot_nn(left_side, right_side):
    return jnp.dot(left_side, right_side, preferred_element_type=F32)


def dot_nt(left_side, right_side):
    return lax.dot_general(
        left_side, right_side, (((1,), (1,)), ((), ())), preferred_element_type=F32
    )


def dot_tn(left_side, right_side):
    return lax.dot_general(
        left_side, right_side, (((0,), (0,)), ((), ())), preferred_element_type=F32
    )


class Weight:
    def __init__(self, half, own, other, dest, sems):
        rows = own.shape[0]
        self.dest = dest
        self.copies = [
            pltpu.make_async_copy(own, dest.at[pl.ds(half * rows, rows)], sems.at[0]),
            pltpu.make_async_copy(other, dest.at[pl.ds((1 - half) * rows, rows)], sems.at[1]),
        ]
        for copy in self.copies:
            copy.start()

    def get(self):
        for copy in self.copies:
            copy.wait()
        self.copies = []
        return self.dest[...]


def whole(smalls, at, size):
    return jnp.concatenate([smalls[0:1, at : at + size], smalls[1:2, at : at + size]], axis=1)


def split_heads(tensor):
    lane = lax.broadcasted_iota(jnp.int32, tensor.shape, 1)
    zero = jnp.zeros_like(tensor)
    return jnp.concatenate(
        [jnp.where(lane < 64, tensor, zero), jnp.where(lane < 64, zero, tensor)], axis=0
    )


def join_heads(tensor):
    lane = lax.broadcasted_iota(jnp.int32, (LENGTH, 128), 1)
    return jnp.where(lane < 64, tensor[:LENGTH], tensor[LENGTH:])


def normalize(values):
    center = values - jnp.mean(values, axis=-1, keepdims=True)
    spread = jnp.mean(center * center, axis=-1, keepdims=True)
    inverse = lax.rsqrt(spread + EPSILON)
    return center * inverse, inverse


def normalize_back(upstream, gain, normal, inverse):
    scaled = upstream * gain
    first = jnp.mean(scaled, axis=-1, keepdims=True)
    second = jnp.mean(scaled * normal, axis=-1, keepdims=True)
    return inverse * (scaled - first - normal * second)


def gelu_parts(values):
    size = jnp.abs(values)
    below = 1.0 + (0.3275911 * math.sqrt(0.5)) * size
    t = pl.reciprocal(below, approx=True)
    t = t * (2.0 - below * t)
    series = t * (
        0.5 * 0.254829592
        + t
        * (
            0.5 * -0.284496736
            + t * (0.5 * 1.421413741 + t * (0.5 * -1.453152027 + t * (0.5 * 1.061405429)))
        )
    )
    bell = jnp.exp(-0.5 * values * values)
    tail = series * bell
    share = jnp.where(values >= 0.0, 1.0 - tail, tail)
    return values * share, share + values * bell * (1.0 / math.sqrt(2.0 * math.pi))


def column_sum(values):
    return jnp.sum(values, axis=0, keepdims=True)


def put_halves(target, at, row):
    size = row.shape[1] // 2
    target[0:1, at : at + size] = row[:, :size]
    target[1:2, at : at + size] = row[:, size:]


def places():
    for index in range(2 * PAIRS):
        chain, pair = divmod(index, PAIRS)
        rows = pl.ds(chain * LENGTH, LENGTH)
        yield index, chain, rows, [pl.ds((pair + block * PAIRS) * 128, 128) for block in range(3)]


def attend_body(h, wqkv, wout, smalls, lens, half, qkv, probs, mixed, normal1, inverse1, u):
    x = h[...]
    bias = jnp.concatenate(
        [smalls[0:1, :WIDTH], jnp.zeros((1, WIDTH), F32), smalls[1:2, :WIDTH]], axis=1
    )
    qkv[...] = (dot_nn(x, wqkv.get()) + bias).astype(LOW)
    for index, chain, rows, (at_q, at_k, at_v) in places():
        scores = dot_nt(split_heads(qkv[rows, at_q]), qkv[rows, at_k]) * SCALE
        key = lax.broadcasted_iota(jnp.int32, scores.shape, 1)
        scores = jnp.where(key < lens[half[0], chain], scores, -1000000000.0)
        grown = jnp.exp(scores - jnp.max(scores, axis=-1, keepdims=True))
        weights = (grown * (1.0 / jnp.sum(grown, axis=-1, keepdims=True))).astype(LOW)
        if probs is not None:
            probs[index] = weights
        mixed[rows, at_q] = join_heads(dot_nn(weights, qkv[rows, at_v])).astype(LOW)
    branch = dot_nn(mixed[...], wout.get()) + whole(smalls, B_OUT, 384)
    normal, inverse = normalize(x.astype(F32) + branch)
    if normal1 is not None:
        normal1[...] = normal
        inverse1[...] = inverse
    u[...] = (normal * whole(smalls, N1G, 384) + whole(smalls, N1B, 384)).astype(LOW)


CHUNK = 1024


def feed_body(u, wup, wdown, smalls, slope, active, normal2, inverse2, y):
    x = u[...]
    bias = whole(smalls, B_UP, 1536)
    up = wup.get()
    for at in range(0, HIDDEN, CHUNK):
        grown, tangent = gelu_parts(dot_nn(x, up[:, at : at + CHUNK]) + bias[:, at : at + CHUNK])
        active[:, at : at + CHUNK] = grown.astype(LOW)
        if slope is not None:
            slope[:, at : at + CHUNK] = tangent.astype(LOW)
    total = x.astype(F32) + whole(smalls, B_DOWN, 384) + dot_nn(active[...], wdown.get())
    normal, inverse = normalize(total)
    if normal2 is not None:
        normal2[...] = normal
        inverse2[...] = inverse
    y[...] = (normal * whole(smalls, N2G, 384) + whole(smalls, N2B, 384)).astype(LOW)


def feed_back_body(
    up, wup, wdown, smalls, slope, normal1, inverse1, normal2, inverse2, gz, ga, gr1, gb, gsmall
):
    normal = normal2[...]
    put_halves(gsmall, N2G, column_sum(up * normal))
    put_halves(gsmall, N2B, column_sum(up))
    grad = normalize_back(up, whole(smalls, N2G, 384), normal, inverse2[...])
    z = grad.astype(LOW)
    gz[...] = z
    put_halves(gsmall, B_DOWN, column_sum(z.astype(F32)))
    down = wdown.get()
    sums = []
    for at in range(0, HIDDEN, CHUNK):
        inner = dot_nt(z, down[at : at + CHUNK, :]) * slope[:, at : at + CHUNK].astype(F32)
        a = inner.astype(LOW)
        ga[:, at : at + CHUNK] = a
        sums.append(column_sum(a.astype(F32)))
    put_halves(gsmall, B_UP, jnp.concatenate(sums, axis=1))
    up = grad + dot_nt(ga[...], wup.get())
    normal = normal1[...]
    put_halves(gsmall, N1G, column_sum(up * normal))
    put_halves(gsmall, N1B, column_sum(up))
    grad = normalize_back(up, whole(smalls, N1G, 384), normal, inverse1[...])
    gr1[...] = grad
    b = grad.astype(LOW)
    gb[...] = b
    put_halves(gsmall, B_OUT, column_sum(b.astype(F32)))


def heads_back_body(gb, wout, qkv, probs, gqkv, gqv, go):
    go[...] = dot_nt(gb[...], wout.get()).astype(LOW)
    for index, chain, rows, (at_q, at_k, at_v) in places():
        k = qkv[rows, at_k]
        g = split_heads(go[rows, at_q])
        weights = probs[index]
        wide = weights.astype(F32)
        inner = dot_nt(g, qkv[rows, at_v])
        inner = wide * (inner - jnp.sum(wide * inner, axis=-1, keepdims=True))
        s = inner.astype(LOW)
        gqkv[rows, at_q] = (join_heads(dot_nn(s, k)) * SCALE).astype(LOW)
        gqkv[rows, at_k] = (dot_tn(s, split_heads(qkv[rows, at_q])) * SCALE).astype(LOW)
        gqkv[rows, at_v] = dot_tn(weights, g).astype(LOW)
    if gqv is not None:
        gqv[0:1, :] = column_sum(gqkv[:, :WIDTH].astype(F32))
        gqv[1:2, :] = column_sum(gqkv[:, 2 * WIDTH :].astype(F32))


def span_rows(spans, half):
    row = lax.broadcasted_iota(jnp.int32, (ROWS, 1), 0)
    inside = row < 0
    for chain in range(2):
        start = spans[half[0], chain, 0] + chain * LENGTH
        end = spans[half[0], chain, 1] + chain * LENGTH
        inside = inside | ((row >= start) & (row < end))
    return inside


def pick_halves(half, own, other, smalls):
    low = half[0] == 0
    smalls[0:1, :] = jnp.where(low, own[:, :SMALL], other[:, :SMALL])
    smalls[1:2, :] = jnp.where(low, other[:, :SMALL], own[:, :SMALL])


VMEM = pl.BlockSpec(memory_space=pltpu.VMEM)
SMEM = pl.BlockSpec(memory_space=pltpu.SMEM)
ANY = pl.BlockSpec(memory_space=pl.ANY)
SMALL_SCRATCH = pltpu.VMEM((2, SMALL), F32)
QKV_SHAPE = (ROWS, 3 * WIDTH)
PROBS_SHAPE = (2 * PAIRS, 2 * LENGTH, LENGTH)
ROW_SHAPE = (ROWS, WIDTH)
FEED_SHAPE = (ROWS, HIDDEN)
MACS = ROWS * WIDTH * WIDTH * 2
ATTEND_WEIGHTS = [pltpu.VMEM((WIDTH, 3 * WIDTH), LOW), pltpu.VMEM((WIDTH, WIDTH), LOW)]
FEED_WEIGHTS = [pltpu.VMEM((WIDTH, HIDDEN), LOW), pltpu.VMEM((HIDDEN, WIDTH), LOW)]


def shape(dims, kind=LOW):
    return jax.ShapeDtypeStruct(dims, kind)


def kernel_call(body, ins, outs, scratch, flops, moved, name, out_specs=None):
    return pl.pallas_call(
        body,
        in_specs=ins,
        out_specs=out_specs or [VMEM] * len(outs),
        out_shape=outs,
        scratch_shapes=scratch,
        compiler_params=pltpu.CompilerParams(vmem_limit_bytes=VMEM_LIMIT),
        cost_estimate=pl.CostEstimate(flops=flops, bytes_accessed=moved, transcendentals=0),
        name=name,
    )


def attend_first(inputs, half, lens, spans, weights, smalls):
    def body(x, half, lens, spans, so, sp, qo, qp, oo, op, u, h, raw, small, qkv, mixed, wq, wo, sems):
        enter = pltpu.make_async_copy(x.at[half[0]], raw, sems.at[2, 0])
        enter.start()
        wqkv = Weight(half[0], qo, qp, wq, sems.at[0])
        wout = Weight(half[0], oo, op, wo, sems.at[1])
        pick_halves(half, so, sp, small)
        enter.wait()
        mask = so[:, SMALL:].astype(LOW)
        h[...] = jnp.where(span_rows(spans, half), mask, raw[...].reshape(ROWS, WIDTH))
        attend_body(h, wqkv, wout, small, lens, half, qkv, None, mixed, None, None, u)

    return kernel_call(
        body,
        [ANY, SMEM, SMEM, SMEM, VMEM, VMEM] + [ANY] * 4,
        [shape(ROW_SHAPE), shape(ROW_SHAPE)],
        [
            pltpu.VMEM((2, LENGTH, WIDTH), LOW),
            SMALL_SCRATCH,
            pltpu.VMEM(QKV_SHAPE, LOW),
            pltpu.VMEM(ROW_SHAPE, LOW),
            *ATTEND_WEIGHTS,
            pltpu.SemaphoreType.DMA((3, 2)),
        ],
        4 * MACS,
        8000000,
        "attend_first",
    )(inputs, half, lens, spans, *smalls, *weights[0], *weights[1])


def feed_first(u, half, weights, smalls):
    def body(u, half, so, sp, uo, up, do, dp, y, small, active, wu, wd, sems):
        wup = Weight(half[0], uo, up, wu, sems.at[0])
        wdown = Weight(half[0], do, dp, wd, sems.at[1])
        pick_halves(half, so, sp, small)
        feed_body(u, wup, wdown, small, None, active, None, None, y)

    return kernel_call(
        body,
        [VMEM, SMEM, VMEM, VMEM] + [ANY] * 4,
        [shape(ROW_SHAPE)],
        [
            SMALL_SCRATCH,
            pltpu.VMEM(FEED_SHAPE, LOW),
            *FEED_WEIGHTS,
            pltpu.SemaphoreType.DMA((2, 2)),
        ],
        8 * MACS,
        14000000,
        "feed_first",
    )(u, half, *smalls, *weights[2], *weights[3])[0]


KEPT = [
    shape(ROW_SHAPE),
    shape(QKV_SHAPE),
    shape(PROBS_SHAPE),
    shape(ROW_SHAPE),
    shape(ROW_SHAPE, F32),
    shape((ROWS, 1), F32),
    shape(ROW_SHAPE),
    shape(FEED_SHAPE),
    shape(FEED_SHAPE),
    shape(ROW_SHAPE, F32),
    shape((ROWS, 1), F32),
    shape(ROW_SHAPE),
]


def middle(h0, received, cotangent, half, first, lens, weights, smalls):
    def body(h0, received, cot, half, first, lens, so, sp, qo, qp, oo, op, uo, up, do, dp, *rest):
        outs, rest = rest[: len(KEPT)], rest[len(KEPT) :]
        gh, small, gz, ga, gr1, gb, gsmall, gqkv, go, raw, wq, wo, wu, wd = rest[:14]
        keeps, sems, out_sems, raw_sem = rest[14:-3], *rest[-3:]
        h, qkv, probs, mixed, normal1, inverse1, u, slope, active, normal2, inverse2, y = keeps
        wqkv = Weight(half[0], qo, qp, wq, sems.at[0])
        wout = Weight(half[0], oo, op, wo, sems.at[1])
        wup = Weight(half[0], uo, up, wu, sems.at[2])
        wdown = Weight(half[0], do, dp, wd, sems.at[3])
        enter = pltpu.make_async_copy(cot.at[half[0]], raw, raw_sem)
        enter.start()
        pick_halves(half, so, sp, small)
        leaving = []

        def leave(places):
            for place in places:
                copy = pltpu.make_async_copy(keeps[place], outs[place], out_sems.at[place])
                copy.start()
                leaving.append(copy)

        h[...] = jnp.where(first[0] > 0, h0[...], received[...])
        attend_body(h, wqkv, wout, small, lens, half, qkv, probs, mixed, normal1, inverse1, u)
        leave(range(7))
        feed_body(u, wup, wdown, small, slope, active, normal2, inverse2, y)
        leave(range(7, 12))
        enter.wait()
        upstream = raw[...].reshape(ROWS, WIDTH).astype(F32)
        feed_back_body(
            upstream, wup, wdown, small, slope, normal1, inverse1, normal2, inverse2, gz, ga, gr1, gb, gsmall
        )
        heads_back_body(gb, wout, qkv, probs, gqkv, None, go)
        gh[...] = (gr1[...] + dot_nt(gqkv[...], wqkv.get())).astype(LOW)
        for copy in leaving:
            copy.wait()

    return kernel_call(
        body,
        [VMEM, VMEM, ANY, SMEM, SMEM, SMEM, VMEM, VMEM] + [ANY] * 8,
        KEPT + [shape(ROW_SHAPE)],
        [
            SMALL_SCRATCH,
            pltpu.VMEM(ROW_SHAPE, LOW),
            pltpu.VMEM(FEED_SHAPE, LOW),
            pltpu.VMEM(ROW_SHAPE, F32),
            pltpu.VMEM(ROW_SHAPE, LOW),
            SMALL_SCRATCH,
            pltpu.VMEM(QKV_SHAPE, LOW),
            pltpu.VMEM(ROW_SHAPE, LOW),
            pltpu.VMEM((2, LENGTH, WIDTH), LOW),
            *ATTEND_WEIGHTS,
            *FEED_WEIGHTS,
            *[pltpu.VMEM(kept.shape, kept.dtype) for kept in KEPT],
            pltpu.SemaphoreType.DMA((4, 2)),
            pltpu.SemaphoreType.DMA((len(KEPT),)),
            pltpu.SemaphoreType.DMA,
        ],
        24 * MACS,
        45000000,
        "middle",
        [ANY] * len(KEPT) + [VMEM],
    )(
        h0, received, cotangent, half, first, lens, *smalls,
        *weights[0], *weights[1], *weights[2], *weights[3],
    )


def half_columns(ref, which):
    size = ref.shape[1] // 2
    return ref[:, pl.ds(pl.multiple_of(which * size, 128), size)]


def store_folded(target, at, tensor):
    rows, wide = tensor.shape
    for block in range(wide // WIDTH):
        target[at + block * rows : at + (block + 1) * rows, :] = tensor[
            :, block * WIDTH : (block + 1) * WIDTH
        ].astype(LOW)


class Leaving:
    def __init__(self, sems):
        self.sems = sems
        self.copies = []

    def send(self, source, target):
        copy = pltpu.make_async_copy(source, target, self.sems.at[len(self.copies)])
        copy.start()
        self.copies.append(copy)

    def wait(self):
        for copy in self.copies:
            copy.wait()


TOKEN = shape((8, 128), F32)


def back_feed(cotangent, returned, half, first, weights, smalls, kept):
    u, slope, active, n1, i1, n2, i2 = kept

    def body(cot, returned, half, first, so, sp, uo, up, do, dp, u, slope, active, n1, i1, n2, i2, *rest):
        other, own, gr1, gb, gsmall, gz, ga, vother, vown, small, raw, wu, wd, sems, out_sems = rest
        enter = pltpu.make_async_copy(cot.at[half[0]], raw, sems.at[2, 0])
        enter.start()
        wdown = Weight(half[0], do, dp, wd, sems.at[1])
        wup = Weight(half[0], uo, up, wu, sems.at[0])
        pick_halves(half, so, sp, small)
        enter.wait()
        upstream = jnp.where(first[0] > 0, returned[...], raw[...].reshape(ROWS, WIDTH))
        feed_back_body(
            upstream.astype(F32), wup, wdown, small, slope, n1, i1, n2, i2, gz, ga, gr1, gb, gsmall
        )
        leaving = Leaving(out_sems)
        for which, local, target in ((1 - half[0], vother, other), (half[0], vown, own)):
            local[:1536, :] = dot_tn(half_columns(active, which), gz[...]).astype(LOW)
            leaving.send(local.at[pl.ds(0, 1536)], target.at[pl.ds(0, 1536)])
            store_folded(local, 1536, dot_tn(half_columns(u, which), ga[...]))
            leaving.send(local.at[pl.ds(1536, 1536)], target.at[pl.ds(1536, 1536)])
        leaving.wait()

    return kernel_call(
        body,
        [ANY, VMEM, SMEM, SMEM, VMEM, VMEM] + [ANY] * 4 + [VMEM] * 7,
        [
            shape((3072, WIDTH)),
            shape((3072, WIDTH)),
            shape(ROW_SHAPE, F32),
            shape(ROW_SHAPE),
            shape((2, SMALL), F32),
        ],
        [
            pltpu.VMEM(ROW_SHAPE, LOW),
            pltpu.VMEM(FEED_SHAPE, LOW),
            pltpu.VMEM((3072, WIDTH), LOW),
            pltpu.VMEM((3072, WIDTH), LOW),
            SMALL_SCRATCH,
            pltpu.VMEM((2, LENGTH, WIDTH), LOW),
            *FEED_WEIGHTS,
            pltpu.SemaphoreType.DMA((3, 2)),
            pltpu.SemaphoreType.DMA((4,)),
        ],
        16 * MACS,
        36000000,
        "back_feed",
        [ANY, ANY, VMEM, VMEM, VMEM],
    )(
        cotangent, returned, half, first, *smalls, *weights[2], *weights[3],
        u, slope, active, n1, i1, n2, i2,
    )


def back_heads(gb, half, weights, gsmall, h, qkv, probs, mixed):
    def body(gb, half, oo, op, gsmall, h, qkv, probs, mixed, *rest):
        other, own, small_other, small_own, gqkv, token, go, gqv, vother, vown, wo, sems, out_sems = rest
        wout = Weight(half[0], oo, op, wo, sems)
        heads_back_body(gb, wout, qkv, probs, gqkv, gqv, go)
        leaving = Leaving(out_sems)
        for which, local, target in ((1 - half[0], vother, other), (half[0], vown, own)):
            store_folded(local, 0, dot_tn(half_columns(h, which), gqkv[...]))
            local[1152:, :] = dot_tn(half_columns(mixed, which), gb[...]).astype(LOW)
            leaving.send(local, target)
        for which, target in ((1 - half[0], small_other), (half[0], small_own)):
            target[:, :WIDTH] = gqv[pl.ds(which, 1), :]
            target[:, WIDTH:] = gsmall[pl.ds(which, 1), WIDTH:]
        token[...] = jnp.zeros(token.shape, F32)
        leaving.wait()

    return kernel_call(
        body,
        [VMEM, SMEM] + [ANY] * 2 + [VMEM] * 5,
        [
            shape((1536, WIDTH)),
            shape((1536, WIDTH)),
            shape((1, SMALL), F32),
            shape((1, SMALL), F32),
            shape(QKV_SHAPE),
            TOKEN,
        ],
        [
            pltpu.VMEM(ROW_SHAPE, LOW),
            pltpu.VMEM((2, WIDTH), F32),
            pltpu.VMEM((1536, WIDTH), LOW),
            pltpu.VMEM((1536, WIDTH), LOW),
            ATTEND_WEIGHTS[1],
            pltpu.SemaphoreType.DMA((2,)),
            pltpu.SemaphoreType.DMA((2,)),
        ],
        6 * MACS,
        16000000,
        "back_heads",
        [ANY, ANY] + [VMEM] * 4,
    )(gb, half, *weights[1], gsmall, h, qkv, probs, mixed)


def back_input(gqkv, gr1, half, first, spans, weights, after):
    def body(gqkv, gr1, half, first, spans, qo, qp, after, gh, gmask, wq, sems):
        wqkv = Weight(half[0], qo, qp, wq, sems)
        full = gr1[...] + dot_nt(gqkv[...], wqkv.get())
        dropped = span_rows(spans, half) & (first[0] > 0)
        zero = jnp.zeros_like(full)
        gh[...] = jnp.where(dropped, zero, full).astype(LOW)
        gmask[...] = column_sum(jnp.where(dropped, full, zero))

    return kernel_call(
        body,
        [VMEM, VMEM, SMEM, SMEM, SMEM] + [ANY] * 3,
        [shape(ROW_SHAPE), shape((1, WIDTH), F32)],
        [ATTEND_WEIGHTS[0], pltpu.SemaphoreType.DMA((2,))],
        3 * MACS,
        6000000,
        "back_input",
    )(gqkv, gr1, half, first, spans, *weights[0], after)


TAIL = 16
BLOCK = 48


def add_low(left_side, right_side):
    return (left_side.astype(F32) + right_side.astype(F32)).astype(LOW)


def add_rows(target, at, left, right, source, rows):
    for start in range(0, rows, BLOCK):
        size = min(BLOCK, rows - start)
        place = pl.ds(source + start, size)
        if not isinstance(source, int):
            place = pl.ds(pl.multiple_of(source + start, 16), size)
        target[at + start : at + start + size, :] = add_low(left[place, :], right[place, :])


def halve(bit, keep, got, new_keep, new_send):
    tail = 2 * new_keep.shape[0] - keep.shape[0]
    rows = new_keep.shape[0] - tail
    for target, which in ((new_send, 1 - bit), (new_keep, bit)):
        add_rows(target, 0, keep, got, which * rows, rows)
        if tail:
            target[rows:, :] = add_low(keep[2 * rows :, :], got[2 * rows :, :])


def grow(bit, value, got, target):
    rows = value.shape[0]
    target[pl.ds(pl.multiple_of(bit * rows, 16), rows), :] = value[...]
    target[pl.ds(pl.multiple_of((1 - bit) * rows, 16), rows), :] = got[...]


def ordered(name, body, ins, outs, bits, after):
    count = len(ins)

    def kernel(bits, after, *refs):
        body(bits, refs[:count], refs[count:-1])
        refs[-1][...] = jnp.zeros(TOKEN.shape, F32)

    moved = 2 * sum(math.prod(each.shape) for each in list(ins) + list(outs))
    result = kernel_call(
        kernel, [SMEM, ANY] + [VMEM] * count, list(outs) + [TOKEN], [], moved, moved, name
    )(bits, after, *ins)
    return result[:-1], result[-1]


def partner(x, axis, bit):
    return lax.ppermute(x, axis, [(i, i ^ 1 << bit) for i in range(lax.axis_size(axis))])


ORDERS = (
    (("zw", "zu", "xw", "xu"), ("xw", "xu", "zw", "zu")),
    (("zu", "zw", "xu", "xw"), ("xu", "xw", "zu", "zw")),
    (("xw", "xu", "zw", "zu"), ("zw", "zu", "xw", "xu")),
)


def flip_dp(index, bit):
    z, x, y = index // 8, index // 2 % 4, index % 2
    if bit == "zw":
        z ^= 1
    elif bit == "zu":
        z ^= 3
    elif bit == "xw":
        x ^= 1
    elif bit == "xu":
        x ^= 3
    else:
        y ^= 1
    return z * 8 + x * 2 + y


def exchange(value, part, step):
    pairs = []
    for section in range(4):
        bit = "y" if step is None else ORDERS[part][section % 2][step]
        for index in range(32):
            pairs.append((section * 32 + index, section * 32 + flip_dp(index, bit)))
    return lax.ppermute(value, ("section", "dp"), pairs)


def own_bits(core):
    index = lax.axis_index("dp")
    z, x = index // 8, index // 2 % 4
    bits = {
        "zu": z // 2,
        "zw": (z // 2) ^ (z % 2),
        "xu": x // 2,
        "xw": (x // 2) ^ (x % 2),
    }
    table = [
        jnp.where(core == 0, bits[order[0][step]], bits[order[1][step]])
        for order in ORDERS
        for step in range(4)
    ]
    return jnp.stack(table).astype(jnp.int32)


def pack_vectors(vectors):
    size = sum(vector.shape[0] for vector in vectors)
    total = jnp.zeros((size,), F32)
    at = 0
    for vector in vectors:
        total = total + jnp.pad(vector.astype(F32), (at, size - at - vector.shape[0]))
        at += vector.shape[0]
    return total.reshape(1, size)


def per_device(
    inputs,
    cotangent,
    lengths,
    cdr_spans,
    mask_vector,
    w_qkv,
    qv_bias,
    w_out,
    b_out,
    norm1_gain,
    norm1_bias,
    w_up,
    b_up,
    w_down,
    b_down,
    norm2_gain,
    norm2_bias,
):
    section_index = lax.axis_index("section")
    core = section_index % 2
    half = core.astype(jnp.int32).reshape(1)
    first = (section_index < 2).astype(jnp.int32).reshape(1)
    bits = own_bits(core)
    small = pack_vectors(
        (
            qv_bias,
            b_out,
            norm1_gain,
            norm1_bias,
            b_up,
            b_down,
            norm2_gain,
            norm2_bias,
            mask_vector,
        )
    )
    smalls = (small, partner(small, "section", 0))
    weights = [(tensor, partner(tensor, "section", 0)) for tensor in (w_qkv, w_out, w_up, w_down)]

    u, h0 = attend_first(inputs, half, lengths, cdr_spans, weights, smalls)
    first_out = feed_first(u, half, weights, smalls)
    received = lax.ppermute(first_out, "section", [(0, 2), (1, 3)])
    kept = middle(h0, received, cotangent, half, first, lengths, weights, smalls)
    h, qkv, probs, mixed, normal1, inverse1, u, slope, active, normal2, inverse2, output = kept[:12]
    returned = lax.ppermute(kept[12], "section", [(2, 0), (3, 1)])

    x_other, x_own, gr1, gb, gsmall = back_feed(
        cotangent,
        returned,
        half,
        first,
        weights,
        smalls,
        (u, slope, active, normal1, inverse1, normal2, inverse2),
    )
    x_got = partner(x_other, "section", 0)
    y_other, y_own, small_other, small_own, gqkv, token = back_heads(
        gb, half, weights, gsmall, h, qkv, probs, mixed
    )
    y_got = partner(y_other, "section", 0)
    small_got = partner(small_other, "section", 0)

    def row_shapes(*counts):
        return [shape((count, WIDTH)) for count in counts]

    def start_x(bits, ins, outs):
        own, got = ins
        for part in range(2):
            for target, which in (
                (outs[2 * part + 1], 1 - bits[4 * part]),
                (outs[2 * part], bits[4 * part]),
            ):
                add_rows(target, 0, own, got, part * 1536 + which * 768, 768)

    (keep_a, send_a, keep_b, send_b), token = ordered(
        "start_x", start_x, (x_own, x_got), row_shapes(768, 768, 768, 768), bits, token
    )
    got_a, got_b = exchange(send_a, 0, 0), exchange(send_b, 1, 0)

    gh, gmask = back_input(gqkv, gr1, half, first, cdr_spans, weights, token)

    def start_y(bits, ins, outs):
        own, got, small_own, small_got, gmask = ins
        keep, send = outs
        total = small_own[...] + small_got[...]
        rows = [total[:, at : at + WIDTH] for at in range(0, SMALL, WIDTH)]
        rows += [gmask[...], jnp.zeros((TAIL - 7, WIDTH), F32)]
        tail = jnp.concatenate(rows, axis=0).astype(LOW)
        for target, which in ((send, 1 - bits[8]), (keep, bits[8])):
            add_rows(target, 0, own, got, which * 768, 768)
            target[768:, :] = tail

    (keep_y, send_y), token = ordered(
        "start_y",
        start_y,
        (y_own, y_got, small_own, small_got, gmask),
        row_shapes(768 + TAIL, 768 + TAIL),
        bits,
        token,
    )
    got_y = exchange(send_y, 2, 0)

    rows = 768
    for step in range(1, 4):
        rows //= 2

        def halve_x(bits, ins, outs, step=step):
            for part in range(2):
                halve(bits[4 * part + step], *ins[2 * part : 2 * part + 2], *outs[2 * part : 2 * part + 2])

        (keep_a, send_a, keep_b, send_b), token = ordered(
            "halve_x", halve_x, (keep_a, got_a, keep_b, got_b), row_shapes(*[rows] * 4), bits, token
        )
        got_a, got_b = exchange(send_a, 0, step), exchange(send_b, 1, step)

        def halve_y(bits, ins, outs, step=step):
            halve(bits[8 + step], *ins, *outs)

        (keep_y, send_y), token = ordered(
            "halve_y", halve_y, (keep_y, got_y), row_shapes(*[rows + TAIL] * 2), bits, token
        )
        got_y = exchange(send_y, 2, step)

    def across_x(bits, ins, outs):
        add_rows(outs[0], 0, ins[0], ins[1], 0, rows)
        add_rows(outs[0], rows, ins[2], ins[3], 0, rows)

    (both,), token = ordered(
        "across_x", across_x, (keep_a, got_a, keep_b, got_b), row_shapes(2 * rows), bits, token
    )
    both_got = exchange(both, 0, None)

    def across_y(bits, ins, outs):
        add_rows(outs[0], 0, ins[0], ins[1], 0, rows + TAIL)

    (sum_y,), token = ordered(
        "across_y", across_y, (keep_y, got_y), row_shapes(rows + TAIL), bits, token
    )
    sum_got = exchange(sum_y, 2, None)

    def part_x(bits, ins, outs):
        add_rows(outs[0], 0, ins[0], ins[1], 0, rows)
        add_rows(outs[1], 0, ins[0], ins[1], rows, rows)

    (value_a, value_b), token = ordered(
        "part_x", part_x, (both, both_got), row_shapes(rows, rows), bits, token
    )
    got_a, got_b = exchange(value_a, 0, 3), exchange(value_b, 1, 3)

    def part_y(bits, ins, outs):
        add_rows(outs[0], 0, ins[0], ins[1], 0, rows)
        outs[1][...] = add_low(ins[0][rows:, :], ins[1][rows:, :])

    (value_y, tail), token = ordered(
        "part_y", part_y, (sum_y, sum_got), row_shapes(rows, TAIL), bits, token
    )
    got_y = exchange(value_y, 2, 3)
    mask_rows, mask_got = tail, partner(tail, "section", 0)

    for step in (3, 2, 1):
        rows *= 2

        def grow_x(bits, ins, outs, step=step):
            for part in range(2):
                grow(bits[4 * part + step], ins[2 * part], ins[2 * part + 1], outs[part])

        (value_a, value_b), token = ordered(
            "grow_x", grow_x, (value_a, got_a, value_b, got_b), row_shapes(rows, rows), bits, token
        )
        got_a, got_b = exchange(value_a, 0, step - 1), exchange(value_b, 1, step - 1)

        def grow_y(bits, ins, outs, step=step):
            grow(bits[8 + step], *ins[:2], outs[0])
            if step > 1:
                outs[1][...] = add_low(ins[2][...], ins[3][...])

        if step > 1:
            (value_y, mask_rows), token = ordered(
                "grow_y",
                grow_y,
                (value_y, got_y, mask_rows, mask_got),
                row_shapes(rows, TAIL),
                bits,
                token,
            )
            if step == 3:
                mask_got = partner(mask_rows, "section", 1)
        else:
            (value_y,), token = ordered(
                "grow_y", grow_y, (value_y, got_y), row_shapes(rows), bits, token
            )
        got_y = exchange(value_y, 2, step - 1)

    mask_grad = mask_rows[6].astype(F32)

    def unfold(value, got, bit, count):
        lower = jnp.where(bit == 0, value, got)
        upper = jnp.where(bit == 0, got, value)
        full = jnp.concatenate([lower, upper], axis=0)
        if count == 1:
            return full
        return jnp.concatenate(jnp.split(full, count, axis=0), axis=1)

    flat_small = tail[:6].reshape(-1).astype(F32)
    out_small = []
    at = 0
    for size in SIZES:
        out_small.append(flat_small[at : at + size])
        at += size
    g_qv, g_bo, g_n1g, g_n1b, g_bu, g_bd, g_n2g, g_n2b = out_small
    late = unfold(value_y, got_y, bits[8], 4)
    return (
        output.reshape(1, 2, LENGTH, WIDTH),
        gh.reshape(1, 2, LENGTH, WIDTH),
        mask_grad,
        late[:, : 3 * WIDTH].astype(F32),
        g_qv,
        late[:, 3 * WIDTH :].astype(F32),
        g_bo,
        g_n1g,
        g_n1b,
        unfold(value_b, got_b, bits[4], 4).astype(F32),
        g_bu,
        unfold(value_a, got_a, bits[0], 1).astype(F32),
        g_bd,
        g_n2g,
        g_n2b,
    )


def solution(mesh):
    in_specs = (
        P(None, "dp", None, None),
        P(None, "dp", None, None),
        P(None, "dp"),
        P(None, "dp", None),
        P(),
        P("section", None),
        P("section"),
        P("section", None),
        P("section"),
        P("section"),
        P("section"),
        P("section", None),
        P("section"),
        P("section", None),
        P("section"),
        P("section"),
        P("section"),
    )
    out_specs = (
        P("section", "dp", None, None),
        P("section", "dp", None, None),
        P(),
        P("section", None),
        P("section"),
        P("section", None),
        P("section"),
        P("section"),
        P("section"),
        P("section", None),
        P("section"),
        P("section", None),
        P("section"),
        P("section"),
        P("section"),
    )
    return jax.shard_map(
        per_device, mesh=mesh, in_specs=in_specs, out_specs=out_specs, check_vma=False
    )
```

```python
import functools
import math

import jax
import jax.numpy as jnp
from jax import lax
from jax.experimental import pallas as pl
from jax.experimental.pallas import tpu as pltpu
from jax.sharding import PartitionSpec as P

EPSILON = 1e-05
F32 = jnp.float32
LOW = jnp.bfloat16
WIDTH = 768
LENGTH = 160
ROWS = 320
HIDDEN = 3072
PAIRS = 6
SCALE = 0.125
SIZES = (768, 384, 384, 384, 1536, 384, 384, 384)
QV, B_OUT, N1G, N1B, B_UP, B_DOWN, N2G, N2B = (sum(SIZES[:at]) for at in range(8))
SMALL = sum(SIZES)
VMEM_LIMIT = 58 * 1024 * 1024


def dot_nn(left_side, right_side):
    return jnp.dot(left_side, right_side, preferred_element_type=F32)


def dot_nt(left_side, right_side):
    return lax.dot_general(
        left_side, right_side, (((1,), (1,)), ((), ())), preferred_element_type=F32
    )


def dot_tn(left_side, right_side):
    return lax.dot_general(
        left_side, right_side, (((0,), (0,)), ((), ())), preferred_element_type=F32
    )


class Weight:
    def __init__(self, half, own, other, dest, sems):
        rows = own.shape[0]
        self.dest = dest
        self.copies = [
            pltpu.make_async_copy(own, dest.at[pl.ds(half * rows, rows)], sems.at[0]),
            pltpu.make_async_copy(other, dest.at[pl.ds((1 - half) * rows, rows)], sems.at[1]),
        ]
        for copy in self.copies:
            copy.start()

    def get(self):
        for copy in self.copies:
            copy.wait()
        self.copies = []
        return self.dest[...]


def whole(smalls, at, size):
    return jnp.concatenate([smalls[0:1, at : at + size], smalls[1:2, at : at + size]], axis=1)


def split_heads(tensor):
    lane = lax.broadcasted_iota(jnp.int32, tensor.shape, 1)
    zero = jnp.zeros_like(tensor)
    return jnp.concatenate(
        [jnp.where(lane < 64, tensor, zero), jnp.where(lane < 64, zero, tensor)], axis=0
    )


def join_heads(tensor):
    lane = lax.broadcasted_iota(jnp.int32, (LENGTH, 128), 1)
    return jnp.where(lane < 64, tensor[:LENGTH], tensor[LENGTH:])


def normalize(values):
    center = values - jnp.mean(values, axis=-1, keepdims=True)
    spread = jnp.mean(center * center, axis=-1, keepdims=True)
    inverse = lax.rsqrt(spread + EPSILON)
    return center * inverse, inverse


def normalize_back(upstream, gain, normal, inverse):
    scaled = upstream * gain
    first = jnp.mean(scaled, axis=-1, keepdims=True)
    second = jnp.mean(scaled * normal, axis=-1, keepdims=True)
    return inverse * (scaled - first - normal * second)


def gelu_parts(values):
    size = jnp.abs(values)
    below = 1.0 + (0.3275911 * math.sqrt(0.5)) * size
    t = pl.reciprocal(below, approx=True)
    t = t * (2.0 - below * t)
    series = t * (
        0.5 * 0.254829592
        + t
        * (
            0.5 * -0.284496736
            + t * (0.5 * 1.421413741 + t * (0.5 * -1.453152027 + t * (0.5 * 1.061405429)))
        )
    )
    bell = jnp.exp(-0.5 * values * values)
    tail = series * bell
    share = jnp.where(values >= 0.0, 1.0 - tail, tail)
    return values * share, share + values * bell * (1.0 / math.sqrt(2.0 * math.pi))


def column_sum(values):
    return jnp.sum(values, axis=0, keepdims=True)


def put_halves(target, at, row):
    size = row.shape[1] // 2
    target[0:1, at : at + size] = row[:, :size]
    target[1:2, at : at + size] = row[:, size:]


def places():
    for index in range(2 * PAIRS):
        chain, pair = divmod(index, PAIRS)
        rows = pl.ds(chain * LENGTH, LENGTH)
        yield index, chain, rows, [pl.ds((pair + block * PAIRS) * 128, 128) for block in range(3)]


def attend_body(h, wqkv, wout, smalls, lens, half, qkv, probs, mixed, normal1, inverse1, u):
    x = h[...]
    bias = jnp.concatenate(
        [smalls[0:1, :WIDTH], jnp.zeros((1, WIDTH), F32), smalls[1:2, :WIDTH]], axis=1
    )
    qkv[...] = (dot_nn(x, wqkv.get()) + bias).astype(LOW)
    for index, chain, rows, (at_q, at_k, at_v) in places():
        scores = dot_nt(split_heads(qkv[rows, at_q]), qkv[rows, at_k]) * SCALE
        key = lax.broadcasted_iota(jnp.int32, scores.shape, 1)
        scores = jnp.where(key < lens[half[0], chain], scores, -1000000000.0)
        grown = jnp.exp(scores - jnp.max(scores, axis=-1, keepdims=True))
        weights = (grown * (1.0 / jnp.sum(grown, axis=-1, keepdims=True))).astype(LOW)
        if probs is not None:
            probs[index] = weights
        mixed[rows, at_q] = join_heads(dot_nn(weights, qkv[rows, at_v])).astype(LOW)
    branch = dot_nn(mixed[...], wout.get()) + whole(smalls, B_OUT, 384)
    normal, inverse = normalize(x.astype(F32) + branch)
    if normal1 is not None:
        normal1[...] = normal
        inverse1[...] = inverse
    u[...] = (normal * whole(smalls, N1G, 384) + whole(smalls, N1B, 384)).astype(LOW)


CHUNK = 1024


def feed_body(u, wup, wdown, smalls, slope, active, normal2, inverse2, y):
    x = u[...]
    bias = whole(smalls, B_UP, 1536)
    up = wup.get()
    for at in range(0, HIDDEN, CHUNK):
        grown, tangent = gelu_parts(dot_nn(x, up[:, at : at + CHUNK]) + bias[:, at : at + CHUNK])
        active[:, at : at + CHUNK] = grown.astype(LOW)
        if slope is not None:
            slope[:, at : at + CHUNK] = tangent.astype(LOW)
    total = x.astype(F32) + whole(smalls, B_DOWN, 384) + dot_nn(active[...], wdown.get())
    normal, inverse = normalize(total)
    if normal2 is not None:
        normal2[...] = normal
        inverse2[...] = inverse
    y[...] = (normal * whole(smalls, N2G, 384) + whole(smalls, N2B, 384)).astype(LOW)


def top_back_body(up, smalls, normal2, inverse2, gr2, gz, gsmall):
    normal = normal2[...]
    put_halves(gsmall, N2G, column_sum(up * normal))
    put_halves(gsmall, N2B, column_sum(up))
    grad = normalize_back(up, whole(smalls, N2G, 384), normal, inverse2[...])
    z = grad.astype(LOW)
    gz[...] = z
    put_halves(gsmall, B_DOWN, column_sum(z.astype(F32)))
    gr2[...] = grad


def feed_back_body(gr2, gz, wup, wdown, smalls, slope, normal1, inverse1, ga, gr1, gb, gsmall):
    z = gz[...]
    down = wdown.get()
    sums = []
    for at in range(0, HIDDEN, CHUNK):
        inner = dot_nt(z, down[at : at + CHUNK, :]) * slope[:, at : at + CHUNK].astype(F32)
        a = inner.astype(LOW)
        ga[:, at : at + CHUNK] = a
        sums.append(column_sum(a.astype(F32)))
    put_halves(gsmall, B_UP, jnp.concatenate(sums, axis=1))
    up = gr2[...] + dot_nt(ga[...], wup.get())
    normal = normal1[...]
    put_halves(gsmall, N1G, column_sum(up * normal))
    put_halves(gsmall, N1B, column_sum(up))
    grad = normalize_back(up, whole(smalls, N1G, 384), normal, inverse1[...])
    gr1[...] = grad
    b = grad.astype(LOW)
    gb[...] = b
    put_halves(gsmall, B_OUT, column_sum(b.astype(F32)))


def heads_back_body(gb, wout, qkv, probs, gqkv, gqv, go):
    go[...] = dot_nt(gb[...], wout.get()).astype(LOW)
    for index, chain, rows, (at_q, at_k, at_v) in places():
        k = qkv[rows, at_k]
        g = split_heads(go[rows, at_q])
        weights = probs[index]
        wide = weights.astype(F32)
        inner = dot_nt(g, qkv[rows, at_v])
        inner = wide * (inner - jnp.sum(wide * inner, axis=-1, keepdims=True))
        s = inner.astype(LOW)
        gqkv[rows, at_q] = (join_heads(dot_nn(s, k)) * SCALE).astype(LOW)
        gqkv[rows, at_k] = (dot_tn(s, split_heads(qkv[rows, at_q])) * SCALE).astype(LOW)
        gqkv[rows, at_v] = dot_tn(weights, g).astype(LOW)
    if gqv is not None:
        gqv[0:1, :] = column_sum(gqkv[:, :WIDTH].astype(F32))
        gqv[1:2, :] = column_sum(gqkv[:, 2 * WIDTH :].astype(F32))


def span_rows(spans, half):
    row = lax.broadcasted_iota(jnp.int32, (ROWS, 1), 0)
    inside = row < 0
    for chain in range(2):
        start = spans[half[0], chain, 0] + chain * LENGTH
        end = spans[half[0], chain, 1] + chain * LENGTH
        inside = inside | ((row >= start) & (row < end))
    return inside


def pick_halves(half, own, other, smalls):
    low = half[0] == 0
    smalls[0:1, :] = jnp.where(low, own[:, :SMALL], other[:, :SMALL])
    smalls[1:2, :] = jnp.where(low, other[:, :SMALL], own[:, :SMALL])


VMEM = pl.BlockSpec(memory_space=pltpu.VMEM)
SMEM = pl.BlockSpec(memory_space=pltpu.SMEM)
ANY = pl.BlockSpec(memory_space=pl.ANY)
SMALL_SCRATCH = pltpu.VMEM((2, SMALL), F32)
QKV_SHAPE = (ROWS, 3 * WIDTH)
PROBS_SHAPE = (2 * PAIRS, 2 * LENGTH, LENGTH)
ROW_SHAPE = (ROWS, WIDTH)
FEED_SHAPE = (ROWS, HIDDEN)
MACS = ROWS * WIDTH * WIDTH * 2
ATTEND_WEIGHTS = [pltpu.VMEM((WIDTH, 3 * WIDTH), LOW), pltpu.VMEM((WIDTH, WIDTH), LOW)]
FEED_WEIGHTS = [pltpu.VMEM((WIDTH, HIDDEN), LOW), pltpu.VMEM((HIDDEN, WIDTH), LOW)]


def shape(dims, kind=LOW):
    return jax.ShapeDtypeStruct(dims, kind)


def kernel_call(body, ins, outs, scratch, flops, moved, name, out_specs=None, grant=VMEM_LIMIT):
    return pl.pallas_call(
        body,
        in_specs=ins,
        out_specs=out_specs or [VMEM] * len(outs),
        out_shape=outs,
        scratch_shapes=scratch,
        compiler_params=pltpu.CompilerParams(vmem_limit_bytes=grant),
        cost_estimate=pl.CostEstimate(flops=flops, bytes_accessed=moved, transcendentals=0),
        name=name,
    )


def attend_first(inputs, half, lens, spans, weights, smalls):
    def body(x, half, lens, spans, so, sp, qo, qp, oo, op, u, h, raw, small, qkv, mixed, wq, wo, sems):
        enter = pltpu.make_async_copy(x.at[half[0]], raw, sems.at[2, 0])
        enter.start()
        wqkv = Weight(half[0], qo, qp, wq, sems.at[0])
        wout = Weight(half[0], oo, op, wo, sems.at[1])
        pick_halves(half, so, sp, small)
        enter.wait()
        mask = so[:, SMALL:].astype(LOW)
        h[...] = jnp.where(span_rows(spans, half), mask, raw[...].reshape(ROWS, WIDTH))
        attend_body(h, wqkv, wout, small, lens, half, qkv, None, mixed, None, None, u)

    return kernel_call(
        body,
        [ANY, SMEM, SMEM, SMEM, VMEM, VMEM] + [ANY] * 4,
        [shape(ROW_SHAPE), shape(ROW_SHAPE)],
        [
            pltpu.VMEM((2, LENGTH, WIDTH), LOW),
            SMALL_SCRATCH,
            pltpu.VMEM(QKV_SHAPE, LOW),
            pltpu.VMEM(ROW_SHAPE, LOW),
            *ATTEND_WEIGHTS,
            pltpu.SemaphoreType.DMA((3, 2)),
        ],
        4 * MACS,
        8000000,
        "attend_first",
    )(inputs, half, lens, spans, *smalls, *weights[0], *weights[1])


def feed_first(u, half, weights, smalls):
    def body(u, half, so, sp, uo, up, do, dp, y, small, active, wu, wd, sems):
        wup = Weight(half[0], uo, up, wu, sems.at[0])
        wdown = Weight(half[0], do, dp, wd, sems.at[1])
        pick_halves(half, so, sp, small)
        feed_body(u, wup, wdown, small, None, active, None, None, y)

    return kernel_call(
        body,
        [VMEM, SMEM, VMEM, VMEM] + [ANY] * 4,
        [shape(ROW_SHAPE)],
        [
            SMALL_SCRATCH,
            pltpu.VMEM(FEED_SHAPE, LOW),
            *FEED_WEIGHTS,
            pltpu.SemaphoreType.DMA((2, 2)),
        ],
        8 * MACS,
        14000000,
        "feed_first",
    )(u, half, *smalls, *weights[2], *weights[3])[0]


KEPT = [
    shape(ROW_SHAPE),
    shape(QKV_SHAPE),
    shape(PROBS_SHAPE),
    shape(ROW_SHAPE),
    shape(ROW_SHAPE, F32),
    shape((ROWS, 1), F32),
    shape(ROW_SHAPE),
    shape(FEED_SHAPE),
    shape(FEED_SHAPE),
    shape(ROW_SHAPE, F32),
    shape((ROWS, 1), F32),
    shape(ROW_SHAPE),
]


def middle(h0, received, cotangent, half, first, lens, weights, smalls):
    def body(h0, received, cot, half, first, lens, so, sp, qo, qp, oo, op, uo, up, do, dp, *rest):
        outs, rest = rest[: len(KEPT)], rest[len(KEPT) :]
        gh, small, gr2, gz, ga, gr1, gb, gsmall, gqkv, go, raw, wq, wo, wu, wd = rest[:15]
        keeps, sems, out_sems, raw_sem = rest[15:-3], *rest[-3:]
        h, qkv, probs, mixed, normal1, inverse1, u, slope, active, normal2, inverse2, y = keeps
        wqkv = Weight(half[0], qo, qp, wq, sems.at[0])
        wout = Weight(half[0], oo, op, wo, sems.at[1])
        wup = Weight(half[0], uo, up, wu, sems.at[2])
        wdown = Weight(half[0], do, dp, wd, sems.at[3])
        enter = pltpu.make_async_copy(cot.at[half[0]], raw, raw_sem)
        enter.start()
        pick_halves(half, so, sp, small)
        leaving = []

        def leave(places):
            for place in places:
                copy = pltpu.make_async_copy(keeps[place], outs[place], out_sems.at[place])
                copy.start()
                leaving.append(copy)

        h[...] = jnp.where(first[0] > 0, h0[...], received[...])
        attend_body(h, wqkv, wout, small, lens, half, qkv, probs, mixed, normal1, inverse1, u)
        leave(range(7))
        feed_body(u, wup, wdown, small, slope, active, normal2, inverse2, y)
        leave(range(7, 12))
        enter.wait()
        upstream = raw[...].reshape(ROWS, WIDTH).astype(F32)
        top_back_body(upstream, small, normal2, inverse2, gr2, gz, gsmall)
        feed_back_body(gr2, gz, wup, wdown, small, slope, normal1, inverse1, ga, gr1, gb, gsmall)
        heads_back_body(gb, wout, qkv, probs, gqkv, None, go)
        gh[...] = (gr1[...] + dot_nt(gqkv[...], wqkv.get())).astype(LOW)
        for copy in leaving:
            copy.wait()

    return kernel_call(
        body,
        [VMEM, VMEM, ANY, SMEM, SMEM, SMEM, VMEM, VMEM] + [ANY] * 8,
        KEPT + [shape(ROW_SHAPE)],
        [
            SMALL_SCRATCH,
            pltpu.VMEM(ROW_SHAPE, F32),
            pltpu.VMEM(ROW_SHAPE, LOW),
            pltpu.VMEM(FEED_SHAPE, LOW),
            pltpu.VMEM(ROW_SHAPE, F32),
            pltpu.VMEM(ROW_SHAPE, LOW),
            SMALL_SCRATCH,
            pltpu.VMEM(QKV_SHAPE, LOW),
            pltpu.VMEM(ROW_SHAPE, LOW),
            pltpu.VMEM((2, LENGTH, WIDTH), LOW),
            *ATTEND_WEIGHTS,
            *FEED_WEIGHTS,
            *[pltpu.VMEM(kept.shape, kept.dtype) for kept in KEPT],
            pltpu.SemaphoreType.DMA((4, 2)),
            pltpu.SemaphoreType.DMA((len(KEPT),)),
            pltpu.SemaphoreType.DMA,
        ],
        24 * MACS,
        45000000,
        "middle",
        [ANY] * len(KEPT) + [VMEM],
    )(
        h0, received, cotangent, half, first, lens, *smalls,
        *weights[0], *weights[1], *weights[2], *weights[3],
    )


MIB = 1024 * 1024


def half_columns(ref, which):
    size = ref.shape[1] // 2
    return ref[:, pl.ds(pl.multiple_of(which * size, 128), size)]


def store_folded(target, at, tensor):
    rows, wide = tensor.shape
    for block in range(wide // WIDTH):
        target[at + block * rows : at + (block + 1) * rows, :] = tensor[
            :, block * WIDTH : (block + 1) * WIDTH
        ].astype(LOW)


class Leaving:
    def __init__(self, sems):
        self.sems = sems
        self.copies = []

    def send(self, source, target):
        copy = pltpu.make_async_copy(source, target, self.sems.at[len(self.copies)])
        copy.start()
        self.copies.append(copy)

    def wait(self):
        for copy in self.copies:
            copy.wait()


TOKEN = shape((8, 128), F32)
GRAD_SHAPE = (1536, WIDTH)
GRAD_SCRATCH = pltpu.VMEM(GRAD_SHAPE, LOW)


def back_top(cotangent, returned, half, first, smalls, active, n2, i2):
    def body(cot, returned, half, first, so, sp, active, n2, i2, *rest):
        other, own, gr2, gz, gsmall, vother, vown, small, raw, sem, out_sems = rest
        enter = pltpu.make_async_copy(cot.at[half[0]], raw, sem)
        enter.start()
        pick_halves(half, so, sp, small)
        enter.wait()
        upstream = jnp.where(first[0] > 0, returned[...], raw[...].reshape(ROWS, WIDTH))
        top_back_body(upstream.astype(F32), small, n2, i2, gr2, gz, gsmall)
        leaving = Leaving(out_sems)
        for which, local, target in ((1 - half[0], vother, other), (half[0], vown, own)):
            local[...] = dot_tn(half_columns(active, which), gz[...]).astype(LOW)
            leaving.send(local, target)
        leaving.wait()

    return kernel_call(
        body,
        [ANY, VMEM, SMEM, SMEM, VMEM, VMEM, VMEM, VMEM, VMEM],
        [
            shape(GRAD_SHAPE),
            shape(GRAD_SHAPE),
            shape(ROW_SHAPE, F32),
            shape(ROW_SHAPE),
            shape((2, SMALL), F32),
        ],
        [
            GRAD_SCRATCH,
            GRAD_SCRATCH,
            SMALL_SCRATCH,
            pltpu.VMEM((2, LENGTH, WIDTH), LOW),
            pltpu.SemaphoreType.DMA,
            pltpu.SemaphoreType.DMA((2,)),
        ],
        4 * MACS,
        12000000,
        "back_top",
        [ANY, ANY, VMEM, VMEM, VMEM],
        32 * MIB,
    )(cotangent, returned, half, first, *smalls, active, n2, i2)


def back_feed(gr2, gz, half, weights, smalls, u, slope, n1, i1):
    def body(gr2, gz, half, so, sp, uo, up, do, dp, u, slope, n1, i1, *rest):
        other, own, gr1, gb, gsmall, token, ga, vother, vown, small, wu, wd, sems, out_sems = rest
        wdown = Weight(half[0], do, dp, wd, sems.at[1])
        wup = Weight(half[0], uo, up, wu, sems.at[0])
        pick_halves(half, so, sp, small)
        feed_back_body(gr2, gz, wup, wdown, small, slope, n1, i1, ga, gr1, gb, gsmall)
        leaving = Leaving(out_sems)
        for which, local, target in ((1 - half[0], vother, other), (half[0], vown, own)):
            store_folded(local, 0, dot_tn(half_columns(u, which), ga[...]))
            leaving.send(local, target)
        token[...] = jnp.zeros(token.shape, F32)
        leaving.wait()

    return kernel_call(
        body,
        [VMEM, VMEM, SMEM, VMEM, VMEM] + [ANY] * 4 + [VMEM] * 4,
        [
            shape(GRAD_SHAPE),
            shape(GRAD_SHAPE),
            shape(ROW_SHAPE, F32),
            shape(ROW_SHAPE),
            shape((2, SMALL), F32),
            TOKEN,
        ],
        [
            pltpu.VMEM(FEED_SHAPE, LOW),
            GRAD_SCRATCH,
            GRAD_SCRATCH,
            SMALL_SCRATCH,
            *FEED_WEIGHTS,
            pltpu.SemaphoreType.DMA((2, 2)),
            pltpu.SemaphoreType.DMA((2,)),
        ],
        12 * MACS,
        30000000,
        "back_feed",
        [ANY, ANY, VMEM, VMEM, VMEM, VMEM],
        44 * MIB,
    )(gr2, gz, half, *smalls, *weights[2], *weights[3], u, slope, n1, i1)


def back_heads(gb, half, weights, top_small, low_small, h, qkv, probs, mixed, after):
    def body(gb, half, oo, op, top, low, h, qkv, probs, mixed, after, *rest):
        other, own, small_other, small_own, gqkv, token, go, gqv, vother, vown, wo, sems, out_sems = rest
        wout = Weight(half[0], oo, op, wo, sems)
        heads_back_body(gb, wout, qkv, probs, gqkv, gqv, go)
        leaving = Leaving(out_sems)
        for which, local, target in ((1 - half[0], vother, other), (half[0], vown, own)):
            store_folded(local, 0, dot_tn(half_columns(h, which), gqkv[...]))
            local[1152:, :] = dot_tn(half_columns(mixed, which), gb[...]).astype(LOW)
            leaving.send(local, target)
        for which, target in ((1 - half[0], small_other), (half[0], small_own)):
            target[:, :WIDTH] = gqv[pl.ds(which, 1), :]
            target[:, WIDTH:B_DOWN] = low[pl.ds(which, 1), WIDTH:B_DOWN]
            target[:, B_DOWN:] = top[pl.ds(which, 1), B_DOWN:]
        token[...] = jnp.zeros(token.shape, F32)
        leaving.wait()

    return kernel_call(
        body,
        [VMEM, SMEM] + [ANY] * 2 + [VMEM] * 6 + [ANY],
        [
            shape(GRAD_SHAPE),
            shape(GRAD_SHAPE),
            shape((1, SMALL), F32),
            shape((1, SMALL), F32),
            shape(QKV_SHAPE),
            TOKEN,
        ],
        [
            pltpu.VMEM(ROW_SHAPE, LOW),
            pltpu.VMEM((2, WIDTH), F32),
            GRAD_SCRATCH,
            GRAD_SCRATCH,
            ATTEND_WEIGHTS[1],
            pltpu.SemaphoreType.DMA((2,)),
            pltpu.SemaphoreType.DMA((2,)),
        ],
        6 * MACS,
        16000000,
        "back_heads",
        [ANY, ANY] + [VMEM] * 4,
        36 * MIB,
    )(gb, half, *weights[1], top_small, low_small, h, qkv, probs, mixed, after)


def back_input(gqkv, gr1, half, first, spans, weights, after):
    def body(gqkv, gr1, half, first, spans, qo, qp, after, gh, gmask, token, wq, sems):
        wqkv = Weight(half[0], qo, qp, wq, sems)
        full = gr1[...] + dot_nt(gqkv[...], wqkv.get())
        dropped = span_rows(spans, half) & (first[0] > 0)
        zero = jnp.zeros_like(full)
        gh[...] = jnp.where(dropped, zero, full).astype(LOW)
        gmask[...] = column_sum(jnp.where(dropped, full, zero))
        token[...] = jnp.zeros(token.shape, F32)

    return kernel_call(
        body,
        [VMEM, VMEM, SMEM, SMEM, SMEM] + [ANY] * 3,
        [shape(ROW_SHAPE), shape((1, WIDTH), F32), TOKEN],
        [ATTEND_WEIGHTS[0], pltpu.SemaphoreType.DMA((2,))],
        3 * MACS,
        6000000,
        "back_input",
        None,
        18 * MIB,
    )(gqkv, gr1, half, first, spans, *weights[0], after)


TAIL = 16
BLOCK = 96


def add_rows(target, sources, at, rows):
    for start in range(0, rows, BLOCK):
        size = min(BLOCK, rows - start)
        place = pl.ds(at + start, size)
        if not isinstance(at, int):
            place = pl.ds(pl.multiple_of(at + start, 16), size)
        total = sources[0][place, :].astype(F32)
        for source in sources[1:]:
            total = total + source[place, :].astype(F32)
        target[start : start + size, :] = total.astype(LOW)


def ordered(name, body, ins, outs, where, after, out_specs=None, scratch=()):
    count, made = len(ins), len(outs)

    def kernel(where, after, *refs):
        refs[count + made][...] = jnp.zeros(TOKEN.shape, F32)
        body(where, refs[:count], refs[count : count + made] + refs[count + made + 1 :])

    moved = 2 * sum(math.prod(each.shape) for each in list(ins) + list(outs))
    result = kernel_call(
        kernel,
        [SMEM, ANY] + [VMEM] * count,
        list(outs) + [TOKEN],
        list(scratch),
        moved,
        moved,
        name,
        (out_specs or [VMEM] * made) + [VMEM],
        16 * MIB,
    )(where, after, *ins)
    return result[:made], result[made]


def partner(x, axis, bit):
    return lax.ppermute(x, axis, [(i, i ^ 1 << bit) for i in range(lax.axis_size(axis))])


def moved_on(index, axis, steps):
    z, x, y = index // 8, index // 2 % 4, index % 2
    if axis == "z":
        z = (z + steps) % 4
    elif axis == "x":
        x = (x + steps) % 4
    else:
        y ^= 1
    return z * 8 + x * 2 + y


def shift(value, level, steps):
    pairs = []
    for section in range(4):
        axis = "y" if level is None else "zx"[(section + level) % 2]
        for index in range(32):
            pairs.append((section * 32 + index, section * 32 + moved_on(index, axis, steps)))
    return lax.ppermute(value, ("section", "dp"), pairs)


def ring_places(core):
    index = lax.axis_index("dp")
    z, x = index // 8, index // 2 % 4
    return jnp.stack([jnp.where(core == 0, z, x), jnp.where(core == 0, x, z)]).astype(jnp.int32)


class Chain:
    def __init__(self, name, where, tail=0):
        self.name = name
        self.where = where
        self.tail = tail
        self.rows = GRAD_SHAPE[0]

    def kernel(self, name, body, ins, outs, token, *more):
        return ordered(self.name + name, body, ins, outs, self.where, token, *more)

    def scatter(self, level):
        self.sent = [shift(send, level, steps) for steps, send in zip((1, 2, 3), self.sends)]

    def start(self, own, got, token, tail_ins=(), tail_body=None):
        rows, extra = self.rows // 4, self.tail

        def body(where, ins, outs):
            if extra:
                tail = tail_body(ins[2:])
            for steps in range(4):
                quarter = (where[0] + steps) % 4
                add_rows(outs[steps], ins[:2], quarter * rows, rows)
                if extra:
                    outs[steps][rows:, :] = tail

        (self.keep, *self.sends), token = self.kernel(
            "start", body, (own, got) + tuple(tail_ins), [shape((rows + extra, WIDTH))] * 4, token
        )
        self.rows = rows
        self.scatter(0)
        return token

    def again(self, token):
        whole_rows, rows, extra = self.rows, self.rows // 4, self.tail

        def body(where, ins, outs):
            for steps in range(4):
                quarter = (where[1] + steps) % 4
                add_rows(outs[steps], ins, quarter * rows, rows)
            if extra:
                total = ins[0][whole_rows:, :].astype(F32)
                for each in ins[1:]:
                    total = total + each[whole_rows:, :].astype(F32)
                for out in outs:
                    out[rows:, :] = total.astype(LOW)

        (self.keep, *self.sends), token = self.kernel(
            "again", body, (self.keep, *self.sent), [shape((rows + extra, WIDTH))] * 4, token
        )
        self.rows = rows
        self.scatter(1)
        return token

    def across(self, token):
        rows = self.rows + self.tail

        def body(where, ins, outs):
            add_rows(outs[0], ins, 0, rows)

        (self.keep,), token = self.kernel(
            "across", body, (self.keep, *self.sent), [shape((rows, WIDTH))], token
        )
        self.got = shift(self.keep, None, 0)
        return token

    def gather(self, level):
        self.sent = [shift(self.value, level, steps) for steps in (1, 2, 3)]

    def total(self, token):
        rows, extra = self.rows, self.tail

        def body(where, ins, outs):
            add_rows(outs[0], ins, 0, rows)
            if extra:
                outs[1][...] = (ins[0][rows:, :].astype(F32) + ins[1][rows:, :].astype(F32)).astype(LOW)

        outs = [shape((rows, WIDTH))] + ([shape((extra, WIDTH))] if extra else [])
        results, token = self.kernel("total", body, (self.keep, self.got), outs, token)
        self.value = results[0]
        self.tail_sum = results[1] if extra else None
        self.gather(1)
        return token

    def back(self, token, more_ins=(), more_outs=(), more_body=None):
        rows = self.rows

        def body(where, ins, outs):
            for steps in range(4):
                quarter = (where[1] - steps + 4) % 4
                outs[0][pl.ds(pl.multiple_of(quarter * rows, 16), rows), :] = ins[steps][...]
            if more_body is not None:
                more_body(ins[4:], outs[1:])

        (self.value, *more), token = self.kernel(
            "back",
            body,
            (self.value, *self.sent) + tuple(more_ins),
            [shape((4 * rows, WIDTH))] + list(more_outs),
            token,
        )
        self.rows = 4 * rows
        self.gather(0)
        return more, token

    def finish(self, token, outs, by_rows):
        rows = self.rows

        def body(where, ins, refs):
            targets, wide, sems = refs[: len(outs)], refs[-2], refs[-1]
            for steps in range(4):
                quarter = (where[0] - steps + 4) % 4
                wide[steps] = ins[steps][...].astype(F32)

                def copy(target):
                    return pltpu.make_async_copy(wide.at[steps], target, sems.at[steps])

                at = pl.multiple_of(quarter * rows, 128)
                if by_rows:
                    copy(targets[0].at[pl.ds(at, rows)]).start()
                elif len(targets) == 1:
                    columns = pl.multiple_of(quarter * WIDTH, 128)
                    copy(targets[0].at[:, pl.ds(columns, WIDTH)]).start()
                else:

                    @pl.when(quarter < 3)
                    def _():
                        columns = pl.multiple_of(quarter * WIDTH, 128)
                        copy(targets[0].at[:, pl.ds(columns, WIDTH)]).start()

                    @pl.when(quarter == 3)
                    def _():
                        copy(targets[1]).start()

            for steps in range(4):
                if by_rows:
                    target = targets[0].at[pl.ds(0, rows)]
                else:
                    target = targets[0].at[:, pl.ds(0, WIDTH)]
                pltpu.make_async_copy(wide.at[steps], target, sems.at[steps]).wait()

        return self.kernel(
            "finish",
            body,
            (self.value, *self.sent),
            outs,
            token,
            [ANY] * len(outs),
            (pltpu.VMEM((4, rows, WIDTH), F32), pltpu.SemaphoreType.DMA((4,))),
        )


def pack_vectors(vectors):
    size = sum(vector.shape[0] for vector in vectors)
    total = jnp.zeros((size,), F32)
    at = 0
    for vector in vectors:
        total = total + jnp.pad(vector.astype(F32), (at, size - at - vector.shape[0]))
        at += vector.shape[0]
    return total.reshape(1, size)


def per_device(
    inputs,
    cotangent,
    lengths,
    cdr_spans,
    mask_vector,
    w_qkv,
    qv_bias,
    w_out,
    b_out,
    norm1_gain,
    norm1_bias,
    w_up,
    b_up,
    w_down,
    b_down,
    norm2_gain,
    norm2_bias,
):
    section_index = lax.axis_index("section")
    core = section_index % 2
    half = core.astype(jnp.int32).reshape(1)
    first = (section_index < 2).astype(jnp.int32).reshape(1)
    where = ring_places(core)
    small = pack_vectors(
        (
            qv_bias,
            b_out,
            norm1_gain,
            norm1_bias,
            b_up,
            b_down,
            norm2_gain,
            norm2_bias,
            mask_vector,
        )
    )
    smalls = (small, partner(small, "section", 0))
    weights = [(tensor, partner(tensor, "section", 0)) for tensor in (w_qkv, w_out, w_up, w_down)]

    u, h0 = attend_first(inputs, half, lengths, cdr_spans, weights, smalls)
    first_out = feed_first(u, half, weights, smalls)
    received = lax.ppermute(first_out, "section", [(0, 2), (1, 3)])
    kept = middle(h0, received, cotangent, half, first, lengths, weights, smalls)
    h, qkv, probs, mixed, normal1, inverse1, u, slope, active, normal2, inverse2, output = kept[:12]
    returned = lax.ppermute(kept[12], "section", [(2, 0), (3, 1)])

    a_other, a_own, gr2, gz, top_small = back_top(
        cotangent, returned, half, first, smalls, active, normal2, inverse2
    )
    a_got = partner(a_other, "section", 0)
    b_other, b_own, gr1, gb, low_small, token = back_feed(
        gr2, gz, half, weights, smalls, u, slope, normal1, inverse1
    )
    b_got = partner(b_other, "section", 0)
    a, b, y = Chain("a_", where), Chain("b_", where), Chain("y_", where, TAIL)
    token = a.start(a_own, a_got, token)
    y_other, y_own, small_other, small_own, gqkv, token = back_heads(
        gb, half, weights, top_small, low_small, h, qkv, probs, mixed, token
    )
    y_got = partner(y_other, "section", 0)
    small_got = partner(small_other, "section", 0)
    token = b.start(b_own, b_got, token)
    token = a.again(token)
    gh, gmask, token = back_input(gqkv, gr1, half, first, cdr_spans, weights, token)

    def tail_rows(ins):
        small_own, small_got, gmask = ins
        total = small_own[...] + small_got[...]
        rows = [total[:, at : at + WIDTH] for at in range(0, SMALL, WIDTH)]
        rows += [gmask[...], jnp.zeros((TAIL - 7, WIDTH), F32)]
        return jnp.concatenate(rows, axis=0).astype(LOW)

    token = y.start(y_own, y_got, token, (small_own, small_got, gmask), tail_rows)
    token = a.across(token)
    token = b.again(token)
    token = a.total(token)
    token = b.across(token)
    _, token = a.back(token)
    token = y.again(token)
    token = b.total(token)
    token = y.across(token)
    _, token = b.back(token)
    token = y.total(token)
    mask_got = partner(y.tail_sum, "section", 0)
    (g_down,), token = a.finish(token, [shape((1536, WIDTH), F32)], True)

    def add_tails(ins, outs):
        outs[0][...] = (ins[0][...].astype(F32) + ins[1][...].astype(F32)).astype(LOW)

    (mask_rows,), token = y.back(
        token, (y.tail_sum, mask_got), (shape((TAIL, WIDTH)),), add_tails
    )
    mask_got = partner(mask_rows, "section", 1)
    mask_grad = mask_rows[6].astype(F32) + mask_got[6].astype(F32)
    (g_up,), token = b.finish(token, [shape((384, 3072), F32)], False)
    (g_qkv, g_out), token = y.finish(
        token, [shape((384, 2304), F32), shape((384, WIDTH), F32)], False
    )

    flat_small = y.tail_sum[:6].reshape(-1).astype(F32)
    out_small = []
    at = 0
    for size in SIZES:
        out_small.append(flat_small[at : at + size])
        at += size
    g_qv, g_bo, g_n1g, g_n1b, g_bu, g_bd, g_n2g, g_n2b = out_small
    return (
        output.reshape(1, 2, LENGTH, WIDTH),
        gh.reshape(1, 2, LENGTH, WIDTH),
        mask_grad,
        g_qkv,
        g_qv,
        g_out,
        g_bo,
        g_n1g,
        g_n1b,
        g_up,
        g_bu,
        g_down,
        g_bd,
        g_n2g,
        g_n2b,
    )


def solution(mesh):
    in_specs = (
        P(None, "dp", None, None),
        P(None, "dp", None, None),
        P(None, "dp"),
        P(None, "dp", None),
        P(),
        P("section", None),
        P("section"),
        P("section", None),
        P("section"),
        P("section"),
        P("section"),
        P("section", None),
        P("section"),
        P("section", None),
        P("section"),
        P("section"),
        P("section"),
    )
    out_specs = (
        P("section", "dp", None, None),
        P("section", "dp", None, None),
        P(),
        P("section", None),
        P("section"),
        P("section", None),
        P("section"),
        P("section"),
        P("section"),
        P("section", None),
        P("section"),
        P("section", None),
        P("section"),
        P("section"),
        P("section"),
    )
    return jax.shard_map(
        per_device, mesh=mesh, in_specs=in_specs, out_specs=out_specs, check_vma=False
    )
```

```python
import functools
import math

import jax
import jax.numpy as jnp
from jax import lax
from jax.experimental import pallas as pl
from jax.experimental.pallas import tpu as pltpu
from jax.sharding import PartitionSpec as P

EPSILON = 1e-05
F32 = jnp.float32
LOW = jnp.bfloat16
WIDTH = 768
LENGTH = 160
ROWS = 320
HIDDEN = 3072
PAIRS = 6
SCALE = 0.125
SIZES = (768, 384, 384, 384, 1536, 384, 384, 384)
QV, B_OUT, N1G, N1B, B_UP, B_DOWN, N2G, N2B = (sum(SIZES[:at]) for at in range(8))
SMALL = sum(SIZES)
VMEM_LIMIT = 58 * 1024 * 1024


def dot_nn(left_side, right_side):
    return jnp.dot(left_side, right_side, preferred_element_type=F32)


def dot_nt(left_side, right_side):
    return lax.dot_general(
        left_side, right_side, (((1,), (1,)), ((), ())), preferred_element_type=F32
    )


def dot_tn(left_side, right_side):
    return lax.dot_general(
        left_side, right_side, (((0,), (0,)), ((), ())), preferred_element_type=F32
    )


class Weight:
    def __init__(self, half, own, other, dest, sems):
        rows = own.shape[0]
        self.dest = dest
        self.copies = [
            pltpu.make_async_copy(own, dest.at[pl.ds(half * rows, rows)], sems.at[0]),
            pltpu.make_async_copy(other, dest.at[pl.ds((1 - half) * rows, rows)], sems.at[1]),
        ]
        for copy in self.copies:
            copy.start()

    def get(self):
        for copy in self.copies:
            copy.wait()
        self.copies = []
        return self.dest[...]


def whole(smalls, at, size):
    return jnp.concatenate([smalls[0:1, at : at + size], smalls[1:2, at : at + size]], axis=1)


def split_heads(tensor):
    lane = lax.broadcasted_iota(jnp.int32, tensor.shape, 1)
    zero = jnp.zeros_like(tensor)
    return jnp.concatenate(
        [jnp.where(lane < 64, tensor, zero), jnp.where(lane < 64, zero, tensor)], axis=0
    )


def join_heads(tensor):
    lane = lax.broadcasted_iota(jnp.int32, (LENGTH, 128), 1)
    return jnp.where(lane < 64, tensor[:LENGTH], tensor[LENGTH:])


def normalize(values):
    center = values - jnp.mean(values, axis=-1, keepdims=True)
    spread = jnp.mean(center * center, axis=-1, keepdims=True)
    inverse = lax.rsqrt(spread + EPSILON)
    return center * inverse, inverse


def normalize_back(upstream, gain, normal, inverse):
    scaled = upstream * gain
    first = jnp.mean(scaled, axis=-1, keepdims=True)
    second = jnp.mean(scaled * normal, axis=-1, keepdims=True)
    return inverse * (scaled - first - normal * second)


def gelu_parts(values):
    size = jnp.abs(values)
    below = 1.0 + (0.3275911 * math.sqrt(0.5)) * size
    t = pl.reciprocal(below, approx=True)
    t = t * (2.0 - below * t)
    series = t * (
        0.5 * 0.254829592
        + t
        * (
            0.5 * -0.284496736
            + t * (0.5 * 1.421413741 + t * (0.5 * -1.453152027 + t * (0.5 * 1.061405429)))
        )
    )
    bell = jnp.exp(-0.5 * values * values)
    tail = series * bell
    share = jnp.where(values >= 0.0, 1.0 - tail, tail)
    return values * share, share + values * bell * (1.0 / math.sqrt(2.0 * math.pi))


def column_sum(values):
    return jnp.sum(values, axis=0, keepdims=True)


def put_halves(target, at, row):
    size = row.shape[1] // 2
    target[0:1, at : at + size] = row[:, :size]
    target[1:2, at : at + size] = row[:, size:]


def places():
    for index in range(2 * PAIRS):
        chain, pair = divmod(index, PAIRS)
        rows = pl.ds(chain * LENGTH, LENGTH)
        yield index, chain, rows, [pl.ds((pair + block * PAIRS) * 128, 128) for block in range(3)]


def attend_body(h, wqkv, wout, smalls, lens, half, qkv, probs, mixed, normal1, inverse1, u):
    x = h[...]
    bias = jnp.concatenate(
        [smalls[0:1, :WIDTH], jnp.zeros((1, WIDTH), F32), smalls[1:2, :WIDTH]], axis=1
    )
    qkv[...] = (dot_nn(x, wqkv.get()) + bias).astype(LOW)
    for index, chain, rows, (at_q, at_k, at_v) in places():
        scores = dot_nt(split_heads(qkv[rows, at_q]), qkv[rows, at_k]) * SCALE
        key = lax.broadcasted_iota(jnp.int32, scores.shape, 1)
        scores = jnp.where(key < lens[half[0], chain], scores, -1000000000.0)
        grown = jnp.exp(scores - jnp.max(scores, axis=-1, keepdims=True))
        weights = (grown * (1.0 / jnp.sum(grown, axis=-1, keepdims=True))).astype(LOW)
        if probs is not None:
            probs[index] = weights
        mixed[rows, at_q] = join_heads(dot_nn(weights, qkv[rows, at_v])).astype(LOW)
    branch = dot_nn(mixed[...], wout.get()) + whole(smalls, B_OUT, 384)
    normal, inverse = normalize(x.astype(F32) + branch)
    if normal1 is not None:
        normal1[...] = normal
        inverse1[...] = inverse
    u[...] = (normal * whole(smalls, N1G, 384) + whole(smalls, N1B, 384)).astype(LOW)


CHUNK = 1024


def feed_body(u, wup, wdown, smalls, slope, active, normal2, inverse2, y):
    x = u[...]
    bias = whole(smalls, B_UP, 1536)
    up = wup.get()
    for at in range(0, HIDDEN, CHUNK):
        grown, tangent = gelu_parts(dot_nn(x, up[:, at : at + CHUNK]) + bias[:, at : at + CHUNK])
        active[:, at : at + CHUNK] = grown.astype(LOW)
        if slope is not None:
            slope[:, at : at + CHUNK] = tangent.astype(LOW)
    total = x.astype(F32) + whole(smalls, B_DOWN, 384) + dot_nn(active[...], wdown.get())
    normal, inverse = normalize(total)
    if normal2 is not None:
        normal2[...] = normal
        inverse2[...] = inverse
    y[...] = (normal * whole(smalls, N2G, 384) + whole(smalls, N2B, 384)).astype(LOW)


def top_back_body(up, smalls, normal2, inverse2, gr2, gz, gsmall):
    normal = normal2[...]
    put_halves(gsmall, N2G, column_sum(up * normal))
    put_halves(gsmall, N2B, column_sum(up))
    grad = normalize_back(up, whole(smalls, N2G, 384), normal, inverse2[...])
    z = grad.astype(LOW)
    gz[...] = z
    put_halves(gsmall, B_DOWN, column_sum(z.astype(F32)))
    gr2[...] = grad


def feed_back_body(gr2, gz, wup, wdown, smalls, slope, normal1, inverse1, ga, gr1, gb, gsmall):
    z = gz[...]
    down = wdown.get()
    sums = []
    for at in range(0, HIDDEN, CHUNK):
        inner = dot_nt(z, down[at : at + CHUNK, :]) * slope[:, at : at + CHUNK].astype(F32)
        a = inner.astype(LOW)
        ga[:, at : at + CHUNK] = a
        sums.append(column_sum(a.astype(F32)))
    put_halves(gsmall, B_UP, jnp.concatenate(sums, axis=1))
    up = gr2[...] + dot_nt(ga[...], wup.get())
    normal = normal1[...]
    put_halves(gsmall, N1G, column_sum(up * normal))
    put_halves(gsmall, N1B, column_sum(up))
    grad = normalize_back(up, whole(smalls, N1G, 384), normal, inverse1[...])
    gr1[...] = grad
    b = grad.astype(LOW)
    gb[...] = b
    put_halves(gsmall, B_OUT, column_sum(b.astype(F32)))


def heads_back_body(gb, wout, qkv, probs, gqkv, gqv, go):
    go[...] = dot_nt(gb[...], wout.get()).astype(LOW)
    for index, chain, rows, (at_q, at_k, at_v) in places():
        k = qkv[rows, at_k]
        g = split_heads(go[rows, at_q])
        weights = probs[index]
        wide = weights.astype(F32)
        inner = dot_nt(g, qkv[rows, at_v])
        inner = wide * (inner - jnp.sum(wide * inner, axis=-1, keepdims=True))
        s = inner.astype(LOW)
        gqkv[rows, at_q] = (join_heads(dot_nn(s, k)) * SCALE).astype(LOW)
        gqkv[rows, at_k] = (dot_tn(s, split_heads(qkv[rows, at_q])) * SCALE).astype(LOW)
        gqkv[rows, at_v] = dot_tn(weights, g).astype(LOW)
    if gqv is not None:
        gqv[0:1, :] = column_sum(gqkv[:, :WIDTH].astype(F32))
        gqv[1:2, :] = column_sum(gqkv[:, 2 * WIDTH :].astype(F32))


def span_rows(spans, half):
    row = lax.broadcasted_iota(jnp.int32, (ROWS, 1), 0)
    inside = row < 0
    for chain in range(2):
        start = spans[half[0], chain, 0] + chain * LENGTH
        end = spans[half[0], chain, 1] + chain * LENGTH
        inside = inside | ((row >= start) & (row < end))
    return inside


def pick_halves(half, own, other, smalls):
    low = half[0] == 0
    smalls[0:1, :] = jnp.where(low, own[:, :SMALL], other[:, :SMALL])
    smalls[1:2, :] = jnp.where(low, other[:, :SMALL], own[:, :SMALL])


VMEM = pl.BlockSpec(memory_space=pltpu.VMEM)
SMEM = pl.BlockSpec(memory_space=pltpu.SMEM)
ANY = pl.BlockSpec(memory_space=pl.ANY)
SMALL_SCRATCH = pltpu.VMEM((2, SMALL), F32)
QKV_SHAPE = (ROWS, 3 * WIDTH)
PROBS_SHAPE = (2 * PAIRS, 2 * LENGTH, LENGTH)
ROW_SHAPE = (ROWS, WIDTH)
FEED_SHAPE = (ROWS, HIDDEN)
MACS = ROWS * WIDTH * WIDTH * 2
ATTEND_WEIGHTS = [pltpu.VMEM((WIDTH, 3 * WIDTH), LOW), pltpu.VMEM((WIDTH, WIDTH), LOW)]
FEED_WEIGHTS = [pltpu.VMEM((WIDTH, HIDDEN), LOW), pltpu.VMEM((HIDDEN, WIDTH), LOW)]


def shape(dims, kind=LOW):
    return jax.ShapeDtypeStruct(dims, kind)


def kernel_call(body, ins, outs, scratch, flops, moved, name, out_specs=None, grant=VMEM_LIMIT):
    return pl.pallas_call(
        body,
        in_specs=ins,
        out_specs=out_specs or [VMEM] * len(outs),
        out_shape=outs,
        scratch_shapes=scratch,
        compiler_params=pltpu.CompilerParams(vmem_limit_bytes=grant),
        cost_estimate=pl.CostEstimate(flops=flops, bytes_accessed=moved, transcendentals=0),
        name=name,
    )


def attend_first(inputs, half, lens, spans, weights, smalls):
    def body(x, half, lens, spans, so, sp, qo, qp, oo, op, u, h, raw, small, qkv, mixed, wq, wo, sems):
        enter = pltpu.make_async_copy(x.at[half[0]], raw, sems.at[2, 0])
        enter.start()
        wqkv = Weight(half[0], qo, qp, wq, sems.at[0])
        wout = Weight(half[0], oo, op, wo, sems.at[1])
        pick_halves(half, so, sp, small)
        enter.wait()
        mask = so[:, SMALL:].astype(LOW)
        h[...] = jnp.where(span_rows(spans, half), mask, raw[...].reshape(ROWS, WIDTH))
        attend_body(h, wqkv, wout, small, lens, half, qkv, None, mixed, None, None, u)

    return kernel_call(
        body,
        [ANY, SMEM, SMEM, SMEM, VMEM, VMEM] + [ANY] * 4,
        [shape(ROW_SHAPE), shape(ROW_SHAPE)],
        [
            pltpu.VMEM((2, LENGTH, WIDTH), LOW),
            SMALL_SCRATCH,
            pltpu.VMEM(QKV_SHAPE, LOW),
            pltpu.VMEM(ROW_SHAPE, LOW),
            *ATTEND_WEIGHTS,
            pltpu.SemaphoreType.DMA((3, 2)),
        ],
        40 * MACS,
        80000000,
        "attend_first",
    )(inputs, half, lens, spans, *smalls, *weights[0], *weights[1])


def feed_first(u, half, weights, smalls):
    def body(u, half, so, sp, uo, up, do, dp, y, small, active, wu, wd, sems):
        wup = Weight(half[0], uo, up, wu, sems.at[0])
        wdown = Weight(half[0], do, dp, wd, sems.at[1])
        pick_halves(half, so, sp, small)
        feed_body(u, wup, wdown, small, None, active, None, None, y)

    return kernel_call(
        body,
        [VMEM, SMEM, VMEM, VMEM] + [ANY] * 4,
        [shape(ROW_SHAPE)],
        [
            SMALL_SCRATCH,
            pltpu.VMEM(FEED_SHAPE, LOW),
            *FEED_WEIGHTS,
            pltpu.SemaphoreType.DMA((2, 2)),
        ],
        8 * MACS,
        14000000,
        "feed_first",
    )(u, half, *smalls, *weights[2], *weights[3])[0]


KEPT = [
    shape(ROW_SHAPE),
    shape(QKV_SHAPE),
    shape(PROBS_SHAPE),
    shape(ROW_SHAPE),
    shape(ROW_SHAPE, F32),
    shape((ROWS, 1), F32),
    shape(ROW_SHAPE),
    shape(FEED_SHAPE),
    shape(FEED_SHAPE),
    shape(ROW_SHAPE, F32),
    shape((ROWS, 1), F32),
    shape(ROW_SHAPE),
]


def middle(h0, received, cotangent, half, first, lens, weights, smalls):
    def body(h0, received, cot, half, first, lens, so, sp, qo, qp, oo, op, uo, up, do, dp, *rest):
        outs, rest = rest[: len(KEPT)], rest[len(KEPT) :]
        gh, small, gr2, gz, ga, gr1, gb, gsmall, gqkv, go, raw, wq, wo, wu, wd = rest[:15]
        keeps, sems, out_sems, raw_sem = rest[15:-3], *rest[-3:]
        h, qkv, probs, mixed, normal1, inverse1, u, slope, active, normal2, inverse2, y = keeps
        wqkv = Weight(half[0], qo, qp, wq, sems.at[0])
        wout = Weight(half[0], oo, op, wo, sems.at[1])
        wup = Weight(half[0], uo, up, wu, sems.at[2])
        wdown = Weight(half[0], do, dp, wd, sems.at[3])
        enter = pltpu.make_async_copy(cot.at[half[0]], raw, raw_sem)
        enter.start()
        pick_halves(half, so, sp, small)
        leaving = []

        def leave(places):
            for place in places:
                copy = pltpu.make_async_copy(keeps[place], outs[place], out_sems.at[place])
                copy.start()
                leaving.append(copy)

        h[...] = jnp.where(first[0] > 0, h0[...], received[...])
        attend_body(h, wqkv, wout, small, lens, half, qkv, probs, mixed, normal1, inverse1, u)
        leave(range(7))
        feed_body(u, wup, wdown, small, slope, active, normal2, inverse2, y)
        leave(range(7, 12))
        enter.wait()
        upstream = raw[...].reshape(ROWS, WIDTH).astype(F32)
        top_back_body(upstream, small, normal2, inverse2, gr2, gz, gsmall)
        feed_back_body(gr2, gz, wup, wdown, small, slope, normal1, inverse1, ga, gr1, gb, gsmall)
        heads_back_body(gb, wout, qkv, probs, gqkv, None, go)
        gh[...] = (gr1[...] + dot_nt(gqkv[...], wqkv.get())).astype(LOW)
        for copy in leaving:
            copy.wait()

    return kernel_call(
        body,
        [VMEM, VMEM, ANY, SMEM, SMEM, SMEM, VMEM, VMEM] + [ANY] * 8,
        KEPT + [shape(ROW_SHAPE)],
        [
            SMALL_SCRATCH,
            pltpu.VMEM(ROW_SHAPE, F32),
            pltpu.VMEM(ROW_SHAPE, LOW),
            pltpu.VMEM(FEED_SHAPE, LOW),
            pltpu.VMEM(ROW_SHAPE, F32),
            pltpu.VMEM(ROW_SHAPE, LOW),
            SMALL_SCRATCH,
            pltpu.VMEM(QKV_SHAPE, LOW),
            pltpu.VMEM(ROW_SHAPE, LOW),
            pltpu.VMEM((2, LENGTH, WIDTH), LOW),
            *ATTEND_WEIGHTS,
            *FEED_WEIGHTS,
            *[pltpu.VMEM(kept.shape, kept.dtype) for kept in KEPT],
            pltpu.SemaphoreType.DMA((4, 2)),
            pltpu.SemaphoreType.DMA((len(KEPT),)),
            pltpu.SemaphoreType.DMA,
        ],
        24 * MACS,
        45000000,
        "middle",
        [ANY] * len(KEPT) + [VMEM],
    )(
        h0, received, cotangent, half, first, lens, *smalls,
        *weights[0], *weights[1], *weights[2], *weights[3],
    )


MIB = 1024 * 1024


def half_columns(ref, which):
    size = ref.shape[1] // 2
    return ref[:, pl.ds(pl.multiple_of(which * size, 128), size)]


def store_folded(target, at, tensor):
    rows, wide = tensor.shape
    for block in range(wide // WIDTH):
        target[at + block * rows : at + (block + 1) * rows, :] = tensor[
            :, block * WIDTH : (block + 1) * WIDTH
        ].astype(LOW)


class Leaving:
    def __init__(self, sems):
        self.sems = sems
        self.copies = []

    def send(self, source, target):
        copy = pltpu.make_async_copy(source, target, self.sems.at[len(self.copies)])
        copy.start()
        self.copies.append(copy)

    def wait(self):
        for copy in self.copies:
            copy.wait()


TOKEN = shape((8, 128), F32)
GRAD_SHAPE = (1536, WIDTH)
GRAD_SCRATCH = pltpu.VMEM(GRAD_SHAPE, LOW)


def back_top(cotangent, returned, half, first, smalls, active, n2, i2):
    def body(cot, returned, half, first, so, sp, active, n2, i2, *rest):
        other, own, gr2, gz, gsmall, vother, vown, small, raw, sem, out_sems = rest
        enter = pltpu.make_async_copy(cot.at[half[0]], raw, sem)
        enter.start()
        pick_halves(half, so, sp, small)
        enter.wait()
        upstream = jnp.where(first[0] > 0, returned[...], raw[...].reshape(ROWS, WIDTH))
        top_back_body(upstream.astype(F32), small, n2, i2, gr2, gz, gsmall)
        leaving = Leaving(out_sems)
        for which, local, target in ((1 - half[0], vother, other), (half[0], vown, own)):
            local[...] = dot_tn(half_columns(active, which), gz[...]).astype(LOW)
            leaving.send(local, target)
        leaving.wait()

    return kernel_call(
        body,
        [ANY, VMEM, SMEM, SMEM, VMEM, VMEM, VMEM, VMEM, VMEM],
        [
            shape(GRAD_SHAPE),
            shape(GRAD_SHAPE),
            shape(ROW_SHAPE, F32),
            shape(ROW_SHAPE),
            shape((2, SMALL), F32),
        ],
        [
            GRAD_SCRATCH,
            GRAD_SCRATCH,
            SMALL_SCRATCH,
            pltpu.VMEM((2, LENGTH, WIDTH), LOW),
            pltpu.SemaphoreType.DMA,
            pltpu.SemaphoreType.DMA((2,)),
        ],
        4 * MACS,
        12000000,
        "back_top",
        [ANY, ANY, VMEM, VMEM, VMEM],
        32 * MIB,
    )(cotangent, returned, half, first, *smalls, active, n2, i2)


def back_feed(gr2, gz, half, weights, smalls, u, slope, n1, i1):
    def body(gr2, gz, half, so, sp, uo, up, do, dp, u, slope, n1, i1, *rest):
        other, own, gr1, gb, gsmall, token, ga, vother, vown, small, wu, wd, sems, out_sems = rest
        wdown = Weight(half[0], do, dp, wd, sems.at[1])
        wup = Weight(half[0], uo, up, wu, sems.at[0])
        pick_halves(half, so, sp, small)
        feed_back_body(gr2, gz, wup, wdown, small, slope, n1, i1, ga, gr1, gb, gsmall)
        leaving = Leaving(out_sems)
        for which, local, target in ((1 - half[0], vother, other), (half[0], vown, own)):
            store_folded(local, 0, dot_tn(half_columns(u, which), ga[...]))
            leaving.send(local, target)
        token[...] = jnp.zeros(token.shape, F32)
        leaving.wait()

    return kernel_call(
        body,
        [VMEM, VMEM, SMEM, VMEM, VMEM] + [ANY] * 4 + [VMEM] * 4,
        [
            shape(GRAD_SHAPE),
            shape(GRAD_SHAPE),
            shape(ROW_SHAPE, F32),
            shape(ROW_SHAPE),
            shape((2, SMALL), F32),
            TOKEN,
        ],
        [
            pltpu.VMEM(FEED_SHAPE, LOW),
            GRAD_SCRATCH,
            GRAD_SCRATCH,
            SMALL_SCRATCH,
            *FEED_WEIGHTS,
            pltpu.SemaphoreType.DMA((2, 2)),
            pltpu.SemaphoreType.DMA((2,)),
        ],
        240 * MACS,
        600000000,
        "back_feed",
        [ANY, ANY, VMEM, VMEM, VMEM, VMEM],
        44 * MIB,
    )(gr2, gz, half, *smalls, *weights[2], *weights[3], u, slope, n1, i1)


def back_heads(gb, half, weights, top_small, low_small, h, qkv, probs, mixed, after):
    def body(gb, half, oo, op, top, low, h, qkv, probs, mixed, after, *rest):
        other, own, small_other, small_own, gqkv, token, go, gqv, vother, vown, wo, sems, out_sems = rest
        wout = Weight(half[0], oo, op, wo, sems)
        heads_back_body(gb, wout, qkv, probs, gqkv, gqv, go)
        leaving = Leaving(out_sems)
        for which, local, target in ((1 - half[0], vother, other), (half[0], vown, own)):
            store_folded(local, 0, dot_tn(half_columns(h, which), gqkv[...]))
            local[1152:, :] = dot_tn(half_columns(mixed, which), gb[...]).astype(LOW)
            leaving.send(local, target)
        for which, target in ((1 - half[0], small_other), (half[0], small_own)):
            target[:, :WIDTH] = gqv[pl.ds(which, 1), :]
            target[:, WIDTH:B_DOWN] = low[pl.ds(which, 1), WIDTH:B_DOWN]
            target[:, B_DOWN:] = top[pl.ds(which, 1), B_DOWN:]
        token[...] = jnp.zeros(token.shape, F32)
        leaving.wait()

    return kernel_call(
        body,
        [VMEM, SMEM] + [ANY] * 2 + [VMEM] * 6 + [ANY],
        [
            shape(GRAD_SHAPE),
            shape(GRAD_SHAPE),
            shape((1, SMALL), F32),
            shape((1, SMALL), F32),
            shape(QKV_SHAPE),
            TOKEN,
        ],
        [
            pltpu.VMEM(ROW_SHAPE, LOW),
            pltpu.VMEM((2, WIDTH), F32),
            GRAD_SCRATCH,
            GRAD_SCRATCH,
            ATTEND_WEIGHTS[1],
            pltpu.SemaphoreType.DMA((2,)),
            pltpu.SemaphoreType.DMA((2,)),
        ],
        120 * MACS,
        320000000,
        "back_heads",
        [ANY, ANY] + [VMEM] * 4,
        36 * MIB,
    )(gb, half, *weights[1], top_small, low_small, h, qkv, probs, mixed, after)


def back_input(gqkv, gr1, half, first, spans, weights, after):
    def body(gqkv, gr1, half, first, spans, qo, qp, after, gh, gmask, token, wq, sems):
        wqkv = Weight(half[0], qo, qp, wq, sems)
        full = gr1[...] + dot_nt(gqkv[...], wqkv.get())
        dropped = span_rows(spans, half) & (first[0] > 0)
        zero = jnp.zeros_like(full)
        gh[...] = jnp.where(dropped, zero, full).astype(LOW)
        gmask[...] = column_sum(jnp.where(dropped, full, zero))
        token[...] = jnp.zeros(token.shape, F32)

    return kernel_call(
        body,
        [VMEM, VMEM, SMEM, SMEM, SMEM] + [ANY] * 3,
        [shape(ROW_SHAPE), shape((1, WIDTH), F32), TOKEN],
        [ATTEND_WEIGHTS[0], pltpu.SemaphoreType.DMA((2,))],
        60 * MACS,
        120000000,
        "back_input",
        None,
        18 * MIB,
    )(gqkv, gr1, half, first, spans, *weights[0], after)


TAIL = 16
BLOCK = 96


def add_rows(target, sources, at, rows):
    for start in range(0, rows, BLOCK):
        size = min(BLOCK, rows - start)
        place = pl.ds(at + start, size)
        if not isinstance(at, int):
            place = pl.ds(pl.multiple_of(at + start, 16), size)
        total = sources[0][place, :].astype(F32)
        for source in sources[1:]:
            total = total + source[place, :].astype(F32)
        target[start : start + size, :] = total.astype(LOW)


def ordered(name, body, ins, outs, where, after, out_specs=None, scratch=()):
    count, made = len(ins), len(outs)

    def kernel(where, after, *refs):
        refs[count + made][...] = jnp.zeros(TOKEN.shape, F32)
        body(where, refs[:count], refs[count : count + made] + refs[count + made + 1 :])

    moved = 1000
    result = kernel_call(
        kernel,
        [SMEM, ANY] + [VMEM] * count,
        list(outs) + [TOKEN],
        list(scratch),
        moved,
        moved,
        name,
        (out_specs or [VMEM] * made) + [VMEM],
        16 * MIB,
    )(where, after, *ins)
    return result[:made], result[made]


def partner(x, axis, bit):
    return lax.ppermute(x, axis, [(i, i ^ 1 << bit) for i in range(lax.axis_size(axis))])


ORDERS = (
    (("zw", "zu", "xw", "xu"), ("xw", "xu", "zw", "zu")),
    (("zu", "zw", "xu", "xw"), ("xu", "xw", "zu", "zw")),
)


def flip_dp(index, bit):
    z, x, y = index // 8, index // 2 % 4, index % 2
    if bit == "zw":
        z ^= 1
    elif bit == "zu":
        z ^= 3
    elif bit == "xw":
        x ^= 1
    elif bit == "xu":
        x ^= 3
    else:
        y ^= 1
    return z * 8 + x * 2 + y


def exchange(value, part, step):
    pairs = []
    for section in range(4):
        bit = "y" if step is None else ORDERS[part][section % 2][step]
        for index in range(32):
            pairs.append((section * 32 + index, section * 32 + flip_dp(index, bit)))
    return lax.ppermute(value, ("section", "dp"), pairs)


def own_bits(core):
    index = lax.axis_index("dp")
    z, x = index // 8, index // 2 % 4
    bits = {
        "zu": z // 2,
        "zw": (z // 2) ^ (z % 2),
        "xu": x // 2,
        "xw": (x // 2) ^ (x % 2),
    }
    table = [
        jnp.where(core == 0, bits[order[0][step]], bits[order[1][step]])
        for order in ORDERS
        for step in range(4)
    ]
    return jnp.stack(table).astype(jnp.int32)


def row_shapes(*counts):
    return [shape((count, WIDTH)) for count in counts]


def add_tail(target, rows, sources, at, extra):
    if extra:
        total = sources[0][at : at + extra, :].astype(F32)
        for source in sources[1:]:
            total = total + source[at : at + extra, :].astype(F32)
        target[rows : rows + extra, :] = total.astype(LOW)


class Chain:
    def __init__(self, name, bits, tail=0):
        self.name = name
        self.bits = bits
        self.tail = (0, tail)
        self.keep = [None, None]
        self.got = [None, None]

    def kernel(self, name, body, ins, outs, token, *more):
        return ordered(self.name + name, body, ins, outs, self.bits, token, *more)

    def send(self, part, value, step):
        self.got[part] = exchange(value, part, step)

    def start_part(self, part, own, got, token, at=0, rows=GRAD_SHAPE[0], tail_ins=(), tail_body=None):
        self.rows = rows // 2
        half_rows, extra = self.rows, self.tail[part]

        def body(bits, ins, outs):
            bit = bits[4 * part]
            for target, which in ((outs[1], 1 - bit), (outs[0], bit)):
                add_rows(target, ins[:2], at + which * half_rows, half_rows)
            if extra:
                tail = tail_body(ins[2:])
                for target in outs:
                    target[half_rows:, :] = tail

        (self.keep[part], sent), token = self.kernel(
            "start",
            body,
            (own, got) + tuple(tail_ins),
            row_shapes(*[half_rows + extra] * 2),
            token,
        )
        self.send(part, sent, 0)
        return token

    def halve(self, step, token):
        self.rows //= 2
        rows, tails = self.rows, self.tail

        def body(bits, ins, outs):
            for part in range(2):
                bit = bits[4 * part + step]
                pair = ins[2 * part : 2 * part + 2]
                for target, which in ((outs[2 * part + 1], 1 - bit), (outs[2 * part], bit)):
                    add_rows(target, pair, which * rows, rows)
                    add_tail(target, rows, pair, 2 * rows, tails[part])

        ins = (self.keep[0], self.got[0], self.keep[1], self.got[1])
        counts = [rows + tails[0]] * 2 + [rows + tails[1]] * 2
        outs, token = self.kernel("halve", body, ins, row_shapes(*counts), token)
        for part in range(2):
            self.keep[part] = outs[2 * part]
            self.send(part, outs[2 * part + 1], step)
        return token

    def across(self, token):
        rows, extra = self.rows, self.tail[1]

        def body(bits, ins, outs):
            add_rows(outs[0].at[pl.ds(0, rows)], ins[:2], 0, rows)
            add_rows(outs[0].at[pl.ds(rows, rows)], ins[2:], 0, rows)
            add_tail(outs[0], 2 * rows, ins[2:], rows, extra)

        ins = (self.keep[0], self.got[0], self.keep[1], self.got[1])
        (self.both,), token = self.kernel(
            "across", body, ins, row_shapes(2 * rows + extra), token
        )
        self.both_got = exchange(self.both, 0, None)
        return token

    def part(self, token):
        rows, extra = self.rows, self.tail[1]

        def body(bits, ins, outs):
            add_rows(outs[0], ins, 0, rows)
            add_rows(outs[1], ins, rows, rows)
            if extra:
                add_rows(outs[2], ins, 2 * rows, extra)

        counts = [rows, rows] + ([extra] if extra else [])
        outs, token = self.kernel(
            "part", body, (self.both, self.both_got), row_shapes(*counts), token
        )
        self.keep = list(outs[:2])
        self.tail_sum = outs[2] if extra else None
        for part in range(2):
            self.send(part, self.keep[part], 3)
        return token

    def double(self, step, token, more_ins=(), more_outs=(), more_body=None):
        rows = self.rows

        def body(bits, ins, outs):
            for part in range(2):
                bit = bits[4 * part + step]
                for which, source in ((bit, ins[2 * part]), (1 - bit, ins[2 * part + 1])):
                    outs[part][pl.ds(pl.multiple_of(which * rows, 16), rows), :] = source[...]
            if more_body is not None:
                more_body(ins[4:], outs[2:])

        ins = (self.keep[0], self.got[0], self.keep[1], self.got[1]) + tuple(more_ins)
        results, token = self.kernel(
            "double", body, ins, row_shapes(2 * rows, 2 * rows) + list(more_outs), token
        )
        self.keep, more = list(results[:2]), results[2:]
        self.rows = 2 * rows
        for part in range(2):
            self.send(part, self.keep[part], step - 1)
        return more, token

    def finish(self, token, outs, pieces):
        rows = self.rows

        def body(bits, ins, refs):
            targets, wide, sems = refs[: len(outs)], refs[-2], refs[-1]
            copies = []
            for part in range(2):
                for source, which in ((0, bits[4 * part]), (1, 1 - bits[4 * part])):
                    here = wide.at[part, pl.ds(pl.multiple_of(which * rows, 16), rows)]
                    here[...] = ins[2 * part + source][...].astype(F32)
                at = 0
                for size, place in pieces[part]:
                    copy = pltpu.make_async_copy(
                        wide.at[part, pl.ds(at, size)], place(targets), sems.at[len(copies)]
                    )
                    copy.start()
                    copies.append(copy)
                    at += size
            for copy in copies:
                copy.wait()

        ins = (self.keep[0], self.got[0], self.keep[1], self.got[1])
        count = len(pieces[0]) + len(pieces[1])
        return self.kernel(
            "finish",
            body,
            ins,
            outs,
            token,
            [ANY] * len(outs),
            (pltpu.VMEM((2, 2 * rows, WIDTH), F32), pltpu.SemaphoreType.DMA((count,))),
        )


def pack_vectors(vectors):
    size = sum(vector.shape[0] for vector in vectors)
    total = jnp.zeros((size,), F32)
    at = 0
    for vector in vectors:
        total = total + jnp.pad(vector.astype(F32), (at, size - at - vector.shape[0]))
        at += vector.shape[0]
    return total.reshape(1, size)


def per_device(
    inputs,
    cotangent,
    lengths,
    cdr_spans,
    mask_vector,
    w_qkv,
    qv_bias,
    w_out,
    b_out,
    norm1_gain,
    norm1_bias,
    w_up,
    b_up,
    w_down,
    b_down,
    norm2_gain,
    norm2_bias,
):
    section_index = lax.axis_index("section")
    core = section_index % 2
    half = core.astype(jnp.int32).reshape(1)
    first = (section_index < 2).astype(jnp.int32).reshape(1)
    bits = own_bits(core)
    small = pack_vectors(
        (
            qv_bias,
            b_out,
            norm1_gain,
            norm1_bias,
            b_up,
            b_down,
            norm2_gain,
            norm2_bias,
            mask_vector,
        )
    )
    smalls = (small, partner(small, "section", 0))
    weights = [(tensor, partner(tensor, "section", 0)) for tensor in (w_qkv, w_out, w_up, w_down)]

    u, h0 = attend_first(inputs, half, lengths, cdr_spans, weights, smalls)
    first_out = feed_first(u, half, weights, smalls)
    received = lax.ppermute(first_out, "section", [(0, 2), (1, 3)])
    kept = middle(h0, received, cotangent, half, first, lengths, weights, smalls)
    h, qkv, probs, mixed, normal1, inverse1, u, slope, active, normal2, inverse2, output = kept[:12]
    returned = lax.ppermute(kept[12], "section", [(2, 0), (3, 1)])

    a_other, a_own, gr2, gz, top_small = back_top(
        cotangent, returned, half, first, smalls, active, normal2, inverse2
    )
    a_got = partner(a_other, "section", 0)
    b_other, b_own, gr1, gb, low_small, token = back_feed(
        gr2, gz, half, weights, smalls, u, slope, normal1, inverse1
    )
    b_got = partner(b_other, "section", 0)
    x, y = Chain("x_", bits), Chain("y_", bits, TAIL)
    token = x.start_part(0, a_own, a_got, token)
    token = x.start_part(1, b_own, b_got, token)
    y_other, y_own, small_other, small_own, gqkv, token = back_heads(
        gb, half, weights, top_small, low_small, h, qkv, probs, mixed, token
    )
    y_got = partner(y_other, "section", 0)
    small_got = partner(small_other, "section", 0)
    token = x.halve(1, token)
    gh, gmask, token = back_input(gqkv, gr1, half, first, cdr_spans, weights, token)

    def tail_rows(ins):
        small_own, small_got, gmask = ins
        total = small_own[...] + small_got[...]
        rows = [total[:, at : at + WIDTH] for at in range(0, SMALL, WIDTH)]
        rows += [gmask[...], jnp.zeros((TAIL - 7, WIDTH), F32)]
        return jnp.concatenate(rows, axis=0).astype(LOW)

    token = y.start_part(0, y_own, y_got, token, 0, 768)
    token = y.start_part(
        1, y_own, y_got, token, 768, 768, (small_own, small_got, gmask), tail_rows
    )
    token = x.halve(2, token)
    token = y.halve(1, token)
    token = x.halve(3, token)
    token = y.halve(2, token)
    token = x.across(token)
    token = y.halve(3, token)
    token = x.part(token)
    token = y.across(token)
    _, token = x.double(3, token)
    token = y.part(token)
    mask_got = partner(y.tail_sum, "section", 0)
    _, token = x.double(2, token)

    def add_tails(ins, outs):
        outs[0][...] = (ins[0][...].astype(F32) + ins[1][...].astype(F32)).astype(LOW)

    (mask_rows,), token = y.double(
        3, token, (y.tail_sum, mask_got), row_shapes(TAIL), add_tails
    )
    mask_got = partner(mask_rows, "section", 1)
    _, token = y.double(2, token)
    _, token = x.double(1, token)
    mask_grad = mask_rows[6].astype(F32) + mask_got[6].astype(F32)
    _, token = y.double(1, token)
    columns = [pl.ds(block * WIDTH, WIDTH) for block in range(4)]
    (g_down, g_up), token = x.finish(
        token,
        [shape((1536, WIDTH), F32), shape((384, HIDDEN), F32)],
        (
            [(1536, lambda refs: refs[0])],
            [(384, lambda refs, at=at: refs[1].at[:, at]) for at in columns],
        ),
    )
    (g_qkv, g_out), token = y.finish(
        token,
        [shape((384, 3 * WIDTH), F32), shape((384, WIDTH), F32)],
        (
            [(384, lambda refs, at=at: refs[0].at[:, at]) for at in columns[:2]],
            [(384, lambda refs: refs[0].at[:, columns[2]]), (384, lambda refs: refs[1])],
        ),
    )

    flat_small = y.tail_sum[:6].reshape(-1).astype(F32)
    out_small = []
    at = 0
    for size in SIZES:
        out_small.append(flat_small[at : at + size])
        at += size
    g_qv, g_bo, g_n1g, g_n1b, g_bu, g_bd, g_n2g, g_n2b = out_small
    return (
        output.reshape(1, 2, LENGTH, WIDTH),
        gh.reshape(1, 2, LENGTH, WIDTH),
        mask_grad,
        g_qkv,
        g_qv,
        g_out,
        g_bo,
        g_n1g,
        g_n1b,
        g_up,
        g_bu,
        g_down,
        g_bd,
        g_n2g,
        g_n2b,
    )


def solution(mesh):
    in_specs = (
        P(None, "dp", None, None),
        P(None, "dp", None, None),
        P(None, "dp"),
        P(None, "dp", None),
        P(),
        P("section", None),
        P("section"),
        P("section", None),
        P("section"),
        P("section"),
        P("section"),
        P("section", None),
        P("section"),
        P("section", None),
        P("section"),
        P("section"),
        P("section"),
    )
    out_specs = (
        P("section", "dp", None, None),
        P("section", "dp", None, None),
        P(),
        P("section", None),
        P("section"),
        P("section", None),
        P("section"),
        P("section"),
        P("section"),
        P("section", None),
        P("section"),
        P("section", None),
        P("section"),
        P("section"),
        P("section"),
    )
    return jax.shard_map(
        per_device, mesh=mesh, in_specs=in_specs, out_specs=out_specs, check_vma=False
    )
```

```python
import functools
import math

import jax
import jax.numpy as jnp
from jax import lax
from jax.experimental import pallas as pl
from jax.experimental.pallas import tpu as pltpu
from jax.sharding import PartitionSpec as P

EPSILON = 1e-05
F32 = jnp.float32
LOW = jnp.bfloat16
WIDTH = 768
LENGTH = 160
ROWS = 320
HIDDEN = 3072
PAIRS = 6
SCALE = 0.125
SIZES = (768, 384, 384, 384, 1536, 384, 384, 384)
QV, B_OUT, N1G, N1B, B_UP, B_DOWN, N2G, N2B = (sum(SIZES[:at]) for at in range(8))
SMALL = sum(SIZES)
VMEM_LIMIT = 63 * 1024 * 1024


def dot_nn(left_side, right_side):
    return jnp.dot(left_side, right_side, preferred_element_type=F32)


def dot_nt(left_side, right_side):
    return lax.dot_general(
        left_side, right_side, (((1,), (1,)), ((), ())), preferred_element_type=F32
    )


def dot_tn(left_side, right_side):
    return lax.dot_general(
        left_side, right_side, (((0,), (0,)), ((), ())), preferred_element_type=F32
    )


class Weight:
    def __init__(self, half, own, other, dest, sems):
        rows = own.shape[0]
        self.dest = dest
        self.copies = [
            pltpu.make_async_copy(own, dest.at[pl.ds(half * rows, rows)], sems.at[0]),
            pltpu.make_async_copy(other, dest.at[pl.ds((1 - half) * rows, rows)], sems.at[1]),
        ]
        for copy in self.copies:
            copy.start()

    def get(self):
        for copy in self.copies:
            copy.wait()
        self.copies = []
        return self.dest[...]


def whole(smalls, at, size):
    return jnp.concatenate([smalls[0:1, at : at + size], smalls[1:2, at : at + size]], axis=1)


def split_heads(tensor):
    lane = lax.broadcasted_iota(jnp.int32, tensor.shape, 1)
    zero = jnp.zeros_like(tensor)
    return jnp.concatenate(
        [jnp.where(lane < 64, tensor, zero), jnp.where(lane < 64, zero, tensor)], axis=0
    )


def join_heads(tensor):
    lane = lax.broadcasted_iota(jnp.int32, (LENGTH, 128), 1)
    return jnp.where(lane < 64, tensor[:LENGTH], tensor[LENGTH:])


def normalize(values):
    center = values - jnp.mean(values, axis=-1, keepdims=True)
    spread = jnp.mean(center * center, axis=-1, keepdims=True)
    inverse = lax.rsqrt(spread + EPSILON)
    return center * inverse, inverse


def normalize_back(upstream, gain, normal, inverse):
    scaled = upstream * gain
    first = jnp.mean(scaled, axis=-1, keepdims=True)
    second = jnp.mean(scaled * normal, axis=-1, keepdims=True)
    return inverse * (scaled - first - normal * second)


def gelu_parts(values):
    size = jnp.abs(values)
    below = 1.0 + (0.3275911 * math.sqrt(0.5)) * size
    t = pl.reciprocal(below, approx=True)
    t = t * (2.0 - below * t)
    series = t * (
        0.5 * 0.254829592
        + t
        * (
            0.5 * -0.284496736
            + t * (0.5 * 1.421413741 + t * (0.5 * -1.453152027 + t * (0.5 * 1.061405429)))
        )
    )
    bell = jnp.exp(-0.5 * values * values)
    tail = series * bell
    share = jnp.where(values >= 0.0, 1.0 - tail, tail)
    return values * share, share + values * bell * (1.0 / math.sqrt(2.0 * math.pi))


def column_sum(values):
    return jnp.sum(values, axis=0, keepdims=True)


def put_halves(target, at, row):
    size = row.shape[1] // 2
    target[0:1, at : at + size] = row[:, :size]
    target[1:2, at : at + size] = row[:, size:]


def places():
    for index in range(2 * PAIRS):
        chain, pair = divmod(index, PAIRS)
        rows = pl.ds(chain * LENGTH, LENGTH)
        yield index, chain, rows, [pl.ds((pair + block * PAIRS) * 128, 128) for block in range(3)]


def attend_body(h, wqkv, wout, smalls, lens, half, qkv, probs, mixed, normal1, inverse1, u):
    x = h[...]
    bias = jnp.concatenate(
        [smalls[0:1, :WIDTH], jnp.zeros((1, WIDTH), F32), smalls[1:2, :WIDTH]], axis=1
    )
    qkv[...] = (dot_nn(x, wqkv.get()) + bias).astype(LOW)
    for index, chain, rows, (at_q, at_k, at_v) in places():
        scores = dot_nt(split_heads(qkv[rows, at_q]), qkv[rows, at_k]) * SCALE
        key = lax.broadcasted_iota(jnp.int32, scores.shape, 1)
        scores = jnp.where(key < lens[half[0], chain], scores, -1000000000.0)
        grown = jnp.exp(scores - jnp.max(scores, axis=-1, keepdims=True))
        weights = (grown * (1.0 / jnp.sum(grown, axis=-1, keepdims=True))).astype(LOW)
        if probs is not None:
            probs[index] = weights
        mixed[rows, at_q] = join_heads(dot_nn(weights, qkv[rows, at_v])).astype(LOW)
    branch = dot_nn(mixed[...], wout.get()) + whole(smalls, B_OUT, 384)
    normal, inverse = normalize(x.astype(F32) + branch)
    if normal1 is not None:
        normal1[...] = normal
        inverse1[...] = inverse
    u[...] = (normal * whole(smalls, N1G, 384) + whole(smalls, N1B, 384)).astype(LOW)


CHUNK = 1024


def feed_body(u, wup, wdown, smalls, slope, active, normal2, inverse2, y):
    x = u[...]
    bias = whole(smalls, B_UP, 1536)
    up = wup.get()
    for at in range(0, HIDDEN, CHUNK):
        grown, tangent = gelu_parts(dot_nn(x, up[:, at : at + CHUNK]) + bias[:, at : at + CHUNK])
        active[:, at : at + CHUNK] = grown.astype(LOW)
        if slope is not None:
            slope[:, at : at + CHUNK] = tangent.astype(LOW)
    total = x.astype(F32) + whole(smalls, B_DOWN, 384) + dot_nn(active[...], wdown.get())
    normal, inverse = normalize(total)
    if normal2 is not None:
        normal2[...] = normal
        inverse2[...] = inverse
    y[...] = (normal * whole(smalls, N2G, 384) + whole(smalls, N2B, 384)).astype(LOW)


def top_back_body(up, smalls, normal2, inverse2, gr2, gz, gsmall):
    normal = normal2[...]
    put_halves(gsmall, N2G, column_sum(up * normal))
    put_halves(gsmall, N2B, column_sum(up))
    grad = normalize_back(up, whole(smalls, N2G, 384), normal, inverse2[...])
    z = grad.astype(LOW)
    gz[...] = z
    put_halves(gsmall, B_DOWN, column_sum(z.astype(F32)))
    gr2[...] = grad


def feed_back_body(gr2, gz, wup, wdown, smalls, slope, normal1, inverse1, ga, gr1, gb, gsmall):
    z = gz[...]
    down = wdown.get()
    sums = []
    for at in range(0, HIDDEN, CHUNK):
        inner = dot_nt(z, down[at : at + CHUNK, :]) * slope[:, at : at + CHUNK].astype(F32)
        a = inner.astype(LOW)
        ga[:, at : at + CHUNK] = a
        sums.append(column_sum(a.astype(F32)))
    put_halves(gsmall, B_UP, jnp.concatenate(sums, axis=1))
    up = gr2[...] + dot_nt(ga[...], wup.get())
    normal = normal1[...]
    put_halves(gsmall, N1G, column_sum(up * normal))
    put_halves(gsmall, N1B, column_sum(up))
    grad = normalize_back(up, whole(smalls, N1G, 384), normal, inverse1[...])
    gr1[...] = grad
    b = grad.astype(LOW)
    gb[...] = b
    put_halves(gsmall, B_OUT, column_sum(b.astype(F32)))


def heads_back_body(gb, wout, qkv, probs, gqkv, gqv, go):
    go[...] = dot_nt(gb[...], wout.get()).astype(LOW)
    for index, chain, rows, (at_q, at_k, at_v) in places():
        k = qkv[rows, at_k]
        g = split_heads(go[rows, at_q])
        weights = probs[index]
        wide = weights.astype(F32)
        inner = dot_nt(g, qkv[rows, at_v])
        inner = wide * (inner - jnp.sum(wide * inner, axis=-1, keepdims=True))
        s = inner.astype(LOW)
        gqkv[rows, at_q] = (join_heads(dot_nn(s, k)) * SCALE).astype(LOW)
        gqkv[rows, at_k] = (dot_tn(s, split_heads(qkv[rows, at_q])) * SCALE).astype(LOW)
        gqkv[rows, at_v] = dot_tn(weights, g).astype(LOW)
    if gqv is not None:
        gqv[0:1, :] = column_sum(gqkv[:, :WIDTH].astype(F32))
        gqv[1:2, :] = column_sum(gqkv[:, 2 * WIDTH :].astype(F32))


def span_rows(spans, half):
    row = lax.broadcasted_iota(jnp.int32, (ROWS, 1), 0)
    inside = row < 0
    for chain in range(2):
        start = spans[half[0], chain, 0] + chain * LENGTH
        end = spans[half[0], chain, 1] + chain * LENGTH
        inside = inside | ((row >= start) & (row < end))
    return inside


def pick_halves(half, own, other, smalls):
    low = half[0] == 0
    smalls[0:1, :] = jnp.where(low, own[:, :SMALL], other[:, :SMALL])
    smalls[1:2, :] = jnp.where(low, other[:, :SMALL], own[:, :SMALL])


VMEM = pl.BlockSpec(memory_space=pltpu.VMEM)
SMEM = pl.BlockSpec(memory_space=pltpu.SMEM)
ANY = pl.BlockSpec(memory_space=pl.ANY)
SMALL_SCRATCH = pltpu.VMEM((2, SMALL), F32)
QKV_SHAPE = (ROWS, 3 * WIDTH)
PROBS_SHAPE = (2 * PAIRS, 2 * LENGTH, LENGTH)
ROW_SHAPE = (ROWS, WIDTH)
FEED_SHAPE = (ROWS, HIDDEN)
MACS = ROWS * WIDTH * WIDTH * 2
ATTEND_WEIGHTS = [pltpu.VMEM((WIDTH, 3 * WIDTH), LOW), pltpu.VMEM((WIDTH, WIDTH), LOW)]
FEED_WEIGHTS = [pltpu.VMEM((WIDTH, HIDDEN), LOW), pltpu.VMEM((HIDDEN, WIDTH), LOW)]


def shape(dims, kind=LOW):
    return jax.ShapeDtypeStruct(dims, kind)


def kernel_call(body, ins, outs, scratch, flops, moved, name, out_specs=None, grant=VMEM_LIMIT):
    return pl.pallas_call(
        body,
        in_specs=ins,
        out_specs=out_specs or [VMEM] * len(outs),
        out_shape=outs,
        scratch_shapes=scratch,
        compiler_params=pltpu.CompilerParams(vmem_limit_bytes=grant),
        cost_estimate=pl.CostEstimate(flops=flops, bytes_accessed=moved, transcendentals=0),
        name=name,
    )


def attend_first(inputs, half, lens, spans, weights, smalls):
    def body(x, half, lens, spans, so, sp, qo, qp, oo, op, u, h, raw, small, qkv, mixed, wq, wo, sems):
        enter = pltpu.make_async_copy(x.at[half[0]], raw, sems.at[2, 0])
        enter.start()
        wqkv = Weight(half[0], qo, qp, wq, sems.at[0])
        wout = Weight(half[0], oo, op, wo, sems.at[1])
        pick_halves(half, so, sp, small)
        enter.wait()
        mask = so[:, SMALL:].astype(LOW)
        h[...] = jnp.where(span_rows(spans, half), mask, raw[...].reshape(ROWS, WIDTH))
        attend_body(h, wqkv, wout, small, lens, half, qkv, None, mixed, None, None, u)

    return kernel_call(
        body,
        [ANY, SMEM, SMEM, SMEM, VMEM, VMEM] + [ANY] * 4,
        [shape(ROW_SHAPE), shape(ROW_SHAPE)],
        [
            pltpu.VMEM((2, LENGTH, WIDTH), LOW),
            SMALL_SCRATCH,
            pltpu.VMEM(QKV_SHAPE, LOW),
            pltpu.VMEM(ROW_SHAPE, LOW),
            *ATTEND_WEIGHTS,
            pltpu.SemaphoreType.DMA((3, 2)),
        ],
        40 * MACS,
        80000000,
        "attend_first",
    )(inputs, half, lens, spans, *smalls, *weights[0], *weights[1])


def feed_first(u, half, weights, smalls):
    def body(u, half, so, sp, uo, up, do, dp, y, small, active, wu, wd, sems):
        wup = Weight(half[0], uo, up, wu, sems.at[0])
        wdown = Weight(half[0], do, dp, wd, sems.at[1])
        pick_halves(half, so, sp, small)
        feed_body(u, wup, wdown, small, None, active, None, None, y)

    return kernel_call(
        body,
        [VMEM, SMEM, VMEM, VMEM] + [ANY] * 4,
        [shape(ROW_SHAPE)],
        [
            SMALL_SCRATCH,
            pltpu.VMEM(FEED_SHAPE, LOW),
            *FEED_WEIGHTS,
            pltpu.SemaphoreType.DMA((2, 2)),
        ],
        8 * MACS,
        14000000,
        "feed_first",
    )(u, half, *smalls, *weights[2], *weights[3])[0]


KEPT = [
    shape(ROW_SHAPE),
    shape(QKV_SHAPE),
    shape(PROBS_SHAPE),
    shape(ROW_SHAPE),
    shape(ROW_SHAPE, F32),
    shape((ROWS, 1), F32),
    shape(ROW_SHAPE),
    shape(FEED_SHAPE),
    shape(FEED_SHAPE),
    shape(ROW_SHAPE, F32),
    shape((ROWS, 1), F32),
    shape(ROW_SHAPE),
]


def middle(h0, received, cotangent, half, first, lens, weights, smalls):
    def body(h0, received, cot, half, first, lens, so, sp, qo, qp, oo, op, uo, up, do, dp, *rest):
        outs, rest = rest[: len(KEPT)], rest[len(KEPT) :]
        gh, small, gr2, gz, ga, gr1, gb, gsmall, gqkv, go, raw, wq, wo, wu, wd = rest[:15]
        keeps, sems, out_sems, raw_sem = rest[15:-3], *rest[-3:]
        h, qkv, probs, mixed, normal1, inverse1, u, slope, active, normal2, inverse2, y = keeps
        wqkv = Weight(half[0], qo, qp, wq, sems.at[0])
        wout = Weight(half[0], oo, op, wo, sems.at[1])
        wup = Weight(half[0], uo, up, wu, sems.at[2])
        wdown = Weight(half[0], do, dp, wd, sems.at[3])
        enter = pltpu.make_async_copy(cot.at[half[0]], raw, raw_sem)
        enter.start()
        pick_halves(half, so, sp, small)
        leaving = []

        def leave(places):
            for place in places:
                copy = pltpu.make_async_copy(keeps[place], outs[place], out_sems.at[place])
                copy.start()
                leaving.append(copy)

        h[...] = jnp.where(first[0] > 0, h0[...], received[...])
        attend_body(h, wqkv, wout, small, lens, half, qkv, probs, mixed, normal1, inverse1, u)
        leave(range(7))
        feed_body(u, wup, wdown, small, slope, active, normal2, inverse2, y)
        leave(range(7, 12))
        enter.wait()
        upstream = raw[...].reshape(ROWS, WIDTH).astype(F32)
        top_back_body(upstream, small, normal2, inverse2, gr2, gz, gsmall)
        feed_back_body(gr2, gz, wup, wdown, small, slope, normal1, inverse1, ga, gr1, gb, gsmall)
        heads_back_body(gb, wout, qkv, probs, gqkv, None, go)
        gh[...] = (gr1[...] + dot_nt(gqkv[...], wqkv.get())).astype(LOW)
        for copy in leaving:
            copy.wait()

    return kernel_call(
        body,
        [VMEM, VMEM, ANY, SMEM, SMEM, SMEM, VMEM, VMEM] + [ANY] * 8,
        KEPT + [shape(ROW_SHAPE)],
        [
            SMALL_SCRATCH,
            pltpu.VMEM(ROW_SHAPE, F32),
            pltpu.VMEM(ROW_SHAPE, LOW),
            pltpu.VMEM(FEED_SHAPE, LOW),
            pltpu.VMEM(ROW_SHAPE, F32),
            pltpu.VMEM(ROW_SHAPE, LOW),
            SMALL_SCRATCH,
            pltpu.VMEM(QKV_SHAPE, LOW),
            pltpu.VMEM(ROW_SHAPE, LOW),
            pltpu.VMEM((2, LENGTH, WIDTH), LOW),
            *ATTEND_WEIGHTS,
            *FEED_WEIGHTS,
            *[pltpu.VMEM(kept.shape, kept.dtype) for kept in KEPT],
            pltpu.SemaphoreType.DMA((4, 2)),
            pltpu.SemaphoreType.DMA((len(KEPT),)),
            pltpu.SemaphoreType.DMA,
        ],
        24 * MACS,
        45000000,
        "middle",
        [ANY] * len(KEPT) + [VMEM],
    )(
        h0, received, cotangent, half, first, lens, *smalls,
        *weights[0], *weights[1], *weights[2], *weights[3],
    )


MIB = 1024 * 1024


def half_columns(ref, which):
    size = ref.shape[1] // 2
    return ref[:, pl.ds(pl.multiple_of(which * size, 128), size)]


def store_folded(target, at, tensor):
    rows, wide = tensor.shape
    for block in range(wide // WIDTH):
        target[at + block * rows : at + (block + 1) * rows, :] = tensor[
            :, block * WIDTH : (block + 1) * WIDTH
        ].astype(LOW)


class Leaving:
    def __init__(self, sems):
        self.sems = sems
        self.copies = []

    def send(self, source, target):
        copy = pltpu.make_async_copy(source, target, self.sems.at[len(self.copies)])
        copy.start()
        self.copies.append(copy)

    def wait(self):
        for copy in self.copies:
            copy.wait()


TOKEN = shape((8, 128), F32)
GRAD_SHAPE = (1536, WIDTH)
GRAD_SCRATCH = pltpu.VMEM(GRAD_SHAPE, LOW)


def back_top(cotangent, returned, half, first, smalls, active, n2, i2):
    def body(cot, returned, half, first, so, sp, active, n2, i2, *rest):
        other, own, gr2, gz, gsmall, vother, vown, small, raw, sem, out_sems = rest
        enter = pltpu.make_async_copy(cot.at[half[0]], raw, sem)
        enter.start()
        pick_halves(half, so, sp, small)
        enter.wait()
        upstream = jnp.where(first[0] > 0, returned[...], raw[...].reshape(ROWS, WIDTH))
        top_back_body(upstream.astype(F32), small, n2, i2, gr2, gz, gsmall)
        leaving = Leaving(out_sems)
        for which, local, target in ((1 - half[0], vother, other), (half[0], vown, own)):
            local[...] = dot_tn(half_columns(active, which), gz[...]).astype(LOW)
            leaving.send(local, target)
        leaving.wait()

    return kernel_call(
        body,
        [ANY, VMEM, SMEM, SMEM, VMEM, VMEM, VMEM, VMEM, VMEM],
        [
            shape(GRAD_SHAPE),
            shape(GRAD_SHAPE),
            shape(ROW_SHAPE, F32),
            shape(ROW_SHAPE),
            shape((2, SMALL), F32),
        ],
        [
            GRAD_SCRATCH,
            GRAD_SCRATCH,
            SMALL_SCRATCH,
            pltpu.VMEM((2, LENGTH, WIDTH), LOW),
            pltpu.SemaphoreType.DMA,
            pltpu.SemaphoreType.DMA((2,)),
        ],
        4 * MACS,
        12000000,
        "back_top",
        [ANY, ANY, VMEM, VMEM, VMEM],
        56 * MIB,
    )(cotangent, returned, half, first, *smalls, active, n2, i2)


def back_feed(gr2, gz, half, weights, smalls, u, slope, n1, i1):
    def body(gr2, gz, half, so, sp, uo, up, do, dp, u, slope, n1, i1, *rest):
        other, own, gr1, gb, gsmall, token, ga, vother, vown, small, wu, wd, sems, out_sems = rest
        wdown = Weight(half[0], do, dp, wd, sems.at[1])
        wup = Weight(half[0], uo, up, wu, sems.at[0])
        pick_halves(half, so, sp, small)
        feed_back_body(gr2, gz, wup, wdown, small, slope, n1, i1, ga, gr1, gb, gsmall)
        leaving = Leaving(out_sems)
        for which, local, target in ((1 - half[0], vother, other), (half[0], vown, own)):
            store_folded(local, 0, dot_tn(half_columns(u, which), ga[...]))
            leaving.send(local, target)
        token[...] = jnp.zeros(token.shape, F32)
        leaving.wait()

    return kernel_call(
        body,
        [VMEM, VMEM, SMEM, VMEM, VMEM] + [ANY] * 4 + [VMEM] * 4,
        [
            shape(GRAD_SHAPE),
            shape(GRAD_SHAPE),
            shape(ROW_SHAPE, F32),
            shape(ROW_SHAPE),
            shape((2, SMALL), F32),
            TOKEN,
        ],
        [
            pltpu.VMEM(FEED_SHAPE, LOW),
            GRAD_SCRATCH,
            GRAD_SCRATCH,
            SMALL_SCRATCH,
            *FEED_WEIGHTS,
            pltpu.SemaphoreType.DMA((2, 2)),
            pltpu.SemaphoreType.DMA((2,)),
        ],
        240 * MACS,
        600000000,
        "back_feed",
        [ANY, ANY, VMEM, VMEM, VMEM, VMEM],
        36 * MIB,
    )(gr2, gz, half, *smalls, *weights[2], *weights[3], u, slope, n1, i1)


def back_heads(gb, half, weights, top_small, low_small, h, qkv, probs, mixed, after):
    def body(gb, half, oo, op, top, low, h, qkv, probs, mixed, after, *rest):
        other, own, small_other, small_own, gqkv, token, go, gqv, vother, vown, wo, sems, out_sems = rest
        wout = Weight(half[0], oo, op, wo, sems)
        heads_back_body(gb, wout, qkv, probs, gqkv, gqv, go)
        leaving = Leaving(out_sems)
        for which, local, target in ((1 - half[0], vother, other), (half[0], vown, own)):
            store_folded(local, 0, dot_tn(half_columns(h, which), gqkv[...]))
            local[1152:, :] = dot_tn(half_columns(mixed, which), gb[...]).astype(LOW)
            leaving.send(local, target)
        for which, target in ((1 - half[0], small_other), (half[0], small_own)):
            target[:, :WIDTH] = gqv[pl.ds(which, 1), :]
            target[:, WIDTH:B_DOWN] = low[pl.ds(which, 1), WIDTH:B_DOWN]
            target[:, B_DOWN:] = top[pl.ds(which, 1), B_DOWN:]
        token[...] = jnp.zeros(token.shape, F32)
        leaving.wait()

    return kernel_call(
        body,
        [VMEM, SMEM] + [ANY] * 2 + [VMEM] * 6 + [ANY],
        [
            shape(GRAD_SHAPE),
            shape(GRAD_SHAPE),
            shape((1, SMALL), F32),
            shape((1, SMALL), F32),
            shape(QKV_SHAPE),
            TOKEN,
        ],
        [
            pltpu.VMEM(ROW_SHAPE, LOW),
            pltpu.VMEM((2, WIDTH), F32),
            GRAD_SCRATCH,
            GRAD_SCRATCH,
            ATTEND_WEIGHTS[1],
            pltpu.SemaphoreType.DMA((2,)),
            pltpu.SemaphoreType.DMA((2,)),
        ],
        120 * MACS,
        320000000,
        "back_heads",
        [ANY, ANY] + [VMEM] * 4,
        36 * MIB,
    )(gb, half, *weights[1], top_small, low_small, h, qkv, probs, mixed, after)


def back_input(gqkv, gr1, half, first, spans, weights, after):
    def body(gqkv, gr1, half, first, spans, qo, qp, after, gh, gmask, token, wq, sems):
        wqkv = Weight(half[0], qo, qp, wq, sems)
        full = gr1[...] + dot_nt(gqkv[...], wqkv.get())
        dropped = span_rows(spans, half) & (first[0] > 0)
        zero = jnp.zeros_like(full)
        gh[...] = jnp.where(dropped, zero, full).astype(LOW)
        gmask[...] = column_sum(jnp.where(dropped, full, zero))
        token[...] = jnp.zeros(token.shape, F32)

    return kernel_call(
        body,
        [VMEM, VMEM, SMEM, SMEM, SMEM] + [ANY] * 3,
        [shape(ROW_SHAPE), shape((1, WIDTH), F32), TOKEN],
        [ATTEND_WEIGHTS[0], pltpu.SemaphoreType.DMA((2,))],
        60 * MACS,
        120000000,
        "back_input",
        None,
        18 * MIB,
    )(gqkv, gr1, half, first, spans, *weights[0], after)


TAIL = 16
BLOCK = 96


def add_rows(target, sources, at, rows):
    for start in range(0, rows, BLOCK):
        size = min(BLOCK, rows - start)
        place = pl.ds(at + start, size)
        if not isinstance(at, int):
            place = pl.ds(pl.multiple_of(at + start, 16), size)
        total = sources[0][place, :].astype(F32)
        for source in sources[1:]:
            total = total + source[place, :].astype(F32)
        target[start : start + size, :] = total.astype(LOW)


def ordered(name, body, ins, outs, where, after, out_specs=None, scratch=()):
    count, made = len(ins), len(outs)

    def kernel(where, after, *refs):
        refs[count + made][...] = jnp.zeros(TOKEN.shape, F32)
        body(where, refs[:count], refs[count : count + made] + refs[count + made + 1 :])

    moved = 1000
    result = kernel_call(
        kernel,
        [SMEM, ANY] + [VMEM] * count,
        list(outs) + [TOKEN],
        list(scratch),
        moved,
        moved,
        name,
        (out_specs or [VMEM] * made) + [VMEM],
        16 * MIB,
    )(where, after, *ins)
    return result[:made], result[made]


def partner(x, axis, bit):
    return lax.ppermute(x, axis, [(i, i ^ 1 << bit) for i in range(lax.axis_size(axis))])


ORDERS = (
    (("zw", "zu", "xw", "xu"), ("xw", "xu", "zw", "zu")),
    (("zu", "zw", "xu", "xw"), ("xu", "xw", "zu", "zw")),
)


def flip_dp(index, bit):
    z, x, y = index // 8, index // 2 % 4, index % 2
    if bit == "zw":
        z ^= 1
    elif bit == "zu":
        z ^= 3
    elif bit == "xw":
        x ^= 1
    elif bit == "xu":
        x ^= 3
    else:
        y ^= 1
    return z * 8 + x * 2 + y


def exchange(value, part, step):
    pairs = []
    for section in range(4):
        bit = "y" if step is None else ORDERS[part][section % 2][step]
        for index in range(32):
            pairs.append((section * 32 + index, section * 32 + flip_dp(index, bit)))
    return lax.ppermute(value, ("section", "dp"), pairs)


def own_bits(core):
    index = lax.axis_index("dp")
    z, x = index // 8, index // 2 % 4
    bits = {
        "zu": z // 2,
        "zw": (z // 2) ^ (z % 2),
        "xu": x // 2,
        "xw": (x // 2) ^ (x % 2),
    }
    table = [
        jnp.where(core == 0, bits[order[0][step]], bits[order[1][step]])
        for order in ORDERS
        for step in range(4)
    ]
    return jnp.stack(table).astype(jnp.int32)


def row_shapes(*counts):
    return [shape((count, WIDTH)) for count in counts]


def add_tail(target, rows, sources, at, extra):
    if extra:
        total = sources[0][at : at + extra, :].astype(F32)
        for source in sources[1:]:
            total = total + source[at : at + extra, :].astype(F32)
        target[rows : rows + extra, :] = total.astype(LOW)


class Chain:
    def __init__(self, name, bits, tail=0):
        self.name = name
        self.bits = bits
        self.tail = (0, tail)
        self.keep = [None, None]
        self.got = [None, None]

    def kernel(self, name, body, ins, outs, token, *more):
        return ordered(self.name + name, body, ins, outs, self.bits, token, *more)

    def send(self, part, value, step):
        self.got[part] = exchange(value, part, step)

    def start_part(self, part, own, got, token, at=0, rows=GRAD_SHAPE[0], tail_ins=(), tail_body=None):
        self.rows = rows // 2
        half_rows, extra = self.rows, self.tail[part]

        def body(bits, ins, outs):
            bit = bits[4 * part]
            for target, which in ((outs[1], 1 - bit), (outs[0], bit)):
                add_rows(target, ins[:2], at + which * half_rows, half_rows)
            if extra:
                tail = tail_body(ins[2:])
                for target in outs:
                    target[half_rows:, :] = tail

        (self.keep[part], sent), token = self.kernel(
            "start",
            body,
            (own, got) + tuple(tail_ins),
            row_shapes(*[half_rows + extra] * 2),
            token,
        )
        self.send(part, sent, 0)
        return token

    def halve(self, step, token):
        self.rows //= 2
        rows, tails = self.rows, self.tail

        def body(bits, ins, outs):
            for part in range(2):
                bit = bits[4 * part + step]
                pair = ins[2 * part : 2 * part + 2]
                for target, which in ((outs[2 * part + 1], 1 - bit), (outs[2 * part], bit)):
                    add_rows(target, pair, which * rows, rows)
                    add_tail(target, rows, pair, 2 * rows, tails[part])

        ins = (self.keep[0], self.got[0], self.keep[1], self.got[1])
        counts = [rows + tails[0]] * 2 + [rows + tails[1]] * 2
        outs, token = self.kernel("halve", body, ins, row_shapes(*counts), token)
        for part in range(2):
            self.keep[part] = outs[2 * part]
            self.send(part, outs[2 * part + 1], step)
        return token

    def across(self, token):
        rows, extra = self.rows, self.tail[1]

        def body(bits, ins, outs):
            add_rows(outs[0].at[pl.ds(0, rows)], ins[:2], 0, rows)
            add_rows(outs[0].at[pl.ds(rows, rows)], ins[2:], 0, rows)
            add_tail(outs[0], 2 * rows, ins[2:], rows, extra)

        ins = (self.keep[0], self.got[0], self.keep[1], self.got[1])
        (self.both,), token = self.kernel(
            "across", body, ins, row_shapes(2 * rows + extra), token
        )
        self.both_got = exchange(self.both, 0, None)
        return token

    def part(self, token, more_outs=(), more_body=None):
        rows, extra = self.rows, self.tail[1]

        def body(bits, ins, outs):
            add_rows(outs[0], ins, 0, rows)
            add_rows(outs[1], ins, rows, rows)
            if extra:
                add_rows(outs[2], ins, 2 * rows, extra)
                more_body(outs[2][...].astype(F32), outs[3:])

        counts = [rows, rows] + ([extra] if extra else [])
        outs, token = self.kernel(
            "part",
            body,
            (self.both, self.both_got),
            row_shapes(*counts) + list(more_outs),
            token,
        )
        self.keep = list(outs[:2])
        self.tail_sum = outs[2] if extra else None
        for part in range(2):
            self.send(part, self.keep[part], 3)
        return outs[3:], token

    def double(self, step, token, more_ins=(), more_outs=(), more_body=None):
        rows = self.rows

        def body(bits, ins, outs):
            for part in range(2):
                bit = bits[4 * part + step]
                for which, source in ((bit, ins[2 * part]), (1 - bit, ins[2 * part + 1])):
                    outs[part][pl.ds(pl.multiple_of(which * rows, 16), rows), :] = source[...]
            if more_body is not None:
                more_body(ins[4:], outs[2:])

        ins = (self.keep[0], self.got[0], self.keep[1], self.got[1]) + tuple(more_ins)
        results, token = self.kernel(
            "double", body, ins, row_shapes(2 * rows, 2 * rows) + list(more_outs), token
        )
        self.keep, more = list(results[:2]), results[2:]
        self.rows = 2 * rows
        for part in range(2):
            self.send(part, self.keep[part], step - 1)
        return more, token

    def finish(self, token, outs, pieces):
        rows = self.rows

        def body(bits, ins, refs):
            targets, wide, sems = refs[: len(outs)], refs[-2], refs[-1]
            copies = []
            for part in range(2):
                for source, which in ((0, bits[4 * part]), (1, 1 - bits[4 * part])):
                    here = wide.at[part, pl.ds(pl.multiple_of(which * rows, 16), rows)]
                    here[...] = ins[2 * part + source][...].astype(F32)
                at = 0
                for size, place in pieces[part]:
                    copy = pltpu.make_async_copy(
                        wide.at[part, pl.ds(at, size)], place(targets), sems.at[len(copies)]
                    )
                    copy.start()
                    copies.append(copy)
                    at += size
            for copy in copies:
                copy.wait()

        ins = (self.keep[0], self.got[0], self.keep[1], self.got[1])
        count = len(pieces[0]) + len(pieces[1])
        return self.kernel(
            "finish",
            body,
            ins,
            outs,
            token,
            [ANY] * len(outs),
            (pltpu.VMEM((2, 2 * rows, WIDTH), F32), pltpu.SemaphoreType.DMA((count,))),
        )


def pack_vectors(vectors):
    size = sum(vector.shape[0] for vector in vectors)
    total = jnp.zeros((size,), F32)
    at = 0
    for vector in vectors:
        total = total + jnp.pad(vector.astype(F32), (at, size - at - vector.shape[0]))
        at += vector.shape[0]
    return total.reshape(1, size)


def per_device(
    inputs,
    cotangent,
    lengths,
    cdr_spans,
    mask_vector,
    w_qkv,
    qv_bias,
    w_out,
    b_out,
    norm1_gain,
    norm1_bias,
    w_up,
    b_up,
    w_down,
    b_down,
    norm2_gain,
    norm2_bias,
):
    section_index = lax.axis_index("section")
    core = section_index % 2
    half = core.astype(jnp.int32).reshape(1)
    first = (section_index < 2).astype(jnp.int32).reshape(1)
    bits = own_bits(core)
    small = pack_vectors(
        (
            qv_bias,
            b_out,
            norm1_gain,
            norm1_bias,
            b_up,
            b_down,
            norm2_gain,
            norm2_bias,
            mask_vector,
        )
    )
    small_got = partner(small, "section", 0)
    got_qkv, got_out = partner((w_qkv, w_out), "section", 0)
    w_up, w_down, got_qkv, got_out, small_got = lax.optimization_barrier(
        (w_up, w_down, got_qkv, got_out, small_got)
    )
    smalls = (small, small_got)
    got_up, got_down = partner((w_up, w_down), "section", 0)
    weights = [(w_qkv, got_qkv), (w_out, got_out), (w_up, got_up), (w_down, got_down)]

    u, h0 = attend_first(inputs, half, lengths, cdr_spans, weights, smalls)
    first_out = feed_first(u, half, weights, smalls)
    received = lax.ppermute(first_out, "section", [(0, 2), (1, 3)])
    kept = middle(h0, received, cotangent, half, first, lengths, weights, smalls)
    h, qkv, probs, mixed, normal1, inverse1, u, slope, active, normal2, inverse2, output = kept[:12]
    returned = lax.ppermute(kept[12], "section", [(2, 0), (3, 1)])

    a_other, a_own, gr2, gz, top_small = back_top(
        cotangent, returned, half, first, smalls, active, normal2, inverse2
    )
    a_got = partner(a_other, "section", 0)
    b_other, b_own, gr1, gb, low_small, token = back_feed(
        gr2, gz, half, weights, smalls, u, slope, normal1, inverse1
    )
    b_got = partner(b_other, "section", 0)
    x, y = Chain("x_", bits), Chain("y_", bits, TAIL)
    token = x.start_part(0, a_own, a_got, token)
    token = x.start_part(1, b_own, b_got, token)
    y_other, y_own, small_other, small_own, gqkv, token = back_heads(
        gb, half, weights, top_small, low_small, h, qkv, probs, mixed, token
    )
    y_got = partner(y_other, "section", 0)
    small_got = partner(small_other, "section", 0)
    token = x.halve(1, token)
    gh, gmask, token = back_input(gqkv, gr1, half, first, cdr_spans, weights, token)

    def tail_rows(ins):
        small_own, small_got, gmask = ins
        total = small_own[...] + small_got[...]
        rows = [total[:, at : at + WIDTH] for at in range(0, SMALL, WIDTH)]
        rows += [gmask[...], jnp.zeros((TAIL - 7, WIDTH), F32)]
        return jnp.concatenate(rows, axis=0).astype(LOW)

    token = y.start_part(0, y_own, y_got, token, 0, 768)
    token = y.start_part(
        1, y_own, y_got, token, 768, 768, (small_own, small_got, gmask), tail_rows
    )
    token = x.halve(2, token)
    token = y.halve(1, token)
    token = x.halve(3, token)
    token = y.halve(2, token)
    token = x.across(token)
    token = y.halve(3, token)
    _, token = x.part(token)
    token = y.across(token)
    _, token = x.double(3, token)

    def small_outputs(tail, outs):
        flat = jnp.concatenate([tail[row : row + 1, :] for row in range(6)], axis=1)
        at = 0
        for out, size in zip(outs, SIZES):
            out[...] = flat[0, at : at + size]
            at += size

    out_small, token = y.part(token, [shape((size,), F32) for size in SIZES], small_outputs)
    mask_got = partner(y.tail_sum, "section", 0)
    _, token = x.double(2, token)

    def add_tails(ins, outs):
        outs[0][...] = (ins[0][...].astype(F32) + ins[1][...].astype(F32)).astype(LOW)

    (mask_rows,), token = y.double(
        3, token, (y.tail_sum, mask_got), row_shapes(TAIL), add_tails
    )
    mask_got = partner(mask_rows, "section", 1)
    _, token = x.double(1, token)

    def mask_output(ins, outs):
        outs[0][...] = ins[0][6, :].astype(F32) + ins[1][6, :].astype(F32)

    (mask_grad,), token = y.double(
        2, token, (mask_rows, mask_got), [shape((WIDTH,), F32)], mask_output
    )
    _, token = y.double(1, token)
    columns = [pl.ds(block * WIDTH, WIDTH) for block in range(4)]
    (g_down, g_up), token = x.finish(
        token,
        [shape((1536, WIDTH), F32), shape((384, HIDDEN), F32)],
        (
            [(1536, lambda refs: refs[0])],
            [(384, lambda refs, at=at: refs[1].at[:, at]) for at in columns],
        ),
    )
    (g_qkv, g_out), token = y.finish(
        token,
        [shape((384, 3 * WIDTH), F32), shape((384, WIDTH), F32)],
        (
            [(384, lambda refs, at=at: refs[0].at[:, at]) for at in columns[:2]],
            [(384, lambda refs: refs[0].at[:, columns[2]]), (384, lambda refs: refs[1])],
        ),
    )

    g_qv, g_bo, g_n1g, g_n1b, g_bu, g_bd, g_n2g, g_n2b = out_small
    return (
        output.reshape(1, 2, LENGTH, WIDTH),
        gh.reshape(1, 2, LENGTH, WIDTH),
        mask_grad,
        g_qkv,
        g_qv,
        g_out,
        g_bo,
        g_n1g,
        g_n1b,
        g_up,
        g_bu,
        g_down,
        g_bd,
        g_n2g,
        g_n2b,
    )


def solution(mesh):
    in_specs = (
        P(None, "dp", None, None),
        P(None, "dp", None, None),
        P(None, "dp"),
        P(None, "dp", None),
        P(),
        P("section", None),
        P("section"),
        P("section", None),
        P("section"),
        P("section"),
        P("section"),
        P("section", None),
        P("section"),
        P("section", None),
        P("section"),
        P("section"),
        P("section"),
    )
    out_specs = (
        P("section", "dp", None, None),
        P("section", "dp", None, None),
        P(),
        P("section", None),
        P("section"),
        P("section", None),
        P("section"),
        P("section"),
        P("section"),
        P("section", None),
        P("section"),
        P("section", None),
        P("section"),
        P("section"),
        P("section"),
    )
    return jax.shard_map(
        per_device, mesh=mesh, in_specs=in_specs, out_specs=out_specs, check_vma=False
    )
```

```python
import functools
import math

import jax
import jax.numpy as jnp
from jax import lax
from jax.experimental import pallas as pl
from jax.experimental.pallas import tpu as pltpu
from jax.sharding import PartitionSpec as P

EPSILON = 1e-05
F32 = jnp.float32
LOW = jnp.bfloat16
WIDTH = 768
LENGTH = 160
ROWS = 320
HIDDEN = 3072
PAIRS = 6
SCALE = 0.125
SIZES = (768, 384, 384, 384, 1536, 384, 384, 384)
QV, B_OUT, N1G, N1B, B_UP, B_DOWN, N2G, N2B = (sum(SIZES[:at]) for at in range(8))
SMALL = sum(SIZES)
VMEM_LIMIT = 63 * 1024 * 1024


def dot_nn(left_side, right_side):
    return jnp.dot(left_side, right_side, preferred_element_type=F32)


def dot_nt(left_side, right_side):
    return lax.dot_general(
        left_side, right_side, (((1,), (1,)), ((), ())), preferred_element_type=F32
    )


def dot_tn(left_side, right_side):
    return lax.dot_general(
        left_side, right_side, (((0,), (0,)), ((), ())), preferred_element_type=F32
    )


class Weight:
    def __init__(self, half, own, other, dest, sems):
        rows = own.shape[0]
        self.dest = dest
        self.copies = [
            pltpu.make_async_copy(own, dest.at[pl.ds(half * rows, rows)], sems.at[0]),
            pltpu.make_async_copy(other, dest.at[pl.ds((1 - half) * rows, rows)], sems.at[1]),
        ]
        for copy in self.copies:
            copy.start()

    def get(self):
        for copy in self.copies:
            copy.wait()
        self.copies = []
        return self.dest[...]


def whole(smalls, at, size):
    return jnp.concatenate([smalls[0:1, at : at + size], smalls[1:2, at : at + size]], axis=1)


def split_heads(tensor):
    lane = lax.broadcasted_iota(jnp.int32, tensor.shape, 1)
    zero = jnp.zeros_like(tensor)
    return jnp.concatenate(
        [jnp.where(lane < 64, tensor, zero), jnp.where(lane < 64, zero, tensor)], axis=0
    )


def join_heads(tensor):
    lane = lax.broadcasted_iota(jnp.int32, (LENGTH, 128), 1)
    return jnp.where(lane < 64, tensor[:LENGTH], tensor[LENGTH:])


def normalize(values):
    center = values - jnp.mean(values, axis=-1, keepdims=True)
    spread = jnp.mean(center * center, axis=-1, keepdims=True)
    inverse = lax.rsqrt(spread + EPSILON)
    return center * inverse, inverse


def normalize_back(upstream, gain, normal, inverse):
    scaled = upstream * gain
    first = jnp.mean(scaled, axis=-1, keepdims=True)
    second = jnp.mean(scaled * normal, axis=-1, keepdims=True)
    return inverse * (scaled - first - normal * second)


def gelu_parts(values):
    size = jnp.abs(values)
    below = 1.0 + (0.3275911 * math.sqrt(0.5)) * size
    t = pl.reciprocal(below, approx=True)
    t = t * (2.0 - below * t)
    series = t * (
        0.5 * 0.254829592
        + t
        * (
            0.5 * -0.284496736
            + t * (0.5 * 1.421413741 + t * (0.5 * -1.453152027 + t * (0.5 * 1.061405429)))
        )
    )
    bell = jnp.exp(-0.5 * values * values)
    tail = series * bell
    share = jnp.where(values >= 0.0, 1.0 - tail, tail)
    return values * share, share + values * bell * (1.0 / math.sqrt(2.0 * math.pi))


def column_sum(values):
    return jnp.sum(values, axis=0, keepdims=True)


def put_halves(target, at, row):
    size = row.shape[1] // 2
    target[0:1, at : at + size] = row[:, :size]
    target[1:2, at : at + size] = row[:, size:]


def places():
    for index in range(2 * PAIRS):
        chain, pair = divmod(index, PAIRS)
        rows = pl.ds(chain * LENGTH, LENGTH)
        yield index, chain, rows, [pl.ds((pair + block * PAIRS) * 128, 128) for block in range(3)]


def attend_body(h, wqkv, wout, smalls, lens, half, qkv, probs, mixed, normal1, inverse1, u):
    x = h[...]
    bias = jnp.concatenate(
        [smalls[0:1, :WIDTH], jnp.zeros((1, WIDTH), F32), smalls[1:2, :WIDTH]], axis=1
    )
    qkv[...] = (dot_nn(x, wqkv.get()) + bias).astype(LOW)
    for index, chain, rows, (at_q, at_k, at_v) in places():
        scores = dot_nt(split_heads(qkv[rows, at_q]), qkv[rows, at_k]) * SCALE
        key = lax.broadcasted_iota(jnp.int32, scores.shape, 1)
        scores = jnp.where(key < lens[half[0], chain], scores, -1000000000.0)
        grown = jnp.exp(scores - jnp.max(scores, axis=-1, keepdims=True))
        weights = (grown * (1.0 / jnp.sum(grown, axis=-1, keepdims=True))).astype(LOW)
        if probs is not None:
            probs[index] = weights
        mixed[rows, at_q] = join_heads(dot_nn(weights, qkv[rows, at_v])).astype(LOW)
    branch = dot_nn(mixed[...], wout.get()) + whole(smalls, B_OUT, 384)
    normal, inverse = normalize(x.astype(F32) + branch)
    if normal1 is not None:
        normal1[...] = normal
        inverse1[...] = inverse
    u[...] = (normal * whole(smalls, N1G, 384) + whole(smalls, N1B, 384)).astype(LOW)


CHUNK = 1024


def feed_body(u, wup, wdown, smalls, slope, active, normal2, inverse2, y):
    x = u[...]
    bias = whole(smalls, B_UP, 1536)
    up = wup.get()
    for at in range(0, HIDDEN, CHUNK):
        grown, tangent = gelu_parts(dot_nn(x, up[:, at : at + CHUNK]) + bias[:, at : at + CHUNK])
        active[:, at : at + CHUNK] = grown.astype(LOW)
        if slope is not None:
            slope[:, at : at + CHUNK] = tangent.astype(LOW)
    total = x.astype(F32) + whole(smalls, B_DOWN, 384) + dot_nn(active[...], wdown.get())
    normal, inverse = normalize(total)
    if normal2 is not None:
        normal2[...] = normal
        inverse2[...] = inverse
    y[...] = (normal * whole(smalls, N2G, 384) + whole(smalls, N2B, 384)).astype(LOW)


def top_back_body(up, smalls, normal2, inverse2, gr2, gz, gsmall):
    normal = normal2[...]
    put_halves(gsmall, N2G, column_sum(up * normal))
    put_halves(gsmall, N2B, column_sum(up))
    grad = normalize_back(up, whole(smalls, N2G, 384), normal, inverse2[...])
    z = grad.astype(LOW)
    gz[...] = z
    put_halves(gsmall, B_DOWN, column_sum(z.astype(F32)))
    gr2[...] = grad


def feed_back_body(gr2, gz, wup, wdown, smalls, slope, normal1, inverse1, ga, gr1, gb, gsmall):
    z = gz[...]
    down = wdown.get()
    sums = []
    for at in range(0, HIDDEN, CHUNK):
        inner = dot_nt(z, down[at : at + CHUNK, :]) * slope[:, at : at + CHUNK].astype(F32)
        a = inner.astype(LOW)
        ga[:, at : at + CHUNK] = a
        sums.append(column_sum(a.astype(F32)))
    put_halves(gsmall, B_UP, jnp.concatenate(sums, axis=1))
    up = gr2[...] + dot_nt(ga[...], wup.get())
    normal = normal1[...]
    put_halves(gsmall, N1G, column_sum(up * normal))
    put_halves(gsmall, N1B, column_sum(up))
    grad = normalize_back(up, whole(smalls, N1G, 384), normal, inverse1[...])
    gr1[...] = grad
    b = grad.astype(LOW)
    gb[...] = b
    put_halves(gsmall, B_OUT, column_sum(b.astype(F32)))


def heads_back_body(gb, wout, qkv, probs, gqkv, gqv, go):
    go[...] = dot_nt(gb[...], wout.get()).astype(LOW)
    for index, chain, rows, (at_q, at_k, at_v) in places():
        k = qkv[rows, at_k]
        g = split_heads(go[rows, at_q])
        weights = probs[index]
        wide = weights.astype(F32)
        inner = dot_nt(g, qkv[rows, at_v])
        inner = wide * (inner - jnp.sum(wide * inner, axis=-1, keepdims=True))
        s = inner.astype(LOW)
        gqkv[rows, at_q] = (join_heads(dot_nn(s, k)) * SCALE).astype(LOW)
        gqkv[rows, at_k] = (dot_tn(s, split_heads(qkv[rows, at_q])) * SCALE).astype(LOW)
        gqkv[rows, at_v] = dot_tn(weights, g).astype(LOW)
    if gqv is not None:
        gqv[0:1, :] = column_sum(gqkv[:, :WIDTH].astype(F32))
        gqv[1:2, :] = column_sum(gqkv[:, 2 * WIDTH :].astype(F32))


def span_rows(spans, half):
    row = lax.broadcasted_iota(jnp.int32, (ROWS, 1), 0)
    inside = row < 0
    for chain in range(2):
        start = spans[half[0], chain, 0] + chain * LENGTH
        end = spans[half[0], chain, 1] + chain * LENGTH
        inside = inside | ((row >= start) & (row < end))
    return inside


def pick_halves(half, own, other, smalls):
    low = half[0] == 0
    smalls[0:1, :] = jnp.where(low, own[:, :SMALL], other[:, :SMALL])
    smalls[1:2, :] = jnp.where(low, other[:, :SMALL], own[:, :SMALL])


VMEM = pl.BlockSpec(memory_space=pltpu.VMEM)
SMEM = pl.BlockSpec(memory_space=pltpu.SMEM)
ANY = pl.BlockSpec(memory_space=pl.ANY)
SMALL_SCRATCH = pltpu.VMEM((2, SMALL), F32)
QKV_SHAPE = (ROWS, 3 * WIDTH)
PROBS_SHAPE = (2 * PAIRS, 2 * LENGTH, LENGTH)
ROW_SHAPE = (ROWS, WIDTH)
FEED_SHAPE = (ROWS, HIDDEN)
MACS = ROWS * WIDTH * WIDTH * 2
ATTEND_WEIGHTS = [pltpu.VMEM((WIDTH, 3 * WIDTH), LOW), pltpu.VMEM((WIDTH, WIDTH), LOW)]
FEED_WEIGHTS = [pltpu.VMEM((WIDTH, HIDDEN), LOW), pltpu.VMEM((HIDDEN, WIDTH), LOW)]


def shape(dims, kind=LOW):
    return jax.ShapeDtypeStruct(dims, kind)


def kernel_call(body, ins, outs, scratch, flops, moved, name, out_specs=None, grant=VMEM_LIMIT):
    return pl.pallas_call(
        body,
        in_specs=ins,
        out_specs=out_specs or [VMEM] * len(outs),
        out_shape=outs,
        scratch_shapes=scratch,
        compiler_params=pltpu.CompilerParams(vmem_limit_bytes=grant),
        cost_estimate=pl.CostEstimate(flops=flops, bytes_accessed=moved, transcendentals=0),
        name=name,
    )


def attend_first(inputs, half, lens, spans, weights, smalls):
    def body(x, half, lens, spans, so, sp, qo, qp, oo, op, u, h, raw, small, qkv, mixed, wq, wo, sems):
        enter = pltpu.make_async_copy(x.at[half[0]], raw, sems.at[2, 0])
        enter.start()
        wqkv = Weight(half[0], qo, qp, wq, sems.at[0])
        wout = Weight(half[0], oo, op, wo, sems.at[1])
        pick_halves(half, so, sp, small)
        enter.wait()
        mask = so[:, SMALL:].astype(LOW)
        h[...] = jnp.where(span_rows(spans, half), mask, raw[...].reshape(ROWS, WIDTH))
        attend_body(h, wqkv, wout, small, lens, half, qkv, None, mixed, None, None, u)

    return kernel_call(
        body,
        [ANY, SMEM, SMEM, SMEM, VMEM, VMEM] + [ANY] * 4,
        [shape(ROW_SHAPE), shape(ROW_SHAPE)],
        [
            pltpu.VMEM((2, LENGTH, WIDTH), LOW),
            SMALL_SCRATCH,
            pltpu.VMEM(QKV_SHAPE, LOW),
            pltpu.VMEM(ROW_SHAPE, LOW),
            *ATTEND_WEIGHTS,
            pltpu.SemaphoreType.DMA((3, 2)),
        ],
        40 * MACS,
        80000000,
        "attend_first",
    )(inputs, half, lens, spans, *smalls, *weights[0], *weights[1])


def feed_first(u, half, weights, smalls):
    def body(u, half, so, sp, uo, up, do, dp, y, small, active, wu, wd, sems):
        wup = Weight(half[0], uo, up, wu, sems.at[0])
        wdown = Weight(half[0], do, dp, wd, sems.at[1])
        pick_halves(half, so, sp, small)
        feed_body(u, wup, wdown, small, None, active, None, None, y)

    return kernel_call(
        body,
        [VMEM, SMEM, VMEM, VMEM] + [ANY] * 4,
        [shape(ROW_SHAPE)],
        [
            SMALL_SCRATCH,
            pltpu.VMEM(FEED_SHAPE, LOW),
            *FEED_WEIGHTS,
            pltpu.SemaphoreType.DMA((2, 2)),
        ],
        8 * MACS,
        14000000,
        "feed_first",
    )(u, half, *smalls, *weights[2], *weights[3])[0]


KEPT = [
    shape(ROW_SHAPE),
    shape(QKV_SHAPE),
    shape(PROBS_SHAPE),
    shape(ROW_SHAPE),
    shape(ROW_SHAPE, F32),
    shape((ROWS, 1), F32),
    shape(ROW_SHAPE),
    shape(FEED_SHAPE),
    shape(FEED_SHAPE),
    shape(ROW_SHAPE, F32),
    shape((ROWS, 1), F32),
    shape(ROW_SHAPE),
]


def middle(h0, received, cotangent, half, first, lens, weights, smalls):
    def body(h0, received, cot, half, first, lens, so, sp, qo, qp, oo, op, uo, up, do, dp, *rest):
        outs, rest = rest[: len(KEPT)], rest[len(KEPT) :]
        gh, small, gr2, gz, ga, gr1, gb, gsmall, gqkv, go, raw, wq, wo, wu, wd = rest[:15]
        keeps, sems, out_sems, raw_sem = rest[15:-3], *rest[-3:]
        h, qkv, probs, mixed, normal1, inverse1, u, slope, active, normal2, inverse2, y = keeps
        wqkv = Weight(half[0], qo, qp, wq, sems.at[0])
        wout = Weight(half[0], oo, op, wo, sems.at[1])
        wup = Weight(half[0], uo, up, wu, sems.at[2])
        wdown = Weight(half[0], do, dp, wd, sems.at[3])
        enter = pltpu.make_async_copy(cot.at[half[0]], raw, raw_sem)
        enter.start()
        pick_halves(half, so, sp, small)
        leaving = []

        def leave(places):
            for place in places:
                copy = pltpu.make_async_copy(keeps[place], outs[place], out_sems.at[place])
                copy.start()
                leaving.append(copy)

        h[...] = jnp.where(first[0] > 0, h0[...], received[...])
        attend_body(h, wqkv, wout, small, lens, half, qkv, probs, mixed, normal1, inverse1, u)
        leave(range(7))
        feed_body(u, wup, wdown, small, slope, active, normal2, inverse2, y)
        leave(range(7, 12))
        enter.wait()
        upstream = raw[...].reshape(ROWS, WIDTH).astype(F32)
        top_back_body(upstream, small, normal2, inverse2, gr2, gz, gsmall)
        feed_back_body(gr2, gz, wup, wdown, small, slope, normal1, inverse1, ga, gr1, gb, gsmall)
        heads_back_body(gb, wout, qkv, probs, gqkv, None, go)
        gh[...] = (gr1[...] + dot_nt(gqkv[...], wqkv.get())).astype(LOW)
        for copy in leaving:
            copy.wait()

    return kernel_call(
        body,
        [VMEM, VMEM, ANY, SMEM, SMEM, SMEM, VMEM, VMEM] + [ANY] * 8,
        KEPT + [shape(ROW_SHAPE)],
        [
            SMALL_SCRATCH,
            pltpu.VMEM(ROW_SHAPE, F32),
            pltpu.VMEM(ROW_SHAPE, LOW),
            pltpu.VMEM(FEED_SHAPE, LOW),
            pltpu.VMEM(ROW_SHAPE, F32),
            pltpu.VMEM(ROW_SHAPE, LOW),
            SMALL_SCRATCH,
            pltpu.VMEM(QKV_SHAPE, LOW),
            pltpu.VMEM(ROW_SHAPE, LOW),
            pltpu.VMEM((2, LENGTH, WIDTH), LOW),
            *ATTEND_WEIGHTS,
            *FEED_WEIGHTS,
            *[pltpu.VMEM(kept.shape, kept.dtype) for kept in KEPT],
            pltpu.SemaphoreType.DMA((4, 2)),
            pltpu.SemaphoreType.DMA((len(KEPT),)),
            pltpu.SemaphoreType.DMA,
        ],
        24 * MACS,
        45000000,
        "middle",
        [ANY] * len(KEPT) + [VMEM],
    )(
        h0, received, cotangent, half, first, lens, *smalls,
        *weights[0], *weights[1], *weights[2], *weights[3],
    )


MIB = 1024 * 1024


def half_columns(ref, which):
    size = ref.shape[1] // 2
    return ref[:, pl.ds(pl.multiple_of(which * size, 128), size)]


def store_folded(target, at, tensor):
    rows, wide = tensor.shape
    for block in range(wide // WIDTH):
        target[at + block * rows : at + (block + 1) * rows, :] = tensor[
            :, block * WIDTH : (block + 1) * WIDTH
        ].astype(LOW)


class Leaving:
    def __init__(self, sems):
        self.sems = sems
        self.copies = []

    def send(self, source, target):
        copy = pltpu.make_async_copy(source, target, self.sems.at[len(self.copies)])
        copy.start()
        self.copies.append(copy)

    def wait(self):
        for copy in self.copies:
            copy.wait()


TOKEN = shape((8, 128), F32)
GRAD_SHAPE = (1536, WIDTH)
GRAD_SCRATCH = pltpu.VMEM(GRAD_SHAPE, LOW)


def back_feed(cotangent, returned, half, first, weights, smalls, kept):
    u, slope, active, n1, i1, n2, i2 = kept

    def body(cot, returned, half, first, so, sp, uo, up, do, dp, u, slope, active, n1, i1, n2, i2, *rest):
        outs, rest = rest[:8], rest[8:]
        down_other, down_own, up_other, up_own, gr1, gb, gsmall, token = outs
        gr2, gz, ga, v0, v1, v2, v3, small, raw, wu, wd, sems, out_sems = rest
        enter = pltpu.make_async_copy(cot.at[half[0]], raw, sems.at[2, 0])
        enter.start()
        wdown = Weight(half[0], do, dp, wd, sems.at[1])
        wup = Weight(half[0], uo, up, wu, sems.at[0])
        pick_halves(half, so, sp, small)
        enter.wait()
        upstream = jnp.where(first[0] > 0, returned[...], raw[...].reshape(ROWS, WIDTH))
        top_back_body(upstream.astype(F32), small, n2, i2, gr2, gz, gsmall)
        leaving = Leaving(out_sems)
        for which, local, target in ((1 - half[0], v0, down_other), (half[0], v1, down_own)):
            local[...] = dot_tn(half_columns(active, which), gz[...]).astype(LOW)
            leaving.send(local, target)
        feed_back_body(gr2, gz, wup, wdown, small, slope, n1, i1, ga, gr1, gb, gsmall)
        for which, local, target in ((1 - half[0], v2, up_other), (half[0], v3, up_own)):
            store_folded(local, 0, dot_tn(half_columns(u, which), ga[...]))
            leaving.send(local, target)
        token[...] = jnp.zeros(token.shape, F32)
        leaving.wait()

    return kernel_call(
        body,
        [ANY, VMEM, SMEM, SMEM, VMEM, VMEM] + [ANY] * 4 + [VMEM] * 7,
        [shape(GRAD_SHAPE)] * 4
        + [shape(ROW_SHAPE, F32), shape(ROW_SHAPE), shape((2, SMALL), F32), TOKEN],
        [
            pltpu.VMEM(ROW_SHAPE, F32),
            pltpu.VMEM(ROW_SHAPE, LOW),
            pltpu.VMEM(FEED_SHAPE, LOW),
            *[GRAD_SCRATCH] * 4,
            SMALL_SCRATCH,
            pltpu.VMEM((2, LENGTH, WIDTH), LOW),
            *FEED_WEIGHTS,
            pltpu.SemaphoreType.DMA((3, 2)),
            pltpu.SemaphoreType.DMA((4,)),
        ],
        200 * MACS,
        600000000,
        "back_feed",
        [ANY] * 4 + [VMEM] * 4,
    )(
        cotangent, returned, half, first, *smalls, *weights[2], *weights[3],
        u, slope, active, n1, i1, n2, i2,
    )


def back_attend(gb, gr1, half, first, spans, weights, gsmall, h, qkv, probs, mixed, after):
    def body(gb, gr1, half, first, spans, oo, op, qo, qp, gsmall, h, qkv, probs, mixed, after, *rest):
        outs, rest = rest[:6], rest[6:]
        other, own, small_other, small_own, gh, token = outs
        gqkv, go, gqv, vother, vown, wo, wq, sems, out_sems = rest
        wout = Weight(half[0], oo, op, wo, sems.at[0])
        wqkv = Weight(half[0], qo, qp, wq, sems.at[1])
        heads_back_body(gb, wout, qkv, probs, gqkv, gqv, go)
        leaving = Leaving(out_sems)
        for which, local, target in ((1 - half[0], vother, other), (half[0], vown, own)):
            store_folded(local, 0, dot_tn(half_columns(h, which), gqkv[...]))
            local[1152:, :] = dot_tn(half_columns(mixed, which), gb[...]).astype(LOW)
            leaving.send(local, target)
        full = gr1[...] + dot_nt(gqkv[...], wqkv.get())
        dropped = span_rows(spans, half) & (first[0] > 0)
        zero = jnp.zeros_like(full)
        gh[...] = jnp.where(dropped, zero, full).astype(LOW)
        gmask = column_sum(jnp.where(dropped, full, zero))
        for which, target in ((1 - half[0], small_other), (half[0], small_own)):
            target[:, :WIDTH] = gqv[pl.ds(which, 1), :]
            target[:, WIDTH:SMALL] = gsmall[pl.ds(which, 1), WIDTH:]
            target[:, SMALL:] = gmask
        token[...] = jnp.zeros(token.shape, F32)
        leaving.wait()

    return kernel_call(
        body,
        [VMEM, VMEM, SMEM, SMEM, SMEM] + [ANY] * 4 + [VMEM] * 5 + [ANY],
        [
            shape(GRAD_SHAPE),
            shape(GRAD_SHAPE),
            shape((1, SMALL + WIDTH), F32),
            shape((1, SMALL + WIDTH), F32),
            shape(ROW_SHAPE),
            TOKEN,
        ],
        [
            pltpu.VMEM(QKV_SHAPE, LOW),
            pltpu.VMEM(ROW_SHAPE, LOW),
            pltpu.VMEM((2, WIDTH), F32),
            GRAD_SCRATCH,
            GRAD_SCRATCH,
            ATTEND_WEIGHTS[1],
            ATTEND_WEIGHTS[0],
            pltpu.SemaphoreType.DMA((2, 2)),
            pltpu.SemaphoreType.DMA((2,)),
        ],
        180 * MACS,
        400000000,
        "back_attend",
        [ANY, ANY] + [VMEM] * 4,
        40 * MIB,
    )(
        gb, gr1, half, first, spans, *weights[1], *weights[0],
        gsmall, h, qkv, probs, mixed, after,
    )


TAIL = 16
BLOCK = 96


def add_rows(target, sources, at, rows):
    for start in range(0, rows, BLOCK):
        size = min(BLOCK, rows - start)
        place = pl.ds(at + start, size)
        if not isinstance(at, int):
            place = pl.ds(pl.multiple_of(at + start, 16), size)
        total = sources[0][place, :].astype(F32)
        for source in sources[1:]:
            total = total + source[place, :].astype(F32)
        target[start : start + size, :] = total.astype(LOW)


def ordered(name, body, ins, outs, where, after, out_specs=None, scratch=(), moved=1000):
    count, made = len(ins), len(outs)

    def kernel(where, after, *refs):
        refs[count + made][...] = jnp.zeros(TOKEN.shape, F32)
        body(where, refs[:count], refs[count : count + made] + refs[count + made + 1 :])

    result = kernel_call(
        kernel,
        [SMEM, ANY] + [VMEM] * count,
        list(outs) + [TOKEN],
        list(scratch),
        moved,
        moved,
        name,
        (out_specs or [VMEM] * made) + [VMEM],
        16 * MIB,
    )(where, after, *ins)
    return result[:made], result[made]


def partner(x, axis, bit):
    return lax.ppermute(x, axis, [(i, i ^ 1 << bit) for i in range(lax.axis_size(axis))])


def moved_on(index, axis, steps):
    z, x, y = index // 8, index // 2 % 4, index % 2
    if axis == "z":
        z = steps(z)
    elif axis == "x":
        x = steps(x)
    else:
        y = steps(y)
    return z * 8 + x * 2 + y


def send_along(value, axes, place):
    pairs = []
    for section in range(4):
        for index in range(32):
            to = moved_on(index, axes[section % 2], place)
            pairs.append((section * 32 + index, section * 32 + to))
    return lax.ppermute(value, ("section", "dp"), pairs)


def exchange(value, part, step):
    flip = 1 if part == step else 3
    return send_along(value, "zx", lambda place: place ^ flip)


def turn(value, steps):
    return send_along(value, "xz", lambda place: (place + steps) % 4)


def across_y(value):
    return send_along(value, "yy", lambda place: place ^ 1)


def own_places(core):
    index = lax.axis_index("dp")
    z, x = index // 8, index // 2 % 4
    ring = jnp.where(core == 0, z, x)
    high = ring // 2
    low = high ^ (ring % 2)
    table = [low, high, high, low, jnp.where(core == 0, x, z)]
    return jnp.stack(table).astype(jnp.int32)


def row_shapes(*counts):
    return [shape((count, WIDTH)) for count in counts]


def add_tail(target, rows, sources, at, extra):
    if extra:
        total = sources[0][at : at + extra, :].astype(F32)
        for source in sources[1:]:
            total = total + source[at : at + extra, :].astype(F32)
        target[rows : rows + extra, :] = total.astype(LOW)


def gate(token):
    def body(after, out):
        out[...] = jnp.zeros(TOKEN.shape, F32)

    return kernel_call(body, [ANY], [TOKEN], [], 60 * MACS, 120000000, "gate", None, 16 * MIB)(
        token
    )[0]


class Chain:
    def __init__(self, name, places, tail=0):
        self.name = name
        self.places = places
        self.tail = (0, tail)
        self.keep = [None, None]
        self.got = [None, None]

    def kernel(self, name, body, ins, outs, token, *more):
        return ordered(self.name + name, body, ins, outs, self.places, token, *more)

    def pairs(self):
        return (self.keep[0], self.got[0], self.keep[1], self.got[1])

    def start_part(self, part, own, got, token, at=0, rows=GRAD_SHAPE[0], tail_ins=(), tail_body=None):
        self.rows = rows // 2
        half_rows, extra = self.rows, self.tail[part]

        def body(places, ins, outs):
            bit = places[2 * part]
            for target, which in ((outs[1], 1 - bit), (outs[0], bit)):
                add_rows(target, ins[:2], at + which * half_rows, half_rows)
            if extra:
                tail = tail_body(ins[2:])
                for target in outs:
                    target[half_rows:, :] = tail

        (self.keep[part], sent), token = self.kernel(
            "start",
            body,
            (own, got) + tuple(tail_ins),
            row_shapes(*[half_rows + extra] * 2),
            token,
        )
        self.got[part] = exchange(sent, part, 0)
        return token

    def halve(self, token):
        self.rows //= 2
        rows, tails = self.rows, self.tail

        def body(places, ins, outs):
            for part in range(2):
                bit = places[2 * part + 1]
                pair = ins[2 * part : 2 * part + 2]
                for target, which in ((outs[2 * part + 1], 1 - bit), (outs[2 * part], bit)):
                    add_rows(target, pair, which * rows, rows)
                    add_tail(target, rows, pair, 2 * rows, tails[part])

        counts = [rows + tails[0]] * 2 + [rows + tails[1]] * 2
        outs, token = self.kernel(
            "halve", body, self.pairs(), row_shapes(*counts), token
        )
        for part in range(2):
            self.keep[part] = outs[2 * part]
            self.got[part] = exchange(outs[2 * part + 1], part, 1)
        return token

    def cross(self, token):
        whole_rows, extra = self.rows, self.tail[1]
        rows = whole_rows // 2

        def body(places, ins, refs):
            outs, total = refs[:4], refs[4]
            add_rows(total.at[pl.ds(0, whole_rows)], ins[:2], 0, whole_rows)
            add_rows(total.at[pl.ds(whole_rows, whole_rows)], ins[2:], 0, whole_rows)
            for steps in range(4):
                quarter = (places[4] + steps) % 4
                outs[steps][:rows, :] = total[pl.ds(pl.multiple_of(quarter * rows, 16), rows), :]
                add_tail(outs[steps], rows, ins[2:], whole_rows, extra)

        (self.own, *sends), token = self.kernel(
            "cross",
            body,
            self.pairs(),
            row_shapes(*[rows + extra] * 4),
            token,
            None,
            (pltpu.VMEM((2 * whole_rows, WIDTH), LOW),),
        )
        self.rows = rows
        self.ring = [turn(send, steps) for steps, send in zip((1, 2, 3), sends)]
        return token

    def across(self, token):
        rows = self.rows + self.tail[1]

        def body(places, ins, outs):
            add_rows(outs[0], ins, 0, rows)

        (self.own,), token = self.kernel(
            "across", body, (self.own, *self.ring), row_shapes(rows), token
        )
        self.other = across_y(self.own)
        return token

    def total(self, token, more_outs=(), more_body=None):
        rows, extra = self.rows, self.tail[1]

        def body(places, ins, outs):
            add_rows(outs[0], ins, 0, rows)
            if extra:
                add_rows(outs[1], ins, rows, extra)
                more_body(outs[1][...].astype(F32), outs[2:])

        counts = [rows] + ([extra] if extra else [])
        outs, token = self.kernel(
            "total", body, (self.own, self.other), row_shapes(*counts) + list(more_outs), token
        )
        self.own = outs[0]
        self.tail_sum = outs[1] if extra else None
        self.ring = [turn(self.own, steps) for steps in (1, 2, 3)]
        return outs[2:], token

    def back(self, token, more_ins=(), more_outs=(), more_body=None):
        rows = self.rows

        def body(places, ins, refs):
            outs, total = refs[:-1], refs[-1]
            for steps in range(4):
                quarter = (places[4] - steps + 4) % 4
                total[pl.ds(pl.multiple_of(quarter * rows, 16), rows), :] = ins[steps][...]
            outs[0][...] = total[: 2 * rows, :]
            outs[1][...] = total[2 * rows :, :]
            if more_body is not None:
                more_body(ins[4:], outs[2:])

        outs, token = self.kernel(
            "back",
            body,
            (self.own, *self.ring) + tuple(more_ins),
            row_shapes(2 * rows, 2 * rows) + list(more_outs),
            token,
            None,
            (pltpu.VMEM((4 * rows, WIDTH), LOW),),
        )
        self.rows = 2 * rows
        self.keep = list(outs[:2])
        self.got = [exchange(self.keep[part], part, 1) for part in range(2)]
        return outs[2:], token

    def double(self, token):
        rows = self.rows

        def body(places, ins, outs):
            for part in range(2):
                bit = places[2 * part + 1]
                for which, source in ((bit, ins[2 * part]), (1 - bit, ins[2 * part + 1])):
                    outs[part][pl.ds(pl.multiple_of(which * rows, 16), rows), :] = source[...]

        outs, token = self.kernel(
            "double", body, self.pairs(), row_shapes(2 * rows, 2 * rows), token
        )
        self.rows = 2 * rows
        self.keep = list(outs)
        self.got = [exchange(self.keep[part], part, 0) for part in range(2)]
        return token

    def finish(self, token, outs, pieces):
        rows = self.rows

        def body(places, ins, refs):
            targets, wide, sems = refs[: len(outs)], refs[-2], refs[-1]
            copies = []
            for part in range(2):
                for source, which in ((0, places[2 * part]), (1, 1 - places[2 * part])):
                    here = wide.at[part, pl.ds(pl.multiple_of(which * rows, 16), rows)]
                    here[...] = ins[2 * part + source][...].astype(F32)
                at = 0
                for size, place in pieces[part]:
                    copy = pltpu.make_async_copy(
                        wide.at[part, pl.ds(at, size)], place(targets), sems.at[len(copies)]
                    )
                    copy.start()
                    copies.append(copy)
                    at += size
            for copy in copies:
                copy.wait()

        count = len(pieces[0]) + len(pieces[1])
        return self.kernel(
            "finish",
            body,
            self.pairs(),
            outs,
            token,
            [ANY] * len(outs),
            (pltpu.VMEM((2, 2 * rows, WIDTH), F32), pltpu.SemaphoreType.DMA((count,))),
        )


def pack_vectors(vectors):
    size = sum(vector.shape[0] for vector in vectors)
    total = jnp.zeros((size,), F32)
    at = 0
    for vector in vectors:
        total = total + jnp.pad(vector.astype(F32), (at, size - at - vector.shape[0]))
        at += vector.shape[0]
    return total.reshape(1, size)


def per_device(
    inputs,
    cotangent,
    lengths,
    cdr_spans,
    mask_vector,
    w_qkv,
    qv_bias,
    w_out,
    b_out,
    norm1_gain,
    norm1_bias,
    w_up,
    b_up,
    w_down,
    b_down,
    norm2_gain,
    norm2_bias,
):
    section_index = lax.axis_index("section")
    core = section_index % 2
    half = core.astype(jnp.int32).reshape(1)
    first = (section_index < 2).astype(jnp.int32).reshape(1)
    places = own_places(core)
    small = pack_vectors(
        (
            qv_bias,
            b_out,
            norm1_gain,
            norm1_bias,
            b_up,
            b_down,
            norm2_gain,
            norm2_bias,
            mask_vector,
        )
    )
    small_got = partner(small, "section", 0)
    got_qkv, got_out = partner((w_qkv, w_out), "section", 0)
    w_up, w_down, got_qkv, got_out, small_got = lax.optimization_barrier(
        (w_up, w_down, got_qkv, got_out, small_got)
    )
    smalls = (small, small_got)
    got_up, got_down = partner((w_up, w_down), "section", 0)
    weights = [(w_qkv, got_qkv), (w_out, got_out), (w_up, got_up), (w_down, got_down)]

    u, h0 = attend_first(inputs, half, lengths, cdr_spans, weights, smalls)
    first_out = feed_first(u, half, weights, smalls)
    received = lax.ppermute(first_out, "section", [(0, 2), (1, 3)])
    kept = middle(h0, received, cotangent, half, first, lengths, weights, smalls)
    h, qkv, probs, mixed, normal1, inverse1, u, slope, active, normal2, inverse2, output = kept[:12]
    returned = lax.ppermute(kept[12], "section", [(2, 0), (3, 1)])

    a_other, a_own, b_other, b_own, gr1, gb, gsmall, token = back_feed(
        cotangent,
        returned,
        half,
        first,
        weights,
        smalls,
        (u, slope, active, normal1, inverse1, normal2, inverse2),
    )
    a_got = partner(a_other, "section", 0)
    b_got = partner(b_other, "section", 0)
    x, y = Chain("x_", places), Chain("y_", places, TAIL)
    token = x.start_part(0, a_own, a_got, token)
    token = x.start_part(1, b_own, b_got, token)
    y_other, y_own, small_other, small_own, gh, token = back_attend(
        gb, gr1, half, first, cdr_spans, weights, gsmall, h, qkv, probs, mixed, token
    )
    y_got = partner(y_other, "section", 0)
    small_got = partner(small_other, "section", 0)
    token = x.halve(token)
    token = gate(token)

    def tail_rows(ins):
        total = ins[0][...] + ins[1][...]
        rows = [total[:, at : at + WIDTH] for at in range(0, SMALL + WIDTH, WIDTH)]
        rows.append(jnp.zeros((TAIL - len(rows), WIDTH), F32))
        return jnp.concatenate(rows, axis=0).astype(LOW)

    token = y.start_part(0, y_own, y_got, token, 0, 768)
    token = y.start_part(1, y_own, y_got, token, 768, 768, (small_own, small_got), tail_rows)
    token = x.cross(token)
    token = y.halve(token)
    token = x.across(token)
    token = y.cross(token)
    _, token = x.total(token)
    token = y.across(token)
    _, token = x.back(token)

    def small_outputs(tail, outs):
        flat = jnp.concatenate([tail[row : row + 1, :] for row in range(6)], axis=1)
        at = 0
        for out, size in zip(outs, SIZES):
            out[...] = flat[0, at : at + size]
            at += size

    out_small, token = y.total(token, [shape((size,), F32) for size in SIZES], small_outputs)
    mask_got = partner(y.tail_sum, "section", 1)
    token = x.double(token)

    def mask_output(ins, outs):
        outs[0][...] = ins[0][6, :].astype(F32) + ins[1][6, :].astype(F32)

    (mask_grad,), token = y.back(
        token, (y.tail_sum, mask_got), [shape((WIDTH,), F32)], mask_output
    )
    token = y.double(token)
    columns = [pl.ds(block * WIDTH, WIDTH) for block in range(4)]
    (g_down, g_up), token = x.finish(
        token,
        [shape((1536, WIDTH), F32), shape((384, HIDDEN), F32)],
        (
            [(1536, lambda refs: refs[0])],
            [(384, lambda refs, at=at: refs[1].at[:, at]) for at in columns],
        ),
    )
    (g_qkv, g_out), token = y.finish(
        token,
        [shape((384, 3 * WIDTH), F32), shape((384, WIDTH), F32)],
        (
            [(384, lambda refs, at=at: refs[0].at[:, at]) for at in columns[:2]],
            [(384, lambda refs: refs[0].at[:, columns[2]]), (384, lambda refs: refs[1])],
        ),
    )

    g_qv, g_bo, g_n1g, g_n1b, g_bu, g_bd, g_n2g, g_n2b = out_small
    return (
        output.reshape(1, 2, LENGTH, WIDTH),
        gh.reshape(1, 2, LENGTH, WIDTH),
        mask_grad,
        g_qkv,
        g_qv,
        g_out,
        g_bo,
        g_n1g,
        g_n1b,
        g_up,
        g_bu,
        g_down,
        g_bd,
        g_n2g,
        g_n2b,
    )


def solution(mesh):
    in_specs = (
        P(None, "dp", None, None),
        P(None, "dp", None, None),
        P(None, "dp"),
        P(None, "dp", None),
        P(),
        P("section", None),
        P("section"),
        P("section", None),
        P("section"),
        P("section"),
        P("section"),
        P("section", None),
        P("section"),
        P("section", None),
        P("section"),
        P("section"),
        P("section"),
    )
    out_specs = (
        P("section", "dp", None, None),
        P("section", "dp", None, None),
        P(),
        P("section", None),
        P("section"),
        P("section", None),
        P("section"),
        P("section"),
        P("section"),
        P("section", None),
        P("section"),
        P("section", None),
        P("section"),
        P("section"),
        P("section"),
    )
    return jax.shard_map(
        per_device, mesh=mesh, in_specs=in_specs, out_specs=out_specs, check_vma=False
    )
```

```python
import functools
import math

import jax
import jax.numpy as jnp
from jax import lax
from jax.experimental import pallas as pl
from jax.experimental.pallas import tpu as pltpu
from jax.sharding import PartitionSpec as P

EPSILON = 1e-05
F32 = jnp.float32
LOW = jnp.bfloat16
WIDTH = 768
LENGTH = 160
ROWS = 320
HIDDEN = 3072
PAIRS = 6
SCALE = 0.125
SIZES = (768, 384, 384, 384, 1536, 384, 384, 384)
QV, B_OUT, N1G, N1B, B_UP, B_DOWN, N2G, N2B = (sum(SIZES[:at]) for at in range(8))
SMALL = sum(SIZES)
VMEM_LIMIT = 63 * 1024 * 1024


def dot_nn(left_side, right_side):
    return jnp.dot(left_side, right_side, preferred_element_type=F32)


def dot_nt(left_side, right_side):
    return lax.dot_general(
        left_side, right_side, (((1,), (1,)), ((), ())), preferred_element_type=F32
    )


def dot_tn(left_side, right_side):
    return lax.dot_general(
        left_side, right_side, (((0,), (0,)), ((), ())), preferred_element_type=F32
    )


class Weight:
    def __init__(self, half, own, other, dest, sems):
        rows = own.shape[0]
        self.dest = dest
        self.copies = [
            pltpu.make_async_copy(own, dest.at[pl.ds(half * rows, rows)], sems.at[0]),
            pltpu.make_async_copy(other, dest.at[pl.ds((1 - half) * rows, rows)], sems.at[1]),
        ]
        for copy in self.copies:
            copy.start()

    def get(self):
        for copy in self.copies:
            copy.wait()
        self.copies = []
        return self.dest[...]


def whole(smalls, at, size):
    return jnp.concatenate([smalls[0:1, at : at + size], smalls[1:2, at : at + size]], axis=1)


def split_heads(tensor):
    lane = lax.broadcasted_iota(jnp.int32, tensor.shape, 1)
    zero = jnp.zeros_like(tensor)
    return jnp.concatenate(
        [jnp.where(lane < 64, tensor, zero), jnp.where(lane < 64, zero, tensor)], axis=0
    )


def join_heads(tensor):
    lane = lax.broadcasted_iota(jnp.int32, (LENGTH, 128), 1)
    return jnp.where(lane < 64, tensor[:LENGTH], tensor[LENGTH:])


def normalize(values):
    center = values - jnp.mean(values, axis=-1, keepdims=True)
    spread = jnp.mean(center * center, axis=-1, keepdims=True)
    inverse = lax.rsqrt(spread + EPSILON)
    return center * inverse, inverse


def normalize_back(upstream, gain, normal, inverse):
    scaled = upstream * gain
    first = jnp.mean(scaled, axis=-1, keepdims=True)
    second = jnp.mean(scaled * normal, axis=-1, keepdims=True)
    return inverse * (scaled - first - normal * second)


def gelu_parts(values):
    size = jnp.abs(values)
    below = 1.0 + (0.3275911 * math.sqrt(0.5)) * size
    t = pl.reciprocal(below, approx=True)
    t = t * (2.0 - below * t)
    series = t * (
        0.5 * 0.254829592
        + t
        * (
            0.5 * -0.284496736
            + t * (0.5 * 1.421413741 + t * (0.5 * -1.453152027 + t * (0.5 * 1.061405429)))
        )
    )
    bell = jnp.exp(-0.5 * values * values)
    tail = series * bell
    share = jnp.where(values >= 0.0, 1.0 - tail, tail)
    return values * share, share + values * bell * (1.0 / math.sqrt(2.0 * math.pi))


def column_sum(values):
    return jnp.sum(values, axis=0, keepdims=True)


def put_halves(target, at, row):
    size = row.shape[1] // 2
    target[0:1, at : at + size] = row[:, :size]
    target[1:2, at : at + size] = row[:, size:]


def places():
    for index in range(2 * PAIRS):
        chain, pair = divmod(index, PAIRS)
        rows = pl.ds(chain * LENGTH, LENGTH)
        yield index, chain, rows, [pl.ds((pair + block * PAIRS) * 128, 128) for block in range(3)]


def attend_body(h, wqkv, wout, smalls, lens, half, qkv, probs, mixed, normal1, inverse1, u):
    x = h[...]
    bias = jnp.concatenate(
        [smalls[0:1, :WIDTH], jnp.zeros((1, WIDTH), F32), smalls[1:2, :WIDTH]], axis=1
    )
    qkv[...] = (dot_nn(x, wqkv.get()) + bias).astype(LOW)
    for index, chain, rows, (at_q, at_k, at_v) in places():
        scores = dot_nt(split_heads(qkv[rows, at_q]), qkv[rows, at_k]) * SCALE
        key = lax.broadcasted_iota(jnp.int32, scores.shape, 1)
        scores = jnp.where(key < lens[half[0], chain], scores, -1000000000.0)
        grown = jnp.exp(scores - jnp.max(scores, axis=-1, keepdims=True))
        weights = (grown * (1.0 / jnp.sum(grown, axis=-1, keepdims=True))).astype(LOW)
        if probs is not None:
            probs[index] = weights
        mixed[rows, at_q] = join_heads(dot_nn(weights, qkv[rows, at_v])).astype(LOW)
    branch = dot_nn(mixed[...], wout.get()) + whole(smalls, B_OUT, 384)
    normal, inverse = normalize(x.astype(F32) + branch)
    if normal1 is not None:
        normal1[...] = normal
        inverse1[...] = inverse
    u[...] = (normal * whole(smalls, N1G, 384) + whole(smalls, N1B, 384)).astype(LOW)


CHUNK = 1024


def feed_body(u, wup, wdown, smalls, slope, active, normal2, inverse2, y):
    x = u[...]
    bias = whole(smalls, B_UP, 1536)
    up = wup.get()
    for at in range(0, HIDDEN, CHUNK):
        grown, tangent = gelu_parts(dot_nn(x, up[:, at : at + CHUNK]) + bias[:, at : at + CHUNK])
        active[:, at : at + CHUNK] = grown.astype(LOW)
        if slope is not None:
            slope[:, at : at + CHUNK] = tangent.astype(LOW)
    total = x.astype(F32) + whole(smalls, B_DOWN, 384) + dot_nn(active[...], wdown.get())
    normal, inverse = normalize(total)
    if normal2 is not None:
        normal2[...] = normal
        inverse2[...] = inverse
    y[...] = (normal * whole(smalls, N2G, 384) + whole(smalls, N2B, 384)).astype(LOW)


def top_back_body(up, smalls, normal2, inverse2, gr2, gz, gsmall):
    normal = normal2[...]
    put_halves(gsmall, N2G, column_sum(up * normal))
    put_halves(gsmall, N2B, column_sum(up))
    grad = normalize_back(up, whole(smalls, N2G, 384), normal, inverse2[...])
    z = grad.astype(LOW)
    gz[...] = z
    put_halves(gsmall, B_DOWN, column_sum(z.astype(F32)))
    gr2[...] = grad


def feed_back_body(gr2, gz, wup, wdown, smalls, slope, normal1, inverse1, ga, gr1, gb, gsmall):
    z = gz[...]
    down = wdown.get()
    sums = []
    for at in range(0, HIDDEN, CHUNK):
        inner = dot_nt(z, down[at : at + CHUNK, :]) * slope[:, at : at + CHUNK].astype(F32)
        a = inner.astype(LOW)
        ga[:, at : at + CHUNK] = a
        sums.append(column_sum(a.astype(F32)))
    put_halves(gsmall, B_UP, jnp.concatenate(sums, axis=1))
    up = gr2[...] + dot_nt(ga[...], wup.get())
    normal = normal1[...]
    put_halves(gsmall, N1G, column_sum(up * normal))
    put_halves(gsmall, N1B, column_sum(up))
    grad = normalize_back(up, whole(smalls, N1G, 384), normal, inverse1[...])
    gr1[...] = grad
    b = grad.astype(LOW)
    gb[...] = b
    put_halves(gsmall, B_OUT, column_sum(b.astype(F32)))


def heads_back_body(gb, wout, qkv, probs, gqkv, gqv, go):
    go[...] = dot_nt(gb[...], wout.get()).astype(LOW)
    for index, chain, rows, (at_q, at_k, at_v) in places():
        k = qkv[rows, at_k]
        g = split_heads(go[rows, at_q])
        weights = probs[index]
        wide = weights.astype(F32)
        inner = dot_nt(g, qkv[rows, at_v])
        inner = wide * (inner - jnp.sum(wide * inner, axis=-1, keepdims=True))
        s = inner.astype(LOW)
        gqkv[rows, at_q] = (join_heads(dot_nn(s, k)) * SCALE).astype(LOW)
        gqkv[rows, at_k] = (dot_tn(s, split_heads(qkv[rows, at_q])) * SCALE).astype(LOW)
        gqkv[rows, at_v] = dot_tn(weights, g).astype(LOW)
    if gqv is not None:
        gqv[0:1, :] = column_sum(gqkv[:, :WIDTH].astype(F32))
        gqv[1:2, :] = column_sum(gqkv[:, 2 * WIDTH :].astype(F32))


def span_rows(spans, half):
    row = lax.broadcasted_iota(jnp.int32, (ROWS, 1), 0)
    inside = row < 0
    for chain in range(2):
        start = spans[half[0], chain, 0] + chain * LENGTH
        end = spans[half[0], chain, 1] + chain * LENGTH
        inside = inside | ((row >= start) & (row < end))
    return inside


def pick_halves(half, own, other, smalls):
    low = half[0] == 0
    smalls[0:1, :] = jnp.where(low, own[:, :SMALL], other[:, :SMALL])
    smalls[1:2, :] = jnp.where(low, other[:, :SMALL], own[:, :SMALL])


VMEM = pl.BlockSpec(memory_space=pltpu.VMEM)
SMEM = pl.BlockSpec(memory_space=pltpu.SMEM)
ANY = pl.BlockSpec(memory_space=pl.ANY)
SMALL_SCRATCH = pltpu.VMEM((2, SMALL), F32)
QKV_SHAPE = (ROWS, 3 * WIDTH)
PROBS_SHAPE = (2 * PAIRS, 2 * LENGTH, LENGTH)
ROW_SHAPE = (ROWS, WIDTH)
FEED_SHAPE = (ROWS, HIDDEN)
MACS = ROWS * WIDTH * WIDTH * 2
ATTEND_WEIGHTS = [pltpu.VMEM((WIDTH, 3 * WIDTH), LOW), pltpu.VMEM((WIDTH, WIDTH), LOW)]
FEED_WEIGHTS = [pltpu.VMEM((WIDTH, HIDDEN), LOW), pltpu.VMEM((HIDDEN, WIDTH), LOW)]


def shape(dims, kind=LOW):
    return jax.ShapeDtypeStruct(dims, kind)


def kernel_call(body, ins, outs, scratch, flops, moved, name, out_specs=None, grant=VMEM_LIMIT):
    return pl.pallas_call(
        body,
        in_specs=ins,
        out_specs=out_specs or [VMEM] * len(outs),
        out_shape=outs,
        scratch_shapes=scratch,
        compiler_params=pltpu.CompilerParams(vmem_limit_bytes=grant),
        cost_estimate=pl.CostEstimate(flops=flops, bytes_accessed=moved, transcendentals=0),
        name=name,
    )


def attend_first(inputs, half, lens, spans, weights, smalls):
    def body(x, half, lens, spans, so, sp, qo, qp, oo, op, u, h, raw, small, qkv, mixed, wq, wo, sems):
        enter = pltpu.make_async_copy(x.at[half[0]], raw, sems.at[2, 0])
        enter.start()
        wqkv = Weight(half[0], qo, qp, wq, sems.at[0])
        wout = Weight(half[0], oo, op, wo, sems.at[1])
        pick_halves(half, so, sp, small)
        enter.wait()
        mask = so[:, SMALL:].astype(LOW)
        h[...] = jnp.where(span_rows(spans, half), mask, raw[...].reshape(ROWS, WIDTH))
        attend_body(h, wqkv, wout, small, lens, half, qkv, None, mixed, None, None, u)

    return kernel_call(
        body,
        [ANY, SMEM, SMEM, SMEM, VMEM, VMEM] + [ANY] * 4,
        [shape(ROW_SHAPE), shape(ROW_SHAPE)],
        [
            pltpu.VMEM((2, LENGTH, WIDTH), LOW),
            SMALL_SCRATCH,
            pltpu.VMEM(QKV_SHAPE, LOW),
            pltpu.VMEM(ROW_SHAPE, LOW),
            *ATTEND_WEIGHTS,
            pltpu.SemaphoreType.DMA((3, 2)),
        ],
        40 * MACS,
        80000000,
        "attend_first",
    )(inputs, half, lens, spans, *smalls, *weights[0], *weights[1])


def feed_first(u, half, weights, smalls):
    def body(u, half, so, sp, uo, up, do, dp, y, small, active, wu, wd, sems):
        wup = Weight(half[0], uo, up, wu, sems.at[0])
        wdown = Weight(half[0], do, dp, wd, sems.at[1])
        pick_halves(half, so, sp, small)
        feed_body(u, wup, wdown, small, None, active, None, None, y)

    return kernel_call(
        body,
        [VMEM, SMEM, VMEM, VMEM] + [ANY] * 4,
        [shape(ROW_SHAPE)],
        [
            SMALL_SCRATCH,
            pltpu.VMEM(FEED_SHAPE, LOW),
            *FEED_WEIGHTS,
            pltpu.SemaphoreType.DMA((2, 2)),
        ],
        8 * MACS,
        14000000,
        "feed_first",
    )(u, half, *smalls, *weights[2], *weights[3])[0]


KEPT = [
    shape(ROW_SHAPE),
    shape(QKV_SHAPE),
    shape(PROBS_SHAPE),
    shape(ROW_SHAPE),
    shape(ROW_SHAPE, F32),
    shape((ROWS, 1), F32),
    shape(ROW_SHAPE),
    shape(FEED_SHAPE),
    shape(FEED_SHAPE),
    shape(ROW_SHAPE, F32),
    shape((ROWS, 1), F32),
    shape(ROW_SHAPE),
]


def middle(h0, received, cotangent, half, first, lens, weights, smalls):
    def body(h0, received, cot, half, first, lens, so, sp, qo, qp, oo, op, uo, up, do, dp, *rest):
        outs, rest = rest[: len(KEPT)], rest[len(KEPT) :]
        gh, small, gr2, gz, ga, gr1, gb, gsmall, gqkv, go, raw, wq, wo, wu, wd = rest[:15]
        keeps, sems, out_sems, raw_sem = rest[15:-3], *rest[-3:]
        h, qkv, probs, mixed, normal1, inverse1, u, slope, active, normal2, inverse2, y = keeps
        wqkv = Weight(half[0], qo, qp, wq, sems.at[0])
        wout = Weight(half[0], oo, op, wo, sems.at[1])
        wup = Weight(half[0], uo, up, wu, sems.at[2])
        wdown = Weight(half[0], do, dp, wd, sems.at[3])
        enter = pltpu.make_async_copy(cot.at[half[0]], raw, raw_sem)
        enter.start()
        pick_halves(half, so, sp, small)
        leaving = []

        def leave(places):
            for place in places:
                copy = pltpu.make_async_copy(keeps[place], outs[place], out_sems.at[place])
                copy.start()
                leaving.append(copy)

        h[...] = jnp.where(first[0] > 0, h0[...], received[...])
        attend_body(h, wqkv, wout, small, lens, half, qkv, probs, mixed, normal1, inverse1, u)
        leave(range(7))
        feed_body(u, wup, wdown, small, slope, active, normal2, inverse2, y)
        leave(range(7, 12))
        enter.wait()
        upstream = raw[...].reshape(ROWS, WIDTH).astype(F32)
        top_back_body(upstream, small, normal2, inverse2, gr2, gz, gsmall)
        feed_back_body(gr2, gz, wup, wdown, small, slope, normal1, inverse1, ga, gr1, gb, gsmall)
        heads_back_body(gb, wout, qkv, probs, gqkv, None, go)
        gh[...] = (gr1[...] + dot_nt(gqkv[...], wqkv.get())).astype(LOW)
        for copy in leaving:
            copy.wait()

    return kernel_call(
        body,
        [VMEM, VMEM, ANY, SMEM, SMEM, SMEM, VMEM, VMEM] + [ANY] * 8,
        KEPT + [shape(ROW_SHAPE)],
        [
            SMALL_SCRATCH,
            pltpu.VMEM(ROW_SHAPE, F32),
            pltpu.VMEM(ROW_SHAPE, LOW),
            pltpu.VMEM(FEED_SHAPE, LOW),
            pltpu.VMEM(ROW_SHAPE, F32),
            pltpu.VMEM(ROW_SHAPE, LOW),
            SMALL_SCRATCH,
            pltpu.VMEM(QKV_SHAPE, LOW),
            pltpu.VMEM(ROW_SHAPE, LOW),
            pltpu.VMEM((2, LENGTH, WIDTH), LOW),
            *ATTEND_WEIGHTS,
            *FEED_WEIGHTS,
            *[pltpu.VMEM(kept.shape, kept.dtype) for kept in KEPT],
            pltpu.SemaphoreType.DMA((4, 2)),
            pltpu.SemaphoreType.DMA((len(KEPT),)),
            pltpu.SemaphoreType.DMA,
        ],
        24 * MACS,
        45000000,
        "middle",
        [ANY] * len(KEPT) + [VMEM],
    )(
        h0, received, cotangent, half, first, lens, *smalls,
        *weights[0], *weights[1], *weights[2], *weights[3],
    )


MIB = 1024 * 1024


def half_columns(ref, which):
    size = ref.shape[1] // 2
    return ref[:, pl.ds(pl.multiple_of(which * size, 128), size)]


def store_folded(target, at, tensor):
    rows, wide = tensor.shape
    for block in range(wide // WIDTH):
        target[at + block * rows : at + (block + 1) * rows, :] = tensor[
            :, block * WIDTH : (block + 1) * WIDTH
        ].astype(LOW)


class Arriving:
    def __init__(self, pairs, sems):
        self.copies = {}
        for place, (name, source, dest) in enumerate(pairs):
            copy = pltpu.make_async_copy(source, dest, sems.at[place])
            copy.start()
            self.copies[name] = (copy, dest)

    def get(self, name):
        copy, dest = self.copies[name]
        copy.wait()
        return dest


class Leaving:
    def __init__(self, sems):
        self.sems = sems
        self.copies = []

    def send(self, source, target):
        copy = pltpu.make_async_copy(source, target, self.sems.at[len(self.copies)])
        copy.start()
        self.copies.append(copy)

    def wait(self):
        for copy in self.copies:
            copy.wait()


TOKEN = shape((8, 128), F32)
GRAD_SHAPE = (1536, WIDTH)
GRAD_SCRATCH = pltpu.VMEM(GRAD_SHAPE, LOW)


def back_feed(cotangent, returned, half, first, weights, smalls, kept):
    u, slope, active, n1, i1, n2, i2 = kept

    def body(cot, returned, half, first, so, sp, i1, n2, i2, uo, up, do, dp, u, slope, active, n1, *rest):
        outs, rest = rest[:8], rest[8:]
        down_other, down_own, up_other, up_own, gr1, gb, gsmall, token = outs
        gr2, gz, ga, v0, v1, v2, v3, small, raw, wu, wd, vu, vs, va, vn, sems, in_sems, out_sems = rest
        enter = pltpu.make_async_copy(cot.at[half[0]], raw, sems.at[2, 0])
        enter.start()
        arriving = Arriving([("active", active, va)], in_sems)
        wdown = Weight(half[0], do, dp, wd, sems.at[1])
        later = Arriving(
            [("slope", slope, vs), ("normal", n1, vn), ("u", u, vu)],
            in_sems.at[pl.ds(1, 3)],
        )
        wup = Weight(half[0], uo, up, wu, sems.at[0])
        pick_halves(half, so, sp, small)
        enter.wait()
        upstream = jnp.where(first[0] > 0, returned[...], raw[...].reshape(ROWS, WIDTH))
        top_back_body(upstream.astype(F32), small, n2, i2, gr2, gz, gsmall)
        leaving = Leaving(out_sems)
        arriving.get("active")
        for which, local, target in ((1 - half[0], v0, down_other), (half[0], v1, down_own)):
            local[...] = dot_tn(half_columns(va, which), gz[...]).astype(LOW)
            leaving.send(local, target)
        later.get("slope")
        later.get("normal")
        feed_back_body(gr2, gz, wup, wdown, small, vs, vn, i1, ga, gr1, gb, gsmall)
        later.get("u")
        for which, local, target in ((1 - half[0], v2, up_other), (half[0], v3, up_own)):
            store_folded(local, 0, dot_tn(half_columns(vu, which), ga[...]))
            leaving.send(local, target)
        token[...] = jnp.zeros(token.shape, F32)
        leaving.wait()

    return kernel_call(
        body,
        [ANY, VMEM, SMEM, SMEM] + [VMEM] * 5 + [ANY] * 8,
        [shape(GRAD_SHAPE)] * 4
        + [shape(ROW_SHAPE, F32), shape(ROW_SHAPE), shape((2, SMALL), F32), TOKEN],
        [
            pltpu.VMEM(ROW_SHAPE, F32),
            pltpu.VMEM(ROW_SHAPE, LOW),
            pltpu.VMEM(FEED_SHAPE, LOW),
            *[GRAD_SCRATCH] * 4,
            SMALL_SCRATCH,
            pltpu.VMEM((2, LENGTH, WIDTH), LOW),
            *FEED_WEIGHTS,
            pltpu.VMEM(ROW_SHAPE, LOW),
            pltpu.VMEM(FEED_SHAPE, LOW),
            pltpu.VMEM(FEED_SHAPE, LOW),
            pltpu.VMEM(ROW_SHAPE, F32),
            pltpu.SemaphoreType.DMA((3, 2)),
            pltpu.SemaphoreType.DMA((4,)),
            pltpu.SemaphoreType.DMA((4,)),
        ],
        200 * MACS,
        600000000,
        "back_feed",
        [ANY] * 4 + [VMEM] * 4,
    )(
        cotangent, returned, half, first, *smalls, i1, n2, i2, *weights[2], *weights[3],
        u, slope, active, n1,
    )


def back_attend(gb, gr1, half, first, spans, weights, gsmall, h, qkv, probs, mixed):
    def body(gb, half, first, spans, gsmall, oo, op, qo, qp, gr1, h, qkv, probs, mixed, *rest):
        outs, rest = rest[:6], rest[6:]
        other, own, small_other, small_own, gh, token = outs
        gqkv, go, gqv, vother, vown, wo, wq, vr, vh, vq, vp, vm, sems, in_sems, out_sems = rest
        wout = Weight(half[0], oo, op, wo, sems.at[0])
        arriving = Arriving(
            [("qkv", qkv, vq), ("probs", probs, vp), ("h", h, vh), ("mixed", mixed, vm), ("gr1", gr1, vr)],
            in_sems,
        )
        wqkv = Weight(half[0], qo, qp, wq, sems.at[1])
        arriving.get("qkv")
        arriving.get("probs")
        heads_back_body(gb, wout, vq, vp, gqkv, gqv, go)
        leaving = Leaving(out_sems)
        arriving.get("h")
        arriving.get("mixed")
        for which, local, target in ((1 - half[0], vother, other), (half[0], vown, own)):
            store_folded(local, 0, dot_tn(half_columns(vh, which), gqkv[...]))
            local[1152:, :] = dot_tn(half_columns(vm, which), gb[...]).astype(LOW)
            leaving.send(local, target)
        arriving.get("gr1")
        full = vr[...] + dot_nt(gqkv[...], wqkv.get())
        dropped = span_rows(spans, half) & (first[0] > 0)
        zero = jnp.zeros_like(full)
        gh[...] = jnp.where(dropped, zero, full).astype(LOW)
        gmask = column_sum(jnp.where(dropped, full, zero))
        for which, target in ((1 - half[0], small_other), (half[0], small_own)):
            target[:, :WIDTH] = gqv[pl.ds(which, 1), :]
            target[:, WIDTH:SMALL] = gsmall[pl.ds(which, 1), WIDTH:]
            target[:, SMALL:] = gmask
        token[...] = jnp.zeros(token.shape, F32)
        leaving.wait()

    return kernel_call(
        body,
        [VMEM, SMEM, SMEM, SMEM, VMEM] + [ANY] * 9,
        [
            shape(GRAD_SHAPE),
            shape(GRAD_SHAPE),
            shape((1, SMALL + WIDTH), F32),
            shape((1, SMALL + WIDTH), F32),
            shape(ROW_SHAPE),
            TOKEN,
        ],
        [
            pltpu.VMEM(QKV_SHAPE, LOW),
            pltpu.VMEM(ROW_SHAPE, LOW),
            pltpu.VMEM((2, WIDTH), F32),
            GRAD_SCRATCH,
            GRAD_SCRATCH,
            ATTEND_WEIGHTS[1],
            ATTEND_WEIGHTS[0],
            pltpu.VMEM(ROW_SHAPE, F32),
            pltpu.VMEM(ROW_SHAPE, LOW),
            pltpu.VMEM(QKV_SHAPE, LOW),
            pltpu.VMEM(PROBS_SHAPE, LOW),
            pltpu.VMEM(ROW_SHAPE, LOW),
            pltpu.SemaphoreType.DMA((2, 2)),
            pltpu.SemaphoreType.DMA((5,)),
            pltpu.SemaphoreType.DMA((2,)),
        ],
        180 * MACS,
        400000000,
        "back_attend",
        [ANY, ANY] + [VMEM] * 4,
    )(gb, half, first, spans, gsmall, *weights[1], *weights[0], gr1, h, qkv, probs, mixed)


TAIL = 16
BLOCK = 96


def add_rows(target, sources, at, rows):
    for start in range(0, rows, BLOCK):
        size = min(BLOCK, rows - start)
        place = pl.ds(at + start, size)
        if not isinstance(at, int):
            place = pl.ds(pl.multiple_of(at + start, 16), size)
        total = sources[0][place, :].astype(F32)
        for source in sources[1:]:
            total = total + source[place, :].astype(F32)
        target[start : start + size, :] = total.astype(LOW)


def ordered(name, body, ins, outs, where, after, out_specs=None, scratch=(), moved=30000000000):
    count, made = len(ins), len(outs)

    def kernel(where, after, *refs):
        refs[count + made][...] = jnp.zeros(TOKEN.shape, F32)
        body(where, refs[:count], refs[count : count + made] + refs[count + made + 1 :])

    result = kernel_call(
        kernel,
        [SMEM, ANY] + [VMEM] * count,
        list(outs) + [TOKEN],
        list(scratch),
        moved,
        moved,
        name,
        (out_specs or [VMEM] * made) + [VMEM],
        16 * MIB,
    )(where, after, *ins)
    return result[:made], result[made]


def partner(x, axis, bit):
    return lax.ppermute(x, axis, [(i, i ^ 1 << bit) for i in range(lax.axis_size(axis))])


def moved_on(index, axis, steps):
    z, x, y = index // 8, index // 2 % 4, index % 2
    if axis == "z":
        z = steps(z)
    elif axis == "x":
        x = steps(x)
    else:
        y = steps(y)
    return z * 8 + x * 2 + y


def send_along(value, axes, place):
    pairs = []
    for section in range(4):
        for index in range(32):
            to = moved_on(index, axes[section % 2], place)
            pairs.append((section * 32 + index, section * 32 + to))
    return lax.ppermute(value, ("section", "dp"), pairs)


def exchange(value, part, step):
    flip = 1 if part == step else 3
    return send_along(value, "zx", lambda place: place ^ flip)


def turn(value, steps):
    return send_along(value, "xz", lambda place: (place + steps) % 4)


def across_y(value):
    return send_along(value, "yy", lambda place: place ^ 1)


def own_places(core):
    index = lax.axis_index("dp")
    z, x = index // 8, index // 2 % 4
    ring = jnp.where(core == 0, z, x)
    high = ring // 2
    low = high ^ (ring % 2)
    table = [low, high, high, low, jnp.where(core == 0, x, z)]
    return jnp.stack(table).astype(jnp.int32)


def row_shapes(*counts):
    return [shape((count, WIDTH)) for count in counts]


def add_tail(target, rows, sources, at, extra):
    if extra:
        total = sources[0][at : at + extra, :].astype(F32)
        for source in sources[1:]:
            total = total + source[at : at + extra, :].astype(F32)
        target[rows : rows + extra, :] = total.astype(LOW)


class Chain:
    def __init__(self, name, places, tail=0):
        self.name = name
        self.places = places
        self.tail = (0, tail)
        self.keep = [None, None]
        self.got = [None, None]

    def kernel(self, name, body, ins, outs, token, *more):
        return ordered(self.name + name, body, ins, outs, self.places, token, *more)

    def pairs(self):
        return (self.keep[0], self.got[0], self.keep[1], self.got[1])

    def start(self, sources, rows, token, tail_ins=(), tail_body=None):
        self.rows = rows // 2
        half_rows, tails = self.rows, self.tail
        arrays = []
        for own, got, _ in sources:
            arrays += [own, got]

        def body(places, ins, outs):
            for part in range(2):
                bit, at = places[2 * part], sources[part][2]
                pair = ins[2 * part : 2 * part + 2]
                for target, which in ((outs[2 * part + 1], 1 - bit), (outs[2 * part], bit)):
                    add_rows(target, pair, at + which * half_rows, half_rows)
                    if tails[part]:
                        target[half_rows:, :] = tail_body(ins[4:])

        counts = [half_rows + tails[0]] * 2 + [half_rows + tails[1]] * 2
        outs, token = self.kernel(
            "start", body, tuple(arrays) + tuple(tail_ins), row_shapes(*counts), token
        )
        for part in range(2):
            self.keep[part] = outs[2 * part]
            self.got[part] = exchange(outs[2 * part + 1], part, 0)
        return token

    def halve(self, token):
        self.rows //= 2
        rows, tails = self.rows, self.tail

        def body(places, ins, outs):
            for part in range(2):
                bit = places[2 * part + 1]
                pair = ins[2 * part : 2 * part + 2]
                for target, which in ((outs[2 * part + 1], 1 - bit), (outs[2 * part], bit)):
                    add_rows(target, pair, which * rows, rows)
                    add_tail(target, rows, pair, 2 * rows, tails[part])

        counts = [rows + tails[0]] * 2 + [rows + tails[1]] * 2
        outs, token = self.kernel(
            "halve", body, self.pairs(), row_shapes(*counts), token
        )
        for part in range(2):
            self.keep[part] = outs[2 * part]
            self.got[part] = exchange(outs[2 * part + 1], part, 1)
        return token

    def cross(self, token):
        whole_rows, extra = self.rows, self.tail[1]
        rows = whole_rows // 2

        def body(places, ins, refs):
            outs, total = refs[:4], refs[4]
            add_rows(total.at[pl.ds(0, whole_rows)], ins[:2], 0, whole_rows)
            add_rows(total.at[pl.ds(whole_rows, whole_rows)], ins[2:], 0, whole_rows)
            for steps in range(4):
                quarter = (places[4] + steps) % 4
                outs[steps][:rows, :] = total[pl.ds(pl.multiple_of(quarter * rows, 16), rows), :]
                add_tail(outs[steps], rows, ins[2:], whole_rows, extra)

        (self.own, *sends), token = self.kernel(
            "cross",
            body,
            self.pairs(),
            row_shapes(*[rows + extra] * 4),
            token,
            None,
            (pltpu.VMEM((2 * whole_rows, WIDTH), LOW),),
        )
        self.rows = rows
        self.ring = [turn(send, steps) for steps, send in zip((1, 2, 3), sends)]
        return token

    def across(self, token):
        rows = self.rows + self.tail[1]

        def body(places, ins, outs):
            add_rows(outs[0], ins, 0, rows)

        (self.own,), token = self.kernel(
            "across", body, (self.own, *self.ring), row_shapes(rows), token
        )
        self.other = across_y(self.own)
        return token

    def total(self, token, more_outs=(), more_body=None):
        rows, extra = self.rows, self.tail[1]

        def body(places, ins, outs):
            add_rows(outs[0], ins, 0, rows)
            if extra:
                add_rows(outs[1], ins, rows, extra)
                more_body(outs[1][...].astype(F32), outs[2:])

        counts = [rows] + ([extra] if extra else [])
        outs, token = self.kernel(
            "total", body, (self.own, self.other), row_shapes(*counts) + list(more_outs), token
        )
        self.own = outs[0]
        self.tail_sum = outs[1] if extra else None
        self.ring = [turn(self.own, steps) for steps in (1, 2, 3)]
        return outs[2:], token

    def back(self, token, more_ins=(), more_outs=(), more_body=None):
        rows = self.rows

        def body(places, ins, refs):
            outs, total = refs[:-1], refs[-1]
            for steps in range(4):
                quarter = (places[4] - steps + 4) % 4
                total[pl.ds(pl.multiple_of(quarter * rows, 16), rows), :] = ins[steps][...]
            outs[0][...] = total[: 2 * rows, :]
            outs[1][...] = total[2 * rows :, :]
            if more_body is not None:
                more_body(ins[4:], outs[2:])

        outs, token = self.kernel(
            "back",
            body,
            (self.own, *self.ring) + tuple(more_ins),
            row_shapes(2 * rows, 2 * rows) + list(more_outs),
            token,
            None,
            (pltpu.VMEM((4 * rows, WIDTH), LOW),),
        )
        self.rows = 2 * rows
        self.keep = list(outs[:2])
        self.got = [exchange(self.keep[part], part, 1) for part in range(2)]
        return outs[2:], token

    def double(self, token):
        rows = self.rows

        def body(places, ins, outs):
            for part in range(2):
                bit = places[2 * part + 1]
                for which, source in ((bit, ins[2 * part]), (1 - bit, ins[2 * part + 1])):
                    outs[part][pl.ds(pl.multiple_of(which * rows, 16), rows), :] = source[...]

        outs, token = self.kernel(
            "double", body, self.pairs(), row_shapes(2 * rows, 2 * rows), token
        )
        self.rows = 2 * rows
        self.keep = list(outs)
        self.got = [exchange(self.keep[part], part, 0) for part in range(2)]
        return token

    def finish(self, token, outs, pieces):
        rows = self.rows

        def body(places, ins, refs):
            targets, wide, sems = refs[: len(outs)], refs[-2], refs[-1]
            copies = []
            for part in range(2):
                for source, which in ((0, places[2 * part]), (1, 1 - places[2 * part])):
                    here = wide.at[part, pl.ds(pl.multiple_of(which * rows, 16), rows)]
                    here[...] = ins[2 * part + source][...].astype(F32)
                at = 0
                for size, place in pieces[part]:
                    copy = pltpu.make_async_copy(
                        wide.at[part, pl.ds(at, size)], place(targets), sems.at[len(copies)]
                    )
                    copy.start()
                    copies.append(copy)
                    at += size
            for copy in copies:
                copy.wait()

        count = len(pieces[0]) + len(pieces[1])
        return self.kernel(
            "finish",
            body,
            self.pairs(),
            outs,
            token,
            [ANY] * len(outs),
            (pltpu.VMEM((2, 2 * rows, WIDTH), F32), pltpu.SemaphoreType.DMA((count,))),
        )


def pack_vectors(vectors):
    size = sum(vector.shape[0] for vector in vectors)
    total = jnp.zeros((size,), F32)
    at = 0
    for vector in vectors:
        total = total + jnp.pad(vector.astype(F32), (at, size - at - vector.shape[0]))
        at += vector.shape[0]
    return total.reshape(1, size)


def per_device(
    inputs,
    cotangent,
    lengths,
    cdr_spans,
    mask_vector,
    w_qkv,
    qv_bias,
    w_out,
    b_out,
    norm1_gain,
    norm1_bias,
    w_up,
    b_up,
    w_down,
    b_down,
    norm2_gain,
    norm2_bias,
):
    section_index = lax.axis_index("section")
    core = section_index % 2
    half = core.astype(jnp.int32).reshape(1)
    first = (section_index < 2).astype(jnp.int32).reshape(1)
    places = own_places(core)
    small = pack_vectors(
        (
            qv_bias,
            b_out,
            norm1_gain,
            norm1_bias,
            b_up,
            b_down,
            norm2_gain,
            norm2_bias,
            mask_vector,
        )
    )
    small_got = partner(small, "section", 0)
    got_qkv, got_out = partner((w_qkv, w_out), "section", 0)
    w_up, w_down, got_qkv, got_out, small_got = lax.optimization_barrier(
        (w_up, w_down, got_qkv, got_out, small_got)
    )
    smalls = (small, small_got)
    got_up, got_down = partner((w_up, w_down), "section", 0)
    weights = [(w_qkv, got_qkv), (w_out, got_out), (w_up, got_up), (w_down, got_down)]

    u, h0 = attend_first(inputs, half, lengths, cdr_spans, weights, smalls)
    first_out = feed_first(u, half, weights, smalls)
    received = lax.ppermute(first_out, "section", [(0, 2), (1, 3)])
    kept = middle(h0, received, cotangent, half, first, lengths, weights, smalls)
    h, qkv, probs, mixed, normal1, inverse1, u, slope, active, normal2, inverse2, output = kept[:12]
    returned = lax.ppermute(kept[12], "section", [(2, 0), (3, 1)])

    a_other, a_own, b_other, b_own, gr1, gb, gsmall, token = back_feed(
        cotangent,
        returned,
        half,
        first,
        weights,
        smalls,
        (u, slope, active, normal1, inverse1, normal2, inverse2),
    )
    a_got = partner(a_other, "section", 0)
    b_got = partner(b_other, "section", 0)
    x, y = Chain("x_", places), Chain("y_", places, TAIL)
    y_other, y_own, small_other, small_own, gh, token = back_attend(
        gb, gr1, half, first, cdr_spans, weights, gsmall, h, qkv, probs, mixed
    )
    y_got = partner(y_other, "section", 0)
    small_got = partner(small_other, "section", 0)
    token = x.start([(a_own, a_got, 0), (b_own, b_got, 0)], 1536, token)

    def tail_rows(ins):
        total = ins[0][...] + ins[1][...]
        rows = [total[:, at : at + WIDTH] for at in range(0, SMALL + WIDTH, WIDTH)]
        rows.append(jnp.zeros((TAIL - len(rows), WIDTH), F32))
        return jnp.concatenate(rows, axis=0).astype(LOW)

    token = y.start(
        [(y_own, y_got, 0), (y_own, y_got, 768)], 768, token, (small_own, small_got), tail_rows
    )
    token = x.halve(token)
    token = y.halve(token)
    token = x.cross(token)
    token = y.cross(token)
    token = x.across(token)
    token = y.across(token)
    _, token = x.total(token)

    def small_outputs(tail, outs):
        flat = jnp.concatenate([tail[row : row + 1, :] for row in range(6)], axis=1)
        at = 0
        for out, size in zip(outs, SIZES):
            out[...] = flat[0, at : at + size]
            at += size

    out_small, token = y.total(token, [shape((size,), F32) for size in SIZES], small_outputs)
    mask_got = partner(y.tail_sum, "section", 1)
    _, token = x.back(token)

    def mask_output(ins, outs):
        outs[0][...] = ins[0][6, :].astype(F32) + ins[1][6, :].astype(F32)

    (mask_grad,), token = y.back(
        token, (y.tail_sum, mask_got), [shape((WIDTH,), F32)], mask_output
    )
    token = x.double(token)
    token = y.double(token)
    columns = [pl.ds(block * WIDTH, WIDTH) for block in range(4)]
    (g_down, g_up), token = x.finish(
        token,
        [shape((1536, WIDTH), F32), shape((384, HIDDEN), F32)],
        (
            [(1536, lambda refs: refs[0])],
            [(384, lambda refs, at=at: refs[1].at[:, at]) for at in columns],
        ),
    )
    (g_qkv, g_out), token = y.finish(
        token,
        [shape((384, 3 * WIDTH), F32), shape((384, WIDTH), F32)],
        (
            [(384, lambda refs, at=at: refs[0].at[:, at]) for at in columns[:2]],
            [(384, lambda refs: refs[0].at[:, columns[2]]), (384, lambda refs: refs[1])],
        ),
    )

    g_qv, g_bo, g_n1g, g_n1b, g_bu, g_bd, g_n2g, g_n2b = out_small
    return (
        output.reshape(1, 2, LENGTH, WIDTH),
        gh.reshape(1, 2, LENGTH, WIDTH),
        mask_grad,
        g_qkv,
        g_qv,
        g_out,
        g_bo,
        g_n1g,
        g_n1b,
        g_up,
        g_bu,
        g_down,
        g_bd,
        g_n2g,
        g_n2b,
    )


def solution(mesh):
    in_specs = (
        P(None, "dp", None, None),
        P(None, "dp", None, None),
        P(None, "dp"),
        P(None, "dp", None),
        P(),
        P("section", None),
        P("section"),
        P("section", None),
        P("section"),
        P("section"),
        P("section"),
        P("section", None),
        P("section"),
        P("section", None),
        P("section"),
        P("section"),
        P("section"),
    )
    out_specs = (
        P("section", "dp", None, None),
        P("section", "dp", None, None),
        P(),
        P("section", None),
        P("section"),
        P("section", None),
        P("section"),
        P("section"),
        P("section"),
        P("section", None),
        P("section"),
        P("section", None),
        P("section"),
        P("section"),
        P("section"),
    )
    return jax.shard_map(
        per_device, mesh=mesh, in_specs=in_specs, out_specs=out_specs, check_vma=False
    )
```

```python
import functools
import math

import jax
import jax.numpy as jnp
from jax import lax
from jax.experimental import pallas as pl
from jax.experimental.pallas import tpu as pltpu
from jax.sharding import PartitionSpec as P

EPSILON = 1e-05
F32 = jnp.float32
LOW = jnp.bfloat16
WIDTH = 768
LENGTH = 160
ROWS = 320
HIDDEN = 3072
PAIRS = 6
SCALE = 0.125
SIZES = (768, 384, 384, 384, 1536, 384, 384, 384)
QV, B_OUT, N1G, N1B, B_UP, B_DOWN, N2G, N2B = (sum(SIZES[:at]) for at in range(8))
SMALL = sum(SIZES)
VMEM_LIMIT = 63 * 1024 * 1024
BIG_GRANT = 61 * 1024 * 1024


def dot_nn(left_side, right_side):
    return jnp.dot(left_side, right_side, preferred_element_type=F32)


def dot_nt(left_side, right_side):
    return lax.dot_general(
        left_side, right_side, (((1,), (1,)), ((), ())), preferred_element_type=F32
    )


def dot_tn(left_side, right_side):
    return lax.dot_general(
        left_side, right_side, (((0,), (0,)), ((), ())), preferred_element_type=F32
    )


class Weight:
    def __init__(self, half, own, other, dest, sems):
        rows = own.shape[0]
        self.dest = dest
        self.copies = [
            pltpu.make_async_copy(own, dest.at[pl.ds(half * rows, rows)], sems.at[0]),
            pltpu.make_async_copy(other, dest.at[pl.ds((1 - half) * rows, rows)], sems.at[1]),
        ]
        for copy in self.copies:
            copy.start()

    def get(self):
        for copy in self.copies:
            copy.wait()
        self.copies = []
        return self.dest[...]


def whole(smalls, at, size):
    return jnp.concatenate([smalls[0:1, at : at + size], smalls[1:2, at : at + size]], axis=1)


def split_heads(tensor):
    lane = lax.broadcasted_iota(jnp.int32, tensor.shape, 1)
    zero = jnp.zeros_like(tensor)
    return jnp.concatenate(
        [jnp.where(lane < 64, tensor, zero), jnp.where(lane < 64, zero, tensor)], axis=0
    )


def join_heads(tensor):
    lane = lax.broadcasted_iota(jnp.int32, (LENGTH, 128), 1)
    return jnp.where(lane < 64, tensor[:LENGTH], tensor[LENGTH:])


def normalize(values):
    center = values - jnp.mean(values, axis=-1, keepdims=True)
    spread = jnp.mean(center * center, axis=-1, keepdims=True)
    inverse = lax.rsqrt(spread + EPSILON)
    return center * inverse, inverse


def normalize_back(upstream, gain, normal, inverse):
    scaled = upstream * gain
    first = jnp.mean(scaled, axis=-1, keepdims=True)
    second = jnp.mean(scaled * normal, axis=-1, keepdims=True)
    return inverse * (scaled - first - normal * second)


def gelu_parts(values):
    size = jnp.abs(values)
    below = 1.0 + (0.3275911 * math.sqrt(0.5)) * size
    t = pl.reciprocal(below, approx=True)
    t = t * (2.0 - below * t)
    series = t * (
        0.5 * 0.254829592
        + t
        * (
            0.5 * -0.284496736
            + t * (0.5 * 1.421413741 + t * (0.5 * -1.453152027 + t * (0.5 * 1.061405429)))
        )
    )
    bell = jnp.exp(-0.5 * values * values)
    tail = series * bell
    share = jnp.where(values >= 0.0, 1.0 - tail, tail)
    return values * share, share + values * bell * (1.0 / math.sqrt(2.0 * math.pi))


def column_sum(values):
    return jnp.sum(values, axis=0, keepdims=True)


def put_halves(target, at, row):
    size = row.shape[1] // 2
    target[0:1, at : at + size] = row[:, :size]
    target[1:2, at : at + size] = row[:, size:]


def places():
    for index in range(2 * PAIRS):
        chain, pair = divmod(index, PAIRS)
        rows = pl.ds(chain * LENGTH, LENGTH)
        yield index, chain, rows, [pl.ds((pair + block * PAIRS) * 128, 128) for block in range(3)]


def attend_body(h, wqkv, wout, smalls, lens, half, qkv, probs, mixed, normal1, inverse1, u):
    x = h[...]
    bias = jnp.concatenate(
        [smalls[0:1, :WIDTH], jnp.zeros((1, WIDTH), F32), smalls[1:2, :WIDTH]], axis=1
    )
    qkv[...] = (dot_nn(x, wqkv.get()) + bias).astype(LOW)
    for index, chain, rows, (at_q, at_k, at_v) in places():
        scores = dot_nt(split_heads(qkv[rows, at_q]), qkv[rows, at_k]) * SCALE
        key = lax.broadcasted_iota(jnp.int32, scores.shape, 1)
        scores = jnp.where(key < lens[half[0], chain], scores, -1000000000.0)
        grown = jnp.exp(scores - jnp.max(scores, axis=-1, keepdims=True))
        weights = (grown * (1.0 / jnp.sum(grown, axis=-1, keepdims=True))).astype(LOW)
        if probs is not None:
            probs[index] = weights
        mixed[rows, at_q] = join_heads(dot_nn(weights, qkv[rows, at_v])).astype(LOW)
    branch = dot_nn(mixed[...], wout.get()) + whole(smalls, B_OUT, 384)
    normal, inverse = normalize(x.astype(F32) + branch)
    if normal1 is not None:
        normal1[...] = normal
        inverse1[...] = inverse
    u[...] = (normal * whole(smalls, N1G, 384) + whole(smalls, N1B, 384)).astype(LOW)


CHUNK = 1024


def feed_body(u, wup, wdown, smalls, slope, active, normal2, inverse2, y):
    x = u[...]
    bias = whole(smalls, B_UP, 1536)
    up = wup.get()
    for at in range(0, HIDDEN, CHUNK):
        grown, tangent = gelu_parts(dot_nn(x, up[:, at : at + CHUNK]) + bias[:, at : at + CHUNK])
        active[:, at : at + CHUNK] = grown.astype(LOW)
        if slope is not None:
            slope[:, at : at + CHUNK] = tangent.astype(LOW)
    total = x.astype(F32) + whole(smalls, B_DOWN, 384) + dot_nn(active[...], wdown.get())
    normal, inverse = normalize(total)
    if normal2 is not None:
        normal2[...] = normal
        inverse2[...] = inverse
    y[...] = (normal * whole(smalls, N2G, 384) + whole(smalls, N2B, 384)).astype(LOW)


def top_back_body(up, smalls, normal2, inverse2, gr2, gz, gsmall):
    normal = normal2[...]
    put_halves(gsmall, N2G, column_sum(up * normal))
    put_halves(gsmall, N2B, column_sum(up))
    grad = normalize_back(up, whole(smalls, N2G, 384), normal, inverse2[...])
    z = grad.astype(LOW)
    gz[...] = z
    put_halves(gsmall, B_DOWN, column_sum(z.astype(F32)))
    gr2[...] = grad


def feed_back_body(gr2, gz, wup, wdown, smalls, slope, normal1, inverse1, ga, gr1, gb, gsmall):
    z = gz[...]
    down = wdown.get()
    sums = []
    for at in range(0, HIDDEN, CHUNK):
        inner = dot_nt(z, down[at : at + CHUNK, :]) * slope[:, at : at + CHUNK].astype(F32)
        a = inner.astype(LOW)
        ga[:, at : at + CHUNK] = a
        sums.append(column_sum(a.astype(F32)))
    put_halves(gsmall, B_UP, jnp.concatenate(sums, axis=1))
    up = gr2[...] + dot_nt(ga[...], wup.get())
    normal = normal1[...]
    put_halves(gsmall, N1G, column_sum(up * normal))
    put_halves(gsmall, N1B, column_sum(up))
    grad = normalize_back(up, whole(smalls, N1G, 384), normal, inverse1[...])
    gr1[...] = grad
    b = grad.astype(LOW)
    gb[...] = b
    put_halves(gsmall, B_OUT, column_sum(b.astype(F32)))


def heads_back_body(gb, wout, qkv, probs, gqkv, gqv, go):
    go[...] = dot_nt(gb[...], wout.get()).astype(LOW)
    for index, chain, rows, (at_q, at_k, at_v) in places():
        k = qkv[rows, at_k]
        g = split_heads(go[rows, at_q])
        weights = probs[index]
        wide = weights.astype(F32)
        inner = dot_nt(g, qkv[rows, at_v])
        inner = wide * (inner - jnp.sum(wide * inner, axis=-1, keepdims=True))
        s = inner.astype(LOW)
        gqkv[rows, at_q] = (join_heads(dot_nn(s, k)) * SCALE).astype(LOW)
        gqkv[rows, at_k] = (dot_tn(s, split_heads(qkv[rows, at_q])) * SCALE).astype(LOW)
        gqkv[rows, at_v] = dot_tn(weights, g).astype(LOW)
    if gqv is not None:
        gqv[0:1, :] = column_sum(gqkv[:, :WIDTH].astype(F32))
        gqv[1:2, :] = column_sum(gqkv[:, 2 * WIDTH :].astype(F32))


def span_rows(spans, half):
    row = lax.broadcasted_iota(jnp.int32, (ROWS, 1), 0)
    inside = row < 0
    for chain in range(2):
        start = spans[half[0], chain, 0] + chain * LENGTH
        end = spans[half[0], chain, 1] + chain * LENGTH
        inside = inside | ((row >= start) & (row < end))
    return inside


def pick_halves(half, own, other, smalls):
    low = half[0] == 0
    smalls[0:1, :] = jnp.where(low, own[:, :SMALL], other[:, :SMALL])
    smalls[1:2, :] = jnp.where(low, other[:, :SMALL], own[:, :SMALL])


VMEM = pl.BlockSpec(memory_space=pltpu.VMEM)
SMEM = pl.BlockSpec(memory_space=pltpu.SMEM)
ANY = pl.BlockSpec(memory_space=pl.ANY)
SMALL_SCRATCH = pltpu.VMEM((2, SMALL), F32)
QKV_SHAPE = (ROWS, 3 * WIDTH)
PROBS_SHAPE = (2 * PAIRS, 2 * LENGTH, LENGTH)
ROW_SHAPE = (ROWS, WIDTH)
FEED_SHAPE = (ROWS, HIDDEN)
MACS = ROWS * WIDTH * WIDTH * 2
ATTEND_WEIGHTS = [pltpu.VMEM((WIDTH, 3 * WIDTH), LOW), pltpu.VMEM((WIDTH, WIDTH), LOW)]
FEED_WEIGHTS = [pltpu.VMEM((WIDTH, HIDDEN), LOW), pltpu.VMEM((HIDDEN, WIDTH), LOW)]


def shape(dims, kind=LOW):
    return jax.ShapeDtypeStruct(dims, kind)


def enter_cotangent(half, own, swapped, raw, sem):
    @pl.when(half[0] == 0)
    def _():
        pltpu.make_async_copy(own.at[0], raw, sem).start()

    @pl.when(half[0] == 1)
    def _():
        pltpu.make_async_copy(swapped, raw, sem).start()

    return pltpu.make_async_copy(swapped, raw, sem)


def kernel_call(body, ins, outs, scratch, flops, moved, name, out_specs=None, grant=VMEM_LIMIT):
    return pl.pallas_call(
        body,
        in_specs=ins,
        out_specs=out_specs or [VMEM] * len(outs),
        out_shape=outs,
        scratch_shapes=scratch,
        compiler_params=pltpu.CompilerParams(vmem_limit_bytes=grant),
        cost_estimate=pl.CostEstimate(flops=flops, bytes_accessed=moved, transcendentals=0),
        name=name,
    )


def attend_first(inputs, half, lens, spans, weights, smalls):
    def body(x, half, lens, spans, so, sp, qo, qp, oo, op, u, h, raw, small, qkv, mixed, wq, wo, sems):
        enter = pltpu.make_async_copy(x.at[half[0]], raw, sems.at[2, 0])
        enter.start()
        wqkv = Weight(half[0], qo, qp, wq, sems.at[0])
        wout = Weight(half[0], oo, op, wo, sems.at[1])
        pick_halves(half, so, sp, small)
        enter.wait()
        mask = so[:, SMALL:].astype(LOW)
        h[...] = jnp.where(span_rows(spans, half), mask, raw[...].reshape(ROWS, WIDTH))
        attend_body(h, wqkv, wout, small, lens, half, qkv, None, mixed, None, None, u)

    return kernel_call(
        body,
        [ANY, SMEM, SMEM, SMEM, VMEM, VMEM] + [ANY] * 4,
        [shape(ROW_SHAPE), shape(ROW_SHAPE)],
        [
            pltpu.VMEM((2, LENGTH, WIDTH), LOW),
            SMALL_SCRATCH,
            pltpu.VMEM(QKV_SHAPE, LOW),
            pltpu.VMEM(ROW_SHAPE, LOW),
            *ATTEND_WEIGHTS,
            pltpu.SemaphoreType.DMA((3, 2)),
        ],
        40 * MACS,
        80000000,
        "attend_first",
    )(inputs, half, lens, spans, *smalls, *weights[0], *weights[1])


def feed_first(u, half, weights, smalls):
    def body(u, half, so, sp, uo, up, do, dp, y, small, active, wu, wd, sems):
        wup = Weight(half[0], uo, up, wu, sems.at[0])
        wdown = Weight(half[0], do, dp, wd, sems.at[1])
        pick_halves(half, so, sp, small)
        feed_body(u, wup, wdown, small, None, active, None, None, y)

    return kernel_call(
        body,
        [VMEM, SMEM, VMEM, VMEM] + [ANY] * 4,
        [shape(ROW_SHAPE)],
        [
            SMALL_SCRATCH,
            pltpu.VMEM(FEED_SHAPE, LOW),
            *FEED_WEIGHTS,
            pltpu.SemaphoreType.DMA((2, 2)),
        ],
        8 * MACS,
        14000000,
        "feed_first",
    )(u, half, *smalls, *weights[2], *weights[3])[0]


KEPT = [
    shape(ROW_SHAPE),
    shape(QKV_SHAPE),
    shape(PROBS_SHAPE),
    shape(ROW_SHAPE),
    shape(ROW_SHAPE, F32),
    shape((ROWS, 1), F32),
    shape(ROW_SHAPE),
    shape(FEED_SHAPE),
    shape(FEED_SHAPE),
    shape(ROW_SHAPE, F32),
    shape((ROWS, 1), F32),
    shape(ROW_SHAPE),
]


def middle(h0, received, cotangent, swapped, half, first, lens, weights, smalls):
    def body(h0, received, cot, swap, half, first, lens, so, sp, qo, qp, oo, op, uo, up, do, dp, *rest):
        outs, rest = rest[: len(KEPT)], rest[len(KEPT) :]
        both, rest = rest[0], rest[1:]
        gh, small, gr2, gz, ga, gr1, gb, gsmall, gqkv, go, raw, wq, wo, wu, wd = rest[:15]
        keeps, sems, out_sems, raw_sem = rest[15:-3], *rest[-3:]
        h, qkv, probs, mixed, normal1, inverse1, u, slope, active, normal2, inverse2, y = keeps
        wqkv = Weight(half[0], qo, qp, wq, sems.at[0])
        wout = Weight(half[0], oo, op, wo, sems.at[1])
        wup = Weight(half[0], uo, up, wu, sems.at[2])
        wdown = Weight(half[0], do, dp, wd, sems.at[3])
        enter = enter_cotangent(half, cot, swap, raw, raw_sem)
        pick_halves(half, so, sp, small)
        leaving = []

        def leave(places):
            for place in places:
                copy = pltpu.make_async_copy(keeps[place], outs[place], out_sems.at[place])
                copy.start()
                leaving.append(copy)

        h[...] = jnp.where(first[0] > 0, h0[...], received[...])
        attend_body(h, wqkv, wout, small, lens, half, qkv, probs, mixed, normal1, inverse1, u)
        leave(range(7))
        feed_body(u, wup, wdown, small, slope, active, normal2, inverse2, y)
        leave(range(7, 12))
        output = pltpu.make_async_copy(y, both.at[0], out_sems.at[len(KEPT)])
        output.start()
        leaving.append(output)
        enter.wait()
        upstream = raw[...].reshape(ROWS, WIDTH).astype(F32)
        top_back_body(upstream, small, normal2, inverse2, gr2, gz, gsmall)
        feed_back_body(gr2, gz, wup, wdown, small, slope, normal1, inverse1, ga, gr1, gb, gsmall)
        heads_back_body(gb, wout, qkv, probs, gqkv, None, go)
        gh[...] = (gr1[...] + dot_nt(gqkv[...], wqkv.get())).astype(LOW)
        output = pltpu.make_async_copy(gh, both.at[1], out_sems.at[len(KEPT) + 1])
        output.start()
        leaving.append(output)
        for copy in leaving:
            copy.wait()

    return kernel_call(
        body,
        [VMEM, VMEM, ANY, ANY, SMEM, SMEM, SMEM, VMEM, VMEM] + [ANY] * 8,
        KEPT + [shape((2, ROWS, WIDTH)), shape(ROW_SHAPE)],
        [
            SMALL_SCRATCH,
            pltpu.VMEM(ROW_SHAPE, F32),
            pltpu.VMEM(ROW_SHAPE, LOW),
            pltpu.VMEM(FEED_SHAPE, LOW),
            pltpu.VMEM(ROW_SHAPE, F32),
            pltpu.VMEM(ROW_SHAPE, LOW),
            SMALL_SCRATCH,
            pltpu.VMEM(QKV_SHAPE, LOW),
            pltpu.VMEM(ROW_SHAPE, LOW),
            pltpu.VMEM((2, LENGTH, WIDTH), LOW),
            *ATTEND_WEIGHTS,
            *FEED_WEIGHTS,
            *[pltpu.VMEM(kept.shape, kept.dtype) for kept in KEPT],
            pltpu.SemaphoreType.DMA((4, 2)),
            pltpu.SemaphoreType.DMA((len(KEPT) + 2,)),
            pltpu.SemaphoreType.DMA,
        ],
        24 * MACS,
        45000000,
        "middle",
        [ANY] * len(KEPT) + [ANY, VMEM],
        BIG_GRANT,
    )(
        h0, received, cotangent, swapped, half, first, lens, *smalls,
        *weights[0], *weights[1], *weights[2], *weights[3],
    )


MIB = 1024 * 1024


def half_columns(ref, which):
    size = ref.shape[1] // 2
    return ref[:, pl.ds(pl.multiple_of(which * size, 128), size)]


def store_folded(target, at, tensor):
    rows, wide = tensor.shape
    for block in range(wide // WIDTH):
        target[at + block * rows : at + (block + 1) * rows, :] = tensor[
            :, block * WIDTH : (block + 1) * WIDTH
        ].astype(LOW)


class Arriving:
    def __init__(self, pairs, sems):
        self.copies = {}
        for place, (name, source, dest) in enumerate(pairs):
            copy = pltpu.make_async_copy(source, dest, sems.at[place])
            copy.start()
            self.copies[name] = (copy, dest)

    def get(self, name):
        copy, dest = self.copies[name]
        copy.wait()
        return dest


class Leaving:
    def __init__(self, sems):
        self.sems = sems
        self.copies = []

    def send(self, source, target):
        copy = pltpu.make_async_copy(source, target, self.sems.at[len(self.copies)])
        copy.start()
        self.copies.append(copy)

    def wait(self):
        for copy in self.copies:
            copy.wait()


TOKEN = shape((8, 128), F32)
GRAD_SHAPE = (1536, WIDTH)
GRAD_SCRATCH = pltpu.VMEM(GRAD_SHAPE, LOW)


def back_feed(cotangent, swapped, returned, half, first, weights, smalls, kept):
    u, slope, active, n1, i1, n2, i2 = kept

    def body(cot, swap, returned, half, first, so, sp, i1, n2, i2, uo, up, do, dp, u, slope, active, n1, *rest):
        outs, rest = rest[:8], rest[8:]
        down_other, down_own, up_other, up_own, gr1, gb, gsmall, token = outs
        gr2, gz, ga, v0, v1, v2, v3, small, raw, wu, wd, vu, vs, va, vn, sems, in_sems, out_sems = rest
        enter = enter_cotangent(half, cot, swap, raw, sems.at[2, 0])
        arriving = Arriving([("active", active, va)], in_sems)
        wdown = Weight(half[0], do, dp, wd, sems.at[1])
        later = Arriving(
            [("slope", slope, vs), ("normal", n1, vn), ("u", u, vu)],
            in_sems.at[pl.ds(1, 3)],
        )
        wup = Weight(half[0], uo, up, wu, sems.at[0])
        pick_halves(half, so, sp, small)
        enter.wait()
        upstream = jnp.where(first[0] > 0, returned[...], raw[...].reshape(ROWS, WIDTH))
        top_back_body(upstream.astype(F32), small, n2, i2, gr2, gz, gsmall)
        leaving = Leaving(out_sems)
        arriving.get("active")
        for which, local, target in ((1 - half[0], v0, down_other), (half[0], v1, down_own)):
            local[...] = dot_tn(half_columns(va, which), gz[...]).astype(LOW)
            leaving.send(local, target)
        later.get("slope")
        later.get("normal")
        feed_back_body(gr2, gz, wup, wdown, small, vs, vn, i1, ga, gr1, gb, gsmall)
        later.get("u")
        for which, local, target in ((1 - half[0], v2, up_other), (half[0], v3, up_own)):
            store_folded(local, 0, dot_tn(half_columns(vu, which), ga[...]))
            leaving.send(local, target)
        token[...] = jnp.zeros(token.shape, F32)
        leaving.wait()

    return kernel_call(
        body,
        [ANY, ANY, VMEM, SMEM, SMEM] + [VMEM] * 5 + [ANY] * 8,
        [shape(GRAD_SHAPE)] * 4
        + [shape(ROW_SHAPE, F32), shape(ROW_SHAPE), shape((2, SMALL), F32), TOKEN],
        [
            pltpu.VMEM(ROW_SHAPE, F32),
            pltpu.VMEM(ROW_SHAPE, LOW),
            pltpu.VMEM(FEED_SHAPE, LOW),
            *[GRAD_SCRATCH] * 4,
            SMALL_SCRATCH,
            pltpu.VMEM((2, LENGTH, WIDTH), LOW),
            *FEED_WEIGHTS,
            pltpu.VMEM(ROW_SHAPE, LOW),
            pltpu.VMEM(FEED_SHAPE, LOW),
            pltpu.VMEM(FEED_SHAPE, LOW),
            pltpu.VMEM(ROW_SHAPE, F32),
            pltpu.SemaphoreType.DMA((3, 2)),
            pltpu.SemaphoreType.DMA((4,)),
            pltpu.SemaphoreType.DMA((4,)),
        ],
        200 * MACS,
        600000000,
        "back_feed",
        [ANY] * 4 + [VMEM] * 4,
        BIG_GRANT,
    )(
        cotangent, swapped, returned, half, first, *smalls, i1, n2, i2, *weights[2], *weights[3],
        u, slope, active, n1,
    )


def back_attend(gb, gr1, half, first, spans, weights, gsmall, h, qkv, probs, mixed):
    def body(gb, half, first, spans, gsmall, oo, op, qo, qp, gr1, h, qkv, probs, mixed, *rest):
        outs, rest = rest[:6], rest[6:]
        other, own, small_other, small_own, gh, token = outs
        gqkv, go, gqv, vother, vown, wo, wq, vr, vh, vq, vp, vm, sems, in_sems, out_sems = rest
        wout = Weight(half[0], oo, op, wo, sems.at[0])
        arriving = Arriving(
            [("qkv", qkv, vq), ("probs", probs, vp), ("h", h, vh), ("mixed", mixed, vm), ("gr1", gr1, vr)],
            in_sems,
        )
        wqkv = Weight(half[0], qo, qp, wq, sems.at[1])
        arriving.get("qkv")
        arriving.get("probs")
        heads_back_body(gb, wout, vq, vp, gqkv, gqv, go)
        leaving = Leaving(out_sems)
        arriving.get("h")
        arriving.get("mixed")
        for which, local, target in ((1 - half[0], vother, other), (half[0], vown, own)):
            store_folded(local, 0, dot_tn(half_columns(vh, which), gqkv[...]))
            local[1152:, :] = dot_tn(half_columns(vm, which), gb[...]).astype(LOW)
            leaving.send(local, target)
        arriving.get("gr1")
        full = vr[...] + dot_nt(gqkv[...], wqkv.get())
        dropped = span_rows(spans, half) & (first[0] > 0)
        zero = jnp.zeros_like(full)
        gh[...] = jnp.where(dropped, zero, full).astype(LOW)
        gmask = column_sum(jnp.where(dropped, full, zero))
        for which, target in ((1 - half[0], small_other), (half[0], small_own)):
            target[:, :WIDTH] = gqv[pl.ds(which, 1), :]
            target[:, WIDTH:SMALL] = gsmall[pl.ds(which, 1), WIDTH:]
            target[:, SMALL:] = gmask
        token[...] = jnp.zeros(token.shape, F32)
        leaving.wait()

    return kernel_call(
        body,
        [VMEM, SMEM, SMEM, SMEM, VMEM] + [ANY] * 9,
        [
            shape(GRAD_SHAPE),
            shape(GRAD_SHAPE),
            shape((1, SMALL + WIDTH), F32),
            shape((1, SMALL + WIDTH), F32),
            shape(ROW_SHAPE),
            TOKEN,
        ],
        [
            pltpu.VMEM(QKV_SHAPE, LOW),
            pltpu.VMEM(ROW_SHAPE, LOW),
            pltpu.VMEM((2, WIDTH), F32),
            GRAD_SCRATCH,
            GRAD_SCRATCH,
            ATTEND_WEIGHTS[1],
            ATTEND_WEIGHTS[0],
            pltpu.VMEM(ROW_SHAPE, F32),
            pltpu.VMEM(ROW_SHAPE, LOW),
            pltpu.VMEM(QKV_SHAPE, LOW),
            pltpu.VMEM(PROBS_SHAPE, LOW),
            pltpu.VMEM(ROW_SHAPE, LOW),
            pltpu.SemaphoreType.DMA((2, 2)),
            pltpu.SemaphoreType.DMA((5,)),
            pltpu.SemaphoreType.DMA((2,)),
        ],
        180 * MACS,
        400000000,
        "back_attend",
        [ANY, ANY] + [VMEM] * 4,
    )(gb, half, first, spans, gsmall, *weights[1], *weights[0], gr1, h, qkv, probs, mixed)


TAIL = 16
BLOCK = 96


def add_rows(target, sources, at, rows):
    for start in range(0, rows, BLOCK):
        size = min(BLOCK, rows - start)
        place = pl.ds(at + start, size)
        if not isinstance(at, int):
            place = pl.ds(pl.multiple_of(at + start, 16), size)
        if len(sources) == 2:
            target[start : start + size, :] = sources[0][place, :] + sources[1][place, :]
            continue
        total = sources[0][place, :].astype(F32)
        for source in sources[1:]:
            total = total + source[place, :].astype(F32)
        target[start : start + size, :] = total.astype(LOW)


def ordered(
    name, body, ins, outs, where, after, out_specs=None, scratch=(), in_specs=None, grant=16, aliases=None
):
    count, made = len(ins), len(outs)

    def kernel(where, after, *refs):
        refs[count + made][...] = jnp.zeros(TOKEN.shape, F32)
        body(where, refs[:count], refs[count : count + made] + refs[count + made + 1 :])

    result = pl.pallas_call(
        kernel,
        in_specs=[SMEM, ANY] + (in_specs or [VMEM] * count),
        out_specs=(out_specs or [VMEM] * made) + [VMEM],
        out_shape=list(outs) + [TOKEN],
        scratch_shapes=list(scratch),
        input_output_aliases=aliases or {},
        compiler_params=pltpu.CompilerParams(vmem_limit_bytes=grant * MIB),
        cost_estimate=pl.CostEstimate(
            flops=30000000000, bytes_accessed=30000000000, transcendentals=0
        ),
        name=name,
    )(where, after, *ins)
    return result[:made], result[made]


def partner(x, axis, bit):
    return lax.ppermute(x, axis, [(i, i ^ 1 << bit) for i in range(lax.axis_size(axis))])


def moved_on(index, axis, steps):
    z, x, y = index // 8, index // 2 % 4, index % 2
    if axis == "z":
        z = steps(z)
    elif axis == "x":
        x = steps(x)
    else:
        y = steps(y)
    return z * 8 + x * 2 + y


def send_along(value, axes, place):
    pairs = []
    for section in range(4):
        for index in range(32):
            to = moved_on(index, axes[section % 2], place)
            pairs.append((section * 32 + index, section * 32 + to))
    return lax.ppermute(value, ("section", "dp"), pairs)


def exchange(value, part, step):
    flip = 1 if part == step else 3
    return send_along(value, "zx", lambda place: place ^ flip)


def turn(value, steps):
    return send_along(value, "xz", lambda place: (place + steps) % 4)


def across_y(value):
    return send_along(value, "yy", lambda place: place ^ 1)


def swap_core_one(value):
    pairs = [
        (section * 32 + index, section * 32 + (index ^ 1)) for section in (1, 3) for index in range(32)
    ]
    return lax.ppermute(value, ("section", "dp"), pairs)


def between_layers(value, back):
    pairs = []
    for core in range(2):
        for index in range(32):
            pair = (core * 32 + index, (core + 2) * 32 + (index ^ core))
            pairs.append(pair[::-1] if back else pair)
    return lax.ppermute(value, ("section", "dp"), pairs)


def own_places(core):
    index = lax.axis_index("dp")
    z, x = index // 8, index // 2 % 4
    ring = jnp.where(core == 0, z, x)
    high = ring // 2
    low = high ^ (ring % 2)
    table = [low, high, high, low, jnp.where(core == 0, x, z)]
    return jnp.stack(table).astype(jnp.int32)


def row_shapes(*counts):
    return [shape((count, WIDTH)) for count in counts]


def add_tail(target, rows, sources, at, extra):
    if extra:
        total = sources[0][at : at + extra, :].astype(F32)
        for source in sources[1:]:
            total = total + source[at : at + extra, :].astype(F32)
        target[rows : rows + extra, :] = total.astype(LOW)


class Chain:
    def __init__(self, name, places, tail=0):
        self.name = name
        self.places = places
        self.tail = (0, tail)
        self.keep = [None, None]
        self.got = [None, None]

    def kernel(self, name, body, ins, outs, token, *more, **named):
        return ordered(self.name + name, body, ins, outs, self.places, token, *more, **named)

    def pairs(self):
        return (self.keep[0], self.got[0], self.keep[1], self.got[1])

    def start(self, sources, rows, token, tail_ins=(), tail_body=None):
        self.rows = rows // 2
        half_rows, tails = self.rows, self.tail
        arrays = []
        for own, got, _ in sources:
            arrays += [own, got]
        sizes = [pltpu.VMEM((rows, WIDTH), LOW)] * 4

        def body(places, ins, refs):
            outs, held, sems = refs[:4], refs[4:8], refs[8]
            copies = []
            for index in range(4):
                at = sources[index // 2][2]
                copy = pltpu.make_async_copy(
                    ins[index].at[pl.ds(at, rows)], held[index], sems.at[index]
                )
                copy.start()
                copies.append(copy)
            for part in range(2):
                bit = places[2 * part]
                pair = held[2 * part : 2 * part + 2]
                copies[2 * part].wait()
                copies[2 * part + 1].wait()
                for target, which in ((outs[2 * part + 1], 1 - bit), (outs[2 * part], bit)):
                    add_rows(target, pair, which * half_rows, half_rows)
                    if tails[part]:
                        target[half_rows:, :] = tail_body(ins[4:])

        counts = [half_rows + tails[0]] * 2 + [half_rows + tails[1]] * 2
        outs, token = self.kernel(
            "start",
            body,
            tuple(arrays) + tuple(tail_ins),
            row_shapes(*counts),
            token,
            scratch=(*sizes, pltpu.SemaphoreType.DMA((4,))),
            in_specs=[ANY] * 4 + [VMEM] * len(tail_ins),
            grant=50,
        )
        for part in range(2):
            self.keep[part] = outs[2 * part]
            self.got[part] = exchange(outs[2 * part + 1], part, 0)
        return token

    def halve(self, token):
        self.rows //= 2
        rows, tails = self.rows, self.tail

        def body(places, ins, outs):
            for part in range(2):
                bit = places[2 * part + 1]
                pair = ins[2 * part : 2 * part + 2]
                for target, which in ((outs[2 * part + 1], 1 - bit), (outs[2 * part], bit)):
                    add_rows(target, pair, which * rows, rows)
                    add_tail(target, rows, pair, 2 * rows, tails[part])

        counts = [rows + tails[0]] * 2 + [rows + tails[1]] * 2
        outs, token = self.kernel(
            "halve", body, self.pairs(), row_shapes(*counts), token
        )
        for part in range(2):
            self.keep[part] = outs[2 * part]
            self.got[part] = exchange(outs[2 * part + 1], part, 1)
        return token

    def cross(self, token):
        whole_rows, extra = self.rows, self.tail[1]
        rows = whole_rows // 2

        def body(places, ins, refs):
            outs, total = refs[:4], refs[4]
            add_rows(total.at[pl.ds(0, whole_rows)], ins[:2], 0, whole_rows)
            add_rows(total.at[pl.ds(whole_rows, whole_rows)], ins[2:], 0, whole_rows)
            for steps in range(4):
                quarter = (places[4] + steps) % 4
                outs[steps][:rows, :] = total[pl.ds(pl.multiple_of(quarter * rows, 16), rows), :]
                add_tail(outs[steps], rows, ins[2:], whole_rows, extra)

        (self.own, *sends), token = self.kernel(
            "cross",
            body,
            self.pairs(),
            row_shapes(*[rows + extra] * 4),
            token,
            None,
            (pltpu.VMEM((2 * whole_rows, WIDTH), LOW),),
        )
        self.rows = rows
        self.ring = [turn(send, steps) for steps, send in zip((1, 2, 3), sends)]
        return token

    def across(self, token):
        rows = self.rows + self.tail[1]

        def body(places, ins, outs):
            add_rows(outs[0], ins, 0, rows)

        (self.own,), token = self.kernel(
            "across", body, (self.own, *self.ring), row_shapes(rows), token
        )
        self.other = across_y(self.own)
        return token

    def total(self, token, more_outs=(), more_body=None):
        rows, extra = self.rows, self.tail[1]

        def body(places, ins, outs):
            add_rows(outs[0], ins, 0, rows)
            if extra:
                add_rows(outs[1], ins, rows, extra)
                more_body(outs[1][...].astype(F32), outs[2:])

        counts = [rows] + ([extra] if extra else [])
        outs, token = self.kernel(
            "total", body, (self.own, self.other), row_shapes(*counts) + list(more_outs), token
        )
        self.own = outs[0]
        self.tail_sum = outs[1] if extra else None
        self.ring = [turn(self.own, steps) for steps in (1, 2, 3)]
        return outs[2:], token

    def back(self, token, more_ins=(), more_outs=(), more_body=None):
        rows = self.rows

        def body(places, ins, refs):
            outs, total = refs[:-1], refs[-1]
            for steps in range(4):
                quarter = (places[4] - steps + 4) % 4
                total[pl.ds(pl.multiple_of(quarter * rows, 16), rows), :] = ins[steps][...]
            outs[0][...] = total[: 2 * rows, :]
            outs[1][...] = total[2 * rows :, :]
            if more_body is not None:
                more_body(ins[4:], outs[2:])

        outs, token = self.kernel(
            "back",
            body,
            (self.own, *self.ring) + tuple(more_ins),
            row_shapes(2 * rows, 2 * rows) + list(more_outs),
            token,
            None,
            (pltpu.VMEM((4 * rows, WIDTH), LOW),),
        )
        self.rows = 2 * rows
        self.keep = list(outs[:2])
        self.got = [exchange(self.keep[part], part, 1) for part in range(2)]
        return outs[2:], token

    def double(self, token):
        rows = self.rows

        def body(places, ins, outs):
            for part in range(2):
                bit = places[2 * part + 1]
                for which, source in ((bit, ins[2 * part]), (1 - bit, ins[2 * part + 1])):
                    outs[part][pl.ds(pl.multiple_of(which * rows, 16), rows), :] = source[...]

        outs, token = self.kernel(
            "double", body, self.pairs(), row_shapes(2 * rows, 2 * rows), token
        )
        self.rows = 2 * rows
        self.keep = list(outs)
        self.got = [exchange(self.keep[part], part, 0) for part in range(2)]
        return token

    def finish(self, token, outs, place, got):
        rows = self.rows
        mine = tuple(self.got if got else self.keep)
        kept = tuple(outs) if got else ()

        def body(places, ins, refs):
            targets, wide, sems = refs[: len(outs)], refs[-2], refs[-1]
            waits = []
            for part in range(2):
                bit = places[2 * part]
                half = 1 - bit if got else bit
                wide[part] = ins[part][...].astype(F32)
                at = 0
                for size, starts in place(targets, part, half):
                    source, sem = wide.at[part, pl.ds(at, size)], sems.at[len(waits)]
                    starts(source, sem)
                    waits.append((size, source, sem))
                    at += size
            for size, source, sem in waits:
                pltpu.make_async_copy(source, wide.at[0, pl.ds(0, size)], sem).wait()

        return self.kernel(
            "finish",
            body,
            mine + kept,
            [shape(out.shape, F32) for out in outs],
            token,
            out_specs=[ANY] * len(outs),
            scratch=(pltpu.VMEM((2, rows, WIDTH), F32), pltpu.SemaphoreType.DMA((4,))),
            in_specs=[VMEM] * 2 + [ANY] * len(kept),
            grant=24,
            aliases={4 + index: index for index in range(len(kept))},
        )


def copy_to(target):
    return lambda source, sem: pltpu.make_async_copy(source, target, sem).start()


def block_columns(block):
    return pl.ds(pl.multiple_of(block * WIDTH, 128), WIDTH)


def place_x(refs, part, half):
    down, up = refs
    if part == 0:
        return [(768, copy_to(down.at[pl.ds(pl.multiple_of(half * 768, 8), 768)]))]
    return [(384, copy_to(up.at[:, block_columns(2 * half + block)])) for block in range(2)]


def place_y(refs, part, half):
    qkv, out = refs
    if part == 0:
        return [(384, copy_to(qkv.at[:, block_columns(half)]))]

    def starts(source, sem):
        @pl.when(half == 0)
        def _():
            copy_to(qkv.at[:, block_columns(2)])(source, sem)

        @pl.when(half == 1)
        def _():
            copy_to(out)(source, sem)

    return [(384, starts)]


def pack_vectors(vectors):
    size = sum(vector.shape[0] for vector in vectors)
    total = jnp.zeros((size,), F32)
    at = 0
    for vector in vectors:
        total = total + jnp.pad(vector.astype(F32), (at, size - at - vector.shape[0]))
        at += vector.shape[0]
    return total.reshape(1, size)


def per_device(
    inputs,
    cotangent,
    lengths,
    cdr_spans,
    mask_vector,
    w_qkv,
    qv_bias,
    w_out,
    b_out,
    norm1_gain,
    norm1_bias,
    w_up,
    b_up,
    w_down,
    b_down,
    norm2_gain,
    norm2_bias,
):
    section_index = lax.axis_index("section")
    core = section_index % 2
    half = core.astype(jnp.int32).reshape(1)
    first = (section_index < 2).astype(jnp.int32).reshape(1)
    places = own_places(core)
    small = pack_vectors(
        (
            qv_bias,
            b_out,
            norm1_gain,
            norm1_bias,
            b_up,
            b_down,
            norm2_gain,
            norm2_bias,
            mask_vector,
        )
    )
    small_got = partner(small, "section", 0)
    got_qkv, got_out = partner((w_qkv, w_out), "section", 0)
    w_up, w_down, got_qkv, got_out, small_got = lax.optimization_barrier(
        (w_up, w_down, got_qkv, got_out, small_got)
    )
    smalls = (small, small_got)
    got_up, got_down = partner((w_up, w_down), "section", 0)
    weights = [(w_qkv, got_qkv), (w_out, got_out), (w_up, got_up), (w_down, got_down)]

    swapped = swap_core_one(lax.dynamic_index_in_dim(cotangent, 1, 0, keepdims=False))
    lens_got = swap_core_one(lengths)
    swaps = (core == 1) & (section_index >= 2)
    layer_lens = jnp.where(swaps, lens_got, lengths)

    u, h0 = attend_first(inputs, half, lengths, cdr_spans, weights, smalls)
    first_out = feed_first(u, half, weights, smalls)
    received = between_layers(first_out, False)
    kept = middle(h0, received, cotangent, swapped, half, first, layer_lens, weights, smalls)
    h, qkv, probs, mixed, normal1, inverse1, u, slope, active, normal2, inverse2, output = kept[:12]
    returned = between_layers(kept[13], True)
    both, returned = lax.optimization_barrier((kept[12], returned))
    both_got = swap_core_one(both)

    a_other, a_own, b_other, b_own, gr1, gb, gsmall, token = back_feed(
        cotangent,
        swapped,
        returned,
        half,
        first,
        weights,
        smalls,
        (u, slope, active, normal1, inverse1, normal2, inverse2),
    )
    a_got = partner(a_other, "section", 0)
    b_got = partner(b_other, "section", 0)
    x, y = Chain("x_", places), Chain("y_", places, TAIL)
    y_other, y_own, small_other, small_own, gh, token = back_attend(
        gb, gr1, half, first, cdr_spans, weights, gsmall, h, qkv, probs, mixed
    )
    y_got = partner(y_other, "section", 0)
    small_got = partner(small_other, "section", 0)
    token = x.start([(a_own, a_got, 0), (b_own, b_got, 0)], 1536, token)

    def tail_rows(ins):
        total = ins[0][...] + ins[1][...]
        rows = [total[:, at : at + WIDTH] for at in range(0, SMALL + WIDTH, WIDTH)]
        rows.append(jnp.zeros((TAIL - len(rows), WIDTH), F32))
        return jnp.concatenate(rows, axis=0).astype(LOW)

    token = y.start(
        [(y_own, y_got, 0), (y_own, y_got, 768)], 768, token, (small_own, small_got), tail_rows
    )
    token = x.halve(token)
    token = y.halve(token)
    token = x.cross(token)
    token = y.cross(token)
    token = x.across(token)
    token = y.across(token)
    _, token = x.total(token)

    def small_outputs(tail, outs):
        flat = jnp.concatenate([tail[row : row + 1, :] for row in range(6)], axis=1)
        at = 0
        for out, size in zip(outs, SIZES):
            out[...] = flat[0, at : at + size]
            at += size

    out_small, token = y.total(token, [shape((size,), F32) for size in SIZES], small_outputs)
    mask_got = partner(y.tail_sum, "section", 1)
    _, token = x.back(token)

    def mask_output(ins, outs):
        outs[0][...] = ins[0][6, :].astype(F32) + ins[1][6, :].astype(F32)

    (mask_grad,), token = y.back(
        token, (y.tail_sum, mask_got), [shape((WIDTH,), F32)], mask_output
    )
    token = x.double(token)
    token = y.double(token)
    gradients_x = [shape((1536, WIDTH), F32), shape((384, HIDDEN), F32)]
    gradients_y = [shape((384, 3 * WIDTH), F32), shape((384, WIDTH), F32)]
    both_got, token = lax.optimization_barrier((both_got, token))
    gradients_x, token = x.finish(token, gradients_x, place_x, False)
    gradients_y, token = y.finish(token, gradients_y, place_y, False)
    (g_down, g_up), token = x.finish(token, gradients_x, place_x, True)
    (g_qkv, g_out), token = y.finish(token, gradients_y, place_y, True)
    output = jnp.where(swaps, both_got[0], output)
    gh = jnp.where(swaps, both_got[1], gh)

    g_qv, g_bo, g_n1g, g_n1b, g_bu, g_bd, g_n2g, g_n2b = out_small
    return (
        output.reshape(1, 2, LENGTH, WIDTH),
        gh.reshape(1, 2, LENGTH, WIDTH),
        mask_grad,
        g_qkv,
        g_qv,
        g_out,
        g_bo,
        g_n1g,
        g_n1b,
        g_up,
        g_bu,
        g_down,
        g_bd,
        g_n2g,
        g_n2b,
    )


def solution(mesh):
    in_specs = (
        P(None, "dp", None, None),
        P(None, "dp", None, None),
        P(None, "dp"),
        P(None, "dp", None),
        P(),
        P("section", None),
        P("section"),
        P("section", None),
        P("section"),
        P("section"),
        P("section"),
        P("section", None),
        P("section"),
        P("section", None),
        P("section"),
        P("section"),
        P("section"),
    )
    out_specs = (
        P("section", "dp", None, None),
        P("section", "dp", None, None),
        P(),
        P("section", None),
        P("section"),
        P("section", None),
        P("section"),
        P("section"),
        P("section"),
        P("section", None),
        P("section"),
        P("section", None),
        P("section"),
        P("section"),
        P("section"),
    )
    return jax.shard_map(
        per_device, mesh=mesh, in_specs=in_specs, out_specs=out_specs, check_vma=False
    )
```

```python
import functools
import math

import jax
import jax.numpy as jnp
from jax import lax
from jax.experimental import pallas as pl
from jax.experimental.pallas import tpu as pltpu
from jax.sharding import PartitionSpec as P

EPSILON = 1e-05
F32 = jnp.float32
LOW = jnp.bfloat16
WIDTH = 768
LENGTH = 160
ROWS = 320
HIDDEN = 3072
PAIRS = 6
SCALE = 0.125
SIZES = (768, 384, 384, 384, 1536, 384, 384, 384)
QV, B_OUT, N1G, N1B, B_UP, B_DOWN, N2G, N2B = (sum(SIZES[:at]) for at in range(8))
SMALL = sum(SIZES)
VMEM_LIMIT = 63 * 1024 * 1024
BIG_GRANT = 61 * 1024 * 1024


def dot_nn(left_side, right_side):
    return jnp.dot(left_side, right_side, preferred_element_type=F32)


def dot_nt(left_side, right_side):
    return lax.dot_general(
        left_side, right_side, (((1,), (1,)), ((), ())), preferred_element_type=F32
    )


def dot_tn(left_side, right_side):
    return lax.dot_general(
        left_side, right_side, (((0,), (0,)), ((), ())), preferred_element_type=F32
    )


class Weight:
    def __init__(self, half, own, other, dest, sems):
        rows = own.shape[0]
        self.dest = dest
        self.copies = [
            pltpu.make_async_copy(own, dest.at[pl.ds(half * rows, rows)], sems.at[0]),
            pltpu.make_async_copy(other, dest.at[pl.ds((1 - half) * rows, rows)], sems.at[1]),
        ]
        for copy in self.copies:
            copy.start()

    def get(self):
        for copy in self.copies:
            copy.wait()
        self.copies = []
        return self.dest[...]


def whole(smalls, at, size):
    return jnp.concatenate([smalls[0:1, at : at + size], smalls[1:2, at : at + size]], axis=1)


def split_heads(tensor):
    lane = lax.broadcasted_iota(jnp.int32, tensor.shape, 1)
    zero = jnp.zeros_like(tensor)
    return jnp.concatenate(
        [jnp.where(lane < 64, tensor, zero), jnp.where(lane < 64, zero, tensor)], axis=0
    )


def join_heads(tensor):
    lane = lax.broadcasted_iota(jnp.int32, (LENGTH, 128), 1)
    return jnp.where(lane < 64, tensor[:LENGTH], tensor[LENGTH:])


def normalize(values):
    center = values - jnp.mean(values, axis=-1, keepdims=True)
    spread = jnp.mean(center * center, axis=-1, keepdims=True)
    inverse = lax.rsqrt(spread + EPSILON)
    return center * inverse, inverse


def normalize_back(upstream, gain, normal, inverse):
    scaled = upstream * gain
    first = jnp.mean(scaled, axis=-1, keepdims=True)
    second = jnp.mean(scaled * normal, axis=-1, keepdims=True)
    return inverse * (scaled - first - normal * second)


def gelu_parts(values):
    size = jnp.abs(values)
    below = 1.0 + (0.3275911 * math.sqrt(0.5)) * size
    t = pl.reciprocal(below, approx=True)
    t = t * (2.0 - below * t)
    series = t * (
        0.5 * 0.254829592
        + t
        * (
            0.5 * -0.284496736
            + t * (0.5 * 1.421413741 + t * (0.5 * -1.453152027 + t * (0.5 * 1.061405429)))
        )
    )
    bell = jnp.exp(-0.5 * values * values)
    tail = series * bell
    share = jnp.where(values >= 0.0, 1.0 - tail, tail)
    return values * share, share + values * bell * (1.0 / math.sqrt(2.0 * math.pi))


def column_sum(values):
    return jnp.sum(values, axis=0, keepdims=True)


def put_halves(target, at, row):
    size = row.shape[1] // 2
    target[0:1, at : at + size] = row[:, :size]
    target[1:2, at : at + size] = row[:, size:]


def places():
    for index in range(2 * PAIRS):
        chain, pair = divmod(index, PAIRS)
        rows = pl.ds(chain * LENGTH, LENGTH)
        yield index, chain, rows, [pl.ds((pair + block * PAIRS) * 128, 128) for block in range(3)]


def attend_body(h, wqkv, wout, smalls, lens, half, qkv, probs, mixed, normal1, inverse1, u):
    x = h[...]
    bias = jnp.concatenate(
        [smalls[0:1, :WIDTH], jnp.zeros((1, WIDTH), F32), smalls[1:2, :WIDTH]], axis=1
    )
    qkv[...] = (dot_nn(x, wqkv.get()) + bias).astype(LOW)
    for index, chain, rows, (at_q, at_k, at_v) in places():
        scores = dot_nt(split_heads(qkv[rows, at_q]), qkv[rows, at_k]) * SCALE
        key = lax.broadcasted_iota(jnp.int32, scores.shape, 1)
        scores = jnp.where(key < lens[half[0], chain], scores, -1000000000.0)
        grown = jnp.exp(scores - jnp.max(scores, axis=-1, keepdims=True))
        weights = (grown * (1.0 / jnp.sum(grown, axis=-1, keepdims=True))).astype(LOW)
        if probs is not None:
            probs[index] = weights
        mixed[rows, at_q] = join_heads(dot_nn(weights, qkv[rows, at_v])).astype(LOW)
    branch = dot_nn(mixed[...], wout.get()) + whole(smalls, B_OUT, 384)
    normal, inverse = normalize(x.astype(F32) + branch)
    if normal1 is not None:
        normal1[...] = normal
        inverse1[...] = inverse
    u[...] = (normal * whole(smalls, N1G, 384) + whole(smalls, N1B, 384)).astype(LOW)


CHUNK = 1024


def feed_body(u, wup, wdown, smalls, slope, active, normal2, inverse2, y):
    x = u[...]
    bias = whole(smalls, B_UP, 1536)
    up = wup.get()
    for at in range(0, HIDDEN, CHUNK):
        grown, tangent = gelu_parts(dot_nn(x, up[:, at : at + CHUNK]) + bias[:, at : at + CHUNK])
        active[:, at : at + CHUNK] = grown.astype(LOW)
        if slope is not None:
            slope[:, at : at + CHUNK] = tangent.astype(LOW)
    total = x.astype(F32) + whole(smalls, B_DOWN, 384) + dot_nn(active[...], wdown.get())
    normal, inverse = normalize(total)
    if normal2 is not None:
        normal2[...] = normal
        inverse2[...] = inverse
    y[...] = (normal * whole(smalls, N2G, 384) + whole(smalls, N2B, 384)).astype(LOW)


def top_back_body(up, smalls, normal2, inverse2, gr2, gz, gsmall):
    normal = normal2[...]
    put_halves(gsmall, N2G, column_sum(up * normal))
    put_halves(gsmall, N2B, column_sum(up))
    grad = normalize_back(up, whole(smalls, N2G, 384), normal, inverse2[...])
    z = grad.astype(LOW)
    gz[...] = z
    put_halves(gsmall, B_DOWN, column_sum(z.astype(F32)))
    gr2[...] = grad


def feed_back_body(gr2, gz, wup, wdown, smalls, slope, normal1, inverse1, ga, gr1, gb, gsmall):
    z = gz[...]
    down = wdown.get()
    sums = []
    for at in range(0, HIDDEN, CHUNK):
        inner = dot_nt(z, down[at : at + CHUNK, :]) * slope[:, at : at + CHUNK].astype(F32)
        a = inner.astype(LOW)
        ga[:, at : at + CHUNK] = a
        sums.append(column_sum(a.astype(F32)))
    put_halves(gsmall, B_UP, jnp.concatenate(sums, axis=1))
    up = gr2[...] + dot_nt(ga[...], wup.get())
    normal = normal1[...]
    put_halves(gsmall, N1G, column_sum(up * normal))
    put_halves(gsmall, N1B, column_sum(up))
    grad = normalize_back(up, whole(smalls, N1G, 384), normal, inverse1[...])
    gr1[...] = grad
    b = grad.astype(LOW)
    gb[...] = b
    put_halves(gsmall, B_OUT, column_sum(b.astype(F32)))


def heads_back_body(gb, wout, qkv, probs, gqkv, gqv, go):
    go[...] = dot_nt(gb[...], wout.get()).astype(LOW)
    for index, chain, rows, (at_q, at_k, at_v) in places():
        k = qkv[rows, at_k]
        g = split_heads(go[rows, at_q])
        weights = probs[index]
        wide = weights.astype(F32)
        inner = dot_nt(g, qkv[rows, at_v])
        inner = wide * (inner - jnp.sum(wide * inner, axis=-1, keepdims=True))
        s = inner.astype(LOW)
        gqkv[rows, at_q] = (join_heads(dot_nn(s, k)) * SCALE).astype(LOW)
        gqkv[rows, at_k] = (dot_tn(s, split_heads(qkv[rows, at_q])) * SCALE).astype(LOW)
        gqkv[rows, at_v] = dot_tn(weights, g).astype(LOW)
    if gqv is not None:
        gqv[0:1, :] = column_sum(gqkv[:, :WIDTH].astype(F32))
        gqv[1:2, :] = column_sum(gqkv[:, 2 * WIDTH :].astype(F32))


def span_rows(spans, half):
    row = lax.broadcasted_iota(jnp.int32, (ROWS, 1), 0)
    inside = row < 0
    for chain in range(2):
        start = spans[half[0], chain, 0] + chain * LENGTH
        end = spans[half[0], chain, 1] + chain * LENGTH
        inside = inside | ((row >= start) & (row < end))
    return inside


def pick_halves(half, own, other, smalls):
    low = half[0] == 0
    smalls[0:1, :] = jnp.where(low, own[:, :SMALL], other[:, :SMALL])
    smalls[1:2, :] = jnp.where(low, other[:, :SMALL], own[:, :SMALL])


VMEM = pl.BlockSpec(memory_space=pltpu.VMEM)
SMEM = pl.BlockSpec(memory_space=pltpu.SMEM)
ANY = pl.BlockSpec(memory_space=pl.ANY)
SMALL_SCRATCH = pltpu.VMEM((2, SMALL), F32)
QKV_SHAPE = (ROWS, 3 * WIDTH)
PROBS_SHAPE = (2 * PAIRS, 2 * LENGTH, LENGTH)
ROW_SHAPE = (ROWS, WIDTH)
FEED_SHAPE = (ROWS, HIDDEN)
MACS = ROWS * WIDTH * WIDTH * 2
ATTEND_WEIGHTS = [pltpu.VMEM((WIDTH, 3 * WIDTH), LOW), pltpu.VMEM((WIDTH, WIDTH), LOW)]
FEED_WEIGHTS = [pltpu.VMEM((WIDTH, HIDDEN), LOW), pltpu.VMEM((HIDDEN, WIDTH), LOW)]


def shape(dims, kind=LOW):
    return jax.ShapeDtypeStruct(dims, kind)


def enter_cotangent(half, own, swapped, raw, sem):
    @pl.when(half[0] == 0)
    def _():
        pltpu.make_async_copy(own.at[0], raw, sem).start()

    @pl.when(half[0] == 1)
    def _():
        pltpu.make_async_copy(swapped.at[1], raw, sem).start()

    return pltpu.make_async_copy(swapped.at[1], raw, sem)


def kernel_call(body, ins, outs, scratch, flops, moved, name, out_specs=None, grant=VMEM_LIMIT):
    return pl.pallas_call(
        body,
        in_specs=ins,
        out_specs=out_specs or [VMEM] * len(outs),
        out_shape=outs,
        scratch_shapes=scratch,
        compiler_params=pltpu.CompilerParams(vmem_limit_bytes=grant),
        cost_estimate=pl.CostEstimate(flops=flops, bytes_accessed=moved, transcendentals=0),
        name=name,
    )


def attend_first(inputs, half, lens, spans, weights, smalls):
    def body(x, half, lens, spans, so, sp, qo, qp, oo, op, u, h, raw, small, qkv, mixed, wq, wo, sems):
        enter = pltpu.make_async_copy(x.at[half[0]], raw, sems.at[2, 0])
        enter.start()
        wqkv = Weight(half[0], qo, qp, wq, sems.at[0])
        wout = Weight(half[0], oo, op, wo, sems.at[1])
        pick_halves(half, so, sp, small)
        enter.wait()
        mask = so[:, SMALL:].astype(LOW)
        h[...] = jnp.where(span_rows(spans, half), mask, raw[...].reshape(ROWS, WIDTH))
        attend_body(h, wqkv, wout, small, lens, half, qkv, None, mixed, None, None, u)

    return kernel_call(
        body,
        [ANY, SMEM, SMEM, SMEM, VMEM, VMEM] + [ANY] * 4,
        [shape(ROW_SHAPE), shape(ROW_SHAPE)],
        [
            pltpu.VMEM((2, LENGTH, WIDTH), LOW),
            SMALL_SCRATCH,
            pltpu.VMEM(QKV_SHAPE, LOW),
            pltpu.VMEM(ROW_SHAPE, LOW),
            *ATTEND_WEIGHTS,
            pltpu.SemaphoreType.DMA((3, 2)),
        ],
        40 * MACS,
        80000000,
        "attend_first",
    )(inputs, half, lens, spans, *smalls, *weights[0], *weights[1])


def feed_first(u, half, weights, smalls):
    def body(u, half, so, sp, uo, up, do, dp, y, small, active, wu, wd, sems):
        wup = Weight(half[0], uo, up, wu, sems.at[0])
        wdown = Weight(half[0], do, dp, wd, sems.at[1])
        pick_halves(half, so, sp, small)
        feed_body(u, wup, wdown, small, None, active, None, None, y)

    return kernel_call(
        body,
        [VMEM, SMEM, VMEM, VMEM] + [ANY] * 4,
        [shape(ROW_SHAPE)],
        [
            SMALL_SCRATCH,
            pltpu.VMEM(FEED_SHAPE, LOW),
            *FEED_WEIGHTS,
            pltpu.SemaphoreType.DMA((2, 2)),
        ],
        8 * MACS,
        14000000,
        "feed_first",
    )(u, half, *smalls, *weights[2], *weights[3])[0]


KEPT = [
    shape(ROW_SHAPE),
    shape(QKV_SHAPE),
    shape(PROBS_SHAPE),
    shape(ROW_SHAPE),
    shape(ROW_SHAPE, F32),
    shape((ROWS, 1), F32),
    shape(ROW_SHAPE),
    shape(FEED_SHAPE),
    shape(FEED_SHAPE),
    shape(ROW_SHAPE, F32),
    shape((ROWS, 1), F32),
    shape(ROW_SHAPE),
]


def middle(h0, received, cotangent, swapped, half, first, lens, weights, smalls):
    def body(h0, received, cot, swap, half, first, lens, so, sp, qo, qp, oo, op, uo, up, do, dp, *rest):
        outs, rest = rest[: len(KEPT)], rest[len(KEPT) :]
        both, rest = rest[0], rest[1:]
        gh, small, gr2, gz, ga, gr1, gb, gsmall, gqkv, go, raw, wq, wo, wu, wd = rest[:15]
        keeps, sems, out_sems, raw_sem = rest[15:-3], *rest[-3:]
        h, qkv, probs, mixed, normal1, inverse1, u, slope, active, normal2, inverse2, y = keeps
        wqkv = Weight(half[0], qo, qp, wq, sems.at[0])
        wout = Weight(half[0], oo, op, wo, sems.at[1])
        wup = Weight(half[0], uo, up, wu, sems.at[2])
        wdown = Weight(half[0], do, dp, wd, sems.at[3])
        enter = enter_cotangent(half, cot, swap, raw, raw_sem)
        pick_halves(half, so, sp, small)
        leaving = []

        def leave(places):
            for place in places:
                copy = pltpu.make_async_copy(keeps[place], outs[place], out_sems.at[place])
                copy.start()
                leaving.append(copy)

        h[...] = jnp.where(first[0] > 0, h0[...], received[...])
        attend_body(h, wqkv, wout, small, lens, half, qkv, probs, mixed, normal1, inverse1, u)
        leave(range(7))
        feed_body(u, wup, wdown, small, slope, active, normal2, inverse2, y)
        leave(range(7, 12))
        output = pltpu.make_async_copy(y, both.at[0], out_sems.at[len(KEPT)])
        output.start()
        leaving.append(output)
        enter.wait()
        upstream = raw[...].reshape(ROWS, WIDTH).astype(F32)
        top_back_body(upstream, small, normal2, inverse2, gr2, gz, gsmall)
        feed_back_body(gr2, gz, wup, wdown, small, slope, normal1, inverse1, ga, gr1, gb, gsmall)
        heads_back_body(gb, wout, qkv, probs, gqkv, None, go)
        gh[...] = (gr1[...] + dot_nt(gqkv[...], wqkv.get())).astype(LOW)
        output = pltpu.make_async_copy(gh, both.at[1], out_sems.at[len(KEPT) + 1])
        output.start()
        leaving.append(output)
        for copy in leaving:
            copy.wait()

    return kernel_call(
        body,
        [VMEM, VMEM, ANY, ANY, SMEM, SMEM, SMEM, VMEM, VMEM] + [ANY] * 8,
        KEPT + [shape((2, ROWS, WIDTH)), shape(ROW_SHAPE)],
        [
            SMALL_SCRATCH,
            pltpu.VMEM(ROW_SHAPE, F32),
            pltpu.VMEM(ROW_SHAPE, LOW),
            pltpu.VMEM(FEED_SHAPE, LOW),
            pltpu.VMEM(ROW_SHAPE, F32),
            pltpu.VMEM(ROW_SHAPE, LOW),
            SMALL_SCRATCH,
            pltpu.VMEM(QKV_SHAPE, LOW),
            pltpu.VMEM(ROW_SHAPE, LOW),
            pltpu.VMEM((2, LENGTH, WIDTH), LOW),
            *ATTEND_WEIGHTS,
            *FEED_WEIGHTS,
            *[pltpu.VMEM(kept.shape, kept.dtype) for kept in KEPT],
            pltpu.SemaphoreType.DMA((4, 2)),
            pltpu.SemaphoreType.DMA((len(KEPT) + 2,)),
            pltpu.SemaphoreType.DMA,
        ],
        24 * MACS,
        45000000,
        "middle",
        [ANY] * len(KEPT) + [ANY, VMEM],
        BIG_GRANT,
    )(
        h0, received, cotangent, swapped, half, first, lens, *smalls,
        *weights[0], *weights[1], *weights[2], *weights[3],
    )


MIB = 1024 * 1024


def half_columns(ref, which):
    size = ref.shape[1] // 2
    return ref[:, pl.ds(pl.multiple_of(which * size, 128), size)]


def store_folded(target, at, tensor):
    rows, wide = tensor.shape
    for block in range(wide // WIDTH):
        target[at + block * rows : at + (block + 1) * rows, :] = tensor[
            :, block * WIDTH : (block + 1) * WIDTH
        ].astype(LOW)


class Arriving:
    def __init__(self, pairs, sems):
        self.copies = {}
        for place, (name, source, dest) in enumerate(pairs):
            copy = pltpu.make_async_copy(source, dest, sems.at[place])
            copy.start()
            self.copies[name] = (copy, dest)

    def get(self, name):
        copy, dest = self.copies[name]
        copy.wait()
        return dest


class Leaving:
    def __init__(self, sems):
        self.sems = sems
        self.copies = []

    def send(self, source, target):
        copy = pltpu.make_async_copy(source, target, self.sems.at[len(self.copies)])
        copy.start()
        self.copies.append(copy)

    def wait(self):
        for copy in self.copies:
            copy.wait()


TOKEN = shape((8, 128), F32)
GRAD_SHAPE = (1536, WIDTH)
GRAD_SCRATCH = pltpu.VMEM(GRAD_SHAPE, LOW)


def back_feed(cotangent, swapped, returned, half, first, weights, smalls, kept):
    u, slope, active, n1, i1, n2, i2 = kept

    def body(cot, swap, returned, half, first, so, sp, i1, n2, i2, uo, up, do, dp, u, slope, active, n1, *rest):
        outs, rest = rest[:8], rest[8:]
        down_other, down_own, up_other, up_own, gr1, gb, gsmall, token = outs
        gr2, gz, ga, v0, v1, v2, v3, small, raw, wu, wd, vu, vs, va, vn, sems, in_sems, out_sems = rest
        enter = enter_cotangent(half, cot, swap, raw, sems.at[2, 0])
        arriving = Arriving([("active", active, va)], in_sems)
        wdown = Weight(half[0], do, dp, wd, sems.at[1])
        later = Arriving(
            [("slope", slope, vs), ("normal", n1, vn), ("u", u, vu)],
            in_sems.at[pl.ds(1, 3)],
        )
        wup = Weight(half[0], uo, up, wu, sems.at[0])
        pick_halves(half, so, sp, small)
        enter.wait()
        upstream = jnp.where(first[0] > 0, returned[...], raw[...].reshape(ROWS, WIDTH))
        top_back_body(upstream.astype(F32), small, n2, i2, gr2, gz, gsmall)
        leaving = Leaving(out_sems)
        arriving.get("active")
        for which, local, target in ((1 - half[0], v0, down_other), (half[0], v1, down_own)):
            local[...] = dot_tn(half_columns(va, which), gz[...]).astype(LOW)
            leaving.send(local, target)
        later.get("slope")
        later.get("normal")
        feed_back_body(gr2, gz, wup, wdown, small, vs, vn, i1, ga, gr1, gb, gsmall)
        later.get("u")
        for which, local, target in ((1 - half[0], v2, up_other), (half[0], v3, up_own)):
            store_folded(local, 0, dot_tn(half_columns(vu, which), ga[...]))
            leaving.send(local, target)
        token[...] = jnp.zeros(token.shape, F32)
        leaving.wait()

    return kernel_call(
        body,
        [ANY, ANY, VMEM, SMEM, SMEM] + [VMEM] * 5 + [ANY] * 8,
        [shape(GRAD_SHAPE)] * 4
        + [shape(ROW_SHAPE, F32), shape(ROW_SHAPE), shape((2, SMALL), F32), TOKEN],
        [
            pltpu.VMEM(ROW_SHAPE, F32),
            pltpu.VMEM(ROW_SHAPE, LOW),
            pltpu.VMEM(FEED_SHAPE, LOW),
            *[GRAD_SCRATCH] * 4,
            SMALL_SCRATCH,
            pltpu.VMEM((2, LENGTH, WIDTH), LOW),
            *FEED_WEIGHTS,
            pltpu.VMEM(ROW_SHAPE, LOW),
            pltpu.VMEM(FEED_SHAPE, LOW),
            pltpu.VMEM(FEED_SHAPE, LOW),
            pltpu.VMEM(ROW_SHAPE, F32),
            pltpu.SemaphoreType.DMA((3, 2)),
            pltpu.SemaphoreType.DMA((4,)),
            pltpu.SemaphoreType.DMA((4,)),
        ],
        200 * MACS,
        600000000,
        "back_feed",
        [ANY] * 4 + [VMEM] * 4,
        BIG_GRANT,
    )(
        cotangent, swapped, returned, half, first, *smalls, i1, n2, i2, *weights[2], *weights[3],
        u, slope, active, n1,
    )


def back_attend(gb, gr1, half, first, spans, weights, gsmall, h, qkv, probs, mixed):
    def body(gb, half, first, spans, gsmall, oo, op, qo, qp, gr1, h, qkv, probs, mixed, *rest):
        outs, rest = rest[:6], rest[6:]
        other, own, small_other, small_own, gh, token = outs
        gqkv, go, gqv, vother, vown, wo, wq, vr, vh, vq, vp, vm, sems, in_sems, out_sems = rest
        wout = Weight(half[0], oo, op, wo, sems.at[0])
        arriving = Arriving(
            [("qkv", qkv, vq), ("probs", probs, vp), ("h", h, vh), ("mixed", mixed, vm), ("gr1", gr1, vr)],
            in_sems,
        )
        wqkv = Weight(half[0], qo, qp, wq, sems.at[1])
        arriving.get("qkv")
        arriving.get("probs")
        heads_back_body(gb, wout, vq, vp, gqkv, gqv, go)
        leaving = Leaving(out_sems)
        arriving.get("h")
        arriving.get("mixed")
        for which, local, target in ((1 - half[0], vother, other), (half[0], vown, own)):
            store_folded(local, 0, dot_tn(half_columns(vh, which), gqkv[...]))
            local[1152:, :] = dot_tn(half_columns(vm, which), gb[...]).astype(LOW)
            leaving.send(local, target)
        arriving.get("gr1")
        full = vr[...] + dot_nt(gqkv[...], wqkv.get())
        dropped = span_rows(spans, half) & (first[0] > 0)
        zero = jnp.zeros_like(full)
        gh[...] = jnp.where(dropped, zero, full).astype(LOW)
        gmask = column_sum(jnp.where(dropped, full, zero))
        for which, target in ((1 - half[0], small_other), (half[0], small_own)):
            target[:, :WIDTH] = gqv[pl.ds(which, 1), :]
            target[:, WIDTH:SMALL] = gsmall[pl.ds(which, 1), WIDTH:]
            target[:, SMALL:] = gmask
        token[...] = jnp.zeros(token.shape, F32)
        leaving.wait()

    return kernel_call(
        body,
        [VMEM, SMEM, SMEM, SMEM, VMEM] + [ANY] * 9,
        [
            shape(GRAD_SHAPE),
            shape(GRAD_SHAPE),
            shape((1, SMALL + WIDTH), F32),
            shape((1, SMALL + WIDTH), F32),
            shape(ROW_SHAPE),
            TOKEN,
        ],
        [
            pltpu.VMEM(QKV_SHAPE, LOW),
            pltpu.VMEM(ROW_SHAPE, LOW),
            pltpu.VMEM((2, WIDTH), F32),
            GRAD_SCRATCH,
            GRAD_SCRATCH,
            ATTEND_WEIGHTS[1],
            ATTEND_WEIGHTS[0],
            pltpu.VMEM(ROW_SHAPE, F32),
            pltpu.VMEM(ROW_SHAPE, LOW),
            pltpu.VMEM(QKV_SHAPE, LOW),
            pltpu.VMEM(PROBS_SHAPE, LOW),
            pltpu.VMEM(ROW_SHAPE, LOW),
            pltpu.SemaphoreType.DMA((2, 2)),
            pltpu.SemaphoreType.DMA((5,)),
            pltpu.SemaphoreType.DMA((2,)),
        ],
        180 * MACS,
        400000000,
        "back_attend",
        [ANY, ANY] + [VMEM] * 4,
    )(gb, half, first, spans, gsmall, *weights[1], *weights[0], gr1, h, qkv, probs, mixed)


TAIL = 16
BLOCK = 96


def add_rows(target, sources, at, rows):
    for start in range(0, rows, BLOCK):
        size = min(BLOCK, rows - start)
        place = pl.ds(at + start, size)
        if not isinstance(at, int):
            place = pl.ds(pl.multiple_of(at + start, 16), size)
        if len(sources) == 2:
            target[start : start + size, :] = sources[0][place, :] + sources[1][place, :]
            continue
        total = sources[0][place, :].astype(F32)
        for source in sources[1:]:
            total = total + source[place, :].astype(F32)
        target[start : start + size, :] = total.astype(LOW)


LONG = 30000000000


def ordered(
    name, body, ins, outs, where, after, out_specs=None, scratch=(), in_specs=None, grant=16, aliases=None,
    flops=LONG,
):
    count, made = len(ins), len(outs)

    def kernel(where, after, *refs):
        refs[count + made][...] = jnp.zeros(TOKEN.shape, F32)
        body(where, refs[:count], refs[count : count + made] + refs[count + made + 1 :])

    result = pl.pallas_call(
        kernel,
        in_specs=[SMEM, ANY] + (in_specs or [VMEM] * count),
        out_specs=(out_specs or [VMEM] * made) + [VMEM],
        out_shape=list(outs) + [TOKEN],
        scratch_shapes=list(scratch),
        input_output_aliases=aliases or {},
        compiler_params=pltpu.CompilerParams(vmem_limit_bytes=grant * MIB),
        cost_estimate=pl.CostEstimate(flops=flops, bytes_accessed=flops, transcendentals=0),
        name=name,
    )(where, after, *ins)
    return result[:made], result[made]


def partner(x, axis, bit):
    return lax.ppermute(x, axis, [(i, i ^ 1 << bit) for i in range(lax.axis_size(axis))])


def moved_on(index, axis, steps):
    z, x, y = index // 8, index // 2 % 4, index % 2
    if axis == "z":
        z = steps(z)
    elif axis == "x":
        x = steps(x)
    else:
        y = steps(y)
    return z * 8 + x * 2 + y


def send_along(value, axes, place):
    pairs = []
    for section in range(4):
        for index in range(32):
            to = moved_on(index, axes[section % 2], place)
            pairs.append((section * 32 + index, section * 32 + to))
    return lax.ppermute(value, ("section", "dp"), pairs)


def exchange(value, part, step):
    flip = 1 if part == step else 3
    return send_along(value, "zx", lambda place: place ^ flip)


def turn(value, steps):
    return send_along(value, "xz", lambda place: (place + steps) % 4)


def across_y(value):
    return send_along(value, "yy", lambda place: place ^ 1)


def swap_core_one(value):
    pairs = [
        (section * 32 + index, section * 32 + (index ^ 1)) for section in (1, 3) for index in range(32)
    ]
    return lax.ppermute(value, ("section", "dp"), pairs)


def between_layers(value, back):
    pairs = []
    for core in range(2):
        for index in range(32):
            pair = (core * 32 + index, (core + 2) * 32 + (index ^ core))
            pairs.append(pair[::-1] if back else pair)
    return lax.ppermute(value, ("section", "dp"), pairs)


def own_places(core):
    index = lax.axis_index("dp")
    z, x = index // 8, index // 2 % 4
    ring = jnp.where(core == 0, z, x)
    high = ring // 2
    low = high ^ (ring % 2)
    table = [low, high, high, low, jnp.where(core == 0, x, z)]
    return jnp.stack(table).astype(jnp.int32)


def row_shapes(*counts):
    return [shape((count, WIDTH)) for count in counts]


def add_tail(target, rows, sources, at, extra):
    if extra:
        total = sources[0][at : at + extra, :].astype(F32)
        for source in sources[1:]:
            total = total + source[at : at + extra, :].astype(F32)
        target[rows : rows + extra, :] = total.astype(LOW)


class Chain:
    def __init__(self, name, places, tail=0):
        self.name = name
        self.places = places
        self.tail = (0, tail)
        self.keep = [None, None]
        self.got = [None, None]

    def kernel(self, name, body, ins, outs, token, *more, **named):
        return ordered(self.name + name, body, ins, outs, self.places, token, *more, **named)

    def pairs(self):
        return (self.keep[0], self.got[0], self.keep[1], self.got[1])

    def start(self, sources, rows, token, tail_ins=(), tail_body=None):
        self.rows = rows // 2
        half_rows, tails = self.rows, self.tail
        arrays = []
        for own, got, _ in sources:
            arrays += [own, got]

        def body(places, ins, outs):
            for part in range(2):
                bit, at = places[2 * part], sources[part][2]
                pair = ins[2 * part : 2 * part + 2]
                for target, which in ((outs[2 * part + 1], 1 - bit), (outs[2 * part], bit)):
                    add_rows(target, pair, at + which * half_rows, half_rows)
                    if tails[part]:
                        target[half_rows:, :] = tail_body(ins[4:])

        counts = [half_rows + tails[0]] * 2 + [half_rows + tails[1]] * 2
        outs, token = self.kernel(
            "start", body, tuple(arrays) + tuple(tail_ins), row_shapes(*counts), token
        )
        for part in range(2):
            self.keep[part] = outs[2 * part]
            self.got[part] = exchange(outs[2 * part + 1], part, 0)
        return token

    def halve(self, token):
        self.rows //= 2
        rows, tails = self.rows, self.tail

        def body(places, ins, outs):
            for part in range(2):
                bit = places[2 * part + 1]
                pair = ins[2 * part : 2 * part + 2]
                for target, which in ((outs[2 * part + 1], 1 - bit), (outs[2 * part], bit)):
                    add_rows(target, pair, which * rows, rows)
                    add_tail(target, rows, pair, 2 * rows, tails[part])

        counts = [rows + tails[0]] * 2 + [rows + tails[1]] * 2
        outs, token = self.kernel(
            "halve", body, self.pairs(), row_shapes(*counts), token
        )
        for part in range(2):
            self.keep[part] = outs[2 * part]
            self.got[part] = exchange(outs[2 * part + 1], part, 1)
        return token

    def cross(self, token):
        whole_rows, extra = self.rows, self.tail[1]
        rows = whole_rows // 2

        def body(places, ins, refs):
            outs, total = refs[:4], refs[4]
            add_rows(total.at[pl.ds(0, whole_rows)], ins[:2], 0, whole_rows)
            add_rows(total.at[pl.ds(whole_rows, whole_rows)], ins[2:], 0, whole_rows)
            for steps in range(4):
                quarter = (places[4] + steps) % 4
                outs[steps][:rows, :] = total[pl.ds(pl.multiple_of(quarter * rows, 16), rows), :]
                add_tail(outs[steps], rows, ins[2:], whole_rows, extra)

        (self.own, *sends), token = self.kernel(
            "cross",
            body,
            self.pairs(),
            row_shapes(*[rows + extra] * 4),
            token,
            None,
            (pltpu.VMEM((2 * whole_rows, WIDTH), LOW),),
        )
        self.rows = rows
        self.ring = [turn(send, steps) for steps, send in zip((1, 2, 3), sends)]
        return token

    def across(self, token):
        rows = self.rows + self.tail[1]

        def body(places, ins, outs):
            add_rows(outs[0], ins, 0, rows)

        (self.own,), token = self.kernel(
            "across", body, (self.own, *self.ring), row_shapes(rows), token
        )
        self.other = across_y(self.own)
        return token

    def total(self, token, more_outs=(), more_body=None):
        rows, extra = self.rows, self.tail[1]

        def body(places, ins, outs):
            add_rows(outs[0], ins, 0, rows)
            if extra:
                add_rows(outs[1], ins, rows, extra)
                more_body(outs[1][...].astype(F32), outs[2:])

        counts = [rows] + ([extra] if extra else [])
        outs, token = self.kernel(
            "total", body, (self.own, self.other), row_shapes(*counts) + list(more_outs), token
        )
        self.own = outs[0]
        self.tail_sum = outs[1] if extra else None
        self.ring = [turn(self.own, steps) for steps in (1, 2, 3)]
        return outs[2:], token

    def back(self, token, more_ins=(), more_outs=(), more_body=None):
        rows = self.rows

        def body(places, ins, refs):
            outs, total = refs[:-1], refs[-1]
            for steps in range(4):
                quarter = (places[4] - steps + 4) % 4
                total[pl.ds(pl.multiple_of(quarter * rows, 16), rows), :] = ins[steps][...]
            outs[0][...] = total[: 2 * rows, :]
            outs[1][...] = total[2 * rows :, :]
            if more_body is not None:
                more_body(ins[4:], outs[2:])

        outs, token = self.kernel(
            "back",
            body,
            (self.own, *self.ring) + tuple(more_ins),
            row_shapes(2 * rows, 2 * rows) + list(more_outs),
            token,
            None,
            (pltpu.VMEM((4 * rows, WIDTH), LOW),),
        )
        self.rows = 2 * rows
        self.keep = list(outs[:2])
        self.got = [exchange(self.keep[part], part, 1) for part in range(2)]
        return outs[2:], token

    def double(self, token, flops):
        rows = self.rows

        def body(places, ins, outs):
            for part in range(2):
                bit = places[2 * part + 1]
                for which, source in ((bit, ins[2 * part]), (1 - bit, ins[2 * part + 1])):
                    outs[part][pl.ds(pl.multiple_of(which * rows, 16), rows), :] = source[...]

        outs, token = self.kernel(
            "double", body, self.pairs(), row_shapes(2 * rows, 2 * rows), token, flops=flops
        )
        self.rows = 2 * rows
        self.keep = list(outs)
        self.got = [exchange(self.keep[part], part, 0) for part in range(2)]
        return token

    def finish(self, token, outs, place, got, flops):
        rows = self.rows
        mine = tuple(self.got if got else self.keep)
        kept = tuple(outs) if got else ()

        def body(places, ins, refs):
            targets, wide, sems = refs[: len(outs)], refs[-2], refs[-1]
            waits = []
            for part in range(2):
                bit = places[2 * part]
                half = 1 - bit if got else bit
                wide[part] = ins[part][...].astype(F32)
                at = 0
                for size, starts in place(targets, part, half):
                    source, sem = wide.at[part, pl.ds(at, size)], sems.at[len(waits)]
                    starts(source, sem)
                    waits.append((size, source, sem))
                    at += size
            for size, source, sem in waits:
                pltpu.make_async_copy(source, wide.at[0, pl.ds(0, size)], sem).wait()

        return self.kernel(
            "finish",
            body,
            mine + kept,
            [shape(out.shape, F32) for out in outs],
            token,
            out_specs=[ANY] * len(outs),
            scratch=(pltpu.VMEM((2, rows, WIDTH), F32), pltpu.SemaphoreType.DMA((4,))),
            in_specs=[VMEM] * 2 + [ANY] * len(kept),
            grant=24,
            flops=flops,
            aliases={4 + index: index for index in range(len(kept))},
        )


def copy_to(target):
    return lambda source, sem: pltpu.make_async_copy(source, target, sem).start()


def block_columns(block):
    return pl.ds(pl.multiple_of(block * WIDTH, 128), WIDTH)


def place_x(refs, part, half):
    down, up = refs
    if part == 0:
        return [(768, copy_to(down.at[pl.ds(pl.multiple_of(half * 768, 8), 768)]))]
    return [(384, copy_to(up.at[:, block_columns(2 * half + block)])) for block in range(2)]


def place_y(refs, part, half):
    qkv, out = refs
    if part == 0:
        return [(384, copy_to(qkv.at[:, block_columns(half)]))]

    def starts(source, sem):
        @pl.when(half == 0)
        def _():
            copy_to(qkv.at[:, block_columns(2)])(source, sem)

        @pl.when(half == 1)
        def _():
            copy_to(out)(source, sem)

    return [(384, starts)]


def pack_vectors(vectors):
    size = sum(vector.shape[0] for vector in vectors)
    total = jnp.zeros((size,), F32)
    at = 0
    for vector in vectors:
        total = total + jnp.pad(vector.astype(F32), (at, size - at - vector.shape[0]))
        at += vector.shape[0]
    return total.reshape(1, size)


def per_device(
    inputs,
    cotangent,
    lengths,
    cdr_spans,
    mask_vector,
    w_qkv,
    qv_bias,
    w_out,
    b_out,
    norm1_gain,
    norm1_bias,
    w_up,
    b_up,
    w_down,
    b_down,
    norm2_gain,
    norm2_bias,
):
    section_index = lax.axis_index("section")
    core = section_index % 2
    half = core.astype(jnp.int32).reshape(1)
    first = (section_index < 2).astype(jnp.int32).reshape(1)
    places = own_places(core)
    small = pack_vectors(
        (
            qv_bias,
            b_out,
            norm1_gain,
            norm1_bias,
            b_up,
            b_down,
            norm2_gain,
            norm2_bias,
            mask_vector,
        )
    )
    small_got = partner(small, "section", 0)
    got_qkv, got_out = partner((w_qkv, w_out), "section", 0)
    w_up, w_down, got_qkv, got_out, small_got = lax.optimization_barrier(
        (w_up, w_down, got_qkv, got_out, small_got)
    )
    smalls = (small, small_got)
    got_up, got_down = partner((w_up, w_down), "section", 0)
    weights = [(w_qkv, got_qkv), (w_out, got_out), (w_up, got_up), (w_down, got_down)]

    swapped = swap_core_one(cotangent)
    lens_got = swap_core_one(lengths)
    swaps = (core == 1) & (section_index >= 2)
    layer_lens = jnp.where(swaps, lens_got, lengths)

    u, h0 = attend_first(inputs, half, lengths, cdr_spans, weights, smalls)
    first_out = feed_first(u, half, weights, smalls)
    received = between_layers(first_out, False)
    kept = middle(h0, received, cotangent, swapped, half, first, layer_lens, weights, smalls)
    h, qkv, probs, mixed, normal1, inverse1, u, slope, active, normal2, inverse2, output = kept[:12]
    returned = between_layers(kept[13], True)
    both, returned = lax.optimization_barrier((kept[12], returned))
    both_got = swap_core_one(both)

    a_other, a_own, b_other, b_own, gr1, gb, gsmall, token = back_feed(
        cotangent,
        swapped,
        returned,
        half,
        first,
        weights,
        smalls,
        (u, slope, active, normal1, inverse1, normal2, inverse2),
    )
    a_got = partner(a_other, "section", 0)
    b_got = partner(b_other, "section", 0)
    x, y = Chain("x_", places), Chain("y_", places, TAIL)
    y_other, y_own, small_other, small_own, gh, token = back_attend(
        gb, gr1, half, first, cdr_spans, weights, gsmall, h, qkv, probs, mixed
    )
    y_got = partner(y_other, "section", 0)
    small_got = partner(small_other, "section", 0)
    token = x.start([(a_own, a_got, 0), (b_own, b_got, 0)], 1536, token)

    def tail_rows(ins):
        total = ins[0][...] + ins[1][...]
        rows = [total[:, at : at + WIDTH] for at in range(0, SMALL + WIDTH, WIDTH)]
        rows.append(jnp.zeros((TAIL - len(rows), WIDTH), F32))
        return jnp.concatenate(rows, axis=0).astype(LOW)

    token = y.start(
        [(y_own, y_got, 0), (y_own, y_got, 768)], 768, token, (small_own, small_got), tail_rows
    )
    token = x.halve(token)
    token = y.halve(token)
    token = x.cross(token)
    token = y.cross(token)
    token = x.across(token)
    token = y.across(token)
    _, token = x.total(token)

    def small_outputs(tail, outs):
        flat = jnp.concatenate([tail[row : row + 1, :] for row in range(6)], axis=1)
        at = 0
        for out, size in zip(outs, SIZES):
            out[...] = flat[0, at : at + size]
            at += size

    out_small, token = y.total(token, [shape((size,), F32) for size in SIZES], small_outputs)
    mask_got = partner(y.tail_sum, "section", 1)
    _, token = x.back(token)

    def mask_output(ins, outs):
        outs[0][...] = ins[0][6, :].astype(F32) + ins[1][6, :].astype(F32)

    (mask_grad,), token = y.back(
        token, (y.tail_sum, mask_got), [shape((WIDTH,), F32)], mask_output
    )
    gradients_x = [shape((1536, WIDTH), F32), shape((384, HIDDEN), F32)]
    gradients_y = [shape((384, 3 * WIDTH), F32), shape((384, WIDTH), F32)]
    token = x.double(token, LONG)
    gradients_x, token = x.finish(token, gradients_x, place_x, False, LONG)
    token = y.double(token, 0)
    gradients_y, token = y.finish(token, gradients_y, place_y, False, 0)
    both_got, token = lax.optimization_barrier((both_got, token))
    (g_down, g_up), token = x.finish(token, gradients_x, place_x, True, LONG)
    (g_qkv, g_out), token = y.finish(token, gradients_y, place_y, True, LONG)
    output = jnp.where(swaps, both_got[0], output)
    gh = jnp.where(swaps, both_got[1], gh)

    g_qv, g_bo, g_n1g, g_n1b, g_bu, g_bd, g_n2g, g_n2b = out_small
    return (
        output.reshape(1, 2, LENGTH, WIDTH),
        gh.reshape(1, 2, LENGTH, WIDTH),
        mask_grad,
        g_qkv,
        g_qv,
        g_out,
        g_bo,
        g_n1g,
        g_n1b,
        g_up,
        g_bu,
        g_down,
        g_bd,
        g_n2g,
        g_n2b,
    )


def solution(mesh):
    in_specs = (
        P(None, "dp", None, None),
        P(None, "dp", None, None),
        P(None, "dp"),
        P(None, "dp", None),
        P(),
        P("section", None),
        P("section"),
        P("section", None),
        P("section"),
        P("section"),
        P("section"),
        P("section", None),
        P("section"),
        P("section", None),
        P("section"),
        P("section"),
        P("section"),
    )
    out_specs = (
        P("section", "dp", None, None),
        P("section", "dp", None, None),
        P(),
        P("section", None),
        P("section"),
        P("section", None),
        P("section"),
        P("section"),
        P("section"),
        P("section", None),
        P("section"),
        P("section", None),
        P("section"),
        P("section"),
        P("section"),
    )
    return jax.shard_map(
        per_device, mesh=mesh, in_specs=in_specs, out_specs=out_specs, check_vma=False
    )
```

```python
import functools
import math

import jax
import jax.numpy as jnp
from jax import lax
from jax.experimental import pallas as pl
from jax.experimental.pallas import tpu as pltpu
from jax.sharding import PartitionSpec as P

EPSILON = 1e-05
F32 = jnp.float32
LOW = jnp.bfloat16
WIDTH = 768
LENGTH = 160
ROWS = 320
HIDDEN = 3072
PAIRS = 6
SCALE = 0.125
SIZES = (768, 384, 384, 384, 1536, 384, 384, 384)
QV, B_OUT, N1G, N1B, B_UP, B_DOWN, N2G, N2B = (sum(SIZES[:at]) for at in range(8))
SMALL = sum(SIZES)
VMEM_LIMIT = 63 * 1024 * 1024
BIG_GRANT = 61 * 1024 * 1024


def dot_nn(left_side, right_side):
    return jnp.dot(left_side, right_side, preferred_element_type=F32)


def dot_nt(left_side, right_side):
    return lax.dot_general(
        left_side, right_side, (((1,), (1,)), ((), ())), preferred_element_type=F32
    )


def dot_tn(left_side, right_side):
    return lax.dot_general(
        left_side, right_side, (((0,), (0,)), ((), ())), preferred_element_type=F32
    )


class Weight:
    def __init__(self, half, own, other, dest, sems, start=True):
        rows = own.shape[0]
        self.dest = dest
        self.copies = [
            pltpu.make_async_copy(own, dest.at[pl.ds(half * rows, rows)], sems.at[0]),
            pltpu.make_async_copy(other, dest.at[pl.ds((1 - half) * rows, rows)], sems.at[1]),
        ]
        if start:
            self.start()

    def start(self):
        for copy in self.copies:
            copy.start()

    def get(self):
        for copy in self.copies:
            copy.wait()
        self.copies = []
        return self.dest[...]


def whole(smalls, at, size):
    return jnp.concatenate([smalls[0:1, at : at + size], smalls[1:2, at : at + size]], axis=1)


def split_heads(tensor):
    lane = lax.broadcasted_iota(jnp.int32, tensor.shape, 1)
    zero = jnp.zeros_like(tensor)
    return jnp.concatenate(
        [jnp.where(lane < 64, tensor, zero), jnp.where(lane < 64, zero, tensor)], axis=0
    )


def join_heads(tensor):
    lane = lax.broadcasted_iota(jnp.int32, (LENGTH, 128), 1)
    return jnp.where(lane < 64, tensor[:LENGTH], tensor[LENGTH:])


def normalize(values):
    center = values - jnp.mean(values, axis=-1, keepdims=True)
    spread = jnp.mean(center * center, axis=-1, keepdims=True)
    inverse = lax.rsqrt(spread + EPSILON)
    return center * inverse, inverse


def normalize_back(upstream, gain, normal, inverse):
    scaled = upstream * gain
    first = jnp.mean(scaled, axis=-1, keepdims=True)
    second = jnp.mean(scaled * normal, axis=-1, keepdims=True)
    return inverse * (scaled - first - normal * second)


def gelu_parts(values):
    size = jnp.abs(values)
    below = 1.0 + (0.3275911 * math.sqrt(0.5)) * size
    t = pl.reciprocal(below, approx=True)
    t = t * (2.0 - below * t)
    series = t * (
        0.5 * 0.254829592
        + t
        * (
            0.5 * -0.284496736
            + t * (0.5 * 1.421413741 + t * (0.5 * -1.453152027 + t * (0.5 * 1.061405429)))
        )
    )
    bell = jnp.exp(-0.5 * values * values)
    tail = series * bell
    share = jnp.where(values >= 0.0, 1.0 - tail, tail)
    return values * share, share + values * bell * (1.0 / math.sqrt(2.0 * math.pi))


def column_sum(values):
    return jnp.sum(values, axis=0, keepdims=True)


def put_halves(target, at, row):
    size = row.shape[1] // 2
    target[0:1, at : at + size] = row[:, :size]
    target[1:2, at : at + size] = row[:, size:]


def places():
    for index in range(2 * PAIRS):
        chain, pair = divmod(index, PAIRS)
        rows = pl.ds(chain * LENGTH, LENGTH)
        yield index, chain, rows, [pl.ds((pair + block * PAIRS) * 128, 128) for block in range(3)]


def attend_body(h, wqkv, wout, smalls, lens, half, qkv, probs, mixed, normal1, inverse1, u, later):
    x = h[...]
    bias = jnp.concatenate(
        [smalls[0:1, :WIDTH], jnp.zeros((1, WIDTH), F32), smalls[1:2, :WIDTH]], axis=1
    )
    matrix = wqkv.get()
    for each in later:
        each.start()
    qkv[...] = (dot_nn(x, matrix) + bias).astype(LOW)
    for index, chain, rows, (at_q, at_k, at_v) in places():
        scores = dot_nt(qkv[rows, at_k], split_heads(qkv[rows, at_q])) * SCALE
        key = lax.broadcasted_iota(jnp.int32, scores.shape, 0)
        scores = jnp.where(key < lens[half[0], chain], scores, -1000000000.0)
        grown = jnp.exp(scores - jnp.max(scores, axis=0, keepdims=True))
        weights = (grown * (1.0 / jnp.sum(grown, axis=0, keepdims=True))).astype(LOW)
        if probs is not None:
            probs[index] = weights
        mixed[rows, at_q] = join_heads(dot_tn(weights, qkv[rows, at_v])).astype(LOW)
    branch = dot_nn(mixed[...], wout.get()) + whole(smalls, B_OUT, 384)
    normal, inverse = normalize(x.astype(F32) + branch)
    if normal1 is not None:
        normal1[...] = normal
        inverse1[...] = inverse
    u[...] = (normal * whole(smalls, N1G, 384) + whole(smalls, N1B, 384)).astype(LOW)


CHUNK = 1024


def feed_body(u, wup, wdown, smalls, slope, active, normal2, inverse2, y, later=()):
    x = u[...]
    bias = whole(smalls, B_UP, 1536)
    up = wup.get()
    for each in later:
        each.start()
    for at in range(0, HIDDEN, CHUNK):
        grown, tangent = gelu_parts(dot_nn(x, up[:, at : at + CHUNK]) + bias[:, at : at + CHUNK])
        active[:, at : at + CHUNK] = grown.astype(LOW)
        if slope is not None:
            slope[:, at : at + CHUNK] = tangent.astype(LOW)
    total = x.astype(F32) + whole(smalls, B_DOWN, 384) + dot_nn(active[...], wdown.get())
    normal, inverse = normalize(total)
    if normal2 is not None:
        normal2[...] = normal
        inverse2[...] = inverse
    y[...] = (normal * whole(smalls, N2G, 384) + whole(smalls, N2B, 384)).astype(LOW)


def top_back_body(up, smalls, normal2, inverse2, gr2, gz, gsmall):
    normal = normal2[...]
    put_halves(gsmall, N2G, column_sum(up * normal))
    put_halves(gsmall, N2B, column_sum(up))
    grad = normalize_back(up, whole(smalls, N2G, 384), normal, inverse2[...])
    z = grad.astype(LOW)
    gz[...] = z
    put_halves(gsmall, B_DOWN, column_sum(z.astype(F32)))
    gr2[...] = grad


def feed_back_body(gr2, gz, wup, wdown, smalls, slope, normal1, inverse1, ga, gr1, gb, gsmall):
    z = gz[...]
    down = wdown.get()
    sums = []
    for at in range(0, HIDDEN, CHUNK):
        inner = dot_nt(z, down[at : at + CHUNK, :]) * slope[:, at : at + CHUNK].astype(F32)
        a = inner.astype(LOW)
        ga[:, at : at + CHUNK] = a
        sums.append(column_sum(a.astype(F32)))
    put_halves(gsmall, B_UP, jnp.concatenate(sums, axis=1))
    up = gr2[...] + dot_nt(ga[...], wup.get())
    normal = normal1[...]
    put_halves(gsmall, N1G, column_sum(up * normal))
    put_halves(gsmall, N1B, column_sum(up))
    grad = normalize_back(up, whole(smalls, N1G, 384), normal, inverse1[...])
    gr1[...] = grad
    b = grad.astype(LOW)
    gb[...] = b
    put_halves(gsmall, B_OUT, column_sum(b.astype(F32)))


def heads_back_body(gb, wout, qkv, probs, gqkv, gqv, go):
    go[...] = dot_nt(gb[...], wout.get()).astype(LOW)
    for index, chain, rows, (at_q, at_k, at_v) in places():
        k = qkv[rows, at_k]
        g = split_heads(go[rows, at_q])
        weights = probs[index]
        wide = weights.astype(F32)
        inner = dot_nt(qkv[rows, at_v], g)
        inner = wide * (inner - jnp.sum(wide * inner, axis=0, keepdims=True))
        s = inner.astype(LOW)
        gqkv[rows, at_q] = (join_heads(dot_tn(s, k)) * SCALE).astype(LOW)
        gqkv[rows, at_k] = (dot_nn(s, split_heads(qkv[rows, at_q])) * SCALE).astype(LOW)
        gqkv[rows, at_v] = dot_nn(weights, g).astype(LOW)
    if gqv is not None:
        gqv[0:1, :] = column_sum(gqkv[:, :WIDTH].astype(F32))
        gqv[1:2, :] = column_sum(gqkv[:, 2 * WIDTH :].astype(F32))


def span_rows(spans, half):
    row = lax.broadcasted_iota(jnp.int32, (ROWS, 1), 0)
    inside = row < 0
    for chain in range(2):
        start = spans[half[0], chain, 0] + chain * LENGTH
        end = spans[half[0], chain, 1] + chain * LENGTH
        inside = inside | ((row >= start) & (row < end))
    return inside


def pick_halves(half, own, other, smalls):
    low = half[0] == 0
    smalls[0:1, :] = jnp.where(low, own[:, :SMALL], other[:, :SMALL])
    smalls[1:2, :] = jnp.where(low, other[:, :SMALL], own[:, :SMALL])


VMEM = pl.BlockSpec(memory_space=pltpu.VMEM)
SMEM = pl.BlockSpec(memory_space=pltpu.SMEM)
ANY = pl.BlockSpec(memory_space=pl.ANY)
SMALL_SCRATCH = pltpu.VMEM((2, SMALL), F32)
QKV_SHAPE = (ROWS, 3 * WIDTH)
PROBS_SHAPE = (2 * PAIRS, LENGTH, 2 * LENGTH)
ROW_SHAPE = (ROWS, WIDTH)
FEED_SHAPE = (ROWS, HIDDEN)
MACS = ROWS * WIDTH * WIDTH * 2
ATTEND_WEIGHTS = [pltpu.VMEM((WIDTH, 3 * WIDTH), LOW), pltpu.VMEM((WIDTH, WIDTH), LOW)]
FEED_WEIGHTS = [pltpu.VMEM((WIDTH, HIDDEN), LOW), pltpu.VMEM((HIDDEN, WIDTH), LOW)]


def shape(dims, kind=LOW):
    return jax.ShapeDtypeStruct(dims, kind)


def enter_cotangent(half, own, swapped, raw, sem):
    @pl.when(half[0] == 0)
    def _():
        pltpu.make_async_copy(own.at[0], raw, sem).start()

    @pl.when(half[0] == 1)
    def _():
        pltpu.make_async_copy(swapped.at[1], raw, sem).start()

    return pltpu.make_async_copy(swapped.at[1], raw, sem)


def kernel_call(body, ins, outs, scratch, flops, moved, name, out_specs=None, grant=VMEM_LIMIT):
    return pl.pallas_call(
        body,
        in_specs=ins,
        out_specs=out_specs or [VMEM] * len(outs),
        out_shape=outs,
        scratch_shapes=scratch,
        compiler_params=pltpu.CompilerParams(vmem_limit_bytes=grant),
        cost_estimate=pl.CostEstimate(flops=flops, bytes_accessed=moved, transcendentals=0),
        name=name,
    )


def attend_first(inputs, half, lens, spans, weights, smalls):
    def body(x, half, lens, spans, so, sp, qo, qp, oo, op, u, h, raw, small, qkv, mixed, wq, wo, sems):
        enter = pltpu.make_async_copy(x.at[half[0]], raw, sems.at[2, 0])
        enter.start()
        wqkv = Weight(half[0], qo, qp, wq, sems.at[0])
        wout = Weight(half[0], oo, op, wo, sems.at[1], False)
        pick_halves(half, so, sp, small)
        enter.wait()
        mask = so[:, SMALL:].astype(LOW)
        h[...] = jnp.where(span_rows(spans, half), mask, raw[...].reshape(ROWS, WIDTH))
        attend_body(h, wqkv, wout, small, lens, half, qkv, None, mixed, None, None, u, [wout])

    return kernel_call(
        body,
        [ANY, SMEM, SMEM, SMEM, VMEM, VMEM] + [ANY] * 4,
        [shape(ROW_SHAPE), shape(ROW_SHAPE)],
        [
            pltpu.VMEM((2, LENGTH, WIDTH), LOW),
            SMALL_SCRATCH,
            pltpu.VMEM(QKV_SHAPE, LOW),
            pltpu.VMEM(ROW_SHAPE, LOW),
            *ATTEND_WEIGHTS,
            pltpu.SemaphoreType.DMA((3, 2)),
        ],
        40 * MACS,
        80000000,
        "attend_first",
    )(inputs, half, lens, spans, *smalls, *weights[0], *weights[1])


def feed_first(u, half, weights, smalls):
    def body(u, half, so, sp, uo, up, do, dp, y, small, active, wu, wd, sems):
        wup = Weight(half[0], uo, up, wu, sems.at[0])
        wdown = Weight(half[0], do, dp, wd, sems.at[1], False)
        pick_halves(half, so, sp, small)
        feed_body(u, wup, wdown, small, None, active, None, None, y, [wdown])

    return kernel_call(
        body,
        [VMEM, SMEM, VMEM, VMEM] + [ANY] * 4,
        [shape(ROW_SHAPE)],
        [
            SMALL_SCRATCH,
            pltpu.VMEM(FEED_SHAPE, LOW),
            *FEED_WEIGHTS,
            pltpu.SemaphoreType.DMA((2, 2)),
        ],
        8 * MACS,
        14000000,
        "feed_first",
    )(u, half, *smalls, *weights[2], *weights[3])[0]


KEPT = [
    shape(ROW_SHAPE),
    shape(QKV_SHAPE),
    shape(PROBS_SHAPE),
    shape(ROW_SHAPE),
    shape(ROW_SHAPE, F32),
    shape((ROWS, 1), F32),
    shape(ROW_SHAPE),
    shape(FEED_SHAPE),
    shape(FEED_SHAPE),
    shape(ROW_SHAPE, F32),
    shape((ROWS, 1), F32),
    shape(ROW_SHAPE),
]


def middle(h0, received, cotangent, swapped, half, first, lens, weights, smalls):
    def body(h0, received, cot, swap, half, first, lens, so, sp, qo, qp, oo, op, uo, up, do, dp, *rest):
        outs, rest = rest[: len(KEPT)], rest[len(KEPT) :]
        both, rest = rest[0], rest[1:]
        gh, small, gr2, gz, ga, gr1, gb, gsmall, gqkv, go, raw, wq, wo, wu, wd = rest[:15]
        keeps, sems, out_sems, raw_sem = rest[15:-3], *rest[-3:]
        h, qkv, probs, mixed, normal1, inverse1, u, slope, active, normal2, inverse2, y = keeps
        wqkv = Weight(half[0], qo, qp, wq, sems.at[0])
        wout = Weight(half[0], oo, op, wo, sems.at[1], False)
        wup = Weight(half[0], uo, up, wu, sems.at[2], False)
        wdown = Weight(half[0], do, dp, wd, sems.at[3], False)
        pick_halves(half, so, sp, small)
        leaving = []

        def leave(places):
            for place in places:
                copy = pltpu.make_async_copy(keeps[place], outs[place], out_sems.at[place])
                copy.start()
                leaving.append(copy)

        h[...] = jnp.where(first[0] > 0, h0[...], received[...])
        attend_body(
            h, wqkv, wout, small, lens, half, qkv, probs, mixed, normal1, inverse1, u,
            [wout, wup, wdown],
        )
        enter = enter_cotangent(half, cot, swap, raw, raw_sem)
        leave(range(7))
        feed_body(u, wup, wdown, small, slope, active, normal2, inverse2, y)
        leave(range(7, 12))
        output = pltpu.make_async_copy(y, both.at[0], out_sems.at[len(KEPT)])
        output.start()
        leaving.append(output)
        enter.wait()
        upstream = raw[...].reshape(ROWS, WIDTH).astype(F32)
        top_back_body(upstream, small, normal2, inverse2, gr2, gz, gsmall)
        feed_back_body(gr2, gz, wup, wdown, small, slope, normal1, inverse1, ga, gr1, gb, gsmall)
        heads_back_body(gb, wout, qkv, probs, gqkv, None, go)
        gh[...] = (gr1[...] + dot_nt(gqkv[...], wqkv.get())).astype(LOW)
        output = pltpu.make_async_copy(gh, both.at[1], out_sems.at[len(KEPT) + 1])
        output.start()
        leaving.append(output)
        for copy in leaving:
            copy.wait()

    return kernel_call(
        body,
        [VMEM, VMEM, ANY, ANY, SMEM, SMEM, SMEM, VMEM, VMEM] + [ANY] * 8,
        KEPT + [shape((2, ROWS, WIDTH)), shape(ROW_SHAPE)],
        [
            SMALL_SCRATCH,
            pltpu.VMEM(ROW_SHAPE, F32),
            pltpu.VMEM(ROW_SHAPE, LOW),
            pltpu.VMEM(FEED_SHAPE, LOW),
            pltpu.VMEM(ROW_SHAPE, F32),
            pltpu.VMEM(ROW_SHAPE, LOW),
            SMALL_SCRATCH,
            pltpu.VMEM(QKV_SHAPE, LOW),
            pltpu.VMEM(ROW_SHAPE, LOW),
            pltpu.VMEM((2, LENGTH, WIDTH), LOW),
            *ATTEND_WEIGHTS,
            *FEED_WEIGHTS,
            *[pltpu.VMEM(kept.shape, kept.dtype) for kept in KEPT],
            pltpu.SemaphoreType.DMA((4, 2)),
            pltpu.SemaphoreType.DMA((len(KEPT) + 2,)),
            pltpu.SemaphoreType.DMA,
        ],
        24 * MACS,
        45000000,
        "middle",
        [ANY] * len(KEPT) + [ANY, VMEM],
        BIG_GRANT,
    )(
        h0, received, cotangent, swapped, half, first, lens, *smalls,
        *weights[0], *weights[1], *weights[2], *weights[3],
    )


MIB = 1024 * 1024


def half_columns(ref, which):
    size = ref.shape[1] // 2
    return ref[:, pl.ds(pl.multiple_of(which * size, 128), size)]


class Arriving:
    def __init__(self, pairs, sems):
        self.copies = {}
        for place, (name, source, dest) in enumerate(pairs):
            copy = pltpu.make_async_copy(source, dest, sems.at[place])
            copy.start()
            self.copies[name] = (copy, dest)

    def get(self, name):
        copy, dest = self.copies[name]
        copy.wait()
        return dest


class Leaving:
    def __init__(self, sems):
        self.sems = sems
        self.copies = []

    def send(self, source, target):
        copy = pltpu.make_async_copy(source, target, self.sems.at[len(self.copies)])
        copy.start()
        self.copies.append(copy)

    def wait(self):
        for copy in self.copies:
            copy.wait()


def send_folded(leaving, local, target, left_side, right):
    for block in range(right.shape[1] // WIDTH):
        rows = pl.ds(block * 384, 384)
        grad = dot_tn(left_side, right[:, block * WIDTH : (block + 1) * WIDTH])
        local[rows, :] = grad.astype(LOW)
        leaving.send(local.at[rows], target.at[rows])


TOKEN = shape((8, 128), F32)
GRAD_SHAPE = (1536, WIDTH)
GRAD_SCRATCH = pltpu.VMEM(GRAD_SHAPE, LOW)


def back_feed(cotangent, swapped, returned, half, first, weights, smalls, kept):
    u, slope, active, n1, i1, n2, i2 = kept

    def body(cot, swap, returned, half, first, so, sp, i1, n2, i2, uo, up, do, dp, u, slope, active, n1, *rest):
        outs, rest = rest[:8], rest[8:]
        down_other, down_own, up_other, up_own, gr1, gb, gsmall, token = outs
        gr2, gz, ga, v0, v1, v2, v3, small, raw, wu, wd, vu, vs, va, vn, sems, in_sems, out_sems = rest
        enter = enter_cotangent(half, cot, swap, raw, sems.at[2, 0])
        arriving = Arriving([("active", active, va)], in_sems)
        wdown = Weight(half[0], do, dp, wd, sems.at[1], False)
        wup = Weight(half[0], uo, up, wu, sems.at[0], False)
        pick_halves(half, so, sp, small)
        enter.wait()
        upstream = jnp.where(first[0] > 0, returned[...], raw[...].reshape(ROWS, WIDTH))
        top_back_body(upstream.astype(F32), small, n2, i2, gr2, gz, gsmall)
        leaving = Leaving(out_sems)
        arriving.get("active")
        wdown.start()
        later = Arriving(
            [("slope", slope, vs), ("normal", n1, vn), ("u", u, vu)],
            in_sems.at[pl.ds(1, 3)],
        )
        for which, local, target in ((1 - half[0], v0, down_other), (half[0], v1, down_own)):
            local[...] = dot_tn(half_columns(va, which), gz[...]).astype(LOW)
            leaving.send(local, target)
        wup.start()
        later.get("slope")
        later.get("normal")
        feed_back_body(gr2, gz, wup, wdown, small, vs, vn, i1, ga, gr1, gb, gsmall)
        later.get("u")
        for which, local, target in ((1 - half[0], v2, up_other), (half[0], v3, up_own)):
            send_folded(leaving, local, target, half_columns(vu, which), ga)
        token[...] = jnp.zeros(token.shape, F32)
        leaving.wait()

    return kernel_call(
        body,
        [ANY, ANY, VMEM, SMEM, SMEM] + [VMEM] * 5 + [ANY] * 8,
        [shape(GRAD_SHAPE)] * 4
        + [shape(ROW_SHAPE, F32), shape(ROW_SHAPE), shape((2, SMALL), F32), TOKEN],
        [
            pltpu.VMEM(ROW_SHAPE, F32),
            pltpu.VMEM(ROW_SHAPE, LOW),
            pltpu.VMEM(FEED_SHAPE, LOW),
            *[GRAD_SCRATCH] * 4,
            SMALL_SCRATCH,
            pltpu.VMEM((2, LENGTH, WIDTH), LOW),
            *FEED_WEIGHTS,
            pltpu.VMEM(ROW_SHAPE, LOW),
            pltpu.VMEM(FEED_SHAPE, LOW),
            pltpu.VMEM(FEED_SHAPE, LOW),
            pltpu.VMEM(ROW_SHAPE, F32),
            pltpu.SemaphoreType.DMA((3, 2)),
            pltpu.SemaphoreType.DMA((4,)),
            pltpu.SemaphoreType.DMA((10,)),
        ],
        200 * MACS,
        600000000,
        "back_feed",
        [ANY] * 4 + [VMEM] * 4,
        BIG_GRANT,
    )(
        cotangent, swapped, returned, half, first, *smalls, i1, n2, i2, *weights[2], *weights[3],
        u, slope, active, n1,
    )


def back_attend(gb, gr1, half, first, spans, weights, gsmall, h, qkv, probs, mixed):
    def body(gb, half, first, spans, gsmall, oo, op, qo, qp, gr1, h, qkv, probs, mixed, *rest):
        outs, rest = rest[:6], rest[6:]
        other, own, small_other, small_own, gh, token = outs
        gqkv, go, gqv, vother, vown, wo, wq, vr, vh, vq, vp, vm, sems, in_sems, out_sems = rest
        wout = Weight(half[0], oo, op, wo, sems.at[0])
        arriving = Arriving([("qkv", qkv, vq), ("probs", probs, vp)], in_sems)
        wqkv = Weight(half[0], qo, qp, wq, sems.at[1], False)
        arriving.get("qkv")
        arriving.get("probs")
        wqkv.start()
        late = Arriving([("h", h, vh), ("mixed", mixed, vm), ("gr1", gr1, vr)], in_sems.at[pl.ds(2, 3)])
        heads_back_body(gb, wout, vq, vp, gqkv, gqv, go)
        leaving = Leaving(out_sems)
        late.get("h")
        late.get("mixed")
        for which, local, target in ((1 - half[0], vother, other), (half[0], vown, own)):
            send_folded(leaving, local, target, half_columns(vh, which), gqkv)
            local[1152:, :] = dot_tn(half_columns(vm, which), gb[...]).astype(LOW)
            leaving.send(local.at[pl.ds(1152, 384)], target.at[pl.ds(1152, 384)])
        late.get("gr1")
        full = vr[...] + dot_nt(gqkv[...], wqkv.get())
        dropped = span_rows(spans, half) & (first[0] > 0)
        zero = jnp.zeros_like(full)
        gh[...] = jnp.where(dropped, zero, full).astype(LOW)
        gmask = column_sum(jnp.where(dropped, full, zero))
        for which, target in ((1 - half[0], small_other), (half[0], small_own)):
            target[:, :WIDTH] = gqv[pl.ds(which, 1), :]
            target[:, WIDTH:SMALL] = gsmall[pl.ds(which, 1), WIDTH:]
            target[:, SMALL:] = gmask
        token[...] = jnp.zeros(token.shape, F32)
        leaving.wait()

    return kernel_call(
        body,
        [VMEM, SMEM, SMEM, SMEM, VMEM] + [ANY] * 9,
        [
            shape(GRAD_SHAPE),
            shape(GRAD_SHAPE),
            shape((1, SMALL + WIDTH), F32),
            shape((1, SMALL + WIDTH), F32),
            shape(ROW_SHAPE),
            TOKEN,
        ],
        [
            pltpu.VMEM(QKV_SHAPE, LOW),
            pltpu.VMEM(ROW_SHAPE, LOW),
            pltpu.VMEM((2, WIDTH), F32),
            GRAD_SCRATCH,
            GRAD_SCRATCH,
            ATTEND_WEIGHTS[1],
            ATTEND_WEIGHTS[0],
            pltpu.VMEM(ROW_SHAPE, F32),
            pltpu.VMEM(ROW_SHAPE, LOW),
            pltpu.VMEM(QKV_SHAPE, LOW),
            pltpu.VMEM(PROBS_SHAPE, LOW),
            pltpu.VMEM(ROW_SHAPE, LOW),
            pltpu.SemaphoreType.DMA((2, 2)),
            pltpu.SemaphoreType.DMA((5,)),
            pltpu.SemaphoreType.DMA((8,)),
        ],
        180 * MACS,
        400000000,
        "back_attend",
        [ANY, ANY] + [VMEM] * 4,
    )(gb, half, first, spans, gsmall, *weights[1], *weights[0], gr1, h, qkv, probs, mixed)


TAIL = 16
BLOCK = 96


def add_rows(target, sources, at, rows):
    for start in range(0, rows, BLOCK):
        size = min(BLOCK, rows - start)
        place = pl.ds(at + start, size)
        if not isinstance(at, int):
            place = pl.ds(pl.multiple_of(at + start, 16), size)
        if len(sources) == 2:
            target[start : start + size, :] = sources[0][place, :] + sources[1][place, :]
            continue
        total = sources[0][place, :].astype(F32)
        for source in sources[1:]:
            total = total + source[place, :].astype(F32)
        target[start : start + size, :] = total.astype(LOW)


LONG = 30000000000


def ordered(
    name, body, ins, outs, where, after, out_specs=None, scratch=(), in_specs=None, grant=16, aliases=None,
    flops=LONG,
):
    count, made = len(ins), len(outs)

    def kernel(where, after, *refs):
        refs[count + made][...] = jnp.zeros(TOKEN.shape, F32)
        body(where, refs[:count], refs[count : count + made] + refs[count + made + 1 :])

    result = pl.pallas_call(
        kernel,
        in_specs=[SMEM, ANY] + (in_specs or [VMEM] * count),
        out_specs=(out_specs or [VMEM] * made) + [VMEM],
        out_shape=list(outs) + [TOKEN],
        scratch_shapes=list(scratch),
        input_output_aliases=aliases or {},
        compiler_params=pltpu.CompilerParams(vmem_limit_bytes=grant * MIB),
        cost_estimate=pl.CostEstimate(flops=flops, bytes_accessed=flops, transcendentals=0),
        name=name,
    )(where, after, *ins)
    return result[:made], result[made]


def partner(x, axis, bit):
    return lax.ppermute(x, axis, [(i, i ^ 1 << bit) for i in range(lax.axis_size(axis))])


def moved_on(index, axis, steps):
    z, x, y = index // 8, index // 2 % 4, index % 2
    if axis == "z":
        z = steps(z)
    elif axis == "x":
        x = steps(x)
    else:
        y = steps(y)
    return z * 8 + x * 2 + y


def send_along(value, axes, place):
    pairs = []
    for section in range(4):
        for index in range(32):
            to = moved_on(index, axes[section % 2], place)
            pairs.append((section * 32 + index, section * 32 + to))
    return lax.ppermute(value, ("section", "dp"), pairs)


def exchange(value, part, step):
    flip = 1 if part == step else 3
    return send_along(value, "zx", lambda place: place ^ flip)


def turn(value, steps):
    return send_along(value, "xz", lambda place: (place + steps) % 4)


def across_y(value):
    return send_along(value, "yy", lambda place: place ^ 1)


def swap_core_one(value):
    pairs = [
        (section * 32 + index, section * 32 + (index ^ 1)) for section in (1, 3) for index in range(32)
    ]
    return lax.ppermute(value, ("section", "dp"), pairs)


def between_layers(value, back):
    pairs = []
    for core in range(2):
        for index in range(32):
            pair = (core * 32 + index, (core + 2) * 32 + (index ^ core))
            pairs.append(pair[::-1] if back else pair)
    return lax.ppermute(value, ("section", "dp"), pairs)


def own_places(core):
    index = lax.axis_index("dp")
    z, x = index // 8, index // 2 % 4
    ring = jnp.where(core == 0, z, x)
    high = ring // 2
    low = high ^ (ring % 2)
    table = [low, high, high, low, jnp.where(core == 0, x, z)]
    return jnp.stack(table).astype(jnp.int32)


def row_shapes(*counts):
    return [shape((count, WIDTH)) for count in counts]


def add_tail(target, rows, sources, at, extra):
    if extra:
        total = sources[0][at : at + extra, :].astype(F32)
        for source in sources[1:]:
            total = total + source[at : at + extra, :].astype(F32)
        target[rows : rows + extra, :] = total.astype(LOW)


class Chain:
    def __init__(self, name, places, tail=0):
        self.name = name
        self.places = places
        self.tail = (0, tail)
        self.keep = [None, None]
        self.got = [None, None]

    def kernel(self, name, body, ins, outs, token, *more, **named):
        return ordered(self.name + name, body, ins, outs, self.places, token, *more, **named)

    def pairs(self):
        return (self.keep[0], self.got[0], self.keep[1], self.got[1])

    def start(self, sources, rows, token, tail_ins=(), tail_body=None):
        self.rows = rows // 2
        half_rows, tails = self.rows, self.tail
        arrays = []
        for own, got, _ in sources:
            arrays += [own, got]

        def body(places, ins, outs):
            for part in range(2):
                bit, at = places[2 * part], sources[part][2]
                pair = ins[2 * part : 2 * part + 2]
                for target, which in ((outs[2 * part + 1], 1 - bit), (outs[2 * part], bit)):
                    add_rows(target, pair, at + which * half_rows, half_rows)
                    if tails[part]:
                        target[half_rows:, :] = tail_body(ins[4:])

        counts = [half_rows + tails[0]] * 2 + [half_rows + tails[1]] * 2
        outs, token = self.kernel(
            "start", body, tuple(arrays) + tuple(tail_ins), row_shapes(*counts), token
        )
        for part in range(2):
            self.keep[part] = outs[2 * part]
            self.got[part] = exchange(outs[2 * part + 1], part, 0)
        return token

    def halve(self, token):
        self.rows //= 2
        rows, tails = self.rows, self.tail

        def body(places, ins, outs):
            for part in range(2):
                bit = places[2 * part + 1]
                pair = ins[2 * part : 2 * part + 2]
                for target, which in ((outs[2 * part + 1], 1 - bit), (outs[2 * part], bit)):
                    add_rows(target, pair, which * rows, rows)
                    add_tail(target, rows, pair, 2 * rows, tails[part])

        counts = [rows + tails[0]] * 2 + [rows + tails[1]] * 2
        outs, token = self.kernel(
            "halve", body, self.pairs(), row_shapes(*counts), token
        )
        for part in range(2):
            self.keep[part] = outs[2 * part]
            self.got[part] = exchange(outs[2 * part + 1], part, 1)
        return token

    def cross(self, token):
        whole_rows, extra = self.rows, self.tail[1]
        rows = whole_rows // 2

        def body(places, ins, refs):
            outs, total = refs[:4], refs[4]
            add_rows(total.at[pl.ds(0, whole_rows)], ins[:2], 0, whole_rows)
            add_rows(total.at[pl.ds(whole_rows, whole_rows)], ins[2:], 0, whole_rows)
            for steps in range(4):
                quarter = (places[4] + steps) % 4
                outs[steps][:rows, :] = total[pl.ds(pl.multiple_of(quarter * rows, 16), rows), :]
                add_tail(outs[steps], rows, ins[2:], whole_rows, extra)

        (self.own, *sends), token = self.kernel(
            "cross",
            body,
            self.pairs(),
            row_shapes(*[rows + extra] * 4),
            token,
            None,
            (pltpu.VMEM((2 * whole_rows, WIDTH), LOW),),
        )
        self.rows = rows
        self.ring = [turn(send, steps) for steps, send in zip((1, 2, 3), sends)]
        return token

    def across(self, token):
        rows = self.rows + self.tail[1]

        def body(places, ins, outs):
            add_rows(outs[0], ins, 0, rows)

        (self.own,), token = self.kernel(
            "across", body, (self.own, *self.ring), row_shapes(rows), token
        )
        self.other = across_y(self.own)
        return token

    def total(self, token, more_outs=(), more_body=None):
        rows, extra = self.rows, self.tail[1]

        def body(places, ins, outs):
            add_rows(outs[0], ins, 0, rows)
            if extra:
                add_rows(outs[1], ins, rows, extra)
                more_body(outs[1][...].astype(F32), outs[2:])

        counts = [rows] + ([extra] if extra else [])
        outs, token = self.kernel(
            "total", body, (self.own, self.other), row_shapes(*counts) + list(more_outs), token
        )
        self.own = outs[0]
        self.tail_sum = outs[1] if extra else None
        self.ring = [turn(self.own, steps) for steps in (1, 2, 3)]
        return outs[2:], token

    def back(self, token, more_ins=(), more_outs=(), more_body=None):
        rows = self.rows

        def body(places, ins, refs):
            outs, total = refs[:-1], refs[-1]
            for steps in range(4):
                quarter = (places[4] - steps + 4) % 4
                total[pl.ds(pl.multiple_of(quarter * rows, 16), rows), :] = ins[steps][...]
            outs[0][...] = total[: 2 * rows, :]
            outs[1][...] = total[2 * rows :, :]
            if more_body is not None:
                more_body(ins[4:], outs[2:])

        outs, token = self.kernel(
            "back",
            body,
            (self.own, *self.ring) + tuple(more_ins),
            row_shapes(2 * rows, 2 * rows) + list(more_outs),
            token,
            None,
            (pltpu.VMEM((4 * rows, WIDTH), LOW),),
        )
        self.rows = 2 * rows
        self.keep = list(outs[:2])
        self.got = [exchange(self.keep[part], part, 1) for part in range(2)]
        return outs[2:], token

    def double(self, token, flops):
        rows = self.rows

        def body(places, ins, outs):
            for part in range(2):
                bit = places[2 * part + 1]
                for which, source in ((bit, ins[2 * part]), (1 - bit, ins[2 * part + 1])):
                    outs[part][pl.ds(pl.multiple_of(which * rows, 16), rows), :] = source[...]

        outs, token = self.kernel(
            "double", body, self.pairs(), row_shapes(2 * rows, 2 * rows), token, flops=flops
        )
        self.rows = 2 * rows
        self.keep = list(outs)
        self.got = [exchange(self.keep[part], part, 0) for part in range(2)]
        return token

    def finish(self, token, outs, place, got, flops):
        rows = self.rows
        mine = tuple(self.got if got else self.keep)
        kept = tuple(outs) if got else ()

        def body(places, ins, refs):
            targets, wide, sems = refs[: len(outs)], refs[-2], refs[-1]
            waits = []
            for part in range(2):
                bit = places[2 * part]
                half = 1 - bit if got else bit
                wide[part] = ins[part][...].astype(F32)
                at = 0
                for size, starts in place(targets, part, half):
                    source, sem = wide.at[part, pl.ds(at, size)], sems.at[len(waits)]
                    starts(source, sem)
                    waits.append((size, source, sem))
                    at += size
            for size, source, sem in waits:
                pltpu.make_async_copy(source, wide.at[0, pl.ds(0, size)], sem).wait()

        return self.kernel(
            "finish",
            body,
            mine + kept,
            [shape(out.shape, F32) for out in outs],
            token,
            out_specs=[ANY] * len(outs),
            scratch=(pltpu.VMEM((2, rows, WIDTH), F32), pltpu.SemaphoreType.DMA((4,))),
            in_specs=[VMEM] * 2 + [ANY] * len(kept),
            grant=24,
            flops=flops,
            aliases={4 + index: index for index in range(len(kept))},
        )


def copy_to(target):
    return lambda source, sem: pltpu.make_async_copy(source, target, sem).start()


def block_columns(block):
    return pl.ds(pl.multiple_of(block * WIDTH, 128), WIDTH)


def place_x(refs, part, half):
    down, up = refs
    if part == 0:
        return [(768, copy_to(down.at[pl.ds(pl.multiple_of(half * 768, 8), 768)]))]
    return [(384, copy_to(up.at[:, block_columns(2 * half + block)])) for block in range(2)]


def place_y(refs, part, half):
    qkv, out = refs
    if part == 0:
        return [(384, copy_to(qkv.at[:, block_columns(half)]))]

    def starts(source, sem):
        @pl.when(half == 0)
        def _():
            copy_to(qkv.at[:, block_columns(2)])(source, sem)

        @pl.when(half == 1)
        def _():
            copy_to(out)(source, sem)

    return [(384, starts)]


def pack_vectors(vectors):
    size = sum(vector.shape[0] for vector in vectors)
    total = jnp.zeros((size,), F32)
    at = 0
    for vector in vectors:
        total = total + jnp.pad(vector.astype(F32), (at, size - at - vector.shape[0]))
        at += vector.shape[0]
    return total.reshape(1, size)


def per_device(
    inputs,
    cotangent,
    lengths,
    cdr_spans,
    mask_vector,
    w_qkv,
    qv_bias,
    w_out,
    b_out,
    norm1_gain,
    norm1_bias,
    w_up,
    b_up,
    w_down,
    b_down,
    norm2_gain,
    norm2_bias,
):
    section_index = lax.axis_index("section")
    core = section_index % 2
    half = core.astype(jnp.int32).reshape(1)
    first = (section_index < 2).astype(jnp.int32).reshape(1)
    places = own_places(core)
    small = pack_vectors(
        (
            qv_bias,
            b_out,
            norm1_gain,
            norm1_bias,
            b_up,
            b_down,
            norm2_gain,
            norm2_bias,
            mask_vector,
        )
    )
    small_got = partner(small, "section", 0)
    got_qkv, got_out = partner((w_qkv, w_out), "section", 0)
    w_up, w_down, got_qkv, got_out, small_got = lax.optimization_barrier(
        (w_up, w_down, got_qkv, got_out, small_got)
    )
    smalls = (small, small_got)
    got_up, got_down = partner((w_up, w_down), "section", 0)
    weights = [(w_qkv, got_qkv), (w_out, got_out), (w_up, got_up), (w_down, got_down)]

    swapped = swap_core_one(cotangent)
    lens_got = swap_core_one(lengths)
    swaps = (core == 1) & (section_index >= 2)
    layer_lens = jnp.where(swaps, lens_got, lengths)

    u, h0 = attend_first(inputs, half, lengths, cdr_spans, weights, smalls)
    first_out = feed_first(u, half, weights, smalls)
    received = between_layers(first_out, False)
    kept = middle(h0, received, cotangent, swapped, half, first, layer_lens, weights, smalls)
    h, qkv, probs, mixed, normal1, inverse1, u, slope, active, normal2, inverse2, output = kept[:12]
    returned = between_layers(kept[13], True)

    a_other, a_own, b_other, b_own, gr1, gb, gsmall, token = back_feed(
        cotangent,
        swapped,
        returned,
        half,
        first,
        weights,
        smalls,
        (u, slope, active, normal1, inverse1, normal2, inverse2),
    )
    a_got = partner(a_other, "section", 0)
    b_got = partner(b_other, "section", 0)
    x, y = Chain("x_", places), Chain("y_", places, TAIL)
    y_other, y_own, small_other, small_own, gh, token = back_attend(
        gb, gr1, half, first, cdr_spans, weights, gsmall, h, qkv, probs, mixed
    )
    y_got = partner(y_other, "section", 0)
    small_got = partner(small_other, "section", 0)
    token = x.start([(a_own, a_got, 0), (b_own, b_got, 0)], 1536, token)

    def tail_rows(ins):
        total = ins[0][...] + ins[1][...]
        rows = [total[:, at : at + WIDTH] for at in range(0, SMALL + WIDTH, WIDTH)]
        rows.append(jnp.zeros((TAIL - len(rows), WIDTH), F32))
        return jnp.concatenate(rows, axis=0).astype(LOW)

    token = y.start(
        [(y_own, y_got, 0), (y_own, y_got, 768)], 768, token, (small_own, small_got), tail_rows
    )
    both, token = lax.optimization_barrier((kept[12], token))
    both_got = swap_core_one(both)
    token = x.halve(token)
    token = y.halve(token)
    token = x.cross(token)
    token = y.cross(token)
    token = x.across(token)
    token = y.across(token)
    _, token = x.total(token)

    def small_outputs(tail, outs):
        flat = jnp.concatenate([tail[row : row + 1, :] for row in range(6)], axis=1)
        at = 0
        for out, size in zip(outs, SIZES):
            out[...] = flat[0, at : at + size]
            at += size

    out_small, token = y.total(token, [shape((size,), F32) for size in SIZES], small_outputs)
    mask_got = partner(y.tail_sum, "section", 1)
    _, token = x.back(token)

    def mask_output(ins, outs):
        outs[0][...] = ins[0][6, :].astype(F32) + ins[1][6, :].astype(F32)

    (mask_grad,), token = y.back(
        token, (y.tail_sum, mask_got), [shape((WIDTH,), F32)], mask_output
    )
    gradients_x = [shape((1536, WIDTH), F32), shape((384, HIDDEN), F32)]
    gradients_y = [shape((384, 3 * WIDTH), F32), shape((384, WIDTH), F32)]
    token = x.double(token, LONG)
    gradients_x, token = x.finish(token, gradients_x, place_x, False, LONG)
    token = y.double(token, 0)
    gradients_y, token = y.finish(token, gradients_y, place_y, False, 0)
    both_got, token = lax.optimization_barrier((both_got, token))
    (g_down, g_up), token = x.finish(token, gradients_x, place_x, True, LONG)
    (g_qkv, g_out), token = y.finish(token, gradients_y, place_y, True, LONG)
    output = jnp.where(swaps, both_got[0], output)
    gh = jnp.where(swaps, both_got[1], gh)

    g_qv, g_bo, g_n1g, g_n1b, g_bu, g_bd, g_n2g, g_n2b = out_small
    return (
        output.reshape(1, 2, LENGTH, WIDTH),
        gh.reshape(1, 2, LENGTH, WIDTH),
        mask_grad,
        g_qkv,
        g_qv,
        g_out,
        g_bo,
        g_n1g,
        g_n1b,
        g_up,
        g_bu,
        g_down,
        g_bd,
        g_n2g,
        g_n2b,
    )


def solution(mesh):
    in_specs = (
        P(None, "dp", None, None),
        P(None, "dp", None, None),
        P(None, "dp"),
        P(None, "dp", None),
        P(),
        P("section", None),
        P("section"),
        P("section", None),
        P("section"),
        P("section"),
        P("section"),
        P("section", None),
        P("section"),
        P("section", None),
        P("section"),
        P("section"),
        P("section"),
    )
    out_specs = (
        P("section", "dp", None, None),
        P("section", "dp", None, None),
        P(),
        P("section", None),
        P("section"),
        P("section", None),
        P("section"),
        P("section"),
        P("section"),
        P("section", None),
        P("section"),
        P("section", None),
        P("section"),
        P("section"),
        P("section"),
    )
    return jax.shard_map(
        per_device, mesh=mesh, in_specs=in_specs, out_specs=out_specs, check_vma=False
    )
```

```python
import functools
import math

import jax
import jax.numpy as jnp
from jax import lax
from jax.experimental import pallas as pl
from jax.experimental.pallas import tpu as pltpu
from jax.sharding import PartitionSpec as P

EPSILON = 1e-05
F32 = jnp.float32
LOW = jnp.bfloat16
WIDTH = 768
LENGTH = 160
ROWS = 320
HIDDEN = 3072
PAIRS = 6
SCALE = 0.125
SIZES = (768, 384, 384, 384, 1536, 384, 384, 384)
QV, B_OUT, N1G, N1B, B_UP, B_DOWN, N2G, N2B = (sum(SIZES[:at]) for at in range(8))
SMALL = sum(SIZES)
VMEM_LIMIT = 63 * 1024 * 1024
BIG_GRANT = 61 * 1024 * 1024


def dot_nn(left_side, right_side):
    return jnp.dot(left_side, right_side, preferred_element_type=F32)


def dot_nt(left_side, right_side):
    return lax.dot_general(
        left_side, right_side, (((1,), (1,)), ((), ())), preferred_element_type=F32
    )


def dot_tn(left_side, right_side):
    return lax.dot_general(
        left_side, right_side, (((0,), (0,)), ((), ())), preferred_element_type=F32
    )


class Weight:
    def __init__(self, half, own, other, dest, sems, start=True, chunks=1):
        rows, wide = own.shape
        self.dest = dest
        self.wide = wide // chunks
        self.copies = []
        for chunk in range(chunks):
            at = pl.ds(chunk * self.wide, self.wide)
            for side, source in enumerate((own, other)):
                which = half if side == 0 else 1 - half
                place = dest.at[pl.ds(which * rows, rows)]
                if chunks > 1:
                    source, place = source.at[:, at], place.at[:, at]
                self.copies.append(
                    pltpu.make_async_copy(source, place, sems.at[2 * chunk + side])
                )
        if start:
            self.start()

    def start(self):
        for copy in self.copies:
            copy.start()

    def get(self):
        for copy in self.copies:
            copy.wait()
        self.copies = []
        return self.dest[...]

    def chunk(self, index):
        for copy in self.copies[:2]:
            copy.wait()
        self.copies = self.copies[2:]
        return self.dest[:, index * self.wide : (index + 1) * self.wide]


def whole(smalls, at, size):
    return jnp.concatenate([smalls[0:1, at : at + size], smalls[1:2, at : at + size]], axis=1)


def split_heads(tensor):
    lane = lax.broadcasted_iota(jnp.int32, tensor.shape, 1)
    zero = jnp.zeros_like(tensor)
    return jnp.concatenate(
        [jnp.where(lane < 64, tensor, zero), jnp.where(lane < 64, zero, tensor)], axis=0
    )


def join_heads(tensor):
    lane = lax.broadcasted_iota(jnp.int32, (LENGTH, 128), 1)
    return jnp.where(lane < 64, tensor[:LENGTH], tensor[LENGTH:])


def normalize(values):
    center = values - jnp.mean(values, axis=-1, keepdims=True)
    spread = jnp.mean(center * center, axis=-1, keepdims=True)
    inverse = lax.rsqrt(spread + EPSILON)
    return center * inverse, inverse


def normalize_back(upstream, gain, normal, inverse):
    scaled = upstream * gain
    first = jnp.mean(scaled, axis=-1, keepdims=True)
    second = jnp.mean(scaled * normal, axis=-1, keepdims=True)
    return inverse * (scaled - first - normal * second)


def gelu_parts(values):
    size = jnp.abs(values)
    below = 1.0 + (0.3275911 * math.sqrt(0.5)) * size
    t = pl.reciprocal(below, approx=True)
    t = t * (2.0 - below * t)
    series = t * (
        0.5 * 0.254829592
        + t
        * (
            0.5 * -0.284496736
            + t * (0.5 * 1.421413741 + t * (0.5 * -1.453152027 + t * (0.5 * 1.061405429)))
        )
    )
    bell = jnp.exp(-0.5 * values * values)
    tail = series * bell
    share = jnp.where(values >= 0.0, 1.0 - tail, tail)
    return values * share, share + values * bell * (1.0 / math.sqrt(2.0 * math.pi))


def column_sum(values):
    return jnp.sum(values, axis=0, keepdims=True)


def put_halves(target, at, row):
    size = row.shape[1] // 2
    target[0:1, at : at + size] = row[:, :size]
    target[1:2, at : at + size] = row[:, size:]


def places():
    for index in range(2 * PAIRS):
        chain, pair = divmod(index, PAIRS)
        rows = pl.ds(chain * LENGTH, LENGTH)
        yield index, chain, rows, [pl.ds((pair + block * PAIRS) * 128, 128) for block in range(3)]


def attend_body(h, wqkv, wout, smalls, lens, half, qkv, probs, mixed, normal1, inverse1, u, later):
    x = h[...]
    bias = jnp.concatenate(
        [smalls[0:1, :WIDTH], jnp.zeros((1, WIDTH), F32), smalls[1:2, :WIDTH]], axis=1
    )
    for block in range(3):
        at = block * WIDTH
        matrix = wqkv.chunk(block)
        if block == 0:
            for each in later:
                each.start()
        qkv[:, at : at + WIDTH] = (dot_nn(x, matrix) + bias[:, at : at + WIDTH]).astype(LOW)
    for index, chain, rows, (at_q, at_k, at_v) in places():
        scores = dot_nt(qkv[rows, at_k], split_heads(qkv[rows, at_q])) * SCALE
        key = lax.broadcasted_iota(jnp.int32, scores.shape, 0)
        scores = jnp.where(key < lens[half[0], chain], scores, -1000000000.0)
        grown = jnp.exp(scores - jnp.max(scores, axis=0, keepdims=True))
        weights = (grown * (1.0 / jnp.sum(grown, axis=0, keepdims=True))).astype(LOW)
        if probs is not None:
            probs[index] = weights
        mixed[rows, at_q] = join_heads(dot_tn(weights, qkv[rows, at_v])).astype(LOW)
    branch = dot_nn(mixed[...], wout.get()) + whole(smalls, B_OUT, 384)
    normal, inverse = normalize(x.astype(F32) + branch)
    if normal1 is not None:
        normal1[...] = normal
        inverse1[...] = inverse
    u[...] = (normal * whole(smalls, N1G, 384) + whole(smalls, N1B, 384)).astype(LOW)


CHUNK = 1024


def feed_body(u, wup, wdown, smalls, slope, active, normal2, inverse2, y, later=()):
    x = u[...]
    bias = whole(smalls, B_UP, 1536)
    for at in range(0, HIDDEN, CHUNK):
        up = wup.chunk(at // CHUNK)
        if at == 0:
            for each in later:
                each.start()
        grown, tangent = gelu_parts(dot_nn(x, up) + bias[:, at : at + CHUNK])
        active[:, at : at + CHUNK] = grown.astype(LOW)
        if slope is not None:
            slope[:, at : at + CHUNK] = tangent.astype(LOW)
    total = x.astype(F32) + whole(smalls, B_DOWN, 384) + dot_nn(active[...], wdown.get())
    normal, inverse = normalize(total)
    if normal2 is not None:
        normal2[...] = normal
        inverse2[...] = inverse
    y[...] = (normal * whole(smalls, N2G, 384) + whole(smalls, N2B, 384)).astype(LOW)


def top_back_body(up, smalls, normal2, inverse2, gr2, gz, gsmall):
    normal = normal2[...]
    put_halves(gsmall, N2G, column_sum(up * normal))
    put_halves(gsmall, N2B, column_sum(up))
    grad = normalize_back(up, whole(smalls, N2G, 384), normal, inverse2[...])
    z = grad.astype(LOW)
    gz[...] = z
    put_halves(gsmall, B_DOWN, column_sum(z.astype(F32)))
    gr2[...] = grad


def feed_back_body(gr2, gz, wup, wdown, smalls, slope, normal1, inverse1, ga, gr1, gb, gsmall):
    z = gz[...]
    down = wdown.get()
    sums = []
    for at in range(0, HIDDEN, CHUNK):
        inner = dot_nt(z, down[at : at + CHUNK, :]) * slope[:, at : at + CHUNK].astype(F32)
        a = inner.astype(LOW)
        ga[:, at : at + CHUNK] = a
        sums.append(column_sum(a.astype(F32)))
    put_halves(gsmall, B_UP, jnp.concatenate(sums, axis=1))
    up = gr2[...] + dot_nt(ga[...], wup.get())
    normal = normal1[...]
    put_halves(gsmall, N1G, column_sum(up * normal))
    put_halves(gsmall, N1B, column_sum(up))
    grad = normalize_back(up, whole(smalls, N1G, 384), normal, inverse1[...])
    gr1[...] = grad
    b = grad.astype(LOW)
    gb[...] = b
    put_halves(gsmall, B_OUT, column_sum(b.astype(F32)))


def heads_back_body(gb, wout, qkv, probs, gqkv, gqv, go):
    go[...] = dot_nt(gb[...], wout.get()).astype(LOW)
    for index, chain, rows, (at_q, at_k, at_v) in places():
        k = qkv[rows, at_k]
        g = split_heads(go[rows, at_q])
        weights = probs[index]
        wide = weights.astype(F32)
        inner = dot_nt(qkv[rows, at_v], g)
        inner = wide * (inner - jnp.sum(wide * inner, axis=0, keepdims=True))
        s = inner.astype(LOW)
        gqkv[rows, at_q] = (join_heads(dot_tn(s, k)) * SCALE).astype(LOW)
        gqkv[rows, at_k] = (dot_nn(s, split_heads(qkv[rows, at_q])) * SCALE).astype(LOW)
        gqkv[rows, at_v] = dot_nn(weights, g).astype(LOW)
    if gqv is not None:
        gqv[0:1, :] = column_sum(gqkv[:, :WIDTH].astype(F32))
        gqv[1:2, :] = column_sum(gqkv[:, 2 * WIDTH :].astype(F32))


def span_rows(spans, half):
    row = lax.broadcasted_iota(jnp.int32, (ROWS, 1), 0)
    inside = row < 0
    for chain in range(2):
        start = spans[half[0], chain, 0] + chain * LENGTH
        end = spans[half[0], chain, 1] + chain * LENGTH
        inside = inside | ((row >= start) & (row < end))
    return inside


def pick_halves(half, own, other, smalls):
    low = half[0] == 0
    smalls[0:1, :] = jnp.where(low, own[:, :SMALL], other[:, :SMALL])
    smalls[1:2, :] = jnp.where(low, other[:, :SMALL], own[:, :SMALL])


VMEM = pl.BlockSpec(memory_space=pltpu.VMEM)
SMEM = pl.BlockSpec(memory_space=pltpu.SMEM)
ANY = pl.BlockSpec(memory_space=pl.ANY)
SMALL_SCRATCH = pltpu.VMEM((2, SMALL), F32)
QKV_SHAPE = (ROWS, 3 * WIDTH)
PROBS_SHAPE = (2 * PAIRS, LENGTH, 2 * LENGTH)
ROW_SHAPE = (ROWS, WIDTH)
FEED_SHAPE = (ROWS, HIDDEN)
MACS = ROWS * WIDTH * WIDTH * 2
ATTEND_WEIGHTS = [pltpu.VMEM((WIDTH, 3 * WIDTH), LOW), pltpu.VMEM((WIDTH, WIDTH), LOW)]
FEED_WEIGHTS = [pltpu.VMEM((WIDTH, HIDDEN), LOW), pltpu.VMEM((HIDDEN, WIDTH), LOW)]


def shape(dims, kind=LOW):
    return jax.ShapeDtypeStruct(dims, kind)


def enter_cotangent(half, own, swapped, raw, sem):
    @pl.when(half[0] == 0)
    def _():
        pltpu.make_async_copy(own.at[0], raw, sem).start()

    @pl.when(half[0] == 1)
    def _():
        pltpu.make_async_copy(swapped.at[1], raw, sem).start()

    return pltpu.make_async_copy(swapped.at[1], raw, sem)


def kernel_call(body, ins, outs, scratch, flops, moved, name, out_specs=None, grant=VMEM_LIMIT):
    return pl.pallas_call(
        body,
        in_specs=ins,
        out_specs=out_specs or [VMEM] * len(outs),
        out_shape=outs,
        scratch_shapes=scratch,
        compiler_params=pltpu.CompilerParams(vmem_limit_bytes=grant),
        cost_estimate=pl.CostEstimate(flops=flops, bytes_accessed=moved, transcendentals=0),
        name=name,
    )


def attend_first(inputs, half, lens, spans, weights, smalls):
    def body(x, half, lens, spans, so, sp, qo, qp, oo, op, u, h, raw, small, qkv, mixed, wq, wo, sems):
        enter = pltpu.make_async_copy(x.at[half[0]], raw, sems.at[2, 0])
        enter.start()
        wqkv = Weight(half[0], qo, qp, wq, sems.at[0], True, 3)
        wout = Weight(half[0], oo, op, wo, sems.at[1], False)
        pick_halves(half, so, sp, small)
        enter.wait()
        mask = so[:, SMALL:].astype(LOW)
        h[...] = jnp.where(span_rows(spans, half), mask, raw[...].reshape(ROWS, WIDTH))
        attend_body(h, wqkv, wout, small, lens, half, qkv, None, mixed, None, None, u, [wout])

    return kernel_call(
        body,
        [ANY, SMEM, SMEM, SMEM, VMEM, VMEM] + [ANY] * 4,
        [shape(ROW_SHAPE), shape(ROW_SHAPE)],
        [
            pltpu.VMEM((2, LENGTH, WIDTH), LOW),
            SMALL_SCRATCH,
            pltpu.VMEM(QKV_SHAPE, LOW),
            pltpu.VMEM(ROW_SHAPE, LOW),
            *ATTEND_WEIGHTS,
            pltpu.SemaphoreType.DMA((3, 6)),
        ],
        40 * MACS,
        80000000,
        "attend_first",
    )(inputs, half, lens, spans, *smalls, *weights[0], *weights[1])


def feed_first(u, half, weights, smalls):
    def body(u, half, so, sp, uo, up, do, dp, y, small, active, wu, wd, sems):
        wup = Weight(half[0], uo, up, wu, sems.at[0], True, 3)
        wdown = Weight(half[0], do, dp, wd, sems.at[1], False)
        pick_halves(half, so, sp, small)
        feed_body(u, wup, wdown, small, None, active, None, None, y, [wdown])

    return kernel_call(
        body,
        [VMEM, SMEM, VMEM, VMEM] + [ANY] * 4,
        [shape(ROW_SHAPE)],
        [
            SMALL_SCRATCH,
            pltpu.VMEM(FEED_SHAPE, LOW),
            *FEED_WEIGHTS,
            pltpu.SemaphoreType.DMA((2, 6)),
        ],
        8 * MACS,
        14000000,
        "feed_first",
    )(u, half, *smalls, *weights[2], *weights[3])[0]


KEPT = [
    shape(ROW_SHAPE),
    shape(QKV_SHAPE),
    shape(PROBS_SHAPE),
    shape(ROW_SHAPE),
    shape(ROW_SHAPE, F32),
    shape((ROWS, 1), F32),
    shape(ROW_SHAPE),
    shape(FEED_SHAPE),
    shape(FEED_SHAPE),
    shape(ROW_SHAPE, F32),
    shape((ROWS, 1), F32),
    shape(ROW_SHAPE),
]


def middle(h0, received, cotangent, swapped, half, first, lens, weights, smalls):
    def body(h0, received, cot, swap, half, first, lens, so, sp, qo, qp, oo, op, uo, up, do, dp, *rest):
        outs, rest = rest[: len(KEPT)], rest[len(KEPT) :]
        both, rest = rest[0], rest[1:]
        gh, small, gr2, gz, ga, gr1, gb, gsmall, gqkv, go, raw, wq, wo, wu, wd = rest[:15]
        keeps, sems, out_sems, raw_sem = rest[15:-3], *rest[-3:]
        h, qkv, probs, mixed, normal1, inverse1, u, slope, active, normal2, inverse2, y = keeps
        wqkv = Weight(half[0], qo, qp, wq, sems.at[0], True, 3)
        wout = Weight(half[0], oo, op, wo, sems.at[1])
        wup = Weight(half[0], uo, up, wu, sems.at[2], True, 3)
        wdown = Weight(half[0], do, dp, wd, sems.at[3])
        enter = enter_cotangent(half, cot, swap, raw, raw_sem)
        pick_halves(half, so, sp, small)
        leaving = []

        def leave(places):
            for place in places:
                copy = pltpu.make_async_copy(keeps[place], outs[place], out_sems.at[place])
                copy.start()
                leaving.append(copy)

        h[...] = jnp.where(first[0] > 0, h0[...], received[...])
        attend_body(
            h, wqkv, wout, small, lens, half, qkv, probs, mixed, normal1, inverse1, u, ()
        )
        leave(range(7))
        feed_body(u, wup, wdown, small, slope, active, normal2, inverse2, y)
        leave(range(7, 12))
        output = pltpu.make_async_copy(y, both.at[0], out_sems.at[len(KEPT)])
        output.start()
        leaving.append(output)
        enter.wait()
        upstream = raw[...].reshape(ROWS, WIDTH).astype(F32)
        top_back_body(upstream, small, normal2, inverse2, gr2, gz, gsmall)
        feed_back_body(gr2, gz, wup, wdown, small, slope, normal1, inverse1, ga, gr1, gb, gsmall)
        heads_back_body(gb, wout, qkv, probs, gqkv, None, go)
        gh[...] = (gr1[...] + dot_nt(gqkv[...], wqkv.get())).astype(LOW)
        output = pltpu.make_async_copy(gh, both.at[1], out_sems.at[len(KEPT) + 1])
        output.start()
        leaving.append(output)
        for copy in leaving:
            copy.wait()

    return kernel_call(
        body,
        [VMEM, VMEM, ANY, ANY, SMEM, SMEM, SMEM, VMEM, VMEM] + [ANY] * 8,
        KEPT + [shape((2, ROWS, WIDTH)), shape(ROW_SHAPE)],
        [
            SMALL_SCRATCH,
            pltpu.VMEM(ROW_SHAPE, F32),
            pltpu.VMEM(ROW_SHAPE, LOW),
            pltpu.VMEM(FEED_SHAPE, LOW),
            pltpu.VMEM(ROW_SHAPE, F32),
            pltpu.VMEM(ROW_SHAPE, LOW),
            SMALL_SCRATCH,
            pltpu.VMEM(QKV_SHAPE, LOW),
            pltpu.VMEM(ROW_SHAPE, LOW),
            pltpu.VMEM((2, LENGTH, WIDTH), LOW),
            *ATTEND_WEIGHTS,
            *FEED_WEIGHTS,
            *[pltpu.VMEM(kept.shape, kept.dtype) for kept in KEPT],
            pltpu.SemaphoreType.DMA((4, 6)),
            pltpu.SemaphoreType.DMA((len(KEPT) + 2,)),
            pltpu.SemaphoreType.DMA,
        ],
        24 * MACS,
        45000000,
        "middle",
        [ANY] * len(KEPT) + [ANY, VMEM],
        BIG_GRANT,
    )(
        h0, received, cotangent, swapped, half, first, lens, *smalls,
        *weights[0], *weights[1], *weights[2], *weights[3],
    )


MIB = 1024 * 1024


def half_columns(ref, which):
    size = ref.shape[1] // 2
    return ref[:, pl.ds(pl.multiple_of(which * size, 128), size)]


class Arriving:
    def __init__(self, pairs, sems):
        self.copies = {}
        for place, (name, source, dest) in enumerate(pairs):
            copy = pltpu.make_async_copy(source, dest, sems.at[place])
            copy.start()
            self.copies[name] = (copy, dest)

    def get(self, name):
        copy, dest = self.copies[name]
        copy.wait()
        return dest


class Leaving:
    def __init__(self, sems):
        self.sems = sems
        self.copies = []

    def send(self, source, target):
        copy = pltpu.make_async_copy(source, target, self.sems.at[len(self.copies)])
        copy.start()
        self.copies.append(copy)

    def wait(self):
        for copy in self.copies:
            copy.wait()


def send_folded(leaving, local, target, left_side, right):
    for block in range(right.shape[1] // WIDTH):
        rows = pl.ds(block * 384, 384)
        grad = dot_tn(left_side, right[:, block * WIDTH : (block + 1) * WIDTH])
        local[rows, :] = grad.astype(LOW)
        leaving.send(local.at[rows], target.at[rows])


TOKEN = shape((8, 128), F32)
GRAD_SHAPE = (1536, WIDTH)
GRAD_SCRATCH = pltpu.VMEM(GRAD_SHAPE, LOW)


def back_feed(cotangent, swapped, returned, half, first, weights, smalls, kept):
    u, slope, active, n1, i1, n2, i2 = kept

    def body(cot, swap, returned, half, first, so, sp, i1, n2, i2, uo, up, do, dp, u, slope, active, n1, *rest):
        outs, rest = rest[:8], rest[8:]
        down_other, down_own, up_other, up_own, gr1, gb, gsmall, token = outs
        gr2, gz, ga, v0, v1, v2, v3, small, raw, wu, wd, vu, vs, va, vn, sems, in_sems, out_sems = rest
        enter = enter_cotangent(half, cot, swap, raw, sems.at[2, 0])
        arriving = Arriving([("active", active, va)], in_sems)
        wdown = Weight(half[0], do, dp, wd, sems.at[1])
        later = Arriving(
            [("slope", slope, vs), ("normal", n1, vn), ("u", u, vu)],
            in_sems.at[pl.ds(1, 3)],
        )
        wup = Weight(half[0], uo, up, wu, sems.at[0])
        pick_halves(half, so, sp, small)
        enter.wait()
        upstream = jnp.where(first[0] > 0, returned[...], raw[...].reshape(ROWS, WIDTH))
        top_back_body(upstream.astype(F32), small, n2, i2, gr2, gz, gsmall)
        leaving = Leaving(out_sems)
        arriving.get("active")
        for which, local, target in ((1 - half[0], v0, down_other), (half[0], v1, down_own)):
            local[...] = dot_tn(half_columns(va, which), gz[...]).astype(LOW)
            leaving.send(local, target)
        later.get("slope")
        later.get("normal")
        feed_back_body(gr2, gz, wup, wdown, small, vs, vn, i1, ga, gr1, gb, gsmall)
        later.get("u")
        for which, local, target in ((1 - half[0], v2, up_other), (half[0], v3, up_own)):
            send_folded(leaving, local, target, half_columns(vu, which), ga)
        token[...] = jnp.zeros(token.shape, F32)
        leaving.wait()

    return kernel_call(
        body,
        [ANY, ANY, VMEM, SMEM, SMEM] + [VMEM] * 5 + [ANY] * 8,
        [shape(GRAD_SHAPE)] * 4
        + [shape(ROW_SHAPE, F32), shape(ROW_SHAPE), shape((2, SMALL), F32), TOKEN],
        [
            pltpu.VMEM(ROW_SHAPE, F32),
            pltpu.VMEM(ROW_SHAPE, LOW),
            pltpu.VMEM(FEED_SHAPE, LOW),
            *[GRAD_SCRATCH] * 4,
            SMALL_SCRATCH,
            pltpu.VMEM((2, LENGTH, WIDTH), LOW),
            *FEED_WEIGHTS,
            pltpu.VMEM(ROW_SHAPE, LOW),
            pltpu.VMEM(FEED_SHAPE, LOW),
            pltpu.VMEM(FEED_SHAPE, LOW),
            pltpu.VMEM(ROW_SHAPE, F32),
            pltpu.SemaphoreType.DMA((3, 2)),
            pltpu.SemaphoreType.DMA((4,)),
            pltpu.SemaphoreType.DMA((10,)),
        ],
        200 * MACS,
        600000000,
        "back_feed",
        [ANY] * 4 + [VMEM] * 4,
        BIG_GRANT,
    )(
        cotangent, swapped, returned, half, first, *smalls, i1, n2, i2, *weights[2], *weights[3],
        u, slope, active, n1,
    )


def back_attend(gb, gr1, half, first, spans, weights, gsmall, h, qkv, probs, mixed):
    def body(gb, half, first, spans, gsmall, oo, op, qo, qp, gr1, h, qkv, probs, mixed, *rest):
        outs, rest = rest[:6], rest[6:]
        other, own, small_other, small_own, gh, token = outs
        gqkv, go, gqv, vother, vown, wo, wq, vr, vh, vq, vp, vm, sems, in_sems, out_sems = rest
        wout = Weight(half[0], oo, op, wo, sems.at[0])
        arriving = Arriving([("qkv", qkv, vq), ("probs", probs, vp)], in_sems)
        wqkv = Weight(half[0], qo, qp, wq, sems.at[1], False)
        arriving.get("qkv")
        arriving.get("probs")
        wqkv.start()
        late = Arriving([("h", h, vh), ("mixed", mixed, vm), ("gr1", gr1, vr)], in_sems.at[pl.ds(2, 3)])
        heads_back_body(gb, wout, vq, vp, gqkv, gqv, go)
        leaving = Leaving(out_sems)
        late.get("h")
        late.get("mixed")
        for which, local, target in ((1 - half[0], vother, other), (half[0], vown, own)):
            send_folded(leaving, local, target, half_columns(vh, which), gqkv)
            local[1152:, :] = dot_tn(half_columns(vm, which), gb[...]).astype(LOW)
            leaving.send(local.at[pl.ds(1152, 384)], target.at[pl.ds(1152, 384)])
        late.get("gr1")
        full = vr[...] + dot_nt(gqkv[...], wqkv.get())
        dropped = span_rows(spans, half) & (first[0] > 0)
        zero = jnp.zeros_like(full)
        gh[...] = jnp.where(dropped, zero, full).astype(LOW)
        gmask = column_sum(jnp.where(dropped, full, zero))
        for which, target in ((1 - half[0], small_other), (half[0], small_own)):
            target[:, :WIDTH] = gqv[pl.ds(which, 1), :]
            target[:, WIDTH:SMALL] = gsmall[pl.ds(which, 1), WIDTH:]
            target[:, SMALL:] = gmask
        token[...] = jnp.zeros(token.shape, F32)
        leaving.wait()

    return kernel_call(
        body,
        [VMEM, SMEM, SMEM, SMEM, VMEM] + [ANY] * 9,
        [
            shape(GRAD_SHAPE),
            shape(GRAD_SHAPE),
            shape((1, SMALL + WIDTH), F32),
            shape((1, SMALL + WIDTH), F32),
            shape(ROW_SHAPE),
            TOKEN,
        ],
        [
            pltpu.VMEM(QKV_SHAPE, LOW),
            pltpu.VMEM(ROW_SHAPE, LOW),
            pltpu.VMEM((2, WIDTH), F32),
            GRAD_SCRATCH,
            GRAD_SCRATCH,
            ATTEND_WEIGHTS[1],
            ATTEND_WEIGHTS[0],
            pltpu.VMEM(ROW_SHAPE, F32),
            pltpu.VMEM(ROW_SHAPE, LOW),
            pltpu.VMEM(QKV_SHAPE, LOW),
            pltpu.VMEM(PROBS_SHAPE, LOW),
            pltpu.VMEM(ROW_SHAPE, LOW),
            pltpu.SemaphoreType.DMA((2, 2)),
            pltpu.SemaphoreType.DMA((5,)),
            pltpu.SemaphoreType.DMA((8,)),
        ],
        180 * MACS,
        400000000,
        "back_attend",
        [ANY, ANY] + [VMEM] * 4,
    )(gb, half, first, spans, gsmall, *weights[1], *weights[0], gr1, h, qkv, probs, mixed)


TAIL = 16
BLOCK = 96


def add_rows(target, sources, at, rows):
    for start in range(0, rows, BLOCK):
        size = min(BLOCK, rows - start)
        place = pl.ds(at + start, size)
        if not isinstance(at, int):
            place = pl.ds(pl.multiple_of(at + start, 16), size)
        if len(sources) == 2:
            target[start : start + size, :] = sources[0][place, :] + sources[1][place, :]
            continue
        total = sources[0][place, :].astype(F32)
        for source in sources[1:]:
            total = total + source[place, :].astype(F32)
        target[start : start + size, :] = total.astype(LOW)


LONG = 30000000000


def ordered(
    name, body, ins, outs, where, after, out_specs=None, scratch=(), in_specs=None, grant=16, aliases=None,
    flops=LONG,
):
    count, made = len(ins), len(outs)

    def kernel(where, after, *refs):
        refs[count + made][...] = jnp.zeros(TOKEN.shape, F32)
        body(where, refs[:count], refs[count : count + made] + refs[count + made + 1 :])

    result = pl.pallas_call(
        kernel,
        in_specs=[SMEM, ANY] + (in_specs or [VMEM] * count),
        out_specs=(out_specs or [VMEM] * made) + [VMEM],
        out_shape=list(outs) + [TOKEN],
        scratch_shapes=list(scratch),
        input_output_aliases=aliases or {},
        compiler_params=pltpu.CompilerParams(vmem_limit_bytes=grant * MIB),
        cost_estimate=pl.CostEstimate(flops=flops, bytes_accessed=flops, transcendentals=0),
        name=name,
    )(where, after, *ins)
    return result[:made], result[made]


def partner(x, axis, bit):
    return lax.ppermute(x, axis, [(i, i ^ 1 << bit) for i in range(lax.axis_size(axis))])


def moved_on(index, axis, steps):
    z, x, y = index // 8, index // 2 % 4, index % 2
    if axis == "z":
        z = steps(z)
    elif axis == "x":
        x = steps(x)
    else:
        y = steps(y)
    return z * 8 + x * 2 + y


def send_along(value, axes, place):
    pairs = []
    for section in range(4):
        for index in range(32):
            to = moved_on(index, axes[section % 2], place)
            pairs.append((section * 32 + index, section * 32 + to))
    return lax.ppermute(value, ("section", "dp"), pairs)


def exchange(value, part, step):
    flip = 1 if part == step else 3
    return send_along(value, "zx", lambda place: place ^ flip)


def turn(value, steps):
    return send_along(value, "xz", lambda place: (place + steps) % 4)


def across_y(value):
    return send_along(value, "yy", lambda place: place ^ 1)


def swap_core_one(value):
    pairs = [
        (section * 32 + index, section * 32 + (index ^ 1)) for section in (1, 3) for index in range(32)
    ]
    return lax.ppermute(value, ("section", "dp"), pairs)


def between_layers(value, back):
    pairs = []
    for core in range(2):
        for index in range(32):
            pair = (core * 32 + index, (core + 2) * 32 + (index ^ core))
            pairs.append(pair[::-1] if back else pair)
    return lax.ppermute(value, ("section", "dp"), pairs)


def own_places(core):
    index = lax.axis_index("dp")
    z, x = index // 8, index // 2 % 4
    ring = jnp.where(core == 0, z, x)
    high = ring // 2
    low = high ^ (ring % 2)
    table = [low, high, high, low, jnp.where(core == 0, x, z)]
    return jnp.stack(table).astype(jnp.int32)


def row_shapes(*counts):
    return [shape((count, WIDTH)) for count in counts]


def add_tail(target, rows, sources, at, extra):
    if extra:
        total = sources[0][at : at + extra, :].astype(F32)
        for source in sources[1:]:
            total = total + source[at : at + extra, :].astype(F32)
        target[rows : rows + extra, :] = total.astype(LOW)


class Chain:
    def __init__(self, name, places, tail=0):
        self.name = name
        self.places = places
        self.tail = (0, tail)
        self.keep = [None, None]
        self.got = [None, None]

    def kernel(self, name, body, ins, outs, token, *more, **named):
        return ordered(self.name + name, body, ins, outs, self.places, token, *more, **named)

    def pairs(self):
        return (self.keep[0], self.got[0], self.keep[1], self.got[1])

    def start(self, sources, rows, token, tail_ins=(), tail_body=None):
        self.rows = rows // 2
        half_rows, tails = self.rows, self.tail
        arrays = []
        for own, got, _ in sources:
            arrays += [own, got]

        def body(places, ins, outs):
            for part in range(2):
                bit, at = places[2 * part], sources[part][2]
                pair = ins[2 * part : 2 * part + 2]
                for target, which in ((outs[2 * part + 1], 1 - bit), (outs[2 * part], bit)):
                    add_rows(target, pair, at + which * half_rows, half_rows)
                    if tails[part]:
                        target[half_rows:, :] = tail_body(ins[4:])

        counts = [half_rows + tails[0]] * 2 + [half_rows + tails[1]] * 2
        outs, token = self.kernel(
            "start", body, tuple(arrays) + tuple(tail_ins), row_shapes(*counts), token
        )
        for part in range(2):
            self.keep[part] = outs[2 * part]
            self.got[part] = exchange(outs[2 * part + 1], part, 0)
        return token

    def start_copied(self, sources, rows, token, tail_ins=(), tail_body=None):
        self.rows = rows // 2
        half_rows, tails = self.rows, self.tail
        arrays = []
        for own, got, _ in sources:
            arrays += [own, got]
        sizes = [pltpu.VMEM((rows, WIDTH), LOW)] * 4

        def body(places, ins, refs):
            outs, held, sems = refs[:4], refs[4:8], refs[8]
            copies = []
            for index in range(4):
                at = sources[index // 2][2]
                copy = pltpu.make_async_copy(
                    ins[index].at[pl.ds(at, rows)], held[index], sems.at[index]
                )
                copy.start()
                copies.append(copy)
            for part in range(2):
                bit = places[2 * part]
                pair = held[2 * part : 2 * part + 2]
                copies[2 * part].wait()
                copies[2 * part + 1].wait()
                for target, which in ((outs[2 * part + 1], 1 - bit), (outs[2 * part], bit)):
                    add_rows(target, pair, which * half_rows, half_rows)
                    if tails[part]:
                        target[half_rows:, :] = tail_body(ins[4:])

        counts = [half_rows + tails[0]] * 2 + [half_rows + tails[1]] * 2
        outs, token = self.kernel(
            "start",
            body,
            tuple(arrays) + tuple(tail_ins),
            row_shapes(*counts),
            token,
            scratch=(*sizes, pltpu.SemaphoreType.DMA((4,))),
            in_specs=[ANY] * 4 + [VMEM] * len(tail_ins),
            grant=63,
        )
        for part in range(2):
            self.keep[part] = outs[2 * part]
            self.got[part] = exchange(outs[2 * part + 1], part, 0)
        return token

    def halve(self, token):
        self.rows //= 2
        rows, tails = self.rows, self.tail

        def body(places, ins, outs):
            for part in range(2):
                bit = places[2 * part + 1]
                pair = ins[2 * part : 2 * part + 2]
                for target, which in ((outs[2 * part + 1], 1 - bit), (outs[2 * part], bit)):
                    add_rows(target, pair, which * rows, rows)
                    add_tail(target, rows, pair, 2 * rows, tails[part])

        counts = [rows + tails[0]] * 2 + [rows + tails[1]] * 2
        outs, token = self.kernel(
            "halve", body, self.pairs(), row_shapes(*counts), token
        )
        for part in range(2):
            self.keep[part] = outs[2 * part]
            self.got[part] = exchange(outs[2 * part + 1], part, 1)
        return token

    def cross(self, token):
        whole_rows, extra = self.rows, self.tail[1]
        rows = whole_rows // 2

        def body(places, ins, refs):
            outs, total = refs[:4], refs[4]
            add_rows(total.at[pl.ds(0, whole_rows)], ins[:2], 0, whole_rows)
            add_rows(total.at[pl.ds(whole_rows, whole_rows)], ins[2:], 0, whole_rows)
            for steps in range(4):
                quarter = (places[4] + steps) % 4
                outs[steps][:rows, :] = total[pl.ds(pl.multiple_of(quarter * rows, 16), rows), :]
                add_tail(outs[steps], rows, ins[2:], whole_rows, extra)

        (self.own, *sends), token = self.kernel(
            "cross",
            body,
            self.pairs(),
            row_shapes(*[rows + extra] * 4),
            token,
            None,
            (pltpu.VMEM((2 * whole_rows, WIDTH), LOW),),
        )
        self.rows = rows
        self.ring = [turn(send, steps) for steps, send in zip((1, 2, 3), sends)]
        return token

    def across(self, token):
        rows = self.rows + self.tail[1]

        def body(places, ins, outs):
            add_rows(outs[0], ins, 0, rows)

        (self.own,), token = self.kernel(
            "across", body, (self.own, *self.ring), row_shapes(rows), token
        )
        self.other = across_y(self.own)
        return token

    def total(self, token, more_outs=(), more_body=None):
        rows, extra = self.rows, self.tail[1]

        def body(places, ins, outs):
            add_rows(outs[0], ins, 0, rows)
            if extra:
                add_rows(outs[1], ins, rows, extra)
                more_body(outs[1][...].astype(F32), outs[2:])

        counts = [rows] + ([extra] if extra else [])
        outs, token = self.kernel(
            "total", body, (self.own, self.other), row_shapes(*counts) + list(more_outs), token
        )
        self.own = outs[0]
        self.tail_sum = outs[1] if extra else None
        self.ring = [turn(self.own, steps) for steps in (1, 2, 3)]
        return outs[2:], token

    def back(self, token, more_ins=(), more_outs=(), more_body=None):
        rows = self.rows

        def body(places, ins, refs):
            outs, total = refs[:-1], refs[-1]
            for steps in range(4):
                quarter = (places[4] - steps + 4) % 4
                total[pl.ds(pl.multiple_of(quarter * rows, 16), rows), :] = ins[steps][...]
            outs[0][...] = total[: 2 * rows, :]
            outs[1][...] = total[2 * rows :, :]
            if more_body is not None:
                more_body(ins[4:], outs[2:])

        outs, token = self.kernel(
            "back",
            body,
            (self.own, *self.ring) + tuple(more_ins),
            row_shapes(2 * rows, 2 * rows) + list(more_outs),
            token,
            None,
            (pltpu.VMEM((4 * rows, WIDTH), LOW),),
        )
        self.rows = 2 * rows
        self.keep = list(outs[:2])
        self.got = [exchange(self.keep[part], part, 1) for part in range(2)]
        return outs[2:], token

    def double(self, token, flops):
        rows = self.rows

        def body(places, ins, outs):
            for part in range(2):
                bit = places[2 * part + 1]
                for which, source in ((bit, ins[2 * part]), (1 - bit, ins[2 * part + 1])):
                    outs[part][pl.ds(pl.multiple_of(which * rows, 16), rows), :] = source[...]

        outs, token = self.kernel(
            "double", body, self.pairs(), row_shapes(2 * rows, 2 * rows), token, flops=flops
        )
        self.rows = 2 * rows
        self.keep = list(outs)
        self.got = [exchange(self.keep[part], part, 0) for part in range(2)]
        return token

    def finish(self, token, outs, place, got, flops, more_ins=(), more_outs=(), more_body=None):
        rows = self.rows
        mine = tuple(self.got if got else self.keep)
        kept = tuple(outs) if got else ()

        def body(places, ins, refs):
            targets, wide, sems = refs[: len(outs)], refs[-2], refs[-1]
            if more_body is not None:
                more_body(ins[2 + len(kept) :], refs[len(outs) : -2])
            waits = []
            for part in range(2):
                bit = places[2 * part]
                half = 1 - bit if got else bit
                wide[part] = ins[part][...].astype(F32)
                at = 0
                for size, starts in place(targets, part, half):
                    source, sem = wide.at[part, pl.ds(at, size)], sems.at[len(waits)]
                    starts(source, sem)
                    waits.append((size, source, sem))
                    at += size
            for size, source, sem in waits:
                pltpu.make_async_copy(source, wide.at[0, pl.ds(0, size)], sem).wait()

        return self.kernel(
            "finish",
            body,
            mine + kept + tuple(more_ins),
            [shape(out.shape, F32) for out in outs] + list(more_outs),
            token,
            out_specs=[ANY] * len(outs) + [VMEM] * len(more_outs),
            scratch=(pltpu.VMEM((2, rows, WIDTH), F32), pltpu.SemaphoreType.DMA((4,))),
            in_specs=[VMEM] * 2 + [ANY] * len(kept) + [VMEM] * len(more_ins),
            grant=24,
            flops=flops,
            aliases={4 + index: index for index in range(len(kept))},
        )


def copy_to(target):
    return lambda source, sem: pltpu.make_async_copy(source, target, sem).start()


def block_columns(block):
    return pl.ds(pl.multiple_of(block * WIDTH, 128), WIDTH)


def place_x(refs, part, half):
    down, up = refs
    if part == 0:
        return [(768, copy_to(down.at[pl.ds(pl.multiple_of(half * 768, 8), 768)]))]
    return [(384, copy_to(up.at[:, block_columns(2 * half + block)])) for block in range(2)]


def place_y(refs, part, half):
    qkv, out = refs
    if part == 0:
        return [(384, copy_to(qkv.at[:, block_columns(half)]))]

    def starts(source, sem):
        @pl.when(half == 0)
        def _():
            copy_to(qkv.at[:, block_columns(2)])(source, sem)

        @pl.when(half == 1)
        def _():
            copy_to(out)(source, sem)

    return [(384, starts)]


def pack_vectors(vectors):
    size = sum(vector.shape[0] for vector in vectors)
    total = jnp.zeros((size,), F32)
    at = 0
    for vector in vectors:
        total = total + jnp.pad(vector.astype(F32), (at, size - at - vector.shape[0]))
        at += vector.shape[0]
    return total.reshape(1, size)


def per_device(
    inputs,
    cotangent,
    lengths,
    cdr_spans,
    mask_vector,
    w_qkv,
    qv_bias,
    w_out,
    b_out,
    norm1_gain,
    norm1_bias,
    w_up,
    b_up,
    w_down,
    b_down,
    norm2_gain,
    norm2_bias,
):
    section_index = lax.axis_index("section")
    core = section_index % 2
    half = core.astype(jnp.int32).reshape(1)
    first = (section_index < 2).astype(jnp.int32).reshape(1)
    places = own_places(core)
    small = pack_vectors(
        (
            qv_bias,
            b_out,
            norm1_gain,
            norm1_bias,
            b_up,
            b_down,
            norm2_gain,
            norm2_bias,
            mask_vector,
        )
    )
    small_got = partner(small, "section", 0)
    got_qkv, got_out = partner((w_qkv, w_out), "section", 0)
    w_up, w_down, got_qkv, got_out, small_got = lax.optimization_barrier(
        (w_up, w_down, got_qkv, got_out, small_got)
    )
    smalls = (small, small_got)
    got_up, got_down = partner((w_up, w_down), "section", 0)
    weights = [(w_qkv, got_qkv), (w_out, got_out), (w_up, got_up), (w_down, got_down)]

    swapped = swap_core_one(cotangent)
    lens_got = swap_core_one(lengths)
    swaps = (core == 1) & (section_index >= 2)
    layer_lens = jnp.where(swaps, lens_got, lengths)

    u, h0 = attend_first(inputs, half, lengths, cdr_spans, weights, smalls)
    first_out = feed_first(u, half, weights, smalls)
    received = between_layers(first_out, False)
    kept = middle(h0, received, cotangent, swapped, half, first, layer_lens, weights, smalls)
    h, qkv, probs, mixed, normal1, inverse1, u, slope, active, normal2, inverse2, output = kept[:12]
    returned = between_layers(kept[13], True)

    a_other, a_own, b_other, b_own, gr1, gb, gsmall, token = back_feed(
        cotangent,
        swapped,
        returned,
        half,
        first,
        weights,
        smalls,
        (u, slope, active, normal1, inverse1, normal2, inverse2),
    )
    a_got = partner(a_other, "section", 0)
    b_got = partner(b_other, "section", 0)
    x, y = Chain("x_", places), Chain("y_", places, TAIL)
    y_other, y_own, small_other, small_own, gh, token = back_attend(
        gb, gr1, half, first, cdr_spans, weights, gsmall, h, qkv, probs, mixed
    )
    y_got = partner(y_other, "section", 0)
    small_got = partner(small_other, "section", 0)
    token = x.start_copied([(a_own, a_got, 0), (b_own, b_got, 0)], 1536, token)

    def tail_rows(ins):
        total = ins[0][...] + ins[1][...]
        rows = [total[:, at : at + WIDTH] for at in range(0, SMALL + WIDTH, WIDTH)]
        rows.append(jnp.zeros((TAIL - len(rows), WIDTH), F32))
        return jnp.concatenate(rows, axis=0).astype(LOW)

    token = y.start(
        [(y_own, y_got, 0), (y_own, y_got, 768)], 768, token, (small_own, small_got), tail_rows
    )
    both, token = lax.optimization_barrier((kept[12], token))
    both_got = swap_core_one(both)
    token = x.halve(token)
    token = y.halve(token)
    token = x.cross(token)
    token = y.cross(token)
    token = x.across(token)
    token = y.across(token)
    _, token = x.total(token)

    def small_outputs(tail, outs):
        flat = jnp.concatenate([tail[row : row + 1, :] for row in range(6)], axis=1)
        at = 0
        for out, size in zip(outs, SIZES):
            out[...] = flat[0, at : at + size]
            at += size

    out_small, token = y.total(token, [shape((size,), F32) for size in SIZES], small_outputs)
    _, token = x.back(token)

    def mask_output(ins, outs):
        outs[0][...] = ins[0][6, :].astype(F32) + ins[1][6, :].astype(F32)

    _, token = y.back(token)
    gradients_x = [shape((1536, WIDTH), F32), shape((384, HIDDEN), F32)]
    gradients_y = [shape((384, 3 * WIDTH), F32), shape((384, WIDTH), F32)]
    token = x.double(token, LONG)
    gradients_x, token = x.finish(token, gradients_x, place_x, False, LONG)
    token = y.double(token, 0)
    tail_sum, token = lax.optimization_barrier((y.tail_sum, token))
    mask_got = partner(tail_sum, "section", 1)
    gradients_y, token = y.finish(token, gradients_y, place_y, False, 0)
    both_got, token = lax.optimization_barrier((both_got, token))
    (g_down, g_up), token = x.finish(token, gradients_x, place_x, True, LONG)
    (g_qkv, g_out, mask_grad), token = y.finish(
        token,
        gradients_y,
        place_y,
        True,
        LONG,
        (tail_sum, mask_got),
        [shape((WIDTH,), F32)],
        mask_output,
    )
    output = jnp.where(swaps, both_got[0], output)
    gh = jnp.where(swaps, both_got[1], gh)

    g_qv, g_bo, g_n1g, g_n1b, g_bu, g_bd, g_n2g, g_n2b = out_small
    return (
        output.reshape(1, 2, LENGTH, WIDTH),
        gh.reshape(1, 2, LENGTH, WIDTH),
        mask_grad,
        g_qkv,
        g_qv,
        g_out,
        g_bo,
        g_n1g,
        g_n1b,
        g_up,
        g_bu,
        g_down,
        g_bd,
        g_n2g,
        g_n2b,
    )


def solution(mesh):
    in_specs = (
        P(None, "dp", None, None),
        P(None, "dp", None, None),
        P(None, "dp"),
        P(None, "dp", None),
        P(),
        P("section", None),
        P("section"),
        P("section", None),
        P("section"),
        P("section"),
        P("section"),
        P("section", None),
        P("section"),
        P("section", None),
        P("section"),
        P("section"),
        P("section"),
    )
    out_specs = (
        P("section", "dp", None, None),
        P("section", "dp", None, None),
        P(),
        P("section", None),
        P("section"),
        P("section", None),
        P("section"),
        P("section"),
        P("section"),
        P("section", None),
        P("section"),
        P("section", None),
        P("section"),
        P("section"),
        P("section"),
    )
    return jax.shard_map(
        per_device, mesh=mesh, in_specs=in_specs, out_specs=out_specs, check_vma=False
    )
```

```python
import functools
import math

import jax
import jax.numpy as jnp
from jax import lax
from jax.experimental import pallas as pl
from jax.experimental.pallas import tpu as pltpu
from jax.sharding import PartitionSpec as P

EPSILON = 1e-05
F32 = jnp.float32
LOW = jnp.bfloat16
WIDTH = 768
LENGTH = 160
ROWS = 320
HIDDEN = 3072
PAIRS = 6
SCALE = 0.125
SIZES = (768, 384, 384, 384, 1536, 384, 384, 384)
QV, B_OUT, N1G, N1B, B_UP, B_DOWN, N2G, N2B = (sum(SIZES[:at]) for at in range(8))
SMALL = sum(SIZES)
VMEM_LIMIT = 63 * 1024 * 1024
BIG_GRANT = 46 * 1024 * 1024


def dot_nn(left_side, right_side):
    return jnp.dot(left_side, right_side, preferred_element_type=F32)


def dot_nt(left_side, right_side):
    return lax.dot_general(
        left_side, right_side, (((1,), (1,)), ((), ())), preferred_element_type=F32
    )


def dot_tn(left_side, right_side):
    return lax.dot_general(
        left_side, right_side, (((0,), (0,)), ((), ())), preferred_element_type=F32
    )


class Weight:
    def __init__(self, half, own, other, dest, sems, start=True, chunks=1):
        rows, wide = own.shape
        self.dest = dest
        self.wide = wide // chunks
        self.copies = []
        for chunk in range(chunks):
            at = pl.ds(chunk * self.wide, self.wide)
            for side, source in enumerate((own, other)):
                which = half if side == 0 else 1 - half
                place = dest.at[pl.ds(which * rows, rows)]
                if chunks > 1:
                    source, place = source.at[:, at], place.at[:, at]
                self.copies.append(
                    pltpu.make_async_copy(source, place, sems.at[2 * chunk + side])
                )
        if start:
            self.start()

    def start(self):
        for copy in self.copies:
            copy.start()

    def get(self):
        for copy in self.copies:
            copy.wait()
        self.copies = []
        return self.dest[...]

    def chunk(self, index):
        for copy in self.copies[:2]:
            copy.wait()
        self.copies = self.copies[2:]
        return self.dest[:, index * self.wide : (index + 1) * self.wide]


class Ready:
    def __init__(self, ref, chunks=1):
        self.ref = ref
        self.wide = ref.shape[1] // chunks

    def get(self):
        return self.ref[...]

    def chunk(self, index):
        return self.ref[:, index * self.wide : (index + 1) * self.wide]


def whole(smalls, at, size):
    return jnp.concatenate([smalls[0:1, at : at + size], smalls[1:2, at : at + size]], axis=1)


def split_heads(tensor):
    lane = lax.broadcasted_iota(jnp.int32, tensor.shape, 1)
    zero = jnp.zeros_like(tensor)
    return jnp.concatenate(
        [jnp.where(lane < 64, tensor, zero), jnp.where(lane < 64, zero, tensor)], axis=0
    )


def join_heads(tensor):
    lane = lax.broadcasted_iota(jnp.int32, (LENGTH, 128), 1)
    return jnp.where(lane < 64, tensor[:LENGTH], tensor[LENGTH:])


def normalize(values):
    center = values - jnp.mean(values, axis=-1, keepdims=True)
    spread = jnp.mean(center * center, axis=-1, keepdims=True)
    inverse = lax.rsqrt(spread + EPSILON)
    return center * inverse, inverse


def normalize_back(upstream, gain, normal, inverse):
    scaled = upstream * gain
    first = jnp.mean(scaled, axis=-1, keepdims=True)
    second = jnp.mean(scaled * normal, axis=-1, keepdims=True)
    return inverse * (scaled - first - normal * second)


def gelu_parts(values):
    size = jnp.abs(values)
    below = 1.0 + (0.3275911 * math.sqrt(0.5)) * size
    t = pl.reciprocal(below, approx=True)
    t = t * (2.0 - below * t)
    series = t * (
        0.5 * 0.254829592
        + t
        * (
            0.5 * -0.284496736
            + t * (0.5 * 1.421413741 + t * (0.5 * -1.453152027 + t * (0.5 * 1.061405429)))
        )
    )
    bell = jnp.exp(-0.5 * values * values)
    tail = series * bell
    share = jnp.where(values >= 0.0, 1.0 - tail, tail)
    return values * share, share + values * bell * (1.0 / math.sqrt(2.0 * math.pi))


def column_sum(values):
    return jnp.sum(values, axis=0, keepdims=True)


def put_halves(target, at, row):
    size = row.shape[1] // 2
    target[0:1, at : at + size] = row[:, :size]
    target[1:2, at : at + size] = row[:, size:]


def places():
    for index in range(2 * PAIRS):
        chain, pair = divmod(index, PAIRS)
        rows = pl.ds(chain * LENGTH, LENGTH)
        yield index, chain, rows, [pl.ds((pair + block * PAIRS) * 128, 128) for block in range(3)]


def attend_body(h, wqkv, wout, smalls, lens, half, qkv, probs, mixed, normal1, inverse1, u, later):
    x = h[...]
    bias = jnp.concatenate(
        [smalls[0:1, :WIDTH], jnp.zeros((1, WIDTH), F32), smalls[1:2, :WIDTH]], axis=1
    )
    for block in range(3):
        at = block * WIDTH
        matrix = wqkv.chunk(block)
        if block == 0:
            for each in later:
                each.start()
        qkv[:, at : at + WIDTH] = (dot_nn(x, matrix) + bias[:, at : at + WIDTH]).astype(LOW)
    for index, chain, rows, (at_q, at_k, at_v) in places():
        scores = dot_nt(qkv[rows, at_k], split_heads(qkv[rows, at_q])) * SCALE
        key = lax.broadcasted_iota(jnp.int32, scores.shape, 0)
        scores = jnp.where(key < lens[half[0], chain], scores, -1000000000.0)
        grown = jnp.exp(scores - jnp.max(scores, axis=0, keepdims=True))
        weights = (grown * (1.0 / jnp.sum(grown, axis=0, keepdims=True))).astype(LOW)
        if probs is not None:
            probs[index] = weights
        mixed[rows, at_q] = join_heads(dot_tn(weights, qkv[rows, at_v])).astype(LOW)
    branch = dot_nn(mixed[...], wout.get()) + whole(smalls, B_OUT, 384)
    normal, inverse = normalize(x.astype(F32) + branch)
    if normal1 is not None:
        normal1[...] = normal
        inverse1[...] = inverse
    u[...] = (normal * whole(smalls, N1G, 384) + whole(smalls, N1B, 384)).astype(LOW)


CHUNK = 1024


def feed_body(u, wup, wdown, smalls, slope, active, normal2, inverse2, y, later=()):
    x = u[...]
    bias = whole(smalls, B_UP, 1536)
    def grow(part, at):
        grown, tangent = gelu_parts(part + bias[:, at : at + CHUNK])
        active[:, at : at + CHUNK] = grown.astype(LOW)
        if slope is not None:
            slope[:, at : at + CHUNK] = tangent.astype(LOW)

    up = wup.chunk(0)
    for each in later:
        each.start()
    grow(dot_nn(x, up), 0)
    up, last = wup.chunk(1), wup.chunk(2)
    grow(dot_nn(x, up), CHUNK)
    part = dot_nn(x, last)
    down = wdown.get()
    grow(part, 2 * CHUNK)
    total = x.astype(F32) + whole(smalls, B_DOWN, 384) + dot_nn(active[...], down)
    normal, inverse = normalize(total)
    if normal2 is not None:
        normal2[...] = normal
        inverse2[...] = inverse
    y[...] = (normal * whole(smalls, N2G, 384) + whole(smalls, N2B, 384)).astype(LOW)


def top_back_body(up, smalls, normal2, inverse2, gr2, gz, gsmall):
    normal = normal2[...]
    put_halves(gsmall, N2G, column_sum(up * normal))
    put_halves(gsmall, N2B, column_sum(up))
    grad = normalize_back(up, whole(smalls, N2G, 384), normal, inverse2[...])
    z = grad.astype(LOW)
    gz[...] = z
    put_halves(gsmall, B_DOWN, column_sum(z.astype(F32)))
    gr2[...] = grad


def feed_back_body(gr2, gz, wup, wdown, smalls, slope, normal1, inverse1, ga, gr1, gb, gsmall):
    z = gz[...]
    down = wdown.get()
    sums = []
    for at in range(0, HIDDEN, CHUNK):
        inner = dot_nt(z, down[at : at + CHUNK, :]) * slope[:, at : at + CHUNK].astype(F32)
        a = inner.astype(LOW)
        ga[:, at : at + CHUNK] = a
        sums.append(column_sum(a.astype(F32)))
    put_halves(gsmall, B_UP, jnp.concatenate(sums, axis=1))
    up = gr2[...] + dot_nt(ga[...], wup.get())
    normal = normal1[...]
    put_halves(gsmall, N1G, column_sum(up * normal))
    put_halves(gsmall, N1B, column_sum(up))
    grad = normalize_back(up, whole(smalls, N1G, 384), normal, inverse1[...])
    gr1[...] = grad
    b = grad.astype(LOW)
    gb[...] = b
    put_halves(gsmall, B_OUT, column_sum(b.astype(F32)))


def heads_back_body(gb, wout, qkv, probs, gqkv, gqv, go):
    go[...] = dot_nt(gb[...], wout.get()).astype(LOW)
    for index, chain, rows, (at_q, at_k, at_v) in places():
        k = qkv[rows, at_k]
        g = split_heads(go[rows, at_q])
        weights = probs[index]
        wide = weights.astype(F32)
        inner = dot_nt(qkv[rows, at_v], g)
        inner = wide * (inner - jnp.sum(wide * inner, axis=0, keepdims=True))
        s = inner.astype(LOW)
        gqkv[rows, at_q] = (join_heads(dot_tn(s, k)) * SCALE).astype(LOW)
        gqkv[rows, at_k] = (dot_nn(s, split_heads(qkv[rows, at_q])) * SCALE).astype(LOW)
        gqkv[rows, at_v] = dot_nn(weights, g).astype(LOW)
    if gqv is not None:
        gqv[0:1, :] = column_sum(gqkv[:, :WIDTH].astype(F32))
        gqv[1:2, :] = column_sum(gqkv[:, 2 * WIDTH :].astype(F32))


def span_rows(spans, half):
    row = lax.broadcasted_iota(jnp.int32, (ROWS, 1), 0)
    inside = row < 0
    for chain in range(2):
        start = spans[half[0], chain, 0] + chain * LENGTH
        end = spans[half[0], chain, 1] + chain * LENGTH
        inside = inside | ((row >= start) & (row < end))
    return inside


def pick_halves(half, own, other, smalls):
    low = half[0] == 0
    smalls[0:1, :] = jnp.where(low, own[:, :SMALL], other[:, :SMALL])
    smalls[1:2, :] = jnp.where(low, other[:, :SMALL], own[:, :SMALL])


VMEM = pl.BlockSpec(memory_space=pltpu.VMEM)
SMEM = pl.BlockSpec(memory_space=pltpu.SMEM)
ANY = pl.BlockSpec(memory_space=pl.ANY)
SMALL_SCRATCH = pltpu.VMEM((2, SMALL), F32)
QKV_SHAPE = (ROWS, 3 * WIDTH)
PROBS_SHAPE = (2 * PAIRS, LENGTH, 2 * LENGTH)
ROW_SHAPE = (ROWS, WIDTH)
FEED_SHAPE = (ROWS, HIDDEN)
MACS = ROWS * WIDTH * WIDTH * 2
ATTEND_WEIGHTS = [pltpu.VMEM((WIDTH, 3 * WIDTH), LOW), pltpu.VMEM((WIDTH, WIDTH), LOW)]
FEED_WEIGHTS = [pltpu.VMEM((WIDTH, HIDDEN), LOW), pltpu.VMEM((HIDDEN, WIDTH), LOW)]


def shape(dims, kind=LOW):
    return jax.ShapeDtypeStruct(dims, kind)


def enter_cotangent(half, own, swapped, raw, sem):
    @pl.when(half[0] == 0)
    def _():
        pltpu.make_async_copy(own.at[0], raw, sem).start()

    @pl.when(half[0] == 1)
    def _():
        pltpu.make_async_copy(swapped.at[1], raw, sem).start()

    return pltpu.make_async_copy(swapped.at[1], raw, sem)


def kernel_call(body, ins, outs, scratch, flops, moved, name, out_specs=None, grant=VMEM_LIMIT):
    return pl.pallas_call(
        body,
        in_specs=ins,
        out_specs=out_specs or [VMEM] * len(outs),
        out_shape=outs,
        scratch_shapes=scratch,
        compiler_params=pltpu.CompilerParams(vmem_limit_bytes=grant),
        cost_estimate=pl.CostEstimate(flops=flops, bytes_accessed=moved, transcendentals=0),
        name=name,
    )


def attend_first(inputs, half, lens, spans, weights, smalls):
    def body(x, half, lens, spans, so, sp, qo, qp, oo, op, u, h, raw, small, qkv, mixed, wq, wo, sems):
        enter = pltpu.make_async_copy(x.at[half[0]], raw, sems.at[2, 0])
        enter.start()
        wqkv = Weight(half[0], qo, qp, wq, sems.at[0], True, 3)
        wout = Weight(half[0], oo, op, wo, sems.at[1], False)
        pick_halves(half, so, sp, small)
        enter.wait()
        mask = so[:, SMALL:].astype(LOW)
        h[...] = jnp.where(span_rows(spans, half), mask, raw[...].reshape(ROWS, WIDTH))
        attend_body(h, wqkv, wout, small, lens, half, qkv, None, mixed, None, None, u, [wout])

    return kernel_call(
        body,
        [ANY, SMEM, SMEM, SMEM, VMEM, VMEM] + [ANY] * 4,
        [shape(ROW_SHAPE), shape(ROW_SHAPE)],
        [
            pltpu.VMEM((2, LENGTH, WIDTH), LOW),
            SMALL_SCRATCH,
            pltpu.VMEM(QKV_SHAPE, LOW),
            pltpu.VMEM(ROW_SHAPE, LOW),
            *ATTEND_WEIGHTS,
            pltpu.SemaphoreType.DMA((3, 6)),
        ],
        40 * MACS,
        80000000,
        "attend_first",
    )(inputs, half, lens, spans, *smalls, *weights[0], *weights[1])


def feed_first(u, half, weights, smalls):
    def body(u, half, so, sp, uo, up, do, dp, y, small, active, wu, wd, sems):
        wup = Weight(half[0], uo, up, wu, sems.at[0], True, 3)
        wdown = Weight(half[0], do, dp, wd, sems.at[1], False)
        pick_halves(half, so, sp, small)
        feed_body(u, wup, wdown, small, None, active, None, None, y, [wdown])

    return kernel_call(
        body,
        [VMEM, SMEM, VMEM, VMEM] + [ANY] * 4,
        [shape(ROW_SHAPE)],
        [
            SMALL_SCRATCH,
            pltpu.VMEM(FEED_SHAPE, LOW),
            *FEED_WEIGHTS,
            pltpu.SemaphoreType.DMA((2, 6)),
        ],
        8 * MACS,
        14000000,
        "feed_first",
    )(u, half, *smalls, *weights[2], *weights[3])[0]


def assemble(half, weights):
    def body(half, *refs):
        sems = refs[12]
        wholes = [
            Weight(half[0], refs[2 * place], refs[2 * place + 1], refs[8 + place], sems.at[place])
            for place in range(4)
        ]
        for each in wholes:
            for copy in each.copies:
                copy.wait()

    sides = [side for pair in weights for side in pair]
    return kernel_call(
        body,
        [SMEM] + [ANY] * 8,
        [
            shape((WIDTH, 3 * WIDTH)),
            shape((WIDTH, WIDTH)),
            shape((WIDTH, HIDDEN)),
            shape((HIDDEN, WIDTH)),
        ],
        [pltpu.SemaphoreType.DMA((4, 2))],
        20 * MACS,
        60000000,
        "assemble",
        None,
        BIG_GRANT,
    )(half, *sides)


KEPT = [
    shape(ROW_SHAPE),
    shape(QKV_SHAPE),
    shape(PROBS_SHAPE),
    shape(ROW_SHAPE),
    shape(ROW_SHAPE, F32),
    shape((ROWS, 1), F32),
    shape(ROW_SHAPE),
    shape(FEED_SHAPE),
    shape(FEED_SHAPE),
    shape(ROW_SHAPE, F32),
    shape((ROWS, 1), F32),
    shape(ROW_SHAPE),
]


def middle(h0, received, cotangent, swapped, half, first, lens, weights, smalls):
    def body(h0, received, cot, swap, half, first, lens, so, sp, wq, wo, wu, wd, *rest):
        outs, rest = rest[: len(KEPT)], rest[len(KEPT) :]
        both, rest = rest[0], rest[1:]
        gh, small, gr2, gz, ga, gr1, gb, gsmall, gqkv, go, raw = rest[:11]
        keeps, out_sems, raw_sem = rest[11:-2], *rest[-2:]
        h, qkv, probs, mixed, normal1, inverse1, u, slope, active, normal2, inverse2, y = keeps
        wqkv, wout, wup, wdown = Ready(wq, 3), Ready(wo), Ready(wu, 3), Ready(wd)
        enter = enter_cotangent(half, cot, swap, raw, raw_sem)
        pick_halves(half, so, sp, small)
        leaving = []

        def leave(places):
            for place in places:
                copy = pltpu.make_async_copy(keeps[place], outs[place], out_sems.at[place])
                copy.start()
                leaving.append(copy)

        h[...] = jnp.where(first[0] > 0, h0[...], received[...])
        attend_body(
            h, wqkv, wout, small, lens, half, qkv, probs, mixed, normal1, inverse1, u, ()
        )
        leave(range(7))
        feed_body(u, wup, wdown, small, slope, active, normal2, inverse2, y)
        leave(range(7, 12))
        output = pltpu.make_async_copy(y, both.at[0], out_sems.at[len(KEPT)])
        output.start()
        leaving.append(output)
        enter.wait()
        upstream = raw[...].reshape(ROWS, WIDTH).astype(F32)
        top_back_body(upstream, small, normal2, inverse2, gr2, gz, gsmall)
        feed_back_body(gr2, gz, wup, wdown, small, slope, normal1, inverse1, ga, gr1, gb, gsmall)
        heads_back_body(gb, wout, qkv, probs, gqkv, None, go)
        gh[...] = (gr1[...] + dot_nt(gqkv[...], wqkv.get())).astype(LOW)
        output = pltpu.make_async_copy(gh, both.at[1], out_sems.at[len(KEPT) + 1])
        output.start()
        leaving.append(output)
        for copy in leaving:
            copy.wait()

    return kernel_call(
        body,
        [VMEM, VMEM, ANY, ANY, SMEM, SMEM, SMEM, VMEM, VMEM] + [VMEM] * 4,
        KEPT + [shape((2, ROWS, WIDTH)), shape(ROW_SHAPE)],
        [
            SMALL_SCRATCH,
            pltpu.VMEM(ROW_SHAPE, F32),
            pltpu.VMEM(ROW_SHAPE, LOW),
            pltpu.VMEM(FEED_SHAPE, LOW),
            pltpu.VMEM(ROW_SHAPE, F32),
            pltpu.VMEM(ROW_SHAPE, LOW),
            SMALL_SCRATCH,
            pltpu.VMEM(QKV_SHAPE, LOW),
            pltpu.VMEM(ROW_SHAPE, LOW),
            pltpu.VMEM((2, LENGTH, WIDTH), LOW),
            *[pltpu.VMEM(kept.shape, kept.dtype) for kept in KEPT],
            pltpu.SemaphoreType.DMA((len(KEPT) + 2,)),
            pltpu.SemaphoreType.DMA,
        ],
        24 * MACS,
        45000000,
        "middle",
        [ANY] * len(KEPT) + [ANY, VMEM],
        BIG_GRANT,
    )(
        h0, received, cotangent, swapped, half, first, lens, *smalls, *weights
    )


MIB = 1024 * 1024


def half_columns(ref, which):
    size = ref.shape[1] // 2
    return ref[:, pl.ds(pl.multiple_of(which * size, 128), size)]


class Arriving:
    def __init__(self, pairs, sems):
        self.copies = {}
        for place, (name, source, dest) in enumerate(pairs):
            copy = pltpu.make_async_copy(source, dest, sems.at[place])
            copy.start()
            self.copies[name] = (copy, dest)

    def get(self, name):
        copy, dest = self.copies[name]
        copy.wait()
        return dest


class Leaving:
    def __init__(self, sems):
        self.sems = sems
        self.copies = []

    def send(self, source, target):
        copy = pltpu.make_async_copy(source, target, self.sems.at[len(self.copies)])
        copy.start()
        self.copies.append(copy)

    def wait(self):
        for copy in self.copies:
            copy.wait()


def send_folded(leaving, local, target, left_side, right):
    for block in range(right.shape[1] // WIDTH):
        rows = pl.ds(block * 384, 384)
        grad = dot_tn(left_side, right[:, block * WIDTH : (block + 1) * WIDTH])
        local[rows, :] = grad.astype(LOW)
        leaving.send(local.at[rows], target.at[rows])


TOKEN = shape((8, 128), F32)
GRAD_SHAPE = (1536, WIDTH)
GRAD_SCRATCH = pltpu.VMEM(GRAD_SHAPE, LOW)


def back_feed(cotangent, swapped, returned, half, first, weights, smalls, kept):
    u, slope, active, n1, i1, n2, i2 = kept

    def body(cot, swap, returned, half, first, so, sp, i1, n2, i2, wu, wd, u, slope, active, n1, *rest):
        outs, rest = rest[:8], rest[8:]
        down_other, down_own, up_other, up_own, gr1, gb, gsmall, token = outs
        gr2, gz, ga, v0, v1, v2, v3, small, raw, vu, vs, va, vn, raw_sem, in_sems, out_sems = rest
        enter = enter_cotangent(half, cot, swap, raw, raw_sem)
        arriving = Arriving([("active", active, va)], in_sems)
        wdown, wup = Ready(wd), Ready(wu)
        later = Arriving(
            [("slope", slope, vs), ("normal", n1, vn), ("u", u, vu)],
            in_sems.at[pl.ds(1, 3)],
        )
        pick_halves(half, so, sp, small)
        enter.wait()
        upstream = jnp.where(first[0] > 0, returned[...], raw[...].reshape(ROWS, WIDTH))
        top_back_body(upstream.astype(F32), small, n2, i2, gr2, gz, gsmall)
        leaving = Leaving(out_sems)
        arriving.get("active")
        for which, local, target in ((1 - half[0], v0, down_other), (half[0], v1, down_own)):
            local[...] = dot_tn(half_columns(va, which), gz[...]).astype(LOW)
            leaving.send(local, target)
        later.get("slope")
        later.get("normal")
        feed_back_body(gr2, gz, wup, wdown, small, vs, vn, i1, ga, gr1, gb, gsmall)
        later.get("u")
        for which, local, target in ((1 - half[0], v2, up_other), (half[0], v3, up_own)):
            send_folded(leaving, local, target, half_columns(vu, which), ga)
        token[...] = jnp.zeros(token.shape, F32)
        leaving.wait()

    return kernel_call(
        body,
        [ANY, ANY, VMEM, SMEM, SMEM] + [VMEM] * 7 + [ANY] * 4,
        [shape(GRAD_SHAPE)] * 4
        + [shape(ROW_SHAPE, F32), shape(ROW_SHAPE), shape((2, SMALL), F32), TOKEN],
        [
            pltpu.VMEM(ROW_SHAPE, F32),
            pltpu.VMEM(ROW_SHAPE, LOW),
            pltpu.VMEM(FEED_SHAPE, LOW),
            *[GRAD_SCRATCH] * 4,
            SMALL_SCRATCH,
            pltpu.VMEM((2, LENGTH, WIDTH), LOW),
            pltpu.VMEM(ROW_SHAPE, LOW),
            pltpu.VMEM(FEED_SHAPE, LOW),
            pltpu.VMEM(FEED_SHAPE, LOW),
            pltpu.VMEM(ROW_SHAPE, F32),
            pltpu.SemaphoreType.DMA,
            pltpu.SemaphoreType.DMA((4,)),
            pltpu.SemaphoreType.DMA((10,)),
        ],
        200 * MACS,
        600000000,
        "back_feed",
        [ANY] * 4 + [VMEM] * 4,
        BIG_GRANT,
    )(
        cotangent, swapped, returned, half, first, *smalls, i1, n2, i2, weights[2], weights[3],
        u, slope, active, n1,
    )


def back_attend(gb, gr1, half, first, spans, weights, gsmall, h, qkv, probs, mixed):
    def body(gb, half, first, spans, gsmall, wo, wq, gr1, h, qkv, probs, mixed, *rest):
        outs, rest = rest[:6], rest[6:]
        other, own, small_other, small_own, gh, token = outs
        gqkv, go, gqv, vother, vown, vr, vh, vq, vp, vm, in_sems, out_sems = rest
        wout, wqkv = Ready(wo), Ready(wq)
        arriving = Arriving([("qkv", qkv, vq), ("probs", probs, vp)], in_sems)
        arriving.get("qkv")
        arriving.get("probs")
        late = Arriving([("h", h, vh), ("mixed", mixed, vm), ("gr1", gr1, vr)], in_sems.at[pl.ds(2, 3)])
        heads_back_body(gb, wout, vq, vp, gqkv, gqv, go)
        leaving = Leaving(out_sems)
        late.get("h")
        late.get("mixed")
        for which, local, target in ((1 - half[0], vother, other), (half[0], vown, own)):
            send_folded(leaving, local, target, half_columns(vh, which), gqkv)
            local[1152:, :] = dot_tn(half_columns(vm, which), gb[...]).astype(LOW)
            leaving.send(local.at[pl.ds(1152, 384)], target.at[pl.ds(1152, 384)])
        late.get("gr1")
        full = vr[...] + dot_nt(gqkv[...], wqkv.get())
        dropped = span_rows(spans, half) & (first[0] > 0)
        zero = jnp.zeros_like(full)
        gh[...] = jnp.where(dropped, zero, full).astype(LOW)
        gmask = column_sum(jnp.where(dropped, full, zero))
        for which, target in ((1 - half[0], small_other), (half[0], small_own)):
            target[:, :WIDTH] = gqv[pl.ds(which, 1), :]
            target[:, WIDTH:SMALL] = gsmall[pl.ds(which, 1), WIDTH:]
            target[:, SMALL:] = gmask
        token[...] = jnp.zeros(token.shape, F32)
        leaving.wait()

    return kernel_call(
        body,
        [VMEM, SMEM, SMEM, SMEM, VMEM, VMEM, VMEM] + [ANY] * 5,
        [
            shape(GRAD_SHAPE),
            shape(GRAD_SHAPE),
            shape((1, SMALL + WIDTH), F32),
            shape((1, SMALL + WIDTH), F32),
            shape(ROW_SHAPE),
            TOKEN,
        ],
        [
            pltpu.VMEM(QKV_SHAPE, LOW),
            pltpu.VMEM(ROW_SHAPE, LOW),
            pltpu.VMEM((2, WIDTH), F32),
            GRAD_SCRATCH,
            GRAD_SCRATCH,
            pltpu.VMEM(ROW_SHAPE, F32),
            pltpu.VMEM(ROW_SHAPE, LOW),
            pltpu.VMEM(QKV_SHAPE, LOW),
            pltpu.VMEM(PROBS_SHAPE, LOW),
            pltpu.VMEM(ROW_SHAPE, LOW),
            pltpu.SemaphoreType.DMA((5,)),
            pltpu.SemaphoreType.DMA((8,)),
        ],
        180 * MACS,
        400000000,
        "back_attend",
        [ANY, ANY] + [VMEM] * 4,
        BIG_GRANT,
    )(gb, half, first, spans, gsmall, weights[1], weights[0], gr1, h, qkv, probs, mixed)


TAIL = 16
BLOCK = 96


def add_rows(target, sources, at, rows):
    for start in range(0, rows, BLOCK):
        size = min(BLOCK, rows - start)
        place = pl.ds(at + start, size)
        if not isinstance(at, int):
            place = pl.ds(pl.multiple_of(at + start, 16), size)
        if len(sources) == 2:
            target[start : start + size, :] = sources[0][place, :] + sources[1][place, :]
            continue
        total = sources[0][place, :].astype(F32)
        for source in sources[1:]:
            total = total + source[place, :].astype(F32)
        target[start : start + size, :] = total.astype(LOW)


LONG = 30000000000


def ordered(
    name, body, ins, outs, where, after, out_specs=None, scratch=(), in_specs=None, grant=16, aliases=None,
    flops=LONG,
):
    count, made = len(ins), len(outs)

    def kernel(where, after, *refs):
        refs[count + made][...] = jnp.zeros(TOKEN.shape, F32)
        body(where, refs[:count], refs[count : count + made] + refs[count + made + 1 :])

    result = pl.pallas_call(
        kernel,
        in_specs=[SMEM, ANY] + (in_specs or [VMEM] * count),
        out_specs=(out_specs or [VMEM] * made) + [VMEM],
        out_shape=list(outs) + [TOKEN],
        scratch_shapes=list(scratch),
        input_output_aliases=aliases or {},
        compiler_params=pltpu.CompilerParams(vmem_limit_bytes=grant * MIB),
        cost_estimate=pl.CostEstimate(flops=flops, bytes_accessed=flops, transcendentals=0),
        name=name,
    )(where, after, *ins)
    return result[:made], result[made]


def partner(x, axis, bit):
    return lax.ppermute(x, axis, [(i, i ^ 1 << bit) for i in range(lax.axis_size(axis))])


def moved_on(index, axis, steps):
    z, x, y = index // 8, index // 2 % 4, index % 2
    if axis == "z":
        z = steps(z)
    elif axis == "x":
        x = steps(x)
    else:
        y = steps(y)
    return z * 8 + x * 2 + y


def send_along(value, axes, place):
    pairs = []
    for section in range(4):
        for index in range(32):
            to = moved_on(index, axes[section % 2], place)
            pairs.append((section * 32 + index, section * 32 + to))
    return lax.ppermute(value, ("section", "dp"), pairs)


def exchange(value, part, step):
    flip = 1 if part == step else 3
    return send_along(value, "zx", lambda place: place ^ flip)


def turn(value, steps):
    return send_along(value, "xz", lambda place: (place + steps) % 4)


def across_y(value):
    return send_along(value, "yy", lambda place: place ^ 1)


def swap_core_one(value):
    pairs = [
        (section * 32 + index, section * 32 + (index ^ 1)) for section in (1, 3) for index in range(32)
    ]
    return lax.ppermute(value, ("section", "dp"), pairs)


def between_layers(value, back):
    pairs = []
    for core in range(2):
        for index in range(32):
            pair = (core * 32 + index, (core + 2) * 32 + (index ^ core))
            pairs.append(pair[::-1] if back else pair)
    return lax.ppermute(value, ("section", "dp"), pairs)


def own_places(core):
    index = lax.axis_index("dp")
    z, x = index // 8, index // 2 % 4
    ring = jnp.where(core == 0, z, x)
    high = ring // 2
    low = high ^ (ring % 2)
    table = [low, high, high, low, jnp.where(core == 0, x, z)]
    return jnp.stack(table).astype(jnp.int32)


def row_shapes(*counts):
    return [shape((count, WIDTH)) for count in counts]


def add_tail(target, rows, sources, at, extra):
    if extra:
        total = sources[0][at : at + extra, :].astype(F32)
        for source in sources[1:]:
            total = total + source[at : at + extra, :].astype(F32)
        target[rows : rows + extra, :] = total.astype(LOW)


class Chain:
    def __init__(self, name, places, tail=0):
        self.name = name
        self.places = places
        self.tail = (0, tail)
        self.keep = [None, None]
        self.got = [None, None]

    def kernel(self, name, body, ins, outs, token, *more, **named):
        return ordered(self.name + name, body, ins, outs, self.places, token, *more, **named)

    def pairs(self):
        return (self.keep[0], self.got[0], self.keep[1], self.got[1])

    def start(self, sources, rows, token, tail_ins=(), tail_body=None):
        self.rows = rows // 2
        half_rows, tails = self.rows, self.tail
        arrays = []
        for own, got, _ in sources:
            arrays += [own, got]

        def body(places, ins, outs):
            for part in range(2):
                bit, at = places[2 * part], sources[part][2]
                pair = ins[2 * part : 2 * part + 2]
                for target, which in ((outs[2 * part + 1], 1 - bit), (outs[2 * part], bit)):
                    add_rows(target, pair, at + which * half_rows, half_rows)
                    if tails[part]:
                        target[half_rows:, :] = tail_body(ins[4:])

        counts = [half_rows + tails[0]] * 2 + [half_rows + tails[1]] * 2
        outs, token = self.kernel(
            "start", body, tuple(arrays) + tuple(tail_ins), row_shapes(*counts), token
        )
        for part in range(2):
            self.keep[part] = outs[2 * part]
            self.got[part] = exchange(outs[2 * part + 1], part, 0)
        return token

    def start_copied(self, sources, rows, token, tail_ins=(), tail_body=None):
        self.rows = rows // 2
        half_rows, tails = self.rows, self.tail
        arrays = []
        for own, got, _ in sources:
            arrays += [own, got]
        sizes = [pltpu.VMEM((rows, WIDTH), LOW)] * 4

        def body(places, ins, refs):
            outs, held, sems = refs[:4], refs[4:8], refs[8]
            copies = []
            for index in range(4):
                at = sources[index // 2][2]
                copy = pltpu.make_async_copy(
                    ins[index].at[pl.ds(at, rows)], held[index], sems.at[index]
                )
                copy.start()
                copies.append(copy)
            for part in range(2):
                bit = places[2 * part]
                pair = held[2 * part : 2 * part + 2]
                copies[2 * part].wait()
                copies[2 * part + 1].wait()
                for target, which in ((outs[2 * part + 1], 1 - bit), (outs[2 * part], bit)):
                    add_rows(target, pair, which * half_rows, half_rows)
                    if tails[part]:
                        target[half_rows:, :] = tail_body(ins[4:])

        counts = [half_rows + tails[0]] * 2 + [half_rows + tails[1]] * 2
        outs, token = self.kernel(
            "start",
            body,
            tuple(arrays) + tuple(tail_ins),
            row_shapes(*counts),
            token,
            scratch=(*sizes, pltpu.SemaphoreType.DMA((4,))),
            in_specs=[ANY] * 4 + [VMEM] * len(tail_ins),
            grant=63,
        )
        for part in range(2):
            self.keep[part] = outs[2 * part]
            self.got[part] = exchange(outs[2 * part + 1], part, 0)
        return token

    def halve(self, token):
        self.rows //= 2
        rows, tails = self.rows, self.tail

        def body(places, ins, outs):
            for part in range(2):
                bit = places[2 * part + 1]
                pair = ins[2 * part : 2 * part + 2]
                for target, which in ((outs[2 * part + 1], 1 - bit), (outs[2 * part], bit)):
                    add_rows(target, pair, which * rows, rows)
                    add_tail(target, rows, pair, 2 * rows, tails[part])

        counts = [rows + tails[0]] * 2 + [rows + tails[1]] * 2
        outs, token = self.kernel(
            "halve", body, self.pairs(), row_shapes(*counts), token
        )
        for part in range(2):
            self.keep[part] = outs[2 * part]
            self.got[part] = exchange(outs[2 * part + 1], part, 1)
        return token

    def cross(self, token):
        whole_rows, extra = self.rows, self.tail[1]
        rows = whole_rows // 2

        def body(places, ins, refs):
            outs, total = refs[:4], refs[4]
            add_rows(total.at[pl.ds(0, whole_rows)], ins[:2], 0, whole_rows)
            add_rows(total.at[pl.ds(whole_rows, whole_rows)], ins[2:], 0, whole_rows)
            for steps in range(4):
                quarter = (places[4] + steps) % 4
                outs[steps][:rows, :] = total[pl.ds(pl.multiple_of(quarter * rows, 16), rows), :]
                add_tail(outs[steps], rows, ins[2:], whole_rows, extra)

        (self.own, *sends), token = self.kernel(
            "cross",
            body,
            self.pairs(),
            row_shapes(*[rows + extra] * 4),
            token,
            None,
            (pltpu.VMEM((2 * whole_rows, WIDTH), LOW),),
        )
        self.rows = rows
        self.ring = [turn(send, steps) for steps, send in zip((1, 2, 3), sends)]
        return token

    def across(self, token):
        rows = self.rows + self.tail[1]

        def body(places, ins, outs):
            add_rows(outs[0], ins, 0, rows)

        (self.own,), token = self.kernel(
            "across", body, (self.own, *self.ring), row_shapes(rows), token
        )
        self.other = across_y(self.own)
        return token

    def total(self, token, more_outs=(), more_body=None):
        rows, extra = self.rows, self.tail[1]

        def body(places, ins, outs):
            add_rows(outs[0], ins, 0, rows)
            if extra:
                add_rows(outs[1], ins, rows, extra)
                more_body(outs[1][...].astype(F32), outs[2:])

        counts = [rows] + ([extra] if extra else [])
        outs, token = self.kernel(
            "total", body, (self.own, self.other), row_shapes(*counts) + list(more_outs), token
        )
        self.own = outs[0]
        self.tail_sum = outs[1] if extra else None
        self.ring = [turn(self.own, steps) for steps in (1, 2, 3)]
        return outs[2:], token

    def back(self, token, more_ins=(), more_outs=(), more_body=None):
        rows = self.rows

        def body(places, ins, refs):
            outs, total = refs[:-1], refs[-1]
            for steps in range(4):
                quarter = (places[4] - steps + 4) % 4
                total[pl.ds(pl.multiple_of(quarter * rows, 16), rows), :] = ins[steps][...]
            outs[0][...] = total[: 2 * rows, :]
            outs[1][...] = total[2 * rows :, :]
            if more_body is not None:
                more_body(ins[4:], outs[2:])

        outs, token = self.kernel(
            "back",
            body,
            (self.own, *self.ring) + tuple(more_ins),
            row_shapes(2 * rows, 2 * rows) + list(more_outs),
            token,
            None,
            (pltpu.VMEM((4 * rows, WIDTH), LOW),),
        )
        self.rows = 2 * rows
        self.keep = list(outs[:2])
        self.got = [exchange(self.keep[part], part, 1) for part in range(2)]
        return outs[2:], token

    def double(self, token, flops):
        rows = self.rows

        def body(places, ins, outs):
            for part in range(2):
                bit = places[2 * part + 1]
                for which, source in ((bit, ins[2 * part]), (1 - bit, ins[2 * part + 1])):
                    outs[part][pl.ds(pl.multiple_of(which * rows, 16), rows), :] = source[...]

        outs, token = self.kernel(
            "double", body, self.pairs(), row_shapes(2 * rows, 2 * rows), token, flops=flops
        )
        self.rows = 2 * rows
        self.keep = list(outs)
        self.got = [exchange(self.keep[part], part, 0) for part in range(2)]
        return token

    def finish(self, token, outs, place, got, flops, more_ins=(), more_outs=(), more_body=None):
        rows = self.rows
        mine = tuple(self.got if got else self.keep)
        kept = tuple(outs) if got else ()

        def body(places, ins, refs):
            targets, wide, sems = refs[: len(outs)], refs[-2], refs[-1]
            if more_body is not None:
                more_body(ins[2 + len(kept) :], refs[len(outs) : -2])
            waits = []
            for part in range(2):
                bit = places[2 * part]
                half = 1 - bit if got else bit
                wide[part] = ins[part][...].astype(F32)
                at = 0
                for size, starts in place(targets, part, half):
                    source, sem = wide.at[part, pl.ds(at, size)], sems.at[len(waits)]
                    starts(source, sem)
                    waits.append((size, source, sem))
                    at += size
            for size, source, sem in waits:
                pltpu.make_async_copy(source, wide.at[0, pl.ds(0, size)], sem).wait()

        return self.kernel(
            "finish",
            body,
            mine + kept + tuple(more_ins),
            [shape(out.shape, F32) for out in outs] + list(more_outs),
            token,
            out_specs=[ANY] * len(outs) + [VMEM] * len(more_outs),
            scratch=(pltpu.VMEM((2, rows, WIDTH), F32), pltpu.SemaphoreType.DMA((4,))),
            in_specs=[VMEM] * 2 + [ANY] * len(kept) + [VMEM] * len(more_ins),
            grant=24,
            flops=flops,
            aliases={4 + index: index for index in range(len(kept))},
        )


def copy_to(target):
    return lambda source, sem: pltpu.make_async_copy(source, target, sem).start()


def block_columns(block):
    return pl.ds(pl.multiple_of(block * WIDTH, 128), WIDTH)


def place_x(refs, part, half):
    down, up = refs
    if part == 0:
        return [(768, copy_to(down.at[pl.ds(pl.multiple_of(half * 768, 8), 768)]))]
    return [(384, copy_to(up.at[:, block_columns(2 * half + block)])) for block in range(2)]


def place_y(refs, part, half):
    qkv, out = refs
    if part == 0:
        return [(384, copy_to(qkv.at[:, block_columns(half)]))]

    def starts(source, sem):
        @pl.when(half == 0)
        def _():
            copy_to(qkv.at[:, block_columns(2)])(source, sem)

        @pl.when(half == 1)
        def _():
            copy_to(out)(source, sem)

    return [(384, starts)]


def pack_vectors(vectors):
    size = sum(vector.shape[0] for vector in vectors)
    total = jnp.zeros((size,), F32)
    at = 0
    for vector in vectors:
        total = total + jnp.pad(vector.astype(F32), (at, size - at - vector.shape[0]))
        at += vector.shape[0]
    return total.reshape(1, size)


def per_device(
    inputs,
    cotangent,
    lengths,
    cdr_spans,
    mask_vector,
    w_qkv,
    qv_bias,
    w_out,
    b_out,
    norm1_gain,
    norm1_bias,
    w_up,
    b_up,
    w_down,
    b_down,
    norm2_gain,
    norm2_bias,
):
    section_index = lax.axis_index("section")
    core = section_index % 2
    half = core.astype(jnp.int32).reshape(1)
    first = (section_index < 2).astype(jnp.int32).reshape(1)
    places = own_places(core)
    small = pack_vectors(
        (
            qv_bias,
            b_out,
            norm1_gain,
            norm1_bias,
            b_up,
            b_down,
            norm2_gain,
            norm2_bias,
            mask_vector,
        )
    )
    small_got = partner(small, "section", 0)
    got_qkv, got_out = partner((w_qkv, w_out), "section", 0)
    w_up, w_down, got_qkv, got_out, small_got = lax.optimization_barrier(
        (w_up, w_down, got_qkv, got_out, small_got)
    )
    smalls = (small, small_got)
    got_up, got_down = partner((w_up, w_down), "section", 0)
    weights = [(w_qkv, got_qkv), (w_out, got_out), (w_up, got_up), (w_down, got_down)]

    swapped = swap_core_one(cotangent)
    lens_got = swap_core_one(lengths)
    swaps = (core == 1) & (section_index >= 2)
    layer_lens = jnp.where(swaps, lens_got, lengths)

    u, h0 = attend_first(inputs, half, lengths, cdr_spans, weights, smalls)
    first_out = feed_first(u, half, weights, smalls)
    first_out, weights = lax.optimization_barrier((first_out, weights))
    received = between_layers(first_out, False)
    matrices = assemble(half, weights)
    kept = middle(h0, received, cotangent, swapped, half, first, layer_lens, matrices, smalls)
    h, qkv, probs, mixed, normal1, inverse1, u, slope, active, normal2, inverse2, output = kept[:12]
    returned = between_layers(kept[13], True)

    a_other, a_own, b_other, b_own, gr1, gb, gsmall, token = back_feed(
        cotangent,
        swapped,
        returned,
        half,
        first,
        matrices,
        smalls,
        (u, slope, active, normal1, inverse1, normal2, inverse2),
    )
    a_got = partner(a_other, "section", 0)
    b_got = partner(b_other, "section", 0)
    x, y = Chain("x_", places), Chain("y_", places, TAIL)
    y_other, y_own, small_other, small_own, gh, token = back_attend(
        gb, gr1, half, first, cdr_spans, matrices, gsmall, h, qkv, probs, mixed
    )
    y_got = partner(y_other, "section", 0)
    small_got = partner(small_other, "section", 0)
    token = x.start_copied([(a_own, a_got, 0), (b_own, b_got, 0)], 1536, token)

    def tail_rows(ins):
        total = ins[0][...] + ins[1][...]
        rows = [total[:, at : at + WIDTH] for at in range(0, SMALL + WIDTH, WIDTH)]
        rows.append(jnp.zeros((TAIL - len(rows), WIDTH), F32))
        return jnp.concatenate(rows, axis=0).astype(LOW)

    token = y.start(
        [(y_own, y_got, 0), (y_own, y_got, 768)], 768, token, (small_own, small_got), tail_rows
    )
    both, token = lax.optimization_barrier((kept[12], token))
    both_got = swap_core_one(both)
    token = x.halve(token)
    token = y.halve(token)
    token = x.cross(token)
    token = y.cross(token)
    token = x.across(token)
    token = y.across(token)
    _, token = x.total(token)

    def small_outputs(tail, outs):
        flat = jnp.concatenate([tail[row : row + 1, :] for row in range(6)], axis=1)
        at = 0
        for out, size in zip(outs, SIZES):
            out[...] = flat[0, at : at + size]
            at += size

    out_small, token = y.total(token, [shape((size,), F32) for size in SIZES], small_outputs)
    _, token = x.back(token)

    def mask_output(ins, outs):
        outs[0][...] = ins[0][6, :].astype(F32) + ins[1][6, :].astype(F32)

    _, token = y.back(token)
    gradients_x = [shape((1536, WIDTH), F32), shape((384, HIDDEN), F32)]
    gradients_y = [shape((384, 3 * WIDTH), F32), shape((384, WIDTH), F32)]
    token = x.double(token, LONG)
    gradients_x, token = x.finish(token, gradients_x, place_x, False, LONG)
    token = y.double(token, 0)
    tail_sum, token = lax.optimization_barrier((y.tail_sum, token))
    mask_got = partner(tail_sum, "section", 1)
    gradients_y, token = y.finish(token, gradients_y, place_y, False, 0)
    both_got, token = lax.optimization_barrier((both_got, token))
    (g_down, g_up), token = x.finish(token, gradients_x, place_x, True, LONG)
    (g_qkv, g_out, mask_grad), token = y.finish(
        token,
        gradients_y,
        place_y,
        True,
        LONG,
        (tail_sum, mask_got),
        [shape((WIDTH,), F32)],
        mask_output,
    )
    output = jnp.where(swaps, both_got[0], output)
    gh = jnp.where(swaps, both_got[1], gh)

    g_qv, g_bo, g_n1g, g_n1b, g_bu, g_bd, g_n2g, g_n2b = out_small
    return (
        output.reshape(1, 2, LENGTH, WIDTH),
        gh.reshape(1, 2, LENGTH, WIDTH),
        mask_grad,
        g_qkv,
        g_qv,
        g_out,
        g_bo,
        g_n1g,
        g_n1b,
        g_up,
        g_bu,
        g_down,
        g_bd,
        g_n2g,
        g_n2b,
    )


def solution(mesh):
    in_specs = (
        P(None, "dp", None, None),
        P(None, "dp", None, None),
        P(None, "dp"),
        P(None, "dp", None),
        P(),
        P("section", None),
        P("section"),
        P("section", None),
        P("section"),
        P("section"),
        P("section"),
        P("section", None),
        P("section"),
        P("section", None),
        P("section"),
        P("section"),
        P("section"),
    )
    out_specs = (
        P("section", "dp", None, None),
        P("section", "dp", None, None),
        P(),
        P("section", None),
        P("section"),
        P("section", None),
        P("section"),
        P("section"),
        P("section"),
        P("section", None),
        P("section"),
        P("section", None),
        P("section"),
        P("section"),
        P("section"),
    )
    return jax.shard_map(
        per_device, mesh=mesh, in_specs=in_specs, out_specs=out_specs, check_vma=False
    )
```

```python
import functools
import math

import jax
import jax.numpy as jnp
from jax import lax
from jax.experimental import pallas as pl
from jax.experimental.pallas import tpu as pltpu
from jax.sharding import PartitionSpec as P

EPSILON = 1e-05
F32 = jnp.float32
LOW = jnp.bfloat16
WIDTH = 768
LENGTH = 160
ROWS = 320
HIDDEN = 3072
PAIRS = 6
SCALE = 0.125
SIZES = (768, 384, 384, 384, 1536, 384, 384, 384)
QV, B_OUT, N1G, N1B, B_UP, B_DOWN, N2G, N2B = (sum(SIZES[:at]) for at in range(8))
SMALL = sum(SIZES)
VMEM_LIMIT = 63 * 1024 * 1024
BIG_GRANT = 61 * 1024 * 1024


def dot_nn(left_side, right_side):
    return jnp.dot(left_side, right_side, preferred_element_type=F32)


def dot_nt(left_side, right_side):
    return lax.dot_general(
        left_side, right_side, (((1,), (1,)), ((), ())), preferred_element_type=F32
    )


def dot_tn(left_side, right_side):
    return lax.dot_general(
        left_side, right_side, (((0,), (0,)), ((), ())), preferred_element_type=F32
    )


class Weight:
    def __init__(self, half, own, other, dest, sems, start=True, chunks=1):
        rows, wide = own.shape
        self.dest = dest
        self.wide = wide // chunks
        self.copies = []
        for chunk in range(chunks):
            at = pl.ds(chunk * self.wide, self.wide)
            for side, source in enumerate((own, other)):
                which = half if side == 0 else 1 - half
                place = dest.at[pl.ds(which * rows, rows)]
                if chunks > 1:
                    source, place = source.at[:, at], place.at[:, at]
                self.copies.append(
                    pltpu.make_async_copy(source, place, sems.at[2 * chunk + side])
                )
        if start:
            self.start()

    def start(self):
        for copy in self.copies:
            copy.start()

    def get(self):
        for copy in self.copies:
            copy.wait()
        self.copies = []
        return self.dest[...]

    def chunk(self, index):
        for copy in self.copies[:2]:
            copy.wait()
        self.copies = self.copies[2:]
        return self.dest[:, index * self.wide : (index + 1) * self.wide]


def whole(smalls, at, size):
    return jnp.concatenate([smalls[0:1, at : at + size], smalls[1:2, at : at + size]], axis=1)


def split_heads(tensor):
    lane = lax.broadcasted_iota(jnp.int32, tensor.shape, 1)
    zero = jnp.zeros_like(tensor)
    return jnp.concatenate(
        [jnp.where(lane < 64, tensor, zero), jnp.where(lane < 64, zero, tensor)], axis=0
    )


def join_heads(tensor):
    lane = lax.broadcasted_iota(jnp.int32, (LENGTH, 128), 1)
    return jnp.where(lane < 64, tensor[:LENGTH], tensor[LENGTH:])


def normalize(values):
    center = values - jnp.mean(values, axis=-1, keepdims=True)
    spread = jnp.mean(center * center, axis=-1, keepdims=True)
    inverse = lax.rsqrt(spread + EPSILON)
    return center * inverse, inverse


def normalize_back(upstream, gain, normal, inverse):
    scaled = upstream * gain
    first = jnp.mean(scaled, axis=-1, keepdims=True)
    second = jnp.mean(scaled * normal, axis=-1, keepdims=True)
    return inverse * (scaled - first - normal * second)


def gelu_parts(values):
    size = jnp.abs(values)
    below = 1.0 + (0.3275911 * math.sqrt(0.5)) * size
    t = pl.reciprocal(below, approx=True)
    t = t * (2.0 - below * t)
    series = t * (
        0.5 * 0.254829592
        + t
        * (
            0.5 * -0.284496736
            + t * (0.5 * 1.421413741 + t * (0.5 * -1.453152027 + t * (0.5 * 1.061405429)))
        )
    )
    bell = jnp.exp(-0.5 * values * values)
    tail = series * bell
    share = jnp.where(values >= 0.0, 1.0 - tail, tail)
    return values * share, share + values * bell * (1.0 / math.sqrt(2.0 * math.pi))


def column_sum(values):
    return jnp.sum(values, axis=0, keepdims=True)


def put_halves(target, at, row):
    size = row.shape[1] // 2
    target[0:1, at : at + size] = row[:, :size]
    target[1:2, at : at + size] = row[:, size:]


def places():
    for index in range(2 * PAIRS):
        chain, pair = divmod(index, PAIRS)
        rows = pl.ds(chain * LENGTH, LENGTH)
        yield index, chain, rows, [pl.ds((pair + block * PAIRS) * 128, 128) for block in range(3)]


def attend_body(h, wqkv, wout, smalls, lens, half, qkv, probs, mixed, normal1, inverse1, u, later):
    x = h[...]
    bias = jnp.concatenate(
        [smalls[0:1, :WIDTH], jnp.zeros((1, WIDTH), F32), smalls[1:2, :WIDTH]], axis=1
    )
    for block in range(3):
        at = block * WIDTH
        matrix = wqkv.chunk(block)
        if block == 0:
            for each in later:
                each.start()
        qkv[:, at : at + WIDTH] = (dot_nn(x, matrix) + bias[:, at : at + WIDTH]).astype(LOW)
    for index, chain, rows, (at_q, at_k, at_v) in places():
        scores = dot_nt(qkv[rows, at_k], split_heads(qkv[rows, at_q])) * SCALE
        key = lax.broadcasted_iota(jnp.int32, scores.shape, 0)
        scores = jnp.where(key < lens[half[0], chain], scores, -1000000000.0)
        grown = jnp.exp(scores - jnp.max(scores, axis=0, keepdims=True))
        weights = (grown * (1.0 / jnp.sum(grown, axis=0, keepdims=True))).astype(LOW)
        if probs is not None:
            probs[index] = weights
        mixed[rows, at_q] = join_heads(dot_tn(weights, qkv[rows, at_v])).astype(LOW)
    branch = dot_nn(mixed[...], wout.get()) + whole(smalls, B_OUT, 384)
    normal, inverse = normalize(x.astype(F32) + branch)
    if normal1 is not None:
        normal1[...] = normal
        inverse1[...] = inverse
    u[...] = (normal * whole(smalls, N1G, 384) + whole(smalls, N1B, 384)).astype(LOW)


CHUNK = 1024


def feed_body(u, wup, wdown, smalls, slope, active, normal2, inverse2, y, later=()):
    x = u[...]
    bias = whole(smalls, B_UP, 1536)
    def grow(part, at):
        grown, tangent = gelu_parts(part + bias[:, at : at + CHUNK])
        active[:, at : at + CHUNK] = grown.astype(LOW)
        if slope is not None:
            slope[:, at : at + CHUNK] = tangent.astype(LOW)

    up = wup.chunk(0)
    for each in later:
        each.start()
    grow(dot_nn(x, up), 0)
    up, last = wup.chunk(1), wup.chunk(2)
    grow(dot_nn(x, up), CHUNK)
    part = dot_nn(x, last)
    down = wdown.get()
    grow(part, 2 * CHUNK)
    total = x.astype(F32) + whole(smalls, B_DOWN, 384) + dot_nn(active[...], down)
    normal, inverse = normalize(total)
    if normal2 is not None:
        normal2[...] = normal
        inverse2[...] = inverse
    y[...] = (normal * whole(smalls, N2G, 384) + whole(smalls, N2B, 384)).astype(LOW)


def top_back_body(up, smalls, normal2, inverse2, gr2, gz, gsmall):
    normal = normal2[...]
    put_halves(gsmall, N2G, column_sum(up * normal))
    put_halves(gsmall, N2B, column_sum(up))
    grad = normalize_back(up, whole(smalls, N2G, 384), normal, inverse2[...])
    z = grad.astype(LOW)
    gz[...] = z
    put_halves(gsmall, B_DOWN, column_sum(z.astype(F32)))
    gr2[...] = grad


def feed_back_body(gr2, gz, wup, wdown, smalls, slope, normal1, inverse1, ga, gr1, gb, gsmall):
    z = gz[...]
    down = wdown.get()
    sums = []
    for at in range(0, HIDDEN, CHUNK):
        inner = dot_nt(z, down[at : at + CHUNK, :]) * slope[:, at : at + CHUNK].astype(F32)
        a = inner.astype(LOW)
        ga[:, at : at + CHUNK] = a
        sums.append(column_sum(a.astype(F32)))
    put_halves(gsmall, B_UP, jnp.concatenate(sums, axis=1))
    up = gr2[...] + dot_nt(ga[...], wup.get())
    normal = normal1[...]
    put_halves(gsmall, N1G, column_sum(up * normal))
    put_halves(gsmall, N1B, column_sum(up))
    grad = normalize_back(up, whole(smalls, N1G, 384), normal, inverse1[...])
    gr1[...] = grad
    b = grad.astype(LOW)
    gb[...] = b
    put_halves(gsmall, B_OUT, column_sum(b.astype(F32)))


def heads_back_body(gb, wout, qkv, probs, gqkv, gqv, go):
    go[...] = dot_nt(gb[...], wout.get()).astype(LOW)
    for index, chain, rows, (at_q, at_k, at_v) in places():
        k = qkv[rows, at_k]
        g = split_heads(go[rows, at_q])
        weights = probs[index]
        wide = weights.astype(F32)
        inner = dot_nt(qkv[rows, at_v], g)
        inner = wide * (inner - jnp.sum(wide * inner, axis=0, keepdims=True))
        s = inner.astype(LOW)
        gqkv[rows, at_q] = (join_heads(dot_tn(s, k)) * SCALE).astype(LOW)
        gqkv[rows, at_k] = (dot_nn(s, split_heads(qkv[rows, at_q])) * SCALE).astype(LOW)
        gqkv[rows, at_v] = dot_nn(weights, g).astype(LOW)
    if gqv is not None:
        gqv[0:1, :] = column_sum(gqkv[:, :WIDTH].astype(F32))
        gqv[1:2, :] = column_sum(gqkv[:, 2 * WIDTH :].astype(F32))


def span_rows(spans, half):
    row = lax.broadcasted_iota(jnp.int32, (ROWS, 1), 0)
    inside = row < 0
    for chain in range(2):
        start = spans[half[0], chain, 0] + chain * LENGTH
        end = spans[half[0], chain, 1] + chain * LENGTH
        inside = inside | ((row >= start) & (row < end))
    return inside


def pick_halves(half, own, other, smalls):
    low = half[0] == 0
    smalls[0:1, :] = jnp.where(low, own[:, :SMALL], other[:, :SMALL])
    smalls[1:2, :] = jnp.where(low, other[:, :SMALL], own[:, :SMALL])


VMEM = pl.BlockSpec(memory_space=pltpu.VMEM)
SMEM = pl.BlockSpec(memory_space=pltpu.SMEM)
ANY = pl.BlockSpec(memory_space=pl.ANY)
SMALL_SCRATCH = pltpu.VMEM((2, SMALL), F32)
QKV_SHAPE = (ROWS, 3 * WIDTH)
PROBS_SHAPE = (2 * PAIRS, LENGTH, 2 * LENGTH)
ROW_SHAPE = (ROWS, WIDTH)
FEED_SHAPE = (ROWS, HIDDEN)
MACS = ROWS * WIDTH * WIDTH * 2
ATTEND_WEIGHTS = [pltpu.VMEM((WIDTH, 3 * WIDTH), LOW), pltpu.VMEM((WIDTH, WIDTH), LOW)]
FEED_WEIGHTS = [pltpu.VMEM((WIDTH, HIDDEN), LOW), pltpu.VMEM((HIDDEN, WIDTH), LOW)]


def shape(dims, kind=LOW):
    return jax.ShapeDtypeStruct(dims, kind)


def enter_cotangent(half, own, swapped, raw, sem):
    @pl.when(half[0] == 0)
    def _():
        pltpu.make_async_copy(own.at[0], raw, sem).start()

    @pl.when(half[0] == 1)
    def _():
        pltpu.make_async_copy(swapped.at[1], raw, sem).start()

    return pltpu.make_async_copy(swapped.at[1], raw, sem)


def kernel_call(body, ins, outs, scratch, flops, moved, name, out_specs=None, grant=VMEM_LIMIT):
    return pl.pallas_call(
        body,
        in_specs=ins,
        out_specs=out_specs or [VMEM] * len(outs),
        out_shape=outs,
        scratch_shapes=scratch,
        compiler_params=pltpu.CompilerParams(vmem_limit_bytes=grant),
        cost_estimate=pl.CostEstimate(flops=flops, bytes_accessed=moved, transcendentals=0),
        name=name,
    )


def attend_first(inputs, half, lens, spans, weights, smalls):
    def body(x, half, lens, spans, so, sp, qo, qp, oo, op, u, h, raw, small, qkv, mixed, wq, wo, sems):
        enter = pltpu.make_async_copy(x.at[half[0]], raw, sems.at[2, 0])
        enter.start()
        wqkv = Weight(half[0], qo, qp, wq, sems.at[0], True, 3)
        wout = Weight(half[0], oo, op, wo, sems.at[1], False)
        pick_halves(half, so, sp, small)
        enter.wait()
        mask = so[:, SMALL:].astype(LOW)
        h[...] = jnp.where(span_rows(spans, half), mask, raw[...].reshape(ROWS, WIDTH))
        attend_body(h, wqkv, wout, small, lens, half, qkv, None, mixed, None, None, u, [wout])

    return kernel_call(
        body,
        [ANY, SMEM, SMEM, SMEM, VMEM, VMEM] + [ANY] * 4,
        [shape(ROW_SHAPE), shape(ROW_SHAPE)],
        [
            pltpu.VMEM((2, LENGTH, WIDTH), LOW),
            SMALL_SCRATCH,
            pltpu.VMEM(QKV_SHAPE, LOW),
            pltpu.VMEM(ROW_SHAPE, LOW),
            *ATTEND_WEIGHTS,
            pltpu.SemaphoreType.DMA((3, 6)),
        ],
        40 * MACS,
        80000000,
        "attend_first",
    )(inputs, half, lens, spans, *smalls, *weights[0], *weights[1])


def feed_first(u, half, weights, smalls):
    def body(u, half, so, sp, uo, up, do, dp, y, small, active, wu, wd, sems):
        wup = Weight(half[0], uo, up, wu, sems.at[0], True, 3)
        wdown = Weight(half[0], do, dp, wd, sems.at[1], False)
        pick_halves(half, so, sp, small)
        feed_body(u, wup, wdown, small, None, active, None, None, y, [wdown])

    return kernel_call(
        body,
        [VMEM, SMEM, VMEM, VMEM] + [ANY] * 4,
        [shape(ROW_SHAPE)],
        [
            SMALL_SCRATCH,
            pltpu.VMEM(FEED_SHAPE, LOW),
            *FEED_WEIGHTS,
            pltpu.SemaphoreType.DMA((2, 6)),
        ],
        8 * MACS,
        14000000,
        "feed_first",
    )(u, half, *smalls, *weights[2], *weights[3])[0]


KEPT = [
    shape(ROW_SHAPE),
    shape(QKV_SHAPE),
    shape(PROBS_SHAPE),
    shape(ROW_SHAPE),
    shape(ROW_SHAPE, F32),
    shape((ROWS, 1), F32),
    shape(ROW_SHAPE),
    shape(FEED_SHAPE),
    shape(FEED_SHAPE),
    shape(ROW_SHAPE, F32),
    shape((ROWS, 1), F32),
    shape(ROW_SHAPE),
]


def middle(h0, received, cotangent, swapped, half, first, lens, weights, smalls):
    def body(h0, received, cot, swap, half, first, lens, so, sp, qo, qp, oo, op, uo, up, do, dp, *rest):
        outs, rest = rest[: len(KEPT)], rest[len(KEPT) :]
        both, rest = rest[0], rest[1:]
        gh, small, gr2, gz, ga, gr1, gb, gsmall, gqkv, go, raw, wq, wo, wu, wd = rest[:15]
        keeps, sems, out_sems, raw_sem = rest[15:-3], *rest[-3:]
        h, qkv, probs, mixed, normal1, inverse1, u, slope, active, normal2, inverse2, y = keeps
        wqkv = Weight(half[0], qo, qp, wq, sems.at[0], True, 3)
        wout = Weight(half[0], oo, op, wo, sems.at[1])
        wup = Weight(half[0], uo, up, wu, sems.at[2], True, 3)
        wdown = Weight(half[0], do, dp, wd, sems.at[3])
        enter = enter_cotangent(half, cot, swap, raw, raw_sem)
        pick_halves(half, so, sp, small)
        leaving = []

        def leave(places):
            for place in places:
                copy = pltpu.make_async_copy(keeps[place], outs[place], out_sems.at[place])
                copy.start()
                leaving.append(copy)

        h[...] = jnp.where(first[0] > 0, h0[...], received[...])
        attend_body(
            h, wqkv, wout, small, lens, half, qkv, probs, mixed, normal1, inverse1, u, ()
        )
        leave(range(7))
        feed_body(u, wup, wdown, small, slope, active, normal2, inverse2, y)
        leave(range(7, 12))
        output = pltpu.make_async_copy(y, both.at[0], out_sems.at[len(KEPT)])
        output.start()
        leaving.append(output)
        enter.wait()
        upstream = raw[...].reshape(ROWS, WIDTH).astype(F32)
        top_back_body(upstream, small, normal2, inverse2, gr2, gz, gsmall)
        feed_back_body(gr2, gz, wup, wdown, small, slope, normal1, inverse1, ga, gr1, gb, gsmall)
        heads_back_body(gb, wout, qkv, probs, gqkv, None, go)
        gh[...] = (gr1[...] + dot_nt(gqkv[...], wqkv.get())).astype(LOW)
        output = pltpu.make_async_copy(gh, both.at[1], out_sems.at[len(KEPT) + 1])
        output.start()
        leaving.append(output)
        for copy in leaving:
            copy.wait()

    return kernel_call(
        body,
        [VMEM, VMEM, ANY, ANY, SMEM, SMEM, SMEM, VMEM, VMEM] + [ANY] * 8,
        KEPT + [shape((2, ROWS, WIDTH)), shape(ROW_SHAPE)],
        [
            SMALL_SCRATCH,
            pltpu.VMEM(ROW_SHAPE, F32),
            pltpu.VMEM(ROW_SHAPE, LOW),
            pltpu.VMEM(FEED_SHAPE, LOW),
            pltpu.VMEM(ROW_SHAPE, F32),
            pltpu.VMEM(ROW_SHAPE, LOW),
            SMALL_SCRATCH,
            pltpu.VMEM(QKV_SHAPE, LOW),
            pltpu.VMEM(ROW_SHAPE, LOW),
            pltpu.VMEM((2, LENGTH, WIDTH), LOW),
            *ATTEND_WEIGHTS,
            *FEED_WEIGHTS,
            *[pltpu.VMEM(kept.shape, kept.dtype) for kept in KEPT],
            pltpu.SemaphoreType.DMA((4, 6)),
            pltpu.SemaphoreType.DMA((len(KEPT) + 2,)),
            pltpu.SemaphoreType.DMA,
        ],
        24 * MACS,
        45000000,
        "middle",
        [ANY] * len(KEPT) + [ANY, VMEM],
        BIG_GRANT,
    )(
        h0, received, cotangent, swapped, half, first, lens, *smalls,
        *weights[0], *weights[1], *weights[2], *weights[3],
    )


MIB = 1024 * 1024


def half_columns(ref, which):
    size = ref.shape[1] // 2
    return ref[:, pl.ds(pl.multiple_of(which * size, 128), size)]


class Arriving:
    def __init__(self, pairs, sems):
        self.copies = {}
        for place, (name, source, dest) in enumerate(pairs):
            copy = pltpu.make_async_copy(source, dest, sems.at[place])
            copy.start()
            self.copies[name] = (copy, dest)

    def get(self, name):
        copy, dest = self.copies[name]
        copy.wait()
        return dest


class Leaving:
    def __init__(self, sems):
        self.sems = sems
        self.copies = []

    def send(self, source, target):
        copy = pltpu.make_async_copy(source, target, self.sems.at[len(self.copies)])
        copy.start()
        self.copies.append(copy)

    def wait(self):
        for copy in self.copies:
            copy.wait()


def send_folded(leaving, local, target, left_side, right):
    for block in range(right.shape[1] // WIDTH):
        rows = pl.ds(block * 384, 384)
        grad = dot_tn(left_side, right[:, block * WIDTH : (block + 1) * WIDTH])
        local[rows, :] = grad.astype(LOW)
        leaving.send(local.at[rows], target.at[rows])


TOKEN = shape((8, 128), F32)
GRAD_SHAPE = (1536, WIDTH)
GRAD_SCRATCH = pltpu.VMEM(GRAD_SHAPE, LOW)


def back_feed(cotangent, swapped, returned, half, first, weights, smalls, kept):
    u, slope, active, n1, i1, n2, i2 = kept

    def body(cot, swap, returned, half, first, so, sp, i1, n2, i2, uo, up, do, dp, u, slope, active, n1, *rest):
        outs, rest = rest[:8], rest[8:]
        down_other, down_own, up_other, up_own, gr1, gb, gsmall, token = outs
        gr2, gz, ga, v0, v1, v2, v3, small, raw, wu, wd, vu, vs, va, vn, sems, in_sems, out_sems = rest
        enter = enter_cotangent(half, cot, swap, raw, sems.at[2, 0])
        arriving = Arriving([("active", active, va)], in_sems)
        wdown = Weight(half[0], do, dp, wd, sems.at[1])
        later = Arriving(
            [("slope", slope, vs), ("normal", n1, vn), ("u", u, vu)],
            in_sems.at[pl.ds(1, 3)],
        )
        wup = Weight(half[0], uo, up, wu, sems.at[0])
        pick_halves(half, so, sp, small)
        enter.wait()
        upstream = jnp.where(first[0] > 0, returned[...], raw[...].reshape(ROWS, WIDTH))
        top_back_body(upstream.astype(F32), small, n2, i2, gr2, gz, gsmall)
        leaving = Leaving(out_sems)
        arriving.get("active")
        for which, local, target in ((1 - half[0], v0, down_other), (half[0], v1, down_own)):
            local[...] = dot_tn(half_columns(va, which), gz[...]).astype(LOW)
            leaving.send(local, target)
        later.get("slope")
        later.get("normal")
        feed_back_body(gr2, gz, wup, wdown, small, vs, vn, i1, ga, gr1, gb, gsmall)
        later.get("u")
        for which, local, target in ((1 - half[0], v2, up_other), (half[0], v3, up_own)):
            send_folded(leaving, local, target, half_columns(vu, which), ga)
        token[...] = jnp.zeros(token.shape, F32)
        leaving.wait()

    return kernel_call(
        body,
        [ANY, ANY, VMEM, SMEM, SMEM] + [VMEM] * 5 + [ANY] * 8,
        [shape(GRAD_SHAPE)] * 4
        + [shape(ROW_SHAPE, F32), shape(ROW_SHAPE), shape((2, SMALL), F32), TOKEN],
        [
            pltpu.VMEM(ROW_SHAPE, F32),
            pltpu.VMEM(ROW_SHAPE, LOW),
            pltpu.VMEM(FEED_SHAPE, LOW),
            *[GRAD_SCRATCH] * 4,
            SMALL_SCRATCH,
            pltpu.VMEM((2, LENGTH, WIDTH), LOW),
            *FEED_WEIGHTS,
            pltpu.VMEM(ROW_SHAPE, LOW),
            pltpu.VMEM(FEED_SHAPE, LOW),
            pltpu.VMEM(FEED_SHAPE, LOW),
            pltpu.VMEM(ROW_SHAPE, F32),
            pltpu.SemaphoreType.DMA((3, 2)),
            pltpu.SemaphoreType.DMA((4,)),
            pltpu.SemaphoreType.DMA((10,)),
        ],
        200 * MACS,
        600000000,
        "back_feed",
        [ANY] * 4 + [VMEM] * 4,
        BIG_GRANT,
    )(
        cotangent, swapped, returned, half, first, *smalls, i1, n2, i2, *weights[2], *weights[3],
        u, slope, active, n1,
    )


def back_attend(gb, gr1, half, first, spans, weights, gsmall, h, qkv, probs, mixed):
    def body(gb, half, first, spans, gsmall, oo, op, qo, qp, gr1, h, qkv, probs, mixed, *rest):
        outs, rest = rest[:6], rest[6:]
        other, own, small_other, small_own, gh, token = outs
        gqkv, go, gqv, vother, vown, wo, wq, vr, vh, vq, vp, vm, sems, in_sems, out_sems = rest
        wout = Weight(half[0], oo, op, wo, sems.at[0])
        arriving = Arriving([("qkv", qkv, vq), ("probs", probs, vp)], in_sems)
        wqkv = Weight(half[0], qo, qp, wq, sems.at[1], False)
        arriving.get("qkv")
        arriving.get("probs")
        wqkv.start()
        late = Arriving([("h", h, vh), ("mixed", mixed, vm), ("gr1", gr1, vr)], in_sems.at[pl.ds(2, 3)])
        heads_back_body(gb, wout, vq, vp, gqkv, gqv, go)
        leaving = Leaving(out_sems)
        late.get("h")
        late.get("mixed")
        for which, local, target in ((1 - half[0], vother, other), (half[0], vown, own)):
            send_folded(leaving, local, target, half_columns(vh, which), gqkv)
            local[1152:, :] = dot_tn(half_columns(vm, which), gb[...]).astype(LOW)
            leaving.send(local.at[pl.ds(1152, 384)], target.at[pl.ds(1152, 384)])
        late.get("gr1")
        full = vr[...] + dot_nt(gqkv[...], wqkv.get())
        dropped = span_rows(spans, half) & (first[0] > 0)
        zero = jnp.zeros_like(full)
        gh[...] = jnp.where(dropped, zero, full).astype(LOW)
        gmask = column_sum(jnp.where(dropped, full, zero))
        for which, target in ((1 - half[0], small_other), (half[0], small_own)):
            target[:, :WIDTH] = gqv[pl.ds(which, 1), :]
            target[:, WIDTH:SMALL] = gsmall[pl.ds(which, 1), WIDTH:]
            target[:, SMALL:] = gmask
        token[...] = jnp.zeros(token.shape, F32)
        leaving.wait()

    return kernel_call(
        body,
        [VMEM, SMEM, SMEM, SMEM, VMEM] + [ANY] * 9,
        [
            shape(GRAD_SHAPE),
            shape(GRAD_SHAPE),
            shape((1, SMALL + WIDTH), F32),
            shape((1, SMALL + WIDTH), F32),
            shape(ROW_SHAPE),
            TOKEN,
        ],
        [
            pltpu.VMEM(QKV_SHAPE, LOW),
            pltpu.VMEM(ROW_SHAPE, LOW),
            pltpu.VMEM((2, WIDTH), F32),
            GRAD_SCRATCH,
            GRAD_SCRATCH,
            ATTEND_WEIGHTS[1],
            ATTEND_WEIGHTS[0],
            pltpu.VMEM(ROW_SHAPE, F32),
            pltpu.VMEM(ROW_SHAPE, LOW),
            pltpu.VMEM(QKV_SHAPE, LOW),
            pltpu.VMEM(PROBS_SHAPE, LOW),
            pltpu.VMEM(ROW_SHAPE, LOW),
            pltpu.SemaphoreType.DMA((2, 2)),
            pltpu.SemaphoreType.DMA((5,)),
            pltpu.SemaphoreType.DMA((8,)),
        ],
        180 * MACS,
        400000000,
        "back_attend",
        [ANY, ANY] + [VMEM] * 4,
    )(gb, half, first, spans, gsmall, *weights[1], *weights[0], gr1, h, qkv, probs, mixed)


TAIL = 16
BLOCK = 96


def add_rows(target, sources, at, rows):
    for start in range(0, rows, BLOCK):
        size = min(BLOCK, rows - start)
        place = pl.ds(at + start, size)
        if not isinstance(at, int):
            place = pl.ds(pl.multiple_of(at + start, 16), size)
        if len(sources) == 2:
            target[start : start + size, :] = sources[0][place, :] + sources[1][place, :]
            continue
        total = sources[0][place, :].astype(F32)
        for source in sources[1:]:
            total = total + source[place, :].astype(F32)
        target[start : start + size, :] = total.astype(LOW)


LONG = 30000000000


def ordered(
    name, body, ins, outs, where, after, out_specs=None, scratch=(), in_specs=None, grant=16, aliases=None,
    flops=LONG,
):
    count, made = len(ins), len(outs)

    def kernel(where, after, *refs):
        refs[count + made][...] = jnp.zeros(TOKEN.shape, F32)
        body(where, refs[:count], refs[count : count + made] + refs[count + made + 1 :])

    result = pl.pallas_call(
        kernel,
        in_specs=[SMEM, ANY] + (in_specs or [VMEM] * count),
        out_specs=(out_specs or [VMEM] * made) + [VMEM],
        out_shape=list(outs) + [TOKEN],
        scratch_shapes=list(scratch),
        input_output_aliases=aliases or {},
        compiler_params=pltpu.CompilerParams(vmem_limit_bytes=grant * MIB),
        cost_estimate=pl.CostEstimate(flops=flops, bytes_accessed=flops, transcendentals=0),
        name=name,
    )(where, after, *ins)
    return result[:made], result[made]


def partner(x, axis, bit):
    return lax.ppermute(x, axis, [(i, i ^ 1 << bit) for i in range(lax.axis_size(axis))])


def moved_on(index, axis, steps):
    z, x, y = index // 8, index // 2 % 4, index % 2
    if axis == "z":
        z = steps(z)
    elif axis == "x":
        x = steps(x)
    else:
        y = steps(y)
    return z * 8 + x * 2 + y


def send_along(value, axes, place):
    pairs = []
    for section in range(4):
        for index in range(32):
            to = moved_on(index, axes[section % 2], place)
            pairs.append((section * 32 + index, section * 32 + to))
    return lax.ppermute(value, ("section", "dp"), pairs)


def exchange(value, part, step):
    flip = 1 if part == step else 3
    return send_along(value, "zx", lambda place: place ^ flip)


def turn(value, steps):
    return send_along(value, "xz", lambda place: (place + steps) % 4)


def across_y(value):
    return send_along(value, "yy", lambda place: place ^ 1)


def swap_core_one(value):
    pairs = [
        (section * 32 + index, section * 32 + (index ^ 1)) for section in (1, 3) for index in range(32)
    ]
    return lax.ppermute(value, ("section", "dp"), pairs)


def between_layers(value, back):
    pairs = []
    for core in range(2):
        for index in range(32):
            pair = (core * 32 + index, (core + 2) * 32 + (index ^ core))
            pairs.append(pair[::-1] if back else pair)
    return lax.ppermute(value, ("section", "dp"), pairs)


def own_places(core):
    index = lax.axis_index("dp")
    z, x = index // 8, index // 2 % 4
    ring = jnp.where(core == 0, z, x)
    high = ring // 2
    low = high ^ (ring % 2)
    table = [low, high, high, low, jnp.where(core == 0, x, z)]
    return jnp.stack(table).astype(jnp.int32)


def row_shapes(*counts):
    return [shape((count, WIDTH)) for count in counts]


def add_tail(target, rows, sources, at, extra):
    if extra:
        total = sources[0][at : at + extra, :].astype(F32)
        for source in sources[1:]:
            total = total + source[at : at + extra, :].astype(F32)
        target[rows : rows + extra, :] = total.astype(LOW)


class Chain:
    def __init__(self, name, places, tail=0):
        self.name = name
        self.places = places
        self.tail = (0, tail)
        self.keep = [None, None]
        self.got = [None, None]

    def kernel(self, name, body, ins, outs, token, *more, **named):
        return ordered(self.name + name, body, ins, outs, self.places, token, *more, **named)

    def pairs(self):
        return (self.keep[0], self.got[0], self.keep[1], self.got[1])

    def first_sum(self, name, sent, token):
        sources, half_rows, tails = self.sources, self.rows, self.tail

        def body(places, ins, refs):
            outs, held, sems = refs[:2], refs[2:6], refs[6]
            copies = []
            for index in range(4):
                bit, at = places[2 * (index // 2)], sources[index // 2][2]
                which = 1 - bit if sent else bit
                rows = pl.ds(pl.multiple_of(at + which * half_rows, 16), half_rows)
                copy = pltpu.make_async_copy(ins[index].at[rows], held[index], sems.at[index])
                copy.start()
                copies.append(copy)
            for part in range(2):
                copies[2 * part].wait()
                copies[2 * part + 1].wait()
                add_rows(outs[part], held[2 * part : 2 * part + 2], 0, half_rows)
                if tails[part]:
                    outs[part][half_rows:, :] = self.tail_body(ins[4:])

        arrays = [array for own, got, _ in sources for array in (own, got)]
        return self.kernel(
            name,
            body,
            (*arrays, *self.tail_ins),
            row_shapes(half_rows + tails[0], half_rows + tails[1]),
            token,
            scratch=(*[pltpu.VMEM((half_rows, WIDTH), LOW)] * 4, pltpu.SemaphoreType.DMA((4,))),
            in_specs=[ANY] * 4 + [VMEM] * len(self.tail_ins),
            grant=63,
        )

    def start(self, sources, rows, token, tail_ins=(), tail_body=None):
        self.rows, self.sources = rows // 2, sources
        self.tail_ins, self.tail_body = tuple(tail_ins), tail_body
        sends, token = self.first_sum("send", True, token)
        self.got = [exchange(sends[part], part, 0) for part in range(2)]
        return token

    def hold(self, token):
        keeps, token = self.first_sum("keep", False, token)
        self.keep = list(keeps)
        return token

    def halve(self, token):
        self.rows //= 2
        rows, tails = self.rows, self.tail

        def body(places, ins, outs):
            for part in range(2):
                bit = places[2 * part + 1]
                pair = ins[2 * part : 2 * part + 2]
                for target, which in ((outs[2 * part + 1], 1 - bit), (outs[2 * part], bit)):
                    add_rows(target, pair, which * rows, rows)
                    add_tail(target, rows, pair, 2 * rows, tails[part])

        counts = [rows + tails[0]] * 2 + [rows + tails[1]] * 2
        outs, token = self.kernel(
            "halve", body, self.pairs(), row_shapes(*counts), token
        )
        for part in range(2):
            self.keep[part] = outs[2 * part]
            self.got[part] = exchange(outs[2 * part + 1], part, 1)
        return token

    def cross(self, token):
        whole_rows, extra = self.rows, self.tail[1]
        rows = whole_rows // 2

        def body(places, ins, refs):
            outs, total = refs[:4], refs[4]
            add_rows(total.at[pl.ds(0, whole_rows)], ins[:2], 0, whole_rows)
            add_rows(total.at[pl.ds(whole_rows, whole_rows)], ins[2:], 0, whole_rows)
            for steps in range(4):
                quarter = (places[4] + steps) % 4
                outs[steps][:rows, :] = total[pl.ds(pl.multiple_of(quarter * rows, 16), rows), :]
                add_tail(outs[steps], rows, ins[2:], whole_rows, extra)

        (self.own, *sends), token = self.kernel(
            "cross",
            body,
            self.pairs(),
            row_shapes(*[rows + extra] * 4),
            token,
            None,
            (pltpu.VMEM((2 * whole_rows, WIDTH), LOW),),
        )
        self.rows = rows
        self.ring = [turn(send, steps) for steps, send in zip((1, 2, 3), sends)]
        return token

    def across(self, token):
        rows = self.rows + self.tail[1]

        def body(places, ins, outs):
            add_rows(outs[0], ins, 0, rows)

        (self.own,), token = self.kernel(
            "across", body, (self.own, *self.ring), row_shapes(rows), token
        )
        self.other = across_y(self.own)
        return token

    def total(self, token, more_outs=(), more_body=None):
        rows, extra = self.rows, self.tail[1]

        def body(places, ins, outs):
            add_rows(outs[0], ins, 0, rows)
            if extra:
                add_rows(outs[1], ins, rows, extra)
                more_body(outs[1][...].astype(F32), outs[2:])

        counts = [rows] + ([extra] if extra else [])
        outs, token = self.kernel(
            "total", body, (self.own, self.other), row_shapes(*counts) + list(more_outs), token
        )
        self.own = outs[0]
        self.tail_sum = outs[1] if extra else None
        self.ring = [turn(self.own, steps) for steps in (1, 2, 3)]
        return outs[2:], token

    def back(self, token, more_ins=(), more_outs=(), more_body=None):
        rows = self.rows

        def body(places, ins, refs):
            outs, total = refs[:-1], refs[-1]
            for steps in range(4):
                quarter = (places[4] - steps + 4) % 4
                total[pl.ds(pl.multiple_of(quarter * rows, 16), rows), :] = ins[steps][...]
            outs[0][...] = total[: 2 * rows, :]
            outs[1][...] = total[2 * rows :, :]
            if more_body is not None:
                more_body(ins[4:], outs[2:])

        outs, token = self.kernel(
            "back",
            body,
            (self.own, *self.ring) + tuple(more_ins),
            row_shapes(2 * rows, 2 * rows) + list(more_outs),
            token,
            None,
            (pltpu.VMEM((4 * rows, WIDTH), LOW),),
        )
        self.rows = 2 * rows
        self.keep = list(outs[:2])
        self.got = [exchange(self.keep[part], part, 1) for part in range(2)]
        return outs[2:], token

    def double(self, token, flops):
        rows = self.rows

        def body(places, ins, outs):
            for part in range(2):
                bit = places[2 * part + 1]
                for which, source in ((bit, ins[2 * part]), (1 - bit, ins[2 * part + 1])):
                    outs[part][pl.ds(pl.multiple_of(which * rows, 16), rows), :] = source[...]

        outs, token = self.kernel(
            "double", body, self.pairs(), row_shapes(2 * rows, 2 * rows), token, flops=flops
        )
        self.rows = 2 * rows
        self.keep = list(outs)
        self.got = [exchange(self.keep[part], part, 0) for part in range(2)]
        return token

    def finish(self, token, outs, place, got, flops, more_ins=(), more_outs=(), more_body=None):
        rows = self.rows
        mine = tuple(self.got if got else self.keep)
        kept = tuple(outs) if got else ()

        def body(places, ins, refs):
            targets, wide, sems = refs[: len(outs)], refs[-2], refs[-1]
            if more_body is not None:
                more_body(ins[2 + len(kept) :], refs[len(outs) : -2])
            waits = []
            for part in range(2):
                bit = places[2 * part]
                half = 1 - bit if got else bit
                wide[part] = ins[part][...].astype(F32)
                at = 0
                for size, starts in place(targets, part, half):
                    source, sem = wide.at[part, pl.ds(at, size)], sems.at[len(waits)]
                    starts(source, sem)
                    waits.append((size, source, sem))
                    at += size
            for size, source, sem in waits:
                pltpu.make_async_copy(source, wide.at[0, pl.ds(0, size)], sem).wait()

        return self.kernel(
            "finish",
            body,
            mine + kept + tuple(more_ins),
            [shape(out.shape, F32) for out in outs] + list(more_outs),
            token,
            out_specs=[ANY] * len(outs) + [VMEM] * len(more_outs),
            scratch=(pltpu.VMEM((2, rows, WIDTH), F32), pltpu.SemaphoreType.DMA((4,))),
            in_specs=[VMEM] * 2 + [ANY] * len(kept) + [VMEM] * len(more_ins),
            grant=24,
            flops=flops,
            aliases={4 + index: index for index in range(len(kept))},
        )


def copy_to(target):
    return lambda source, sem: pltpu.make_async_copy(source, target, sem).start()


def block_columns(block):
    return pl.ds(pl.multiple_of(block * WIDTH, 128), WIDTH)


def place_x(refs, part, half):
    down, up = refs
    if part == 0:
        return [(768, copy_to(down.at[pl.ds(pl.multiple_of(half * 768, 8), 768)]))]
    return [(384, copy_to(up.at[:, block_columns(2 * half + block)])) for block in range(2)]


def place_y(refs, part, half):
    qkv, out = refs
    if part == 0:
        return [(384, copy_to(qkv.at[:, block_columns(half)]))]

    def starts(source, sem):
        @pl.when(half == 0)
        def _():
            copy_to(qkv.at[:, block_columns(2)])(source, sem)

        @pl.when(half == 1)
        def _():
            copy_to(out)(source, sem)

    return [(384, starts)]


def pack_vectors(vectors):
    size = sum(vector.shape[0] for vector in vectors)
    total = jnp.zeros((size,), F32)
    at = 0
    for vector in vectors:
        total = total + jnp.pad(vector.astype(F32), (at, size - at - vector.shape[0]))
        at += vector.shape[0]
    return total.reshape(1, size)


def per_device(
    inputs,
    cotangent,
    lengths,
    cdr_spans,
    mask_vector,
    w_qkv,
    qv_bias,
    w_out,
    b_out,
    norm1_gain,
    norm1_bias,
    w_up,
    b_up,
    w_down,
    b_down,
    norm2_gain,
    norm2_bias,
):
    section_index = lax.axis_index("section")
    core = section_index % 2
    half = core.astype(jnp.int32).reshape(1)
    first = (section_index < 2).astype(jnp.int32).reshape(1)
    places = own_places(core)
    small = pack_vectors(
        (
            qv_bias,
            b_out,
            norm1_gain,
            norm1_bias,
            b_up,
            b_down,
            norm2_gain,
            norm2_bias,
            mask_vector,
        )
    )
    small_got = partner(small, "section", 0)
    got_qkv, got_out = partner((w_qkv, w_out), "section", 0)
    w_up, w_down, got_qkv, got_out, small_got = lax.optimization_barrier(
        (w_up, w_down, got_qkv, got_out, small_got)
    )
    smalls = (small, small_got)
    got_up, got_down = partner((w_up, w_down), "section", 0)
    weights = [(w_qkv, got_qkv), (w_out, got_out), (w_up, got_up), (w_down, got_down)]

    swapped = swap_core_one(cotangent)
    lens_got = swap_core_one(lengths)
    swaps = (core == 1) & (section_index >= 2)
    layer_lens = jnp.where(swaps, lens_got, lengths)

    u, h0 = attend_first(inputs, half, lengths, cdr_spans, weights, smalls)
    first_out = feed_first(u, half, weights, smalls)
    received = between_layers(first_out, False)
    kept = middle(h0, received, cotangent, swapped, half, first, layer_lens, weights, smalls)
    h, qkv, probs, mixed, normal1, inverse1, u, slope, active, normal2, inverse2, output = kept[:12]
    returned = between_layers(kept[13], True)

    a_other, a_own, b_other, b_own, gr1, gb, gsmall, token = back_feed(
        cotangent,
        swapped,
        returned,
        half,
        first,
        weights,
        smalls,
        (u, slope, active, normal1, inverse1, normal2, inverse2),
    )
    a_got = partner(a_other, "section", 0)
    b_got = partner(b_other, "section", 0)
    x, y = Chain("x_", places), Chain("y_", places, TAIL)
    y_other, y_own, small_other, small_own, gh, token = back_attend(
        gb, gr1, half, first, cdr_spans, weights, gsmall, h, qkv, probs, mixed
    )
    y_got = partner(y_other, "section", 0)
    small_got = partner(small_other, "section", 0)
    token = x.start([(a_own, a_got, 0), (b_own, b_got, 0)], 1536, token)

    def tail_rows(ins):
        total = ins[0][...] + ins[1][...]
        rows = [total[:, at : at + WIDTH] for at in range(0, SMALL + WIDTH, WIDTH)]
        rows.append(jnp.zeros((TAIL - len(rows), WIDTH), F32))
        return jnp.concatenate(rows, axis=0).astype(LOW)

    token = y.start(
        [(y_own, y_got, 0), (y_own, y_got, 768)], 768, token, (small_own, small_got), tail_rows
    )
    token = x.hold(token)
    token = y.hold(token)
    both, token = lax.optimization_barrier((kept[12], token))
    both_got = swap_core_one(both)
    token = x.halve(token)
    token = y.halve(token)
    token = x.cross(token)
    token = y.cross(token)
    token = x.across(token)
    token = y.across(token)
    _, token = x.total(token)

    def small_outputs(tail, outs):
        flat = jnp.concatenate([tail[row : row + 1, :] for row in range(6)], axis=1)
        at = 0
        for out, size in zip(outs, SIZES):
            out[...] = flat[0, at : at + size]
            at += size

    out_small, token = y.total(token, [shape((size,), F32) for size in SIZES], small_outputs)
    _, token = x.back(token)

    def mask_output(ins, outs):
        outs[0][...] = ins[0][6, :].astype(F32) + ins[1][6, :].astype(F32)

    _, token = y.back(token)
    gradients_x = [shape((1536, WIDTH), F32), shape((384, HIDDEN), F32)]
    gradients_y = [shape((384, 3 * WIDTH), F32), shape((384, WIDTH), F32)]
    token = x.double(token, LONG)
    gradients_x, token = x.finish(token, gradients_x, place_x, False, LONG)
    token = y.double(token, 0)
    tail_sum, token = lax.optimization_barrier((y.tail_sum, token))
    mask_got = partner(tail_sum, "section", 1)
    gradients_y, token = y.finish(token, gradients_y, place_y, False, 0)
    both_got, token = lax.optimization_barrier((both_got, token))
    (g_down, g_up), token = x.finish(token, gradients_x, place_x, True, LONG)
    (g_qkv, g_out, mask_grad), token = y.finish(
        token,
        gradients_y,
        place_y,
        True,
        LONG,
        (tail_sum, mask_got),
        [shape((WIDTH,), F32)],
        mask_output,
    )
    output = jnp.where(swaps, both_got[0], output)
    gh = jnp.where(swaps, both_got[1], gh)

    g_qv, g_bo, g_n1g, g_n1b, g_bu, g_bd, g_n2g, g_n2b = out_small
    return (
        output.reshape(1, 2, LENGTH, WIDTH),
        gh.reshape(1, 2, LENGTH, WIDTH),
        mask_grad,
        g_qkv,
        g_qv,
        g_out,
        g_bo,
        g_n1g,
        g_n1b,
        g_up,
        g_bu,
        g_down,
        g_bd,
        g_n2g,
        g_n2b,
    )


def solution(mesh):
    in_specs = (
        P(None, "dp", None, None),
        P(None, "dp", None, None),
        P(None, "dp"),
        P(None, "dp", None),
        P(),
        P("section", None),
        P("section"),
        P("section", None),
        P("section"),
        P("section"),
        P("section"),
        P("section", None),
        P("section"),
        P("section", None),
        P("section"),
        P("section"),
        P("section"),
    )
    out_specs = (
        P("section", "dp", None, None),
        P("section", "dp", None, None),
        P(),
        P("section", None),
        P("section"),
        P("section", None),
        P("section"),
        P("section"),
        P("section"),
        P("section", None),
        P("section"),
        P("section", None),
        P("section"),
        P("section"),
        P("section"),
    )
    return jax.shard_map(
        per_device, mesh=mesh, in_specs=in_specs, out_specs=out_specs, check_vma=False
    )
```

```python
import functools
import math

import jax
import jax.numpy as jnp
from jax import lax
from jax.experimental import pallas as pl
from jax.experimental.pallas import tpu as pltpu
from jax.sharding import PartitionSpec as P

EPSILON = 1e-05
F32 = jnp.float32
LOW = jnp.bfloat16
WIDTH = 768
LENGTH = 160
ROWS = 320
HIDDEN = 3072
PAIRS = 6
SCALE = 0.125
SIZES = (768, 384, 384, 384, 1536, 384, 384, 384)
QV, B_OUT, N1G, N1B, B_UP, B_DOWN, N2G, N2B = (sum(SIZES[:at]) for at in range(8))
SMALL = sum(SIZES)
VMEM_LIMIT = 63 * 1024 * 1024
BIG_GRANT = 61 * 1024 * 1024


def dot_nn(left_side, right_side):
    return jnp.dot(left_side, right_side, preferred_element_type=F32)


def dot_nt(left_side, right_side):
    return lax.dot_general(
        left_side, right_side, (((1,), (1,)), ((), ())), preferred_element_type=F32
    )


def dot_tn(left_side, right_side):
    return lax.dot_general(
        left_side, right_side, (((0,), (0,)), ((), ())), preferred_element_type=F32
    )


class Weight:
    def __init__(self, half, own, other, dest, sems, start=True, chunks=1):
        rows, wide = own.shape
        self.dest = dest
        self.wide = wide // chunks
        self.copies = []
        for chunk in range(chunks):
            at = pl.ds(chunk * self.wide, self.wide)
            for side, source in enumerate((own, other)):
                which = half if side == 0 else 1 - half
                place = dest.at[pl.ds(which * rows, rows)]
                if chunks > 1:
                    source, place = source.at[:, at], place.at[:, at]
                self.copies.append(
                    pltpu.make_async_copy(source, place, sems.at[2 * chunk + side])
                )
        if start:
            self.start()

    def start(self):
        for copy in self.copies:
            copy.start()

    def get(self):
        for copy in self.copies:
            copy.wait()
        self.copies = []
        return self.dest[...]

    def chunk(self, index):
        for copy in self.copies[:2]:
            copy.wait()
        self.copies = self.copies[2:]
        return self.dest[:, index * self.wide : (index + 1) * self.wide]


def whole(smalls, at, size):
    return jnp.concatenate([smalls[0:1, at : at + size], smalls[1:2, at : at + size]], axis=1)


def split_heads(tensor):
    lane = lax.broadcasted_iota(jnp.int32, tensor.shape, 1)
    zero = jnp.zeros_like(tensor)
    return jnp.concatenate(
        [jnp.where(lane < 64, tensor, zero), jnp.where(lane < 64, zero, tensor)], axis=0
    )


def join_heads(tensor):
    lane = lax.broadcasted_iota(jnp.int32, (LENGTH, 128), 1)
    return jnp.where(lane < 64, tensor[:LENGTH], tensor[LENGTH:])


def normalize(values):
    center = values - jnp.mean(values, axis=-1, keepdims=True)
    spread = jnp.mean(center * center, axis=-1, keepdims=True)
    inverse = lax.rsqrt(spread + EPSILON)
    return center * inverse, inverse


def normalize_back(upstream, gain, normal, inverse):
    scaled = upstream * gain
    first = jnp.mean(scaled, axis=-1, keepdims=True)
    second = jnp.mean(scaled * normal, axis=-1, keepdims=True)
    return inverse * (scaled - first - normal * second)


def gelu_parts(values):
    size = jnp.abs(values)
    below = 1.0 + (0.3275911 * math.sqrt(0.5)) * size
    t = pl.reciprocal(below, approx=True)
    t = t * (2.0 - below * t)
    series = t * (
        0.5 * 0.254829592
        + t
        * (
            0.5 * -0.284496736
            + t * (0.5 * 1.421413741 + t * (0.5 * -1.453152027 + t * (0.5 * 1.061405429)))
        )
    )
    bell = jnp.exp(-0.5 * values * values)
    tail = series * bell
    share = jnp.where(values >= 0.0, 1.0 - tail, tail)
    return values * share, share + values * bell * (1.0 / math.sqrt(2.0 * math.pi))


def column_sum(values):
    return jnp.sum(values, axis=0, keepdims=True)


def put_halves(target, at, row):
    size = row.shape[1] // 2
    target[0:1, at : at + size] = row[:, :size]
    target[1:2, at : at + size] = row[:, size:]


def places():
    for index in range(2 * PAIRS):
        chain, pair = divmod(index, PAIRS)
        rows = pl.ds(chain * LENGTH, LENGTH)
        yield index, chain, rows, [pl.ds((pair + block * PAIRS) * 128, 128) for block in range(3)]


def attend_body(h, wqkv, wout, smalls, lens, half, qkv, probs, mixed, normal1, inverse1, u, later):
    x = h[...]
    bias = jnp.concatenate(
        [smalls[0:1, :WIDTH], jnp.zeros((1, WIDTH), F32), smalls[1:2, :WIDTH]], axis=1
    )
    for block in range(3):
        at = block * WIDTH
        matrix = wqkv.chunk(block)
        if block == 0:
            for each in later:
                each.start()
        qkv[:, at : at + WIDTH] = (dot_nn(x, matrix) + bias[:, at : at + WIDTH]).astype(LOW)
    for index, chain, rows, (at_q, at_k, at_v) in places():
        scores = dot_nt(qkv[rows, at_k], split_heads(qkv[rows, at_q])) * SCALE
        key = lax.broadcasted_iota(jnp.int32, scores.shape, 0)
        scores = jnp.where(key < lens[half[0], chain], scores, -1000000000.0)
        grown = jnp.exp(scores - jnp.max(scores, axis=0, keepdims=True))
        weights = (grown * (1.0 / jnp.sum(grown, axis=0, keepdims=True))).astype(LOW)
        if probs is not None:
            probs[index] = weights
        mixed[rows, at_q] = join_heads(dot_tn(weights, qkv[rows, at_v])).astype(LOW)
    branch = dot_nn(mixed[...], wout.get()) + whole(smalls, B_OUT, 384)
    normal, inverse = normalize(x.astype(F32) + branch)
    if normal1 is not None:
        normal1[...] = normal
        inverse1[...] = inverse
    u[...] = (normal * whole(smalls, N1G, 384) + whole(smalls, N1B, 384)).astype(LOW)


CHUNK = 1024


def feed_body(u, wup, wdown, smalls, slope, active, normal2, inverse2, y, later=()):
    x = u[...]
    bias = whole(smalls, B_UP, 1536)
    def grow(part, at):
        grown, tangent = gelu_parts(part + bias[:, at : at + CHUNK])
        active[:, at : at + CHUNK] = grown.astype(LOW)
        if slope is not None:
            slope[:, at : at + CHUNK] = tangent.astype(LOW)

    up = wup.chunk(0)
    for each in later:
        each.start()
    grow(dot_nn(x, up), 0)
    up, last = wup.chunk(1), wup.chunk(2)
    grow(dot_nn(x, up), CHUNK)
    part = dot_nn(x, last)
    down = wdown.get()
    grow(part, 2 * CHUNK)
    total = x.astype(F32) + whole(smalls, B_DOWN, 384) + dot_nn(active[...], down)
    normal, inverse = normalize(total)
    if normal2 is not None:
        normal2[...] = normal
        inverse2[...] = inverse
    y[...] = (normal * whole(smalls, N2G, 384) + whole(smalls, N2B, 384)).astype(LOW)


def top_back_body(up, smalls, normal2, inverse2, gr2, gz, gsmall):
    normal = normal2[...]
    put_halves(gsmall, N2G, column_sum(up * normal))
    put_halves(gsmall, N2B, column_sum(up))
    grad = normalize_back(up, whole(smalls, N2G, 384), normal, inverse2[...])
    z = grad.astype(LOW)
    gz[...] = z
    put_halves(gsmall, B_DOWN, column_sum(z.astype(F32)))
    gr2[...] = grad


def feed_back_body(gr2, gz, wup, wdown, smalls, slope, normal1, inverse1, ga, gr1, gb, gsmall):
    z = gz[...]
    down = wdown.get()
    sums = []
    for at in range(0, HIDDEN, CHUNK):
        inner = dot_nt(z, down[at : at + CHUNK, :]) * slope[:, at : at + CHUNK].astype(F32)
        a = inner.astype(LOW)
        ga[:, at : at + CHUNK] = a
        sums.append(column_sum(a.astype(F32)))
    put_halves(gsmall, B_UP, jnp.concatenate(sums, axis=1))
    up = gr2[...] + dot_nt(ga[...], wup.get())
    normal = normal1[...]
    put_halves(gsmall, N1G, column_sum(up * normal))
    put_halves(gsmall, N1B, column_sum(up))
    grad = normalize_back(up, whole(smalls, N1G, 384), normal, inverse1[...])
    gr1[...] = grad
    b = grad.astype(LOW)
    gb[...] = b
    put_halves(gsmall, B_OUT, column_sum(b.astype(F32)))


def heads_back_body(gb, wout, qkv, probs, gqkv, gqv, go):
    go[...] = dot_nt(gb[...], wout.get()).astype(LOW)
    for index, chain, rows, (at_q, at_k, at_v) in places():
        k = qkv[rows, at_k]
        g = split_heads(go[rows, at_q])
        weights = probs[index]
        wide = weights.astype(F32)
        inner = dot_nt(qkv[rows, at_v], g)
        inner = wide * (inner - jnp.sum(wide * inner, axis=0, keepdims=True))
        s = inner.astype(LOW)
        gqkv[rows, at_q] = (join_heads(dot_tn(s, k)) * SCALE).astype(LOW)
        gqkv[rows, at_k] = (dot_nn(s, split_heads(qkv[rows, at_q])) * SCALE).astype(LOW)
        gqkv[rows, at_v] = dot_nn(weights, g).astype(LOW)
    if gqv is not None:
        gqv[0:1, :] = column_sum(gqkv[:, :WIDTH].astype(F32))
        gqv[1:2, :] = column_sum(gqkv[:, 2 * WIDTH :].astype(F32))


def span_rows(spans, half):
    row = lax.broadcasted_iota(jnp.int32, (ROWS, 1), 0)
    inside = row < 0
    for chain in range(2):
        start = spans[half[0], chain, 0] + chain * LENGTH
        end = spans[half[0], chain, 1] + chain * LENGTH
        inside = inside | ((row >= start) & (row < end))
    return inside


def pick_halves(half, own, other, smalls):
    low = half[0] == 0
    smalls[0:1, :] = jnp.where(low, own[:, :SMALL], other[:, :SMALL])
    smalls[1:2, :] = jnp.where(low, other[:, :SMALL], own[:, :SMALL])


VMEM = pl.BlockSpec(memory_space=pltpu.VMEM)
SMEM = pl.BlockSpec(memory_space=pltpu.SMEM)
ANY = pl.BlockSpec(memory_space=pl.ANY)
HBM = pl.BlockSpec(memory_space=pltpu.HBM)
SMALL_SCRATCH = pltpu.VMEM((2, SMALL), F32)
QKV_SHAPE = (ROWS, 3 * WIDTH)
PROBS_SHAPE = (2 * PAIRS, LENGTH, 2 * LENGTH)
ROW_SHAPE = (ROWS, WIDTH)
FEED_SHAPE = (ROWS, HIDDEN)
MACS = ROWS * WIDTH * WIDTH * 2
ATTEND_WEIGHTS = [pltpu.VMEM((WIDTH, 3 * WIDTH), LOW), pltpu.VMEM((WIDTH, WIDTH), LOW)]
FEED_WEIGHTS = [pltpu.VMEM((WIDTH, HIDDEN), LOW), pltpu.VMEM((HIDDEN, WIDTH), LOW)]


def shape(dims, kind=LOW):
    return jax.ShapeDtypeStruct(dims, kind)


def enter_cotangent(half, own, swapped, raw, sem):
    @pl.when(half[0] == 0)
    def _():
        pltpu.make_async_copy(own.at[0], raw, sem).start()

    @pl.when(half[0] == 1)
    def _():
        pltpu.make_async_copy(swapped.at[1], raw, sem).start()

    return pltpu.make_async_copy(swapped.at[1], raw, sem)


def kernel_call(body, ins, outs, scratch, flops, moved, name, out_specs=None, grant=VMEM_LIMIT):
    return pl.pallas_call(
        body,
        in_specs=ins,
        out_specs=out_specs or [VMEM] * len(outs),
        out_shape=outs,
        scratch_shapes=scratch,
        compiler_params=pltpu.CompilerParams(vmem_limit_bytes=grant),
        cost_estimate=pl.CostEstimate(flops=flops, bytes_accessed=moved, transcendentals=0),
        name=name,
    )


def attend_first(inputs, half, lens, spans, weights, smalls):
    def body(x, half, lens, spans, so, sp, qo, qp, oo, op, u, h, raw, small, qkv, mixed, wq, wo, sems):
        enter = pltpu.make_async_copy(x.at[half[0]], raw, sems.at[2, 0])
        enter.start()
        wqkv = Weight(half[0], qo, qp, wq, sems.at[0], True, 3)
        wout = Weight(half[0], oo, op, wo, sems.at[1], False)
        pick_halves(half, so, sp, small)
        enter.wait()
        mask = so[:, SMALL:].astype(LOW)
        h[...] = jnp.where(span_rows(spans, half), mask, raw[...].reshape(ROWS, WIDTH))
        attend_body(h, wqkv, wout, small, lens, half, qkv, None, mixed, None, None, u, [wout])

    return kernel_call(
        body,
        [ANY, SMEM, SMEM, SMEM, VMEM, VMEM] + [ANY] * 4,
        [shape(ROW_SHAPE), shape(ROW_SHAPE)],
        [
            pltpu.VMEM((2, LENGTH, WIDTH), LOW),
            SMALL_SCRATCH,
            pltpu.VMEM(QKV_SHAPE, LOW),
            pltpu.VMEM(ROW_SHAPE, LOW),
            *ATTEND_WEIGHTS,
            pltpu.SemaphoreType.DMA((3, 6)),
        ],
        40 * MACS,
        80000000,
        "attend_first",
    )(inputs, half, lens, spans, *smalls, *weights[0], *weights[1])


def feed_first(u, half, weights, smalls):
    def body(u, half, so, sp, uo, up, do, dp, y, small, active, wu, wd, sems):
        wup = Weight(half[0], uo, up, wu, sems.at[0], True, 3)
        wdown = Weight(half[0], do, dp, wd, sems.at[1], False)
        pick_halves(half, so, sp, small)
        feed_body(u, wup, wdown, small, None, active, None, None, y, [wdown])

    return kernel_call(
        body,
        [VMEM, SMEM, VMEM, VMEM] + [ANY] * 4,
        [shape(ROW_SHAPE)],
        [
            SMALL_SCRATCH,
            pltpu.VMEM(FEED_SHAPE, LOW),
            *FEED_WEIGHTS,
            pltpu.SemaphoreType.DMA((2, 6)),
        ],
        8 * MACS,
        14000000,
        "feed_first",
    )(u, half, *smalls, *weights[2], *weights[3])[0]


KEPT = [
    shape(ROW_SHAPE),
    shape(QKV_SHAPE),
    shape(PROBS_SHAPE),
    shape(ROW_SHAPE),
    shape(ROW_SHAPE, F32),
    shape((ROWS, 1), F32),
    shape(ROW_SHAPE),
    shape(FEED_SHAPE),
    shape(FEED_SHAPE),
    shape(ROW_SHAPE, F32),
    shape((ROWS, 1), F32),
    shape(ROW_SHAPE),
]


def middle(h0, received, cotangent, swapped, half, first, lens, weights, smalls):
    def body(h0, received, cot, swap, half, first, lens, so, sp, qo, qp, oo, op, uo, up, do, dp, *rest):
        outs, rest = rest[: len(KEPT)], rest[len(KEPT) :]
        both, rest = rest[0], rest[1:]
        gh, small, gr2, gz, ga, gr1, gb, gsmall, gqkv, go, raw, wq, wo, wu, wd = rest[:15]
        keeps, sems, out_sems, raw_sem = rest[15:-3], *rest[-3:]
        h, qkv, probs, mixed, normal1, inverse1, u, slope, active, normal2, inverse2, y = keeps
        wqkv = Weight(half[0], qo, qp, wq, sems.at[0], True, 3)
        wout = Weight(half[0], oo, op, wo, sems.at[1])
        wup = Weight(half[0], uo, up, wu, sems.at[2], True, 3)
        wdown = Weight(half[0], do, dp, wd, sems.at[3])
        enter = enter_cotangent(half, cot, swap, raw, raw_sem)
        pick_halves(half, so, sp, small)
        leaving = []

        def leave(places):
            for place in places:
                copy = pltpu.make_async_copy(keeps[place], outs[place], out_sems.at[place])
                copy.start()
                leaving.append(copy)

        h[...] = jnp.where(first[0] > 0, h0[...], received[...])
        attend_body(
            h, wqkv, wout, small, lens, half, qkv, probs, mixed, normal1, inverse1, u, ()
        )
        leave(range(7))
        feed_body(u, wup, wdown, small, slope, active, normal2, inverse2, y)
        leave(range(7, 12))
        output = pltpu.make_async_copy(y, both.at[0], out_sems.at[len(KEPT)])
        output.start()
        leaving.append(output)
        enter.wait()
        upstream = raw[...].reshape(ROWS, WIDTH).astype(F32)
        top_back_body(upstream, small, normal2, inverse2, gr2, gz, gsmall)
        feed_back_body(gr2, gz, wup, wdown, small, slope, normal1, inverse1, ga, gr1, gb, gsmall)
        heads_back_body(gb, wout, qkv, probs, gqkv, None, go)
        gh[...] = (gr1[...] + dot_nt(gqkv[...], wqkv.get())).astype(LOW)
        output = pltpu.make_async_copy(gh, both.at[1], out_sems.at[len(KEPT) + 1])
        output.start()
        leaving.append(output)
        for copy in leaving:
            copy.wait()

    return kernel_call(
        body,
        [VMEM, VMEM, ANY, ANY, SMEM, SMEM, SMEM, VMEM, VMEM] + [ANY] * 8,
        KEPT + [shape((2, ROWS, WIDTH)), shape(ROW_SHAPE)],
        [
            SMALL_SCRATCH,
            pltpu.VMEM(ROW_SHAPE, F32),
            pltpu.VMEM(ROW_SHAPE, LOW),
            pltpu.VMEM(FEED_SHAPE, LOW),
            pltpu.VMEM(ROW_SHAPE, F32),
            pltpu.VMEM(ROW_SHAPE, LOW),
            SMALL_SCRATCH,
            pltpu.VMEM(QKV_SHAPE, LOW),
            pltpu.VMEM(ROW_SHAPE, LOW),
            pltpu.VMEM((2, LENGTH, WIDTH), LOW),
            *ATTEND_WEIGHTS,
            *FEED_WEIGHTS,
            *[pltpu.VMEM(kept.shape, kept.dtype) for kept in KEPT],
            pltpu.SemaphoreType.DMA((4, 6)),
            pltpu.SemaphoreType.DMA((len(KEPT) + 2,)),
            pltpu.SemaphoreType.DMA,
        ],
        24 * MACS,
        45000000,
        "middle",
        [ANY] * len(KEPT) + [ANY, VMEM],
        BIG_GRANT,
    )(
        h0, received, cotangent, swapped, half, first, lens, *smalls,
        *weights[0], *weights[1], *weights[2], *weights[3],
    )


MIB = 1024 * 1024


def half_columns(ref, which):
    size = ref.shape[1] // 2
    return ref[:, pl.ds(pl.multiple_of(which * size, 128), size)]


class Arriving:
    def __init__(self, pairs, sems):
        self.copies = {}
        for place, (name, source, dest) in enumerate(pairs):
            copy = pltpu.make_async_copy(source, dest, sems.at[place])
            copy.start()
            self.copies[name] = (copy, dest)

    def get(self, name):
        copy, dest = self.copies[name]
        copy.wait()
        return dest


class Leaving:
    def __init__(self, sems):
        self.sems = sems
        self.copies = []

    def send(self, source, target):
        copy = pltpu.make_async_copy(source, target, self.sems.at[len(self.copies)])
        copy.start()
        self.copies.append(copy)

    def wait(self):
        for copy in self.copies:
            copy.wait()


def send_folded(leaving, local, target, left_side, right):
    for block in range(right.shape[1] // WIDTH):
        rows = pl.ds(block * 384, 384)
        grad = dot_tn(left_side, right[:, block * WIDTH : (block + 1) * WIDTH])
        local[rows, :] = grad.astype(LOW)
        leaving.send(local.at[rows], target.at[rows])


TOKEN = shape((8, 128), F32)
GRAD_SHAPE = (1536, WIDTH)
GRAD_SCRATCH = pltpu.VMEM(GRAD_SHAPE, LOW)


def back_feed(cotangent, swapped, returned, half, first, weights, smalls, kept):
    u, slope, active, n1, i1, n2, i2 = kept

    def body(cot, swap, returned, half, first, so, sp, i1, n2, i2, uo, up, do, dp, u, slope, active, n1, *rest):
        outs, rest = rest[:8], rest[8:]
        down_other, down_own, up_other, up_own, gr1, gb, gsmall, token = outs
        gr2, gz, ga, v0, v1, v2, v3, small, raw, wu, wd, vu, vs, va, vn, sems, in_sems, out_sems = rest
        enter = enter_cotangent(half, cot, swap, raw, sems.at[2, 0])
        arriving = Arriving([("active", active, va)], in_sems)
        wdown = Weight(half[0], do, dp, wd, sems.at[1])
        later = Arriving(
            [("slope", slope, vs), ("normal", n1, vn), ("u", u, vu)],
            in_sems.at[pl.ds(1, 3)],
        )
        wup = Weight(half[0], uo, up, wu, sems.at[0])
        pick_halves(half, so, sp, small)
        enter.wait()
        upstream = jnp.where(first[0] > 0, returned[...], raw[...].reshape(ROWS, WIDTH))
        top_back_body(upstream.astype(F32), small, n2, i2, gr2, gz, gsmall)
        leaving = Leaving(out_sems)
        arriving.get("active")
        for which, local, target in ((1 - half[0], v0, down_other), (half[0], v1, down_own)):
            local[...] = dot_tn(half_columns(va, which), gz[...]).astype(LOW)
            leaving.send(local, target)
        later.get("slope")
        later.get("normal")
        feed_back_body(gr2, gz, wup, wdown, small, vs, vn, i1, ga, gr1, gb, gsmall)
        later.get("u")
        for which, local, target in ((1 - half[0], v2, up_other), (half[0], v3, up_own)):
            send_folded(leaving, local, target, half_columns(vu, which), ga)
        token[...] = jnp.zeros(token.shape, F32)
        leaving.wait()

    return kernel_call(
        body,
        [ANY, ANY, VMEM, SMEM, SMEM] + [VMEM] * 5 + [ANY] * 8,
        [shape(GRAD_SHAPE)] * 4
        + [shape(ROW_SHAPE, F32), shape(ROW_SHAPE), shape((2, SMALL), F32), TOKEN],
        [
            pltpu.VMEM(ROW_SHAPE, F32),
            pltpu.VMEM(ROW_SHAPE, LOW),
            pltpu.VMEM(FEED_SHAPE, LOW),
            *[GRAD_SCRATCH] * 4,
            SMALL_SCRATCH,
            pltpu.VMEM((2, LENGTH, WIDTH), LOW),
            *FEED_WEIGHTS,
            pltpu.VMEM(ROW_SHAPE, LOW),
            pltpu.VMEM(FEED_SHAPE, LOW),
            pltpu.VMEM(FEED_SHAPE, LOW),
            pltpu.VMEM(ROW_SHAPE, F32),
            pltpu.SemaphoreType.DMA((3, 2)),
            pltpu.SemaphoreType.DMA((4,)),
            pltpu.SemaphoreType.DMA((10,)),
        ],
        200 * MACS,
        600000000,
        "back_feed",
        [ANY] * 4 + [VMEM] * 4,
        BIG_GRANT,
    )(
        cotangent, swapped, returned, half, first, *smalls, i1, n2, i2, *weights[2], *weights[3],
        u, slope, active, n1,
    )


def back_attend(gb, gr1, half, first, spans, weights, gsmall, h, qkv, probs, mixed):
    def body(gb, half, first, spans, gsmall, oo, op, qo, qp, gr1, h, qkv, probs, mixed, *rest):
        outs, rest = rest[:6], rest[6:]
        other, own, small_other, small_own, gh, token = outs
        gqkv, go, gqv, vother, vown, wo, wq, vr, vh, vq, vp, vm, sems, in_sems, out_sems = rest
        wout = Weight(half[0], oo, op, wo, sems.at[0])
        arriving = Arriving([("qkv", qkv, vq), ("probs", probs, vp)], in_sems)
        wqkv = Weight(half[0], qo, qp, wq, sems.at[1], False)
        arriving.get("qkv")
        arriving.get("probs")
        wqkv.start()
        late = Arriving([("h", h, vh), ("mixed", mixed, vm), ("gr1", gr1, vr)], in_sems.at[pl.ds(2, 3)])
        heads_back_body(gb, wout, vq, vp, gqkv, gqv, go)
        leaving = Leaving(out_sems)
        late.get("h")
        late.get("mixed")
        for which, local, target in ((1 - half[0], vother, other), (half[0], vown, own)):
            send_folded(leaving, local, target, half_columns(vh, which), gqkv)
            local[1152:, :] = dot_tn(half_columns(vm, which), gb[...]).astype(LOW)
            leaving.send(local.at[pl.ds(1152, 384)], target.at[pl.ds(1152, 384)])
        late.get("gr1")
        full = vr[...] + dot_nt(gqkv[...], wqkv.get())
        dropped = span_rows(spans, half) & (first[0] > 0)
        zero = jnp.zeros_like(full)
        gh[...] = jnp.where(dropped, zero, full).astype(LOW)
        gmask = column_sum(jnp.where(dropped, full, zero))
        for which, target in ((1 - half[0], small_other), (half[0], small_own)):
            target[:, :WIDTH] = gqv[pl.ds(which, 1), :]
            target[:, WIDTH:SMALL] = gsmall[pl.ds(which, 1), WIDTH:]
            target[:, SMALL:] = gmask
        token[...] = jnp.zeros(token.shape, F32)
        leaving.wait()

    return kernel_call(
        body,
        [VMEM, SMEM, SMEM, SMEM, VMEM] + [ANY] * 9,
        [
            shape(GRAD_SHAPE),
            shape(GRAD_SHAPE),
            shape((1, SMALL + WIDTH), F32),
            shape((1, SMALL + WIDTH), F32),
            shape(ROW_SHAPE),
            TOKEN,
        ],
        [
            pltpu.VMEM(QKV_SHAPE, LOW),
            pltpu.VMEM(ROW_SHAPE, LOW),
            pltpu.VMEM((2, WIDTH), F32),
            GRAD_SCRATCH,
            GRAD_SCRATCH,
            ATTEND_WEIGHTS[1],
            ATTEND_WEIGHTS[0],
            pltpu.VMEM(ROW_SHAPE, F32),
            pltpu.VMEM(ROW_SHAPE, LOW),
            pltpu.VMEM(QKV_SHAPE, LOW),
            pltpu.VMEM(PROBS_SHAPE, LOW),
            pltpu.VMEM(ROW_SHAPE, LOW),
            pltpu.SemaphoreType.DMA((2, 2)),
            pltpu.SemaphoreType.DMA((5,)),
            pltpu.SemaphoreType.DMA((8,)),
        ],
        180 * MACS,
        400000000,
        "back_attend",
        [ANY, ANY] + [VMEM] * 4,
    )(gb, half, first, spans, gsmall, *weights[1], *weights[0], gr1, h, qkv, probs, mixed)


TAIL = 16
BLOCK = 96


def add_rows(target, sources, at, rows):
    for start in range(0, rows, BLOCK):
        size = min(BLOCK, rows - start)
        place = pl.ds(at + start, size)
        if not isinstance(at, int):
            place = pl.ds(pl.multiple_of(at + start, 16), size)
        if len(sources) == 2:
            target[start : start + size, :] = sources[0][place, :] + sources[1][place, :]
            continue
        total = sources[0][place, :].astype(F32)
        for source in sources[1:]:
            total = total + source[place, :].astype(F32)
        target[start : start + size, :] = total.astype(LOW)


LONG = 30000000000


def ordered(
    name, body, ins, outs, where, after, out_specs=None, scratch=(), in_specs=None, grant=16, aliases=None,
    flops=LONG,
):
    count, made = len(ins), len(outs)

    def kernel(where, after, *refs):
        refs[count + made][...] = jnp.zeros(TOKEN.shape, F32)
        body(where, refs[:count], refs[count : count + made] + refs[count + made + 1 :])

    result = pl.pallas_call(
        kernel,
        in_specs=[SMEM, HBM] + (in_specs or [VMEM] * count),
        out_specs=(out_specs or [VMEM] * made) + [VMEM],
        out_shape=list(outs) + [TOKEN],
        scratch_shapes=list(scratch),
        input_output_aliases=aliases or {},
        compiler_params=pltpu.CompilerParams(vmem_limit_bytes=grant * MIB),
        cost_estimate=pl.CostEstimate(flops=flops, bytes_accessed=flops, transcendentals=0),
        name=name,
    )(where, after, *ins)
    return result[:made], result[made]


def partner(x, axis, bit):
    return lax.ppermute(x, axis, [(i, i ^ 1 << bit) for i in range(lax.axis_size(axis))])


def moved_on(index, axis, steps):
    z, x, y = index // 8, index // 2 % 4, index % 2
    if axis == "z":
        z = steps(z)
    elif axis == "x":
        x = steps(x)
    else:
        y = steps(y)
    return z * 8 + x * 2 + y


def send_along(value, axes, place):
    pairs = []
    for section in range(4):
        for index in range(32):
            to = moved_on(index, axes[section % 2], place)
            pairs.append((section * 32 + index, section * 32 + to))
    return lax.ppermute(value, ("section", "dp"), pairs)


def exchange(value, part, step):
    flip = 1 if part == step else 3
    return send_along(value, "zx", lambda place: place ^ flip)


def turn(value, steps):
    return send_along(value, "xz", lambda place: (place + steps) % 4)


def across_y(value):
    return send_along(value, "yy", lambda place: place ^ 1)


def swap_core_one(value):
    pairs = [
        (section * 32 + index, section * 32 + (index ^ 1)) for section in (1, 3) for index in range(32)
    ]
    return lax.ppermute(value, ("section", "dp"), pairs)


def between_layers(value, back):
    pairs = []
    for core in range(2):
        for index in range(32):
            pair = (core * 32 + index, (core + 2) * 32 + (index ^ core))
            pairs.append(pair[::-1] if back else pair)
    return lax.ppermute(value, ("section", "dp"), pairs)


def own_places(core):
    index = lax.axis_index("dp")
    z, x = index // 8, index // 2 % 4
    ring = jnp.where(core == 0, z, x)
    high = ring // 2
    low = high ^ (ring % 2)
    table = [low, high, high, low, jnp.where(core == 0, x, z)]
    return jnp.stack(table).astype(jnp.int32)


def row_shapes(*counts):
    return [shape((count, WIDTH)) for count in counts]


def add_tail(target, rows, sources, at, extra):
    if extra:
        total = sources[0][at : at + extra, :].astype(F32)
        for source in sources[1:]:
            total = total + source[at : at + extra, :].astype(F32)
        target[rows : rows + extra, :] = total.astype(LOW)


class Chain:
    def __init__(self, name, places, tail=0):
        self.name = name
        self.places = places
        self.tail = (0, tail)
        self.keep = [None, None]
        self.got = [None, None]

    def kernel(self, name, body, ins, outs, token, *more, **named):
        return ordered(self.name + name, body, ins, outs, self.places, token, *more, **named)

    def pairs(self):
        return (self.keep[0], self.got[0], self.keep[1], self.got[1])

    def first_sum(self, name, sent, token):
        sources, half_rows, tails = self.sources, self.rows, self.tail

        def body(places, ins, refs):
            outs, held, sems = refs[:2], refs[2:6], refs[6]
            copies = []
            for index in range(4):
                bit, at = places[2 * (index // 2)], sources[index // 2][2]
                which = 1 - bit if sent else bit
                rows = pl.ds(pl.multiple_of(at + which * half_rows, 16), half_rows)
                copy = pltpu.make_async_copy(ins[index].at[rows], held[index], sems.at[index])
                copy.start()
                copies.append(copy)
            for part in range(2):
                copies[2 * part].wait()
                copies[2 * part + 1].wait()
                add_rows(outs[part], held[2 * part : 2 * part + 2], 0, half_rows)
                if tails[part]:
                    outs[part][half_rows:, :] = self.tail_body(ins[4:])

        arrays = [array for own, got, _ in sources for array in (own, got)]
        return self.kernel(
            name,
            body,
            (*arrays, *self.tail_ins),
            row_shapes(half_rows + tails[0], half_rows + tails[1]),
            token,
            scratch=(*[pltpu.VMEM((half_rows, WIDTH), LOW)] * 4, pltpu.SemaphoreType.DMA((4,))),
            in_specs=[HBM] * 4 + [VMEM] * len(self.tail_ins),
            grant=63 if sent else 46,
            flops=LONG if sent else 0,
        )

    def start(self, sources, rows, token, tail_ins=(), tail_body=None):
        self.rows, self.sources = rows // 2, sources
        self.tail_ins, self.tail_body = tuple(tail_ins), tail_body
        sends, token = self.first_sum("send", True, token)
        self.got = [exchange(sends[part], part, 0) for part in range(2)]
        return token

    def hold(self, token):
        keeps, token = self.first_sum("keep", False, token)
        self.keep = list(keeps)
        return token

    def halve(self, token, flops):
        self.rows //= 2
        rows, tails = self.rows, self.tail

        def body(places, ins, outs):
            for part in range(2):
                bit = places[2 * part + 1]
                pair = ins[2 * part : 2 * part + 2]
                for target, which in ((outs[2 * part + 1], 1 - bit), (outs[2 * part], bit)):
                    add_rows(target, pair, which * rows, rows)
                    add_tail(target, rows, pair, 2 * rows, tails[part])

        counts = [rows + tails[0]] * 2 + [rows + tails[1]] * 2
        outs, token = self.kernel(
            "halve", body, self.pairs(), row_shapes(*counts), token, flops=flops
        )
        for part in range(2):
            self.keep[part] = outs[2 * part]
            self.got[part] = exchange(outs[2 * part + 1], part, 1)
        return token

    def cross(self, token):
        whole_rows, extra = self.rows, self.tail[1]
        rows = whole_rows // 2

        def body(places, ins, refs):
            outs, total = refs[:4], refs[4]
            add_rows(total.at[pl.ds(0, whole_rows)], ins[:2], 0, whole_rows)
            add_rows(total.at[pl.ds(whole_rows, whole_rows)], ins[2:], 0, whole_rows)
            for steps in range(4):
                quarter = (places[4] + steps) % 4
                outs[steps][:rows, :] = total[pl.ds(pl.multiple_of(quarter * rows, 16), rows), :]
                add_tail(outs[steps], rows, ins[2:], whole_rows, extra)

        (self.own, *sends), token = self.kernel(
            "cross",
            body,
            self.pairs(),
            row_shapes(*[rows + extra] * 4),
            token,
            None,
            (pltpu.VMEM((2 * whole_rows, WIDTH), LOW),),
        )
        self.rows = rows
        self.ring = [turn(send, steps) for steps, send in zip((1, 2, 3), sends)]
        return token

    def across(self, token):
        rows = self.rows + self.tail[1]

        def body(places, ins, outs):
            add_rows(outs[0], ins, 0, rows)

        (self.own,), token = self.kernel(
            "across", body, (self.own, *self.ring), row_shapes(rows), token
        )
        self.other = across_y(self.own)
        return token

    def total(self, token, more_outs=(), more_body=None):
        rows, extra = self.rows, self.tail[1]

        def body(places, ins, outs):
            add_rows(outs[0], ins, 0, rows)
            if extra:
                add_rows(outs[1], ins, rows, extra)
                more_body(outs[1][...].astype(F32), outs[2:])

        counts = [rows] + ([extra] if extra else [])
        outs, token = self.kernel(
            "total", body, (self.own, self.other), row_shapes(*counts) + list(more_outs), token
        )
        self.own = outs[0]
        self.tail_sum = outs[1] if extra else None
        self.ring = [turn(self.own, steps) for steps in (1, 2, 3)]
        return outs[2:], token

    def back(self, token, more_ins=(), more_outs=(), more_body=None):
        rows = self.rows

        def body(places, ins, refs):
            outs, total = refs[:-1], refs[-1]
            for steps in range(4):
                quarter = (places[4] - steps + 4) % 4
                total[pl.ds(pl.multiple_of(quarter * rows, 16), rows), :] = ins[steps][...]
            outs[0][...] = total[: 2 * rows, :]
            outs[1][...] = total[2 * rows :, :]
            if more_body is not None:
                more_body(ins[4:], outs[2:])

        outs, token = self.kernel(
            "back",
            body,
            (self.own, *self.ring) + tuple(more_ins),
            row_shapes(2 * rows, 2 * rows) + list(more_outs),
            token,
            None,
            (pltpu.VMEM((4 * rows, WIDTH), LOW),),
        )
        self.rows = 2 * rows
        self.keep = list(outs[:2])
        self.got = [exchange(self.keep[part], part, 1) for part in range(2)]
        return outs[2:], token

    def double(self, token, flops):
        rows = self.rows

        def body(places, ins, outs):
            for part in range(2):
                bit = places[2 * part + 1]
                for which, source in ((bit, ins[2 * part]), (1 - bit, ins[2 * part + 1])):
                    outs[part][pl.ds(pl.multiple_of(which * rows, 16), rows), :] = source[...]

        outs, token = self.kernel(
            "double", body, self.pairs(), row_shapes(2 * rows, 2 * rows), token, flops=flops
        )
        self.rows = 2 * rows
        self.keep = list(outs)
        self.got = [exchange(self.keep[part], part, 0) for part in range(2)]
        return token

    def finish(self, token, outs, place, got, flops, more_ins=(), more_outs=(), more_body=None):
        rows = self.rows
        mine = tuple(self.got if got else self.keep)
        kept = tuple(outs) if got else ()

        def body(places, ins, refs):
            targets, wide, sems = refs[: len(outs)], refs[-2], refs[-1]
            if more_body is not None:
                more_body(ins[2 + len(kept) :], refs[len(outs) : -2])
            waits = []
            for part in range(2):
                bit = places[2 * part]
                half = 1 - bit if got else bit
                wide[part] = ins[part][...].astype(F32)
                at = 0
                for size, starts in place(targets, part, half):
                    source, sem = wide.at[part, pl.ds(at, size)], sems.at[len(waits)]
                    starts(source, sem)
                    waits.append((size, source, sem))
                    at += size
            for size, source, sem in waits:
                pltpu.make_async_copy(source, wide.at[0, pl.ds(0, size)], sem).wait()

        return self.kernel(
            "finish",
            body,
            mine + kept + tuple(more_ins),
            [shape(out.shape, F32) for out in outs] + list(more_outs),
            token,
            out_specs=[ANY] * len(outs) + [VMEM] * len(more_outs),
            scratch=(pltpu.VMEM((2, rows, WIDTH), F32), pltpu.SemaphoreType.DMA((4,))),
            in_specs=[VMEM] * 2 + [ANY] * len(kept) + [VMEM] * len(more_ins),
            grant=24,
            flops=flops,
            aliases={4 + index: index for index in range(len(kept))},
        )


def copy_to(target):
    return lambda source, sem: pltpu.make_async_copy(source, target, sem).start()


def block_columns(block):
    return pl.ds(pl.multiple_of(block * WIDTH, 128), WIDTH)


def place_x(refs, part, half):
    down, up = refs
    if part == 0:
        return [(768, copy_to(down.at[pl.ds(pl.multiple_of(half * 768, 8), 768)]))]
    return [(384, copy_to(up.at[:, block_columns(2 * half + block)])) for block in range(2)]


def place_y(refs, part, half):
    qkv, out = refs
    if part == 0:
        return [(384, copy_to(qkv.at[:, block_columns(half)]))]

    def starts(source, sem):
        @pl.when(half == 0)
        def _():
            copy_to(qkv.at[:, block_columns(2)])(source, sem)

        @pl.when(half == 1)
        def _():
            copy_to(out)(source, sem)

    return [(384, starts)]


def pack_vectors(vectors):
    size = sum(vector.shape[0] for vector in vectors)
    total = jnp.zeros((size,), F32)
    at = 0
    for vector in vectors:
        total = total + jnp.pad(vector.astype(F32), (at, size - at - vector.shape[0]))
        at += vector.shape[0]
    return total.reshape(1, size)


def per_device(
    inputs,
    cotangent,
    lengths,
    cdr_spans,
    mask_vector,
    w_qkv,
    qv_bias,
    w_out,
    b_out,
    norm1_gain,
    norm1_bias,
    w_up,
    b_up,
    w_down,
    b_down,
    norm2_gain,
    norm2_bias,
):
    section_index = lax.axis_index("section")
    core = section_index % 2
    half = core.astype(jnp.int32).reshape(1)
    first = (section_index < 2).astype(jnp.int32).reshape(1)
    places = own_places(core)
    small = pack_vectors(
        (
            qv_bias,
            b_out,
            norm1_gain,
            norm1_bias,
            b_up,
            b_down,
            norm2_gain,
            norm2_bias,
            mask_vector,
        )
    )
    small_got = partner(small, "section", 0)
    got_qkv, got_out = partner((w_qkv, w_out), "section", 0)
    w_up, w_down, got_qkv, got_out, small_got = lax.optimization_barrier(
        (w_up, w_down, got_qkv, got_out, small_got)
    )
    smalls = (small, small_got)
    got_up, got_down = partner((w_up, w_down), "section", 0)
    weights = [(w_qkv, got_qkv), (w_out, got_out), (w_up, got_up), (w_down, got_down)]

    swapped = swap_core_one(cotangent)
    lens_got = swap_core_one(lengths)
    swaps = (core == 1) & (section_index >= 2)
    layer_lens = jnp.where(swaps, lens_got, lengths)

    u, h0 = attend_first(inputs, half, lengths, cdr_spans, weights, smalls)
    first_out = feed_first(u, half, weights, smalls)
    received = between_layers(first_out, False)
    kept = middle(h0, received, cotangent, swapped, half, first, layer_lens, weights, smalls)
    h, qkv, probs, mixed, normal1, inverse1, u, slope, active, normal2, inverse2, output = kept[:12]
    returned = between_layers(kept[13], True)

    a_other, a_own, b_other, b_own, gr1, gb, gsmall, token = back_feed(
        cotangent,
        swapped,
        returned,
        half,
        first,
        weights,
        smalls,
        (u, slope, active, normal1, inverse1, normal2, inverse2),
    )
    a_got = partner(a_other, "section", 0)
    b_got = partner(b_other, "section", 0)
    x, y = Chain("x_", places), Chain("y_", places, TAIL)
    y_other, y_own, small_other, small_own, gh, token = back_attend(
        gb, gr1, half, first, cdr_spans, weights, gsmall, h, qkv, probs, mixed
    )
    y_got = partner(y_other, "section", 0)
    small_got = partner(small_other, "section", 0)
    token = x.start([(a_own, a_got, 0), (b_own, b_got, 0)], 1536, token)

    def tail_rows(ins):
        total = ins[0][...] + ins[1][...]
        rows = [total[:, at : at + WIDTH] for at in range(0, SMALL + WIDTH, WIDTH)]
        rows.append(jnp.zeros((TAIL - len(rows), WIDTH), F32))
        return jnp.concatenate(rows, axis=0).astype(LOW)

    token = y.start(
        [(y_own, y_got, 0), (y_own, y_got, 768)], 768, token, (small_own, small_got), tail_rows
    )
    token = x.hold(token)
    token = x.halve(token, 0)
    token = y.hold(token)
    token = y.halve(token, LONG)
    token = x.cross(token)
    both, token = lax.optimization_barrier((kept[12], token))
    both_got = swap_core_one(both)
    token = y.cross(token)
    token = x.across(token)
    token = y.across(token)
    _, token = x.total(token)

    def small_outputs(tail, outs):
        flat = jnp.concatenate([tail[row : row + 1, :] for row in range(6)], axis=1)
        at = 0
        for out, size in zip(outs, SIZES):
            out[...] = flat[0, at : at + size]
            at += size

    out_small, token = y.total(token, [shape((size,), F32) for size in SIZES], small_outputs)
    _, token = x.back(token)

    def mask_output(ins, outs):
        outs[0][...] = ins[0][6, :].astype(F32) + ins[1][6, :].astype(F32)

    _, token = y.back(token)
    gradients_x = [shape((1536, WIDTH), F32), shape((384, HIDDEN), F32)]
    gradients_y = [shape((384, 3 * WIDTH), F32), shape((384, WIDTH), F32)]
    token = x.double(token, LONG)
    gradients_x, token = x.finish(token, gradients_x, place_x, False, LONG)
    token = y.double(token, 0)
    tail_sum, token = lax.optimization_barrier((y.tail_sum, token))
    mask_got = partner(tail_sum, "section", 1)
    gradients_y, token = y.finish(token, gradients_y, place_y, False, 0)
    both_got, token = lax.optimization_barrier((both_got, token))
    (g_down, g_up), token = x.finish(token, gradients_x, place_x, True, LONG)
    (g_qkv, g_out, mask_grad), token = y.finish(
        token,
        gradients_y,
        place_y,
        True,
        LONG,
        (tail_sum, mask_got),
        [shape((WIDTH,), F32)],
        mask_output,
    )
    output = jnp.where(swaps, both_got[0], output)
    gh = jnp.where(swaps, both_got[1], gh)

    g_qv, g_bo, g_n1g, g_n1b, g_bu, g_bd, g_n2g, g_n2b = out_small
    return (
        output.reshape(1, 2, LENGTH, WIDTH),
        gh.reshape(1, 2, LENGTH, WIDTH),
        mask_grad,
        g_qkv,
        g_qv,
        g_out,
        g_bo,
        g_n1g,
        g_n1b,
        g_up,
        g_bu,
        g_down,
        g_bd,
        g_n2g,
        g_n2b,
    )


def solution(mesh):
    in_specs = (
        P(None, "dp", None, None),
        P(None, "dp", None, None),
        P(None, "dp"),
        P(None, "dp", None),
        P(),
        P("section", None),
        P("section"),
        P("section", None),
        P("section"),
        P("section"),
        P("section"),
        P("section", None),
        P("section"),
        P("section", None),
        P("section"),
        P("section"),
        P("section"),
    )
    out_specs = (
        P("section", "dp", None, None),
        P("section", "dp", None, None),
        P(),
        P("section", None),
        P("section"),
        P("section", None),
        P("section"),
        P("section"),
        P("section"),
        P("section", None),
        P("section"),
        P("section", None),
        P("section"),
        P("section"),
        P("section"),
    )
    return jax.shard_map(
        per_device, mesh=mesh, in_specs=in_specs, out_specs=out_specs, check_vma=False
    )
```

```python
import functools
import math

import jax
import jax.numpy as jnp
from jax import lax
from jax.experimental import pallas as pl
from jax.experimental.pallas import tpu as pltpu
from jax.sharding import PartitionSpec as P

EPSILON = 1e-05
F32 = jnp.float32
LOW = jnp.bfloat16
WIDTH = 768
LENGTH = 160
ROWS = 320
HIDDEN = 3072
PAIRS = 6
SCALE = 0.125
SIZES = (768, 384, 384, 384, 1536, 384, 384, 384)
QV, B_OUT, N1G, N1B, B_UP, B_DOWN, N2G, N2B = (sum(SIZES[:at]) for at in range(8))
SMALL = sum(SIZES)
VMEM_LIMIT = 63 * 1024 * 1024
BIG_GRANT = 61 * 1024 * 1024


def dot_nn(left_side, right_side):
    return jnp.dot(left_side, right_side, preferred_element_type=F32)


def dot_nt(left_side, right_side):
    return lax.dot_general(
        left_side, right_side, (((1,), (1,)), ((), ())), preferred_element_type=F32
    )


def dot_tn(left_side, right_side):
    return lax.dot_general(
        left_side, right_side, (((0,), (0,)), ((), ())), preferred_element_type=F32
    )


class Weight:
    def __init__(self, half, own, other, dest, sems, start=True, chunks=1):
        rows, wide = own.shape
        self.dest = dest
        self.wide = wide // chunks
        self.copies = []
        for chunk in range(chunks):
            at = pl.ds(chunk * self.wide, self.wide)
            for side, source in enumerate((own, other)):
                which = half if side == 0 else 1 - half
                place = dest.at[pl.ds(which * rows, rows)]
                if chunks > 1:
                    source, place = source.at[:, at], place.at[:, at]
                self.copies.append(
                    pltpu.make_async_copy(source, place, sems.at[2 * chunk + side])
                )
        if start:
            self.start()

    def start(self):
        for copy in self.copies:
            copy.start()

    def get(self):
        for copy in self.copies:
            copy.wait()
        self.copies = []
        return self.dest[...]

    def chunk(self, index):
        for copy in self.copies[:2]:
            copy.wait()
        self.copies = self.copies[2:]
        return self.dest[:, index * self.wide : (index + 1) * self.wide]


def whole(smalls, at, size):
    return jnp.concatenate([smalls[0:1, at : at + size], smalls[1:2, at : at + size]], axis=1)


def split_heads(tensor):
    lane = lax.broadcasted_iota(jnp.int32, tensor.shape, 1)
    zero = jnp.zeros_like(tensor)
    return jnp.concatenate(
        [jnp.where(lane < 64, tensor, zero), jnp.where(lane < 64, zero, tensor)], axis=0
    )


def join_heads(tensor):
    lane = lax.broadcasted_iota(jnp.int32, (LENGTH, 128), 1)
    return jnp.where(lane < 64, tensor[:LENGTH], tensor[LENGTH:])


def normalize(values):
    center = values - jnp.mean(values, axis=-1, keepdims=True)
    spread = jnp.mean(center * center, axis=-1, keepdims=True)
    inverse = lax.rsqrt(spread + EPSILON)
    return center * inverse, inverse


def normalize_back(upstream, gain, normal, inverse):
    scaled = upstream * gain
    first = jnp.mean(scaled, axis=-1, keepdims=True)
    second = jnp.mean(scaled * normal, axis=-1, keepdims=True)
    return inverse * (scaled - first - normal * second)


def gelu_parts(values):
    size = jnp.abs(values)
    below = 1.0 + (0.3275911 * math.sqrt(0.5)) * size
    t = pl.reciprocal(below, approx=True)
    t = t * (2.0 - below * t)
    series = t * (
        0.5 * 0.254829592
        + t
        * (
            0.5 * -0.284496736
            + t * (0.5 * 1.421413741 + t * (0.5 * -1.453152027 + t * (0.5 * 1.061405429)))
        )
    )
    bell = jnp.exp(-0.5 * values * values)
    tail = series * bell
    share = jnp.where(values >= 0.0, 1.0 - tail, tail)
    return values * share, share + values * bell * (1.0 / math.sqrt(2.0 * math.pi))


def column_sum(values):
    return jnp.sum(values, axis=0, keepdims=True)


def put_halves(target, at, row):
    size = row.shape[1] // 2
    target[0:1, at : at + size] = row[:, :size]
    target[1:2, at : at + size] = row[:, size:]


def places():
    for index in range(2 * PAIRS):
        chain, pair = divmod(index, PAIRS)
        rows = pl.ds(chain * LENGTH, LENGTH)
        yield index, chain, rows, [pl.ds((pair + block * PAIRS) * 128, 128) for block in range(3)]


def attend_body(h, wqkv, wout, smalls, lens, half, qkv, probs, mixed, normal1, inverse1, u, later):
    x = h[...]
    bias = jnp.concatenate(
        [smalls[0:1, :WIDTH], jnp.zeros((1, WIDTH), F32), smalls[1:2, :WIDTH]], axis=1
    )
    for block in range(3):
        at = block * WIDTH
        matrix = wqkv.chunk(block)
        if block == 0:
            for each in later:
                each.start()
        qkv[:, at : at + WIDTH] = (dot_nn(x, matrix) + bias[:, at : at + WIDTH]).astype(LOW)
    for index, chain, rows, (at_q, at_k, at_v) in places():
        scores = dot_nt(qkv[rows, at_k], split_heads(qkv[rows, at_q])) * SCALE
        key = lax.broadcasted_iota(jnp.int32, scores.shape, 0)
        scores = jnp.where(key < lens[half[0], chain], scores, -1000000000.0)
        grown = jnp.exp(scores - jnp.max(scores, axis=0, keepdims=True))
        weights = (grown * (1.0 / jnp.sum(grown, axis=0, keepdims=True))).astype(LOW)
        if probs is not None:
            probs[index] = weights
        mixed[rows, at_q] = join_heads(dot_tn(weights, qkv[rows, at_v])).astype(LOW)
    branch = dot_nn(mixed[...], wout.get()) + whole(smalls, B_OUT, 384)
    normal, inverse = normalize(x.astype(F32) + branch)
    if normal1 is not None:
        normal1[...] = normal
        inverse1[...] = inverse
    u[...] = (normal * whole(smalls, N1G, 384) + whole(smalls, N1B, 384)).astype(LOW)


CHUNK = 1024


def feed_body(u, wup, wdown, smalls, slope, active, normal2, inverse2, y, later=()):
    x = u[...]
    bias = whole(smalls, B_UP, 1536)
    def grow(part, at):
        grown, tangent = gelu_parts(part + bias[:, at : at + CHUNK])
        active[:, at : at + CHUNK] = grown.astype(LOW)
        if slope is not None:
            slope[:, at : at + CHUNK] = tangent.astype(LOW)

    up = wup.chunk(0)
    for each in later:
        each.start()
    grow(dot_nn(x, up), 0)
    up, last = wup.chunk(1), wup.chunk(2)
    grow(dot_nn(x, up), CHUNK)
    part = dot_nn(x, last)
    down = wdown.get()
    grow(part, 2 * CHUNK)
    total = x.astype(F32) + whole(smalls, B_DOWN, 384) + dot_nn(active[...], down)
    normal, inverse = normalize(total)
    if normal2 is not None:
        normal2[...] = normal
        inverse2[...] = inverse
    y[...] = (normal * whole(smalls, N2G, 384) + whole(smalls, N2B, 384)).astype(LOW)


def top_back_body(up, smalls, normal2, inverse2, gr2, gz, gsmall):
    normal = normal2[...]
    put_halves(gsmall, N2G, column_sum(up * normal))
    put_halves(gsmall, N2B, column_sum(up))
    grad = normalize_back(up, whole(smalls, N2G, 384), normal, inverse2[...])
    z = grad.astype(LOW)
    gz[...] = z
    put_halves(gsmall, B_DOWN, column_sum(z.astype(F32)))
    gr2[...] = grad


def feed_back_body(gr2, gz, wup, wdown, smalls, slope, normal1, inverse1, ga, gr1, gb, gsmall):
    z = gz[...]
    down = wdown.get()
    sums = []
    for at in range(0, HIDDEN, CHUNK):
        inner = dot_nt(z, down[at : at + CHUNK, :]) * slope[:, at : at + CHUNK].astype(F32)
        a = inner.astype(LOW)
        ga[:, at : at + CHUNK] = a
        sums.append(column_sum(a.astype(F32)))
    put_halves(gsmall, B_UP, jnp.concatenate(sums, axis=1))
    up = gr2[...] + dot_nt(ga[...], wup.get())
    normal = normal1[...]
    put_halves(gsmall, N1G, column_sum(up * normal))
    put_halves(gsmall, N1B, column_sum(up))
    grad = normalize_back(up, whole(smalls, N1G, 384), normal, inverse1[...])
    gr1[...] = grad
    b = grad.astype(LOW)
    gb[...] = b
    put_halves(gsmall, B_OUT, column_sum(b.astype(F32)))


def heads_back_body(gb, wout, qkv, probs, gqkv, gqv, go):
    go[...] = dot_nt(gb[...], wout.get()).astype(LOW)
    for index, chain, rows, (at_q, at_k, at_v) in places():
        k = qkv[rows, at_k]
        g = split_heads(go[rows, at_q])
        weights = probs[index]
        wide = weights.astype(F32)
        inner = dot_nt(qkv[rows, at_v], g)
        inner = wide * (inner - jnp.sum(wide * inner, axis=0, keepdims=True))
        s = inner.astype(LOW)
        gqkv[rows, at_q] = (join_heads(dot_tn(s, k)) * SCALE).astype(LOW)
        gqkv[rows, at_k] = (dot_nn(s, split_heads(qkv[rows, at_q])) * SCALE).astype(LOW)
        gqkv[rows, at_v] = dot_nn(weights, g).astype(LOW)
    if gqv is not None:
        gqv[0:1, :] = column_sum(gqkv[:, :WIDTH].astype(F32))
        gqv[1:2, :] = column_sum(gqkv[:, 2 * WIDTH :].astype(F32))


def span_rows(spans, half):
    row = lax.broadcasted_iota(jnp.int32, (ROWS, 1), 0)
    inside = row < 0
    for chain in range(2):
        start = spans[half[0], chain, 0] + chain * LENGTH
        end = spans[half[0], chain, 1] + chain * LENGTH
        inside = inside | ((row >= start) & (row < end))
    return inside


def pick_halves(half, own, other, smalls):
    low = half[0] == 0
    smalls[0:1, :] = jnp.where(low, own[:, :SMALL], other[:, :SMALL])
    smalls[1:2, :] = jnp.where(low, other[:, :SMALL], own[:, :SMALL])


VMEM = pl.BlockSpec(memory_space=pltpu.VMEM)
SMEM = pl.BlockSpec(memory_space=pltpu.SMEM)
ANY = pl.BlockSpec(memory_space=pl.ANY)
HBM = pl.BlockSpec(memory_space=pltpu.HBM)
SMALL_SCRATCH = pltpu.VMEM((2, SMALL), F32)
QKV_SHAPE = (ROWS, 3 * WIDTH)
PROBS_SHAPE = (2 * PAIRS, LENGTH, 2 * LENGTH)
ROW_SHAPE = (ROWS, WIDTH)
FEED_SHAPE = (ROWS, HIDDEN)
MACS = ROWS * WIDTH * WIDTH * 2
ATTEND_WEIGHTS = [pltpu.VMEM((WIDTH, 3 * WIDTH), LOW), pltpu.VMEM((WIDTH, WIDTH), LOW)]
FEED_WEIGHTS = [pltpu.VMEM((WIDTH, HIDDEN), LOW), pltpu.VMEM((HIDDEN, WIDTH), LOW)]


def shape(dims, kind=LOW):
    return jax.ShapeDtypeStruct(dims, kind)


def enter_cotangent(half, own, swapped, raw, sem):
    @pl.when(half[0] == 0)
    def _():
        pltpu.make_async_copy(own.at[0], raw, sem).start()

    @pl.when(half[0] == 1)
    def _():
        pltpu.make_async_copy(swapped.at[1], raw, sem).start()

    return pltpu.make_async_copy(swapped.at[1], raw, sem)


def kernel_call(body, ins, outs, scratch, flops, moved, name, out_specs=None, grant=VMEM_LIMIT):
    return pl.pallas_call(
        body,
        in_specs=ins,
        out_specs=out_specs or [VMEM] * len(outs),
        out_shape=outs,
        scratch_shapes=scratch,
        compiler_params=pltpu.CompilerParams(vmem_limit_bytes=grant),
        cost_estimate=pl.CostEstimate(flops=flops, bytes_accessed=moved, transcendentals=0),
        name=name,
    )


def attend_first(inputs, half, lens, spans, weights, smalls):
    def body(x, half, lens, spans, so, sp, qo, qp, oo, op, u, h, raw, small, qkv, mixed, wq, wo, sems):
        enter = pltpu.make_async_copy(x.at[half[0]], raw, sems.at[2, 0])
        enter.start()
        wqkv = Weight(half[0], qo, qp, wq, sems.at[0], True, 3)
        wout = Weight(half[0], oo, op, wo, sems.at[1], False)
        pick_halves(half, so, sp, small)
        enter.wait()
        mask = so[:, SMALL:].astype(LOW)
        h[...] = jnp.where(span_rows(spans, half), mask, raw[...].reshape(ROWS, WIDTH))
        attend_body(h, wqkv, wout, small, lens, half, qkv, None, mixed, None, None, u, [wout])

    return kernel_call(
        body,
        [ANY, SMEM, SMEM, SMEM, VMEM, VMEM] + [ANY] * 4,
        [shape(ROW_SHAPE), shape(ROW_SHAPE)],
        [
            pltpu.VMEM((2, LENGTH, WIDTH), LOW),
            SMALL_SCRATCH,
            pltpu.VMEM(QKV_SHAPE, LOW),
            pltpu.VMEM(ROW_SHAPE, LOW),
            *ATTEND_WEIGHTS,
            pltpu.SemaphoreType.DMA((3, 6)),
        ],
        40 * MACS,
        80000000,
        "attend_first",
    )(inputs, half, lens, spans, *smalls, *weights[0], *weights[1])


def feed_first(u, half, weights, smalls):
    def body(u, half, so, sp, uo, up, do, dp, y, small, active, wu, wd, sems):
        wup = Weight(half[0], uo, up, wu, sems.at[0], True, 3)
        wdown = Weight(half[0], do, dp, wd, sems.at[1], False)
        pick_halves(half, so, sp, small)
        feed_body(u, wup, wdown, small, None, active, None, None, y, [wdown])

    return kernel_call(
        body,
        [VMEM, SMEM, VMEM, VMEM] + [ANY] * 4,
        [shape(ROW_SHAPE)],
        [
            SMALL_SCRATCH,
            pltpu.VMEM(FEED_SHAPE, LOW),
            *FEED_WEIGHTS,
            pltpu.SemaphoreType.DMA((2, 6)),
        ],
        8 * MACS,
        14000000,
        "feed_first",
    )(u, half, *smalls, *weights[2], *weights[3])[0]


KEPT = [
    shape(ROW_SHAPE),
    shape(QKV_SHAPE),
    shape(PROBS_SHAPE),
    shape(ROW_SHAPE),
    shape(ROW_SHAPE, F32),
    shape((ROWS, 1), F32),
    shape(ROW_SHAPE),
    shape(FEED_SHAPE),
    shape(FEED_SHAPE),
    shape(ROW_SHAPE, F32),
    shape((ROWS, 1), F32),
    shape(ROW_SHAPE),
]


def middle(h0, received, cotangent, swapped, half, first, lens, weights, smalls):
    def body(h0, received, cot, swap, half, first, lens, so, sp, qo, qp, oo, op, uo, up, do, dp, *rest):
        outs, rest = rest[: len(KEPT)], rest[len(KEPT) :]
        both, rest = rest[0], rest[1:]
        gh, small, gr2, gz, ga, gr1, gb, gsmall, gqkv, go, raw, wq, wo, wu, wd = rest[:15]
        keeps, sems, out_sems, raw_sem = rest[15:-3], *rest[-3:]
        h, qkv, probs, mixed, normal1, inverse1, u, slope, active, normal2, inverse2, y = keeps
        wqkv = Weight(half[0], qo, qp, wq, sems.at[0], True, 3)
        wout = Weight(half[0], oo, op, wo, sems.at[1])
        wup = Weight(half[0], uo, up, wu, sems.at[2], True, 3)
        wdown = Weight(half[0], do, dp, wd, sems.at[3])
        enter = enter_cotangent(half, cot, swap, raw, raw_sem)
        pick_halves(half, so, sp, small)
        leaving = []

        def leave(places):
            for place in places:
                copy = pltpu.make_async_copy(keeps[place], outs[place], out_sems.at[place])
                copy.start()
                leaving.append(copy)

        h[...] = jnp.where(first[0] > 0, h0[...], received[...])
        attend_body(
            h, wqkv, wout, small, lens, half, qkv, probs, mixed, normal1, inverse1, u, ()
        )
        leave(range(7))
        feed_body(u, wup, wdown, small, slope, active, normal2, inverse2, y)
        leave(range(7, 12))
        output = pltpu.make_async_copy(y, both.at[0], out_sems.at[len(KEPT)])
        output.start()
        leaving.append(output)
        enter.wait()
        upstream = raw[...].reshape(ROWS, WIDTH).astype(F32)
        top_back_body(upstream, small, normal2, inverse2, gr2, gz, gsmall)
        feed_back_body(gr2, gz, wup, wdown, small, slope, normal1, inverse1, ga, gr1, gb, gsmall)
        heads_back_body(gb, wout, qkv, probs, gqkv, None, go)
        gh[...] = (gr1[...] + dot_nt(gqkv[...], wqkv.get())).astype(LOW)
        output = pltpu.make_async_copy(gh, both.at[1], out_sems.at[len(KEPT) + 1])
        output.start()
        leaving.append(output)
        for copy in leaving:
            copy.wait()

    return kernel_call(
        body,
        [VMEM, VMEM, ANY, ANY, SMEM, SMEM, SMEM, VMEM, VMEM] + [ANY] * 8,
        KEPT + [shape((2, ROWS, WIDTH)), shape(ROW_SHAPE)],
        [
            SMALL_SCRATCH,
            pltpu.VMEM(ROW_SHAPE, F32),
            pltpu.VMEM(ROW_SHAPE, LOW),
            pltpu.VMEM(FEED_SHAPE, LOW),
            pltpu.VMEM(ROW_SHAPE, F32),
            pltpu.VMEM(ROW_SHAPE, LOW),
            SMALL_SCRATCH,
            pltpu.VMEM(QKV_SHAPE, LOW),
            pltpu.VMEM(ROW_SHAPE, LOW),
            pltpu.VMEM((2, LENGTH, WIDTH), LOW),
            *ATTEND_WEIGHTS,
            *FEED_WEIGHTS,
            *[pltpu.VMEM(kept.shape, kept.dtype) for kept in KEPT],
            pltpu.SemaphoreType.DMA((4, 6)),
            pltpu.SemaphoreType.DMA((len(KEPT) + 2,)),
            pltpu.SemaphoreType.DMA,
        ],
        24 * MACS,
        45000000,
        "middle",
        [ANY] * len(KEPT) + [ANY, VMEM],
        BIG_GRANT,
    )(
        h0, received, cotangent, swapped, half, first, lens, *smalls,
        *weights[0], *weights[1], *weights[2], *weights[3],
    )


MIB = 1024 * 1024


def half_columns(ref, which):
    size = ref.shape[1] // 2
    return ref[:, pl.ds(pl.multiple_of(which * size, 128), size)]


class Arriving:
    def __init__(self, pairs, sems):
        self.copies = {}
        for place, (name, source, dest) in enumerate(pairs):
            copy = pltpu.make_async_copy(source, dest, sems.at[place])
            copy.start()
            self.copies[name] = (copy, dest)

    def get(self, name):
        copy, dest = self.copies[name]
        copy.wait()
        return dest


class Leaving:
    def __init__(self, sems):
        self.sems = sems
        self.copies = []

    def send(self, source, target):
        copy = pltpu.make_async_copy(source, target, self.sems.at[len(self.copies)])
        copy.start()
        self.copies.append(copy)

    def wait(self):
        for copy in self.copies:
            copy.wait()


def send_folded(leaving, local, target, left_side, right):
    for block in range(right.shape[1] // WIDTH):
        rows = pl.ds(block * 384, 384)
        grad = dot_tn(left_side, right[:, block * WIDTH : (block + 1) * WIDTH])
        local[rows, :] = grad.astype(LOW)
        leaving.send(local.at[rows], target.at[rows])


TOKEN = shape((8, 128), F32)
GRAD_SHAPE = (1536, WIDTH)
GRAD_SCRATCH = pltpu.VMEM(GRAD_SHAPE, LOW)


def back_feed(cotangent, swapped, returned, half, first, weights, smalls, kept):
    u, slope, active, n1, i1, n2, i2 = kept

    def body(cot, swap, returned, half, first, so, sp, i1, n2, i2, uo, up, do, dp, u, slope, active, n1, *rest):
        outs, rest = rest[:8], rest[8:]
        down_other, down_own, up_other, up_own, gr1, gb, gsmall, token = outs
        gr2, gz, ga, v0, v1, v2, v3, small, raw, wu, wd, vu, vs, va, vn, sems, in_sems, out_sems = rest
        enter = enter_cotangent(half, cot, swap, raw, sems.at[2, 0])
        arriving = Arriving([("active", active, va)], in_sems)
        wdown = Weight(half[0], do, dp, wd, sems.at[1])
        later = Arriving(
            [("slope", slope, vs), ("normal", n1, vn), ("u", u, vu)],
            in_sems.at[pl.ds(1, 3)],
        )
        wup = Weight(half[0], uo, up, wu, sems.at[0])
        pick_halves(half, so, sp, small)
        enter.wait()
        upstream = jnp.where(first[0] > 0, returned[...], raw[...].reshape(ROWS, WIDTH))
        top_back_body(upstream.astype(F32), small, n2, i2, gr2, gz, gsmall)
        leaving = Leaving(out_sems)
        arriving.get("active")
        for which, local, target in ((1 - half[0], v0, down_other), (half[0], v1, down_own)):
            local[...] = dot_tn(half_columns(va, which), gz[...]).astype(LOW)
            leaving.send(local, target)
        later.get("slope")
        later.get("normal")
        feed_back_body(gr2, gz, wup, wdown, small, vs, vn, i1, ga, gr1, gb, gsmall)
        later.get("u")
        for which, local, target in ((1 - half[0], v2, up_other), (half[0], v3, up_own)):
            send_folded(leaving, local, target, half_columns(vu, which), ga)
        token[...] = jnp.zeros(token.shape, F32)
        leaving.wait()

    return kernel_call(
        body,
        [ANY, ANY, VMEM, SMEM, SMEM] + [VMEM] * 5 + [ANY] * 8,
        [shape(GRAD_SHAPE)] * 4
        + [shape(ROW_SHAPE, F32), shape(ROW_SHAPE), shape((2, SMALL), F32), TOKEN],
        [
            pltpu.VMEM(ROW_SHAPE, F32),
            pltpu.VMEM(ROW_SHAPE, LOW),
            pltpu.VMEM(FEED_SHAPE, LOW),
            *[GRAD_SCRATCH] * 4,
            SMALL_SCRATCH,
            pltpu.VMEM((2, LENGTH, WIDTH), LOW),
            *FEED_WEIGHTS,
            pltpu.VMEM(ROW_SHAPE, LOW),
            pltpu.VMEM(FEED_SHAPE, LOW),
            pltpu.VMEM(FEED_SHAPE, LOW),
            pltpu.VMEM(ROW_SHAPE, F32),
            pltpu.SemaphoreType.DMA((3, 2)),
            pltpu.SemaphoreType.DMA((4,)),
            pltpu.SemaphoreType.DMA((10,)),
        ],
        200 * MACS,
        600000000,
        "back_feed",
        [ANY] * 4 + [VMEM] * 4,
        BIG_GRANT,
    )(
        cotangent, swapped, returned, half, first, *smalls, i1, n2, i2, *weights[2], *weights[3],
        u, slope, active, n1,
    )


def back_attend(gb, gr1, half, first, spans, weights, gsmall, h, qkv, probs, mixed):
    def body(gb, half, first, spans, gsmall, oo, op, qo, qp, gr1, h, qkv, probs, mixed, *rest):
        outs, rest = rest[:6], rest[6:]
        other, own, small_other, small_own, gh, token = outs
        gqkv, go, gqv, vother, vown, wo, wq, vr, vh, vq, vp, vm, sems, in_sems, out_sems = rest
        wout = Weight(half[0], oo, op, wo, sems.at[0])
        arriving = Arriving([("qkv", qkv, vq), ("probs", probs, vp)], in_sems)
        wqkv = Weight(half[0], qo, qp, wq, sems.at[1], False)
        arriving.get("qkv")
        arriving.get("probs")
        wqkv.start()
        late = Arriving([("h", h, vh), ("mixed", mixed, vm), ("gr1", gr1, vr)], in_sems.at[pl.ds(2, 3)])
        heads_back_body(gb, wout, vq, vp, gqkv, gqv, go)
        leaving = Leaving(out_sems)
        late.get("h")
        late.get("mixed")
        for which, local, target in ((1 - half[0], vother, other), (half[0], vown, own)):
            send_folded(leaving, local, target, half_columns(vh, which), gqkv)
            local[1152:, :] = dot_tn(half_columns(vm, which), gb[...]).astype(LOW)
            leaving.send(local.at[pl.ds(1152, 384)], target.at[pl.ds(1152, 384)])
        late.get("gr1")
        full = vr[...] + dot_nt(gqkv[...], wqkv.get())
        dropped = span_rows(spans, half) & (first[0] > 0)
        zero = jnp.zeros_like(full)
        gh[...] = jnp.where(dropped, zero, full).astype(LOW)
        gmask = column_sum(jnp.where(dropped, full, zero))
        for which, target in ((1 - half[0], small_other), (half[0], small_own)):
            target[:, :WIDTH] = gqv[pl.ds(which, 1), :]
            target[:, WIDTH:SMALL] = gsmall[pl.ds(which, 1), WIDTH:]
            target[:, SMALL:] = gmask
        token[...] = jnp.zeros(token.shape, F32)
        leaving.wait()

    return kernel_call(
        body,
        [VMEM, SMEM, SMEM, SMEM, VMEM] + [ANY] * 9,
        [
            shape(GRAD_SHAPE),
            shape(GRAD_SHAPE),
            shape((1, SMALL + WIDTH), F32),
            shape((1, SMALL + WIDTH), F32),
            shape(ROW_SHAPE),
            TOKEN,
        ],
        [
            pltpu.VMEM(QKV_SHAPE, LOW),
            pltpu.VMEM(ROW_SHAPE, LOW),
            pltpu.VMEM((2, WIDTH), F32),
            GRAD_SCRATCH,
            GRAD_SCRATCH,
            ATTEND_WEIGHTS[1],
            ATTEND_WEIGHTS[0],
            pltpu.VMEM(ROW_SHAPE, F32),
            pltpu.VMEM(ROW_SHAPE, LOW),
            pltpu.VMEM(QKV_SHAPE, LOW),
            pltpu.VMEM(PROBS_SHAPE, LOW),
            pltpu.VMEM(ROW_SHAPE, LOW),
            pltpu.SemaphoreType.DMA((2, 2)),
            pltpu.SemaphoreType.DMA((5,)),
            pltpu.SemaphoreType.DMA((8,)),
        ],
        180 * MACS,
        400000000,
        "back_attend",
        [ANY, ANY] + [VMEM] * 4,
    )(gb, half, first, spans, gsmall, *weights[1], *weights[0], gr1, h, qkv, probs, mixed)


TAIL = 16
BLOCK = 96


def add_rows(target, sources, at, rows):
    for start in range(0, rows, BLOCK):
        size = min(BLOCK, rows - start)
        place = pl.ds(at + start, size)
        if not isinstance(at, int):
            place = pl.ds(pl.multiple_of(at + start, 16), size)
        if len(sources) == 2:
            target[start : start + size, :] = sources[0][place, :] + sources[1][place, :]
            continue
        total = sources[0][place, :].astype(F32)
        for source in sources[1:]:
            total = total + source[place, :].astype(F32)
        target[start : start + size, :] = total.astype(LOW)


LONG = 30000000000


def ordered(
    name, body, ins, outs, where, after, out_specs=None, scratch=(), in_specs=None, grant=16, aliases=None,
    flops=LONG,
):
    count, made = len(ins), len(outs)

    def kernel(where, after, *refs):
        refs[count + made][...] = jnp.zeros(TOKEN.shape, F32)
        body(where, refs[:count], refs[count : count + made] + refs[count + made + 1 :])

    result = pl.pallas_call(
        kernel,
        in_specs=[SMEM, HBM] + (in_specs or [VMEM] * count),
        out_specs=(out_specs or [VMEM] * made) + [VMEM],
        out_shape=list(outs) + [TOKEN],
        scratch_shapes=list(scratch),
        input_output_aliases=aliases or {},
        compiler_params=pltpu.CompilerParams(vmem_limit_bytes=grant * MIB),
        cost_estimate=pl.CostEstimate(flops=flops, bytes_accessed=flops, transcendentals=0),
        name=name,
    )(where, after, *ins)
    return result[:made], result[made]


def partner(x, axis, bit):
    return lax.ppermute(x, axis, [(i, i ^ 1 << bit) for i in range(lax.axis_size(axis))])


def moved_on(index, axis, steps):
    z, x, y = index // 8, index // 2 % 4, index % 2
    if axis == "z":
        z = steps(z)
    elif axis == "x":
        x = steps(x)
    else:
        y = steps(y)
    return z * 8 + x * 2 + y


def send_along(value, axes, place):
    pairs = []
    for section in range(4):
        for index in range(32):
            to = moved_on(index, axes[section % 2], place)
            pairs.append((section * 32 + index, section * 32 + to))
    return lax.ppermute(value, ("section", "dp"), pairs)


def exchange(value, part, step):
    flip = 1 if part == step else 3
    return send_along(value, "zx", lambda place: place ^ flip)


def turn(value, steps):
    return send_along(value, "xz", lambda place: (place + steps) % 4)


def across_y(value):
    return send_along(value, "yy", lambda place: place ^ 1)


def swap_core_one(value):
    pairs = [
        (section * 32 + index, section * 32 + (index ^ 1)) for section in (1, 3) for index in range(32)
    ]
    return lax.ppermute(value, ("section", "dp"), pairs)


def between_layers(value, back):
    pairs = []
    for core in range(2):
        for index in range(32):
            pair = (core * 32 + index, (core + 2) * 32 + (index ^ core))
            pairs.append(pair[::-1] if back else pair)
    return lax.ppermute(value, ("section", "dp"), pairs)


def own_places(core):
    index = lax.axis_index("dp")
    z, x = index // 8, index // 2 % 4
    ring = jnp.where(core == 0, z, x)
    high = ring // 2
    low = high ^ (ring % 2)
    table = [low, high, high, low, jnp.where(core == 0, x, z)]
    return jnp.stack(table).astype(jnp.int32)


def row_shapes(*counts):
    return [shape((count, WIDTH)) for count in counts]


def add_tail(target, rows, sources, at, extra):
    if extra:
        total = sources[0][at : at + extra, :].astype(F32)
        for source in sources[1:]:
            total = total + source[at : at + extra, :].astype(F32)
        target[rows : rows + extra, :] = total.astype(LOW)


class Chain:
    def __init__(self, name, places, tail=0):
        self.name = name
        self.places = places
        self.tail = (0, tail)
        self.keep = [None, None]
        self.got = [None, None]

    def kernel(self, name, body, ins, outs, token, *more, **named):
        return ordered(self.name + name, body, ins, outs, self.places, token, *more, **named)

    def pairs(self):
        return (self.keep[0], self.got[0], self.keep[1], self.got[1])

    def first_sum(self, name, sent, token):
        sources, half_rows, tails = self.sources, self.rows, self.tail

        def body(places, ins, refs):
            outs, held, sems = refs[:2], refs[2:6], refs[6]
            copies = []
            for index in range(4):
                bit, at = places[2 * (index // 2)], sources[index // 2][2]
                which = 1 - bit if sent else bit
                rows = pl.ds(pl.multiple_of(at + which * half_rows, 16), half_rows)
                copy = pltpu.make_async_copy(ins[index].at[rows], held[index], sems.at[index])
                copy.start()
                copies.append(copy)
            for part in range(2):
                copies[2 * part].wait()
                copies[2 * part + 1].wait()
                add_rows(outs[part], held[2 * part : 2 * part + 2], 0, half_rows)
                if tails[part]:
                    outs[part][half_rows:, :] = self.tail_body(ins[4:])

        arrays = [array for own, got, _ in sources for array in (own, got)]
        return self.kernel(
            name,
            body,
            (*arrays, *self.tail_ins),
            row_shapes(half_rows + tails[0], half_rows + tails[1]),
            token,
            scratch=(*[pltpu.VMEM((half_rows, WIDTH), LOW)] * 4, pltpu.SemaphoreType.DMA((4,))),
            in_specs=[HBM] * 4 + [VMEM] * len(self.tail_ins),
            grant=63 if sent else 46,
            flops=LONG if sent else 0,
        )

    def start(self, sources, rows, token, tail_ins=(), tail_body=None):
        self.rows, self.sources = rows // 2, sources
        self.tail_ins, self.tail_body = tuple(tail_ins), tail_body
        sends, token = self.first_sum("send", True, token)
        self.got = [exchange(sends[part], part, 0) for part in range(2)]
        return token

    def hold(self, token):
        keeps, token = self.first_sum("keep", False, token)
        self.keep = list(keeps)
        return token

    def halve(self, token, flops):
        self.rows //= 2
        rows, tails = self.rows, self.tail

        def body(places, ins, outs):
            for part in range(2):
                bit = places[2 * part + 1]
                pair = ins[2 * part : 2 * part + 2]
                for target, which in ((outs[2 * part + 1], 1 - bit), (outs[2 * part], bit)):
                    add_rows(target, pair, which * rows, rows)
                    add_tail(target, rows, pair, 2 * rows, tails[part])

        counts = [rows + tails[0]] * 2 + [rows + tails[1]] * 2
        outs, token = self.kernel(
            "halve", body, self.pairs(), row_shapes(*counts), token, flops=flops
        )
        for part in range(2):
            self.keep[part] = outs[2 * part]
            self.got[part] = exchange(outs[2 * part + 1], part, 1)
        return token

    def cross(self, token):
        whole_rows, extra = self.rows, self.tail[1]
        rows = whole_rows // 2

        def body(places, ins, refs):
            outs, total = refs[:4], refs[4]
            add_rows(total.at[pl.ds(0, whole_rows)], ins[:2], 0, whole_rows)
            add_rows(total.at[pl.ds(whole_rows, whole_rows)], ins[2:], 0, whole_rows)
            for steps in range(4):
                quarter = (places[4] + steps) % 4
                outs[steps][:rows, :] = total[pl.ds(pl.multiple_of(quarter * rows, 16), rows), :]
                add_tail(outs[steps], rows, ins[2:], whole_rows, extra)

        (self.own, *sends), token = self.kernel(
            "cross",
            body,
            self.pairs(),
            row_shapes(*[rows + extra] * 4),
            token,
            None,
            (pltpu.VMEM((2 * whole_rows, WIDTH), LOW),),
        )
        self.rows = rows
        self.ring = [turn(send, steps) for steps, send in zip((1, 2, 3), sends)]
        return token

    def across(self, token):
        rows = self.rows + self.tail[1]

        def body(places, ins, outs):
            add_rows(outs[0], ins, 0, rows)

        (self.own,), token = self.kernel(
            "across", body, (self.own, *self.ring), row_shapes(rows), token
        )
        self.other = across_y(self.own)
        return token

    def total(self, token, more_outs=(), more_body=None):
        rows, extra = self.rows, self.tail[1]

        def body(places, ins, outs):
            add_rows(outs[0], ins, 0, rows)
            if extra:
                add_rows(outs[1], ins, rows, extra)
                more_body(outs[1][...].astype(F32), outs[2:])

        counts = [rows] + ([extra] if extra else [])
        outs, token = self.kernel(
            "total", body, (self.own, self.other), row_shapes(*counts) + list(more_outs), token
        )
        self.own = outs[0]
        self.tail_sum = outs[1] if extra else None
        self.ring = [turn(self.own, steps) for steps in (1, 2, 3)]
        return outs[2:], token

    def back(self, token, more_ins=(), more_outs=(), more_body=None):
        rows = self.rows

        def body(places, ins, refs):
            outs, total = refs[:-1], refs[-1]
            for steps in range(4):
                quarter = (places[4] - steps + 4) % 4
                total[pl.ds(pl.multiple_of(quarter * rows, 16), rows), :] = ins[steps][...]
            outs[0][...] = total[: 2 * rows, :]
            outs[1][...] = total[2 * rows :, :]
            if more_body is not None:
                more_body(ins[4:], outs[2:])

        outs, token = self.kernel(
            "back",
            body,
            (self.own, *self.ring) + tuple(more_ins),
            row_shapes(2 * rows, 2 * rows) + list(more_outs),
            token,
            None,
            (pltpu.VMEM((4 * rows, WIDTH), LOW),),
        )
        self.rows = 2 * rows
        self.keep = list(outs[:2])
        self.got = [exchange(self.keep[part], part, 1) for part in range(2)]
        return outs[2:], token

    def double(self, token, flops):
        rows = self.rows

        def body(places, ins, outs):
            for part in range(2):
                bit = places[2 * part + 1]
                for which, source in ((bit, ins[2 * part]), (1 - bit, ins[2 * part + 1])):
                    outs[part][pl.ds(pl.multiple_of(which * rows, 16), rows), :] = source[...]

        outs, token = self.kernel(
            "double", body, self.pairs(), row_shapes(2 * rows, 2 * rows), token, flops=flops
        )
        self.rows = 2 * rows
        self.keep = list(outs)
        self.got = [exchange(self.keep[part], part, 0) for part in range(2)]
        return token

    def finish(self, token, outs, place, got, flops, more_ins=(), more_outs=(), more_body=None):
        rows = self.rows
        mine = tuple(self.got if got else self.keep)
        kept = tuple(outs) if got else ()

        def body(places, ins, refs):
            targets, wide, sems = refs[: len(outs)], refs[-2], refs[-1]
            if more_body is not None:
                more_body(ins[2 + len(kept) :], refs[len(outs) : -2])
            waits = []
            for part in range(2):
                bit = places[2 * part]
                half = 1 - bit if got else bit
                wide[part] = ins[part][...].astype(F32)
                at = 0
                for size, starts in place(targets, part, half):
                    source, sem = wide.at[part, pl.ds(at, size)], sems.at[len(waits)]
                    starts(source, sem)
                    waits.append((size, source, sem))
                    at += size
            for size, source, sem in waits:
                pltpu.make_async_copy(source, wide.at[0, pl.ds(0, size)], sem).wait()

        return self.kernel(
            "finish",
            body,
            mine + kept + tuple(more_ins),
            [shape(out.shape, F32) for out in outs] + list(more_outs),
            token,
            out_specs=[ANY] * len(outs) + [VMEM] * len(more_outs),
            scratch=(pltpu.VMEM((2, rows, WIDTH), F32), pltpu.SemaphoreType.DMA((4,))),
            in_specs=[VMEM] * 2 + [ANY] * len(kept) + [VMEM] * len(more_ins),
            grant=24,
            flops=flops,
            aliases={4 + index: index for index in range(len(kept))},
        )


def copy_to(target):
    return lambda source, sem: pltpu.make_async_copy(source, target, sem).start()


def block_columns(block):
    return pl.ds(pl.multiple_of(block * WIDTH, 128), WIDTH)


def place_x(refs, part, half):
    down, up = refs
    if part == 0:
        return [(768, copy_to(down.at[pl.ds(pl.multiple_of(half * 768, 8), 768)]))]
    return [(384, copy_to(up.at[:, block_columns(2 * half + block)])) for block in range(2)]


def place_y(refs, part, half):
    qkv, out = refs
    if part == 0:
        return [(384, copy_to(qkv.at[:, block_columns(half)]))]

    def starts(source, sem):
        @pl.when(half == 0)
        def _():
            copy_to(qkv.at[:, block_columns(2)])(source, sem)

        @pl.when(half == 1)
        def _():
            copy_to(out)(source, sem)

    return [(384, starts)]


def pack_vectors(vectors):
    size = sum(vector.shape[0] for vector in vectors)
    total = jnp.zeros((size,), F32)
    at = 0
    for vector in vectors:
        total = total + jnp.pad(vector.astype(F32), (at, size - at - vector.shape[0]))
        at += vector.shape[0]
    return total.reshape(1, size)


def per_device(
    inputs,
    cotangent,
    lengths,
    cdr_spans,
    mask_vector,
    w_qkv,
    qv_bias,
    w_out,
    b_out,
    norm1_gain,
    norm1_bias,
    w_up,
    b_up,
    w_down,
    b_down,
    norm2_gain,
    norm2_bias,
):
    section_index = lax.axis_index("section")
    core = section_index % 2
    half = core.astype(jnp.int32).reshape(1)
    first = (section_index < 2).astype(jnp.int32).reshape(1)
    places = own_places(core)
    small = pack_vectors(
        (
            qv_bias,
            b_out,
            norm1_gain,
            norm1_bias,
            b_up,
            b_down,
            norm2_gain,
            norm2_bias,
            mask_vector,
        )
    )
    small_got = partner(small, "section", 0)
    got_qkv, got_out = partner((w_qkv, w_out), "section", 0)
    w_up, w_down, got_qkv, got_out, small_got = lax.optimization_barrier(
        (w_up, w_down, got_qkv, got_out, small_got)
    )
    smalls = (small, small_got)
    got_up, got_down = partner((w_up, w_down), "section", 0)
    weights = [(w_qkv, got_qkv), (w_out, got_out), (w_up, got_up), (w_down, got_down)]

    swapped = swap_core_one(cotangent)
    lens_got = swap_core_one(lengths)
    swaps = (core == 1) & (section_index >= 2)
    layer_lens = jnp.where(swaps, lens_got, lengths)

    u, h0 = attend_first(inputs, half, lengths, cdr_spans, weights, smalls)
    first_out = feed_first(u, half, weights, smalls)
    received = between_layers(first_out, False)
    kept = middle(h0, received, cotangent, swapped, half, first, layer_lens, weights, smalls)
    h, qkv, probs, mixed, normal1, inverse1, u, slope, active, normal2, inverse2, output = kept[:12]
    returned = between_layers(kept[13], True)

    a_other, a_own, b_other, b_own, gr1, gb, gsmall, token = back_feed(
        cotangent,
        swapped,
        returned,
        half,
        first,
        weights,
        smalls,
        (u, slope, active, normal1, inverse1, normal2, inverse2),
    )
    a_got = partner(a_other, "section", 0)
    b_got = partner(b_other, "section", 0)
    x, y = Chain("x_", places), Chain("y_", places, TAIL)
    y_other, y_own, small_other, small_own, gh, token = back_attend(
        gb, gr1, half, first, cdr_spans, weights, gsmall, h, qkv, probs, mixed
    )
    y_got = partner(y_other, "section", 0)
    small_got = partner(small_other, "section", 0)
    token = x.start([(a_own, a_got, 0), (b_own, b_got, 0)], 1536, token)

    def tail_rows(ins):
        total = ins[0][...] + ins[1][...]
        rows = [total[:, at : at + WIDTH] for at in range(0, SMALL + WIDTH, WIDTH)]
        rows.append(jnp.zeros((TAIL - len(rows), WIDTH), F32))
        return jnp.concatenate(rows, axis=0).astype(LOW)

    token = y.start(
        [(y_own, y_got, 0), (y_own, y_got, 768)], 768, token, (small_own, small_got), tail_rows
    )
    both, token = lax.optimization_barrier((kept[12], token))
    both_got = swap_core_one(both)
    token = x.hold(token)
    token = x.halve(token, 0)
    token = y.hold(token)
    token = y.halve(token, LONG)
    token = x.cross(token)
    token = y.cross(token)
    token = x.across(token)
    token = y.across(token)
    _, token = x.total(token)

    def small_outputs(tail, outs):
        flat = jnp.concatenate([tail[row : row + 1, :] for row in range(6)], axis=1)
        at = 0
        for out, size in zip(outs, SIZES):
            out[...] = flat[0, at : at + size]
            at += size

    out_small, token = y.total(token, [shape((size,), F32) for size in SIZES], small_outputs)
    _, token = x.back(token)

    def mask_output(ins, outs):
        outs[0][...] = ins[0][6, :].astype(F32) + ins[1][6, :].astype(F32)

    _, token = y.back(token)
    gradients_x = [shape((1536, WIDTH), F32), shape((384, HIDDEN), F32)]
    gradients_y = [shape((384, 3 * WIDTH), F32), shape((384, WIDTH), F32)]
    token = x.double(token, LONG)
    gradients_x, token = x.finish(token, gradients_x, place_x, False, LONG)
    token = y.double(token, 0)
    tail_sum, token = lax.optimization_barrier((y.tail_sum, token))
    mask_got = partner(tail_sum, "section", 1)
    gradients_y, token = y.finish(token, gradients_y, place_y, False, 0)
    both_got, token = lax.optimization_barrier((both_got, token))
    (g_down, g_up), token = x.finish(token, gradients_x, place_x, True, LONG)
    (g_qkv, g_out, mask_grad), token = y.finish(
        token,
        gradients_y,
        place_y,
        True,
        LONG,
        (tail_sum, mask_got),
        [shape((WIDTH,), F32)],
        mask_output,
    )
    output = jnp.where(swaps, both_got[0], output)
    gh = jnp.where(swaps, both_got[1], gh)

    g_qv, g_bo, g_n1g, g_n1b, g_bu, g_bd, g_n2g, g_n2b = out_small
    return (
        output.reshape(1, 2, LENGTH, WIDTH),
        gh.reshape(1, 2, LENGTH, WIDTH),
        mask_grad,
        g_qkv,
        g_qv,
        g_out,
        g_bo,
        g_n1g,
        g_n1b,
        g_up,
        g_bu,
        g_down,
        g_bd,
        g_n2g,
        g_n2b,
    )


def solution(mesh):
    in_specs = (
        P(None, "dp", None, None),
        P(None, "dp", None, None),
        P(None, "dp"),
        P(None, "dp", None),
        P(),
        P("section", None),
        P("section"),
        P("section", None),
        P("section"),
        P("section"),
        P("section"),
        P("section", None),
        P("section"),
        P("section", None),
        P("section"),
        P("section"),
        P("section"),
    )
    out_specs = (
        P("section", "dp", None, None),
        P("section", "dp", None, None),
        P(),
        P("section", None),
        P("section"),
        P("section", None),
        P("section"),
        P("section"),
        P("section"),
        P("section", None),
        P("section"),
        P("section", None),
        P("section"),
        P("section"),
        P("section"),
    )
    return jax.shard_map(
        per_device, mesh=mesh, in_specs=in_specs, out_specs=out_specs, check_vma=False
    )
```

```python
import functools
import math

import jax
import jax.numpy as jnp
from jax import lax
from jax.experimental import pallas as pl
from jax.experimental.pallas import tpu as pltpu
from jax.sharding import PartitionSpec as P

EPSILON = 1e-05
F32 = jnp.float32
LOW = jnp.bfloat16
WIDTH = 768
LENGTH = 160
ROWS = 320
HIDDEN = 3072
PAIRS = 6
SCALE = 0.125
SIZES = (768, 384, 384, 384, 1536, 384, 384, 384)
QV, B_OUT, N1G, N1B, B_UP, B_DOWN, N2G, N2B = (sum(SIZES[:at]) for at in range(8))
SMALL = sum(SIZES)
VMEM_LIMIT = 63 * 1024 * 1024
BIG_GRANT = 61 * 1024 * 1024


def dot_nn(left_side, right_side):
    return jnp.dot(left_side, right_side, preferred_element_type=F32)


def dot_nt(left_side, right_side):
    return lax.dot_general(
        left_side, right_side, (((1,), (1,)), ((), ())), preferred_element_type=F32
    )


def dot_tn(left_side, right_side):
    return lax.dot_general(
        left_side, right_side, (((0,), (0,)), ((), ())), preferred_element_type=F32
    )


class Weight:
    def __init__(self, half, own, other, dest, sems, start=True, chunks=1):
        rows, wide = own.shape
        self.dest = dest
        self.wide = wide // chunks
        self.copies = []
        for chunk in range(chunks):
            at = pl.ds(chunk * self.wide, self.wide)
            for side, source in enumerate((own, other)):
                which = half if side == 0 else 1 - half
                place = dest.at[pl.ds(which * rows, rows)]
                if chunks > 1:
                    source, place = source.at[:, at], place.at[:, at]
                self.copies.append(
                    pltpu.make_async_copy(source, place, sems.at[2 * chunk + side])
                )
        if start:
            self.start()

    def start(self):
        for copy in self.copies:
            copy.start()

    def wait(self):
        for copy in self.copies:
            copy.wait()
        self.copies = []

    def get(self):
        self.wait()
        return self.dest[...]

    def chunk(self, index):
        for copy in self.copies[:2]:
            copy.wait()
        self.copies = self.copies[2:]
        return self.dest[:, index * self.wide : (index + 1) * self.wide]


def whole(smalls, at, size):
    return jnp.concatenate([smalls[0:1, at : at + size], smalls[1:2, at : at + size]], axis=1)


def split_heads(tensor):
    lane = lax.broadcasted_iota(jnp.int32, tensor.shape, 1)
    zero = jnp.zeros_like(tensor)
    return jnp.concatenate(
        [jnp.where(lane < 64, tensor, zero), jnp.where(lane < 64, zero, tensor)], axis=0
    )


def join_heads(tensor):
    lane = lax.broadcasted_iota(jnp.int32, (LENGTH, 128), 1)
    return jnp.where(lane < 64, tensor[:LENGTH], tensor[LENGTH:])


def normalize(values):
    center = values - jnp.mean(values, axis=-1, keepdims=True)
    spread = jnp.mean(center * center, axis=-1, keepdims=True)
    inverse = lax.rsqrt(spread + EPSILON)
    return center * inverse, inverse


def normalize_back(upstream, gain, normal, inverse):
    scaled = upstream * gain
    first = jnp.mean(scaled, axis=-1, keepdims=True)
    second = jnp.mean(scaled * normal, axis=-1, keepdims=True)
    return inverse * (scaled - first - normal * second)


def gelu_parts(values):
    size = jnp.abs(values)
    below = 1.0 + (0.3275911 * math.sqrt(0.5)) * size
    t = pl.reciprocal(below, approx=True)
    t = t * (2.0 - below * t)
    series = t * (
        0.5 * 0.254829592
        + t
        * (
            0.5 * -0.284496736
            + t * (0.5 * 1.421413741 + t * (0.5 * -1.453152027 + t * (0.5 * 1.061405429)))
        )
    )
    bell = jnp.exp(-0.5 * values * values)
    tail = series * bell
    share = jnp.where(values >= 0.0, 1.0 - tail, tail)
    return values * share, share + values * bell * (1.0 / math.sqrt(2.0 * math.pi))


def column_sum(values):
    return jnp.sum(values, axis=0, keepdims=True)


def put_halves(target, at, row):
    size = row.shape[1] // 2
    target[0:1, at : at + size] = row[:, :size]
    target[1:2, at : at + size] = row[:, size:]


def places():
    for index in range(2 * PAIRS):
        chain, pair = divmod(index, PAIRS)
        rows = pl.ds(chain * LENGTH, LENGTH)
        yield index, chain, rows, [pl.ds((pair + block * PAIRS) * 128, 128) for block in range(3)]


def attend_body(
    h, wqkv, wout, smalls, lens, half, qkv, probs, mixed, normal1, inverse1, u, later=(), settle=()
):
    x = h[...]
    bias = jnp.concatenate(
        [smalls[0:1, :WIDTH], jnp.zeros((1, WIDTH), F32), smalls[1:2, :WIDTH]], axis=1
    )
    for block in range(3):
        at = block * WIDTH
        matrix = wqkv.chunk(block)
        if block == 0:
            for each in later:
                each.start()
        qkv[:, at : at + WIDTH] = (dot_nn(x, matrix) + bias[:, at : at + WIDTH]).astype(LOW)
    for index, chain, rows, (at_q, at_k, at_v) in places():
        scores = dot_nt(qkv[rows, at_k], split_heads(qkv[rows, at_q])) * SCALE
        key = lax.broadcasted_iota(jnp.int32, scores.shape, 0)
        scores = jnp.where(key < lens[half[0], chain], scores, -1000000000.0)
        grown = jnp.exp(scores - jnp.max(scores, axis=0, keepdims=True))
        weights = (grown * (1.0 / jnp.sum(grown, axis=0, keepdims=True))).astype(LOW)
        if probs is not None:
            probs[index] = weights
        mixed[rows, at_q] = join_heads(dot_tn(weights, qkv[rows, at_v])).astype(LOW)
    for each in settle:
        each.wait()
    branch = dot_nn(mixed[...], wout.get()) + whole(smalls, B_OUT, 384)
    normal, inverse = normalize(x.astype(F32) + branch)
    if normal1 is not None:
        normal1[...] = normal
        inverse1[...] = inverse
    u[...] = (normal * whole(smalls, N1G, 384) + whole(smalls, N1B, 384)).astype(LOW)


CHUNK = 1024


def feed_body(u, wup, wdown, smalls, slope, active, normal2, inverse2, y, later=()):
    x = u[...]
    bias = whole(smalls, B_UP, 1536)
    def grow(part, at):
        grown, tangent = gelu_parts(part + bias[:, at : at + CHUNK])
        active[:, at : at + CHUNK] = grown.astype(LOW)
        if slope is not None:
            slope[:, at : at + CHUNK] = tangent.astype(LOW)

    up = wup.chunk(0)
    for each in later:
        each.start()
    grow(dot_nn(x, up), 0)
    up, last = wup.chunk(1), wup.chunk(2)
    grow(dot_nn(x, up), CHUNK)
    part = dot_nn(x, last)
    down = wdown.get()
    grow(part, 2 * CHUNK)
    total = x.astype(F32) + whole(smalls, B_DOWN, 384) + dot_nn(active[...], down)
    normal, inverse = normalize(total)
    if normal2 is not None:
        normal2[...] = normal
        inverse2[...] = inverse
    y[...] = (normal * whole(smalls, N2G, 384) + whole(smalls, N2B, 384)).astype(LOW)


def top_back_body(up, smalls, normal2, inverse2, gr2, gz, gsmall):
    normal = normal2[...]
    put_halves(gsmall, N2G, column_sum(up * normal))
    put_halves(gsmall, N2B, column_sum(up))
    grad = normalize_back(up, whole(smalls, N2G, 384), normal, inverse2[...])
    z = grad.astype(LOW)
    gz[...] = z
    put_halves(gsmall, B_DOWN, column_sum(z.astype(F32)))
    gr2[...] = grad


def feed_back_body(gr2, gz, wup, wdown, smalls, slope, normal1, inverse1, ga, gr1, gb, gsmall):
    z = gz[...]
    down = wdown.get()
    sums = []
    for at in range(0, HIDDEN, CHUNK):
        inner = dot_nt(z, down[at : at + CHUNK, :]) * slope[:, at : at + CHUNK].astype(F32)
        a = inner.astype(LOW)
        ga[:, at : at + CHUNK] = a
        sums.append(column_sum(a.astype(F32)))
    put_halves(gsmall, B_UP, jnp.concatenate(sums, axis=1))
    up = gr2[...] + dot_nt(ga[...], wup.get())
    normal = normal1[...]
    put_halves(gsmall, N1G, column_sum(up * normal))
    put_halves(gsmall, N1B, column_sum(up))
    grad = normalize_back(up, whole(smalls, N1G, 384), normal, inverse1[...])
    gr1[...] = grad
    b = grad.astype(LOW)
    gb[...] = b
    put_halves(gsmall, B_OUT, column_sum(b.astype(F32)))


def heads_back_body(gb, wout, qkv, probs, gqkv, gqv, go):
    go[...] = dot_nt(gb[...], wout.get()).astype(LOW)
    for index, chain, rows, (at_q, at_k, at_v) in places():
        k = qkv[rows, at_k]
        g = split_heads(go[rows, at_q])
        weights = probs[index]
        wide = weights.astype(F32)
        inner = dot_nt(qkv[rows, at_v], g)
        inner = wide * (inner - jnp.sum(wide * inner, axis=0, keepdims=True))
        s = inner.astype(LOW)
        gqkv[rows, at_q] = (join_heads(dot_tn(s, k)) * SCALE).astype(LOW)
        gqkv[rows, at_k] = (dot_nn(s, split_heads(qkv[rows, at_q])) * SCALE).astype(LOW)
        gqkv[rows, at_v] = dot_nn(weights, g).astype(LOW)
    if gqv is not None:
        gqv[0:1, :] = column_sum(gqkv[:, :WIDTH].astype(F32))
        gqv[1:2, :] = column_sum(gqkv[:, 2 * WIDTH :].astype(F32))


def span_rows(spans, half):
    row = lax.broadcasted_iota(jnp.int32, (ROWS, 1), 0)
    inside = row < 0
    for chain in range(2):
        start = spans[half[0], chain, 0] + chain * LENGTH
        end = spans[half[0], chain, 1] + chain * LENGTH
        inside = inside | ((row >= start) & (row < end))
    return inside


def pick_halves(half, own, other, smalls):
    low = half[0] == 0
    smalls[0:1, :] = jnp.where(low, own[:, :SMALL], other[:, :SMALL])
    smalls[1:2, :] = jnp.where(low, other[:, :SMALL], own[:, :SMALL])


VMEM = pl.BlockSpec(memory_space=pltpu.VMEM)
SMEM = pl.BlockSpec(memory_space=pltpu.SMEM)
ANY = pl.BlockSpec(memory_space=pl.ANY)
HBM = pl.BlockSpec(memory_space=pltpu.HBM)
SMALL_SCRATCH = pltpu.VMEM((2, SMALL), F32)
QKV_SHAPE = (ROWS, 3 * WIDTH)
PROBS_SHAPE = (2 * PAIRS, LENGTH, 2 * LENGTH)
ROW_SHAPE = (ROWS, WIDTH)
FEED_SHAPE = (ROWS, HIDDEN)
MACS = ROWS * WIDTH * WIDTH * 2
ATTEND_WEIGHTS = [pltpu.VMEM((WIDTH, 3 * WIDTH), LOW), pltpu.VMEM((WIDTH, WIDTH), LOW)]
FEED_WEIGHTS = [pltpu.VMEM((WIDTH, HIDDEN), LOW), pltpu.VMEM((HIDDEN, WIDTH), LOW)]


def shape(dims, kind=LOW):
    return jax.ShapeDtypeStruct(dims, kind)


def enter_cotangent(half, own, swapped, raw, sem):
    @pl.when(half[0] == 0)
    def _():
        pltpu.make_async_copy(own.at[0], raw, sem).start()

    @pl.when(half[0] == 1)
    def _():
        pltpu.make_async_copy(swapped.at[1], raw, sem).start()

    return pltpu.make_async_copy(swapped.at[1], raw, sem)


def kernel_call(body, ins, outs, scratch, flops, moved, name, out_specs=None, grant=VMEM_LIMIT):
    return pl.pallas_call(
        body,
        in_specs=ins,
        out_specs=out_specs or [VMEM] * len(outs),
        out_shape=outs,
        scratch_shapes=scratch,
        compiler_params=pltpu.CompilerParams(vmem_limit_bytes=grant),
        cost_estimate=pl.CostEstimate(flops=flops, bytes_accessed=moved, transcendentals=0),
        name=name,
    )


def attend_first(inputs, half, lens, spans, weights, smalls):
    def body(x, half, lens, spans, so, sp, qo, qp, oo, op, u, h, raw, small, qkv, mixed, wq, wo, sems):
        enter = pltpu.make_async_copy(x.at[half[0]], raw, sems.at[2, 0])
        enter.start()
        wqkv = Weight(half[0], qo, qp, wq, sems.at[0], True, 3)
        wout = Weight(half[0], oo, op, wo, sems.at[1], False)
        pick_halves(half, so, sp, small)
        enter.wait()
        mask = so[:, SMALL:].astype(LOW)
        h[...] = jnp.where(span_rows(spans, half), mask, raw[...].reshape(ROWS, WIDTH))
        attend_body(h, wqkv, wout, small, lens, half, qkv, None, mixed, None, None, u, [wout])

    return kernel_call(
        body,
        [ANY, SMEM, SMEM, SMEM, VMEM, VMEM] + [ANY] * 4,
        [shape(ROW_SHAPE), shape(ROW_SHAPE)],
        [
            pltpu.VMEM((2, LENGTH, WIDTH), LOW),
            SMALL_SCRATCH,
            pltpu.VMEM(QKV_SHAPE, LOW),
            pltpu.VMEM(ROW_SHAPE, LOW),
            *ATTEND_WEIGHTS,
            pltpu.SemaphoreType.DMA((3, 6)),
        ],
        40 * MACS,
        80000000,
        "attend_first",
    )(inputs, half, lens, spans, *smalls, *weights[0], *weights[1])


def feed_first(u, half, weights, smalls):
    def body(u, half, so, sp, uo, up, do, dp, y, small, active, wu, wd, sems):
        wup = Weight(half[0], uo, up, wu, sems.at[0], True, 3)
        wdown = Weight(half[0], do, dp, wd, sems.at[1], False)
        pick_halves(half, so, sp, small)
        feed_body(u, wup, wdown, small, None, active, None, None, y, [wdown])

    return kernel_call(
        body,
        [VMEM, SMEM, VMEM, VMEM] + [ANY] * 4,
        [shape(ROW_SHAPE)],
        [
            SMALL_SCRATCH,
            pltpu.VMEM(FEED_SHAPE, LOW),
            *FEED_WEIGHTS,
            pltpu.SemaphoreType.DMA((2, 6)),
        ],
        8 * MACS,
        14000000,
        "feed_first",
    )(u, half, *smalls, *weights[2], *weights[3])[0]


KEPT = [
    shape(ROW_SHAPE),
    shape(QKV_SHAPE),
    shape(PROBS_SHAPE),
    shape(ROW_SHAPE),
    shape(ROW_SHAPE, F32),
    shape((ROWS, 1), F32),
    shape(ROW_SHAPE),
    shape(FEED_SHAPE),
    shape(FEED_SHAPE),
    shape(ROW_SHAPE, F32),
    shape((ROWS, 1), F32),
    shape(ROW_SHAPE),
]


def middle(h0, received, cotangent, swapped, half, first, lens, weights, smalls):
    def body(h0, received, cot, swap, half, first, lens, so, sp, qo, qp, oo, op, uo, up, do, dp, *rest):
        outs, rest = rest[: len(KEPT)], rest[len(KEPT) :]
        both, rest = rest[0], rest[1:]
        gh, small, gr2, gz, ga, gr1, gb, gsmall, gqkv, go, raw, wq, wo, wu, wd = rest[:15]
        keeps, sems, out_sems, raw_sem = rest[15:-3], *rest[-3:]
        h, qkv, probs, mixed, normal1, inverse1, u, slope, active, normal2, inverse2, y = keeps
        wqkv = Weight(half[0], qo, qp, wq, sems.at[0], True, 3)
        wout = Weight(half[0], oo, op, wo, sems.at[1])
        wup = Weight(half[0], uo, up, wu, sems.at[2], True, 3)
        wdown = Weight(half[0], do, dp, wd, sems.at[3])
        enter = enter_cotangent(half, cot, swap, raw, raw_sem)
        pick_halves(half, so, sp, small)
        leaving = []

        def leave(places):
            for place in places:
                copy = pltpu.make_async_copy(keeps[place], outs[place], out_sems.at[place])
                copy.start()
                leaving.append(copy)

        h[...] = jnp.where(first[0] > 0, h0[...], received[...])
        attend_body(
            h, wqkv, wout, small, lens, half, qkv, probs, mixed, normal1, inverse1, u, (),
            (wout, wup, wdown, enter),
        )
        leave(range(7))
        feed_body(u, wup, wdown, small, slope, active, normal2, inverse2, y)
        leave(range(7, 12))
        output = pltpu.make_async_copy(y, both.at[0], out_sems.at[len(KEPT)])
        output.start()
        leaving.append(output)
        upstream = raw[...].reshape(ROWS, WIDTH).astype(F32)
        top_back_body(upstream, small, normal2, inverse2, gr2, gz, gsmall)
        feed_back_body(gr2, gz, wup, wdown, small, slope, normal1, inverse1, ga, gr1, gb, gsmall)
        heads_back_body(gb, wout, qkv, probs, gqkv, None, go)
        gh[...] = (gr1[...] + dot_nt(gqkv[...], wqkv.get())).astype(LOW)
        output = pltpu.make_async_copy(gh, both.at[1], out_sems.at[len(KEPT) + 1])
        output.start()
        leaving.append(output)
        for copy in leaving:
            copy.wait()

    return kernel_call(
        body,
        [VMEM, VMEM, ANY, ANY, SMEM, SMEM, SMEM, VMEM, VMEM] + [ANY] * 8,
        KEPT + [shape((2, ROWS, WIDTH)), shape(ROW_SHAPE)],
        [
            SMALL_SCRATCH,
            pltpu.VMEM(ROW_SHAPE, F32),
            pltpu.VMEM(ROW_SHAPE, LOW),
            pltpu.VMEM(FEED_SHAPE, LOW),
            pltpu.VMEM(ROW_SHAPE, F32),
            pltpu.VMEM(ROW_SHAPE, LOW),
            SMALL_SCRATCH,
            pltpu.VMEM(QKV_SHAPE, LOW),
            pltpu.VMEM(ROW_SHAPE, LOW),
            pltpu.VMEM((2, LENGTH, WIDTH), LOW),
            *ATTEND_WEIGHTS,
            *FEED_WEIGHTS,
            *[pltpu.VMEM(kept.shape, kept.dtype) for kept in KEPT],
            pltpu.SemaphoreType.DMA((4, 6)),
            pltpu.SemaphoreType.DMA((len(KEPT) + 2,)),
            pltpu.SemaphoreType.DMA,
        ],
        24 * MACS,
        45000000,
        "middle",
        [ANY] * len(KEPT) + [ANY, VMEM],
        BIG_GRANT,
    )(
        h0, received, cotangent, swapped, half, first, lens, *smalls,
        *weights[0], *weights[1], *weights[2], *weights[3],
    )


MIB = 1024 * 1024


def half_columns(ref, which):
    size = ref.shape[1] // 2
    return ref[:, pl.ds(pl.multiple_of(which * size, 128), size)]


class Arriving:
    def __init__(self, pairs, sems):
        self.copies = {}
        for place, (name, source, dest) in enumerate(pairs):
            copy = pltpu.make_async_copy(source, dest, sems.at[place])
            copy.start()
            self.copies[name] = (copy, dest)

    def get(self, name):
        copy, dest = self.copies[name]
        copy.wait()
        return dest


class Leaving:
    def __init__(self, sems):
        self.sems = sems
        self.copies = []

    def send(self, source, target):
        copy = pltpu.make_async_copy(source, target, self.sems.at[len(self.copies)])
        copy.start()
        self.copies.append(copy)

    def wait(self):
        for copy in self.copies:
            copy.wait()


def send_folded(leaving, local, target, left_side, right):
    for block in range(right.shape[1] // WIDTH):
        rows = pl.ds(block * 384, 384)
        grad = dot_tn(left_side, right[:, block * WIDTH : (block + 1) * WIDTH])
        local[rows, :] = grad.astype(LOW)
        leaving.send(local.at[rows], target.at[rows])


TOKEN = shape((8, 128), F32)
GRAD_SHAPE = (1536, WIDTH)
GRAD_SCRATCH = pltpu.VMEM(GRAD_SHAPE, LOW)


def back_feed(cotangent, swapped, returned, half, first, weights, smalls, kept):
    u, slope, active, n1, i1, n2, i2 = kept

    def body(cot, swap, returned, half, first, so, sp, i1, n2, i2, uo, up, do, dp, u, slope, active, n1, *rest):
        outs, rest = rest[:8], rest[8:]
        down_other, down_own, up_other, up_own, gr1, gb, gsmall, token = outs
        gr2, gz, ga, v0, v1, v2, v3, small, raw, wu, wd, vu, vs, va, vn, sems, in_sems, out_sems = rest
        enter = enter_cotangent(half, cot, swap, raw, sems.at[2, 0])
        arriving = Arriving([("active", active, va)], in_sems)
        wdown = Weight(half[0], do, dp, wd, sems.at[1])
        later = Arriving(
            [("slope", slope, vs), ("normal", n1, vn), ("u", u, vu)],
            in_sems.at[pl.ds(1, 3)],
        )
        wup = Weight(half[0], uo, up, wu, sems.at[0])
        pick_halves(half, so, sp, small)
        enter.wait()
        upstream = jnp.where(first[0] > 0, returned[...], raw[...].reshape(ROWS, WIDTH))
        top_back_body(upstream.astype(F32), small, n2, i2, gr2, gz, gsmall)
        leaving = Leaving(out_sems)
        arriving.get("active")
        for which, local, target in ((1 - half[0], v0, down_other), (half[0], v1, down_own)):
            local[...] = dot_tn(half_columns(va, which), gz[...]).astype(LOW)
            leaving.send(local, target)
        for each in ("slope", "normal", "u"):
            later.get(each)
        wdown.wait()
        wup.wait()
        feed_back_body(gr2, gz, wup, wdown, small, vs, vn, i1, ga, gr1, gb, gsmall)
        for which, local, target in ((1 - half[0], v2, up_other), (half[0], v3, up_own)):
            send_folded(leaving, local, target, half_columns(vu, which), ga)
        token[...] = jnp.zeros(token.shape, F32)
        leaving.wait()

    return kernel_call(
        body,
        [ANY, ANY, VMEM, SMEM, SMEM] + [VMEM] * 5 + [ANY] * 8,
        [shape(GRAD_SHAPE)] * 4
        + [shape(ROW_SHAPE, F32), shape(ROW_SHAPE), shape((2, SMALL), F32), TOKEN],
        [
            pltpu.VMEM(ROW_SHAPE, F32),
            pltpu.VMEM(ROW_SHAPE, LOW),
            pltpu.VMEM(FEED_SHAPE, LOW),
            *[GRAD_SCRATCH] * 4,
            SMALL_SCRATCH,
            pltpu.VMEM((2, LENGTH, WIDTH), LOW),
            *FEED_WEIGHTS,
            pltpu.VMEM(ROW_SHAPE, LOW),
            pltpu.VMEM(FEED_SHAPE, LOW),
            pltpu.VMEM(FEED_SHAPE, LOW),
            pltpu.VMEM(ROW_SHAPE, F32),
            pltpu.SemaphoreType.DMA((3, 2)),
            pltpu.SemaphoreType.DMA((4,)),
            pltpu.SemaphoreType.DMA((10,)),
        ],
        200 * MACS,
        600000000,
        "back_feed",
        [ANY] * 4 + [VMEM] * 4,
        BIG_GRANT,
    )(
        cotangent, swapped, returned, half, first, *smalls, i1, n2, i2, *weights[2], *weights[3],
        u, slope, active, n1,
    )


def back_attend(gb, gr1, half, first, spans, weights, gsmall, h, qkv, probs, mixed):
    def body(gb, half, first, spans, gsmall, oo, op, qo, qp, gr1, h, qkv, probs, mixed, *rest):
        outs, rest = rest[:6], rest[6:]
        other, own, small_other, small_own, gh, token = outs
        gqkv, go, gqv, vother, vown, wo, wq, vr, vh, vq, vp, vm, sems, in_sems, out_sems = rest
        wout = Weight(half[0], oo, op, wo, sems.at[0])
        arriving = Arriving([("qkv", qkv, vq), ("probs", probs, vp)], in_sems)
        wqkv = Weight(half[0], qo, qp, wq, sems.at[1], False)
        arriving.get("qkv")
        arriving.get("probs")
        wqkv.start()
        late = Arriving([("h", h, vh), ("mixed", mixed, vm), ("gr1", gr1, vr)], in_sems.at[pl.ds(2, 3)])
        heads_back_body(gb, wout, vq, vp, gqkv, gqv, go)
        leaving = Leaving(out_sems)
        late.get("h")
        late.get("mixed")
        for which, local, target in ((1 - half[0], vother, other), (half[0], vown, own)):
            send_folded(leaving, local, target, half_columns(vh, which), gqkv)
            local[1152:, :] = dot_tn(half_columns(vm, which), gb[...]).astype(LOW)
            leaving.send(local.at[pl.ds(1152, 384)], target.at[pl.ds(1152, 384)])
        late.get("gr1")
        full = vr[...] + dot_nt(gqkv[...], wqkv.get())
        dropped = span_rows(spans, half) & (first[0] > 0)
        zero = jnp.zeros_like(full)
        gh[...] = jnp.where(dropped, zero, full).astype(LOW)
        gmask = column_sum(jnp.where(dropped, full, zero))
        for which, target in ((1 - half[0], small_other), (half[0], small_own)):
            target[:, :WIDTH] = gqv[pl.ds(which, 1), :]
            target[:, WIDTH:SMALL] = gsmall[pl.ds(which, 1), WIDTH:]
            target[:, SMALL:] = gmask
        token[...] = jnp.zeros(token.shape, F32)
        leaving.wait()

    return kernel_call(
        body,
        [VMEM, SMEM, SMEM, SMEM, VMEM] + [ANY] * 9,
        [
            shape(GRAD_SHAPE),
            shape(GRAD_SHAPE),
            shape((1, SMALL + WIDTH), F32),
            shape((1, SMALL + WIDTH), F32),
            shape(ROW_SHAPE),
            TOKEN,
        ],
        [
            pltpu.VMEM(QKV_SHAPE, LOW),
            pltpu.VMEM(ROW_SHAPE, LOW),
            pltpu.VMEM((2, WIDTH), F32),
            GRAD_SCRATCH,
            GRAD_SCRATCH,
            ATTEND_WEIGHTS[1],
            ATTEND_WEIGHTS[0],
            pltpu.VMEM(ROW_SHAPE, F32),
            pltpu.VMEM(ROW_SHAPE, LOW),
            pltpu.VMEM(QKV_SHAPE, LOW),
            pltpu.VMEM(PROBS_SHAPE, LOW),
            pltpu.VMEM(ROW_SHAPE, LOW),
            pltpu.SemaphoreType.DMA((2, 2)),
            pltpu.SemaphoreType.DMA((5,)),
            pltpu.SemaphoreType.DMA((8,)),
        ],
        180 * MACS,
        400000000,
        "back_attend",
        [ANY, ANY] + [VMEM] * 4,
    )(gb, half, first, spans, gsmall, *weights[1], *weights[0], gr1, h, qkv, probs, mixed)


TAIL = 16
BLOCK = 96


def add_rows(target, sources, at, rows):
    for start in range(0, rows, BLOCK):
        size = min(BLOCK, rows - start)
        place = pl.ds(at + start, size)
        if not isinstance(at, int):
            place = pl.ds(pl.multiple_of(at + start, 16), size)
        if len(sources) == 2:
            target[start : start + size, :] = sources[0][place, :] + sources[1][place, :]
            continue
        total = sources[0][place, :].astype(F32)
        for source in sources[1:]:
            total = total + source[place, :].astype(F32)
        target[start : start + size, :] = total.astype(LOW)


LONG = 30000000000


def ordered(
    name, body, ins, outs, where, after, out_specs=None, scratch=(), in_specs=None, grant=16, aliases=None,
    flops=LONG,
):
    count, made = len(ins), len(outs)

    def kernel(where, after, *refs):
        refs[count + made][...] = jnp.zeros(TOKEN.shape, F32)
        body(where, refs[:count], refs[count : count + made] + refs[count + made + 1 :])

    result = pl.pallas_call(
        kernel,
        in_specs=[SMEM, HBM] + (in_specs or [VMEM] * count),
        out_specs=(out_specs or [VMEM] * made) + [VMEM],
        out_shape=list(outs) + [TOKEN],
        scratch_shapes=list(scratch),
        input_output_aliases=aliases or {},
        compiler_params=pltpu.CompilerParams(vmem_limit_bytes=grant * MIB),
        cost_estimate=pl.CostEstimate(flops=flops, bytes_accessed=flops, transcendentals=0),
        name=name,
    )(where, after, *ins)
    return result[:made], result[made]


def partner(x, axis, bit):
    return lax.ppermute(x, axis, [(i, i ^ 1 << bit) for i in range(lax.axis_size(axis))])


def moved_on(index, axis, steps):
    z, x, y = index // 8, index // 2 % 4, index % 2
    if axis == "z":
        z = steps(z)
    elif axis == "x":
        x = steps(x)
    else:
        y = steps(y)
    return z * 8 + x * 2 + y


def send_along(value, axes, place):
    pairs = []
    for section in range(4):
        for index in range(32):
            to = moved_on(index, axes[section % 2], place)
            pairs.append((section * 32 + index, section * 32 + to))
    return lax.ppermute(value, ("section", "dp"), pairs)


def exchange(value, part, step):
    flip = 1 if part == step else 3
    return send_along(value, "zx", lambda place: place ^ flip)


def turn(value, steps):
    return send_along(value, "xz", lambda place: (place + steps) % 4)


def across_y(value):
    return send_along(value, "yy", lambda place: place ^ 1)


def swap_core_one(value):
    pairs = [
        (section * 32 + index, section * 32 + (index ^ 1)) for section in (1, 3) for index in range(32)
    ]
    return lax.ppermute(value, ("section", "dp"), pairs)


def between_layers(value, back):
    pairs = []
    for core in range(2):
        for index in range(32):
            pair = (core * 32 + index, (core + 2) * 32 + (index ^ core))
            pairs.append(pair[::-1] if back else pair)
    return lax.ppermute(value, ("section", "dp"), pairs)


def own_places(core):
    index = lax.axis_index("dp")
    z, x = index // 8, index // 2 % 4
    ring = jnp.where(core == 0, z, x)
    high = ring // 2
    low = high ^ (ring % 2)
    table = [low, high, high, low, jnp.where(core == 0, x, z)]
    return jnp.stack(table).astype(jnp.int32)


def row_shapes(*counts):
    return [shape((count, WIDTH)) for count in counts]


def add_tail(target, rows, sources, at, extra):
    if extra:
        total = sources[0][at : at + extra, :].astype(F32)
        for source in sources[1:]:
            total = total + source[at : at + extra, :].astype(F32)
        target[rows : rows + extra, :] = total.astype(LOW)


class Chain:
    def __init__(self, name, places, tail=0):
        self.name = name
        self.places = places
        self.tail = (0, tail)
        self.keep = [None, None]
        self.got = [None, None]

    def kernel(self, name, body, ins, outs, token, *more, **named):
        return ordered(self.name + name, body, ins, outs, self.places, token, *more, **named)

    def pairs(self):
        return (self.keep[0], self.got[0], self.keep[1], self.got[1])

    def first_sum(self, name, sent, token):
        sources, half_rows, tails = self.sources, self.rows, self.tail

        def body(places, ins, refs):
            outs, held, sems = refs[:2], refs[2:6], refs[6]
            copies = []
            for index in range(4):
                bit, at = places[2 * (index // 2)], sources[index // 2][2]
                which = 1 - bit if sent else bit
                rows = pl.ds(pl.multiple_of(at + which * half_rows, 16), half_rows)
                copy = pltpu.make_async_copy(ins[index].at[rows], held[index], sems.at[index])
                copy.start()
                copies.append(copy)
            for part in range(2):
                copies[2 * part].wait()
                copies[2 * part + 1].wait()
                add_rows(outs[part], held[2 * part : 2 * part + 2], 0, half_rows)
                if tails[part]:
                    outs[part][half_rows:, :] = self.tail_body(ins[4:])

        arrays = [array for own, got, _ in sources for array in (own, got)]
        return self.kernel(
            name,
            body,
            (*arrays, *self.tail_ins),
            row_shapes(half_rows + tails[0], half_rows + tails[1]),
            token,
            scratch=(*[pltpu.VMEM((half_rows, WIDTH), LOW)] * 4, pltpu.SemaphoreType.DMA((4,))),
            in_specs=[HBM] * 4 + [VMEM] * len(self.tail_ins),
            grant=63 if sent else 46,
            flops=LONG if sent else 0,
        )

    def start(self, sources, rows, token, tail_ins=(), tail_body=None):
        self.rows, self.sources = rows // 2, sources
        self.tail_ins, self.tail_body = tuple(tail_ins), tail_body
        sends, token = self.first_sum("send", True, token)
        self.got = [exchange(sends[part], part, 0) for part in range(2)]
        return token

    def hold(self, token):
        keeps, token = self.first_sum("keep", False, token)
        self.keep = list(keeps)
        return token

    def halve(self, token, flops):
        self.rows //= 2
        rows, tails = self.rows, self.tail

        def body(places, ins, outs):
            for part in range(2):
                bit = places[2 * part + 1]
                pair = ins[2 * part : 2 * part + 2]
                for target, which in ((outs[2 * part + 1], 1 - bit), (outs[2 * part], bit)):
                    add_rows(target, pair, which * rows, rows)
                    add_tail(target, rows, pair, 2 * rows, tails[part])

        counts = [rows + tails[0]] * 2 + [rows + tails[1]] * 2
        outs, token = self.kernel(
            "halve", body, self.pairs(), row_shapes(*counts), token, flops=flops
        )
        for part in range(2):
            self.keep[part] = outs[2 * part]
            self.got[part] = exchange(outs[2 * part + 1], part, 1)
        return token

    def cross(self, token):
        whole_rows, extra = self.rows, self.tail[1]
        rows = whole_rows // 2

        def body(places, ins, refs):
            outs, total = refs[:4], refs[4]
            add_rows(total.at[pl.ds(0, whole_rows)], ins[:2], 0, whole_rows)
            add_rows(total.at[pl.ds(whole_rows, whole_rows)], ins[2:], 0, whole_rows)
            for steps in range(4):
                quarter = (places[4] + steps) % 4
                outs[steps][:rows, :] = total[pl.ds(pl.multiple_of(quarter * rows, 16), rows), :]
                add_tail(outs[steps], rows, ins[2:], whole_rows, extra)

        (self.own, *sends), token = self.kernel(
            "cross",
            body,
            self.pairs(),
            row_shapes(*[rows + extra] * 4),
            token,
            None,
            (pltpu.VMEM((2 * whole_rows, WIDTH), LOW),),
        )
        self.rows = rows
        self.ring = [turn(send, steps) for steps, send in zip((1, 2, 3), sends)]
        return token

    def across(self, token):
        rows = self.rows + self.tail[1]

        def body(places, ins, outs):
            add_rows(outs[0], ins, 0, rows)

        (self.own,), token = self.kernel(
            "across", body, (self.own, *self.ring), row_shapes(rows), token
        )
        self.other = across_y(self.own)
        return token

    def total(self, token, more_outs=(), more_body=None):
        rows, extra = self.rows, self.tail[1]

        def body(places, ins, outs):
            add_rows(outs[0], ins, 0, rows)
            if extra:
                add_rows(outs[1], ins, rows, extra)
                more_body(outs[1][...].astype(F32), outs[2:])

        counts = [rows] + ([extra] if extra else [])
        outs, token = self.kernel(
            "total", body, (self.own, self.other), row_shapes(*counts) + list(more_outs), token
        )
        self.own = outs[0]
        self.tail_sum = outs[1] if extra else None
        self.ring = [turn(self.own, steps) for steps in (1, 2, 3)]
        return outs[2:], token

    def back(self, token, more_ins=(), more_outs=(), more_body=None):
        rows = self.rows

        def body(places, ins, refs):
            outs, total = refs[:-1], refs[-1]
            for steps in range(4):
                quarter = (places[4] - steps + 4) % 4
                total[pl.ds(pl.multiple_of(quarter * rows, 16), rows), :] = ins[steps][...]
            outs[0][...] = total[: 2 * rows, :]
            outs[1][...] = total[2 * rows :, :]
            if more_body is not None:
                more_body(ins[4:], outs[2:])

        outs, token = self.kernel(
            "back",
            body,
            (self.own, *self.ring) + tuple(more_ins),
            row_shapes(2 * rows, 2 * rows) + list(more_outs),
            token,
            None,
            (pltpu.VMEM((4 * rows, WIDTH), LOW),),
        )
        self.rows = 2 * rows
        self.keep = list(outs[:2])
        self.got = [exchange(self.keep[part], part, 1) for part in range(2)]
        return outs[2:], token

    def double(self, token, flops):
        rows = self.rows

        def body(places, ins, outs):
            for part in range(2):
                bit = places[2 * part + 1]
                for which, source in ((bit, ins[2 * part]), (1 - bit, ins[2 * part + 1])):
                    outs[part][pl.ds(pl.multiple_of(which * rows, 16), rows), :] = source[...]

        outs, token = self.kernel(
            "double", body, self.pairs(), row_shapes(2 * rows, 2 * rows), token, flops=flops
        )
        self.rows = 2 * rows
        self.keep = list(outs)
        self.got = [exchange(self.keep[part], part, 0) for part in range(2)]
        return token

    def finish(self, token, outs, place, got, flops, more_ins=(), more_outs=(), more_body=None):
        rows = self.rows
        mine = tuple(self.got if got else self.keep)
        kept = tuple(outs) if got else ()

        def body(places, ins, refs):
            targets, wide, sems = refs[: len(outs)], refs[-2], refs[-1]
            if more_body is not None:
                more_body(ins[2 + len(kept) :], refs[len(outs) : -2])
            waits = []
            for part in range(2):
                bit = places[2 * part]
                half = 1 - bit if got else bit
                wide[part] = ins[part][...].astype(F32)
                at = 0
                for size, starts in place(targets, part, half):
                    source, sem = wide.at[part, pl.ds(at, size)], sems.at[len(waits)]
                    starts(source, sem)
                    waits.append((size, source, sem))
                    at += size
            for size, source, sem in waits:
                pltpu.make_async_copy(source, wide.at[0, pl.ds(0, size)], sem).wait()

        return self.kernel(
            "finish",
            body,
            mine + kept + tuple(more_ins),
            [shape(out.shape, F32) for out in outs] + list(more_outs),
            token,
            out_specs=[ANY] * len(outs) + [VMEM] * len(more_outs),
            scratch=(pltpu.VMEM((2, rows, WIDTH), F32), pltpu.SemaphoreType.DMA((4,))),
            in_specs=[VMEM] * 2 + [ANY] * len(kept) + [VMEM] * len(more_ins),
            grant=24,
            flops=flops,
            aliases={4 + index: index for index in range(len(kept))},
        )


def copy_to(target):
    return lambda source, sem: pltpu.make_async_copy(source, target, sem).start()


def block_columns(block):
    return pl.ds(pl.multiple_of(block * WIDTH, 128), WIDTH)


def place_x(refs, part, half):
    down, up = refs
    if part == 0:
        return [(768, copy_to(down.at[pl.ds(pl.multiple_of(half * 768, 8), 768)]))]
    return [(384, copy_to(up.at[:, block_columns(2 * half + block)])) for block in range(2)]


def place_y(refs, part, half):
    qkv, out = refs
    if part == 0:
        return [(384, copy_to(qkv.at[:, block_columns(half)]))]

    def starts(source, sem):
        @pl.when(half == 0)
        def _():
            copy_to(qkv.at[:, block_columns(2)])(source, sem)

        @pl.when(half == 1)
        def _():
            copy_to(out)(source, sem)

    return [(384, starts)]


def pack_vectors(vectors):
    size = sum(vector.shape[0] for vector in vectors)
    total = jnp.zeros((size,), F32)
    at = 0
    for vector in vectors:
        total = total + jnp.pad(vector.astype(F32), (at, size - at - vector.shape[0]))
        at += vector.shape[0]
    return total.reshape(1, size)


def per_device(
    inputs,
    cotangent,
    lengths,
    cdr_spans,
    mask_vector,
    w_qkv,
    qv_bias,
    w_out,
    b_out,
    norm1_gain,
    norm1_bias,
    w_up,
    b_up,
    w_down,
    b_down,
    norm2_gain,
    norm2_bias,
):
    section_index = lax.axis_index("section")
    core = section_index % 2
    half = core.astype(jnp.int32).reshape(1)
    first = (section_index < 2).astype(jnp.int32).reshape(1)
    places = own_places(core)
    small = pack_vectors(
        (
            qv_bias,
            b_out,
            norm1_gain,
            norm1_bias,
            b_up,
            b_down,
            norm2_gain,
            norm2_bias,
            mask_vector,
        )
    )
    small_got = partner(small, "section", 0)
    got_qkv, got_out = partner((w_qkv, w_out), "section", 0)
    w_up, w_down, got_qkv, got_out, small_got = lax.optimization_barrier(
        (w_up, w_down, got_qkv, got_out, small_got)
    )
    smalls = (small, small_got)
    got_up, got_down = partner((w_up, w_down), "section", 0)
    weights = [(w_qkv, got_qkv), (w_out, got_out), (w_up, got_up), (w_down, got_down)]

    swapped = swap_core_one(cotangent)
    lens_got = swap_core_one(lengths)
    swaps = (core == 1) & (section_index >= 2)
    layer_lens = jnp.where(swaps, lens_got, lengths)

    u, h0 = attend_first(inputs, half, lengths, cdr_spans, weights, smalls)
    first_out = feed_first(u, half, weights, smalls)
    received = between_layers(first_out, False)
    kept = middle(h0, received, cotangent, swapped, half, first, layer_lens, weights, smalls)
    h, qkv, probs, mixed, normal1, inverse1, u, slope, active, normal2, inverse2, output = kept[:12]
    returned = between_layers(kept[13], True)

    a_other, a_own, b_other, b_own, gr1, gb, gsmall, token = back_feed(
        cotangent,
        swapped,
        returned,
        half,
        first,
        weights,
        smalls,
        (u, slope, active, normal1, inverse1, normal2, inverse2),
    )
    a_got = partner(a_other, "section", 0)
    b_got = partner(b_other, "section", 0)
    x, y = Chain("x_", places), Chain("y_", places, TAIL)
    y_other, y_own, small_other, small_own, gh, token = back_attend(
        gb, gr1, half, first, cdr_spans, weights, gsmall, h, qkv, probs, mixed
    )
    y_got = partner(y_other, "section", 0)
    small_got = partner(small_other, "section", 0)
    token = x.start([(a_own, a_got, 0), (b_own, b_got, 0)], 1536, token)

    def tail_rows(ins):
        total = ins[0][...] + ins[1][...]
        rows = [total[:, at : at + WIDTH] for at in range(0, SMALL + WIDTH, WIDTH)]
        rows.append(jnp.zeros((TAIL - len(rows), WIDTH), F32))
        return jnp.concatenate(rows, axis=0).astype(LOW)

    token = y.start(
        [(y_own, y_got, 0), (y_own, y_got, 768)], 768, token, (small_own, small_got), tail_rows
    )
    both, token = lax.optimization_barrier((kept[12], token))
    both_got = swap_core_one(both)
    token = x.hold(token)
    token = x.halve(token, 0)
    token = y.hold(token)
    token = y.halve(token, LONG)
    token = x.cross(token)
    token = y.cross(token)
    token = x.across(token)
    token = y.across(token)
    _, token = x.total(token)

    def small_outputs(tail, outs):
        flat = jnp.concatenate([tail[row : row + 1, :] for row in range(6)], axis=1)
        at = 0
        for out, size in zip(outs, SIZES):
            out[...] = flat[0, at : at + size]
            at += size

    _, token = x.back(token)
    out_small, token = y.total(token, [shape((size,), F32) for size in SIZES], small_outputs)

    def mask_output(ins, outs):
        outs[0][...] = ins[0][6, :].astype(F32) + ins[1][6, :].astype(F32)

    _, token = y.back(token)
    gradients_x = [shape((1536, WIDTH), F32), shape((384, HIDDEN), F32)]
    gradients_y = [shape((384, 3 * WIDTH), F32), shape((384, WIDTH), F32)]
    token = x.double(token, LONG)
    gradients_x, token = x.finish(token, gradients_x, place_x, False, LONG)
    token = y.double(token, 0)
    tail_sum, token = lax.optimization_barrier((y.tail_sum, token))
    mask_got = partner(tail_sum, "section", 1)
    gradients_y, token = y.finish(token, gradients_y, place_y, False, 0)
    both_got, token = lax.optimization_barrier((both_got, token))
    (g_down, g_up), token = x.finish(token, gradients_x, place_x, True, LONG)
    (g_qkv, g_out, mask_grad), token = y.finish(
        token,
        gradients_y,
        place_y,
        True,
        LONG,
        (tail_sum, mask_got),
        [shape((WIDTH,), F32)],
        mask_output,
    )
    output = jnp.where(swaps, both_got[0], output)
    gh = jnp.where(swaps, both_got[1], gh)

    g_qv, g_bo, g_n1g, g_n1b, g_bu, g_bd, g_n2g, g_n2b = out_small
    return (
        output.reshape(1, 2, LENGTH, WIDTH),
        gh.reshape(1, 2, LENGTH, WIDTH),
        mask_grad,
        g_qkv,
        g_qv,
        g_out,
        g_bo,
        g_n1g,
        g_n1b,
        g_up,
        g_bu,
        g_down,
        g_bd,
        g_n2g,
        g_n2b,
    )


def solution(mesh):
    in_specs = (
        P(None, "dp", None, None),
        P(None, "dp", None, None),
        P(None, "dp"),
        P(None, "dp", None),
        P(),
        P("section", None),
        P("section"),
        P("section", None),
        P("section"),
        P("section"),
        P("section"),
        P("section", None),
        P("section"),
        P("section", None),
        P("section"),
        P("section"),
        P("section"),
    )
    out_specs = (
        P("section", "dp", None, None),
        P("section", "dp", None, None),
        P(),
        P("section", None),
        P("section"),
        P("section", None),
        P("section"),
        P("section"),
        P("section"),
        P("section", None),
        P("section"),
        P("section", None),
        P("section"),
        P("section"),
        P("section"),
    )
    return jax.shard_map(
        per_device, mesh=mesh, in_specs=in_specs, out_specs=out_specs, check_vma=False
    )
```

```python
import functools
import math

import jax
import jax.numpy as jnp
from jax import lax
from jax.experimental import pallas as pl
from jax.experimental.pallas import tpu as pltpu
from jax.sharding import PartitionSpec as P

EPSILON = 1e-05
F32 = jnp.float32
LOW = jnp.bfloat16
WIDTH = 768
LENGTH = 160
ROWS = 320
HIDDEN = 3072
PAIRS = 6
SCALE = 0.125
SIZES = (768, 384, 384, 384, 1536, 384, 384, 384)
QV, B_OUT, N1G, N1B, B_UP, B_DOWN, N2G, N2B = (sum(SIZES[:at]) for at in range(8))
SMALL = sum(SIZES)
VMEM_LIMIT = 63 * 1024 * 1024
BIG_GRANT = 61 * 1024 * 1024


def dot_nn(left_side, right_side):
    return jnp.dot(left_side, right_side, preferred_element_type=F32)


def dot_nt(left_side, right_side):
    return lax.dot_general(
        left_side, right_side, (((1,), (1,)), ((), ())), preferred_element_type=F32
    )


def dot_tn(left_side, right_side):
    return lax.dot_general(
        left_side, right_side, (((0,), (0,)), ((), ())), preferred_element_type=F32
    )


class Weight:
    def __init__(self, half, own, other, dest, sems, start=True, chunks=1):
        rows, wide = own.shape
        self.dest = dest
        self.wide = wide // chunks
        self.copies = []
        for chunk in range(chunks):
            at = pl.ds(chunk * self.wide, self.wide)
            for side, source in enumerate((own, other)):
                which = half if side == 0 else 1 - half
                place = dest.at[pl.ds(which * rows, rows)]
                if chunks > 1:
                    source, place = source.at[:, at], place.at[:, at]
                self.copies.append(
                    pltpu.make_async_copy(source, place, sems.at[2 * chunk + side])
                )
        if start:
            self.start()

    def start(self):
        for copy in self.copies:
            copy.start()

    def wait(self):
        for copy in self.copies:
            copy.wait()
        self.copies = []

    def get(self):
        self.wait()
        return self.dest[...]

    def chunk(self, index):
        for copy in self.copies[:2]:
            copy.wait()
        self.copies = self.copies[2:]
        return self.dest[:, index * self.wide : (index + 1) * self.wide]


def whole(smalls, at, size):
    return jnp.concatenate([smalls[0:1, at : at + size], smalls[1:2, at : at + size]], axis=1)


def split_heads(tensor):
    lane = lax.broadcasted_iota(jnp.int32, tensor.shape, 1)
    zero = jnp.zeros_like(tensor)
    return jnp.concatenate(
        [jnp.where(lane < 64, tensor, zero), jnp.where(lane < 64, zero, tensor)], axis=0
    )


def join_heads(tensor):
    lane = lax.broadcasted_iota(jnp.int32, (LENGTH, 128), 1)
    return jnp.where(lane < 64, tensor[:LENGTH], tensor[LENGTH:])


def normalize(values):
    center = values - jnp.mean(values, axis=-1, keepdims=True)
    spread = jnp.mean(center * center, axis=-1, keepdims=True)
    inverse = lax.rsqrt(spread + EPSILON)
    return center * inverse, inverse


def normalize_back(upstream, gain, normal, inverse):
    scaled = upstream * gain
    first = jnp.mean(scaled, axis=-1, keepdims=True)
    second = jnp.mean(scaled * normal, axis=-1, keepdims=True)
    return inverse * (scaled - first - normal * second)


def gelu_parts(values):
    size = jnp.abs(values)
    below = 1.0 + (0.3275911 * math.sqrt(0.5)) * size
    t = pl.reciprocal(below, approx=True)
    t = t * (2.0 - below * t)
    series = t * (
        0.5 * 0.254829592
        + t
        * (
            0.5 * -0.284496736
            + t * (0.5 * 1.421413741 + t * (0.5 * -1.453152027 + t * (0.5 * 1.061405429)))
        )
    )
    bell = jnp.exp(-0.5 * values * values)
    tail = series * bell
    share = jnp.where(values >= 0.0, 1.0 - tail, tail)
    return values * share, share + values * bell * (1.0 / math.sqrt(2.0 * math.pi))


def column_sum(values):
    return jnp.sum(values, axis=0, keepdims=True)


def put_halves(target, at, row):
    size = row.shape[1] // 2
    target[0:1, at : at + size] = row[:, :size]
    target[1:2, at : at + size] = row[:, size:]


def places():
    for index in range(2 * PAIRS):
        chain, pair = divmod(index, PAIRS)
        rows = pl.ds(chain * LENGTH, LENGTH)
        yield index, chain, rows, [pl.ds((pair + block * PAIRS) * 128, 128) for block in range(3)]


def attend_body(
    h, wqkv, wout, smalls, lens, half, qkv, probs, mixed, normal1, inverse1, u, later=(), settle=()
):
    x = h[...]
    bias = jnp.concatenate(
        [smalls[0:1, :WIDTH], jnp.zeros((1, WIDTH), F32), smalls[1:2, :WIDTH]], axis=1
    )
    for block in range(3):
        at = block * WIDTH
        matrix = wqkv.chunk(block)
        if block == 0:
            for each in later:
                each.start()
        qkv[:, at : at + WIDTH] = (dot_nn(x, matrix) + bias[:, at : at + WIDTH]).astype(LOW)
    for index, chain, rows, (at_q, at_k, at_v) in places():
        scores = dot_nt(qkv[rows, at_k], split_heads(qkv[rows, at_q])) * SCALE
        key = lax.broadcasted_iota(jnp.int32, scores.shape, 0)
        scores = jnp.where(key < lens[half[0], chain], scores, -1000000000.0)
        grown = jnp.exp(scores - jnp.max(scores, axis=0, keepdims=True))
        weights = (grown * (1.0 / jnp.sum(grown, axis=0, keepdims=True))).astype(LOW)
        if probs is not None:
            probs[index] = weights
        mixed[rows, at_q] = join_heads(dot_tn(weights, qkv[rows, at_v])).astype(LOW)
    for each in settle:
        each.wait()
    branch = dot_nn(mixed[...], wout.get()) + whole(smalls, B_OUT, 384)
    normal, inverse = normalize(x.astype(F32) + branch)
    if normal1 is not None:
        normal1[...] = normal
        inverse1[...] = inverse
    u[...] = (normal * whole(smalls, N1G, 384) + whole(smalls, N1B, 384)).astype(LOW)


CHUNK = 1024


def feed_body(u, wup, wdown, smalls, slope, active, normal2, inverse2, y, later=()):
    x = u[...]
    bias = whole(smalls, B_UP, 1536)
    def grow(part, at):
        grown, tangent = gelu_parts(part + bias[:, at : at + CHUNK])
        active[:, at : at + CHUNK] = grown.astype(LOW)
        if slope is not None:
            slope[:, at : at + CHUNK] = tangent.astype(LOW)

    up = wup.chunk(0)
    for each in later:
        each.start()
    grow(dot_nn(x, up), 0)
    up, last = wup.chunk(1), wup.chunk(2)
    grow(dot_nn(x, up), CHUNK)
    part = dot_nn(x, last)
    down = wdown.get()
    grow(part, 2 * CHUNK)
    total = x.astype(F32) + whole(smalls, B_DOWN, 384) + dot_nn(active[...], down)
    normal, inverse = normalize(total)
    if normal2 is not None:
        normal2[...] = normal
        inverse2[...] = inverse
    y[...] = (normal * whole(smalls, N2G, 384) + whole(smalls, N2B, 384)).astype(LOW)


def top_back_body(up, smalls, normal2, inverse2, gr2, gz, gsmall):
    normal = normal2[...]
    put_halves(gsmall, N2G, column_sum(up * normal))
    put_halves(gsmall, N2B, column_sum(up))
    grad = normalize_back(up, whole(smalls, N2G, 384), normal, inverse2[...])
    z = grad.astype(LOW)
    gz[...] = z
    put_halves(gsmall, B_DOWN, column_sum(z.astype(F32)))
    gr2[...] = grad


def feed_back_body(gr2, gz, wup, wdown, smalls, slope, normal1, inverse1, ga, gr1, gb, gsmall):
    z = gz[...]
    down = wdown.get()
    sums = []
    for at in range(0, HIDDEN, CHUNK):
        inner = dot_nt(z, down[at : at + CHUNK, :]) * slope[:, at : at + CHUNK].astype(F32)
        a = inner.astype(LOW)
        ga[:, at : at + CHUNK] = a
        sums.append(column_sum(a.astype(F32)))
    put_halves(gsmall, B_UP, jnp.concatenate(sums, axis=1))
    up = gr2[...] + dot_nt(ga[...], wup.get())
    normal = normal1[...]
    put_halves(gsmall, N1G, column_sum(up * normal))
    put_halves(gsmall, N1B, column_sum(up))
    grad = normalize_back(up, whole(smalls, N1G, 384), normal, inverse1[...])
    gr1[...] = grad
    b = grad.astype(LOW)
    gb[...] = b
    put_halves(gsmall, B_OUT, column_sum(b.astype(F32)))


def heads_back_body(gb, wout, qkv, probs, gqkv, gqv, go):
    go[...] = dot_nt(gb[...], wout.get()).astype(LOW)
    for index, chain, rows, (at_q, at_k, at_v) in places():
        k = qkv[rows, at_k]
        g = split_heads(go[rows, at_q])
        weights = probs[index]
        wide = weights.astype(F32)
        inner = dot_nt(qkv[rows, at_v], g)
        inner = wide * (inner - jnp.sum(wide * inner, axis=0, keepdims=True))
        s = inner.astype(LOW)
        gqkv[rows, at_q] = (join_heads(dot_tn(s, k)) * SCALE).astype(LOW)
        gqkv[rows, at_k] = (dot_nn(s, split_heads(qkv[rows, at_q])) * SCALE).astype(LOW)
        gqkv[rows, at_v] = dot_nn(weights, g).astype(LOW)
    if gqv is not None:
        gqv[0:1, :] = column_sum(gqkv[:, :WIDTH].astype(F32))
        gqv[1:2, :] = column_sum(gqkv[:, 2 * WIDTH :].astype(F32))


def span_rows(spans, half):
    row = lax.broadcasted_iota(jnp.int32, (ROWS, 1), 0)
    inside = row < 0
    for chain in range(2):
        start = spans[half[0], chain, 0] + chain * LENGTH
        end = spans[half[0], chain, 1] + chain * LENGTH
        inside = inside | ((row >= start) & (row < end))
    return inside


def pick_halves(half, own, other, smalls):
    low = half[0] == 0
    smalls[0:1, :] = jnp.where(low, own[:, :SMALL], other[:, :SMALL])
    smalls[1:2, :] = jnp.where(low, other[:, :SMALL], own[:, :SMALL])


VMEM = pl.BlockSpec(memory_space=pltpu.VMEM)
SMEM = pl.BlockSpec(memory_space=pltpu.SMEM)
ANY = pl.BlockSpec(memory_space=pl.ANY)
HBM = pl.BlockSpec(memory_space=pltpu.HBM)
SMALL_SCRATCH = pltpu.VMEM((2, SMALL), F32)
QKV_SHAPE = (ROWS, 3 * WIDTH)
PROBS_SHAPE = (2 * PAIRS, LENGTH, 2 * LENGTH)
ROW_SHAPE = (ROWS, WIDTH)
FEED_SHAPE = (ROWS, HIDDEN)
MACS = ROWS * WIDTH * WIDTH * 2
ATTEND_WEIGHTS = [pltpu.VMEM((WIDTH, 3 * WIDTH), LOW), pltpu.VMEM((WIDTH, WIDTH), LOW)]
FEED_WEIGHTS = [pltpu.VMEM((WIDTH, HIDDEN), LOW), pltpu.VMEM((HIDDEN, WIDTH), LOW)]


def shape(dims, kind=LOW):
    return jax.ShapeDtypeStruct(dims, kind)


def enter_cotangent(half, own, swapped, raw, sem):
    @pl.when(half[0] == 0)
    def _():
        pltpu.make_async_copy(own.at[0], raw, sem).start()

    @pl.when(half[0] == 1)
    def _():
        pltpu.make_async_copy(swapped.at[1], raw, sem).start()

    return pltpu.make_async_copy(swapped.at[1], raw, sem)


def kernel_call(body, ins, outs, scratch, flops, moved, name, out_specs=None, grant=VMEM_LIMIT):
    return pl.pallas_call(
        body,
        in_specs=ins,
        out_specs=out_specs or [VMEM] * len(outs),
        out_shape=outs,
        scratch_shapes=scratch,
        compiler_params=pltpu.CompilerParams(vmem_limit_bytes=grant),
        cost_estimate=pl.CostEstimate(flops=flops, bytes_accessed=moved, transcendentals=0),
        name=name,
    )


def attend_first(inputs, half, lens, spans, weights, smalls):
    def body(x, half, lens, spans, so, sp, qo, qp, oo, op, u, h, raw, small, qkv, mixed, wq, wo, sems):
        enter = pltpu.make_async_copy(x.at[half[0]], raw, sems.at[2, 0])
        enter.start()
        wqkv = Weight(half[0], qo, qp, wq, sems.at[0], True, 3)
        wout = Weight(half[0], oo, op, wo, sems.at[1], False)
        pick_halves(half, so, sp, small)
        enter.wait()
        mask = so[:, SMALL:].astype(LOW)
        h[...] = jnp.where(span_rows(spans, half), mask, raw[...].reshape(ROWS, WIDTH))
        attend_body(h, wqkv, wout, small, lens, half, qkv, None, mixed, None, None, u, [wout])

    return kernel_call(
        body,
        [ANY, SMEM, SMEM, SMEM, VMEM, VMEM] + [ANY] * 4,
        [shape(ROW_SHAPE), shape(ROW_SHAPE)],
        [
            pltpu.VMEM((2, LENGTH, WIDTH), LOW),
            SMALL_SCRATCH,
            pltpu.VMEM(QKV_SHAPE, LOW),
            pltpu.VMEM(ROW_SHAPE, LOW),
            *ATTEND_WEIGHTS,
            pltpu.SemaphoreType.DMA((3, 6)),
        ],
        40 * MACS,
        80000000,
        "attend_first",
    )(inputs, half, lens, spans, *smalls, *weights[0], *weights[1])


def feed_first(u, half, weights, smalls):
    def body(u, half, so, sp, uo, up, do, dp, y, small, active, wu, wd, sems):
        wup = Weight(half[0], uo, up, wu, sems.at[0], True, 3)
        wdown = Weight(half[0], do, dp, wd, sems.at[1], False)
        pick_halves(half, so, sp, small)
        feed_body(u, wup, wdown, small, None, active, None, None, y, [wdown])

    return kernel_call(
        body,
        [VMEM, SMEM, VMEM, VMEM] + [ANY] * 4,
        [shape(ROW_SHAPE)],
        [
            SMALL_SCRATCH,
            pltpu.VMEM(FEED_SHAPE, LOW),
            *FEED_WEIGHTS,
            pltpu.SemaphoreType.DMA((2, 6)),
        ],
        8 * MACS,
        14000000,
        "feed_first",
    )(u, half, *smalls, *weights[2], *weights[3])[0]


KEPT = [
    shape(ROW_SHAPE),
    shape(QKV_SHAPE),
    shape(PROBS_SHAPE),
    shape(ROW_SHAPE),
    shape(ROW_SHAPE, F32),
    shape((ROWS, 1), F32),
    shape(ROW_SHAPE),
    shape(FEED_SHAPE),
    shape(FEED_SHAPE),
    shape(ROW_SHAPE, F32),
    shape((ROWS, 1), F32),
    shape(ROW_SHAPE),
]


def middle(h0, received, cotangent, swapped, half, first, lens, weights, smalls):
    def body(h0, received, cot, swap, half, first, lens, so, sp, qo, qp, oo, op, uo, up, do, dp, *rest):
        outs, rest = rest[: len(KEPT)], rest[len(KEPT) :]
        both, rest = rest[0], rest[1:]
        gh, small, gr2, gz, ga, gr1, gb, gsmall, gqkv, go, raw, wq, wo, wu, wd = rest[:15]
        keeps, sems, out_sems, raw_sem = rest[15:-3], *rest[-3:]
        h, qkv, probs, mixed, normal1, inverse1, u, slope, active, normal2, inverse2, y = keeps
        wqkv = Weight(half[0], qo, qp, wq, sems.at[0], True, 3)
        wout = Weight(half[0], oo, op, wo, sems.at[1])
        wup = Weight(half[0], uo, up, wu, sems.at[2], True, 3)
        wdown = Weight(half[0], do, dp, wd, sems.at[3])
        enter = enter_cotangent(half, cot, swap, raw, raw_sem)
        pick_halves(half, so, sp, small)
        leaving = []

        def leave(places):
            for place in places:
                copy = pltpu.make_async_copy(keeps[place], outs[place], out_sems.at[place])
                copy.start()
                leaving.append(copy)

        h[...] = jnp.where(first[0] > 0, h0[...], received[...])
        attend_body(
            h, wqkv, wout, small, lens, half, qkv, probs, mixed, normal1, inverse1, u, (),
            (wout, wup, wdown, enter),
        )
        leave(range(7))
        feed_body(u, wup, wdown, small, slope, active, normal2, inverse2, y)
        leave(range(7, 12))
        output = pltpu.make_async_copy(y, both.at[0], out_sems.at[len(KEPT)])
        output.start()
        leaving.append(output)
        upstream = raw[...].reshape(ROWS, WIDTH).astype(F32)
        top_back_body(upstream, small, normal2, inverse2, gr2, gz, gsmall)
        feed_back_body(gr2, gz, wup, wdown, small, slope, normal1, inverse1, ga, gr1, gb, gsmall)
        heads_back_body(gb, wout, qkv, probs, gqkv, None, go)
        gh[...] = (gr1[...] + dot_nt(gqkv[...], wqkv.get())).astype(LOW)
        output = pltpu.make_async_copy(gh, both.at[1], out_sems.at[len(KEPT) + 1])
        output.start()
        leaving.append(output)
        for copy in leaving:
            copy.wait()

    return kernel_call(
        body,
        [VMEM, VMEM, ANY, ANY, SMEM, SMEM, SMEM, VMEM, VMEM] + [ANY] * 8,
        KEPT + [shape((2, ROWS, WIDTH)), shape(ROW_SHAPE)],
        [
            SMALL_SCRATCH,
            pltpu.VMEM(ROW_SHAPE, F32),
            pltpu.VMEM(ROW_SHAPE, LOW),
            pltpu.VMEM(FEED_SHAPE, LOW),
            pltpu.VMEM(ROW_SHAPE, F32),
            pltpu.VMEM(ROW_SHAPE, LOW),
            SMALL_SCRATCH,
            pltpu.VMEM(QKV_SHAPE, LOW),
            pltpu.VMEM(ROW_SHAPE, LOW),
            pltpu.VMEM((2, LENGTH, WIDTH), LOW),
            *ATTEND_WEIGHTS,
            *FEED_WEIGHTS,
            *[pltpu.VMEM(kept.shape, kept.dtype) for kept in KEPT],
            pltpu.SemaphoreType.DMA((4, 6)),
            pltpu.SemaphoreType.DMA((len(KEPT) + 2,)),
            pltpu.SemaphoreType.DMA,
        ],
        24 * MACS,
        45000000,
        "middle",
        [ANY] * len(KEPT) + [ANY, VMEM],
        BIG_GRANT,
    )(
        h0, received, cotangent, swapped, half, first, lens, *smalls,
        *weights[0], *weights[1], *weights[2], *weights[3],
    )


MIB = 1024 * 1024


def half_columns(ref, which):
    size = ref.shape[1] // 2
    return ref[:, pl.ds(pl.multiple_of(which * size, 128), size)]


class Arriving:
    def __init__(self, pairs, sems):
        self.copies = {}
        for place, (name, source, dest) in enumerate(pairs):
            copy = pltpu.make_async_copy(source, dest, sems.at[place])
            copy.start()
            self.copies[name] = (copy, dest)

    def get(self, name):
        copy, dest = self.copies[name]
        copy.wait()
        return dest


class Leaving:
    def __init__(self, sems):
        self.sems = sems
        self.copies = []

    def send(self, source, target):
        copy = pltpu.make_async_copy(source, target, self.sems.at[len(self.copies)])
        copy.start()
        self.copies.append(copy)

    def wait(self):
        for copy in self.copies:
            copy.wait()


def send_folded(leaving, local, target, left_side, right):
    for block in range(right.shape[1] // WIDTH):
        rows = pl.ds(block * 384, 384)
        grad = dot_tn(left_side, right[:, block * WIDTH : (block + 1) * WIDTH])
        local[rows, :] = grad.astype(LOW)
        leaving.send(local.at[rows], target.at[rows])


TOKEN = shape((8, 128), F32)
GRAD_SHAPE = (1536, WIDTH)
GRAD_SCRATCH = pltpu.VMEM(GRAD_SHAPE, LOW)


def back_feed(cotangent, swapped, returned, half, first, weights, smalls, kept):
    u, slope, active, n1, i1, n2, i2 = kept

    def body(cot, swap, returned, half, first, so, sp, i1, n2, i2, uo, up, do, dp, u, slope, active, n1, *rest):
        outs, rest = rest[:8], rest[8:]
        down_other, down_own, up_other, up_own, gr1, gb, gsmall, token = outs
        gr2, gz, ga, v0, v1, v2, v3, small, raw, wu, wd, vu, vs, va, vn, sems, in_sems, out_sems = rest
        enter = enter_cotangent(half, cot, swap, raw, sems.at[2, 0])
        arriving = Arriving([("active", active, va)], in_sems)
        wdown = Weight(half[0], do, dp, wd, sems.at[1])
        later = Arriving(
            [("slope", slope, vs), ("normal", n1, vn), ("u", u, vu)],
            in_sems.at[pl.ds(1, 3)],
        )
        wup = Weight(half[0], uo, up, wu, sems.at[0])
        pick_halves(half, so, sp, small)
        enter.wait()
        upstream = jnp.where(first[0] > 0, returned[...], raw[...].reshape(ROWS, WIDTH))
        top_back_body(upstream.astype(F32), small, n2, i2, gr2, gz, gsmall)
        leaving = Leaving(out_sems)
        arriving.get("active")
        for which, local, target in ((1 - half[0], v0, down_other), (half[0], v1, down_own)):
            local[...] = dot_tn(half_columns(va, which), gz[...]).astype(LOW)
            leaving.send(local, target)
        for each in ("slope", "normal", "u"):
            later.get(each)
        wdown.wait()
        wup.wait()
        feed_back_body(gr2, gz, wup, wdown, small, vs, vn, i1, ga, gr1, gb, gsmall)
        for which, local, target in ((1 - half[0], v2, up_other), (half[0], v3, up_own)):
            send_folded(leaving, local, target, half_columns(vu, which), ga)
        token[...] = jnp.zeros(token.shape, F32)
        leaving.wait()

    return kernel_call(
        body,
        [ANY, ANY, VMEM, SMEM, SMEM] + [VMEM] * 5 + [ANY] * 8,
        [shape(GRAD_SHAPE)] * 4
        + [shape(ROW_SHAPE, F32), shape(ROW_SHAPE), shape((2, SMALL), F32), TOKEN],
        [
            pltpu.VMEM(ROW_SHAPE, F32),
            pltpu.VMEM(ROW_SHAPE, LOW),
            pltpu.VMEM(FEED_SHAPE, LOW),
            *[GRAD_SCRATCH] * 4,
            SMALL_SCRATCH,
            pltpu.VMEM((2, LENGTH, WIDTH), LOW),
            *FEED_WEIGHTS,
            pltpu.VMEM(ROW_SHAPE, LOW),
            pltpu.VMEM(FEED_SHAPE, LOW),
            pltpu.VMEM(FEED_SHAPE, LOW),
            pltpu.VMEM(ROW_SHAPE, F32),
            pltpu.SemaphoreType.DMA((3, 2)),
            pltpu.SemaphoreType.DMA((4,)),
            pltpu.SemaphoreType.DMA((10,)),
        ],
        200 * MACS,
        600000000,
        "back_feed",
        [ANY] * 4 + [VMEM] * 4,
        BIG_GRANT,
    )(
        cotangent, swapped, returned, half, first, *smalls, i1, n2, i2, *weights[2], *weights[3],
        u, slope, active, n1,
    )


def back_attend(gb, gr1, half, first, spans, weights, gsmall, h, qkv, probs, mixed):
    def body(gb, half, first, spans, gsmall, oo, op, qo, qp, gr1, h, qkv, probs, mixed, *rest):
        outs, rest = rest[:6], rest[6:]
        other, own, small_other, small_own, gh, token = outs
        gqkv, go, gqv, vother, vown, wo, wq, vr, vh, vq, vp, vm, sems, in_sems, out_sems = rest
        wout = Weight(half[0], oo, op, wo, sems.at[0])
        arriving = Arriving([("qkv", qkv, vq), ("probs", probs, vp)], in_sems)
        wqkv = Weight(half[0], qo, qp, wq, sems.at[1], False)
        arriving.get("qkv")
        arriving.get("probs")
        wqkv.start()
        late = Arriving([("h", h, vh), ("mixed", mixed, vm), ("gr1", gr1, vr)], in_sems.at[pl.ds(2, 3)])
        heads_back_body(gb, wout, vq, vp, gqkv, gqv, go)
        leaving = Leaving(out_sems)
        late.get("h")
        late.get("mixed")
        for which, local, target in ((1 - half[0], vother, other), (half[0], vown, own)):
            send_folded(leaving, local, target, half_columns(vh, which), gqkv)
            local[1152:, :] = dot_tn(half_columns(vm, which), gb[...]).astype(LOW)
            leaving.send(local.at[pl.ds(1152, 384)], target.at[pl.ds(1152, 384)])
        late.get("gr1")
        full = vr[...] + dot_nt(gqkv[...], wqkv.get())
        dropped = span_rows(spans, half) & (first[0] > 0)
        zero = jnp.zeros_like(full)
        gh[...] = jnp.where(dropped, zero, full).astype(LOW)
        gmask = column_sum(jnp.where(dropped, full, zero))
        for which, target in ((1 - half[0], small_other), (half[0], small_own)):
            target[:, :WIDTH] = gqv[pl.ds(which, 1), :]
            target[:, WIDTH:SMALL] = gsmall[pl.ds(which, 1), WIDTH:]
            target[:, SMALL:] = gmask
        token[...] = jnp.zeros(token.shape, F32)
        leaving.wait()

    return kernel_call(
        body,
        [VMEM, SMEM, SMEM, SMEM, VMEM] + [ANY] * 9,
        [
            shape(GRAD_SHAPE),
            shape(GRAD_SHAPE),
            shape((1, SMALL + WIDTH), F32),
            shape((1, SMALL + WIDTH), F32),
            shape(ROW_SHAPE),
            TOKEN,
        ],
        [
            pltpu.VMEM(QKV_SHAPE, LOW),
            pltpu.VMEM(ROW_SHAPE, LOW),
            pltpu.VMEM((2, WIDTH), F32),
            GRAD_SCRATCH,
            GRAD_SCRATCH,
            ATTEND_WEIGHTS[1],
            ATTEND_WEIGHTS[0],
            pltpu.VMEM(ROW_SHAPE, F32),
            pltpu.VMEM(ROW_SHAPE, LOW),
            pltpu.VMEM(QKV_SHAPE, LOW),
            pltpu.VMEM(PROBS_SHAPE, LOW),
            pltpu.VMEM(ROW_SHAPE, LOW),
            pltpu.SemaphoreType.DMA((2, 2)),
            pltpu.SemaphoreType.DMA((5,)),
            pltpu.SemaphoreType.DMA((8,)),
        ],
        180 * MACS,
        400000000,
        "back_attend",
        [ANY, ANY] + [VMEM] * 4,
    )(gb, half, first, spans, gsmall, *weights[1], *weights[0], gr1, h, qkv, probs, mixed)


TAIL = 16
BLOCK = 96


def add_rows(target, sources, at, rows):
    for start in range(0, rows, BLOCK):
        size = min(BLOCK, rows - start)
        place = pl.ds(at + start, size)
        if not isinstance(at, int):
            place = pl.ds(pl.multiple_of(at + start, 16), size)
        if len(sources) == 2:
            target[start : start + size, :] = sources[0][place, :] + sources[1][place, :]
            continue
        total = sources[0][place, :].astype(F32)
        for source in sources[1:]:
            total = total + source[place, :].astype(F32)
        target[start : start + size, :] = total.astype(LOW)


LONG = 30000000000


def ordered(
    name, body, ins, outs, where, after, out_specs=None, scratch=(), in_specs=None, grant=16, aliases=None,
    flops=LONG,
):
    count, made = len(ins), len(outs)

    def kernel(where, after, *refs):
        refs[count + made][...] = jnp.zeros(TOKEN.shape, F32)
        body(where, refs[:count], refs[count : count + made] + refs[count + made + 1 :])

    result = pl.pallas_call(
        kernel,
        in_specs=[SMEM, HBM] + (in_specs or [VMEM] * count),
        out_specs=(out_specs or [VMEM] * made) + [VMEM],
        out_shape=list(outs) + [TOKEN],
        scratch_shapes=list(scratch),
        input_output_aliases=aliases or {},
        compiler_params=pltpu.CompilerParams(vmem_limit_bytes=grant * MIB),
        cost_estimate=pl.CostEstimate(flops=flops, bytes_accessed=flops, transcendentals=0),
        name=name,
    )(where, after, *ins)
    return result[:made], result[made]


def partner(x, axis, bit):
    return lax.ppermute(x, axis, [(i, i ^ 1 << bit) for i in range(lax.axis_size(axis))])


def moved_on(index, axis, steps):
    z, x, y = index // 8, index // 2 % 4, index % 2
    if axis == "z":
        z = steps(z)
    elif axis == "x":
        x = steps(x)
    else:
        y = steps(y)
    return z * 8 + x * 2 + y


def send_along(value, axes, place):
    pairs = []
    for section in range(4):
        for index in range(32):
            to = moved_on(index, axes[section % 2], place)
            pairs.append((section * 32 + index, section * 32 + to))
    return lax.ppermute(value, ("section", "dp"), pairs)


def exchange(value, part, step):
    flip = 1 if part == step else 3
    return send_along(value, "zx", lambda place: place ^ flip)


def turn(value, steps):
    return send_along(value, "xz", lambda place: (place + steps) % 4)


def across_y(value):
    return send_along(value, "yy", lambda place: place ^ 1)


def swap_core_one(value):
    pairs = [
        (section * 32 + index, section * 32 + (index ^ 1)) for section in (1, 3) for index in range(32)
    ]
    return lax.ppermute(value, ("section", "dp"), pairs)


def between_layers(value, back):
    pairs = []
    for core in range(2):
        for index in range(32):
            pair = (core * 32 + index, (core + 2) * 32 + (index ^ core))
            pairs.append(pair[::-1] if back else pair)
    return lax.ppermute(value, ("section", "dp"), pairs)


def own_places(core):
    index = lax.axis_index("dp")
    z, x = index // 8, index // 2 % 4
    ring = jnp.where(core == 0, z, x)
    high = ring // 2
    low = high ^ (ring % 2)
    table = [low, high, high, low, jnp.where(core == 0, x, z)]
    return jnp.stack(table).astype(jnp.int32)


def row_shapes(*counts):
    return [shape((count, WIDTH)) for count in counts]


def add_tail(target, rows, sources, at, extra):
    if extra:
        total = sources[0][at : at + extra, :].astype(F32)
        for source in sources[1:]:
            total = total + source[at : at + extra, :].astype(F32)
        target[rows : rows + extra, :] = total.astype(LOW)


class Chain:
    def __init__(self, name, places, tail=0):
        self.name = name
        self.places = places
        self.tail = (0, tail)
        self.keep = [None, None]
        self.got = [None, None]

    def kernel(self, name, body, ins, outs, token, *more, **named):
        return ordered(self.name + name, body, ins, outs, self.places, token, *more, **named)

    def pairs(self):
        return (self.keep[0], self.got[0], self.keep[1], self.got[1])

    def first_sum(self, name, sent, token):
        sources, half_rows, tails = self.sources, self.rows, self.tail

        def body(places, ins, refs):
            outs, held, sems = refs[:2], refs[2:6], refs[6]
            copies = []
            for index in range(4):
                bit, at = places[2 * (index // 2)], sources[index // 2][2]
                which = 1 - bit if sent else bit
                rows = pl.ds(pl.multiple_of(at + which * half_rows, 16), half_rows)
                copy = pltpu.make_async_copy(ins[index].at[rows], held[index], sems.at[index])
                copy.start()
                copies.append(copy)
            for part in range(2):
                copies[2 * part].wait()
                copies[2 * part + 1].wait()
                add_rows(outs[part], held[2 * part : 2 * part + 2], 0, half_rows)
                if tails[part]:
                    outs[part][half_rows:, :] = self.tail_body(ins[4:])

        arrays = [array for own, got, _ in sources for array in (own, got)]
        return self.kernel(
            name,
            body,
            (*arrays, *self.tail_ins),
            row_shapes(half_rows + tails[0], half_rows + tails[1]),
            token,
            scratch=(*[pltpu.VMEM((half_rows, WIDTH), LOW)] * 4, pltpu.SemaphoreType.DMA((4,))),
            in_specs=[HBM] * 4 + [VMEM] * len(self.tail_ins),
            grant=63 if sent else 46,
            flops=LONG if sent else 0,
        )

    def start(self, sources, rows, token, tail_ins=(), tail_body=None):
        self.rows, self.sources = rows // 2, sources
        self.tail_ins, self.tail_body = tuple(tail_ins), tail_body
        sends, token = self.first_sum("send", True, token)
        self.got = [exchange(sends[part], part, 0) for part in range(2)]
        return token

    def hold(self, token):
        keeps, token = self.first_sum("keep", False, token)
        self.keep = list(keeps)
        return token

    def halve(self, token, flops):
        self.rows //= 2
        rows, tails = self.rows, self.tail

        def body(places, ins, outs):
            for part in range(2):
                bit = places[2 * part + 1]
                pair = ins[2 * part : 2 * part + 2]
                for target, which in ((outs[2 * part + 1], 1 - bit), (outs[2 * part], bit)):
                    add_rows(target, pair, which * rows, rows)
                    add_tail(target, rows, pair, 2 * rows, tails[part])

        counts = [rows + tails[0]] * 2 + [rows + tails[1]] * 2
        outs, token = self.kernel(
            "halve", body, self.pairs(), row_shapes(*counts), token, flops=flops
        )
        for part in range(2):
            self.keep[part] = outs[2 * part]
            self.got[part] = exchange(outs[2 * part + 1], part, 1)
        return token

    def cross(self, token):
        whole_rows, extra = self.rows, self.tail[1]
        rows = whole_rows // 2

        def body(places, ins, refs):
            outs, total = refs[:4], refs[4]
            add_rows(total.at[pl.ds(0, whole_rows)], ins[:2], 0, whole_rows)
            add_rows(total.at[pl.ds(whole_rows, whole_rows)], ins[2:], 0, whole_rows)
            for steps in range(4):
                quarter = (places[4] + steps) % 4
                outs[steps][:rows, :] = total[pl.ds(pl.multiple_of(quarter * rows, 16), rows), :]
                add_tail(outs[steps], rows, ins[2:], whole_rows, extra)

        (self.own, *sends), token = self.kernel(
            "cross",
            body,
            self.pairs(),
            row_shapes(*[rows + extra] * 4),
            token,
            None,
            (pltpu.VMEM((2 * whole_rows, WIDTH), LOW),),
        )
        self.rows = rows
        self.ring = [turn(send, steps) for steps, send in zip((1, 2, 3), sends)]
        return token

    def across(self, token):
        rows = self.rows + self.tail[1]

        def body(places, ins, outs):
            add_rows(outs[0], ins, 0, rows)

        (self.own,), token = self.kernel(
            "across", body, (self.own, *self.ring), row_shapes(rows), token
        )
        self.other = across_y(self.own)
        return token

    def total(self, token, more_outs=(), more_body=None):
        rows, extra = self.rows, self.tail[1]

        def body(places, ins, outs):
            add_rows(outs[0], ins, 0, rows)
            if extra:
                add_rows(outs[1], ins, rows, extra)
                more_body(outs[1][...].astype(F32), outs[2:])

        counts = [rows] + ([extra] if extra else [])
        outs, token = self.kernel(
            "total", body, (self.own, self.other), row_shapes(*counts) + list(more_outs), token
        )
        self.own = outs[0]
        self.tail_sum = outs[1] if extra else None
        self.ring = [turn(self.own, steps) for steps in (1, 2, 3)]
        return outs[2:], token

    def back(self, token, more_ins=(), more_outs=(), more_body=None):
        rows = self.rows

        def body(places, ins, refs):
            outs, total = refs[:-1], refs[-1]
            for steps in range(4):
                quarter = (places[4] - steps + 4) % 4
                total[pl.ds(pl.multiple_of(quarter * rows, 16), rows), :] = ins[steps][...]
            outs[0][...] = total[: 2 * rows, :]
            outs[1][...] = total[2 * rows :, :]
            if more_body is not None:
                more_body(ins[4:], outs[2:])

        outs, token = self.kernel(
            "back",
            body,
            (self.own, *self.ring) + tuple(more_ins),
            row_shapes(2 * rows, 2 * rows) + list(more_outs),
            token,
            None,
            (pltpu.VMEM((4 * rows, WIDTH), LOW),),
        )
        self.rows = 2 * rows
        self.keep = list(outs[:2])
        self.got = [exchange(self.keep[part], part, 1) for part in range(2)]
        return outs[2:], token

    def double(self, token, flops):
        rows = self.rows

        def body(places, ins, outs):
            for part in range(2):
                bit = places[2 * part + 1]
                for which, source in ((bit, ins[2 * part]), (1 - bit, ins[2 * part + 1])):
                    outs[part][pl.ds(pl.multiple_of(which * rows, 16), rows), :] = source[...]

        outs, token = self.kernel(
            "double", body, self.pairs(), row_shapes(2 * rows, 2 * rows), token, flops=flops
        )
        self.rows = 2 * rows
        self.keep = list(outs)
        self.got = [exchange(self.keep[part], part, 0) for part in range(2)]
        return token

    def finish(self, token, outs, place, got, flops, more_ins=(), more_outs=(), more_body=None):
        rows = self.rows
        mine = tuple(self.got if got else self.keep)
        kept = tuple(outs) if got else ()

        def body(places, ins, refs):
            targets, wide, sems = refs[: len(outs)], refs[-2], refs[-1]
            if more_body is not None:
                more_body(ins[2 + len(kept) :], refs[len(outs) : -2])
            waits = []
            for part in range(2):
                bit = places[2 * part]
                half = 1 - bit if got else bit
                wide[part] = ins[part][...].astype(F32)
                at = 0
                for size, starts in place(targets, part, half):
                    source, sem = wide.at[part, pl.ds(at, size)], sems.at[len(waits)]
                    starts(source, sem)
                    waits.append((size, source, sem))
                    at += size
            for size, source, sem in waits:
                pltpu.make_async_copy(source, wide.at[0, pl.ds(0, size)], sem).wait()

        return self.kernel(
            "finish",
            body,
            mine + kept + tuple(more_ins),
            [shape(out.shape, F32) for out in outs] + list(more_outs),
            token,
            out_specs=[ANY] * len(outs) + [VMEM] * len(more_outs),
            scratch=(pltpu.VMEM((2, rows, WIDTH), F32), pltpu.SemaphoreType.DMA((4,))),
            in_specs=[VMEM] * 2 + [ANY] * len(kept) + [VMEM] * len(more_ins),
            grant=24,
            flops=flops,
            aliases={4 + index: index for index in range(len(kept))},
        )


def copy_to(target):
    return lambda source, sem: pltpu.make_async_copy(source, target, sem).start()


def block_columns(block):
    return pl.ds(pl.multiple_of(block * WIDTH, 128), WIDTH)


def place_x(refs, part, half):
    down, up = refs
    if part == 0:
        return [(768, copy_to(down.at[pl.ds(pl.multiple_of(half * 768, 8), 768)]))]
    return [(384, copy_to(up.at[:, block_columns(2 * half + block)])) for block in range(2)]


def place_y(refs, part, half):
    qkv, out = refs
    if part == 0:
        return [(384, copy_to(qkv.at[:, block_columns(half)]))]

    def starts(source, sem):
        @pl.when(half == 0)
        def _():
            copy_to(qkv.at[:, block_columns(2)])(source, sem)

        @pl.when(half == 1)
        def _():
            copy_to(out)(source, sem)

    return [(384, starts)]


def pack_vectors(vectors):
    size = sum(vector.shape[0] for vector in vectors)
    total = jnp.zeros((size,), F32)
    at = 0
    for vector in vectors:
        total = total + jnp.pad(vector.astype(F32), (at, size - at - vector.shape[0]))
        at += vector.shape[0]
    return total.reshape(1, size)


def per_device(
    inputs,
    cotangent,
    lengths,
    cdr_spans,
    mask_vector,
    w_qkv,
    qv_bias,
    w_out,
    b_out,
    norm1_gain,
    norm1_bias,
    w_up,
    b_up,
    w_down,
    b_down,
    norm2_gain,
    norm2_bias,
):
    section_index = lax.axis_index("section")
    core = section_index % 2
    half = core.astype(jnp.int32).reshape(1)
    first = (section_index < 2).astype(jnp.int32).reshape(1)
    places = own_places(core)
    small = pack_vectors(
        (
            qv_bias,
            b_out,
            norm1_gain,
            norm1_bias,
            b_up,
            b_down,
            norm2_gain,
            norm2_bias,
            mask_vector,
        )
    )
    small_got = partner(small, "section", 0)
    got_qkv, got_out = partner((w_qkv, w_out), "section", 0)
    w_up, w_down, got_qkv, got_out, small_got = lax.optimization_barrier(
        (w_up, w_down, got_qkv, got_out, small_got)
    )
    smalls = (small, small_got)
    got_up, got_down = partner((w_up, w_down), "section", 0)
    weights = [(w_qkv, got_qkv), (w_out, got_out), (w_up, got_up), (w_down, got_down)]

    swapped = swap_core_one(cotangent)
    lens_got = swap_core_one(lengths)
    swaps = (core == 1) & (section_index >= 2)
    layer_lens = jnp.where(swaps, lens_got, lengths)

    u, h0 = attend_first(inputs, half, lengths, cdr_spans, weights, smalls)
    first_out = feed_first(u, half, weights, smalls)
    received = between_layers(first_out, False)
    kept = middle(h0, received, cotangent, swapped, half, first, layer_lens, weights, smalls)
    h, qkv, probs, mixed, normal1, inverse1, u, slope, active, normal2, inverse2, output = kept[:12]
    returned = between_layers(kept[13], True)

    a_other, a_own, b_other, b_own, gr1, gb, gsmall, token = back_feed(
        cotangent,
        swapped,
        returned,
        half,
        first,
        weights,
        smalls,
        (u, slope, active, normal1, inverse1, normal2, inverse2),
    )
    a_got = partner(a_other, "section", 0)
    b_got = partner(b_other, "section", 0)
    x, y = Chain("x_", places), Chain("y_", places, TAIL)
    y_other, y_own, small_other, small_own, gh, token = back_attend(
        gb, gr1, half, first, cdr_spans, weights, gsmall, h, qkv, probs, mixed
    )
    y_got = partner(y_other, "section", 0)
    small_got = partner(small_other, "section", 0)
    token = x.start([(a_own, a_got, 0), (b_own, b_got, 0)], 1536, token)

    def tail_rows(ins):
        total = ins[0][...] + ins[1][...]
        rows = [total[:, at : at + WIDTH] for at in range(0, SMALL + WIDTH, WIDTH)]
        rows.append(jnp.zeros((TAIL - len(rows), WIDTH), F32))
        return jnp.concatenate(rows, axis=0).astype(LOW)

    token = y.start(
        [(y_own, y_got, 0), (y_own, y_got, 768)], 768, token, (small_own, small_got), tail_rows
    )
    both, token = lax.optimization_barrier((kept[12], token))
    both_got = swap_core_one(both)
    token = x.hold(token)
    token = x.halve(token, 0)
    token = y.hold(token)
    token = y.halve(token, LONG)
    both_got, token = lax.optimization_barrier((both_got, token))
    token = x.cross(token)
    token = y.cross(token)
    token = x.across(token)
    token = y.across(token)
    _, token = x.total(token)

    def small_outputs(tail, outs):
        flat = jnp.concatenate([tail[row : row + 1, :] for row in range(6)], axis=1)
        at = 0
        for out, size in zip(outs, SIZES):
            out[...] = flat[0, at : at + size]
            at += size

    out_small, token = y.total(token, [shape((size,), F32) for size in SIZES], small_outputs)
    _, token = x.back(token)

    def mask_output(ins, outs):
        outs[0][...] = ins[0][6, :].astype(F32) + ins[1][6, :].astype(F32)

    _, token = y.back(token)
    gradients_x = [shape((1536, WIDTH), F32), shape((384, HIDDEN), F32)]
    gradients_y = [shape((384, 3 * WIDTH), F32), shape((384, WIDTH), F32)]
    token = x.double(token, LONG)
    gradients_x, token = x.finish(token, gradients_x, place_x, False, LONG)
    token = y.double(token, 0)
    tail_sum, token = lax.optimization_barrier((y.tail_sum, token))
    mask_got = partner(tail_sum, "section", 1)
    gradients_y, token = y.finish(token, gradients_y, place_y, False, 0)
    both_got, token = lax.optimization_barrier((both_got, token))
    (g_down, g_up), token = x.finish(token, gradients_x, place_x, True, LONG)
    (g_qkv, g_out, mask_grad), token = y.finish(
        token,
        gradients_y,
        place_y,
        True,
        LONG,
        (tail_sum, mask_got),
        [shape((WIDTH,), F32)],
        mask_output,
    )
    output = jnp.where(swaps, both_got[0], output)
    gh = jnp.where(swaps, both_got[1], gh)

    g_qv, g_bo, g_n1g, g_n1b, g_bu, g_bd, g_n2g, g_n2b = out_small
    return (
        output.reshape(1, 2, LENGTH, WIDTH),
        gh.reshape(1, 2, LENGTH, WIDTH),
        mask_grad,
        g_qkv,
        g_qv,
        g_out,
        g_bo,
        g_n1g,
        g_n1b,
        g_up,
        g_bu,
        g_down,
        g_bd,
        g_n2g,
        g_n2b,
    )


def solution(mesh):
    in_specs = (
        P(None, "dp", None, None),
        P(None, "dp", None, None),
        P(None, "dp"),
        P(None, "dp", None),
        P(),
        P("section", None),
        P("section"),
        P("section", None),
        P("section"),
        P("section"),
        P("section"),
        P("section", None),
        P("section"),
        P("section", None),
        P("section"),
        P("section"),
        P("section"),
    )
    out_specs = (
        P("section", "dp", None, None),
        P("section", "dp", None, None),
        P(),
        P("section", None),
        P("section"),
        P("section", None),
        P("section"),
        P("section"),
        P("section"),
        P("section", None),
        P("section"),
        P("section", None),
        P("section"),
        P("section"),
        P("section"),
    )
    return jax.shard_map(
        per_device, mesh=mesh, in_specs=in_specs, out_specs=out_specs, check_vma=False
    )
```
